32 devices in a mesh: dp: 16 (over z, y, core), blk: 2 (over x).
Axes of the slice: x: 2, y: 2, z: 4, core: 2. Of those that a mesh axis runs over, the one named last changes fastest.
Arguments:
- queries: bfloat16 [16, 125, 256], P('dp'), may hold values from -6 to 6
- memory: bfloat16 [16, 16384, 256], P('dp', 'blk'), may hold values from -6 to 6
- quarter_turns: int32 [16], P('dp'), may hold values from 0 to 3
- token_order: int32 [16, 16384], P('dp', 'blk'), may hold values from 0 to 16383, each once within a row
- lengths: int32 [16], P('dp'), may hold values from 4096 to 16384, as said below
- attn_in: bfloat16 [2, 3, 256, 256], replicated, may hold values from -0.375 to 0.375
- attn_out: bfloat16 [2, 256, 256], replicated, may hold values from -1 to 1
- attn_bias: bfloat16 [2, 3, 256], replicated, may hold values from -3 to 3
- ffn_in: bfloat16 [256, 2048], replicated, may hold values from -0.375 to 0.375
- ffn_in_bias: bfloat16 [2048], replicated, may hold values from -3 to 3
- ffn_out: bfloat16 [2048, 256], replicated, may hold values from -0.125 to 0.125
- ffn_out_bias: bfloat16 [256], replicated, may hold values from -3 to 3
- norm_gain: bfloat16 [3, 256], replicated, may hold values from 0.25 to 1.75
- norm_bias: bfloat16 [3, 256], replicated, may hold values from -2 to 2
- query_pos: bfloat16 [125, 256], replicated, may hold values from -6 to 6
- out_grad: bfloat16 [16, 125, 256], P('dp'), may hold values from -6 to 6
Outputs:
- result: bfloat16 [16, 125, 256], P('dp')
- queries_grad: bfloat16 [16, 125, 256], P('dp')
- memory_grad: bfloat16 [16, 16384, 256], P('dp', 'blk')
- attn_in_grad: float32 [2, 3, 256, 256], replicated
- attn_out_grad: float32 [2, 256, 256], replicated
- attn_bias_grad: float32 [2, 3, 256], replicated
- ffn_in_grad: float32 [256, 2048], replicated
- ffn_in_bias_grad: float32 [2048], replicated
- ffn_out_grad: float32 [2048, 256], replicated
- ffn_out_bias_grad: float32 [256], replicated
- norm_gain_grad: float32 [3, 256], replicated
- norm_bias_grad: float32 [3, 256], replicated
- query_pos_grad: float32 [125, 256], replicated
The draws below stay inside these ranges and needn't reach their ends.
Inputs may be any that keep to these rules, and one draw needn't show every extreme that they name: `token_order`: each page's row holds every location 0 to 16383 once. `lengths`: a page's valid locations are those below its length; some page has all 16384.
All inputs are finite; a program needn't handle non-finite values.
Results may differ from the reference program's by a relative error of at most 0.0173.
The reference program's roundings to bfloat16 on the way count: a program that leaves them out, or rounds other values in their place, can miss the bound.
Values may be sent and summed in bfloat16 or wider, within the bound.
A program may use at most 320 MiB of HBM per device.

```python
import math
import jax
import jax.numpy as jnp
from jax import lax

D = 256
HEADS = 8
FF = 2048
NQ = 125
HD = 32
SIDE = 128
MEM = 16384
PAGES = 16


def draw_lengths(key, part):
    key = jax.random.fold_in(key, 11)
    first_key, second_key = jax.random.split(key)
    drawn = jax.random.randint(first_key, (PAGES,), MEM // 4, MEM + 1)
    full_page = jax.random.randint(second_key, (), 0, PAGES)
    return jnp.where(jnp.arange(PAGES) == full_page, MEM, drawn).astype(jnp.int32)


def touch_ends(values, stream_key, least, largest):
    longest = values.shape.index(max(values.shape))
    spots = []
    for shift in (0, 1):
        where = [jax.random.randint(jax.random.fold_in(stream_key, axis), (), 0, length) for axis, length in enumerate(values.shape)]
        where[longest] = (where[longest] + shift) % values.shape[longest]
        spots.append(tuple(where))
    return values.at[spots[0]].set(least).at[spots[1]].set(largest)


def shard_levels(key, extent, shards, low, top_value):
    def one(axis_at, shards_of):
        heights = jax.random.uniform(jax.random.fold_in(jax.random.fold_in(key, 6), axis_at), (shards_of,), jnp.float32, low / len(shards), top_value / len(shards))
        return jnp.repeat(jnp.exp(heights), extent[axis_at] // shards_of).reshape((-1,) + (1,) * (len(extent) - axis_at - 1))

    level = one(*shards[0])
    for cut in shards[1:]:
        level = level * one(*cut)
    return level


def bell_draw(key, extent, scale, limit, cuts=(), kind=jnp.bfloat16):
    values = scale * jax.random.normal(key, extent, jnp.float32)
    if cuts:
        values = values * shard_levels(key, extent, cuts, -0.22, 0.18)
    return jnp.clip(values, -limit, limit).astype(kind)


def setup_inputs(seed: int = 0) -> dict:
    splits = jax.random.split(jax.random.key(seed), 17)
    queries = bell_draw(splits[0], (PAGES, NQ, D), 1.0, 6.0, ((0, 16),))
    memory = bell_draw(splits[1], (PAGES, MEM, D), 1.0, 6.0, ((0, 16), (1, 2)))
    quarter_turns = touch_ends(jax.random.randint(splits[2], (PAGES,), 0, 4), jax.random.fold_in(splits[2], 1), 0, 3).astype(jnp.int32)
    token_order = jax.vmap(lambda own: jax.random.permutation(own, MEM))(jax.random.split(splits[3], PAGES)).reshape((PAGES, MEM)).astype(jnp.int32)
    lengths = draw_lengths(jax.random.fold_in(splits[16], 71), 0)
    attn_in = bell_draw(splits[5], (2, 3, D, D), D ** -0.5, 0.375)
    attn_out = bell_draw(splits[6], (2, D, D), (D // 8) ** -0.5, 1.0)
    attn_bias = bell_draw(splits[7], (2, 3, D), 0.5, 3.0)
    ffn_in = bell_draw(splits[8], (D, FF), D ** -0.5, 0.375)
    ffn_in_bias = bell_draw(splits[9], (FF,), 0.5, 3.0)
    ffn_out = bell_draw(splits[10], (FF, D), FF ** -0.5, 0.125)
    ffn_out_bias = bell_draw(splits[11], (D,), 0.5, 3.0)
    norm_gain = jnp.clip(1.0 + 0.15 * jax.random.normal(splits[12], (3, D), jnp.float32), 0.25, 1.75).astype(jnp.bfloat16)
    norm_bias = bell_draw(splits[13], (3, D), 0.3, 2.0)
    query_pos = bell_draw(splits[14], (NQ, D), 1.0, 6.0)
    out_grad = bell_draw(splits[15], (PAGES, NQ, D), 1.0, 6.0, ((0, 16),))
    return {"queries": queries, "memory": memory, "quarter_turns": quarter_turns, "token_order": token_order, "lengths": lengths, "attn_in": attn_in, "attn_out": attn_out, "attn_bias": attn_bias, "ffn_in": ffn_in, "ffn_in_bias": ffn_in_bias, "ffn_out": ffn_out, "ffn_out_bias": ffn_out_bias, "norm_gain": norm_gain, "norm_bias": norm_bias, "query_pos": query_pos, "out_grad": out_grad}


@jax.custom_vjp
def low(v):
    return lax.optimization_barrier(v.astype(jnp.bfloat16)).astype(jnp.float32)

@jax.custom_vjp
def low_back(v):
    return v

def low_keep(v):
    return (low(v), None)

def low_pass(kept, grad):
    return (grad,)

def back_keep(v):
    return (v, None)

def back_low(kept, grad):
    return (low(grad),)
low.defvjp(low_keep, low_pass)
low_back.defvjp(back_keep, back_low)
masked_score = -1e+30
norm_eps = 1e-05

def both_ways(values):
    return low(low_back(values))

def product(left, right):
    return jnp.matmul(left, right, precision=lax.Precision.HIGHEST)

def sine_positions(token_order, quarter_turns):
    top_index = SIDE - 1
    row_at = token_order // SIDE
    col_at = token_order % SIDE
    turned = quarter_turns[:, None]
    row_new = jnp.where(turned == 0, row_at, jnp.where(turned == 1, col_at, jnp.where(turned == 2, top_index - row_at, top_index - col_at)))
    col_new = jnp.where(turned == 0, col_at, jnp.where(turned == 1, top_index - row_at, jnp.where(turned == 2, top_index - col_at, row_at)))
    half_width = D // 2
    channel = jnp.arange(half_width)
    inverse = jnp.exp((channel // 2).astype(jnp.float32) * (-2.0 * math.log(10000.0) / half_width))
    is_even = channel % 2 == 0

    def encode(coord):
        angle = ((coord.astype(jnp.float32) + 1.0) * (2.0 * math.pi / SIDE))[..., None] * inverse
        return jnp.where(is_even, jnp.sin(angle), jnp.cos(angle))
    return jnp.concatenate([encode(row_new), encode(col_new)], axis=-1)

def layer_norm(values, gain, shift):
    average = lax.optimization_barrier(jnp.mean(values, axis=-1, keepdims=True))
    centred = values - average
    variance = lax.optimization_barrier(jnp.mean(centred * centred, axis=-1, keepdims=True))
    return centred * lax.rsqrt(variance + norm_eps) * gain + shift

def attend(query, key_rows, value_rows, allowed):
    pages = query.shape[0]
    split_q = query.reshape(pages, query.shape[1], HEADS, HD)
    split_k = key_rows.reshape(pages, key_rows.shape[1], HEADS, HD)
    split_v = value_rows.reshape(pages, value_rows.shape[1], HEADS, HD)
    scores = low_back(jnp.einsum('pqhd,pkhd->phqk', split_q, split_k, precision=lax.Precision.HIGHEST) * (1.0 / math.sqrt(HD)))
    scores = jnp.where(allowed[:, None, None, :], scores, masked_score)
    weights = low(jax.nn.softmax(scores, axis=-1))
    mixed = jnp.einsum('phqk,pkhd->pqhd', weights, split_v, precision=lax.Precision.HIGHEST)
    return mixed.reshape(pages, query.shape[1], D)

def forward(weights, queries, memory, positions, allowed):
    attn_in, attn_out, attn_bias, ffn_in, ffn_in_bias, ffn_out, ffn_out_bias, norm_gain, norm_bias, query_pos = weights
    mixed_q = low(queries + query_pos)
    query_s = both_ways(product(mixed_q, attn_in[0, 0]) + attn_bias[0, 0])
    key_s = both_ways(product(mixed_q, attn_in[0, 1]))
    value_s = both_ways(product(queries, attn_in[0, 2]) + attn_bias[0, 1])
    every_key = jnp.ones((queries.shape[0], queries.shape[1]), dtype=bool)
    attended = both_ways(attend(query_s, key_s, value_s, every_key))
    branch = low_back(product(attended, attn_out[0]) + attn_bias[0, 2])
    first = layer_norm(queries + branch, norm_gain[0], norm_bias[0])
    cross_q = low(first + query_pos)
    query_c = both_ways(product(cross_q, attn_in[1, 0]) + attn_bias[1, 0])
    key_in = low(memory + positions)
    key_c = both_ways(product(key_in, attn_in[1, 1]))
    value_c = both_ways(product(memory, attn_in[1, 2]) + attn_bias[1, 1])
    attended_c = both_ways(attend(query_c, key_c, value_c, allowed))
    branch_c = low_back(product(attended_c, attn_out[1]) + attn_bias[1, 2])
    second = layer_norm(first + branch_c, norm_gain[1], norm_bias[1])
    ffn_input = low(second)
    hidden = low_back(product(ffn_input, ffn_in) + ffn_in_bias)
    activated = low(jax.nn.gelu(hidden, approximate=False))
    branch_f = low_back(product(activated, ffn_out) + ffn_out_bias)
    return layer_norm(second + branch_f, norm_gain[2], norm_bias[2])

def reference(queries, memory, quarter_turns, token_order, lengths, attn_in, attn_out, attn_bias, ffn_in, ffn_in_bias, ffn_out, ffn_out_bias, norm_gain, norm_bias, query_pos, out_grad):
    params = tuple((weight.astype(jnp.float32) for weight in (attn_in, attn_out, attn_bias, ffn_in, ffn_in_bias, ffn_out, ffn_out_bias, norm_gain, norm_bias, query_pos)))

    def grouped(values):
        return values.reshape((PAGES, 1) + values.shape[1:])
    inputs = (grouped(queries), grouped(memory), grouped(quarter_turns), grouped(token_order), grouped(lengths), grouped(out_grad))

    def one_page(totals, pieces):
        page_q, page_m, page_t, page_o, page_l, page_g = pieces
        positions = sine_positions(page_o, page_t)
        allowed = page_o < page_l[:, None]

        def run_layer(weights, query_in, memory_in):
            return forward(weights, query_in, memory_in, positions, allowed)
        result, pullback = jax.vjp(run_layer, params, page_q.astype(jnp.float32), page_m.astype(jnp.float32))
        weight_grads, query_grad, memory_grad = pullback(page_g.astype(jnp.float32))
        totals = jax.tree.map(jnp.add, totals, weight_grads)
        return (totals, (result.astype(jnp.bfloat16), query_grad.astype(jnp.bfloat16), memory_grad.astype(jnp.bfloat16)))
    start_totals = jax.tree.map(jnp.zeros_like, params)
    totals, outputs = lax.scan(one_page, start_totals, inputs)
    result_all = outputs[0].reshape(PAGES, NQ, D)
    queries_grad = outputs[1].reshape(PAGES, NQ, D)
    memory_grad = outputs[2].reshape(PAGES, MEM, D)
    return (result_all, queries_grad, memory_grad, totals[0], totals[1], totals[2], totals[3], totals[4], totals[5], totals[6], totals[7], totals[8], totals[9])
```

```python
import functools
import math

import jax
import jax.numpy as jnp
import numpy as np
from jax import lax
from jax.experimental import pallas as pl
from jax.experimental.pallas import tpu as pltpu
from jax.sharding import PartitionSpec as P

D = 256
HEADS = 8
HD = D // HEADS
SIDE = 128
NQ = 125
NP = 128
HQ = HEADS * NP
PAIR = 2 * NP
FF = 2048
CHUNK = 512

masked_score = -1e30
norm_eps = 1e-05
scale = 1.0 / math.sqrt(HD)
log2e = math.log2(math.e)

bf16 = jnp.bfloat16
f32 = jnp.float32

ROW_FFN_IN = 0
ROW_FFN_OUT = 2048
ROW_OUT_C = 4096
ROW_SMALL_F = 4352
ROW_Q = 4368
ROW_POS = 5648
ROW_SMALL_Q = 5776
ROWS_PAGE = 5792
ROWS_KEY = 528


def position_table():
    half = D // 2
    channel = np.arange(half)
    inverse = np.exp((channel // 2).astype(np.float32) * np.float32(-2.0 * math.log(10000.0) / half))
    angle = (np.arange(SIDE, dtype=np.float32) + 1.0) * np.float32(2.0 * math.pi / SIDE)
    angle = angle[:, None] * inverse
    rows = np.where(channel % 2 == 0, np.sin(angle), np.cos(angle)).astype(np.float32)
    table = np.zeros((2 * SIDE, D), np.float32)
    table[:SIDE, :half] = rows
    table[SIDE:, half:] = rows
    high = table.astype(jnp.bfloat16)
    low = (table - high.astype(np.float32)).astype(jnp.bfloat16)
    return high, low


def dot(a, b):
    return jnp.dot(a, b, preferred_element_type=f32)


def dot_nt(a, b):
    return lax.dot_general(a, b, (((1,), (1,)), ((), ())), preferred_element_type=f32)


def dot_tn(a, b):
    return lax.dot_general(a, b, (((0,), (0,)), ((), ())), preferred_element_type=f32)


def row_total(values):
    return jnp.sum(values.astype(f32), axis=0, keepdims=True)


def norm_forward(values):
    average = jnp.mean(values, axis=-1, keepdims=True)
    centred = values - average
    variance = jnp.mean(centred * centred, axis=-1, keepdims=True)
    rstd = lax.rsqrt(variance + norm_eps)
    return centred * rstd, rstd


def norm_backward(grad, normed, rstd, gain):
    grad_normed = grad * gain
    first = jnp.mean(grad_normed, axis=-1, keepdims=True)
    second = jnp.mean(grad_normed * normed, axis=-1, keepdims=True)
    grad_in = rstd * (grad_normed - first - normed * second)
    return grad_in, row_total(grad * normed), row_total(grad)


def spread_rows(rows):
    head = lax.broadcasted_iota(jnp.int32, (NP, D), 1) // HD
    return jnp.concatenate(
        [jnp.where(head == h, rows, 0.0) for h in range(HEADS)], axis=0
    ).astype(bf16)


def spread_cols(cols):
    head = lax.broadcasted_iota(jnp.int32, (D, NP), 0) // HD
    return jnp.concatenate(
        [jnp.where(head == h, cols, 0.0) for h in range(HEADS)], axis=1
    ).astype(bf16)


def own_blocks(pairs):
    parts = []
    for pair in pairs:
        parts += [pair[:HD, :NP], pair[HD:, NP:]]
    return jnp.concatenate(parts, axis=0)


def head_rows(row):
    return jnp.concatenate([row[:, NP * h : NP * h + NP] for h in range(HEADS)], axis=0)


def head_line(rows):
    return jnp.concatenate([rows[h : h + 1] for h in range(HEADS)], axis=1)


def per_channel(rows):
    return jnp.concatenate(
        [jnp.broadcast_to(rows[h : h + 1], (HD, NP)) for h in range(HEADS)], axis=0
    )


def head_sums(cols):
    return jnp.concatenate(
        [jnp.sum(cols[HD * h : HD * h + HD], axis=0, keepdims=True) for h in range(HEADS)], axis=0
    )


def pair_cols(p):
    return slice(PAIR * p, PAIR * p + PAIR)


def pair_rows(p):
    return slice(2 * HD * p, 2 * HD * p + 2 * HD)


def layer_kernel(
    tokens,
    queries_in,
    memory_hbm,
    turns_in,
    order_in,
    lengths_in,
    attn_in,
    attn_out,
    attn_bias,
    ffn_in_hbm,
    ffn_in_bias,
    ffn_out_hbm,
    ffn_out_bias,
    norm_gain,
    norm_bias,
    pos_in,
    out_grad_in,
    table_high,
    table_low,
    result_out,
    queries_grad_out,
    memory_grad_hbm,
    page_grads,
    key_grads,
    memory_s,
    key_in_s,
    key_s,
    value_s,
    aux_s,
    probs_s,
    code_s,
    score_a,
    score_b,
    weight_s,
    shifts_s,
    factor_s,
    total_s,
    mixed_s,
    ffn_in_s,
    ffn_out_s,
    gate_s,
    pad_s,
    back_w,
    query_x,
    grad_xt,
    grad_x,
    send_a,
    recv_a,
    send_b,
    recv_b,
    load_sem,
    store_sem,
    link_sem,
):
    member = lax.axis_index("blk")
    partner = (lax.axis_index("dp"), 1 - member)
    chunks = tokens // CHUNK

    barrier = pltpu.get_barrier_semaphore()
    pl.semaphore_signal(barrier, inc=1, device_id=partner, device_id_type=pl.DeviceIdType.MESH)

    load_memory = pltpu.make_async_copy(memory_hbm, memory_s, load_sem.at[0])
    load_ffn_in = pltpu.make_async_copy(ffn_in_hbm, ffn_in_s, load_sem.at[1])
    load_ffn_out = pltpu.make_async_copy(ffn_out_hbm, ffn_out_s, load_sem.at[2])
    load_memory.start()
    load_ffn_in.start()
    load_ffn_out.start()

    bias = attn_bias[...].astype(f32)
    gain = norm_gain[...].astype(f32)
    shift = norm_bias[...].astype(f32)

    order = order_in[...]
    turn = turns_in[0]
    row_at = order >> 7
    col_at = order & 127
    top = SIDE - 1
    row_new = jnp.where(
        turn == 0, row_at, jnp.where(turn == 1, col_at, jnp.where(turn == 2, top - row_at, top - col_at))
    )
    col_new = jnp.where(
        turn == 0, col_at, jnp.where(turn == 1, top - row_at, jnp.where(turn == 2, top - col_at, row_at))
    )
    past = jnp.where(order < lengths_in[0], 0, SIDE * SIDE)
    code_s[...] = (row_new * SIDE + col_new + past).astype(f32)

    pad_s[...] = jnp.zeros_like(pad_s)
    pad_s[0, :NQ] = queries_in[...].astype(f32)
    pad_s[1, :NQ] = pos_in[...].astype(f32)
    pad_s[2, :NQ] = out_grad_in[...].astype(f32)
    queries_f = pad_s[0]
    pos_f = pad_s[1]
    queries_b = queries_f.astype(bf16)
    mixed_q = (queries_f + pos_f).astype(bf16)
    query_self = (dot(mixed_q, attn_in[0]) + bias[0:1]).astype(bf16)
    key_self = dot(mixed_q, attn_in[1]).astype(bf16)
    value_self = (dot(queries_b, attn_in[2]) + bias[1:2]).astype(bf16)
    scores = dot(key_self, spread_cols(query_self.astype(f32).T)) * scale
    own_key = lax.broadcasted_iota(jnp.int32, (NP, HQ), 0) < NQ
    scores = jnp.where(own_key, scores, masked_score)
    raised = jnp.exp(scores - jnp.max(scores, axis=0, keepdims=True))
    probs_self = raised / jnp.sum(raised, axis=0, keepdims=True)
    probs_self_b = probs_self.astype(bf16)
    value_t = value_self.astype(f32).T.astype(bf16)
    attended = own_blocks(
        [dot(value_t[pair_rows(p)], probs_self_b[:, pair_cols(p)]) for p in range(4)]
    ).T.astype(bf16)
    first_normed, first_rstd = norm_forward(queries_f + dot(attended, attn_out[0]) + bias[2:3])
    first = first_normed * gain[0:1] + shift[0:1]
    cross_q = (first + pos_f).astype(bf16)
    query_c = (dot(cross_q, attn_in[3]) + bias[3:4]).astype(bf16)
    query_x[...] = spread_rows(query_c.astype(f32))
    query_xt = spread_cols(query_c.astype(f32).T)
    aux_row = jnp.where(
        lax.broadcasted_iota(jnp.int32, (NP, HQ // 2), 0) == 0, 1.0, 0.0
    ).astype(bf16)
    for g in range(2):
        weight_s[g, :NP] = query_xt[NP * g : NP * g + NP, HQ // 2 * g : HQ // 2 * (g + 1)]
        weight_s[g, NP:] = aux_row
    back_w[:D] = attn_in[4].astype(f32).T.astype(bf16)
    back_w[D:] = attn_in[5].astype(f32).T.astype(bf16)

    load_memory.wait()
    lane = lax.broadcasted_iota(jnp.int32, (CHUNK, NP), 1)
    value_bias = bias[4:5]

    @pl.loop(0, chunks)
    def _(i):
        rows = pl.ds(pl.multiple_of(i * CHUNK, CHUNK), CHUNK)
        line = code_s[pl.ds(i, 1), :]
        code = jnp.concatenate(
            [
                jnp.broadcast_to(line[:, NP * j : NP * j + NP], (NP, NP)).T
                for j in range(CHUNK // NP)
            ],
            axis=0,
        ).astype(jnp.int32)
        row_hot = jnp.where(((code >> 7) & 127) == lane, 1.0, 0.0)
        col_hot = jnp.where((code & 127) == lane, 1.0, 0.0)
        hot = jnp.concatenate([row_hot, col_hot], axis=1).astype(bf16)
        aux_s[rows] = jnp.where((code >= SIDE * SIDE) & (lane == 0), masked_score, 0.0).astype(bf16)
        block = memory_s[rows]
        positions = dot(hot, table_high[...]) + dot(hot, table_low[...])
        key_in = (block.astype(f32) + positions).astype(bf16)
        key_in_s[rows] = key_in
        key_s[rows] = dot(key_in, attn_in[4]).astype(bf16)
        value_s[rows] = (dot(block, attn_in[5]) + value_bias).astype(bf16)

    def score_chunk(i, out):
        rows = pl.ds(pl.multiple_of(i * CHUNK, CHUNK), CHUNK)
        for g in range(2):
            left = jnp.concatenate([key_s[rows, NP * g : NP * g + NP], aux_s[rows]], axis=1)
            out[:, HQ // 2 * g : HQ // 2 * (g + 1)] = dot(left, weight_s[g])

    def attend_chunk(i, scored):
        rows = pl.ds(pl.multiple_of(i * CHUNK, CHUNK), CHUNK)
        value_ct = value_s[rows].T
        for p in range(4):
            cols = pair_cols(p)
            before = total_s[0:1, cols]
            part = scored[:, cols]
            highest = jnp.maximum(
                before, jnp.max(part, axis=0, keepdims=True) * (scale * log2e)
            )
            raised = jnp.exp2(part * (scale * log2e) - highest)
            fade = jnp.exp2(before - highest)
            total_s[0:1, cols] = highest
            total_s[1:2, cols] = total_s[1:2, cols] * fade + jnp.sum(raised, axis=0, keepdims=True)
            shifts_s[pl.ds(i, 1), cols] = highest
            raised_b = raised.astype(bf16)
            probs_s[rows, cols] = raised_b
            mixed_s[pair_rows(p)] = mixed_s[pair_rows(p)] * fade + dot(
                value_ct[pair_rows(p)], raised_b
            )

    total_s[0:1] = jnp.full((1, HQ), -3e38, f32)
    total_s[1:2] = jnp.zeros((1, HQ), f32)
    mixed_s[...] = jnp.zeros_like(mixed_s)
    score_chunk(0, score_a)

    @pl.loop(0, chunks // 2)
    def _(j):
        i = j * 2
        score_chunk(i + 1, score_b)
        attend_chunk(i, score_a)
        score_chunk(jnp.minimum(i + 2, chunks - 1), score_a)
        attend_chunk(i + 1, score_b)

    send_a[:D] = own_blocks([mixed_s[pair_rows(p)] for p in range(4)])
    send_a[D : D + HEADS] = head_rows(total_s[0:1])
    send_a[D + HEADS :] = head_rows(total_s[1:2])
    pl.semaphore_wait(barrier, 1)
    swap_a = pltpu.make_async_remote_copy(
        src_ref=send_a,
        dst_ref=recv_a,
        send_sem=link_sem.at[0],
        recv_sem=link_sem.at[1],
        device_id=partner,
        device_id_type=pl.DeviceIdType.MESH,
    )
    swap_a.start()
    swap_a.wait()
    is_first = member == 0
    own = send_a[...]
    other = recv_a[...]
    left = jnp.where(is_first, own, other)
    right = jnp.where(is_first, other, own)
    high_l, high_r = left[D : D + HEADS], right[D : D + HEADS]
    highest = jnp.maximum(high_l, high_r)
    fade_l = jnp.exp2(high_l - highest)
    fade_r = jnp.exp2(high_r - highest)
    total = left[D + HEADS :] * fade_l + right[D + HEADS :] * fade_r
    mixed_t = left[:D] * per_channel(fade_l / total) + right[:D] * per_channel(fade_r / total)
    log_total = head_line(highest + jnp.log2(total))
    factor_s[...] = jnp.exp2(shifts_s[...] - log_total)
    attended_c = mixed_t.T.astype(bf16)

    second_normed, second_rstd = norm_forward(first + dot(attended_c, attn_out[1]) + bias[5:6])
    second = second_normed * gain[1:2] + shift[1:2]
    ffn_input = second.astype(bf16)
    load_ffn_in.wait()
    hidden = dot(ffn_input, ffn_in_s[...]) + ffn_in_bias[...].astype(f32)
    half_gate = 0.5 + 0.5 * lax.erf(hidden * math.sqrt(0.5))
    activated = (hidden * half_gate).astype(bf16)
    gate_s[...] = half_gate + hidden * jnp.exp(hidden * hidden * -0.5) * (1.0 / math.sqrt(2.0 * math.pi))
    load_ffn_out.wait()
    third_normed, third_rstd = norm_forward(
        second + dot(activated, ffn_out_s[...]) + ffn_out_bias[...].astype(f32)
    )
    result_out[...] = (third_normed * gain[2:3] + shift[2:3])[:NQ].astype(bf16)
    grad_third, gain_grad_2, shift_grad_2 = norm_backward(
        pad_s[2], third_normed, third_rstd, gain[2:3]
    )
    grad_branch_f = grad_third.astype(bf16)
    grad_hidden = (dot_nt(grad_branch_f, ffn_out_s[...]) * gate_s[...]).astype(bf16)
    grad_second = grad_third + dot_nt(grad_hidden, ffn_in_s[...])
    grad_second_in, gain_grad_1, shift_grad_1 = norm_backward(
        grad_second, second_normed, second_rstd, gain[1:2]
    )
    grad_branch_c = grad_second_in.astype(bf16)
    ffn_input_t = second.T.astype(bf16)
    for j in range(FF // D):
        cols = slice(D * j, D * j + D)
        page_grads[ROW_FFN_IN + D * j : ROW_FFN_IN + D * (j + 1)] = dot(ffn_input_t, grad_hidden[:, cols])
        page_grads[ROW_FFN_OUT + D * j : ROW_FFN_OUT + D * (j + 1)] = dot_tn(
            activated[:, cols], grad_branch_f
        )
    page_grads[ROW_OUT_C : ROW_OUT_C + D] = dot_tn(attended_c, grad_branch_c)
    hidden_sum = row_total(grad_hidden)
    page_grads[ROW_SMALL_F : ROW_SMALL_F + 16] = jnp.concatenate(
        [hidden_sum[:, D * j : D * j + D] for j in range(FF // D)]
        + [
            row_total(grad_branch_f),
            row_total(grad_branch_c),
            gain_grad_2,
            shift_grad_2,
            gain_grad_1,
            shift_grad_1,
            jnp.zeros((2, D), f32),
        ],
        axis=0,
    )

    grad_attended_c = dot_nt(grad_branch_c, attn_out[1]).astype(bf16).astype(f32)
    grad_attended_t = grad_attended_c.T
    grad_xt[...] = spread_cols(grad_attended_t)
    grad_x[...] = spread_rows(grad_attended_c)
    inner = head_line(head_sums(grad_attended_t * mixed_t))
    mixed_s[...] = jnp.zeros_like(mixed_s)
    key_grads[...] = jnp.zeros_like(key_grads)

    @pl.loop(0, chunks)
    def _(i):
        rows = pl.ds(pl.multiple_of(i * CHUNK, CHUNK), CHUNK)
        key_ct = key_s[rows].T
        value_c = value_s[rows]
        grads = []
        weights = []
        for p in range(4):
            cols = pair_cols(p)
            grad_probs = dot(value_c, grad_xt[:, cols])
            probs = probs_s[rows, cols].astype(f32) * factor_s[pl.ds(i, 1), cols]
            grad_scores = (probs * (grad_probs - inner[:, cols])).astype(bf16)
            mixed_s[pair_rows(p)] += dot(key_ct[pair_rows(p)], grad_scores)
            grads.append(grad_scores)
            weights.append(probs.astype(bf16))
        grad_key = (dot(jnp.concatenate(grads, axis=1), query_x[...]) * scale).astype(bf16)
        grad_value = dot(jnp.concatenate(weights, axis=1), grad_x[...]).astype(bf16)
        key_grads[:D] += dot_tn(key_in_s[rows], grad_key)
        key_grads[D : 2 * D] += dot_tn(memory_s[rows], grad_value)
        key_grads[2 * D : 2 * D + 1] += row_total(grad_value)
        both = jnp.concatenate([grad_key, grad_value], axis=1)
        memory_s[rows] = dot(both, back_w[...]).astype(bf16)
        pltpu.make_async_copy(memory_s.at[rows], memory_grad_hbm.at[rows], store_sem.at[i]).start()

    send_b[...] = own_blocks([mixed_s[pair_rows(p)] for p in range(4)]) * scale
    swap_b = pltpu.make_async_remote_copy(
        src_ref=send_b,
        dst_ref=recv_b,
        send_sem=link_sem.at[2],
        recv_sem=link_sem.at[3],
        device_id=partner,
        device_id_type=pl.DeviceIdType.MESH,
    )
    swap_b.start()
    swap_b.wait()
    grad_query_c = (send_b[...] + recv_b[...]).T.astype(bf16)

    cross_pos_grad = dot_nt(grad_query_c, attn_in[3])
    grad_first_in, gain_grad_0, shift_grad_0 = norm_backward(
        grad_second_in + cross_pos_grad, first_normed, first_rstd, gain[0:1]
    )
    grad_branch = grad_first_in.astype(bf16)
    grad_attended = dot_nt(grad_branch, attn_out[0]).astype(bf16).astype(f32)
    grad_probs = dot(value_self, spread_cols(grad_attended.T))
    inner_self = jnp.sum(probs_self * grad_probs, axis=0, keepdims=True)
    grad_scores = (probs_self * (grad_probs - inner_self)).astype(bf16)
    key_t = key_self.astype(f32).T.astype(bf16)
    grad_query_s = (
        own_blocks([dot(key_t[pair_rows(p)], grad_scores[:, pair_cols(p)]) for p in range(4)]) * scale
    ).T.astype(bf16)
    grad_key_s = (dot(grad_scores, spread_rows(query_self.astype(f32))) * scale).astype(bf16)
    grad_value_s = dot(probs_self_b, spread_rows(grad_attended)).astype(bf16)
    grad_mixed_q = dot_nt(grad_query_s, attn_in[0]) + dot_nt(grad_key_s, attn_in[1])
    queries_grad_out[...] = (grad_first_in + grad_mixed_q + dot_nt(grad_value_s, attn_in[2]))[
        :NQ
    ].astype(bf16)
    page_grads[ROW_Q : ROW_Q + D] = dot_tn(mixed_q, grad_query_s)
    page_grads[ROW_Q + D : ROW_Q + 2 * D] = dot_tn(mixed_q, grad_key_s)
    page_grads[ROW_Q + 2 * D : ROW_Q + 3 * D] = dot_tn(queries_b, grad_value_s)
    page_grads[ROW_Q + 3 * D : ROW_Q + 4 * D] = dot_tn(cross_q, grad_query_c)
    page_grads[ROW_Q + 4 * D : ROW_Q + 5 * D] = dot_tn(attended, grad_branch)
    page_grads[ROW_POS : ROW_POS + NP] = grad_mixed_q + cross_pos_grad
    page_grads[ROW_SMALL_Q : ROW_SMALL_Q + 16] = jnp.concatenate(
        [
            row_total(grad_query_s),
            row_total(grad_value_s),
            row_total(grad_branch),
            row_total(grad_query_c),
            gain_grad_0,
            shift_grad_0,
            jnp.zeros((10, D), f32),
        ],
        axis=0,
    )

    @pl.loop(0, chunks)
    def _(i):
        rows = pl.ds(pl.multiple_of(i * CHUNK, CHUNK), CHUNK)
        pltpu.make_async_copy(memory_s.at[rows], memory_grad_hbm.at[rows], store_sem.at[i]).wait()


def body(
    queries,
    memory,
    quarter_turns,
    token_order,
    lengths,
    attn_in,
    attn_out,
    attn_bias,
    ffn_in,
    ffn_in_bias,
    ffn_out,
    ffn_out_bias,
    norm_gain,
    norm_bias,
    query_pos,
    out_grad,
):
    tokens = memory.shape[1]
    chunks = tokens // CHUNK
    table_high, table_low = position_table()
    vmem = pl.BlockSpec(memory_space=pltpu.VMEM)
    smem = pl.BlockSpec(memory_space=pltpu.SMEM)
    anywhere = pl.BlockSpec(memory_space=pl.ANY)
    result, queries_grad, memory_grad, page_grads, key_grads = pl.pallas_call(
        functools.partial(layer_kernel, tokens),
        out_shape=[
            jax.ShapeDtypeStruct((NQ, D), bf16),
            jax.ShapeDtypeStruct((NQ, D), bf16),
            jax.ShapeDtypeStruct((tokens, D), bf16),
            jax.ShapeDtypeStruct((ROWS_PAGE, D), f32),
            jax.ShapeDtypeStruct((ROWS_KEY, D), f32),
        ],
        in_specs=[
            vmem,
            anywhere,
            smem,
            vmem,
            smem,
            vmem,
            vmem,
            vmem,
            anywhere,
            vmem,
            anywhere,
            vmem,
            vmem,
            vmem,
            vmem,
            vmem,
            vmem,
            vmem,
        ],
        out_specs=[vmem, vmem, anywhere, vmem, vmem],
        scratch_shapes=[
            pltpu.VMEM((tokens, D), bf16),
            pltpu.VMEM((tokens, D), bf16),
            pltpu.VMEM((tokens, D), bf16),
            pltpu.VMEM((tokens, D), bf16),
            pltpu.VMEM((tokens, NP), bf16),
            pltpu.VMEM((tokens, HQ), bf16),
            pltpu.VMEM((chunks, CHUNK), f32),
            pltpu.VMEM((CHUNK, HQ), f32),
            pltpu.VMEM((CHUNK, HQ), f32),
            pltpu.VMEM((2, D, HQ // 2), bf16),
            pltpu.VMEM((chunks, HQ), f32),
            pltpu.VMEM((chunks, HQ), f32),
            pltpu.VMEM((8, HQ), f32),
            pltpu.VMEM((D, PAIR), f32),
            pltpu.VMEM((D, FF), bf16),
            pltpu.VMEM((FF, D), bf16),
            pltpu.VMEM((NP, FF), f32),
            pltpu.VMEM((3, NP, D), f32),
            pltpu.VMEM((2 * D, D), bf16),
            pltpu.VMEM((HQ, D), bf16),
            pltpu.VMEM((D, HQ), bf16),
            pltpu.VMEM((HQ, D), bf16),
            pltpu.VMEM((D + 2 * HEADS, NP), f32),
            pltpu.VMEM((D + 2 * HEADS, NP), f32),
            pltpu.VMEM((D, NP), f32),
            pltpu.VMEM((D, NP), f32),
            pltpu.SemaphoreType.DMA((3,)),
            pltpu.SemaphoreType.DMA((chunks,)),
            pltpu.SemaphoreType.DMA((4,)),
        ],
        compiler_params=pltpu.CompilerParams(
            collective_id=0, has_side_effects=True, vmem_limit_bytes=62 * 1024 * 1024
        ),
        cost_estimate=pl.CostEstimate(
            flops=2 * 8 * tokens * HQ * D, bytes_accessed=20 << 20, transcendentals=tokens * HQ
        ),
        name="decoder_layer",
    )(
        queries.reshape(NQ, D),
        memory.reshape(tokens, D),
        quarter_turns,
        token_order.reshape(chunks, CHUNK),
        lengths,
        attn_in.reshape(6, D, D),
        attn_out,
        attn_bias.reshape(6, D),
        ffn_in,
        ffn_in_bias.reshape(1, FF),
        ffn_out,
        ffn_out_bias.reshape(1, D),
        norm_gain,
        norm_bias,
        query_pos,
        out_grad.reshape(NQ, D),
        jnp.asarray(table_high),
        jnp.asarray(table_low),
    )
    page = lax.psum(page_grads, "dp")
    key = lax.psum(key_grads, ("dp", "blk"))
    q_grads = page[ROW_Q:ROW_POS].reshape(5, D, D)
    small_f = page[ROW_SMALL_F : ROW_SMALL_F + 16]
    small_q = page[ROW_SMALL_Q : ROW_SMALL_Q + 16]
    attn_in_grad = jnp.stack(
        [q_grads[:3], jnp.concatenate([q_grads[3:4], key[: 2 * D].reshape(2, D, D)])]
    )
    attn_out_grad = jnp.stack([q_grads[4], page[ROW_OUT_C : ROW_OUT_C + D]])
    attn_bias_grad = jnp.stack(
        [small_q[0:3], jnp.stack([small_q[3], key[2 * D], small_f[9]])]
    )
    ffn_in_grad = (
        page[ROW_FFN_IN : ROW_FFN_IN + FF].reshape(FF // D, D, D).transpose(1, 0, 2).reshape(D, FF)
    )
    return (
        result[None],
        queries_grad[None],
        memory_grad[None],
        attn_in_grad,
        attn_out_grad,
        attn_bias_grad,
        ffn_in_grad,
        small_f[:8].reshape(FF),
        page[ROW_FFN_OUT : ROW_FFN_OUT + FF],
        small_f[8],
        jnp.stack([small_q[4], small_f[12], small_f[10]]),
        jnp.stack([small_q[5], small_f[13], small_f[11]]),
        page[ROW_POS : ROW_POS + NQ],
    )


def solution(mesh):
    in_specs = (
        P("dp", None, None),
        P("dp", "blk", None),
        P("dp"),
        P("dp", "blk"),
        P("dp"),
        P(),
        P(),
        P(),
        P(),
        P(),
        P(),
        P(),
        P(),
        P(),
        P(),
        P("dp", None, None),
    )
    out_specs = (
        P("dp", None, None),
        P("dp", None, None),
        P("dp", "blk", None),
        P(),
        P(),
        P(),
        P(),
        P(),
        P(),
        P(),
        P(),
        P(),
        P(),
    )
    return jax.shard_map(body, mesh=mesh, in_specs=in_specs, out_specs=out_specs, check_vma=False)
```

```python
import functools
import math

import jax
import jax.numpy as jnp
import numpy as np
from jax import lax
from jax.experimental import pallas as pl
from jax.experimental.pallas import tpu as pltpu
from jax.sharding import PartitionSpec as P

D = 256
HEADS = 8
HD = D // HEADS
SIDE = 128
NQ = 125
NP = 128
HQ = HEADS * NP
PAIR = 2 * NP
FF = 2048
CHUNK = 512

masked_score = -1e30
norm_eps = 1e-05
scale = 1.0 / math.sqrt(HD)
log2e = math.log2(math.e)

bf16 = jnp.bfloat16
f32 = jnp.float32

ROWS_F = FF + D // 2
ROW_POS = 3 * D
ROW_SMALL = 3 * D + NP
ROWS_T = 4 * D
TILE = 16


def digits_of(pages):
    digits = [(2, 1), (2, 2)]
    stride = 4
    while stride < pages:
        radix = 4 if pages // stride % 4 == 0 else 2
        digits.append((radix, stride))
        stride *= radix
    return digits


def padded(rows, pages):
    unit = TILE * pages
    return (rows + unit - 1) // unit * unit


def position_table():
    half = D // 2
    channel = np.arange(half)
    inverse = np.exp((channel // 2).astype(np.float32) * np.float32(-2.0 * math.log(10000.0) / half))
    angle = (np.arange(SIDE, dtype=np.float32) + 1.0) * np.float32(2.0 * math.pi / SIDE)
    angle = angle[:, None] * inverse
    return np.where(channel % 2 == 0, np.sin(angle), np.cos(angle)).astype(np.float32)


def dot(a, b):
    return jnp.dot(a, b, preferred_element_type=f32)


def dot_nt(a, b):
    return lax.dot_general(a, b, (((1,), (1,)), ((), ())), preferred_element_type=f32)


def dot_tn(a, b):
    return lax.dot_general(a, b, (((0,), (0,)), ((), ())), preferred_element_type=f32)


def row_total(values):
    return jnp.sum(values.astype(f32), axis=0, keepdims=True)


def norm_forward(values):
    average = jnp.mean(values, axis=-1, keepdims=True)
    centred = values - average
    variance = jnp.mean(centred * centred, axis=-1, keepdims=True)
    rstd = lax.rsqrt(variance + norm_eps)
    return centred * rstd, rstd


def norm_backward(grad, normed, rstd, gain):
    grad_normed = grad * gain
    first = jnp.mean(grad_normed, axis=-1, keepdims=True)
    second = jnp.mean(grad_normed * normed, axis=-1, keepdims=True)
    grad_in = rstd * (grad_normed - first - normed * second)
    return grad_in, row_total(grad * normed), row_total(grad)


def spread_rows(rows):
    head = lax.broadcasted_iota(jnp.int32, (NP, D), 1) // HD
    return jnp.concatenate(
        [jnp.where(head == h, rows, 0.0) for h in range(HEADS)], axis=0
    ).astype(bf16)


def spread_cols(cols):
    head = lax.broadcasted_iota(jnp.int32, (D, NP), 0) // HD
    return jnp.concatenate(
        [jnp.where(head == h, cols, 0.0) for h in range(HEADS)], axis=1
    ).astype(bf16)


def own_blocks(pairs):
    parts = []
    for pair in pairs:
        parts += [pair[:HD, :NP], pair[HD:, NP:]]
    return jnp.concatenate(parts, axis=0)


def head_rows(row):
    return jnp.concatenate([row[:, NP * h : NP * h + NP] for h in range(HEADS)], axis=0)


def head_line(rows):
    return jnp.concatenate([rows[h : h + 1] for h in range(HEADS)], axis=1)


def per_channel(rows):
    return jnp.concatenate(
        [jnp.broadcast_to(rows[h : h + 1], (HD, NP)) for h in range(HEADS)], axis=0
    )


def head_sums(cols):
    return jnp.concatenate(
        [jnp.sum(cols[HD * h : HD * h + HD], axis=0, keepdims=True) for h in range(HEADS)], axis=0
    )


def pair_cols(p):
    return slice(PAIR * p, PAIR * p + PAIR)


def pair_rows(p):
    return slice(2 * HD * p, 2 * HD * p + 2 * HD)


class PageSum:
    def __init__(self, pages, rows, landing, whole, sent, arrived):
        self.rows, self.landing, self.whole = rows, landing, whole
        self.sent, self.arrived = sent, arrived
        self.page = lax.axis_index("dp")
        self.member = lax.axis_index("blk")
        self.digits = digits_of(pages)
        self.extents = [rows.shape[0]]
        self.bases = [0]
        self.slots = []
        self.places = []
        slot = 0
        place = 0
        for radix, stride in self.digits:
            digit = self.page // stride % radix
            extent = self.extents[-1] // radix
            self.slots.append(slot)
            self.places.append(place)
            slot += radix - 1
            place += (radix - 1) * extent
            self.bases.append(pl.multiple_of(self.bases[-1] + digit * extent, TILE))
            self.extents.append(extent)
        self.gather_slot = slot
        self.last = len(self.digits)
        self.phases = [self.scatter_phase(s) for s in range(self.last)]
        self.phases.append(self.owned_phase)
        for s in range(self.last - 1, 2, -1):
            self.phases.append(self.spread_phase(s))
        self.phases += [self.sides_phase, self.corners_phase, self.core_phase, self.end_phase]

    @staticmethod
    def landing_rows(pages, rows):
        total, extent = 0, rows
        for radix, _ in digits_of(pages):
            extent //= radix
            total += (radix - 1) * extent
        return total

    @staticmethod
    def copies(pages):
        return sum(radix - 1 for radix, _ in digits_of(pages)) * 2 + 6

    def peer(self, step, hop):
        radix, stride = self.digits[step]
        digit = self.page // stride % radix
        other = lax.rem(digit + hop, radix)
        return (self.page + (other - digit) * stride, self.member), other

    def copy(self, slot, source, target, device):
        return pltpu.make_async_remote_copy(
            src_ref=source,
            dst_ref=target,
            send_sem=self.sent.at[slot],
            recv_sem=self.arrived.at[slot],
            device_id=device,
            device_id_type=pl.DeviceIdType.MESH,
        )

    def scatter_copies(self, step):
        radix, _ = self.digits[step]
        extent = self.extents[step + 1]
        for hop in range(1, radix):
            device, other = self.peer(step, hop)
            start = pl.multiple_of(self.bases[step] + other * extent, TILE)
            place = self.places[step] + (hop - 1) * extent
            yield self.copy(
                self.slots[step] + hop - 1,
                self.rows.at[pl.ds(start, extent)],
                self.landing.at[pl.ds(place, extent)],
                device,
            )

    def scatter_sum(self, step):
        radix, _ = self.digits[step]
        extent = self.extents[step + 1]
        total = self.rows[pl.ds(self.bases[step + 1], extent)].astype(f32)
        for hop in range(1, radix):
            place = self.places[step] + (hop - 1) * extent
            total = total + self.landing[pl.ds(place, extent)].astype(f32)
        return total.astype(bf16)

    def scatter_phase(self, step):
        def run():
            if step > 0:
                self.finish(self.scatter_copies(step - 1))
                self.rows[pl.ds(self.bases[step], self.extents[step])] = self.scatter_sum(step - 1)
            self.begin(self.scatter_copies(step))

        return run

    def gather_copies(self, step):
        radix, _ = self.digits[step]
        place = self.whole.at[self.member, pl.ds(self.bases[step + 1], self.extents[step + 1])]
        for hop in range(1, radix):
            device, _ = self.peer(step, hop)
            yield self.copy(self.gather_slot + self.slots[step] + hop - 1, place, place, device)

    def side_copies(self):
        slot = self.gather_slot + self.slots[1]
        beside, other = self.peer(1, 1)
        across = (self.page, 1 - self.member)
        extent = self.extents[2]
        place = self.whole.at[self.member, pl.ds(self.bases[2], extent)]
        extra = self.gather_slot * 2
        yield self.copy(slot, place, place, beside)
        yield self.copy(extra, place, place, across)

    def corner_copies(self):
        beside, other = self.peer(1, 1)
        across = (self.page, 1 - self.member)
        half = self.extents[2] // 2
        core_base = self.bases[1]
        side_base = pl.multiple_of(core_base + other * self.extents[2], TILE)
        first = self.whole.at[self.member, pl.ds(side_base, half)]
        second = self.whole.at[1 - self.member, pl.ds(pl.multiple_of(self.bases[2] + half, TILE), half)]
        extra = self.gather_slot * 2
        yield self.copy(extra + 1, first, first, across)
        yield self.copy(extra + 2, second, second, beside)

    def core_copies(self):
        device, _ = self.peer(0, 1)
        for m in range(2):
            place = self.whole.at[m, pl.ds(self.bases[1], self.extents[1])]
            yield self.copy(self.gather_slot * 2 + 3 + m, place, place, device)

    def begin(self, copies):
        for copy in copies:
            copy.start()

    def finish(self, copies):
        for copy in copies:
            copy.wait()

    def owned_phase(self):
        self.finish(self.scatter_copies(self.last - 1))
        self.whole[self.member, pl.ds(self.bases[self.last], self.extents[self.last])] = self.scatter_sum(
            self.last - 1
        )
        self.begin(self.gather_copies(self.last - 1))

    def spread_phase(self, step):
        def run():
            self.finish(self.gather_copies(step))
            self.begin(self.gather_copies(step - 1))

        return run

    def sides_phase(self):
        self.finish(self.gather_copies(2))
        self.begin(self.side_copies())

    def corners_phase(self):
        self.finish(self.side_copies())
        self.begin(self.corner_copies())

    def core_phase(self):
        self.finish(self.corner_copies())
        self.begin(self.core_copies())

    def end_phase(self):
        self.finish(self.core_copies())


def layer_kernel(
    tokens,
    pages,
    queries_in,
    memory_hbm,
    turns_in,
    order_in,
    lengths_in,
    attn_in,
    attn_out,
    attn_bias,
    ffn_in_hbm,
    ffn_in_bias,
    ffn_out_hbm,
    ffn_out_bias,
    norm_gain,
    norm_bias,
    pos_in,
    out_grad_in,
    table_in,
    result_out,
    queries_grad_out,
    memory_grad_hbm,
    whole_f_hbm,
    whole_t_hbm,
    memory_s,
    key_in_s,
    key_s,
    value_s,
    aux_s,
    probs_s,
    code_s,
    score_a,
    score_b,
    weight_s,
    table_s,
    shifts_s,
    factor_s,
    total_s,
    mixed_s,
    ffn_in_s,
    ffn_out_s,
    gate_s,
    pad_s,
    back_w,
    query_x,
    grad_xt,
    grad_x,
    send_a,
    recv_a,
    send_b,
    recv_b,
    key_grads,
    send_k,
    recv_k,
    small_s,
    rows_f,
    landing_f,
    whole_f,
    rows_t,
    landing_t,
    whole_t,
    load_sem,
    store_sem,
    link_sem,
    sent_f,
    arrived_f,
    sent_t,
    arrived_t,
):
    member = lax.axis_index("blk")
    partner = (lax.axis_index("dp"), 1 - member)
    chunks = tokens // CHUNK

    sum_f = PageSum(pages, rows_f, landing_f, whole_f, sent_f, arrived_f)
    sum_t = PageSum(pages, rows_t, landing_t, whole_t, sent_t, arrived_t)

    barrier = pltpu.get_barrier_semaphore()
    peers = [partner]
    for step, (radix, _) in enumerate(sum_f.digits):
        peers += [sum_f.peer(step, hop)[0] for hop in range(1, radix)]
    for peer in peers:
        pl.semaphore_signal(barrier, inc=1, device_id=peer, device_id_type=pl.DeviceIdType.MESH)

    load_memory = pltpu.make_async_copy(memory_hbm.at[0], memory_s, load_sem.at[0])
    load_ffn_in = pltpu.make_async_copy(ffn_in_hbm, ffn_in_s, load_sem.at[1])
    load_ffn_out = pltpu.make_async_copy(ffn_out_hbm, ffn_out_s, load_sem.at[2])
    load_memory.start()
    load_ffn_in.start()
    load_ffn_out.start()

    bias = jnp.concatenate([attn_bias[0], attn_bias[1]], axis=0).astype(f32)
    gain = norm_gain[...].astype(f32)
    shift = norm_bias[...].astype(f32)

    order = order_in[...]
    turn = turns_in[0]
    row_at = order >> 7
    col_at = order & 127
    top = SIDE - 1
    row_new = jnp.where(
        turn == 0, row_at, jnp.where(turn == 1, col_at, jnp.where(turn == 2, top - row_at, top - col_at))
    )
    col_new = jnp.where(
        turn == 0, col_at, jnp.where(turn == 1, top - row_at, jnp.where(turn == 2, top - col_at, row_at))
    )
    past = jnp.where(order < lengths_in[0], 0, SIDE * SIDE)
    code_s[...] = (row_new * SIDE + col_new + past).astype(f32)

    pad_s[...] = jnp.zeros_like(pad_s)
    pad_s[0, :NQ] = queries_in[0].astype(f32)
    pad_s[1, :NQ] = pos_in[...].astype(f32)
    pad_s[2, :NQ] = out_grad_in[0].astype(f32)
    queries_f = pad_s[0]
    pos_f = pad_s[1]
    queries_b = queries_f.astype(bf16)
    mixed_q = (queries_f + pos_f).astype(bf16)
    query_self = (dot(mixed_q, attn_in[0, 0]) + bias[0:1]).astype(bf16)
    key_self = dot(mixed_q, attn_in[0, 1]).astype(bf16)
    value_self = (dot(queries_b, attn_in[0, 2]) + bias[1:2]).astype(bf16)
    scores = dot(key_self, spread_cols(query_self.astype(f32).T)) * scale
    own_key = lax.broadcasted_iota(jnp.int32, (NP, HQ), 0) < NQ
    scores = jnp.where(own_key, scores, masked_score)
    raised = jnp.exp(scores - jnp.max(scores, axis=0, keepdims=True))
    probs_self = raised / jnp.sum(raised, axis=0, keepdims=True)
    probs_self_b = probs_self.astype(bf16)
    value_t = value_self.astype(f32).T.astype(bf16)
    attended = own_blocks(
        [dot(value_t[pair_rows(p)], probs_self_b[:, pair_cols(p)]) for p in range(4)]
    ).T.astype(bf16)
    first_normed, first_rstd = norm_forward(queries_f + dot(attended, attn_out[0]) + bias[2:3])
    first = first_normed * gain[0:1] + shift[0:1]
    cross_q = (first + pos_f).astype(bf16)
    query_c = (dot(cross_q, attn_in[1, 0]) + bias[3:4]).astype(bf16)
    query_x[...] = spread_rows(query_c.astype(f32))
    query_xt = spread_cols(query_c.astype(f32).T)
    aux_row = jnp.where(
        lax.broadcasted_iota(jnp.int32, (NP, HQ // 2), 0) == 0, 1.0, 0.0
    ).astype(bf16)
    for g in range(2):
        weight_s[g, :NP] = query_xt[NP * g : NP * g + NP, HQ // 2 * g : HQ // 2 * (g + 1)]
        weight_s[g, NP:] = aux_row
    back_w[:D] = attn_in[1, 1].astype(f32).T.astype(bf16)
    back_w[D:] = attn_in[1, 2].astype(f32).T.astype(bf16)

    table = table_in[...]
    nothing = jnp.zeros((SIDE, D // 2), f32)
    table = jnp.concatenate(
        [jnp.concatenate([table, nothing], axis=1), jnp.concatenate([nothing, table], axis=1)], axis=0
    )
    table_high = table.astype(bf16)
    table_s[0] = table_high
    table_s[1] = (table - table_high.astype(f32)).astype(bf16)

    load_memory.wait()
    lane = lax.broadcasted_iota(jnp.int32, (CHUNK, NP), 1)
    value_bias = bias[4:5]

    @pl.loop(0, chunks)
    def _(i):
        rows = pl.ds(pl.multiple_of(i * CHUNK, CHUNK), CHUNK)
        line = code_s[:, rows]
        code = jnp.concatenate(
            [
                jnp.broadcast_to(line[:, NP * j : NP * j + NP], (NP, NP)).T
                for j in range(CHUNK // NP)
            ],
            axis=0,
        ).astype(jnp.int32)
        row_hot = jnp.where(((code >> 7) & 127) == lane, 1.0, 0.0)
        col_hot = jnp.where((code & 127) == lane, 1.0, 0.0)
        hot = jnp.concatenate([row_hot, col_hot], axis=1).astype(bf16)
        aux_s[rows] = jnp.where((code >= SIDE * SIDE) & (lane == 0), masked_score, 0.0).astype(bf16)
        block = memory_s[rows]
        positions = dot(hot, table_s[0]) + dot(hot, table_s[1])
        key_in = (block.astype(f32) + positions).astype(bf16)
        key_in_s[rows] = key_in
        key_s[rows] = dot(key_in, attn_in[1, 1]).astype(bf16)
        value_s[rows] = (dot(block, attn_in[1, 2]) + value_bias).astype(bf16)

    def score_chunk(i, out):
        rows = pl.ds(pl.multiple_of(i * CHUNK, CHUNK), CHUNK)
        for g in range(2):
            left = jnp.concatenate([key_s[rows, NP * g : NP * g + NP], aux_s[rows]], axis=1)
            out[:, HQ // 2 * g : HQ // 2 * (g + 1)] = dot(left, weight_s[g])

    def attend_chunk(i, scored):
        rows = pl.ds(pl.multiple_of(i * CHUNK, CHUNK), CHUNK)
        value_ct = value_s[rows].T
        for p in range(4):
            cols = pair_cols(p)
            before = total_s[0:1, cols]
            part = scored[:, cols]
            highest = jnp.maximum(
                before, jnp.max(part, axis=0, keepdims=True) * (scale * log2e)
            )
            raised = jnp.exp2(part * (scale * log2e) - highest)
            fade = jnp.exp2(before - highest)
            total_s[0:1, cols] = highest
            total_s[1:2, cols] = total_s[1:2, cols] * fade + jnp.sum(raised, axis=0, keepdims=True)
            shifts_s[pl.ds(i, 1), cols] = highest
            raised_b = raised.astype(bf16)
            probs_s[rows, cols] = raised_b
            mixed_s[pair_rows(p)] = mixed_s[pair_rows(p)] * fade + dot(
                value_ct[pair_rows(p)], raised_b
            )

    total_s[0:1] = jnp.full((1, HQ), -3e38, f32)
    total_s[1:2] = jnp.zeros((1, HQ), f32)
    mixed_s[...] = jnp.zeros_like(mixed_s)
    score_chunk(0, score_a)

    @pl.loop(0, chunks // 2)
    def _(j):
        i = j * 2
        score_chunk(i + 1, score_b)
        attend_chunk(i, score_a)
        score_chunk(jnp.minimum(i + 2, chunks - 1), score_a)
        attend_chunk(i + 1, score_b)

    send_a[:D] = own_blocks([mixed_s[pair_rows(p)] for p in range(4)])
    send_a[D : D + HEADS] = head_rows(total_s[0:1])
    send_a[D + HEADS :] = head_rows(total_s[1:2])
    pl.semaphore_wait(barrier, len(peers))
    swap_a = pltpu.make_async_remote_copy(
        src_ref=send_a,
        dst_ref=recv_a,
        send_sem=link_sem.at[0],
        recv_sem=link_sem.at[1],
        device_id=partner,
        device_id_type=pl.DeviceIdType.MESH,
    )
    swap_a.start()
    swap_a.wait()
    is_first = member == 0
    own = send_a[...]
    other = recv_a[...]
    left = jnp.where(is_first, own, other)
    right = jnp.where(is_first, other, own)
    high_l, high_r = left[D : D + HEADS], right[D : D + HEADS]
    highest = jnp.maximum(high_l, high_r)
    fade_l = jnp.exp2(high_l - highest)
    fade_r = jnp.exp2(high_r - highest)
    total = left[D + HEADS :] * fade_l + right[D + HEADS :] * fade_r
    mixed_t = left[:D] * per_channel(fade_l / total) + right[:D] * per_channel(fade_r / total)
    log_total = head_line(highest + jnp.log2(total))
    factor_s[...] = jnp.exp2(shifts_s[...] - log_total)
    attended_c = mixed_t.T.astype(bf16)

    second_normed, second_rstd = norm_forward(first + dot(attended_c, attn_out[1]) + bias[5:6])
    second = second_normed * gain[1:2] + shift[1:2]
    ffn_input = second.astype(bf16)
    load_ffn_in.wait()
    hidden = dot(ffn_input, ffn_in_s[...]) + ffn_in_bias[...].astype(f32).reshape(1, FF)
    half_gate = 0.5 + 0.5 * lax.erf(hidden * math.sqrt(0.5))
    activated = (hidden * half_gate).astype(bf16)
    gate_s[...] = half_gate + hidden * jnp.exp(hidden * hidden * -0.5) * (1.0 / math.sqrt(2.0 * math.pi))
    load_ffn_out.wait()
    third_normed, third_rstd = norm_forward(
        second + dot(activated, ffn_out_s[...]) + ffn_out_bias[...].astype(f32).reshape(1, D)
    )
    result_out[...] = (third_normed * gain[2:3] + shift[2:3])[:NQ].astype(bf16)
    grad_third, gain_grad_2, shift_grad_2 = norm_backward(
        pad_s[2], third_normed, third_rstd, gain[2:3]
    )
    grad_branch_f = grad_third.astype(bf16)
    grad_hidden = (dot_nt(grad_branch_f, ffn_out_s[...]) * gate_s[...]).astype(bf16)
    grad_second = grad_third + dot_nt(grad_hidden, ffn_in_s[...])
    grad_second_in, gain_grad_1, shift_grad_1 = norm_backward(
        grad_second, second_normed, second_rstd, gain[1:2]
    )
    grad_branch_c = grad_second_in.astype(bf16)
    @pl.when(member == 0)
    def _():
        ffn_input_t = second.T.astype(bf16)
        for j in range(FF // D):
            rows_f[D * j : D * j + D] = dot(ffn_input_t, grad_hidden[:, D * j : D * j + D]).astype(bf16)
        rows_f[FF:ROWS_F] = dot_tn(attended_c[:, : D // 2], grad_branch_c).astype(bf16)

    @pl.when(member == 1)
    def _():
        for j in range(FF // D):
            rows_f[D * j : D * j + D] = dot_tn(activated[:, D * j : D * j + D], grad_branch_f).astype(bf16)
        rows_f[FF:ROWS_F] = dot_tn(attended_c[:, D // 2 :], grad_branch_c).astype(bf16)

    rows_f[ROWS_F:] = jnp.zeros((rows_f.shape[0] - ROWS_F, D), bf16)
    sum_f.phases[0]()
    hidden_sum = row_total(grad_hidden)
    small_s[:16] = jnp.concatenate(
        [hidden_sum[:, D * j : D * j + D] for j in range(FF // D)]
        + [
            row_total(grad_branch_f),
            row_total(grad_branch_c),
            gain_grad_2,
            shift_grad_2,
            gain_grad_1,
            shift_grad_1,
            jnp.zeros((2, D), f32),
        ],
        axis=0,
    )

    grad_attended_c = dot_nt(grad_branch_c, attn_out[1]).astype(bf16).astype(f32)
    grad_attended_t = grad_attended_c.T
    grad_xt[...] = spread_cols(grad_attended_t)
    grad_x[...] = spread_rows(grad_attended_c)
    inner = head_line(head_sums(grad_attended_t * mixed_t))
    mixed_s[...] = jnp.zeros_like(mixed_s)
    key_grads[...] = jnp.zeros_like(key_grads)

    @pl.loop(0, chunks)
    def _(i):
        rows = pl.ds(pl.multiple_of(i * CHUNK, CHUNK), CHUNK)
        key_ct = key_s[rows].T
        value_c = value_s[rows]
        grads = []
        weights = []
        for p in range(4):
            cols = pair_cols(p)
            grad_probs = dot(value_c, grad_xt[:, cols])
            probs = probs_s[rows, cols].astype(f32) * factor_s[pl.ds(i, 1), cols]
            grad_scores = (probs * (grad_probs - inner[:, cols])).astype(bf16)
            mixed_s[pair_rows(p)] += dot(key_ct[pair_rows(p)], grad_scores)
            grads.append(grad_scores)
            weights.append(probs.astype(bf16))
        grad_key = (dot(jnp.concatenate(grads, axis=1), query_x[...]) * scale).astype(bf16)
        grad_value = dot(jnp.concatenate(weights, axis=1), grad_x[...]).astype(bf16)
        key_grads[:D] += dot_tn(key_in_s[rows], grad_key)
        key_grads[D : 2 * D] += dot_tn(memory_s[rows], grad_value)
        key_grads[2 * D : 2 * D + 1] += row_total(grad_value)
        both = jnp.concatenate([grad_key, grad_value], axis=1)
        memory_s[rows] = dot(both, back_w[...]).astype(bf16)
        pltpu.make_async_copy(memory_s.at[rows], memory_grad_hbm.at[0, rows], store_sem.at[i]).start()
        for k, phase in enumerate(sum_f.phases[1:-1]):
            pl.when(i == chunks * (k + 1) // len(sum_f.phases))(phase)

    send_b[...] = own_blocks([mixed_s[pair_rows(p)] for p in range(4)]) * scale
    swap_b = pltpu.make_async_remote_copy(
        src_ref=send_b,
        dst_ref=recv_b,
        send_sem=link_sem.at[2],
        recv_sem=link_sem.at[3],
        device_id=partner,
        device_id_type=pl.DeviceIdType.MESH,
    )
    swap_b.start()
    @pl.when(member == 0)
    def _():
        send_k[:D] = key_grads[D : 2 * D].astype(bf16)
    @pl.when(member == 1)
    def _():
        send_k[:D] = key_grads[:D].astype(bf16)
    send_k[D:] = key_grads[2 * D :].astype(bf16)
    swap_k = pltpu.make_async_remote_copy(
        src_ref=send_k,
        dst_ref=recv_k,
        send_sem=link_sem.at[4],
        recv_sem=link_sem.at[5],
        device_id=partner,
        device_id_type=pl.DeviceIdType.MESH,
    )
    swap_k.start()
    swap_b.wait()
    grad_query_c = (send_b[...] + recv_b[...]).T.astype(bf16)

    cross_pos_grad = dot_nt(grad_query_c, attn_in[1, 0])
    grad_first_in, gain_grad_0, shift_grad_0 = norm_backward(
        grad_second_in + cross_pos_grad, first_normed, first_rstd, gain[0:1]
    )
    grad_branch = grad_first_in.astype(bf16)
    grad_attended = dot_nt(grad_branch, attn_out[0]).astype(bf16).astype(f32)
    grad_probs = dot(value_self, spread_cols(grad_attended.T))
    inner_self = jnp.sum(probs_self * grad_probs, axis=0, keepdims=True)
    grad_scores = (probs_self * (grad_probs - inner_self)).astype(bf16)
    key_t = key_self.astype(f32).T.astype(bf16)
    grad_query_s = (
        own_blocks([dot(key_t[pair_rows(p)], grad_scores[:, pair_cols(p)]) for p in range(4)]) * scale
    ).T.astype(bf16)
    grad_key_s = (dot(grad_scores, spread_rows(query_self.astype(f32))) * scale).astype(bf16)
    grad_value_s = dot(probs_self_b, spread_rows(grad_attended)).astype(bf16)
    grad_mixed_q = dot_nt(grad_query_s, attn_in[0, 0]) + dot_nt(grad_key_s, attn_in[0, 1])
    queries_grad_out[...] = (grad_first_in + grad_mixed_q + dot_nt(grad_value_s, attn_in[0, 2]))[
        :NQ
    ].astype(bf16)
    small_s[16:] = jnp.concatenate(
        [
            row_total(grad_query_s),
            row_total(grad_value_s),
            row_total(grad_branch),
            row_total(grad_query_c),
            gain_grad_0,
            shift_grad_0,
            jnp.zeros((10, D), f32),
        ],
        axis=0,
    )
    swap_k.wait()

    @pl.when(member == 0)
    def _():
        rows_t[:D] = dot_tn(mixed_q, grad_query_s).astype(bf16)
        rows_t[D : 2 * D] = dot_tn(mixed_q, grad_key_s).astype(bf16)
        rows_t[2 * D : 3 * D] = dot_tn(queries_b, grad_value_s).astype(bf16)
        rows_t[3 * D :] = (key_grads[:D] + recv_k[:D].astype(f32)).astype(bf16)

    @pl.when(member == 1)
    def _():
        rows_t[:D] = dot_tn(cross_q, grad_query_c).astype(bf16)
        rows_t[D : 2 * D] = dot_tn(attended, grad_branch).astype(bf16)
        rows_t[2 * D : 3 * D] = (key_grads[D : 2 * D] + recv_k[:D].astype(f32)).astype(bf16)
        rows_t[ROW_POS:ROW_SMALL] = (grad_mixed_q + cross_pos_grad).astype(bf16)
        value_bias_grad = key_grads[2 * D : 2 * D + 1] + recv_k[D : D + TILE].astype(f32)[:1]
        at_22 = lax.broadcasted_iota(jnp.int32, (32, D), 0) == 22
        rows_t[ROW_SMALL : ROW_SMALL + 32] = jnp.where(at_22, value_bias_grad, small_s[...]).astype(bf16)
        rows_t[ROW_SMALL + 32 : ROWS_T] = jnp.zeros((ROWS_T - ROW_SMALL - 32, D), bf16)

    for phase in sum_t.phases[:-1]:
        phase()
    sum_f.phases[-1]()
    store_f = pltpu.make_async_copy(whole_f, whole_f_hbm, load_sem.at[3])
    store_f.start()
    sum_t.phases[-1]()
    store_t = pltpu.make_async_copy(whole_t, whole_t_hbm, load_sem.at[4])
    store_t.start()

    @pl.loop(0, chunks)
    def _(i):
        rows = pl.ds(pl.multiple_of(i * CHUNK, CHUNK), CHUNK)
        pltpu.make_async_copy(memory_s.at[rows], memory_grad_hbm.at[0, rows], store_sem.at[i]).wait()
    store_f.wait()
    store_t.wait()


def finish_kernel(
    result_in,
    queries_grad_in,
    memory_grad_in,
    whole_f,
    whole_t,
    result,
    queries_grad,
    memory_grad,
    attn_in_grad,
    attn_out_grad,
    attn_bias_grad,
    ffn_in_grad,
    ffn_in_bias_grad,
    ffn_out_grad,
    ffn_out_bias_grad,
    norm_gain_grad,
    norm_bias_grad,
    query_pos_grad,
    sem,
):
    move = pltpu.make_async_copy(memory_grad_in, memory_grad, sem)
    move.start()
    result[0] = result_in[...]
    queries_grad[0] = queries_grad_in[...]
    for j in range(FF // D):
        ffn_in_grad[:, D * j : D * j + D] = whole_f[0, D * j : D * j + D].astype(f32)
        ffn_out_grad[D * j : D * j + D] = whole_f[1, D * j : D * j + D].astype(f32)
    attn_out_grad[0] = whole_t[1, D : 2 * D].astype(f32)
    attn_out_grad[1, : D // 2] = whole_f[0, FF:ROWS_F].astype(f32)
    attn_out_grad[1, D // 2 :] = whole_f[1, FF:ROWS_F].astype(f32)
    for j in range(3):
        attn_in_grad[0, j] = whole_t[0, D * j : D * j + D].astype(f32)
    attn_in_grad[1, 0] = whole_t[1, :D].astype(f32)
    attn_in_grad[1, 1] = whole_t[0, 3 * D : 4 * D].astype(f32)
    attn_in_grad[1, 2] = whole_t[1, 2 * D : 3 * D].astype(f32)
    query_pos_grad[...] = whole_t[1, ROW_POS:ROW_SMALL].astype(f32)[:NQ]
    small = whole_t[1, ROW_SMALL : ROW_SMALL + 32].astype(f32)
    ffn_in_bias_grad[...] = jnp.concatenate([small[j : j + 1] for j in range(FF // D)], axis=1)
    ffn_out_bias_grad[...] = small[8:9]
    attn_bias_grad[0] = small[16:19]
    attn_bias_grad[1, 0:1] = small[19:20]
    attn_bias_grad[1, 1:2] = small[22:23]
    attn_bias_grad[1, 2:3] = small[9:10]
    norm_gain_grad[0:1] = small[20:21]
    norm_gain_grad[1:2] = small[12:13]
    norm_gain_grad[2:3] = small[10:11]
    norm_bias_grad[0:1] = small[21:22]
    norm_bias_grad[1:2] = small[13:14]
    norm_bias_grad[2:3] = small[11:12]
    move.wait()


def body(
    pages,
    queries,
    memory,
    quarter_turns,
    token_order,
    lengths,
    attn_in,
    attn_out,
    attn_bias,
    ffn_in,
    ffn_in_bias,
    ffn_out,
    ffn_out_bias,
    norm_gain,
    norm_bias,
    query_pos,
    out_grad,
):
    tokens = memory.shape[1]
    chunks = tokens // CHUNK
    rows_f = padded(ROWS_F, pages)
    rows_t = padded(ROWS_T, pages)
    copies = PageSum.copies(pages)
    vmem = pl.BlockSpec(memory_space=pltpu.VMEM)
    smem = pl.BlockSpec(memory_space=pltpu.SMEM)
    anywhere = pl.BlockSpec(memory_space=pl.ANY)
    parts = pl.pallas_call(
        functools.partial(layer_kernel, tokens, pages),
        out_shape=[
            jax.ShapeDtypeStruct((NQ, D), bf16),
            jax.ShapeDtypeStruct((NQ, D), bf16),
            jax.ShapeDtypeStruct((1, tokens, D), bf16),
            jax.ShapeDtypeStruct((2, rows_f, D), bf16),
            jax.ShapeDtypeStruct((2, rows_t, D), bf16),
        ],
        in_specs=[
            vmem,
            anywhere,
            smem,
            vmem,
            smem,
            vmem,
            vmem,
            vmem,
            anywhere,
            vmem,
            anywhere,
            vmem,
            vmem,
            vmem,
            vmem,
            vmem,
            vmem,
        ],
        out_specs=[vmem, vmem, anywhere, anywhere, anywhere],
        scratch_shapes=[
            pltpu.VMEM((tokens, D), bf16),
            pltpu.VMEM((tokens, D), bf16),
            pltpu.VMEM((tokens, D), bf16),
            pltpu.VMEM((tokens, D), bf16),
            pltpu.VMEM((tokens, NP), bf16),
            pltpu.VMEM((tokens, HQ), bf16),
            pltpu.VMEM((1, tokens), f32),
            pltpu.VMEM((CHUNK, HQ), f32),
            pltpu.VMEM((CHUNK, HQ), f32),
            pltpu.VMEM((2, D, HQ // 2), bf16),
            pltpu.VMEM((2, 2 * SIDE, D), bf16),
            pltpu.VMEM((chunks, HQ), f32),
            pltpu.VMEM((chunks, HQ), f32),
            pltpu.VMEM((8, HQ), f32),
            pltpu.VMEM((D, PAIR), f32),
            pltpu.VMEM((D, FF), bf16),
            pltpu.VMEM((FF, D), bf16),
            pltpu.VMEM((NP, FF), f32),
            pltpu.VMEM((3, NP, D), f32),
            pltpu.VMEM((2 * D, D), bf16),
            pltpu.VMEM((HQ, D), bf16),
            pltpu.VMEM((D, HQ), bf16),
            pltpu.VMEM((HQ, D), bf16),
            pltpu.VMEM((D + 2 * HEADS, NP), f32),
            pltpu.VMEM((D + 2 * HEADS, NP), f32),
            pltpu.VMEM((D, NP), f32),
            pltpu.VMEM((D, NP), f32),
            pltpu.VMEM((2 * D + TILE, D), f32),
            pltpu.VMEM((D + TILE, D), bf16),
            pltpu.VMEM((D + TILE, D), bf16),
            pltpu.VMEM((32, D), f32),
            pltpu.VMEM((rows_f, D), bf16),
            pltpu.VMEM((PageSum.landing_rows(pages, rows_f), D), bf16),
            pltpu.VMEM((2, rows_f, D), bf16),
            pltpu.VMEM((rows_t, D), bf16),
            pltpu.VMEM((PageSum.landing_rows(pages, rows_t), D), bf16),
            pltpu.VMEM((2, rows_t, D), bf16),
            pltpu.SemaphoreType.DMA((5,)),
            pltpu.SemaphoreType.DMA((chunks,)),
            pltpu.SemaphoreType.DMA((6,)),
            pltpu.SemaphoreType.DMA((copies,)),
            pltpu.SemaphoreType.DMA((copies,)),
            pltpu.SemaphoreType.DMA((copies,)),
            pltpu.SemaphoreType.DMA((copies,)),
        ],
        compiler_params=pltpu.CompilerParams(
            collective_id=0, has_side_effects=True, vmem_limit_bytes=62 * 1024 * 1024
        ),
        cost_estimate=pl.CostEstimate(
            flops=2 * 8 * tokens * HQ * D, bytes_accessed=20 << 20, transcendentals=tokens * HQ
        ),
        name="decoder_layer",
    )(
        queries,
        memory,
        quarter_turns,
        token_order,
        lengths,
        attn_in,
        attn_out,
        attn_bias,
        ffn_in,
        ffn_in_bias,
        ffn_out,
        ffn_out_bias,
        norm_gain,
        norm_bias,
        query_pos,
        out_grad,
        jnp.asarray(position_table()),
    )
    outs = pl.pallas_call(
        finish_kernel,
        out_shape=[
            jax.ShapeDtypeStruct((1, NQ, D), bf16),
            jax.ShapeDtypeStruct((1, NQ, D), bf16),
            jax.ShapeDtypeStruct((1, tokens, D), bf16),
            jax.ShapeDtypeStruct((2, 3, D, D), f32),
            jax.ShapeDtypeStruct((2, D, D), f32),
            jax.ShapeDtypeStruct((2, 3, D), f32),
            jax.ShapeDtypeStruct((D, FF), f32),
            jax.ShapeDtypeStruct((1, FF), f32),
            jax.ShapeDtypeStruct((FF, D), f32),
            jax.ShapeDtypeStruct((1, D), f32),
            jax.ShapeDtypeStruct((3, D), f32),
            jax.ShapeDtypeStruct((3, D), f32),
            jax.ShapeDtypeStruct((NQ, D), f32),
        ],
        in_specs=[vmem, vmem, anywhere, vmem, vmem],
        out_specs=[vmem, vmem, anywhere] + [vmem] * 10,
        scratch_shapes=[pltpu.SemaphoreType.DMA],
        compiler_params=pltpu.CompilerParams(vmem_limit_bytes=62 * 1024 * 1024),
        name="write_outputs",
    )(*parts)
    return (*outs[:7], outs[7].reshape(FF), outs[8], outs[9].reshape(D), *outs[10:])


def solution(mesh):
    in_specs = (
        P("dp", None, None),
        P("dp", "blk", None),
        P("dp"),
        P("dp", "blk"),
        P("dp"),
        P(),
        P(),
        P(),
        P(),
        P(),
        P(),
        P(),
        P(),
        P(),
        P(),
        P("dp", None, None),
    )
    out_specs = (
        P("dp", None, None),
        P("dp", None, None),
        P("dp", "blk", None),
        P(),
        P(),
        P(),
        P(),
        P(),
        P(),
        P(),
        P(),
        P(),
        P(),
    )
    layer = functools.partial(body, mesh.shape["dp"])
    return jax.shard_map(layer, mesh=mesh, in_specs=in_specs, out_specs=out_specs, check_vma=False)
```

```python
import functools
import math

import jax
import jax.numpy as jnp
import numpy as np
from jax import lax
from jax.experimental import pallas as pl
from jax.experimental.pallas import tpu as pltpu
from jax.sharding import PartitionSpec as P

D = 256
HEADS = 8
HD = D // HEADS
SIDE = 128
NQ = 125
NP = 128
HQ = HEADS * NP
PAIR = 2 * NP
FF = 2048
CHUNK = 512

masked_score = -1e30
norm_eps = 1e-05
scale = 1.0 / math.sqrt(HD)
log2e = math.log2(math.e)

bf16 = jnp.bfloat16
f32 = jnp.float32

ROWS_F = FF + D // 2
ROW_POS = 3 * D
ROW_SMALL = 3 * D + NP
ROWS_T = 4 * D
TILE = 16


def digits_of(pages):
    digits = [(2, 1), (2, 2)]
    stride = 4
    while stride < pages:
        radix = 4 if pages // stride % 4 == 0 else 2
        digits.append((radix, stride))
        stride *= radix
    return digits


def padded(rows, pages):
    unit = TILE * pages
    return (rows + unit - 1) // unit * unit


def position_table():
    half = D // 2
    channel = np.arange(half)
    inverse = np.exp((channel // 2).astype(np.float32) * np.float32(-2.0 * math.log(10000.0) / half))
    angle = (np.arange(SIDE, dtype=np.float32) + 1.0) * np.float32(2.0 * math.pi / SIDE)
    angle = angle[:, None] * inverse
    return np.where(channel % 2 == 0, np.sin(angle), np.cos(angle)).astype(np.float32)


def dot(a, b):
    return jnp.dot(a, b, preferred_element_type=f32)


def dot_nt(a, b):
    return lax.dot_general(a, b, (((1,), (1,)), ((), ())), preferred_element_type=f32)


def dot_tn(a, b):
    return lax.dot_general(a, b, (((0,), (0,)), ((), ())), preferred_element_type=f32)


def row_total(values):
    return jnp.sum(values.astype(f32), axis=0, keepdims=True)


def norm_forward(values):
    average = jnp.mean(values, axis=-1, keepdims=True)
    centred = values - average
    variance = jnp.mean(centred * centred, axis=-1, keepdims=True)
    rstd = lax.rsqrt(variance + norm_eps)
    return centred * rstd, rstd


def norm_backward(grad, normed, rstd, gain):
    grad_normed = grad * gain
    first = jnp.mean(grad_normed, axis=-1, keepdims=True)
    second = jnp.mean(grad_normed * normed, axis=-1, keepdims=True)
    grad_in = rstd * (grad_normed - first - normed * second)
    return grad_in, row_total(grad * normed), row_total(grad)


def spread_rows(rows):
    head = lax.broadcasted_iota(jnp.int32, (NP, D), 1) // HD
    return jnp.concatenate(
        [jnp.where(head == h, rows, 0.0) for h in range(HEADS)], axis=0
    ).astype(bf16)


def spread_cols(cols):
    head = lax.broadcasted_iota(jnp.int32, (D, NP), 0) // HD
    return jnp.concatenate(
        [jnp.where(head == h, cols, 0.0) for h in range(HEADS)], axis=1
    ).astype(bf16)


def own_blocks(pairs):
    parts = []
    for pair in pairs:
        parts += [pair[:HD, :NP], pair[HD:, NP:]]
    return jnp.concatenate(parts, axis=0)


def head_rows(row):
    return jnp.concatenate([row[:, NP * h : NP * h + NP] for h in range(HEADS)], axis=0)


def head_line(rows):
    return jnp.concatenate([rows[h : h + 1] for h in range(HEADS)], axis=1)


def per_channel(rows):
    return jnp.concatenate(
        [jnp.broadcast_to(rows[h : h + 1], (HD, NP)) for h in range(HEADS)], axis=0
    )


def head_sums(cols):
    return jnp.concatenate(
        [jnp.sum(cols[HD * h : HD * h + HD], axis=0, keepdims=True) for h in range(HEADS)], axis=0
    )


def pair_cols(p):
    return slice(PAIR * p, PAIR * p + PAIR)


def pair_rows(p):
    return slice(2 * HD * p, 2 * HD * p + 2 * HD)


class PageSum:
    def __init__(self, pages, rows, landing, whole, sent, arrived):
        self.rows, self.landing, self.whole = rows, landing, whole
        self.sent, self.arrived = sent, arrived
        self.page = lax.axis_index("dp")
        self.member = lax.axis_index("blk")
        self.digits = digits_of(pages)
        self.extents = [rows.shape[0]]
        self.bases = [0]
        self.slots = []
        self.places = []
        slot = 0
        place = 0
        for radix, stride in self.digits:
            digit = self.page // stride % radix
            extent = self.extents[-1] // radix
            self.slots.append(slot)
            self.places.append(place)
            slot += radix - 1
            place += (radix - 1) * extent
            self.bases.append(pl.multiple_of(self.bases[-1] + digit * extent, TILE))
            self.extents.append(extent)
        self.gather_slot = slot
        self.last = len(self.digits)
        self.phases = [self.scatter_phase(s) for s in range(self.last)]
        self.phases.append(self.owned_phase)
        for s in range(self.last - 1, 2, -1):
            self.phases.append(self.spread_phase(s))
        self.phases += [self.sides_phase, self.corners_phase, self.core_phase, self.end_phase]

    @staticmethod
    def landing_rows(pages, rows):
        total, extent = 0, rows
        for radix, _ in digits_of(pages):
            extent //= radix
            total += (radix - 1) * extent
        return total

    @staticmethod
    def copies(pages):
        return sum(radix - 1 for radix, _ in digits_of(pages)) * 2 + 6

    def peer(self, step, hop):
        radix, stride = self.digits[step]
        digit = self.page // stride % radix
        other = lax.rem(digit + hop, radix)
        return (self.page + (other - digit) * stride, self.member), other

    def copy(self, slot, source, target, device):
        return pltpu.make_async_remote_copy(
            src_ref=source,
            dst_ref=target,
            send_sem=self.sent.at[slot],
            recv_sem=self.arrived.at[slot],
            device_id=device,
            device_id_type=pl.DeviceIdType.MESH,
        )

    def scatter_copies(self, step):
        radix, _ = self.digits[step]
        extent = self.extents[step + 1]
        for hop in range(1, radix):
            device, other = self.peer(step, hop)
            start = pl.multiple_of(self.bases[step] + other * extent, TILE)
            place = self.places[step] + (hop - 1) * extent
            yield self.copy(
                self.slots[step] + hop - 1,
                self.rows.at[pl.ds(start, extent)],
                self.landing.at[pl.ds(place, extent)],
                device,
            )

    def scatter_sum(self, step):
        radix, _ = self.digits[step]
        extent = self.extents[step + 1]
        total = self.rows[pl.ds(self.bases[step + 1], extent)].astype(f32)
        for hop in range(1, radix):
            place = self.places[step] + (hop - 1) * extent
            total = total + self.landing[pl.ds(place, extent)].astype(f32)
        return total.astype(bf16)

    def scatter_phase(self, step):
        def run():
            if step > 0:
                self.finish(self.scatter_copies(step - 1))
                self.rows[pl.ds(self.bases[step], self.extents[step])] = self.scatter_sum(step - 1)
            self.begin(self.scatter_copies(step))

        return run

    def gather_copies(self, step):
        radix, _ = self.digits[step]
        place = self.whole.at[self.member, pl.ds(self.bases[step + 1], self.extents[step + 1])]
        for hop in range(1, radix):
            device, _ = self.peer(step, hop)
            yield self.copy(self.gather_slot + self.slots[step] + hop - 1, place, place, device)

    def side_copies(self):
        slot = self.gather_slot + self.slots[1]
        beside, other = self.peer(1, 1)
        across = (self.page, 1 - self.member)
        extent = self.extents[2]
        place = self.whole.at[self.member, pl.ds(self.bases[2], extent)]
        extra = self.gather_slot * 2
        yield self.copy(slot, place, place, beside)
        yield self.copy(extra, place, place, across)

    def corner_copies(self):
        beside, other = self.peer(1, 1)
        across = (self.page, 1 - self.member)
        half = self.extents[2] // 2
        core_base = self.bases[1]
        side_base = pl.multiple_of(core_base + other * self.extents[2], TILE)
        first = self.whole.at[self.member, pl.ds(side_base, half)]
        second = self.whole.at[1 - self.member, pl.ds(pl.multiple_of(self.bases[2] + half, TILE), half)]
        extra = self.gather_slot * 2
        yield self.copy(extra + 1, first, first, across)
        yield self.copy(extra + 2, second, second, beside)

    def core_copies(self):
        device, _ = self.peer(0, 1)
        for m in range(2):
            place = self.whole.at[m, pl.ds(self.bases[1], self.extents[1])]
            yield self.copy(self.gather_slot * 2 + 3 + m, place, place, device)

    def begin(self, copies):
        for copy in copies:
            copy.start()

    def finish(self, copies):
        for copy in copies:
            copy.wait()

    def owned_phase(self):
        self.finish(self.scatter_copies(self.last - 1))
        self.whole[self.member, pl.ds(self.bases[self.last], self.extents[self.last])] = self.scatter_sum(
            self.last - 1
        )
        self.begin(self.gather_copies(self.last - 1))

    def spread_phase(self, step):
        def run():
            self.finish(self.gather_copies(step))
            self.begin(self.gather_copies(step - 1))

        return run

    def sides_phase(self):
        self.finish(self.gather_copies(2))
        self.begin(self.side_copies())

    def corners_phase(self):
        self.finish(self.side_copies())
        self.begin(self.corner_copies())

    def core_phase(self):
        self.finish(self.corner_copies())
        self.begin(self.core_copies())

    def end_phase(self):
        self.finish(self.core_copies())


def layer_kernel(
    tokens,
    pages,
    queries_in,
    memory_hbm,
    turns_in,
    order_in,
    lengths_in,
    attn_in,
    attn_out,
    attn_bias,
    ffn_in_hbm,
    ffn_in_bias,
    ffn_out_hbm,
    ffn_out_bias,
    norm_gain,
    norm_bias,
    pos_in,
    out_grad_in,
    table_in,
    result_out,
    queries_grad_out,
    memory_grad_hbm,
    whole_f_hbm,
    whole_t_hbm,
    memory_s,
    key_in_s,
    key_s,
    value_s,
    aux_s,
    probs_s,
    code_s,
    score_a,
    score_b,
    weight_s,
    table_s,
    shifts_s,
    factor_s,
    total_s,
    mixed_s,
    ffn_in_s,
    ffn_out_s,
    gate_s,
    pad_s,
    back_w,
    query_x,
    grad_xt,
    grad_x,
    send_a,
    recv_a,
    send_b,
    recv_b,
    key_grads,
    send_k,
    recv_k,
    small_s,
    rows_f,
    landing_f,
    whole_f,
    rows_t,
    landing_t,
    whole_t,
    load_sem,
    store_sem,
    link_sem,
    sent_f,
    arrived_f,
    sent_t,
    arrived_t,
):
    member = lax.axis_index("blk")
    partner = (lax.axis_index("dp"), 1 - member)
    chunks = tokens // CHUNK

    sum_f = PageSum(pages, rows_f, landing_f, whole_f, sent_f, arrived_f)
    sum_t = PageSum(pages, rows_t, landing_t, whole_t, sent_t, arrived_t)

    barrier = pltpu.get_barrier_semaphore()
    peers = [partner]
    for step, (radix, _) in enumerate(sum_f.digits):
        peers += [sum_f.peer(step, hop)[0] for hop in range(1, radix)]
    for peer in peers:
        pl.semaphore_signal(barrier, inc=1, device_id=peer, device_id_type=pl.DeviceIdType.MESH)

    load_memory = pltpu.make_async_copy(memory_hbm.at[0], memory_s, load_sem.at[0])
    load_ffn_in = pltpu.make_async_copy(ffn_in_hbm, ffn_in_s, load_sem.at[1])
    load_ffn_out = pltpu.make_async_copy(ffn_out_hbm, ffn_out_s, load_sem.at[2])
    load_memory.start()
    load_ffn_in.start()
    load_ffn_out.start()

    pairs = [attn_bias[j].astype(f32) for j in range(3)]
    bias = jnp.concatenate([pair[k : k + 1] for k in range(2) for pair in pairs], axis=0)
    gain = norm_gain[...].astype(f32)
    shift = norm_bias[...].astype(f32)

    order = order_in[...]
    turn = turns_in[0]
    row_at = order >> 7
    col_at = order & 127
    top = SIDE - 1
    row_new = jnp.where(
        turn == 0, row_at, jnp.where(turn == 1, col_at, jnp.where(turn == 2, top - row_at, top - col_at))
    )
    col_new = jnp.where(
        turn == 0, col_at, jnp.where(turn == 1, top - row_at, jnp.where(turn == 2, top - col_at, row_at))
    )
    past = jnp.where(order < lengths_in[0], 0, SIDE * SIDE)
    code_s[...] = (row_new * SIDE + col_new + past).astype(f32)

    pad_s[...] = jnp.zeros_like(pad_s)
    pad_s[0, :NQ] = queries_in[0].astype(f32)
    pad_s[1, :NQ] = pos_in[...].astype(f32)
    pad_s[2, :NQ] = out_grad_in[0].astype(f32)
    queries_f = pad_s[0]
    pos_f = pad_s[1]
    queries_b = queries_f.astype(bf16)
    mixed_q = (queries_f + pos_f).astype(bf16)
    query_self = (dot(mixed_q, attn_in[0, 0]) + bias[0:1]).astype(bf16)
    key_self = dot(mixed_q, attn_in[0, 1]).astype(bf16)
    value_self = (dot(queries_b, attn_in[0, 2]) + bias[1:2]).astype(bf16)
    scores = dot(key_self, spread_cols(query_self.astype(f32).T)) * scale
    own_key = lax.broadcasted_iota(jnp.int32, (NP, HQ), 0) < NQ
    scores = jnp.where(own_key, scores, masked_score)
    raised = jnp.exp(scores - jnp.max(scores, axis=0, keepdims=True))
    probs_self = raised / jnp.sum(raised, axis=0, keepdims=True)
    probs_self_b = probs_self.astype(bf16)
    value_t = value_self.astype(f32).T.astype(bf16)
    attended = own_blocks(
        [dot(value_t[pair_rows(p)], probs_self_b[:, pair_cols(p)]) for p in range(4)]
    ).T.astype(bf16)
    first_normed, first_rstd = norm_forward(queries_f + dot(attended, attn_out[0]) + bias[2:3])
    first = first_normed * gain[0:1] + shift[0:1]
    cross_q = (first + pos_f).astype(bf16)
    query_c = (dot(cross_q, attn_in[1, 0]) + bias[3:4]).astype(bf16)
    query_x[...] = spread_rows(query_c.astype(f32))
    query_xt = spread_cols(query_c.astype(f32).T)
    aux_row = jnp.where(
        lax.broadcasted_iota(jnp.int32, (NP, HQ // 2), 0) == 0, 1.0, 0.0
    ).astype(bf16)
    for g in range(2):
        weight_s[g, :NP] = query_xt[NP * g : NP * g + NP, HQ // 2 * g : HQ // 2 * (g + 1)]
        weight_s[g, NP:] = aux_row
    back_w[:D] = attn_in[1, 1].astype(f32).T.astype(bf16)
    back_w[D:] = attn_in[1, 2].astype(f32).T.astype(bf16)

    table = table_in[...]
    nothing = jnp.zeros((SIDE, D // 2), f32)
    table = jnp.concatenate(
        [jnp.concatenate([table, nothing], axis=1), jnp.concatenate([nothing, table], axis=1)], axis=0
    )
    table_high = table.astype(bf16)
    table_s[0] = table_high
    table_s[1] = (table - table_high.astype(f32)).astype(bf16)

    load_memory.wait()
    lane = lax.broadcasted_iota(jnp.int32, (CHUNK, NP), 1)
    value_bias = bias[4:5]

    @pl.loop(0, chunks)
    def _(i):
        rows = pl.ds(pl.multiple_of(i * CHUNK, CHUNK), CHUNK)
        line = code_s[:, rows]
        code = jnp.concatenate(
            [
                jnp.broadcast_to(line[:, NP * j : NP * j + NP], (NP, NP)).T
                for j in range(CHUNK // NP)
            ],
            axis=0,
        ).astype(jnp.int32)
        row_hot = jnp.where(((code >> 7) & 127) == lane, 1.0, 0.0)
        col_hot = jnp.where((code & 127) == lane, 1.0, 0.0)
        hot = jnp.concatenate([row_hot, col_hot], axis=1).astype(bf16)
        aux_s[rows] = jnp.where((code >= SIDE * SIDE) & (lane == 0), masked_score, 0.0).astype(bf16)
        block = memory_s[rows]
        positions = dot(hot, table_s[0]) + dot(hot, table_s[1])
        key_in = (block.astype(f32) + positions).astype(bf16)
        key_in_s[rows] = key_in
        key_s[rows] = dot(key_in, attn_in[1, 1]).astype(bf16)
        value_s[rows] = (dot(block, attn_in[1, 2]) + value_bias).astype(bf16)

    def score_chunk(i, out):
        rows = pl.ds(pl.multiple_of(i * CHUNK, CHUNK), CHUNK)
        for g in range(2):
            left = jnp.concatenate([key_s[rows, NP * g : NP * g + NP], aux_s[rows]], axis=1)
            out[:, HQ // 2 * g : HQ // 2 * (g + 1)] = dot(left, weight_s[g])

    def attend_chunk(i, scored):
        rows = pl.ds(pl.multiple_of(i * CHUNK, CHUNK), CHUNK)
        value_ct = value_s[rows].T
        for p in range(4):
            cols = pair_cols(p)
            before = total_s[0:1, cols]
            part = scored[:, cols]
            highest = jnp.maximum(
                before, jnp.max(part, axis=0, keepdims=True) * (scale * log2e)
            )
            raised = jnp.exp2(part * (scale * log2e) - highest)
            fade = jnp.exp2(before - highest)
            total_s[0:1, cols] = highest
            total_s[1:2, cols] = total_s[1:2, cols] * fade + jnp.sum(raised, axis=0, keepdims=True)
            shifts_s[pl.ds(i, 1), cols] = highest
            raised_b = raised.astype(bf16)
            probs_s[rows, cols] = raised_b
            mixed_s[pair_rows(p)] = mixed_s[pair_rows(p)] * fade + dot(
                value_ct[pair_rows(p)], raised_b
            )

    total_s[0:1] = jnp.full((1, HQ), -3e38, f32)
    total_s[1:2] = jnp.zeros((1, HQ), f32)
    mixed_s[...] = jnp.zeros_like(mixed_s)
    score_chunk(0, score_a)

    @pl.loop(0, chunks // 2)
    def _(j):
        i = j * 2
        score_chunk(i + 1, score_b)
        attend_chunk(i, score_a)
        score_chunk(jnp.minimum(i + 2, chunks - 1), score_a)
        attend_chunk(i + 1, score_b)

    send_a[:D] = own_blocks([mixed_s[pair_rows(p)] for p in range(4)])
    send_a[D : D + HEADS] = head_rows(total_s[0:1])
    send_a[D + HEADS :] = head_rows(total_s[1:2])
    pl.semaphore_wait(barrier, len(peers))
    swap_a = pltpu.make_async_remote_copy(
        src_ref=send_a,
        dst_ref=recv_a,
        send_sem=link_sem.at[0],
        recv_sem=link_sem.at[1],
        device_id=partner,
        device_id_type=pl.DeviceIdType.MESH,
    )
    swap_a.start()
    swap_a.wait()
    is_first = member == 0
    own = send_a[...]
    other = recv_a[...]
    left = jnp.where(is_first, own, other)
    right = jnp.where(is_first, other, own)
    high_l, high_r = left[D : D + HEADS], right[D : D + HEADS]
    highest = jnp.maximum(high_l, high_r)
    fade_l = jnp.exp2(high_l - highest)
    fade_r = jnp.exp2(high_r - highest)
    total = left[D + HEADS :] * fade_l + right[D + HEADS :] * fade_r
    mixed_t = left[:D] * per_channel(fade_l / total) + right[:D] * per_channel(fade_r / total)
    log_total = head_line(highest + jnp.log2(total))
    factor_s[...] = jnp.exp2(shifts_s[...] - log_total)
    attended_c = mixed_t.T.astype(bf16)

    second_normed, second_rstd = norm_forward(first + dot(attended_c, attn_out[1]) + bias[5:6])
    second = second_normed * gain[1:2] + shift[1:2]
    ffn_input = second.astype(bf16)
    load_ffn_in.wait()
    hidden = dot(ffn_input, ffn_in_s[...]) + ffn_in_bias[...].astype(f32).reshape(1, FF)
    half_gate = 0.5 + 0.5 * lax.erf(hidden * math.sqrt(0.5))
    activated = (hidden * half_gate).astype(bf16)
    gate_s[...] = half_gate + hidden * jnp.exp(hidden * hidden * -0.5) * (1.0 / math.sqrt(2.0 * math.pi))
    load_ffn_out.wait()
    third_normed, third_rstd = norm_forward(
        second + dot(activated, ffn_out_s[...]) + ffn_out_bias[...].astype(f32).reshape(1, D)
    )
    result_out[...] = (third_normed * gain[2:3] + shift[2:3])[:NQ].astype(bf16)
    grad_third, gain_grad_2, shift_grad_2 = norm_backward(
        pad_s[2], third_normed, third_rstd, gain[2:3]
    )
    grad_branch_f = grad_third.astype(bf16)
    grad_hidden = (dot_nt(grad_branch_f, ffn_out_s[...]) * gate_s[...]).astype(bf16)
    grad_second = grad_third + dot_nt(grad_hidden, ffn_in_s[...])
    grad_second_in, gain_grad_1, shift_grad_1 = norm_backward(
        grad_second, second_normed, second_rstd, gain[1:2]
    )
    grad_branch_c = grad_second_in.astype(bf16)
    @pl.when(member == 0)
    def _():
        ffn_input_t = second.T.astype(bf16)
        for j in range(FF // D):
            rows_f[D * j : D * j + D] = dot(ffn_input_t, grad_hidden[:, D * j : D * j + D]).astype(bf16)
        rows_f[FF:ROWS_F] = dot_tn(attended_c[:, : D // 2], grad_branch_c).astype(bf16)

    @pl.when(member == 1)
    def _():
        for j in range(FF // D):
            rows_f[D * j : D * j + D] = dot_tn(activated[:, D * j : D * j + D], grad_branch_f).astype(bf16)
        rows_f[FF:ROWS_F] = dot_tn(attended_c[:, D // 2 :], grad_branch_c).astype(bf16)

    rows_f[ROWS_F:] = jnp.zeros((rows_f.shape[0] - ROWS_F, D), bf16)
    sum_f.phases[0]()
    hidden_sum = row_total(grad_hidden)
    small_s[:16] = jnp.concatenate(
        [hidden_sum[:, D * j : D * j + D] for j in range(FF // D)]
        + [
            row_total(grad_branch_f),
            row_total(grad_branch_c),
            gain_grad_2,
            shift_grad_2,
            gain_grad_1,
            shift_grad_1,
            jnp.zeros((2, D), f32),
        ],
        axis=0,
    )

    grad_attended_c = dot_nt(grad_branch_c, attn_out[1]).astype(bf16).astype(f32)
    grad_attended_t = grad_attended_c.T
    grad_xt[...] = spread_cols(grad_attended_t)
    grad_x[...] = spread_rows(grad_attended_c)
    inner = head_line(head_sums(grad_attended_t * mixed_t))
    mixed_s[...] = jnp.zeros_like(mixed_s)
    key_grads[...] = jnp.zeros_like(key_grads)

    @pl.loop(0, chunks)
    def _(i):
        rows = pl.ds(pl.multiple_of(i * CHUNK, CHUNK), CHUNK)
        key_ct = key_s[rows].T
        value_c = value_s[rows]
        grads = []
        weights = []
        for p in range(4):
            cols = pair_cols(p)
            grad_probs = dot(value_c, grad_xt[:, cols])
            probs = probs_s[rows, cols].astype(f32) * factor_s[pl.ds(i, 1), cols]
            grad_scores = (probs * (grad_probs - inner[:, cols])).astype(bf16)
            mixed_s[pair_rows(p)] += dot(key_ct[pair_rows(p)], grad_scores)
            grads.append(grad_scores)
            weights.append(probs.astype(bf16))
        grad_key = (dot(jnp.concatenate(grads, axis=1), query_x[...]) * scale).astype(bf16)
        grad_value = dot(jnp.concatenate(weights, axis=1), grad_x[...]).astype(bf16)
        key_grads[:D] += dot_tn(key_in_s[rows], grad_key)
        key_grads[D : 2 * D] += dot_tn(memory_s[rows], grad_value)
        key_grads[2 * D : 2 * D + 1] += row_total(grad_value)
        both = jnp.concatenate([grad_key, grad_value], axis=1)
        memory_s[rows] = dot(both, back_w[...]).astype(bf16)
        pltpu.make_async_copy(memory_s.at[rows], memory_grad_hbm.at[0, rows], store_sem.at[i]).start()
        for k, phase in enumerate(sum_f.phases[1:-1]):
            pl.when(i == chunks * (k + 1) // len(sum_f.phases))(phase)

    send_b[...] = own_blocks([mixed_s[pair_rows(p)] for p in range(4)]) * scale
    swap_b = pltpu.make_async_remote_copy(
        src_ref=send_b,
        dst_ref=recv_b,
        send_sem=link_sem.at[2],
        recv_sem=link_sem.at[3],
        device_id=partner,
        device_id_type=pl.DeviceIdType.MESH,
    )
    swap_b.start()
    @pl.when(member == 0)
    def _():
        send_k[:D] = key_grads[D : 2 * D].astype(bf16)
    @pl.when(member == 1)
    def _():
        send_k[:D] = key_grads[:D].astype(bf16)
    send_k[D:] = key_grads[2 * D :].astype(bf16)
    swap_k = pltpu.make_async_remote_copy(
        src_ref=send_k,
        dst_ref=recv_k,
        send_sem=link_sem.at[4],
        recv_sem=link_sem.at[5],
        device_id=partner,
        device_id_type=pl.DeviceIdType.MESH,
    )
    swap_k.start()
    swap_b.wait()
    grad_query_c = (send_b[...] + recv_b[...]).T.astype(bf16)

    cross_pos_grad = dot_nt(grad_query_c, attn_in[1, 0])
    grad_first_in, gain_grad_0, shift_grad_0 = norm_backward(
        grad_second_in + cross_pos_grad, first_normed, first_rstd, gain[0:1]
    )
    grad_branch = grad_first_in.astype(bf16)
    grad_attended = dot_nt(grad_branch, attn_out[0]).astype(bf16).astype(f32)
    grad_probs = dot(value_self, spread_cols(grad_attended.T))
    inner_self = jnp.sum(probs_self * grad_probs, axis=0, keepdims=True)
    grad_scores = (probs_self * (grad_probs - inner_self)).astype(bf16)
    key_t = key_self.astype(f32).T.astype(bf16)
    grad_query_s = (
        own_blocks([dot(key_t[pair_rows(p)], grad_scores[:, pair_cols(p)]) for p in range(4)]) * scale
    ).T.astype(bf16)
    grad_key_s = (dot(grad_scores, spread_rows(query_self.astype(f32))) * scale).astype(bf16)
    grad_value_s = dot(probs_self_b, spread_rows(grad_attended)).astype(bf16)
    grad_mixed_q = dot_nt(grad_query_s, attn_in[0, 0]) + dot_nt(grad_key_s, attn_in[0, 1])
    queries_grad_out[...] = (grad_first_in + grad_mixed_q + dot_nt(grad_value_s, attn_in[0, 2]))[
        :NQ
    ].astype(bf16)
    small_s[16:] = jnp.concatenate(
        [
            row_total(grad_query_s),
            row_total(grad_value_s),
            row_total(grad_branch),
            row_total(grad_query_c),
            gain_grad_0,
            shift_grad_0,
            jnp.zeros((10, D), f32),
        ],
        axis=0,
    )
    swap_k.wait()

    @pl.when(member == 0)
    def _():
        rows_t[:D] = dot_tn(mixed_q, grad_query_s).astype(bf16)
        rows_t[D : 2 * D] = dot_tn(mixed_q, grad_key_s).astype(bf16)
        rows_t[2 * D : 3 * D] = dot_tn(queries_b, grad_value_s).astype(bf16)
        rows_t[3 * D :] = (key_grads[:D] + recv_k[:D].astype(f32)).astype(bf16)

    @pl.when(member == 1)
    def _():
        rows_t[:D] = dot_tn(cross_q, grad_query_c).astype(bf16)
        rows_t[D : 2 * D] = dot_tn(attended, grad_branch).astype(bf16)
        rows_t[2 * D : 3 * D] = (key_grads[D : 2 * D] + recv_k[:D].astype(f32)).astype(bf16)
        rows_t[ROW_POS:ROW_SMALL] = (grad_mixed_q + cross_pos_grad).astype(bf16)
        value_bias_grad = key_grads[2 * D : 2 * D + 1] + recv_k[D : D + TILE].astype(f32)[:1]
        at_22 = lax.broadcasted_iota(jnp.int32, (32, D), 0) == 22
        rows_t[ROW_SMALL : ROW_SMALL + 32] = jnp.where(at_22, value_bias_grad, small_s[...]).astype(bf16)
        rows_t[ROW_SMALL + 32 : ROWS_T] = jnp.zeros((ROWS_T - ROW_SMALL - 32, D), bf16)

    for phase in sum_t.phases[:-1]:
        phase()
    sum_f.phases[-1]()
    store_f = pltpu.make_async_copy(whole_f, whole_f_hbm, load_sem.at[3])
    store_f.start()
    sum_t.phases[-1]()
    store_t = pltpu.make_async_copy(whole_t, whole_t_hbm, load_sem.at[4])
    store_t.start()

    @pl.loop(0, chunks)
    def _(i):
        rows = pl.ds(pl.multiple_of(i * CHUNK, CHUNK), CHUNK)
        pltpu.make_async_copy(memory_s.at[rows], memory_grad_hbm.at[0, rows], store_sem.at[i]).wait()
    store_f.wait()
    store_t.wait()


def finish_kernel(
    result_in,
    queries_grad_in,
    memory_grad_in,
    whole_f,
    whole_t,
    result,
    queries_grad,
    memory_grad,
    attn_in_grad,
    attn_out_grad,
    attn_bias_grad,
    ffn_in_grad,
    ffn_in_bias_grad,
    ffn_out_grad,
    ffn_out_bias_grad,
    norm_gain_grad,
    norm_bias_grad,
    query_pos_grad,
    moved,
    in_sem,
    out_sem,
):
    pieces = in_sem.shape[0]
    piece = moved.shape[0] // pieces

    def fetch(j):
        rows = pl.ds(piece * j, piece)
        return pltpu.make_async_copy(memory_grad_in.at[0, rows], moved.at[rows], in_sem.at[j])

    def write(j):
        rows = pl.ds(piece * j, piece)
        return pltpu.make_async_copy(moved.at[rows], memory_grad.at[0, rows], out_sem.at[j])

    for j in range(pieces):
        fetch(j).start()
    result[0] = result_in[...]
    queries_grad[0] = queries_grad_in[...]
    for j in range(FF // D):
        ffn_in_grad[:, D * j : D * j + D] = whole_f[0, D * j : D * j + D].astype(f32)
        ffn_out_grad[D * j : D * j + D] = whole_f[1, D * j : D * j + D].astype(f32)
    for j in range(pieces):
        fetch(j).wait()
        write(j).start()
    attn_out_grad[0] = whole_t[1, D : 2 * D].astype(f32)
    attn_out_grad[1, : D // 2] = whole_f[0, FF:ROWS_F].astype(f32)
    attn_out_grad[1, D // 2 :] = whole_f[1, FF:ROWS_F].astype(f32)
    for j in range(3):
        attn_in_grad[0, j] = whole_t[0, D * j : D * j + D].astype(f32)
    attn_in_grad[1, 0] = whole_t[1, :D].astype(f32)
    attn_in_grad[1, 1] = whole_t[0, 3 * D : 4 * D].astype(f32)
    attn_in_grad[1, 2] = whole_t[1, 2 * D : 3 * D].astype(f32)
    query_pos_grad[...] = whole_t[1, ROW_POS:ROW_SMALL].astype(f32)[:NQ]
    small = whole_t[1, ROW_SMALL : ROW_SMALL + 32].astype(f32)
    ffn_in_bias_grad[...] = jnp.concatenate([small[j : j + 1] for j in range(FF // D)], axis=1)
    ffn_out_bias_grad[...] = small[8:9]
    for j, (own, cross) in enumerate(((16, 19), (17, 22), (18, 9))):
        attn_bias_grad[j, 0:1] = small[own : own + 1]
        attn_bias_grad[j, 1:2] = small[cross : cross + 1]
    norm_gain_grad[0:1] = small[20:21]
    norm_gain_grad[1:2] = small[12:13]
    norm_gain_grad[2:3] = small[10:11]
    norm_bias_grad[0:1] = small[21:22]
    norm_bias_grad[1:2] = small[13:14]
    norm_bias_grad[2:3] = small[11:12]
    for j in range(pieces):
        write(j).wait()


def body(
    pages,
    queries,
    memory,
    quarter_turns,
    token_order,
    lengths,
    attn_in,
    attn_out,
    attn_bias,
    ffn_in,
    ffn_in_bias,
    ffn_out,
    ffn_out_bias,
    norm_gain,
    norm_bias,
    query_pos,
    out_grad,
):
    tokens = memory.shape[1]
    chunks = tokens // CHUNK
    rows_f = padded(ROWS_F, pages)
    rows_t = padded(ROWS_T, pages)
    copies = PageSum.copies(pages)
    vmem = pl.BlockSpec(memory_space=pltpu.VMEM)
    smem = pl.BlockSpec(memory_space=pltpu.SMEM)
    anywhere = pl.BlockSpec(memory_space=pl.ANY)
    parts = pl.pallas_call(
        functools.partial(layer_kernel, tokens, pages),
        out_shape=[
            jax.ShapeDtypeStruct((NQ, D), bf16),
            jax.ShapeDtypeStruct((NQ, D), bf16),
            jax.ShapeDtypeStruct((1, tokens, D), bf16),
            jax.ShapeDtypeStruct((2, rows_f, D), bf16),
            jax.ShapeDtypeStruct((2, rows_t, D), bf16),
        ],
        in_specs=[
            vmem,
            anywhere,
            smem,
            vmem,
            smem,
            vmem,
            vmem,
            vmem,
            anywhere,
            vmem,
            anywhere,
            vmem,
            vmem,
            vmem,
            vmem,
            vmem,
            vmem,
        ],
        out_specs=[vmem, vmem, anywhere, anywhere, anywhere],
        scratch_shapes=[
            pltpu.VMEM((tokens, D), bf16),
            pltpu.VMEM((tokens, D), bf16),
            pltpu.VMEM((tokens, D), bf16),
            pltpu.VMEM((tokens, D), bf16),
            pltpu.VMEM((tokens, NP), bf16),
            pltpu.VMEM((tokens, HQ), bf16),
            pltpu.VMEM((1, tokens), f32),
            pltpu.VMEM((CHUNK, HQ), f32),
            pltpu.VMEM((CHUNK, HQ), f32),
            pltpu.VMEM((2, D, HQ // 2), bf16),
            pltpu.VMEM((2, 2 * SIDE, D), bf16),
            pltpu.VMEM((chunks, HQ), f32),
            pltpu.VMEM((chunks, HQ), f32),
            pltpu.VMEM((8, HQ), f32),
            pltpu.VMEM((D, PAIR), f32),
            pltpu.VMEM((D, FF), bf16),
            pltpu.VMEM((FF, D), bf16),
            pltpu.VMEM((NP, FF), f32),
            pltpu.VMEM((3, NP, D), f32),
            pltpu.VMEM((2 * D, D), bf16),
            pltpu.VMEM((HQ, D), bf16),
            pltpu.VMEM((D, HQ), bf16),
            pltpu.VMEM((HQ, D), bf16),
            pltpu.VMEM((D + 2 * HEADS, NP), f32),
            pltpu.VMEM((D + 2 * HEADS, NP), f32),
            pltpu.VMEM((D, NP), f32),
            pltpu.VMEM((D, NP), f32),
            pltpu.VMEM((2 * D + TILE, D), f32),
            pltpu.VMEM((D + TILE, D), bf16),
            pltpu.VMEM((D + TILE, D), bf16),
            pltpu.VMEM((32, D), f32),
            pltpu.VMEM((rows_f, D), bf16),
            pltpu.VMEM((PageSum.landing_rows(pages, rows_f), D), bf16),
            pltpu.VMEM((2, rows_f, D), bf16),
            pltpu.VMEM((rows_t, D), bf16),
            pltpu.VMEM((PageSum.landing_rows(pages, rows_t), D), bf16),
            pltpu.VMEM((2, rows_t, D), bf16),
            pltpu.SemaphoreType.DMA((5,)),
            pltpu.SemaphoreType.DMA((chunks,)),
            pltpu.SemaphoreType.DMA((6,)),
            pltpu.SemaphoreType.DMA((copies,)),
            pltpu.SemaphoreType.DMA((copies,)),
            pltpu.SemaphoreType.DMA((copies,)),
            pltpu.SemaphoreType.DMA((copies,)),
        ],
        compiler_params=pltpu.CompilerParams(
            collective_id=0, has_side_effects=True, vmem_limit_bytes=62 * 1024 * 1024
        ),
        cost_estimate=pl.CostEstimate(
            flops=2 * 8 * tokens * HQ * D, bytes_accessed=20 << 20, transcendentals=tokens * HQ
        ),
        name="decoder_layer",
    )(
        queries,
        memory,
        quarter_turns,
        token_order,
        lengths,
        attn_in,
        attn_out,
        attn_bias.transpose(1, 0, 2),
        ffn_in,
        ffn_in_bias,
        ffn_out,
        ffn_out_bias,
        norm_gain,
        norm_bias,
        query_pos,
        out_grad,
        jnp.asarray(position_table()),
    )
    outs = pl.pallas_call(
        finish_kernel,
        out_shape=[
            jax.ShapeDtypeStruct((1, NQ, D), bf16),
            jax.ShapeDtypeStruct((1, NQ, D), bf16),
            jax.ShapeDtypeStruct((1, tokens, D), bf16),
            jax.ShapeDtypeStruct((2, 3, D, D), f32),
            jax.ShapeDtypeStruct((2, D, D), f32),
            jax.ShapeDtypeStruct((3, 2, D), f32),
            jax.ShapeDtypeStruct((D, FF), f32),
            jax.ShapeDtypeStruct((1, FF), f32),
            jax.ShapeDtypeStruct((FF, D), f32),
            jax.ShapeDtypeStruct((1, D), f32),
            jax.ShapeDtypeStruct((3, D), f32),
            jax.ShapeDtypeStruct((3, D), f32),
            jax.ShapeDtypeStruct((NQ, D), f32),
        ],
        in_specs=[vmem, vmem, anywhere, vmem, vmem],
        out_specs=[vmem, vmem, anywhere] + [vmem] * 10,
        scratch_shapes=[
            pltpu.VMEM((tokens, D), bf16),
            pltpu.SemaphoreType.DMA((8,)),
            pltpu.SemaphoreType.DMA((8,)),
        ],
        compiler_params=pltpu.CompilerParams(vmem_limit_bytes=62 * 1024 * 1024),
        name="write_outputs",
    )(*parts)
    return (
        *outs[:5],
        outs[5].transpose(1, 0, 2),
        outs[6],
        outs[7].reshape(FF),
        outs[8],
        outs[9].reshape(D),
        *outs[10:],
    )


def solution(mesh):
    in_specs = (
        P("dp", None, None),
        P("dp", "blk", None),
        P("dp"),
        P("dp", "blk"),
        P("dp"),
        P(),
        P(),
        P(),
        P(),
        P(),
        P(),
        P(),
        P(),
        P(),
        P(),
        P("dp", None, None),
    )
    out_specs = (
        P("dp", None, None),
        P("dp", None, None),
        P("dp", "blk", None),
        P(),
        P(),
        P(),
        P(),
        P(),
        P(),
        P(),
        P(),
        P(),
        P(),
    )
    layer = functools.partial(body, mesh.shape["dp"])
    return jax.shard_map(layer, mesh=mesh, in_specs=in_specs, out_specs=out_specs, check_vma=False)
```

```python
import functools
import math

import jax
import jax.numpy as jnp
import numpy as np
from jax import lax
from jax.experimental import pallas as pl
from jax.experimental.pallas import tpu as pltpu
from jax.sharding import PartitionSpec as P

D = 256
HEADS = 8
HD = D // HEADS
SIDE = 128
NQ = 125
NP = 128
HQ = HEADS * NP
PAIR = 2 * NP
FF = 2048
CHUNK = 512

masked_score = -1e30
norm_eps = 1e-05
scale = 1.0 / math.sqrt(HD)
log2e = math.log2(math.e)

bf16 = jnp.bfloat16
f32 = jnp.float32

ROWS_F = FF + D // 2
ROW_POS = 2 * D
ROW_SMALL = 2 * D + NP
ROWS_T = 3 * D
ROWS_K = D
TILE = 16


def digits_of(pages):
    digits = [(2, 1), (2, 2)]
    stride = 4
    while stride < pages:
        radix = 4 if pages // stride % 4 == 0 else 2
        digits.append((radix, stride))
        stride *= radix
    return digits


def padded(rows, pages):
    unit = TILE * pages
    return (rows + unit - 1) // unit * unit


def position_table():
    half = D // 2
    channel = np.arange(half)
    inverse = np.exp((channel // 2).astype(np.float32) * np.float32(-2.0 * math.log(10000.0) / half))
    angle = (np.arange(SIDE, dtype=np.float32) + 1.0) * np.float32(2.0 * math.pi / SIDE)
    angle = angle[:, None] * inverse
    return np.where(channel % 2 == 0, np.sin(angle), np.cos(angle)).astype(np.float32)


def dot(a, b):
    return jnp.dot(a, b, preferred_element_type=f32)


def dot_nt(a, b):
    return lax.dot_general(a, b, (((1,), (1,)), ((), ())), preferred_element_type=f32)


def dot_tn(a, b):
    return lax.dot_general(a, b, (((0,), (0,)), ((), ())), preferred_element_type=f32)


def row_total(values):
    return jnp.sum(values.astype(f32), axis=0, keepdims=True)


def norm_forward(values):
    average = jnp.mean(values, axis=-1, keepdims=True)
    centred = values - average
    variance = jnp.mean(centred * centred, axis=-1, keepdims=True)
    rstd = lax.rsqrt(variance + norm_eps)
    return centred * rstd, rstd


def norm_backward(grad, normed, rstd, gain):
    grad_normed = grad * gain
    first = jnp.mean(grad_normed, axis=-1, keepdims=True)
    second = jnp.mean(grad_normed * normed, axis=-1, keepdims=True)
    grad_in = rstd * (grad_normed - first - normed * second)
    return grad_in, row_total(grad * normed), row_total(grad)


def spread_rows(rows):
    head = lax.broadcasted_iota(jnp.int32, (NP, D), 1) // HD
    return jnp.concatenate(
        [jnp.where(head == h, rows, 0.0) for h in range(HEADS)], axis=0
    ).astype(bf16)


def spread_cols(cols):
    head = lax.broadcasted_iota(jnp.int32, (D, NP), 0) // HD
    return jnp.concatenate(
        [jnp.where(head == h, cols, 0.0) for h in range(HEADS)], axis=1
    ).astype(bf16)


def own_blocks(pairs):
    parts = []
    for pair in pairs:
        parts += [pair[:HD, :NP], pair[HD:, NP:]]
    return jnp.concatenate(parts, axis=0)


def head_rows(row):
    return jnp.concatenate([row[:, NP * h : NP * h + NP] for h in range(HEADS)], axis=0)


def head_line(rows):
    return jnp.concatenate([rows[h : h + 1] for h in range(HEADS)], axis=1)


def per_channel(rows):
    return jnp.concatenate(
        [jnp.broadcast_to(rows[h : h + 1], (HD, NP)) for h in range(HEADS)], axis=0
    )


def head_sums(cols):
    return jnp.concatenate(
        [jnp.sum(cols[HD * h : HD * h + HD], axis=0, keepdims=True) for h in range(HEADS)], axis=0
    )


def pair_cols(p):
    return slice(PAIR * p, PAIR * p + PAIR)


def pair_rows(p):
    return slice(2 * HD * p, 2 * HD * p + 2 * HD)


class PageSum:
    def __init__(self, pages, rows, landing, whole, sent, arrived):
        self.rows, self.landing, self.whole = rows, landing, whole
        self.sent, self.arrived = sent, arrived
        self.page = lax.axis_index("dp")
        self.member = lax.axis_index("blk")
        self.digits = digits_of(pages)
        self.extents = [rows.shape[0]]
        self.bases = [0]
        self.slots = []
        self.places = []
        slot = 0
        place = 0
        for radix, stride in self.digits:
            digit = self.page // stride % radix
            extent = self.extents[-1] // radix
            self.slots.append(slot)
            self.places.append(place)
            slot += radix - 1
            place += (radix - 1) * extent
            self.bases.append(pl.multiple_of(self.bases[-1] + digit * extent, TILE))
            self.extents.append(extent)
        self.gather_slot = slot
        self.last = len(self.digits)
        self.phases = [self.scatter_phase(s) for s in range(self.last)]
        self.phases.append(self.owned_phase)
        for s in range(self.last - 1, 2, -1):
            self.phases.append(self.spread_phase(s))
        self.phases += [self.sides_phase, self.corners_phase, self.core_phase, self.end_phase]

    @staticmethod
    def landing_rows(pages, rows):
        total, extent = 0, rows
        for radix, _ in digits_of(pages):
            extent //= radix
            total += (radix - 1) * extent
        return total

    @staticmethod
    def copies(pages):
        return sum(radix - 1 for radix, _ in digits_of(pages)) * 2 + 6

    def peer(self, step, hop):
        radix, stride = self.digits[step]
        digit = self.page // stride % radix
        other = lax.rem(digit + hop, radix)
        return (self.page + (other - digit) * stride, self.member), other

    def copy(self, slot, source, target, device):
        return pltpu.make_async_remote_copy(
            src_ref=source,
            dst_ref=target,
            send_sem=self.sent.at[slot],
            recv_sem=self.arrived.at[slot],
            device_id=device,
            device_id_type=pl.DeviceIdType.MESH,
        )

    def scatter_copies(self, step):
        radix, _ = self.digits[step]
        extent = self.extents[step + 1]
        for hop in range(1, radix):
            device, other = self.peer(step, hop)
            start = pl.multiple_of(self.bases[step] + other * extent, TILE)
            place = self.places[step] + (hop - 1) * extent
            yield self.copy(
                self.slots[step] + hop - 1,
                self.rows.at[pl.ds(start, extent)],
                self.landing.at[pl.ds(place, extent)],
                device,
            )

    def scatter_sum(self, step):
        radix, _ = self.digits[step]
        extent = self.extents[step + 1]
        total = self.rows[pl.ds(self.bases[step + 1], extent)].astype(f32)
        for hop in range(1, radix):
            place = self.places[step] + (hop - 1) * extent
            total = total + self.landing[pl.ds(place, extent)].astype(f32)
        return total.astype(bf16)

    def scatter_phase(self, step):
        def run():
            if step > 0:
                self.finish(self.scatter_copies(step - 1))
                self.rows[pl.ds(self.bases[step], self.extents[step])] = self.scatter_sum(step - 1)
            self.begin(self.scatter_copies(step))

        return run

    def gather_copies(self, step):
        radix, _ = self.digits[step]
        place = self.whole.at[self.member, pl.ds(self.bases[step + 1], self.extents[step + 1])]
        for hop in range(1, radix):
            device, _ = self.peer(step, hop)
            yield self.copy(self.gather_slot + self.slots[step] + hop - 1, place, place, device)

    def side_copies(self):
        slot = self.gather_slot + self.slots[1]
        beside, other = self.peer(1, 1)
        across = (self.page, 1 - self.member)
        extent = self.extents[2]
        place = self.whole.at[self.member, pl.ds(self.bases[2], extent)]
        extra = self.gather_slot * 2
        yield self.copy(slot, place, place, beside)
        yield self.copy(extra, place, place, across)

    def corner_copies(self):
        beside, other = self.peer(1, 1)
        across = (self.page, 1 - self.member)
        half = self.extents[2] // 2
        core_base = self.bases[1]
        side_base = pl.multiple_of(core_base + other * self.extents[2], TILE)
        first = self.whole.at[self.member, pl.ds(side_base, half)]
        second = self.whole.at[1 - self.member, pl.ds(pl.multiple_of(self.bases[2] + half, TILE), half)]
        extra = self.gather_slot * 2
        yield self.copy(extra + 1, first, first, across)
        yield self.copy(extra + 2, second, second, beside)

    def core_copies(self):
        device, _ = self.peer(0, 1)
        for m in range(2):
            place = self.whole.at[m, pl.ds(self.bases[1], self.extents[1])]
            yield self.copy(self.gather_slot * 2 + 3 + m, place, place, device)

    def begin(self, copies):
        for copy in copies:
            copy.start()

    def finish(self, copies):
        for copy in copies:
            copy.wait()

    def owned_phase(self):
        self.finish(self.scatter_copies(self.last - 1))
        self.whole[self.member, pl.ds(self.bases[self.last], self.extents[self.last])] = self.scatter_sum(
            self.last - 1
        )
        self.begin(self.gather_copies(self.last - 1))

    def spread_phase(self, step):
        def run():
            self.finish(self.gather_copies(step))
            self.begin(self.gather_copies(step - 1))

        return run

    def sides_phase(self):
        self.finish(self.gather_copies(2))
        self.begin(self.side_copies())

    def corners_phase(self):
        self.finish(self.side_copies())
        self.begin(self.corner_copies())

    def core_phase(self):
        self.finish(self.corner_copies())
        self.begin(self.core_copies())

    def end_phase(self):
        self.finish(self.core_copies())


def layer_kernel(
    tokens,
    pages,
    queries_in,
    memory_hbm,
    turns_in,
    order_in,
    lengths_in,
    attn_in,
    attn_out,
    attn_bias,
    ffn_in_hbm,
    ffn_in_bias,
    ffn_out_hbm,
    ffn_out_bias,
    norm_gain,
    norm_bias,
    pos_in,
    out_grad_in,
    table_in,
    result_out,
    queries_grad_out,
    memory_grad_hbm,
    whole_f_hbm,
    whole_t_hbm,
    whole_k_hbm,
    memory_s,
    key_in_s,
    key_s,
    value_s,
    aux_s,
    probs_s,
    code_s,
    score_a,
    score_b,
    weight_s,
    table_s,
    shifts_s,
    factor_s,
    total_s,
    mixed_s,
    ffn_in_s,
    ffn_out_s,
    gate_s,
    pad_s,
    back_w,
    query_x,
    grad_xt,
    grad_x,
    send_a,
    recv_a,
    send_b,
    recv_b,
    key_grads,
    send_k,
    recv_k,
    small_s,
    rows_f,
    landing_f,
    whole_f,
    rows_t,
    landing_t,
    whole_t,
    rows_k,
    landing_k,
    whole_k,
    load_sem,
    store_sem,
    link_sem,
    sent_f,
    arrived_f,
    sent_t,
    arrived_t,
    sent_k,
    arrived_k,
):
    member = lax.axis_index("blk")
    partner = (lax.axis_index("dp"), 1 - member)
    chunks = tokens // CHUNK

    sum_f = PageSum(pages, rows_f, landing_f, whole_f, sent_f, arrived_f)
    sum_t = PageSum(pages, rows_t, landing_t, whole_t, sent_t, arrived_t)
    sum_k = PageSum(pages, rows_k, landing_k, whole_k, sent_k, arrived_k)

    barrier = pltpu.get_barrier_semaphore()
    peers = [partner]
    for step, (radix, _) in enumerate(sum_f.digits):
        peers += [sum_f.peer(step, hop)[0] for hop in range(1, radix)]
    for peer in peers:
        pl.semaphore_signal(barrier, inc=1, device_id=peer, device_id_type=pl.DeviceIdType.MESH)

    load_memory = pltpu.make_async_copy(memory_hbm.at[0], memory_s, load_sem.at[0])
    load_ffn_in = pltpu.make_async_copy(ffn_in_hbm, ffn_in_s, load_sem.at[1])
    load_ffn_out = pltpu.make_async_copy(ffn_out_hbm, ffn_out_s, load_sem.at[2])
    load_memory.start()
    load_ffn_in.start()
    load_ffn_out.start()

    pairs = [attn_bias[j].astype(f32) for j in range(3)]
    bias = jnp.concatenate([pair[k : k + 1] for k in range(2) for pair in pairs], axis=0)
    gain = norm_gain[...].astype(f32)
    shift = norm_bias[...].astype(f32)

    order = order_in[...]
    turn = turns_in[0]
    row_at = order >> 7
    col_at = order & 127
    top = SIDE - 1
    row_new = jnp.where(
        turn == 0, row_at, jnp.where(turn == 1, col_at, jnp.where(turn == 2, top - row_at, top - col_at))
    )
    col_new = jnp.where(
        turn == 0, col_at, jnp.where(turn == 1, top - row_at, jnp.where(turn == 2, top - col_at, row_at))
    )
    past = jnp.where(order < lengths_in[0], 0, SIDE * SIDE)
    code_s[...] = (row_new * SIDE + col_new + past).astype(f32)

    pad_s[...] = jnp.zeros_like(pad_s)
    pad_s[0, :NQ] = queries_in[0].astype(f32)
    pad_s[1, :NQ] = pos_in[...].astype(f32)
    pad_s[2, :NQ] = out_grad_in[0].astype(f32)
    queries_f = pad_s[0]
    pos_f = pad_s[1]
    queries_b = queries_f.astype(bf16)
    mixed_q = (queries_f + pos_f).astype(bf16)
    query_self = (dot(mixed_q, attn_in[0, 0]) + bias[0:1]).astype(bf16)
    key_self = dot(mixed_q, attn_in[0, 1]).astype(bf16)
    value_self = (dot(queries_b, attn_in[0, 2]) + bias[1:2]).astype(bf16)
    scores = dot(key_self, spread_cols(query_self.astype(f32).T)) * scale
    own_key = lax.broadcasted_iota(jnp.int32, (NP, HQ), 0) < NQ
    scores = jnp.where(own_key, scores, masked_score)
    raised = jnp.exp(scores - jnp.max(scores, axis=0, keepdims=True))
    probs_self = raised / jnp.sum(raised, axis=0, keepdims=True)
    probs_self_b = probs_self.astype(bf16)
    value_t = value_self.astype(f32).T.astype(bf16)
    attended = own_blocks(
        [dot(value_t[pair_rows(p)], probs_self_b[:, pair_cols(p)]) for p in range(4)]
    ).T.astype(bf16)
    first_normed, first_rstd = norm_forward(queries_f + dot(attended, attn_out[0]) + bias[2:3])
    first = first_normed * gain[0:1] + shift[0:1]
    cross_q = (first + pos_f).astype(bf16)
    query_c = (dot(cross_q, attn_in[1, 0]) + bias[3:4]).astype(bf16)
    query_x[...] = spread_rows(query_c.astype(f32))
    query_xt = spread_cols(query_c.astype(f32).T)
    aux_row = jnp.where(
        lax.broadcasted_iota(jnp.int32, (NP, HQ // 2), 0) == 0, 1.0, 0.0
    ).astype(bf16)
    for g in range(2):
        weight_s[g, :NP] = query_xt[NP * g : NP * g + NP, HQ // 2 * g : HQ // 2 * (g + 1)]
        weight_s[g, NP:] = aux_row
    back_w[:D] = attn_in[1, 1].astype(f32).T.astype(bf16)
    back_w[D:] = attn_in[1, 2].astype(f32).T.astype(bf16)

    table = table_in[...]
    nothing = jnp.zeros((SIDE, D // 2), f32)
    table = jnp.concatenate(
        [jnp.concatenate([table, nothing], axis=1), jnp.concatenate([nothing, table], axis=1)], axis=0
    )
    table_high = table.astype(bf16)
    table_s[0] = table_high
    table_s[1] = (table - table_high.astype(f32)).astype(bf16)

    load_memory.wait()
    lane = lax.broadcasted_iota(jnp.int32, (CHUNK, NP), 1)
    value_bias = bias[4:5]

    @pl.loop(0, chunks)
    def _(i):
        rows = pl.ds(pl.multiple_of(i * CHUNK, CHUNK), CHUNK)
        line = code_s[:, rows]
        code = jnp.concatenate(
            [
                jnp.broadcast_to(line[:, NP * j : NP * j + NP], (NP, NP)).T
                for j in range(CHUNK // NP)
            ],
            axis=0,
        ).astype(jnp.int32)
        row_hot = jnp.where(((code >> 7) & 127) == lane, 1.0, 0.0)
        col_hot = jnp.where((code & 127) == lane, 1.0, 0.0)
        hot = jnp.concatenate([row_hot, col_hot], axis=1).astype(bf16)
        aux_s[rows] = jnp.where((code >= SIDE * SIDE) & (lane == 0), masked_score, 0.0).astype(bf16)
        block = memory_s[rows]
        positions = dot(hot, table_s[0]) + dot(hot, table_s[1])
        key_in = (block.astype(f32) + positions).astype(bf16)
        key_in_s[rows] = key_in
        key_s[rows] = dot(key_in, attn_in[1, 1]).astype(bf16)
        value_s[rows] = (dot(block, attn_in[1, 2]) + value_bias).astype(bf16)

    def score_chunk(i, out):
        rows = pl.ds(pl.multiple_of(i * CHUNK, CHUNK), CHUNK)
        for g in range(2):
            left = jnp.concatenate([key_s[rows, NP * g : NP * g + NP], aux_s[rows]], axis=1)
            out[:, HQ // 2 * g : HQ // 2 * (g + 1)] = dot(left, weight_s[g])

    def attend_chunk(i, scored):
        rows = pl.ds(pl.multiple_of(i * CHUNK, CHUNK), CHUNK)
        value_ct = value_s[rows].T
        for p in range(4):
            cols = pair_cols(p)
            before = total_s[0:1, cols]
            part = scored[:, cols]
            highest = jnp.maximum(
                before, jnp.max(part, axis=0, keepdims=True) * (scale * log2e)
            )
            raised = jnp.exp2(part * (scale * log2e) - highest)
            fade = jnp.exp2(before - highest)
            total_s[0:1, cols] = highest
            total_s[1:2, cols] = total_s[1:2, cols] * fade + jnp.sum(raised, axis=0, keepdims=True)
            shifts_s[pl.ds(i, 1), cols] = highest
            raised_b = raised.astype(bf16)
            probs_s[rows, cols] = raised_b
            mixed_s[pair_rows(p)] = mixed_s[pair_rows(p)] * fade + dot(
                value_ct[pair_rows(p)], raised_b
            )

    total_s[0:1] = jnp.full((1, HQ), -3e38, f32)
    total_s[1:2] = jnp.zeros((1, HQ), f32)
    mixed_s[...] = jnp.zeros_like(mixed_s)
    score_chunk(0, score_a)

    @pl.loop(0, chunks // 2)
    def _(j):
        i = j * 2
        score_chunk(i + 1, score_b)
        attend_chunk(i, score_a)
        score_chunk(jnp.minimum(i + 2, chunks - 1), score_a)
        attend_chunk(i + 1, score_b)

    send_a[:D] = own_blocks([mixed_s[pair_rows(p)] for p in range(4)])
    send_a[D : D + HEADS] = head_rows(total_s[0:1])
    send_a[D + HEADS :] = head_rows(total_s[1:2])
    pl.semaphore_wait(barrier, len(peers))
    swap_a = pltpu.make_async_remote_copy(
        src_ref=send_a,
        dst_ref=recv_a,
        send_sem=link_sem.at[0],
        recv_sem=link_sem.at[1],
        device_id=partner,
        device_id_type=pl.DeviceIdType.MESH,
    )
    swap_a.start()
    swap_a.wait()
    is_first = member == 0
    own = send_a[...]
    other = recv_a[...]
    left = jnp.where(is_first, own, other)
    right = jnp.where(is_first, other, own)
    high_l, high_r = left[D : D + HEADS], right[D : D + HEADS]
    highest = jnp.maximum(high_l, high_r)
    fade_l = jnp.exp2(high_l - highest)
    fade_r = jnp.exp2(high_r - highest)
    total = left[D + HEADS :] * fade_l + right[D + HEADS :] * fade_r
    mixed_t = left[:D] * per_channel(fade_l / total) + right[:D] * per_channel(fade_r / total)
    log_total = head_line(highest + jnp.log2(total))
    factor_s[...] = jnp.exp2(shifts_s[...] - log_total)
    attended_c = mixed_t.T.astype(bf16)

    second_normed, second_rstd = norm_forward(first + dot(attended_c, attn_out[1]) + bias[5:6])
    second = second_normed * gain[1:2] + shift[1:2]
    ffn_input = second.astype(bf16)
    load_ffn_in.wait()
    hidden = dot(ffn_input, ffn_in_s[...]) + ffn_in_bias[...].astype(f32).reshape(1, FF)
    half_gate = 0.5 + 0.5 * lax.erf(hidden * math.sqrt(0.5))
    activated = (hidden * half_gate).astype(bf16)
    gate_s[...] = half_gate + hidden * jnp.exp(hidden * hidden * -0.5) * (1.0 / math.sqrt(2.0 * math.pi))
    load_ffn_out.wait()
    third_normed, third_rstd = norm_forward(
        second + dot(activated, ffn_out_s[...]) + ffn_out_bias[...].astype(f32).reshape(1, D)
    )
    result_out[...] = (third_normed * gain[2:3] + shift[2:3])[:NQ].astype(bf16)
    grad_third, gain_grad_2, shift_grad_2 = norm_backward(
        pad_s[2], third_normed, third_rstd, gain[2:3]
    )
    grad_branch_f = grad_third.astype(bf16)
    grad_hidden = (dot_nt(grad_branch_f, ffn_out_s[...]) * gate_s[...]).astype(bf16)
    grad_second = grad_third + dot_nt(grad_hidden, ffn_in_s[...])
    grad_second_in, gain_grad_1, shift_grad_1 = norm_backward(
        grad_second, second_normed, second_rstd, gain[1:2]
    )
    grad_branch_c = grad_second_in.astype(bf16)
    @pl.when(member == 0)
    def _():
        ffn_input_t = second.T.astype(bf16)
        for j in range(FF // D):
            rows_f[D * j : D * j + D] = dot(ffn_input_t, grad_hidden[:, D * j : D * j + D]).astype(bf16)
        rows_f[FF:ROWS_F] = dot_tn(attended_c[:, : D // 2], grad_branch_c).astype(bf16)

    @pl.when(member == 1)
    def _():
        for j in range(FF // D):
            rows_f[D * j : D * j + D] = dot_tn(activated[:, D * j : D * j + D], grad_branch_f).astype(bf16)
        rows_f[FF:ROWS_F] = dot_tn(attended_c[:, D // 2 :], grad_branch_c).astype(bf16)

    rows_f[ROWS_F:] = jnp.zeros((rows_f.shape[0] - ROWS_F, D), bf16)
    sum_f.phases[0]()
    grad_attended_c = dot_nt(grad_branch_c, attn_out[1]).astype(bf16).astype(f32)
    hidden_sum = row_total(grad_hidden)
    small_s[:16] = jnp.concatenate(
        [hidden_sum[:, D * j : D * j + D] for j in range(FF // D)]
        + [
            row_total(grad_branch_f),
            row_total(grad_branch_c),
            gain_grad_2,
            shift_grad_2,
            gain_grad_1,
            shift_grad_1,
            row_total(grad_attended_c),
            jnp.zeros((1, D), f32),
        ],
        axis=0,
    )

    grad_attended_t = grad_attended_c.T
    grad_xt[...] = spread_cols(grad_attended_t)
    grad_x[...] = spread_rows(grad_attended_c)
    inner = head_line(head_sums(grad_attended_t * mixed_t))
    mixed_s[...] = jnp.zeros_like(mixed_s)
    key_grads[...] = jnp.zeros_like(key_grads)

    def in_turn(i, phases):
        for k, phase in enumerate(phases):
            pl.when(i == chunks * (k + 1) // len(phases) - 1)(phase)

    @pl.loop(0, chunks)
    def _(i):
        rows = pl.ds(pl.multiple_of(i * CHUNK, CHUNK), CHUNK)
        key_ct = key_s[rows].T
        value_c = value_s[rows]
        weights = []
        for p in range(4):
            cols = pair_cols(p)
            grad_probs = dot(value_c, grad_xt[:, cols])
            probs = probs_s[rows, cols].astype(f32) * factor_s[pl.ds(i, 1), cols]
            grad_scores = (probs * (grad_probs - inner[:, cols])).astype(bf16)
            mixed_s[pair_rows(p)] += dot(key_ct[pair_rows(p)], grad_scores)
            probs_s[rows, cols] = grad_scores
            weights.append(probs.astype(bf16))
        grad_value = dot(jnp.concatenate(weights, axis=1), grad_x[...]).astype(bf16)
        value_s[rows] = grad_value
        key_grads[D:] += dot_tn(memory_s[rows], grad_value)
        in_turn(i, sum_f.phases[1:5])

    send_b[...] = own_blocks([mixed_s[pair_rows(p)] for p in range(4)]) * scale
    swap_b = pltpu.make_async_remote_copy(
        src_ref=send_b,
        dst_ref=recv_b,
        send_sem=link_sem.at[2],
        recv_sem=link_sem.at[3],
        device_id=partner,
        device_id_type=pl.DeviceIdType.MESH,
    )
    swap_b.start()
    swap_b.wait()
    grad_query_c = (send_b[...] + recv_b[...]).T.astype(bf16)

    cross_pos_grad = dot_nt(grad_query_c, attn_in[1, 0])
    grad_first_in, gain_grad_0, shift_grad_0 = norm_backward(
        grad_second_in + cross_pos_grad, first_normed, first_rstd, gain[0:1]
    )
    grad_branch = grad_first_in.astype(bf16)
    grad_attended = dot_nt(grad_branch, attn_out[0]).astype(bf16).astype(f32)
    grad_probs = dot(value_self, spread_cols(grad_attended.T))
    inner_self = jnp.sum(probs_self * grad_probs, axis=0, keepdims=True)
    grad_scores = (probs_self * (grad_probs - inner_self)).astype(bf16)
    key_t = key_self.astype(f32).T.astype(bf16)
    grad_query_s = (
        own_blocks([dot(key_t[pair_rows(p)], grad_scores[:, pair_cols(p)]) for p in range(4)]) * scale
    ).T.astype(bf16)
    grad_key_s = (dot(grad_scores, spread_rows(query_self.astype(f32))) * scale).astype(bf16)
    grad_value_s = dot(probs_self_b, spread_rows(grad_attended)).astype(bf16)
    grad_mixed_q = dot_nt(grad_query_s, attn_in[0, 0]) + dot_nt(grad_key_s, attn_in[0, 1])
    queries_grad_out[...] = (grad_first_in + grad_mixed_q + dot_nt(grad_value_s, attn_in[0, 2]))[
        :NQ
    ].astype(bf16)
    small_s[16:] = jnp.concatenate(
        [
            row_total(grad_query_s),
            row_total(grad_value_s),
            row_total(grad_branch),
            row_total(grad_query_c),
            gain_grad_0,
            shift_grad_0,
            jnp.zeros((10, D), f32),
        ],
        axis=0,
    )
    @pl.when(member == 0)
    def _():
        rows_t[:D] = dot_tn(mixed_q, grad_query_s).astype(bf16)
        rows_t[D : 2 * D] = dot_tn(mixed_q, grad_key_s).astype(bf16)
        rows_t[2 * D : 3 * D] = dot_tn(queries_b, grad_value_s).astype(bf16)

    @pl.when(member == 1)
    def _():
        rows_t[:D] = dot_tn(cross_q, grad_query_c).astype(bf16)
        rows_t[D : 2 * D] = dot_tn(attended, grad_branch).astype(bf16)
        rows_t[ROW_POS:ROW_SMALL] = (grad_mixed_q + cross_pos_grad).astype(bf16)
        rows_t[ROW_SMALL : ROW_SMALL + 32] = small_s[...].astype(bf16)
        rows_t[ROW_SMALL + 32 : ROWS_T] = jnp.zeros((ROWS_T - ROW_SMALL - 32, D), bf16)

    if rows_t.shape[0] > ROWS_T:
        rows_t[ROWS_T:] = jnp.zeros((rows_t.shape[0] - ROWS_T, D), bf16)
    if rows_k.shape[0] > ROWS_K:
        rows_k[ROWS_K:] = jnp.zeros((rows_k.shape[0] - ROWS_K, D), bf16)
    sum_t.phases[0]()

    @pl.loop(0, chunks)
    def _(i):
        rows = pl.ds(pl.multiple_of(i * CHUNK, CHUNK), CHUNK)
        grad_key = (dot(probs_s[rows], query_x[...]) * scale).astype(bf16)
        key_s[rows] = grad_key
        key_grads[:D] += dot_tn(key_in_s[rows], grad_key)
        in_turn(i, [sum_f.phases[5], sum_t.phases[1], *sum_f.phases[6:-1], sum_t.phases[2]])

    @pl.when(member == 0)
    def _():
        send_k[...] = key_grads[D:].astype(bf16)

    @pl.when(member == 1)
    def _():
        send_k[...] = key_grads[:D].astype(bf16)

    swap_k = pltpu.make_async_remote_copy(
        src_ref=send_k,
        dst_ref=recv_k,
        send_sem=link_sem.at[4],
        recv_sem=link_sem.at[5],
        device_id=partner,
        device_id_type=pl.DeviceIdType.MESH,
    )
    swap_k.start()
    sum_t.phases[3]()
    swap_k.wait()

    @pl.when(member == 0)
    def _():
        rows_k[:ROWS_K] = (key_grads[:D] + recv_k[...].astype(f32)).astype(bf16)

    @pl.when(member == 1)
    def _():
        rows_k[:ROWS_K] = (key_grads[D:] + recv_k[...].astype(f32)).astype(bf16)

    sum_k.phases[0]()

    @pl.loop(0, chunks)
    def _(i):
        rows = pl.ds(pl.multiple_of(i * CHUNK, CHUNK), CHUNK)
        both = jnp.concatenate([key_s[rows], value_s[rows]], axis=1)
        memory_s[rows] = dot(both, back_w[...]).astype(bf16)
        pltpu.make_async_copy(memory_s.at[rows], memory_grad_hbm.at[0, rows], store_sem.at[i]).start()
        in_turn(i, [sum_k.phases[1], sum_t.phases[4]])

    sum_f.phases[-1]()
    store_f = pltpu.make_async_copy(whole_f, whole_f_hbm, load_sem.at[3])
    store_f.start()
    for k in range(2, len(sum_k.phases)):
        sum_k.phases[k]()
        if k + 3 < len(sum_t.phases):
            sum_t.phases[k + 3]()
    store_t = pltpu.make_async_copy(whole_t, whole_t_hbm, load_sem.at[4])
    store_t.start()
    store_k = pltpu.make_async_copy(whole_k, whole_k_hbm, load_sem.at[5])
    store_k.start()

    @pl.loop(0, chunks)
    def _(i):
        rows = pl.ds(pl.multiple_of(i * CHUNK, CHUNK), CHUNK)
        pltpu.make_async_copy(memory_s.at[rows], memory_grad_hbm.at[0, rows], store_sem.at[i]).wait()

    store_f.wait()
    store_t.wait()
    store_k.wait()


def finish_kernel(
    result_in,
    queries_grad_in,
    memory_grad_in,
    whole_f,
    whole_t,
    whole_k,
    result,
    queries_grad,
    memory_grad,
    attn_in_grad,
    attn_out_grad,
    attn_bias_grad,
    ffn_in_grad,
    ffn_in_bias_grad,
    ffn_out_grad,
    ffn_out_bias_grad,
    norm_gain_grad,
    norm_bias_grad,
    query_pos_grad,
    moved,
    in_sem,
    out_sem,
):
    pieces = in_sem.shape[0]
    piece = moved.shape[0] // pieces

    def fetch(j):
        rows = pl.ds(piece * j, piece)
        return pltpu.make_async_copy(memory_grad_in.at[0, rows], moved.at[rows], in_sem.at[j])

    def write(j):
        rows = pl.ds(piece * j, piece)
        return pltpu.make_async_copy(moved.at[rows], memory_grad.at[0, rows], out_sem.at[j])

    for j in range(pieces):
        fetch(j).start()
    result[0] = result_in[...]
    queries_grad[0] = queries_grad_in[...]
    for j in range(FF // D):
        ffn_in_grad[:, D * j : D * j + D] = whole_f[0, D * j : D * j + D].astype(f32)
        ffn_out_grad[D * j : D * j + D] = whole_f[1, D * j : D * j + D].astype(f32)
    for j in range(pieces):
        fetch(j).wait()
        write(j).start()
    attn_out_grad[0] = whole_t[1, D : 2 * D].astype(f32)
    attn_out_grad[1, : D // 2] = whole_f[0, FF:ROWS_F].astype(f32)
    attn_out_grad[1, D // 2 :] = whole_f[1, FF:ROWS_F].astype(f32)
    for j in range(3):
        attn_in_grad[0, j] = whole_t[0, D * j : D * j + D].astype(f32)
    attn_in_grad[1, 0] = whole_t[1, :D].astype(f32)
    attn_in_grad[1, 1] = whole_k[0, :D].astype(f32)
    attn_in_grad[1, 2] = whole_k[1, :D].astype(f32)
    query_pos_grad[...] = whole_t[1, ROW_POS:ROW_SMALL].astype(f32)[:NQ]
    small = whole_t[1, ROW_SMALL : ROW_SMALL + 32].astype(f32)
    ffn_in_bias_grad[...] = jnp.concatenate([small[j : j + 1] for j in range(FF // D)], axis=1)
    ffn_out_bias_grad[...] = small[8:9]
    for j, (own, cross) in enumerate(((16, 19), (17, 14), (18, 9))):
        attn_bias_grad[j, 0:1] = small[own : own + 1]
        attn_bias_grad[j, 1:2] = small[cross : cross + 1]
    norm_gain_grad[0:1] = small[20:21]
    norm_gain_grad[1:2] = small[12:13]
    norm_gain_grad[2:3] = small[10:11]
    norm_bias_grad[0:1] = small[21:22]
    norm_bias_grad[1:2] = small[13:14]
    norm_bias_grad[2:3] = small[11:12]
    for j in range(pieces):
        write(j).wait()


def body(
    pages,
    queries,
    memory,
    quarter_turns,
    token_order,
    lengths,
    attn_in,
    attn_out,
    attn_bias,
    ffn_in,
    ffn_in_bias,
    ffn_out,
    ffn_out_bias,
    norm_gain,
    norm_bias,
    query_pos,
    out_grad,
):
    tokens = memory.shape[1]
    chunks = tokens // CHUNK
    rows_f = padded(ROWS_F, pages)
    rows_t = padded(ROWS_T, pages)
    rows_k = padded(ROWS_K, pages)
    copies = PageSum.copies(pages)
    vmem = pl.BlockSpec(memory_space=pltpu.VMEM)
    smem = pl.BlockSpec(memory_space=pltpu.SMEM)
    anywhere = pl.BlockSpec(memory_space=pl.ANY)
    parts = pl.pallas_call(
        functools.partial(layer_kernel, tokens, pages),
        out_shape=[
            jax.ShapeDtypeStruct((NQ, D), bf16),
            jax.ShapeDtypeStruct((NQ, D), bf16),
            jax.ShapeDtypeStruct((1, tokens, D), bf16),
            jax.ShapeDtypeStruct((2, rows_f, D), bf16),
            jax.ShapeDtypeStruct((2, rows_t, D), bf16),
            jax.ShapeDtypeStruct((2, rows_k, D), bf16),
        ],
        in_specs=[
            vmem,
            anywhere,
            smem,
            vmem,
            smem,
            vmem,
            vmem,
            vmem,
            anywhere,
            vmem,
            anywhere,
            vmem,
            vmem,
            vmem,
            vmem,
            vmem,
            vmem,
        ],
        out_specs=[vmem, vmem, anywhere, anywhere, anywhere, anywhere],
        scratch_shapes=[
            pltpu.VMEM((tokens, D), bf16),
            pltpu.VMEM((tokens, D), bf16),
            pltpu.VMEM((tokens, D), bf16),
            pltpu.VMEM((tokens, D), bf16),
            pltpu.VMEM((tokens, NP), bf16),
            pltpu.VMEM((tokens, HQ), bf16),
            pltpu.VMEM((1, tokens), f32),
            pltpu.VMEM((CHUNK, HQ), f32),
            pltpu.VMEM((CHUNK, HQ), f32),
            pltpu.VMEM((2, D, HQ // 2), bf16),
            pltpu.VMEM((2, 2 * SIDE, D), bf16),
            pltpu.VMEM((chunks, HQ), f32),
            pltpu.VMEM((chunks, HQ), f32),
            pltpu.VMEM((8, HQ), f32),
            pltpu.VMEM((D, PAIR), f32),
            pltpu.VMEM((D, FF), bf16),
            pltpu.VMEM((FF, D), bf16),
            pltpu.VMEM((NP, FF), f32),
            pltpu.VMEM((3, NP, D), f32),
            pltpu.VMEM((2 * D, D), bf16),
            pltpu.VMEM((HQ, D), bf16),
            pltpu.VMEM((D, HQ), bf16),
            pltpu.VMEM((HQ, D), bf16),
            pltpu.VMEM((D + 2 * HEADS, NP), f32),
            pltpu.VMEM((D + 2 * HEADS, NP), f32),
            pltpu.VMEM((D, NP), f32),
            pltpu.VMEM((D, NP), f32),
            pltpu.VMEM((2 * D, D), f32),
            pltpu.VMEM((D, D), bf16),
            pltpu.VMEM((D, D), bf16),
            pltpu.VMEM((32, D), f32),
            pltpu.VMEM((rows_f, D), bf16),
            pltpu.VMEM((PageSum.landing_rows(pages, rows_f), D), bf16),
            pltpu.VMEM((2, rows_f, D), bf16),
            pltpu.VMEM((rows_t, D), bf16),
            pltpu.VMEM((PageSum.landing_rows(pages, rows_t), D), bf16),
            pltpu.VMEM((2, rows_t, D), bf16),
            pltpu.VMEM((rows_k, D), bf16),
            pltpu.VMEM((PageSum.landing_rows(pages, rows_k), D), bf16),
            pltpu.VMEM((2, rows_k, D), bf16),
            pltpu.SemaphoreType.DMA((6,)),
            pltpu.SemaphoreType.DMA((chunks,)),
            pltpu.SemaphoreType.DMA((6,)),
            pltpu.SemaphoreType.DMA((copies,)),
            pltpu.SemaphoreType.DMA((copies,)),
            pltpu.SemaphoreType.DMA((copies,)),
            pltpu.SemaphoreType.DMA((copies,)),
            pltpu.SemaphoreType.DMA((copies,)),
            pltpu.SemaphoreType.DMA((copies,)),
        ],
        compiler_params=pltpu.CompilerParams(
            collective_id=0, has_side_effects=True, vmem_limit_bytes=62 * 1024 * 1024
        ),
        cost_estimate=pl.CostEstimate(
            flops=2 * 8 * tokens * HQ * D, bytes_accessed=20 << 20, transcendentals=tokens * HQ
        ),
        name="decoder_layer",
    )(
        queries,
        memory,
        quarter_turns,
        token_order,
        lengths,
        attn_in,
        attn_out,
        attn_bias.transpose(1, 0, 2),
        ffn_in,
        ffn_in_bias,
        ffn_out,
        ffn_out_bias,
        norm_gain,
        norm_bias,
        query_pos,
        out_grad,
        jnp.asarray(position_table()),
    )
    outs = pl.pallas_call(
        finish_kernel,
        out_shape=[
            jax.ShapeDtypeStruct((1, NQ, D), bf16),
            jax.ShapeDtypeStruct((1, NQ, D), bf16),
            jax.ShapeDtypeStruct((1, tokens, D), bf16),
            jax.ShapeDtypeStruct((2, 3, D, D), f32),
            jax.ShapeDtypeStruct((2, D, D), f32),
            jax.ShapeDtypeStruct((3, 2, D), f32),
            jax.ShapeDtypeStruct((D, FF), f32),
            jax.ShapeDtypeStruct((1, FF), f32),
            jax.ShapeDtypeStruct((FF, D), f32),
            jax.ShapeDtypeStruct((1, D), f32),
            jax.ShapeDtypeStruct((3, D), f32),
            jax.ShapeDtypeStruct((3, D), f32),
            jax.ShapeDtypeStruct((NQ, D), f32),
        ],
        in_specs=[vmem, vmem, anywhere, vmem, vmem, vmem],
        out_specs=[vmem, vmem, anywhere] + [vmem] * 10,
        scratch_shapes=[
            pltpu.VMEM((tokens, D), bf16),
            pltpu.SemaphoreType.DMA((8,)),
            pltpu.SemaphoreType.DMA((8,)),
        ],
        compiler_params=pltpu.CompilerParams(vmem_limit_bytes=62 * 1024 * 1024),
        name="write_outputs",
    )(*parts)
    return (
        *outs[:5],
        outs[5].transpose(1, 0, 2),
        outs[6],
        outs[7].reshape(FF),
        outs[8],
        outs[9].reshape(D),
        *outs[10:],
    )


def solution(mesh):
    in_specs = (
        P("dp", None, None),
        P("dp", "blk", None),
        P("dp"),
        P("dp", "blk"),
        P("dp"),
        P(),
        P(),
        P(),
        P(),
        P(),
        P(),
        P(),
        P(),
        P(),
        P(),
        P("dp", None, None),
    )
    out_specs = (
        P("dp", None, None),
        P("dp", None, None),
        P("dp", "blk", None),
        P(),
        P(),
        P(),
        P(),
        P(),
        P(),
        P(),
        P(),
        P(),
        P(),
    )
    layer = functools.partial(body, mesh.shape["dp"])
    return jax.shard_map(layer, mesh=mesh, in_specs=in_specs, out_specs=out_specs, check_vma=False)
```

```python
import functools
import math

import jax
import jax.numpy as jnp
import numpy as np
from jax import lax
from jax.experimental import pallas as pl
from jax.experimental.pallas import tpu as pltpu
from jax.sharding import PartitionSpec as P

D = 256
HEADS = 8
HD = D // HEADS
SIDE = 128
NQ = 125
NP = 128
HQ = HEADS * NP
PAIR = 2 * NP
FF = 2048
CHUNK = 512

masked_score = -1e30
norm_eps = 1e-05
scale = 1.0 / math.sqrt(HD)
log2e = math.log2(math.e)

bf16 = jnp.bfloat16
f32 = jnp.float32

ROWS_F = FF // 2
ROWS_G = FF // 2 + D // 2
ROW_POS = 2 * D
ROW_SMALL = 2 * D + NP
ROWS_T = 3 * D
ROWS_K = 2 * D
TILE = 16


def axes_of(pages):
    axes = {"core": (2, 1), "y": (2, 2)}
    stride = 4
    while stride < pages:
        radix = 4 if pages // stride % 4 == 0 else 2
        axes["z%d" % (len(axes) - 2)] = (radix, stride)
        stride *= radix
    axes["x"] = (2, 0)
    return axes


def far_axes(pages):
    return [(name,) for name in axes_of(pages) if name.startswith("z")]


def sum_groups(pages):
    far = far_axes(pages)
    return [("core",), ("y",), *far], [("core", "y"), *far], [("x", "core", "y"), *far]


def padded(rows, pages):
    unit = TILE * pages
    return (rows + unit - 1) // unit * unit


def position_table():
    half = D // 2
    channel = np.arange(half)
    inverse = np.exp((channel // 2).astype(np.float32) * np.float32(-2.0 * math.log(10000.0) / half))
    angle = (np.arange(SIDE, dtype=np.float32) + 1.0) * np.float32(2.0 * math.pi / SIDE)
    angle = angle[:, None] * inverse
    return np.where(channel % 2 == 0, np.sin(angle), np.cos(angle)).astype(np.float32)


def dot(a, b):
    return jnp.dot(a, b, preferred_element_type=f32)


def dot_nt(a, b):
    return lax.dot_general(a, b, (((1,), (1,)), ((), ())), preferred_element_type=f32)


def dot_tn(a, b):
    return lax.dot_general(a, b, (((0,), (0,)), ((), ())), preferred_element_type=f32)


def row_total(values):
    return jnp.sum(values.astype(f32), axis=0, keepdims=True)


def norm_forward(values):
    average = jnp.mean(values, axis=-1, keepdims=True)
    centred = values - average
    variance = jnp.mean(centred * centred, axis=-1, keepdims=True)
    rstd = lax.rsqrt(variance + norm_eps)
    return centred * rstd, rstd


def norm_backward(grad, normed, rstd, gain):
    grad_normed = grad * gain
    first = jnp.mean(grad_normed, axis=-1, keepdims=True)
    second = jnp.mean(grad_normed * normed, axis=-1, keepdims=True)
    grad_in = rstd * (grad_normed - first - normed * second)
    return grad_in, row_total(grad * normed), row_total(grad)


def spread_rows(rows):
    head = lax.broadcasted_iota(jnp.int32, (NP, D), 1) // HD
    return jnp.concatenate(
        [jnp.where(head == h, rows, 0.0) for h in range(HEADS)], axis=0
    ).astype(bf16)


def spread_cols(cols):
    head = lax.broadcasted_iota(jnp.int32, (D, NP), 0) // HD
    return jnp.concatenate(
        [jnp.where(head == h, cols, 0.0) for h in range(HEADS)], axis=1
    ).astype(bf16)


def own_blocks(pairs):
    parts = []
    for pair in pairs:
        parts += [pair[:HD, :NP], pair[HD:, NP:]]
    return jnp.concatenate(parts, axis=0)


def head_rows(row):
    return jnp.concatenate([row[:, NP * h : NP * h + NP] for h in range(HEADS)], axis=0)


def head_line(rows):
    return jnp.concatenate([rows[h : h + 1] for h in range(HEADS)], axis=1)


def per_channel(rows):
    return jnp.concatenate(
        [jnp.broadcast_to(rows[h : h + 1], (HD, NP)) for h in range(HEADS)], axis=0
    )


def head_sums(cols):
    return jnp.concatenate(
        [jnp.sum(cols[HD * h : HD * h + HD], axis=0, keepdims=True) for h in range(HEADS)], axis=0
    )


def pair_cols(p):
    return slice(PAIR * p, PAIR * p + PAIR)


def pair_rows(p):
    return slice(2 * HD * p, 2 * HD * p + 2 * HD)


class Place:
    def __init__(self, pages):
        self.axes = axes_of(pages)
        self.page = lax.axis_index("dp")
        self.member = lax.axis_index("blk")
        self.digit = {
            name: self.member if name == "x" else lax.rem(self.page // stride, radix)
            for name, (radix, stride) in self.axes.items()
        }

    def size(self, group):
        return math.prod(self.axes[name][0] for name in group)

    def index(self, group):
        index = 0
        for name in group:
            index = index * self.axes[name][0] + self.digit[name]
        return index

    def peer(self, group, hop):
        index = lax.rem(self.index(group) + hop, self.size(group))
        page, member, rest = self.page, self.member, index
        for name in reversed(group):
            radix, stride = self.axes[name]
            digit = lax.rem(rest, radix)
            rest = rest // radix
            if name == "x":
                member = digit
            else:
                page = page + (digit - self.digit[name]) * stride
        return (page, member), index


class PageSum:
    def __init__(self, place, groups, back, rows, landing, whole, sent, arrived):
        self.place, self.groups, self.back = place, groups, back
        self.rows, self.landing, self.whole = rows, landing, whole
        self.sent, self.arrived = sent, arrived
        self.slots = 0
        self.extents = [rows.shape[0]]
        self.bases = [0]
        self.landings = []
        at = 0
        for group in groups:
            size = place.size(group)
            extent = self.extents[-1] // size
            self.landings.append(at)
            at += (size - 1) * extent
            self.bases.append(pl.multiple_of(self.bases[-1] + place.index(group) * extent, TILE))
            self.extents.append(extent)
        last = len(groups)
        moves = [self.scatter_moves(s) for s in range(last)]
        near = 2 if len(groups[0]) == 1 else 1
        moves += [self.gather_moves(s) for s in range(last - 1, near - 1, -1)]
        if back == "first":
            moves.append(self.gather_moves(0))
        elif back == "sides":
            moves += [self.side_moves(), self.corner_moves(), self.core_moves()]
        else:
            moves += [self.across_moves(), self.core_moves()]
        self.phases = [functools.partial(self.step, moves, k) for k in range(len(moves) + 1)]

    @staticmethod
    def landing_rows(pages, groups, rows):
        axes = axes_of(pages)
        total, extent = 0, rows
        for group in groups:
            size = math.prod(axes[name][0] for name in group)
            extent //= size
            total += (size - 1) * extent
        return total

    def step(self, moves, k):
        last = len(self.groups)
        if k > 0:
            for move in moves[k - 1]:
                self.copy(*move).wait()
        if 0 < k <= last:
            total = self.scatter_sum(k - 1)
            region = pl.ds(self.bases[k], self.extents[k])
            if k < last:
                self.rows[region] = total
            elif len(self.whole.shape) == 3:
                self.whole[self.place.member, region] = total
            else:
                self.whole[region] = total
        if k < len(moves):
            for move in moves[k]:
                self.copy(*move).start()

    def copy(self, slot, source, target, device):
        return pltpu.make_async_remote_copy(
            src_ref=source(),
            dst_ref=target(),
            send_sem=self.sent.at[slot],
            recv_sem=self.arrived.at[slot],
            device_id=device,
            device_id_type=pl.DeviceIdType.MESH,
        )

    def new_slot(self):
        self.slots += 1
        return self.slots - 1

    def same(self, device, view):
        return (self.new_slot(), view, view, device)

    def scatter_moves(self, step):
        group = self.groups[step]
        extent = self.extents[step + 1]
        moves = []
        for hop in range(1, self.place.size(group)):
            device, other = self.place.peer(group, hop)
            start = pl.multiple_of(self.bases[step] + other * extent, TILE)
            landing = self.landings[step] + (hop - 1) * extent
            moves.append(
                (
                    self.new_slot(),
                    functools.partial(self.part, self.rows, start, extent),
                    functools.partial(self.part, self.landing, landing, extent),
                    device,
                )
            )
        return moves

    @staticmethod
    def part(ref, start, extent):
        return ref.at[pl.ds(start, extent)]

    def half(self, member, start, extent):
        if len(self.whole.shape) == 3:
            return self.whole.at[member, pl.ds(start, extent)]
        return self.whole.at[pl.ds(start, extent)]

    def scatter_sum(self, step):
        extent = self.extents[step + 1]
        total = self.rows[pl.ds(self.bases[step + 1], extent)].astype(f32)
        for hop in range(1, self.place.size(self.groups[step])):
            landing = self.landings[step] + (hop - 1) * extent
            total = total + self.landing[pl.ds(landing, extent)].astype(f32)
        return total.astype(bf16)

    def gather_moves(self, step):
        group = self.groups[step]
        view = functools.partial(self.half, self.place.member, self.bases[step + 1], self.extents[step + 1])
        return [
            self.same(self.place.peer(group, hop)[0], view) for hop in range(1, self.place.size(group))
        ]

    def own_quarter(self):
        step = 2 if len(self.groups[0]) == 1 else 1
        return self.bases[step], self.extents[step]

    def side_moves(self):
        view = functools.partial(self.half, self.place.member, *self.own_quarter())
        return [self.same(self.place.peer((name,), 1)[0], view) for name in ("y", "x")]

    def corner_moves(self):
        base, extent = self.own_quarter()
        half = extent // 2
        other = pl.multiple_of(base + (1 - 2 * self.place.digit["y"]) * extent, TILE)
        first = functools.partial(self.half, self.place.member, other, half)
        second = functools.partial(
            self.half, 1 - self.place.member, pl.multiple_of(base + half, TILE), half
        )
        return [
            self.same(self.place.peer(("x",), 1)[0], first),
            self.same(self.place.peer(("y",), 1)[0], second),
        ]

    def across_moves(self):
        view = functools.partial(self.half, self.place.member, *self.own_quarter())
        return [self.same(self.place.peer(("x", "y"), hop)[0], view) for hop in range(1, 4)]

    def core_moves(self):
        extent = self.extents[0] // 2
        start = pl.multiple_of(self.place.digit["core"] * extent, TILE)
        device, _ = self.place.peer(("core",), 1)
        return [self.same(device, functools.partial(self.half, m, start, extent)) for m in range(2)]


def clear_rest(ref, used):
    if ref.shape[0] > used:
        ref[used:] = jnp.zeros((ref.shape[0] - used, D), ref.dtype)


def layer_kernel(
    tokens,
    pages,
    queries_in,
    memory_hbm,
    turns_in,
    order_in,
    lengths_in,
    attn_in,
    attn_out,
    attn_bias,
    ffn_in_hbm,
    ffn_in_bias,
    ffn_out_hbm,
    ffn_out_bias,
    norm_gain,
    norm_bias,
    pos_in,
    out_grad_in,
    table_in,
    result_out,
    queries_grad_out,
    memory_grad_hbm,
    whole_f_hbm,
    whole_g_hbm,
    whole_t_hbm,
    whole_k_hbm,
    memory_s,
    key_in_s,
    key_s,
    value_s,
    aux_s,
    probs_s,
    code_s,
    score_a,
    score_b,
    weight_s,
    table_s,
    shifts_s,
    factor_s,
    total_s,
    mixed_s,
    ffn_in_s,
    ffn_out_s,
    gate_s,
    pad_s,
    back_w,
    query_x,
    grad_xt,
    grad_x,
    send_a,
    recv_a,
    send_b,
    recv_b,
    key_grads,
    small_s,
    rows_f,
    landing_f,
    whole_f,
    rows_g,
    landing_g,
    whole_g,
    rows_t,
    landing_t,
    whole_t,
    rows_k,
    landing_k,
    whole_k,
    load_sem,
    store_sem,
    link_sem,
    sent_f,
    arrived_f,
    sent_g,
    arrived_g,
    sent_t,
    arrived_t,
    sent_k,
    arrived_k,
):
    member = lax.axis_index("blk")
    partner = (lax.axis_index("dp"), 1 - member)
    chunks = tokens // CHUNK

    place = Place(pages)
    groups_f, groups_t, groups_k = sum_groups(pages)
    sum_f = PageSum(place, groups_f, "sides", rows_f, landing_f, whole_f, sent_f, arrived_f)
    sum_g = PageSum(place, groups_f, "sides", rows_g, landing_g, whole_g, sent_g, arrived_g)
    sum_t = PageSum(place, groups_t, "across", rows_t, landing_t, whole_t, sent_t, arrived_t)
    sum_k = PageSum(place, groups_k, "first", rows_k, landing_k, whole_k, sent_k, arrived_k)

    barrier = pltpu.get_barrier_semaphore()
    peers = [
        place.peer(group, hop)[0] for group in groups_k for hop in range(1, place.size(group))
    ]
    for peer in peers:
        pl.semaphore_signal(barrier, inc=1, device_id=peer, device_id_type=pl.DeviceIdType.MESH)

    load_memory = pltpu.make_async_copy(memory_hbm.at[0], memory_s, load_sem.at[0])
    load_ffn_in = pltpu.make_async_copy(ffn_in_hbm, ffn_in_s, load_sem.at[1])
    load_ffn_out = pltpu.make_async_copy(ffn_out_hbm, ffn_out_s, load_sem.at[2])
    load_memory.start()
    load_ffn_in.start()
    load_ffn_out.start()

    pairs = [attn_bias[j].astype(f32) for j in range(3)]
    bias = jnp.concatenate([pair[k : k + 1] for k in range(2) for pair in pairs], axis=0)
    gain = norm_gain[...].astype(f32)
    shift = norm_bias[...].astype(f32)

    order = order_in[...]
    turn = turns_in[0]
    row_at = order >> 7
    col_at = order & 127
    top = SIDE - 1
    row_new = jnp.where(
        turn == 0, row_at, jnp.where(turn == 1, col_at, jnp.where(turn == 2, top - row_at, top - col_at))
    )
    col_new = jnp.where(
        turn == 0, col_at, jnp.where(turn == 1, top - row_at, jnp.where(turn == 2, top - col_at, row_at))
    )
    past = jnp.where(order < lengths_in[0], 0, SIDE * SIDE)
    code_s[...] = (row_new * SIDE + col_new + past).astype(f32)

    pad_s[...] = jnp.zeros_like(pad_s)
    pad_s[0, :NQ] = queries_in[0].astype(f32)
    pad_s[1, :NQ] = pos_in[...].astype(f32)
    pad_s[2, :NQ] = out_grad_in[0].astype(f32)
    queries_f = pad_s[0]
    pos_f = pad_s[1]
    queries_b = queries_f.astype(bf16)
    mixed_q = (queries_f + pos_f).astype(bf16)
    query_self = (dot(mixed_q, attn_in[0, 0]) + bias[0:1]).astype(bf16)
    key_self = dot(mixed_q, attn_in[0, 1]).astype(bf16)
    value_self = (dot(queries_b, attn_in[0, 2]) + bias[1:2]).astype(bf16)
    scores = dot(key_self, spread_cols(query_self.astype(f32).T)) * scale
    own_key = lax.broadcasted_iota(jnp.int32, (NP, HQ), 0) < NQ
    scores = jnp.where(own_key, scores, masked_score)
    raised = jnp.exp(scores - jnp.max(scores, axis=0, keepdims=True))
    probs_self = raised / jnp.sum(raised, axis=0, keepdims=True)
    probs_self_b = probs_self.astype(bf16)
    value_t = value_self.astype(f32).T.astype(bf16)
    attended = own_blocks(
        [dot(value_t[pair_rows(p)], probs_self_b[:, pair_cols(p)]) for p in range(4)]
    ).T.astype(bf16)
    first_normed, first_rstd = norm_forward(queries_f + dot(attended, attn_out[0]) + bias[2:3])
    first = first_normed * gain[0:1] + shift[0:1]
    cross_q = (first + pos_f).astype(bf16)
    query_c = (dot(cross_q, attn_in[1, 0]) + bias[3:4]).astype(bf16)
    query_x[...] = spread_rows(query_c.astype(f32))
    query_xt = spread_cols(query_c.astype(f32).T)
    aux_row = jnp.where(
        lax.broadcasted_iota(jnp.int32, (NP, HQ // 2), 0) == 0, 1.0, 0.0
    ).astype(bf16)
    for g in range(2):
        weight_s[g, :NP] = query_xt[NP * g : NP * g + NP, HQ // 2 * g : HQ // 2 * (g + 1)]
        weight_s[g, NP:] = aux_row
    back_w[:D] = attn_in[1, 1].astype(f32).T.astype(bf16)
    back_w[D:] = attn_in[1, 2].astype(f32).T.astype(bf16)

    table = table_in[...]
    nothing = jnp.zeros((SIDE, D // 2), f32)
    table = jnp.concatenate(
        [jnp.concatenate([table, nothing], axis=1), jnp.concatenate([nothing, table], axis=1)], axis=0
    )
    table_high = table.astype(bf16)
    table_s[0] = table_high
    table_s[1] = (table - table_high.astype(f32)).astype(bf16)

    load_memory.wait()
    lane = lax.broadcasted_iota(jnp.int32, (CHUNK, NP), 1)
    value_bias = bias[4:5]

    @pl.loop(0, chunks)
    def _(i):
        rows = pl.ds(pl.multiple_of(i * CHUNK, CHUNK), CHUNK)
        line = code_s[:, rows]
        code = jnp.concatenate(
            [
                jnp.broadcast_to(line[:, NP * j : NP * j + NP], (NP, NP)).T
                for j in range(CHUNK // NP)
            ],
            axis=0,
        ).astype(jnp.int32)
        row_hot = jnp.where(((code >> 7) & 127) == lane, 1.0, 0.0)
        col_hot = jnp.where((code & 127) == lane, 1.0, 0.0)
        hot = jnp.concatenate([row_hot, col_hot], axis=1).astype(bf16)
        aux_s[rows] = jnp.where((code >= SIDE * SIDE) & (lane == 0), masked_score, 0.0).astype(bf16)
        block = memory_s[rows]
        positions = dot(hot, table_s[0]) + dot(hot, table_s[1])
        key_in = (block.astype(f32) + positions).astype(bf16)
        key_in_s[rows] = key_in
        key_s[rows] = dot(key_in, attn_in[1, 1]).astype(bf16)
        value_s[rows] = (dot(block, attn_in[1, 2]) + value_bias).astype(bf16)

    def score_chunk(i, out):
        rows = pl.ds(pl.multiple_of(i * CHUNK, CHUNK), CHUNK)
        for g in range(2):
            left = jnp.concatenate([key_s[rows, NP * g : NP * g + NP], aux_s[rows]], axis=1)
            out[:, HQ // 2 * g : HQ // 2 * (g + 1)] = dot(left, weight_s[g])

    def attend_chunk(i, scored):
        rows = pl.ds(pl.multiple_of(i * CHUNK, CHUNK), CHUNK)
        value_ct = value_s[rows].T
        for p in range(4):
            cols = pair_cols(p)
            before = total_s[0:1, cols]
            part = scored[:, cols]
            highest = jnp.maximum(
                before, jnp.max(part, axis=0, keepdims=True) * (scale * log2e)
            )
            raised = jnp.exp2(part * (scale * log2e) - highest)
            fade = jnp.exp2(before - highest)
            total_s[0:1, cols] = highest
            total_s[1:2, cols] = total_s[1:2, cols] * fade + jnp.sum(raised, axis=0, keepdims=True)
            shifts_s[pl.ds(i, 1), cols] = highest
            raised_b = raised.astype(bf16)
            probs_s[rows, cols] = raised_b
            mixed_s[pair_rows(p)] = mixed_s[pair_rows(p)] * fade + dot(
                value_ct[pair_rows(p)], raised_b
            )

    total_s[0:1] = jnp.full((1, HQ), -3e38, f32)
    total_s[1:2] = jnp.zeros((1, HQ), f32)
    mixed_s[...] = jnp.zeros_like(mixed_s)
    score_chunk(0, score_a)

    @pl.loop(0, chunks // 2)
    def _(j):
        i = j * 2
        score_chunk(i + 1, score_b)
        attend_chunk(i, score_a)
        score_chunk(jnp.minimum(i + 2, chunks - 1), score_a)
        attend_chunk(i + 1, score_b)

    send_a[:D] = own_blocks([mixed_s[pair_rows(p)] for p in range(4)])
    send_a[D : D + HEADS] = head_rows(total_s[0:1])
    send_a[D + HEADS :] = head_rows(total_s[1:2])
    pl.semaphore_wait(barrier, len(peers))
    swap_a = pltpu.make_async_remote_copy(
        src_ref=send_a,
        dst_ref=recv_a,
        send_sem=link_sem.at[0],
        recv_sem=link_sem.at[1],
        device_id=partner,
        device_id_type=pl.DeviceIdType.MESH,
    )
    swap_a.start()
    swap_a.wait()
    is_first = member == 0
    own = send_a[...]
    other = recv_a[...]
    left = jnp.where(is_first, own, other)
    right = jnp.where(is_first, other, own)
    high_l, high_r = left[D : D + HEADS], right[D : D + HEADS]
    highest = jnp.maximum(high_l, high_r)
    fade_l = jnp.exp2(high_l - highest)
    fade_r = jnp.exp2(high_r - highest)
    total = left[D + HEADS :] * fade_l + right[D + HEADS :] * fade_r
    mixed_t = left[:D] * per_channel(fade_l / total) + right[:D] * per_channel(fade_r / total)
    log_total = head_line(highest + jnp.log2(total))
    factor_s[...] = jnp.exp2(shifts_s[...] - log_total)
    attended_c = mixed_t.T.astype(bf16)

    second_normed, second_rstd = norm_forward(first + dot(attended_c, attn_out[1]) + bias[5:6])
    second = second_normed * gain[1:2] + shift[1:2]
    ffn_input = second.astype(bf16)
    load_ffn_in.wait()
    hidden = dot(ffn_input, ffn_in_s[...]) + ffn_in_bias[...].astype(f32).reshape(1, FF)
    half_gate = 0.5 + 0.5 * lax.erf(hidden * math.sqrt(0.5))
    activated = (hidden * half_gate).astype(bf16)
    gate_s[...] = half_gate + hidden * jnp.exp(hidden * hidden * -0.5) * (1.0 / math.sqrt(2.0 * math.pi))
    load_ffn_out.wait()
    third_normed, third_rstd = norm_forward(
        second + dot(activated, ffn_out_s[...]) + ffn_out_bias[...].astype(f32).reshape(1, D)
    )
    result_out[...] = (third_normed * gain[2:3] + shift[2:3])[:NQ].astype(bf16)
    grad_third, gain_grad_2, shift_grad_2 = norm_backward(
        pad_s[2], third_normed, third_rstd, gain[2:3]
    )
    grad_branch_f = grad_third.astype(bf16)
    grad_hidden = (dot_nt(grad_branch_f, ffn_out_s[...]) * gate_s[...]).astype(bf16)
    grad_second = grad_third + dot_nt(grad_hidden, ffn_in_s[...])
    grad_second_in, gain_grad_1, shift_grad_1 = norm_backward(
        grad_second, second_normed, second_rstd, gain[1:2]
    )
    grad_branch_c = grad_second_in.astype(bf16)
    blocks = FF // D
    ffn_input_t = second.T.astype(bf16)

    def ffn_rows(target, first):
        @pl.when(member == 0)
        def _():
            for j in range(blocks // 2):
                cols = slice(D * (first + j), D * (first + j) + D)
                target[D * j : D * j + D] = dot(ffn_input_t, grad_hidden[:, cols]).astype(bf16)

        @pl.when(member == 1)
        def _():
            for j in range(blocks // 2):
                cols = slice(D * (first + j), D * (first + j) + D)
                target[D * j : D * j + D] = dot_tn(activated[:, cols], grad_branch_f).astype(bf16)

    ffn_rows(rows_f, 0)
    sum_f.phases[0]()
    ffn_rows(rows_g, blocks // 2)

    @pl.when(member == 0)
    def _():
        rows_g[ROWS_F:ROWS_G] = dot_tn(attended_c[:, : D // 2], grad_branch_c).astype(bf16)

    @pl.when(member == 1)
    def _():
        rows_g[ROWS_F:ROWS_G] = dot_tn(attended_c[:, D // 2 :], grad_branch_c).astype(bf16)

    clear_rest(rows_f, ROWS_F)
    clear_rest(rows_g, ROWS_G)
    clear_rest(rows_t, ROWS_T)
    clear_rest(rows_k, ROWS_K)
    sum_g.phases[0]()
    grad_attended_c = dot_nt(grad_branch_c, attn_out[1]).astype(bf16).astype(f32)
    hidden_sum = row_total(grad_hidden)
    small_s[:16] = jnp.concatenate(
        [hidden_sum[:, D * j : D * j + D] for j in range(FF // D)]
        + [
            row_total(grad_branch_f),
            row_total(grad_branch_c),
            gain_grad_2,
            shift_grad_2,
            gain_grad_1,
            shift_grad_1,
            row_total(grad_attended_c),
            jnp.zeros((1, D), f32),
        ],
        axis=0,
    )

    grad_attended_t = grad_attended_c.T
    grad_xt[...] = spread_cols(grad_attended_t)
    grad_x[...] = spread_rows(grad_attended_c)
    inner = head_line(head_sums(grad_attended_t * mixed_t))
    mixed_s[...] = jnp.zeros_like(mixed_s)
    key_grads[...] = jnp.zeros_like(key_grads)

    def in_turn(i, phases):
        for k, phase in enumerate(phases):
            pl.when(i == chunks * (k + 1) // (len(phases) + 1))(phase)

    mixed_phases = [phase for pair in zip(sum_f.phases[1:], sum_g.phases[1:]) for phase in pair]

    @pl.loop(0, chunks)
    def _(i):
        rows = pl.ds(pl.multiple_of(i * CHUNK, CHUNK), CHUNK)
        key_ct = key_s[rows].T
        value_c = value_s[rows]
        weights = []
        for p in range(4):
            cols = pair_cols(p)
            grad_probs = dot(value_c, grad_xt[:, cols])
            probs = probs_s[rows, cols].astype(f32) * factor_s[pl.ds(i, 1), cols]
            grad_scores = (probs * (grad_probs - inner[:, cols])).astype(bf16)
            mixed_s[pair_rows(p)] += dot(key_ct[pair_rows(p)], grad_scores)
            probs_s[rows, cols] = grad_scores
            weights.append(probs.astype(bf16))
        grad_value = dot(jnp.concatenate(weights, axis=1), grad_x[...]).astype(bf16)
        value_s[rows] = grad_value
        key_grads[D:] += dot_tn(memory_s[rows], grad_value)
        in_turn(i, mixed_phases[:-2])

    send_b[...] = own_blocks([mixed_s[pair_rows(p)] for p in range(4)]) * scale
    swap_b = pltpu.make_async_remote_copy(
        src_ref=send_b,
        dst_ref=recv_b,
        send_sem=link_sem.at[2],
        recv_sem=link_sem.at[3],
        device_id=partner,
        device_id_type=pl.DeviceIdType.MESH,
    )
    swap_b.start()
    swap_b.wait()
    grad_query_c = (send_b[...] + recv_b[...]).T.astype(bf16)

    cross_pos_grad = dot_nt(grad_query_c, attn_in[1, 0])
    grad_first_in, gain_grad_0, shift_grad_0 = norm_backward(
        grad_second_in + cross_pos_grad, first_normed, first_rstd, gain[0:1]
    )
    grad_branch = grad_first_in.astype(bf16)
    grad_attended = dot_nt(grad_branch, attn_out[0]).astype(bf16).astype(f32)
    grad_probs = dot(value_self, spread_cols(grad_attended.T))
    inner_self = jnp.sum(probs_self * grad_probs, axis=0, keepdims=True)
    grad_scores = (probs_self * (grad_probs - inner_self)).astype(bf16)
    key_t = key_self.astype(f32).T.astype(bf16)
    grad_query_s = (
        own_blocks([dot(key_t[pair_rows(p)], grad_scores[:, pair_cols(p)]) for p in range(4)]) * scale
    ).T.astype(bf16)
    grad_key_s = (dot(grad_scores, spread_rows(query_self.astype(f32))) * scale).astype(bf16)
    grad_value_s = dot(probs_self_b, spread_rows(grad_attended)).astype(bf16)
    grad_mixed_q = dot_nt(grad_query_s, attn_in[0, 0]) + dot_nt(grad_key_s, attn_in[0, 1])
    queries_grad_out[...] = (grad_first_in + grad_mixed_q + dot_nt(grad_value_s, attn_in[0, 2]))[
        :NQ
    ].astype(bf16)
    small_s[16:] = jnp.concatenate(
        [
            row_total(grad_query_s),
            row_total(grad_value_s),
            row_total(grad_branch),
            row_total(grad_query_c),
            gain_grad_0,
            shift_grad_0,
            jnp.zeros((10, D), f32),
        ],
        axis=0,
    )
    @pl.when(member == 0)
    def _():
        rows_t[:D] = dot_tn(mixed_q, grad_query_s).astype(bf16)
        rows_t[D : 2 * D] = dot_tn(mixed_q, grad_key_s).astype(bf16)
        rows_t[2 * D : 3 * D] = dot_tn(queries_b, grad_value_s).astype(bf16)

    @pl.when(member == 1)
    def _():
        rows_t[:D] = dot_tn(cross_q, grad_query_c).astype(bf16)
        rows_t[D : 2 * D] = dot_tn(attended, grad_branch).astype(bf16)
        rows_t[ROW_POS:ROW_SMALL] = (grad_mixed_q + cross_pos_grad).astype(bf16)
        rows_t[ROW_SMALL : ROW_SMALL + 32] = small_s[...].astype(bf16)
        rows_t[ROW_SMALL + 32 : ROWS_T] = jnp.zeros((ROWS_T - ROW_SMALL - 32, D), bf16)

    sum_t.phases[0]()

    @pl.loop(0, chunks)
    def _(i):
        rows = pl.ds(pl.multiple_of(i * CHUNK, CHUNK), CHUNK)
        grad_key = (dot(probs_s[rows], query_x[...]) * scale).astype(bf16)
        key_s[rows] = grad_key
        key_grads[:D] += dot_tn(key_in_s[rows], grad_key)
        in_turn(i, sum_t.phases[1:2])

    rows_k[:ROWS_K] = key_grads[...].astype(bf16)
    sum_k.phases[0]()
    sum_t.phases[2]()

    @pl.loop(0, chunks)
    def _(i):
        rows = pl.ds(pl.multiple_of(i * CHUNK, CHUNK), CHUNK)
        both = jnp.concatenate([key_s[rows], value_s[rows]], axis=1)
        memory_s[rows] = dot(both, back_w[...]).astype(bf16)
        pltpu.make_async_copy(memory_s.at[rows], memory_grad_hbm.at[0, rows], store_sem.at[i]).start()

    sum_k.phases[1]()
    sum_t.phases[3]()
    mixed_phases[-2]()
    mixed_phases[-1]()
    stores = [
        pltpu.make_async_copy(whole, target, load_sem.at[3 + k])
        for k, (whole, target) in enumerate(
            (
                (whole_f, whole_f_hbm),
                (whole_g, whole_g_hbm),
                (whole_t, whole_t_hbm),
                (whole_k, whole_k_hbm),
            )
        )
    ]
    stores[0].start()
    stores[1].start()
    for k in range(2, len(sum_k.phases)):
        sum_k.phases[k]()
        if k + 2 < len(sum_t.phases):
            sum_t.phases[k + 2]()
    stores[2].start()
    stores[3].start()

    @pl.loop(0, chunks)
    def _(i):
        rows = pl.ds(pl.multiple_of(i * CHUNK, CHUNK), CHUNK)
        pltpu.make_async_copy(memory_s.at[rows], memory_grad_hbm.at[0, rows], store_sem.at[i]).wait()

    for store in stores:
        store.wait()


def finish_kernel(
    result_in,
    queries_grad_in,
    memory_grad_in,
    whole_f,
    whole_g,
    whole_t,
    whole_k,
    result,
    queries_grad,
    memory_grad,
    attn_in_grad,
    attn_out_grad,
    attn_bias_grad,
    ffn_in_grad,
    ffn_in_bias_grad,
    ffn_out_grad,
    ffn_out_bias_grad,
    norm_gain_grad,
    norm_bias_grad,
    query_pos_grad,
    moved,
    in_sem,
    out_sem,
):
    pieces = in_sem.shape[0]
    piece = moved.shape[0] // pieces

    def fetch(j):
        rows = pl.ds(piece * j, piece)
        return pltpu.make_async_copy(memory_grad_in.at[0, rows], moved.at[rows], in_sem.at[j])

    def write(j):
        rows = pl.ds(piece * j, piece)
        return pltpu.make_async_copy(moved.at[rows], memory_grad.at[0, rows], out_sem.at[j])

    for j in range(pieces):
        fetch(j).start()
    result[0] = result_in[...]
    queries_grad[0] = queries_grad_in[...]
    for j in range(FF // D):
        piece_at = j % (FF // D // 2) * D
        sums = whole_f if j < FF // D // 2 else whole_g
        ffn_in_grad[:, D * j : D * j + D] = sums[0, piece_at : piece_at + D].astype(f32)
        ffn_out_grad[D * j : D * j + D] = sums[1, piece_at : piece_at + D].astype(f32)
    for j in range(pieces):
        fetch(j).wait()
        write(j).start()
    attn_out_grad[0] = whole_t[1, D : 2 * D].astype(f32)
    attn_out_grad[1, : D // 2] = whole_g[0, ROWS_F:ROWS_G].astype(f32)
    attn_out_grad[1, D // 2 :] = whole_g[1, ROWS_F:ROWS_G].astype(f32)
    for j in range(3):
        attn_in_grad[0, j] = whole_t[0, D * j : D * j + D].astype(f32)
    attn_in_grad[1, 0] = whole_t[1, :D].astype(f32)
    attn_in_grad[1, 1] = whole_k[:D].astype(f32)
    attn_in_grad[1, 2] = whole_k[D : 2 * D].astype(f32)
    query_pos_grad[...] = whole_t[1, ROW_POS:ROW_SMALL].astype(f32)[:NQ]
    small = whole_t[1, ROW_SMALL : ROW_SMALL + 32].astype(f32)
    ffn_in_bias_grad[...] = jnp.concatenate([small[j : j + 1] for j in range(FF // D)], axis=1)
    ffn_out_bias_grad[...] = small[8:9]
    for j, (own, cross) in enumerate(((16, 19), (17, 14), (18, 9))):
        attn_bias_grad[j, 0:1] = small[own : own + 1]
        attn_bias_grad[j, 1:2] = small[cross : cross + 1]
    norm_gain_grad[0:1] = small[20:21]
    norm_gain_grad[1:2] = small[12:13]
    norm_gain_grad[2:3] = small[10:11]
    norm_bias_grad[0:1] = small[21:22]
    norm_bias_grad[1:2] = small[13:14]
    norm_bias_grad[2:3] = small[11:12]
    for j in range(pieces):
        write(j).wait()


def body(
    pages,
    queries,
    memory,
    quarter_turns,
    token_order,
    lengths,
    attn_in,
    attn_out,
    attn_bias,
    ffn_in,
    ffn_in_bias,
    ffn_out,
    ffn_out_bias,
    norm_gain,
    norm_bias,
    query_pos,
    out_grad,
):
    tokens = memory.shape[1]
    chunks = tokens // CHUNK
    groups_f, groups_t, groups_k = sum_groups(pages)
    summed = [
        (padded(ROWS_F, pages), groups_f),
        (padded(ROWS_G, pages), groups_f),
        (padded(ROWS_T, pages), groups_t),
        (padded(ROWS_K, 2 * pages), groups_k),
    ]
    whole_shapes = [(2, rows, D) for rows, _ in summed[:3]] + [(summed[3][0], D)]
    sum_buffers = []
    for (rows, groups), shape in zip(summed, whole_shapes):
        landing = PageSum.landing_rows(pages, groups, rows)
        sum_buffers += [pltpu.VMEM(each, bf16) for each in ((rows, D), (landing, D), shape)]
    copies = 32
    vmem = pl.BlockSpec(memory_space=pltpu.VMEM)
    smem = pl.BlockSpec(memory_space=pltpu.SMEM)
    anywhere = pl.BlockSpec(memory_space=pl.ANY)
    parts = pl.pallas_call(
        functools.partial(layer_kernel, tokens, pages),
        out_shape=[
            jax.ShapeDtypeStruct((NQ, D), bf16),
            jax.ShapeDtypeStruct((NQ, D), bf16),
            jax.ShapeDtypeStruct((1, tokens, D), bf16),
            *(jax.ShapeDtypeStruct(shape, bf16) for shape in whole_shapes),
        ],
        in_specs=[
            vmem,
            anywhere,
            smem,
            vmem,
            smem,
            vmem,
            vmem,
            vmem,
            anywhere,
            vmem,
            anywhere,
            vmem,
            vmem,
            vmem,
            vmem,
            vmem,
            vmem,
        ],
        out_specs=[vmem, vmem, anywhere, anywhere, anywhere, anywhere, anywhere],
        scratch_shapes=[
            pltpu.VMEM((tokens, D), bf16),
            pltpu.VMEM((tokens, D), bf16),
            pltpu.VMEM((tokens, D), bf16),
            pltpu.VMEM((tokens, D), bf16),
            pltpu.VMEM((tokens, NP), bf16),
            pltpu.VMEM((tokens, HQ), bf16),
            pltpu.VMEM((1, tokens), f32),
            pltpu.VMEM((CHUNK, HQ), f32),
            pltpu.VMEM((CHUNK, HQ), f32),
            pltpu.VMEM((2, D, HQ // 2), bf16),
            pltpu.VMEM((2, 2 * SIDE, D), bf16),
            pltpu.VMEM((chunks, HQ), f32),
            pltpu.VMEM((chunks, HQ), f32),
            pltpu.VMEM((8, HQ), f32),
            pltpu.VMEM((D, PAIR), f32),
            pltpu.VMEM((D, FF), bf16),
            pltpu.VMEM((FF, D), bf16),
            pltpu.VMEM((NP, FF), f32),
            pltpu.VMEM((3, NP, D), f32),
            pltpu.VMEM((2 * D, D), bf16),
            pltpu.VMEM((HQ, D), bf16),
            pltpu.VMEM((D, HQ), bf16),
            pltpu.VMEM((HQ, D), bf16),
            pltpu.VMEM((D + 2 * HEADS, NP), f32),
            pltpu.VMEM((D + 2 * HEADS, NP), f32),
            pltpu.VMEM((D, NP), f32),
            pltpu.VMEM((D, NP), f32),
            pltpu.VMEM((2 * D, D), f32),
            pltpu.VMEM((32, D), f32),
            *sum_buffers,
            pltpu.SemaphoreType.DMA((7,)),
            pltpu.SemaphoreType.DMA((chunks,)),
            pltpu.SemaphoreType.DMA((4,)),
            *[pltpu.SemaphoreType.DMA((copies,))] * 8,
        ],
        compiler_params=pltpu.CompilerParams(
            collective_id=0, has_side_effects=True, vmem_limit_bytes=62 * 1024 * 1024
        ),
        cost_estimate=pl.CostEstimate(
            flops=2 * 8 * tokens * HQ * D, bytes_accessed=20 << 20, transcendentals=tokens * HQ
        ),
        name="decoder_layer",
    )(
        queries,
        memory,
        quarter_turns,
        token_order,
        lengths,
        attn_in,
        attn_out,
        attn_bias.transpose(1, 0, 2),
        ffn_in,
        ffn_in_bias,
        ffn_out,
        ffn_out_bias,
        norm_gain,
        norm_bias,
        query_pos,
        out_grad,
        jnp.asarray(position_table()),
    )
    outs = pl.pallas_call(
        finish_kernel,
        out_shape=[
            jax.ShapeDtypeStruct((1, NQ, D), bf16),
            jax.ShapeDtypeStruct((1, NQ, D), bf16),
            jax.ShapeDtypeStruct((1, tokens, D), bf16),
            jax.ShapeDtypeStruct((2, 3, D, D), f32),
            jax.ShapeDtypeStruct((2, D, D), f32),
            jax.ShapeDtypeStruct((3, 2, D), f32),
            jax.ShapeDtypeStruct((D, FF), f32),
            jax.ShapeDtypeStruct((1, FF), f32),
            jax.ShapeDtypeStruct((FF, D), f32),
            jax.ShapeDtypeStruct((1, D), f32),
            jax.ShapeDtypeStruct((3, D), f32),
            jax.ShapeDtypeStruct((3, D), f32),
            jax.ShapeDtypeStruct((NQ, D), f32),
        ],
        in_specs=[vmem, vmem, anywhere, vmem, vmem, vmem, vmem],
        out_specs=[vmem, vmem, anywhere] + [vmem] * 10,
        scratch_shapes=[
            pltpu.VMEM((tokens, D), bf16),
            pltpu.SemaphoreType.DMA((8,)),
            pltpu.SemaphoreType.DMA((8,)),
        ],
        compiler_params=pltpu.CompilerParams(vmem_limit_bytes=62 * 1024 * 1024),
        name="write_outputs",
    )(*parts)
    return (
        *outs[:5],
        outs[5].transpose(1, 0, 2),
        outs[6],
        outs[7].reshape(FF),
        outs[8],
        outs[9].reshape(D),
        *outs[10:],
    )


def solution(mesh):
    in_specs = (
        P("dp", None, None),
        P("dp", "blk", None),
        P("dp"),
        P("dp", "blk"),
        P("dp"),
        P(),
        P(),
        P(),
        P(),
        P(),
        P(),
        P(),
        P(),
        P(),
        P(),
        P("dp", None, None),
    )
    out_specs = (
        P("dp", None, None),
        P("dp", None, None),
        P("dp", "blk", None),
        P(),
        P(),
        P(),
        P(),
        P(),
        P(),
        P(),
        P(),
        P(),
        P(),
    )
    layer = functools.partial(body, mesh.shape["dp"])
    return jax.shard_map(layer, mesh=mesh, in_specs=in_specs, out_specs=out_specs, check_vma=False)
```

```python
import functools
import math

import jax
import jax.numpy as jnp
import numpy as np
from jax import lax
from jax.experimental import pallas as pl
from jax.experimental.pallas import tpu as pltpu
from jax.sharding import PartitionSpec as P

D = 256
HEADS = 8
HD = D // HEADS
SIDE = 128
NQ = 125
NP = 128
HQ = HEADS * NP
PAIR = 2 * NP
FF = 2048
CHUNK = 512

masked_score = -1e30
norm_eps = 1e-05
scale = 1.0 / math.sqrt(HD)
log2e = math.log2(math.e)

bf16 = jnp.bfloat16
f32 = jnp.float32

ROWS_F = FF // 2
ROWS_G = FF // 2 + D // 2
ROW_POS = 2 * D
ROW_SMALL = 2 * D + NP
ROWS_T = 3 * D
ROWS_K = 2 * D
TILE = 16


def axes_of(pages):
    axes = {"core": (2, 1), "y": (2, 2)}
    stride = 4
    while stride < pages:
        radix = 4 if pages // stride % 4 == 0 else 2
        axes["z%d" % (len(axes) - 2)] = (radix, stride)
        stride *= radix
    axes["x"] = (2, 0)
    return axes


def far_axes(pages):
    return [(name,) for name in axes_of(pages) if name.startswith("z")]


def sum_groups(pages):
    far = far_axes(pages)
    return [("core",), ("y",), *far], [("core", "y"), *far], [("x", "core", "y"), *far]


def padded(rows, pages):
    unit = TILE * pages
    return (rows + unit - 1) // unit * unit


def position_table():
    half = D // 2
    channel = np.arange(half)
    inverse = np.exp((channel // 2).astype(np.float32) * np.float32(-2.0 * math.log(10000.0) / half))
    angle = (np.arange(SIDE, dtype=np.float32) + 1.0) * np.float32(2.0 * math.pi / SIDE)
    angle = angle[:, None] * inverse
    return np.where(channel % 2 == 0, np.sin(angle), np.cos(angle)).astype(np.float32)


def dot(a, b):
    return jnp.dot(a, b, preferred_element_type=f32)


def dot_nt(a, b):
    return lax.dot_general(a, b, (((1,), (1,)), ((), ())), preferred_element_type=f32)


def dot_tn(a, b):
    return lax.dot_general(a, b, (((0,), (0,)), ((), ())), preferred_element_type=f32)


def row_total(values):
    return jnp.sum(values.astype(f32), axis=0, keepdims=True)


def norm_forward(values):
    average = jnp.mean(values, axis=-1, keepdims=True)
    centred = values - average
    variance = jnp.mean(centred * centred, axis=-1, keepdims=True)
    rstd = lax.rsqrt(variance + norm_eps)
    return centred * rstd, rstd


def norm_backward(grad, normed, rstd, gain):
    grad_normed = grad * gain
    first = jnp.mean(grad_normed, axis=-1, keepdims=True)
    second = jnp.mean(grad_normed * normed, axis=-1, keepdims=True)
    grad_in = rstd * (grad_normed - first - normed * second)
    return grad_in, row_total(grad * normed), row_total(grad)


def spread_rows(rows):
    head = lax.broadcasted_iota(jnp.int32, (NP, D), 1) // HD
    return jnp.concatenate(
        [jnp.where(head == h, rows, 0.0) for h in range(HEADS)], axis=0
    ).astype(bf16)


def spread_cols(cols):
    head = lax.broadcasted_iota(jnp.int32, (D, NP), 0) // HD
    return jnp.concatenate(
        [jnp.where(head == h, cols, 0.0) for h in range(HEADS)], axis=1
    ).astype(bf16)


def own_blocks(pairs):
    parts = []
    for pair in pairs:
        parts += [pair[:HD, :NP], pair[HD:, NP:]]
    return jnp.concatenate(parts, axis=0)


def head_rows(row):
    return jnp.concatenate([row[:, NP * h : NP * h + NP] for h in range(HEADS)], axis=0)


def head_line(rows):
    return jnp.concatenate([rows[h : h + 1] for h in range(HEADS)], axis=1)


def per_channel(rows):
    return jnp.concatenate(
        [jnp.broadcast_to(rows[h : h + 1], (HD, NP)) for h in range(HEADS)], axis=0
    )


def head_sums(cols):
    return jnp.concatenate(
        [jnp.sum(cols[HD * h : HD * h + HD], axis=0, keepdims=True) for h in range(HEADS)], axis=0
    )


def pair_cols(p):
    return slice(PAIR * p, PAIR * p + PAIR)


def pair_rows(p):
    return slice(2 * HD * p, 2 * HD * p + 2 * HD)


class Place:
    def __init__(self, pages):
        self.axes = axes_of(pages)
        self.page = lax.axis_index("dp")
        self.member = lax.axis_index("blk")
        self.digit = {
            name: self.member if name == "x" else lax.rem(self.page // stride, radix)
            for name, (radix, stride) in self.axes.items()
        }

    def size(self, group):
        return math.prod(self.axes[name][0] for name in group)

    def index(self, group):
        index = 0
        for name in group:
            index = index * self.axes[name][0] + self.digit[name]
        return index

    def peer(self, group, hop):
        index = lax.rem(self.index(group) + hop, self.size(group))
        page, member, rest = self.page, self.member, index
        for name in reversed(group):
            radix, stride = self.axes[name]
            digit = lax.rem(rest, radix)
            rest = rest // radix
            if name == "x":
                member = digit
            else:
                page = page + (digit - self.digit[name]) * stride
        return (page, member), index


class PageSum:
    def __init__(self, place, groups, back, rows, landing, whole, sent, arrived):
        self.place, self.groups, self.back = place, groups, back
        self.rows, self.landing, self.whole = rows, landing, whole
        self.sent, self.arrived = sent, arrived
        self.slots = 0
        self.extents = [rows.shape[0]]
        self.bases = [0]
        self.landings = []
        at = 0
        for group in groups:
            size = place.size(group)
            extent = self.extents[-1] // size
            self.landings.append(at)
            at += (size - 1) * extent
            self.bases.append(pl.multiple_of(self.bases[-1] + place.index(group) * extent, TILE))
            self.extents.append(extent)
        last = len(groups)
        moves = [self.scatter_moves(s) for s in range(last)]
        near = 2 if len(groups[0]) == 1 else 1
        moves += [self.gather_moves(s) for s in range(last - 1, near - 1, -1)]
        if back == "first":
            moves.append(self.gather_moves(0))
        elif back == "sides":
            moves += [self.side_moves(), self.corner_moves(), self.core_moves()]
        else:
            moves += [self.across_moves(), self.core_moves()]
        self.phases = [functools.partial(self.step, moves, k) for k in range(len(moves) + 1)]

    @staticmethod
    def landing_rows(pages, groups, rows):
        axes = axes_of(pages)
        total, extent = 0, rows
        for group in groups:
            size = math.prod(axes[name][0] for name in group)
            extent //= size
            total += (size - 1) * extent
        return total

    def step(self, moves, k):
        last = len(self.groups)
        if k > 0:
            for move in moves[k - 1]:
                self.copy(*move).wait()
        if 0 < k <= last:
            total = self.scatter_sum(k - 1)
            region = pl.ds(self.bases[k], self.extents[k])
            if k < last:
                self.rows[region] = total
            elif len(self.whole.shape) == 3:
                self.whole[self.place.member, region] = total
            else:
                self.whole[region] = total
        if k < len(moves):
            for move in moves[k]:
                self.copy(*move).start()

    def copy(self, slot, source, target, device):
        return pltpu.make_async_remote_copy(
            src_ref=source(),
            dst_ref=target(),
            send_sem=self.sent.at[slot],
            recv_sem=self.arrived.at[slot],
            device_id=device,
            device_id_type=pl.DeviceIdType.MESH,
        )

    def new_slot(self):
        self.slots += 1
        return self.slots - 1

    def same(self, device, view):
        return (self.new_slot(), view, view, device)

    def scatter_moves(self, step):
        group = self.groups[step]
        extent = self.extents[step + 1]
        moves = []
        for hop in range(1, self.place.size(group)):
            device, other = self.place.peer(group, hop)
            start = pl.multiple_of(self.bases[step] + other * extent, TILE)
            landing = self.landings[step] + (hop - 1) * extent
            moves.append(
                (
                    self.new_slot(),
                    functools.partial(self.part, self.rows, start, extent),
                    functools.partial(self.part, self.landing, landing, extent),
                    device,
                )
            )
        return moves

    @staticmethod
    def part(ref, start, extent):
        return ref.at[pl.ds(start, extent)]

    def half(self, member, start, extent):
        if len(self.whole.shape) == 3:
            return self.whole.at[member, pl.ds(start, extent)]
        return self.whole.at[pl.ds(start, extent)]

    def scatter_sum(self, step):
        extent = self.extents[step + 1]
        total = self.rows[pl.ds(self.bases[step + 1], extent)].astype(f32)
        for hop in range(1, self.place.size(self.groups[step])):
            landing = self.landings[step] + (hop - 1) * extent
            total = total + self.landing[pl.ds(landing, extent)].astype(f32)
        return total.astype(bf16)

    def gather_moves(self, step):
        group = self.groups[step]
        view = functools.partial(self.half, self.place.member, self.bases[step + 1], self.extents[step + 1])
        return [
            self.same(self.place.peer(group, hop)[0], view) for hop in range(1, self.place.size(group))
        ]

    def own_quarter(self):
        step = 2 if len(self.groups[0]) == 1 else 1
        return self.bases[step], self.extents[step]

    def side_moves(self):
        view = functools.partial(self.half, self.place.member, *self.own_quarter())
        return [self.same(self.place.peer((name,), 1)[0], view) for name in ("y", "x")]

    def corner_moves(self):
        base, extent = self.own_quarter()
        half = extent // 2
        other = pl.multiple_of(base + (1 - 2 * self.place.digit["y"]) * extent, TILE)
        first = functools.partial(self.half, self.place.member, other, half)
        second = functools.partial(
            self.half, 1 - self.place.member, pl.multiple_of(base + half, TILE), half
        )
        return [
            self.same(self.place.peer(("x",), 1)[0], first),
            self.same(self.place.peer(("y",), 1)[0], second),
        ]

    def across_moves(self):
        view = functools.partial(self.half, self.place.member, *self.own_quarter())
        return [self.same(self.place.peer(("x", "y"), hop)[0], view) for hop in range(1, 4)]

    def core_moves(self):
        extent = self.extents[0] // 2
        start = pl.multiple_of(self.place.digit["core"] * extent, TILE)
        device, _ = self.place.peer(("core",), 1)
        return [self.same(device, functools.partial(self.half, m, start, extent)) for m in range(2)]


def clear_rest(ref, used):
    if ref.shape[0] > used:
        ref[used:] = jnp.zeros((ref.shape[0] - used, D), ref.dtype)


def layer_kernel(
    tokens,
    pages,
    queries_in,
    memory_hbm,
    turns_in,
    order_in,
    lengths_in,
    attn_in,
    attn_out,
    attn_bias,
    ffn_in_hbm,
    ffn_in_bias,
    ffn_out_hbm,
    ffn_out_bias,
    norm_gain,
    norm_bias,
    pos_in,
    out_grad_in,
    table_in,
    result_out,
    queries_grad_out,
    memory_grad_hbm,
    whole_f_hbm,
    whole_g_hbm,
    whole_t_hbm,
    whole_k_hbm,
    memory_s,
    key_in_s,
    key_s,
    value_s,
    aux_s,
    probs_s,
    code_s,
    score_a,
    score_b,
    weight_s,
    table_s,
    shifts_s,
    factor_s,
    total_s,
    mixed_s,
    ffn_in_s,
    ffn_out_s,
    gate_s,
    pad_s,
    back_w,
    query_x,
    grad_xt,
    grad_x,
    send_a,
    recv_a,
    send_b,
    recv_b,
    key_grads,
    small_s,
    rows_f,
    landing_f,
    whole_f,
    rows_g,
    landing_g,
    whole_g,
    rows_t,
    landing_t,
    whole_t,
    rows_k,
    landing_k,
    whole_k,
    load_sem,
    store_sem,
    link_sem,
    sent_f,
    arrived_f,
    sent_g,
    arrived_g,
    sent_t,
    arrived_t,
    sent_k,
    arrived_k,
):
    member = lax.axis_index("blk")
    partner = (lax.axis_index("dp"), 1 - member)
    chunks = tokens // CHUNK

    place = Place(pages)
    groups_f, groups_t, groups_k = sum_groups(pages)
    sum_f = PageSum(place, groups_f, "sides", rows_f, landing_f, whole_f, sent_f, arrived_f)
    sum_g = PageSum(place, groups_f, "sides", rows_g, landing_g, whole_g, sent_g, arrived_g)
    sum_t = PageSum(place, groups_t, "across", rows_t, landing_t, whole_t, sent_t, arrived_t)
    sum_k = PageSum(place, groups_k, "first", rows_k, landing_k, whole_k, sent_k, arrived_k)

    barrier = pltpu.get_barrier_semaphore()
    peers = [
        place.peer(group, hop)[0] for group in groups_k for hop in range(1, place.size(group))
    ]
    for peer in peers:
        pl.semaphore_signal(barrier, inc=1, device_id=peer, device_id_type=pl.DeviceIdType.MESH)

    load_memory = pltpu.make_async_copy(memory_hbm.at[0], memory_s, load_sem.at[0])
    load_ffn_in = pltpu.make_async_copy(ffn_in_hbm, ffn_in_s, load_sem.at[1])
    load_ffn_out = pltpu.make_async_copy(ffn_out_hbm, ffn_out_s, load_sem.at[2])
    load_memory.start()
    load_ffn_in.start()
    load_ffn_out.start()

    pairs = [attn_bias[j].astype(f32) for j in range(3)]
    bias = jnp.concatenate([pair[k : k + 1] for k in range(2) for pair in pairs], axis=0)
    gain = norm_gain[...].astype(f32)
    shift = norm_bias[...].astype(f32)

    order = order_in[...]
    turn = turns_in[0]
    row_at = order >> 7
    col_at = order & 127
    top = SIDE - 1
    row_new = jnp.where(
        turn == 0, row_at, jnp.where(turn == 1, col_at, jnp.where(turn == 2, top - row_at, top - col_at))
    )
    col_new = jnp.where(
        turn == 0, col_at, jnp.where(turn == 1, top - row_at, jnp.where(turn == 2, top - col_at, row_at))
    )
    past = jnp.where(order < lengths_in[0], 0, SIDE * SIDE)
    code_s[...] = (row_new * SIDE + col_new + past).astype(f32)

    pad_s[...] = jnp.zeros_like(pad_s)
    pad_s[0, :NQ] = queries_in[0].astype(f32)
    pad_s[1, :NQ] = pos_in[...].astype(f32)
    pad_s[2, :NQ] = out_grad_in[0].astype(f32)
    queries_f = pad_s[0]
    pos_f = pad_s[1]
    queries_b = queries_f.astype(bf16)
    mixed_q = (queries_f + pos_f).astype(bf16)
    query_self = (dot(mixed_q, attn_in[0, 0]) + bias[0:1]).astype(bf16)
    key_self = dot(mixed_q, attn_in[0, 1]).astype(bf16)
    value_self = (dot(queries_b, attn_in[0, 2]) + bias[1:2]).astype(bf16)
    scores = dot(key_self, spread_cols(query_self.astype(f32).T)) * scale
    own_key = lax.broadcasted_iota(jnp.int32, (NP, HQ), 0) < NQ
    scores = jnp.where(own_key, scores, masked_score)
    raised = jnp.exp(scores - jnp.max(scores, axis=0, keepdims=True))
    probs_self = raised / jnp.sum(raised, axis=0, keepdims=True)
    probs_self_b = probs_self.astype(bf16)
    value_t = value_self.astype(f32).T.astype(bf16)
    attended = own_blocks(
        [dot(value_t[pair_rows(p)], probs_self_b[:, pair_cols(p)]) for p in range(4)]
    ).T.astype(bf16)
    first_normed, first_rstd = norm_forward(queries_f + dot(attended, attn_out[0]) + bias[2:3])
    first = first_normed * gain[0:1] + shift[0:1]
    cross_q = (first + pos_f).astype(bf16)
    query_c = (dot(cross_q, attn_in[1, 0]) + bias[3:4]).astype(bf16)
    query_x[...] = spread_rows(query_c.astype(f32))
    query_xt = spread_cols(query_c.astype(f32).T)
    aux_row = jnp.where(
        lax.broadcasted_iota(jnp.int32, (NP, HQ // 2), 0) == 0, 1.0, 0.0
    ).astype(bf16)
    for g in range(2):
        weight_s[g, :NP] = query_xt[NP * g : NP * g + NP, HQ // 2 * g : HQ // 2 * (g + 1)]
        weight_s[g, NP:] = aux_row
    back_w[:D] = attn_in[1, 1].astype(f32).T.astype(bf16)
    back_w[D:] = attn_in[1, 2].astype(f32).T.astype(bf16)

    table = table_in[...]
    nothing = jnp.zeros((SIDE, D // 2), f32)
    table = jnp.concatenate(
        [jnp.concatenate([table, nothing], axis=1), jnp.concatenate([nothing, table], axis=1)], axis=0
    )
    table_high = table.astype(bf16)
    table_s[0] = table_high
    table_s[1] = (table - table_high.astype(f32)).astype(bf16)

    load_memory.wait()
    lane = lax.broadcasted_iota(jnp.int32, (CHUNK, NP), 1)
    value_bias = bias[4:5]

    @pl.loop(0, chunks)
    def _(i):
        rows = pl.ds(pl.multiple_of(i * CHUNK, CHUNK), CHUNK)
        line = code_s[:, rows]
        code = jnp.concatenate(
            [
                jnp.broadcast_to(line[:, NP * j : NP * j + NP], (NP, NP)).T
                for j in range(CHUNK // NP)
            ],
            axis=0,
        ).astype(jnp.int32)
        row_hot = jnp.where(((code >> 7) & 127) == lane, 1.0, 0.0)
        col_hot = jnp.where((code & 127) == lane, 1.0, 0.0)
        hot = jnp.concatenate([row_hot, col_hot], axis=1).astype(bf16)
        aux_s[rows] = jnp.where((code >= SIDE * SIDE) & (lane == 0), masked_score, 0.0).astype(bf16)
        block = memory_s[rows]
        positions = dot(hot, table_s[0]) + dot(hot, table_s[1])
        key_in = (block.astype(f32) + positions).astype(bf16)
        key_in_s[rows] = key_in
        key_s[rows] = dot(key_in, attn_in[1, 1]).astype(bf16)
        value_s[rows] = (dot(block, attn_in[1, 2]) + value_bias).astype(bf16)

    def score_chunk(i, out):
        rows = pl.ds(pl.multiple_of(i * CHUNK, CHUNK), CHUNK)
        for g in range(2):
            left = jnp.concatenate([key_s[rows, NP * g : NP * g + NP], aux_s[rows]], axis=1)
            out[:, HQ // 2 * g : HQ // 2 * (g + 1)] = dot(left, weight_s[g])

    def attend_chunk(i, scored):
        rows = pl.ds(pl.multiple_of(i * CHUNK, CHUNK), CHUNK)
        value_ct = value_s[rows].T
        for p in range(4):
            cols = pair_cols(p)
            before = total_s[0:1, cols]
            part = scored[:, cols]
            highest = jnp.maximum(
                before, jnp.max(part, axis=0, keepdims=True) * (scale * log2e)
            )
            raised = jnp.exp2(part * (scale * log2e) - highest)
            fade = jnp.exp2(before - highest)
            total_s[0:1, cols] = highest
            total_s[1:2, cols] = total_s[1:2, cols] * fade + jnp.sum(raised, axis=0, keepdims=True)
            shifts_s[pl.ds(i, 1), cols] = highest
            raised_b = raised.astype(bf16)
            probs_s[rows, cols] = raised_b
            mixed_s[pair_rows(p)] = mixed_s[pair_rows(p)] * fade + dot(
                value_ct[pair_rows(p)], raised_b
            )

    total_s[0:1] = jnp.full((1, HQ), -3e38, f32)
    total_s[1:2] = jnp.zeros((1, HQ), f32)
    mixed_s[...] = jnp.zeros_like(mixed_s)
    score_chunk(0, score_a)

    @pl.loop(0, chunks // 2)
    def _(j):
        i = j * 2
        score_chunk(i + 1, score_b)
        attend_chunk(i, score_a)
        score_chunk(jnp.minimum(i + 2, chunks - 1), score_a)
        attend_chunk(i + 1, score_b)

    send_a[:D] = own_blocks([mixed_s[pair_rows(p)] for p in range(4)])
    send_a[D : D + HEADS] = head_rows(total_s[0:1])
    send_a[D + HEADS :] = head_rows(total_s[1:2])
    pl.semaphore_wait(barrier, len(peers))
    swap_a = pltpu.make_async_remote_copy(
        src_ref=send_a,
        dst_ref=recv_a,
        send_sem=link_sem.at[0],
        recv_sem=link_sem.at[1],
        device_id=partner,
        device_id_type=pl.DeviceIdType.MESH,
    )
    swap_a.start()
    swap_a.wait()
    is_first = member == 0
    own = send_a[...]
    other = recv_a[...]
    left = jnp.where(is_first, own, other)
    right = jnp.where(is_first, other, own)
    high_l, high_r = left[D : D + HEADS], right[D : D + HEADS]
    highest = jnp.maximum(high_l, high_r)
    fade_l = jnp.exp2(high_l - highest)
    fade_r = jnp.exp2(high_r - highest)
    total = left[D + HEADS :] * fade_l + right[D + HEADS :] * fade_r
    mixed_t = left[:D] * per_channel(fade_l / total) + right[:D] * per_channel(fade_r / total)
    log_total = head_line(highest + jnp.log2(total))
    factor_s[...] = jnp.exp2(shifts_s[...] - log_total)
    attended_c = mixed_t.T.astype(bf16)

    second_normed, second_rstd = norm_forward(first + dot(attended_c, attn_out[1]) + bias[5:6])
    second = second_normed * gain[1:2] + shift[1:2]
    ffn_input = second.astype(bf16)
    load_ffn_in.wait()
    hidden = dot(ffn_input, ffn_in_s[...]) + ffn_in_bias[...].astype(f32).reshape(1, FF)
    half_gate = 0.5 + 0.5 * lax.erf(hidden * math.sqrt(0.5))
    activated = (hidden * half_gate).astype(bf16)
    gate_s[...] = half_gate + hidden * jnp.exp(hidden * hidden * -0.5) * (1.0 / math.sqrt(2.0 * math.pi))
    load_ffn_out.wait()
    third_normed, third_rstd = norm_forward(
        second + dot(activated, ffn_out_s[...]) + ffn_out_bias[...].astype(f32).reshape(1, D)
    )
    result_out[...] = (third_normed * gain[2:3] + shift[2:3])[:NQ].astype(bf16)
    grad_third, gain_grad_2, shift_grad_2 = norm_backward(
        pad_s[2], third_normed, third_rstd, gain[2:3]
    )
    grad_branch_f = grad_third.astype(bf16)
    grad_hidden = (dot_nt(grad_branch_f, ffn_out_s[...]) * gate_s[...]).astype(bf16)
    grad_second = grad_third + dot_nt(grad_hidden, ffn_in_s[...])
    grad_second_in, gain_grad_1, shift_grad_1 = norm_backward(
        grad_second, second_normed, second_rstd, gain[1:2]
    )
    grad_branch_c = grad_second_in.astype(bf16)
    blocks = FF // D
    ffn_input_t = second.T.astype(bf16)

    def ffn_rows(target, first):
        @pl.when(member == 0)
        def _():
            for j in range(blocks // 2):
                cols = slice(D * (first + j), D * (first + j) + D)
                target[D * j : D * j + D] = dot(ffn_input_t, grad_hidden[:, cols]).astype(bf16)

        @pl.when(member == 1)
        def _():
            for j in range(blocks // 2):
                cols = slice(D * (first + j), D * (first + j) + D)
                target[D * j : D * j + D] = dot_tn(activated[:, cols], grad_branch_f).astype(bf16)

    ffn_rows(rows_f, 0)
    sum_f.phases[0]()
    ffn_rows(rows_g, blocks // 2)

    @pl.when(member == 0)
    def _():
        rows_g[ROWS_F:ROWS_G] = dot_tn(attended_c[:, : D // 2], grad_branch_c).astype(bf16)

    @pl.when(member == 1)
    def _():
        rows_g[ROWS_F:ROWS_G] = dot_tn(attended_c[:, D // 2 :], grad_branch_c).astype(bf16)

    clear_rest(rows_f, ROWS_F)
    clear_rest(rows_g, ROWS_G)
    clear_rest(rows_t, ROWS_T)
    clear_rest(rows_k, ROWS_K)
    sum_g.phases[0]()
    grad_attended_c = dot_nt(grad_branch_c, attn_out[1]).astype(bf16).astype(f32)
    hidden_sum = row_total(grad_hidden)
    small_s[:16] = jnp.concatenate(
        [hidden_sum[:, D * j : D * j + D] for j in range(FF // D)]
        + [
            row_total(grad_branch_f),
            row_total(grad_branch_c),
            gain_grad_2,
            shift_grad_2,
            gain_grad_1,
            shift_grad_1,
            row_total(grad_attended_c),
            jnp.zeros((1, D), f32),
        ],
        axis=0,
    )

    grad_attended_t = grad_attended_c.T
    grad_xt[...] = spread_cols(grad_attended_t)
    grad_x[...] = spread_rows(grad_attended_c)
    inner = head_line(head_sums(grad_attended_t * mixed_t))
    mixed_s[...] = jnp.zeros_like(mixed_s)
    key_grads[...] = jnp.zeros_like(key_grads)

    def in_turn(i, phases):
        for k, phase in enumerate(phases):
            pl.when(i == chunks * (k + 1) // (len(phases) + 1))(phase)

    mixed_phases = [phase for pair in zip(sum_f.phases[1:], sum_g.phases[1:]) for phase in pair]

    @pl.loop(0, chunks)
    def _(i):
        rows = pl.ds(pl.multiple_of(i * CHUNK, CHUNK), CHUNK)
        key_ct = key_s[rows].T
        value_c = value_s[rows]
        weights = []
        for p in range(4):
            cols = pair_cols(p)
            grad_probs = dot(value_c, grad_xt[:, cols])
            probs = probs_s[rows, cols].astype(f32) * factor_s[pl.ds(i, 1), cols]
            grad_scores = (probs * (grad_probs - inner[:, cols])).astype(bf16)
            mixed_s[pair_rows(p)] += dot(key_ct[pair_rows(p)], grad_scores)
            probs_s[rows, cols] = grad_scores
            weights.append(probs.astype(bf16))
        grad_value = dot(jnp.concatenate(weights, axis=1), grad_x[...]).astype(bf16)
        value_s[rows] = grad_value
        key_grads[D:] += dot_tn(memory_s[rows], grad_value)
        in_turn(i, mixed_phases[:8])

    send_b[...] = own_blocks([mixed_s[pair_rows(p)] for p in range(4)]) * scale
    swap_b = pltpu.make_async_remote_copy(
        src_ref=send_b,
        dst_ref=recv_b,
        send_sem=link_sem.at[2],
        recv_sem=link_sem.at[3],
        device_id=partner,
        device_id_type=pl.DeviceIdType.MESH,
    )
    swap_b.start()
    swap_b.wait()
    grad_query_c = (send_b[...] + recv_b[...]).T.astype(bf16)

    cross_pos_grad = dot_nt(grad_query_c, attn_in[1, 0])
    grad_first_in, gain_grad_0, shift_grad_0 = norm_backward(
        grad_second_in + cross_pos_grad, first_normed, first_rstd, gain[0:1]
    )
    grad_branch = grad_first_in.astype(bf16)
    grad_attended = dot_nt(grad_branch, attn_out[0]).astype(bf16).astype(f32)
    grad_probs = dot(value_self, spread_cols(grad_attended.T))
    inner_self = jnp.sum(probs_self * grad_probs, axis=0, keepdims=True)
    grad_scores = (probs_self * (grad_probs - inner_self)).astype(bf16)
    key_t = key_self.astype(f32).T.astype(bf16)
    grad_query_s = (
        own_blocks([dot(key_t[pair_rows(p)], grad_scores[:, pair_cols(p)]) for p in range(4)]) * scale
    ).T.astype(bf16)
    grad_key_s = (dot(grad_scores, spread_rows(query_self.astype(f32))) * scale).astype(bf16)
    grad_value_s = dot(probs_self_b, spread_rows(grad_attended)).astype(bf16)
    grad_mixed_q = dot_nt(grad_query_s, attn_in[0, 0]) + dot_nt(grad_key_s, attn_in[0, 1])
    queries_grad_out[...] = (grad_first_in + grad_mixed_q + dot_nt(grad_value_s, attn_in[0, 2]))[
        :NQ
    ].astype(bf16)
    small_s[16:] = jnp.concatenate(
        [
            row_total(grad_query_s),
            row_total(grad_value_s),
            row_total(grad_branch),
            row_total(grad_query_c),
            gain_grad_0,
            shift_grad_0,
            jnp.zeros((10, D), f32),
        ],
        axis=0,
    )
    @pl.when(member == 0)
    def _():
        rows_t[:D] = dot_tn(mixed_q, grad_query_s).astype(bf16)
        rows_t[D : 2 * D] = dot_tn(mixed_q, grad_key_s).astype(bf16)
        rows_t[2 * D : 3 * D] = dot_tn(queries_b, grad_value_s).astype(bf16)

    @pl.when(member == 1)
    def _():
        rows_t[:D] = dot_tn(cross_q, grad_query_c).astype(bf16)
        rows_t[D : 2 * D] = dot_tn(attended, grad_branch).astype(bf16)
        rows_t[ROW_POS:ROW_SMALL] = (grad_mixed_q + cross_pos_grad).astype(bf16)
        rows_t[ROW_SMALL : ROW_SMALL + 32] = small_s[...].astype(bf16)
        rows_t[ROW_SMALL + 32 : ROWS_T] = jnp.zeros((ROWS_T - ROW_SMALL - 32, D), bf16)

    sum_t.phases[0]()

    @pl.loop(0, chunks)
    def _(i):
        rows = pl.ds(pl.multiple_of(i * CHUNK, CHUNK), CHUNK)
        grad_key = (dot(probs_s[rows], query_x[...]) * scale).astype(bf16)
        key_s[rows] = grad_key
        key_grads[:D] += dot_tn(key_in_s[rows], grad_key)
        in_turn(i, [*mixed_phases[8:10], sum_t.phases[1], *mixed_phases[10:-2]])

    rows_k[:ROWS_K] = key_grads[...].astype(bf16)
    sum_k.phases[0]()
    sum_t.phases[2]()

    @pl.loop(0, chunks)
    def _(i):
        rows = pl.ds(pl.multiple_of(i * CHUNK, CHUNK), CHUNK)
        both = jnp.concatenate([key_s[rows], value_s[rows]], axis=1)
        memory_s[rows] = dot(both, back_w[...]).astype(bf16)
        pltpu.make_async_copy(memory_s.at[rows], memory_grad_hbm.at[0, rows], store_sem.at[i]).start()

    sum_k.phases[1]()
    sum_t.phases[3]()
    mixed_phases[-2]()
    mixed_phases[-1]()
    stores = [
        pltpu.make_async_copy(whole, target, load_sem.at[3 + k])
        for k, (whole, target) in enumerate(
            (
                (whole_f, whole_f_hbm),
                (whole_g, whole_g_hbm),
                (whole_t, whole_t_hbm),
                (whole_k, whole_k_hbm),
            )
        )
    ]
    stores[0].start()
    stores[1].start()
    for k in range(2, len(sum_k.phases)):
        sum_k.phases[k]()
        if k + 2 < len(sum_t.phases):
            sum_t.phases[k + 2]()
    stores[2].start()
    stores[3].start()

    @pl.loop(0, chunks)
    def _(i):
        rows = pl.ds(pl.multiple_of(i * CHUNK, CHUNK), CHUNK)
        pltpu.make_async_copy(memory_s.at[rows], memory_grad_hbm.at[0, rows], store_sem.at[i]).wait()

    for store in stores:
        store.wait()


def finish_kernel(
    result_in,
    queries_grad_in,
    memory_grad_in,
    whole_f,
    whole_g,
    whole_t,
    whole_k,
    result,
    queries_grad,
    memory_grad,
    attn_in_grad,
    attn_out_grad,
    attn_bias_grad,
    ffn_in_grad,
    ffn_in_bias_grad,
    ffn_out_grad,
    ffn_out_bias_grad,
    norm_gain_grad,
    norm_bias_grad,
    query_pos_grad,
    moved,
    in_sem,
    out_sem,
):
    pieces = in_sem.shape[0]
    piece = moved.shape[0] // pieces

    def fetch(j):
        rows = pl.ds(piece * j, piece)
        return pltpu.make_async_copy(memory_grad_in.at[0, rows], moved.at[rows], in_sem.at[j])

    def write(j):
        rows = pl.ds(piece * j, piece)
        return pltpu.make_async_copy(moved.at[rows], memory_grad.at[0, rows], out_sem.at[j])

    for j in range(pieces):
        fetch(j).start()
    result[0] = result_in[...]
    queries_grad[0] = queries_grad_in[...]
    for j in range(FF // D):
        piece_at = j % (FF // D // 2) * D
        sums = whole_f if j < FF // D // 2 else whole_g
        ffn_in_grad[:, D * j : D * j + D] = sums[0, piece_at : piece_at + D].astype(f32)
        ffn_out_grad[D * j : D * j + D] = sums[1, piece_at : piece_at + D].astype(f32)
    for j in range(pieces):
        fetch(j).wait()
        write(j).start()
    attn_out_grad[0] = whole_t[1, D : 2 * D].astype(f32)
    attn_out_grad[1, : D // 2] = whole_g[0, ROWS_F:ROWS_G].astype(f32)
    attn_out_grad[1, D // 2 :] = whole_g[1, ROWS_F:ROWS_G].astype(f32)
    for j in range(3):
        attn_in_grad[0, j] = whole_t[0, D * j : D * j + D].astype(f32)
    attn_in_grad[1, 0] = whole_t[1, :D].astype(f32)
    attn_in_grad[1, 1] = whole_k[:D].astype(f32)
    attn_in_grad[1, 2] = whole_k[D : 2 * D].astype(f32)
    query_pos_grad[...] = whole_t[1, ROW_POS:ROW_SMALL].astype(f32)[:NQ]
    small = whole_t[1, ROW_SMALL : ROW_SMALL + 32].astype(f32)
    ffn_in_bias_grad[...] = jnp.concatenate([small[j : j + 1] for j in range(FF // D)], axis=1)
    ffn_out_bias_grad[...] = small[8:9]
    for j, (own, cross) in enumerate(((16, 19), (17, 14), (18, 9))):
        attn_bias_grad[j, 0:1] = small[own : own + 1]
        attn_bias_grad[j, 1:2] = small[cross : cross + 1]
    norm_gain_grad[0:1] = small[20:21]
    norm_gain_grad[1:2] = small[12:13]
    norm_gain_grad[2:3] = small[10:11]
    norm_bias_grad[0:1] = small[21:22]
    norm_bias_grad[1:2] = small[13:14]
    norm_bias_grad[2:3] = small[11:12]
    for j in range(pieces):
        write(j).wait()


def body(
    pages,
    queries,
    memory,
    quarter_turns,
    token_order,
    lengths,
    attn_in,
    attn_out,
    attn_bias,
    ffn_in,
    ffn_in_bias,
    ffn_out,
    ffn_out_bias,
    norm_gain,
    norm_bias,
    query_pos,
    out_grad,
):
    tokens = memory.shape[1]
    chunks = tokens // CHUNK
    groups_f, groups_t, groups_k = sum_groups(pages)
    summed = [
        (padded(ROWS_F, pages), groups_f),
        (padded(ROWS_G, pages), groups_f),
        (padded(ROWS_T, pages), groups_t),
        (padded(ROWS_K, 2 * pages), groups_k),
    ]
    whole_shapes = [(2, rows, D) for rows, _ in summed[:3]] + [(summed[3][0], D)]
    sum_buffers = []
    for (rows, groups), shape in zip(summed, whole_shapes):
        landing = PageSum.landing_rows(pages, groups, rows)
        sum_buffers += [pltpu.VMEM(each, bf16) for each in ((rows, D), (landing, D), shape)]
    copies = 32
    vmem = pl.BlockSpec(memory_space=pltpu.VMEM)
    smem = pl.BlockSpec(memory_space=pltpu.SMEM)
    anywhere = pl.BlockSpec(memory_space=pl.ANY)
    parts = pl.pallas_call(
        functools.partial(layer_kernel, tokens, pages),
        out_shape=[
            jax.ShapeDtypeStruct((NQ, D), bf16),
            jax.ShapeDtypeStruct((NQ, D), bf16),
            jax.ShapeDtypeStruct((1, tokens, D), bf16),
            *(jax.ShapeDtypeStruct(shape, bf16) for shape in whole_shapes),
        ],
        in_specs=[
            vmem,
            anywhere,
            smem,
            vmem,
            smem,
            vmem,
            vmem,
            vmem,
            anywhere,
            vmem,
            anywhere,
            vmem,
            vmem,
            vmem,
            vmem,
            vmem,
            vmem,
        ],
        out_specs=[vmem, vmem, anywhere, anywhere, anywhere, anywhere, anywhere],
        scratch_shapes=[
            pltpu.VMEM((tokens, D), bf16),
            pltpu.VMEM((tokens, D), bf16),
            pltpu.VMEM((tokens, D), bf16),
            pltpu.VMEM((tokens, D), bf16),
            pltpu.VMEM((tokens, NP), bf16),
            pltpu.VMEM((tokens, HQ), bf16),
            pltpu.VMEM((1, tokens), f32),
            pltpu.VMEM((CHUNK, HQ), f32),
            pltpu.VMEM((CHUNK, HQ), f32),
            pltpu.VMEM((2, D, HQ // 2), bf16),
            pltpu.VMEM((2, 2 * SIDE, D), bf16),
            pltpu.VMEM((chunks, HQ), f32),
            pltpu.VMEM((chunks, HQ), f32),
            pltpu.VMEM((8, HQ), f32),
            pltpu.VMEM((D, PAIR), f32),
            pltpu.VMEM((D, FF), bf16),
            pltpu.VMEM((FF, D), bf16),
            pltpu.VMEM((NP, FF), f32),
            pltpu.VMEM((3, NP, D), f32),
            pltpu.VMEM((2 * D, D), bf16),
            pltpu.VMEM((HQ, D), bf16),
            pltpu.VMEM((D, HQ), bf16),
            pltpu.VMEM((HQ, D), bf16),
            pltpu.VMEM((D + 2 * HEADS, NP), f32),
            pltpu.VMEM((D + 2 * HEADS, NP), f32),
            pltpu.VMEM((D, NP), f32),
            pltpu.VMEM((D, NP), f32),
            pltpu.VMEM((2 * D, D), f32),
            pltpu.VMEM((32, D), f32),
            *sum_buffers,
            pltpu.SemaphoreType.DMA((7,)),
            pltpu.SemaphoreType.DMA((chunks,)),
            pltpu.SemaphoreType.DMA((4,)),
            *[pltpu.SemaphoreType.DMA((copies,))] * 8,
        ],
        compiler_params=pltpu.CompilerParams(
            collective_id=0, has_side_effects=True, vmem_limit_bytes=62 * 1024 * 1024
        ),
        cost_estimate=pl.CostEstimate(
            flops=2 * 8 * tokens * HQ * D, bytes_accessed=20 << 20, transcendentals=tokens * HQ
        ),
        name="decoder_layer",
    )(
        queries,
        memory,
        quarter_turns,
        token_order,
        lengths,
        attn_in,
        attn_out,
        attn_bias.transpose(1, 0, 2),
        ffn_in,
        ffn_in_bias,
        ffn_out,
        ffn_out_bias,
        norm_gain,
        norm_bias,
        query_pos,
        out_grad,
        jnp.asarray(position_table()),
    )
    outs = pl.pallas_call(
        finish_kernel,
        out_shape=[
            jax.ShapeDtypeStruct((1, NQ, D), bf16),
            jax.ShapeDtypeStruct((1, NQ, D), bf16),
            jax.ShapeDtypeStruct((1, tokens, D), bf16),
            jax.ShapeDtypeStruct((2, 3, D, D), f32),
            jax.ShapeDtypeStruct((2, D, D), f32),
            jax.ShapeDtypeStruct((3, 2, D), f32),
            jax.ShapeDtypeStruct((D, FF), f32),
            jax.ShapeDtypeStruct((1, FF), f32),
            jax.ShapeDtypeStruct((FF, D), f32),
            jax.ShapeDtypeStruct((1, D), f32),
            jax.ShapeDtypeStruct((3, D), f32),
            jax.ShapeDtypeStruct((3, D), f32),
            jax.ShapeDtypeStruct((NQ, D), f32),
        ],
        in_specs=[vmem, vmem, anywhere, vmem, vmem, vmem, vmem],
        out_specs=[vmem, vmem, anywhere] + [vmem] * 10,
        scratch_shapes=[
            pltpu.VMEM((tokens, D), bf16),
            pltpu.SemaphoreType.DMA((8,)),
            pltpu.SemaphoreType.DMA((8,)),
        ],
        compiler_params=pltpu.CompilerParams(vmem_limit_bytes=62 * 1024 * 1024),
        name="write_outputs",
    )(*parts)
    return (
        *outs[:5],
        outs[5].transpose(1, 0, 2),
        outs[6],
        outs[7].reshape(FF),
        outs[8],
        outs[9].reshape(D),
        *outs[10:],
    )


def solution(mesh):
    in_specs = (
        P("dp", None, None),
        P("dp", "blk", None),
        P("dp"),
        P("dp", "blk"),
        P("dp"),
        P(),
        P(),
        P(),
        P(),
        P(),
        P(),
        P(),
        P(),
        P(),
        P(),
        P("dp", None, None),
    )
    out_specs = (
        P("dp", None, None),
        P("dp", None, None),
        P("dp", "blk", None),
        P(),
        P(),
        P(),
        P(),
        P(),
        P(),
        P(),
        P(),
        P(),
        P(),
    )
    layer = functools.partial(body, mesh.shape["dp"])
    return jax.shard_map(layer, mesh=mesh, in_specs=in_specs, out_specs=out_specs, check_vma=False)
```

```python
import functools
import math

import jax
import jax.numpy as jnp
import numpy as np
from jax import lax
from jax.experimental import pallas as pl
from jax.experimental.pallas import tpu as pltpu
from jax.sharding import PartitionSpec as P

D = 256
HEADS = 8
HD = D // HEADS
SIDE = 128
NQ = 125
NP = 128
HQ = HEADS * NP
PAIR = 2 * NP
FF = 2048
CHUNK = 512

masked_score = -1e30
norm_eps = 1e-05
scale = 1.0 / math.sqrt(HD)
log2e = math.log2(math.e)

bf16 = jnp.bfloat16
f32 = jnp.float32

ROWS_F = FF // 2
ROW_POS = 2 * D
ROW_SMALL = 2 * D + NP
ROWS_T = 3 * D
ROWS_K = 3 * D
TILE = 16


def axes_of(pages):
    axes = {"core": (2, 1), "y": (2, 2)}
    stride = 4
    while stride < pages:
        radix = 4 if pages // stride % 4 == 0 else 2
        axes["z%d" % (len(axes) - 2)] = (radix, stride)
        stride *= radix
    axes["x"] = (2, 0)
    return axes


def far_axes(pages):
    return [(name,) for name in axes_of(pages) if name.startswith("z")]


def sum_groups(pages):
    far = far_axes(pages)
    return [("core",), ("y",), *far], [("core", "y"), *far], [("x", "core", "y"), *far]


def padded(rows, pages):
    unit = TILE * pages
    return (rows + unit - 1) // unit * unit


def position_table():
    half = D // 2
    channel = np.arange(half)
    inverse = np.exp((channel // 2).astype(np.float32) * np.float32(-2.0 * math.log(10000.0) / half))
    angle = (np.arange(SIDE, dtype=np.float32) + 1.0) * np.float32(2.0 * math.pi / SIDE)
    angle = angle[:, None] * inverse
    return np.where(channel % 2 == 0, np.sin(angle), np.cos(angle)).astype(np.float32)


def dot(a, b):
    return jnp.dot(a, b, preferred_element_type=f32)


def dot_nt(a, b):
    return lax.dot_general(a, b, (((1,), (1,)), ((), ())), preferred_element_type=f32)


def dot_tn(a, b):
    return lax.dot_general(a, b, (((0,), (0,)), ((), ())), preferred_element_type=f32)


def row_total(values):
    return jnp.sum(values.astype(f32), axis=0, keepdims=True)


def norm_forward(values):
    average = jnp.mean(values, axis=-1, keepdims=True)
    centred = values - average
    variance = jnp.mean(centred * centred, axis=-1, keepdims=True)
    rstd = lax.rsqrt(variance + norm_eps)
    return centred * rstd, rstd


def norm_backward(grad, normed, rstd, gain):
    grad_normed = grad * gain
    first = jnp.mean(grad_normed, axis=-1, keepdims=True)
    second = jnp.mean(grad_normed * normed, axis=-1, keepdims=True)
    grad_in = rstd * (grad_normed - first - normed * second)
    return grad_in, row_total(grad * normed), row_total(grad)


def spread_rows(rows):
    head = lax.broadcasted_iota(jnp.int32, (NP, D), 1) // HD
    return jnp.concatenate(
        [jnp.where(head == h, rows, 0.0) for h in range(HEADS)], axis=0
    ).astype(bf16)


def spread_cols(cols):
    head = lax.broadcasted_iota(jnp.int32, (D, NP), 0) // HD
    return jnp.concatenate(
        [jnp.where(head == h, cols, 0.0) for h in range(HEADS)], axis=1
    ).astype(bf16)


def own_heads(full):
    return jnp.concatenate(
        [full[HD * h : HD * h + HD, NP * h : NP * h + NP] for h in range(HEADS)], axis=0
    )


def project_heads(weight_t, sums):
    high = sums.astype(bf16)
    low = (sums - high.astype(f32)).astype(bf16)
    return own_heads(dot(weight_t, high) + dot(weight_t, low))


def own_blocks(pairs):
    parts = []
    for pair in pairs:
        parts += [pair[:HD, :NP], pair[HD:, NP:]]
    return jnp.concatenate(parts, axis=0)


def head_rows(row):
    return jnp.concatenate([row[:, NP * h : NP * h + NP] for h in range(HEADS)], axis=0)


def head_line(rows):
    return jnp.concatenate([rows[h : h + 1] for h in range(HEADS)], axis=1)


def per_channel(rows):
    return jnp.concatenate(
        [jnp.broadcast_to(rows[h : h + 1], (HD, NP)) for h in range(HEADS)], axis=0
    )


def head_sums(cols):
    return jnp.concatenate(
        [jnp.sum(cols[HD * h : HD * h + HD], axis=0, keepdims=True) for h in range(HEADS)], axis=0
    )


def pair_cols(p):
    return slice(PAIR * p, PAIR * p + PAIR)


def pair_rows(p):
    return slice(2 * HD * p, 2 * HD * p + 2 * HD)


class Place:
    def __init__(self, pages):
        self.axes = axes_of(pages)
        self.page = lax.axis_index("dp")
        self.member = lax.axis_index("blk")
        self.digit = {
            name: self.member if name == "x" else lax.rem(self.page // stride, radix)
            for name, (radix, stride) in self.axes.items()
        }

    def size(self, group):
        return math.prod(self.axes[name][0] for name in group)

    def index(self, group):
        index = 0
        for name in group:
            index = index * self.axes[name][0] + self.digit[name]
        return index

    def peer(self, group, hop):
        index = lax.rem(self.index(group) + hop, self.size(group))
        page, member, rest = self.page, self.member, index
        for name in reversed(group):
            radix, stride = self.axes[name]
            digit = lax.rem(rest, radix)
            rest = rest // radix
            if name == "x":
                member = digit
            else:
                page = page + (digit - self.digit[name]) * stride
        return (page, member), index


class PageSum:
    def __init__(self, place, groups, back, rows, landing, whole, sent, arrived):
        self.place, self.groups, self.back = place, groups, back
        self.rows, self.landing, self.whole = rows, landing, whole
        self.sent, self.arrived = sent, arrived
        self.slots = 0
        self.extents = [rows.shape[0]]
        self.bases = [0]
        self.landings = []
        at = 0
        for group in groups:
            size = place.size(group)
            extent = self.extents[-1] // size
            self.landings.append(at)
            at += (size - 1) * extent
            self.bases.append(pl.multiple_of(self.bases[-1] + place.index(group) * extent, TILE))
            self.extents.append(extent)
        last = len(groups)
        moves = [self.scatter_moves(s) for s in range(last)]
        near = 2 if len(groups[0]) == 1 else 1
        moves += [self.gather_moves(s) for s in range(last - 1, near - 1, -1)]
        if back == "first":
            moves.append(self.gather_moves(0))
        elif back == "sides":
            moves += [self.side_moves(), self.corner_moves(), self.core_moves()]
        else:
            moves += [self.across_moves(), self.core_moves()]
        self.phases = [functools.partial(self.step, moves, k) for k in range(len(moves) + 1)]

    @staticmethod
    def landing_rows(pages, groups, rows):
        axes = axes_of(pages)
        total, extent = 0, rows
        for group in groups:
            size = math.prod(axes[name][0] for name in group)
            extent //= size
            total += (size - 1) * extent
        return total

    def step(self, moves, k):
        last = len(self.groups)
        if k > 0:
            for move in moves[k - 1]:
                self.copy(*move).wait()
        if 0 < k <= last:
            total = self.scatter_sum(k - 1)
            region = pl.ds(self.bases[k], self.extents[k])
            if k < last:
                self.rows[region] = total
            elif len(self.whole.shape) == 3:
                self.whole[self.place.member, region] = total
            else:
                self.whole[region] = total
        if k < len(moves):
            for move in moves[k]:
                self.copy(*move).start()

    def copy(self, slot, source, target, device):
        return pltpu.make_async_remote_copy(
            src_ref=source(),
            dst_ref=target(),
            send_sem=self.sent.at[slot],
            recv_sem=self.arrived.at[slot],
            device_id=device,
            device_id_type=pl.DeviceIdType.MESH,
        )

    def new_slot(self):
        self.slots += 1
        return self.slots - 1

    def same(self, device, view):
        return (self.new_slot(), view, view, device)

    def scatter_moves(self, step):
        group = self.groups[step]
        extent = self.extents[step + 1]
        moves = []
        for hop in range(1, self.place.size(group)):
            device, other = self.place.peer(group, hop)
            start = pl.multiple_of(self.bases[step] + other * extent, TILE)
            landing = self.landings[step] + (hop - 1) * extent
            moves.append(
                (
                    self.new_slot(),
                    functools.partial(self.part, self.rows, start, extent),
                    functools.partial(self.part, self.landing, landing, extent),
                    device,
                )
            )
        return moves

    @staticmethod
    def part(ref, start, extent):
        return ref.at[pl.ds(start, extent)]

    def half(self, member, start, extent):
        if len(self.whole.shape) == 3:
            return self.whole.at[member, pl.ds(start, extent)]
        return self.whole.at[pl.ds(start, extent)]

    def scatter_sum(self, step):
        extent = self.extents[step + 1]
        total = self.rows[pl.ds(self.bases[step + 1], extent)].astype(f32)
        for hop in range(1, self.place.size(self.groups[step])):
            landing = self.landings[step] + (hop - 1) * extent
            total = total + self.landing[pl.ds(landing, extent)].astype(f32)
        return total.astype(bf16)

    def gather_moves(self, step):
        group = self.groups[step]
        view = functools.partial(self.half, self.place.member, self.bases[step + 1], self.extents[step + 1])
        return [
            self.same(self.place.peer(group, hop)[0], view) for hop in range(1, self.place.size(group))
        ]

    def own_quarter(self):
        step = 2 if len(self.groups[0]) == 1 else 1
        return self.bases[step], self.extents[step]

    def side_moves(self):
        view = functools.partial(self.half, self.place.member, *self.own_quarter())
        return [self.same(self.place.peer((name,), 1)[0], view) for name in ("y", "x")]

    def corner_moves(self):
        base, extent = self.own_quarter()
        half = extent // 2
        other = pl.multiple_of(base + (1 - 2 * self.place.digit["y"]) * extent, TILE)
        first = functools.partial(self.half, self.place.member, other, half)
        second = functools.partial(
            self.half, 1 - self.place.member, pl.multiple_of(base + half, TILE), half
        )
        return [
            self.same(self.place.peer(("x",), 1)[0], first),
            self.same(self.place.peer(("y",), 1)[0], second),
        ]

    def across_moves(self):
        view = functools.partial(self.half, self.place.member, *self.own_quarter())
        return [self.same(self.place.peer(("x", "y"), hop)[0], view) for hop in range(1, 4)]

    def core_moves(self):
        extent = self.extents[0] // 2
        start = pl.multiple_of(self.place.digit["core"] * extent, TILE)
        device, _ = self.place.peer(("core",), 1)
        return [self.same(device, functools.partial(self.half, m, start, extent)) for m in range(2)]


def clear_rest(ref, used):
    if ref.shape[0] > used:
        ref[used:] = jnp.zeros((ref.shape[0] - used, D), ref.dtype)


def layer_kernel(
    tokens,
    pages,
    queries_in,
    memory_hbm,
    turns_in,
    order_in,
    lengths_in,
    attn_in,
    attn_out,
    attn_bias,
    ffn_in_hbm,
    ffn_in_bias,
    ffn_out_hbm,
    ffn_out_bias,
    norm_gain,
    norm_bias,
    pos_in,
    out_grad_in,
    table_in,
    result_out,
    queries_grad_out,
    memory_grad_hbm,
    whole_f_hbm,
    whole_g_hbm,
    whole_t_hbm,
    whole_k_hbm,
    memory_s,
    key_in_s,
    probs_s,
    grad_scores_s,
    code_s,
    query_kt,
    grad_vt,
    back_s,
    table_s,
    shifts_s,
    factor_s,
    total_s,
    mixed_s,
    pad_s,
    send_a,
    recv_a,
    send_b,
    recv_b,
    small_s,
    rows_f,
    landing_f,
    whole_f,
    rows_g,
    landing_g,
    whole_g,
    rows_t,
    landing_t,
    whole_t,
    rows_k,
    landing_k,
    whole_k,
    load_sem,
    store_sem,
    link_sem,
    sent_f,
    arrived_f,
    sent_g,
    arrived_g,
    sent_t,
    arrived_t,
    sent_k,
    arrived_k,
):
    member = lax.axis_index("blk")
    partner = (lax.axis_index("dp"), 1 - member)
    chunks = tokens // CHUNK

    place = Place(pages)
    groups_f, groups_t, groups_k = sum_groups(pages)
    sum_f = PageSum(place, groups_f, "sides", rows_f, landing_f, whole_f, sent_f, arrived_f)
    sum_g = PageSum(place, groups_f, "sides", rows_g, landing_g, whole_g, sent_g, arrived_g)
    sum_t = PageSum(place, groups_t, "across", rows_t, landing_t, whole_t, sent_t, arrived_t)
    sum_k = PageSum(place, groups_k, "first", rows_k, landing_k, whole_k, sent_k, arrived_k)

    barrier = pltpu.get_barrier_semaphore()
    peers = [
        place.peer(group, hop)[0] for group in groups_k for hop in range(1, place.size(group))
    ]
    for peer in peers:
        pl.semaphore_signal(barrier, inc=1, device_id=peer, device_id_type=pl.DeviceIdType.MESH)

    load_memory = pltpu.make_async_copy(memory_hbm.at[0], memory_s, load_sem.at[0])
    half = FF // 2
    ffn_in_s = [grad_scores_s.at[D * k : D * k + D] for k in range(2)]
    ffn_out_s = grad_scores_s.at[2 * D : 2 * D + FF, :D]
    free = 2 * D + FF
    active_s = [grad_scores_s.at[free + NP * k : free + NP * k + NP] for k in range(2)]
    slope_s = [grad_scores_s.at[free + NP * k : free + NP * k + NP] for k in range(2, 4)]
    load_ffn = [
        pltpu.make_async_copy(ffn_in_hbm.at[:, half * k : half * k + half], ffn_in_s[k], load_sem.at[1 + k])
        for k in range(2)
    ]
    load_ffn.append(pltpu.make_async_copy(ffn_out_hbm, ffn_out_s, load_sem.at[3]))
    load_memory.start()
    for load in load_ffn:
        load.start()

    pairs = [attn_bias[j].astype(f32) for j in range(3)]
    bias = jnp.concatenate([pair[k : k + 1] for k in range(2) for pair in pairs], axis=0)
    gain = norm_gain[...].astype(f32)
    shift = norm_bias[...].astype(f32)

    order = order_in[...]
    turn = turns_in[0]
    row_at = order >> 7
    col_at = order & 127
    top = SIDE - 1
    row_new = jnp.where(
        turn == 0, row_at, jnp.where(turn == 1, col_at, jnp.where(turn == 2, top - row_at, top - col_at))
    )
    col_new = jnp.where(
        turn == 0, col_at, jnp.where(turn == 1, top - row_at, jnp.where(turn == 2, top - col_at, row_at))
    )
    past = jnp.where(order < lengths_in[0], 0, SIDE * SIDE)
    code_s[...] = (row_new * SIDE + col_new + past).astype(f32)

    pad_s[...] = jnp.zeros_like(pad_s)
    pad_s[0, :NQ] = queries_in[0].astype(f32)
    pad_s[1, :NQ] = pos_in[...].astype(f32)
    pad_s[2, :NQ] = out_grad_in[0].astype(f32)
    queries_f = pad_s[0]
    pos_f = pad_s[1]
    queries_b = queries_f.astype(bf16)
    mixed_q = (queries_f + pos_f).astype(bf16)
    query_self = (dot(mixed_q, attn_in[0, 0]) + bias[0:1]).astype(bf16)
    key_self = dot(mixed_q, attn_in[0, 1]).astype(bf16)
    value_self = (dot(queries_b, attn_in[0, 2]) + bias[1:2]).astype(bf16)
    scores = dot(key_self, spread_cols(query_self.astype(f32).T)) * scale
    own_key = lax.broadcasted_iota(jnp.int32, (NP, HQ), 0) < NQ
    scores = jnp.where(own_key, scores, masked_score)
    raised = jnp.exp(scores - jnp.max(scores, axis=0, keepdims=True))
    probs_self = raised / jnp.sum(raised, axis=0, keepdims=True)
    probs_self_b = probs_self.astype(bf16)
    value_t = value_self.astype(f32).T.astype(bf16)
    attended = own_blocks(
        [dot(value_t[pair_rows(p)], probs_self_b[:, pair_cols(p)]) for p in range(4)]
    ).T.astype(bf16)
    first_normed, first_rstd = norm_forward(queries_f + dot(attended, attn_out[0]) + bias[2:3])
    first = first_normed * gain[0:1] + shift[0:1]
    cross_q = (first + pos_f).astype(bf16)
    query_c = (dot(cross_q, attn_in[1, 0]) + bias[3:4]).astype(bf16)
    query_x = spread_rows(query_c.astype(f32))
    query_k = dot(attn_in[1, 1], spread_cols(query_c.astype(f32).T))
    query_kt[...] = (query_k * (scale * log2e)).astype(bf16)
    back_s[:HQ] = (dot_nt(query_x, attn_in[1, 1]) * scale).astype(bf16)
    table = table_in[...]
    nothing = jnp.zeros((SIDE, D // 2), f32)
    table = jnp.concatenate(
        [jnp.concatenate([table, nothing], axis=1), jnp.concatenate([nothing, table], axis=1)], axis=0
    )
    table_high = table.astype(bf16)
    table_s[0] = table_high
    table_s[1] = (table - table_high.astype(f32)).astype(bf16)

    load_memory.wait()
    lane = lax.broadcasted_iota(jnp.int32, (CHUNK, NP), 1)

    @pl.loop(0, chunks)
    def _(i):
        rows = pl.ds(pl.multiple_of(i * CHUNK, CHUNK), CHUNK)
        line = code_s[:, rows]
        code = jnp.concatenate(
            [
                jnp.broadcast_to(line[:, NP * j : NP * j + NP], (NP, NP)).T
                for j in range(CHUNK // NP)
            ],
            axis=0,
        ).astype(jnp.int32)
        row_hot = jnp.where(((code >> 7) & 127) == lane, 1.0, 0.0)
        col_hot = jnp.where((code & 127) == lane, 1.0, 0.0)
        hot = jnp.concatenate([row_hot, col_hot], axis=1).astype(bf16)
        block = memory_s[rows].astype(f32)
        key_in_s[rows] = (block + dot(hot, table_s[0]) + dot(hot, table_s[1])).astype(bf16)

    def score_chunk(i, out, top):
        rows = pl.ds(pl.multiple_of(i * CHUNK, CHUNK), CHUNK)
        line = code_s[:, rows]
        code = jnp.concatenate(
            [
                jnp.broadcast_to(line[:, NP * j : NP * j + NP], (NP, NP)).T
                for j in range(CHUNK // NP)
            ],
            axis=0,
        )
        allowed = code < SIDE * SIDE
        allowed = jnp.concatenate([allowed, allowed], axis=1)
        key_in = key_in_s[rows]
        for p in range(4):
            cols = pair_cols(p)
            part = jnp.where(allowed, dot(key_in, query_kt[:, cols]), masked_score)
            out[:, cols] = part
            top[0:1, cols] = jnp.max(part, axis=0, keepdims=True)

    def attend_chunk(i, scored, top):
        rows = pl.ds(pl.multiple_of(i * CHUNK, CHUNK), CHUNK)
        memory_ct = memory_s[rows].T
        for p in range(4):
            cols = pair_cols(p)
            before = total_s[0:1, cols]
            highest = jnp.maximum(before, top[0:1, cols])
            raised = jnp.exp2(scored[:, cols] - highest)
            fade = jnp.exp2(before - highest)
            total_s[0:1, cols] = highest
            total_s[1:2, cols] = total_s[1:2, cols] * fade + jnp.sum(raised, axis=0, keepdims=True)
            shifts_s[pl.ds(i, 1), cols] = highest
            probs_s[rows, cols] = raised.astype(bf16)
            mixed_s[:, cols] = mixed_s[:, cols] * fade + dot(memory_ct, probs_s[rows, cols])

    total_s[0:1] = jnp.full((1, HQ), -3e38, f32)
    total_s[1:2] = jnp.zeros((1, HQ), f32)
    mixed_s[...] = jnp.zeros_like(mixed_s)
    def attend_all(score_a, score_b, top_a, top_b):
        score_chunk(0, score_a, top_a)

        @pl.loop(0, chunks // 2)
        def _(j):
            i = j * 2
            score_chunk(i + 1, score_b, top_b)
            attend_chunk(i, score_a, top_a)
            score_chunk(jnp.minimum(i + 2, chunks - 1), score_a, top_a)
            attend_chunk(i + 1, score_b, top_b)

    score_buffer = pltpu.VMEM((CHUNK, HQ), f32)
    top_buffer = pltpu.VMEM((8, HQ), f32)
    pl.run_scoped(attend_all, score_buffer, score_buffer, top_buffer, top_buffer)

    value_wt = attn_in[1, 2].astype(f32).T.astype(bf16)
    key_wt = attn_in[1, 1].astype(f32).T.astype(bf16)
    send_a[:D] = project_heads(value_wt, mixed_s[...])
    send_a[D : D + HEADS] = head_rows(total_s[0:1])
    send_a[D + HEADS :] = head_rows(total_s[1:2])
    pl.semaphore_wait(barrier, len(peers))
    swap_a = pltpu.make_async_remote_copy(
        src_ref=send_a,
        dst_ref=recv_a,
        send_sem=link_sem.at[0],
        recv_sem=link_sem.at[1],
        device_id=partner,
        device_id_type=pl.DeviceIdType.MESH,
    )
    swap_a.start()
    swap_a.wait()
    is_first = member == 0
    own = send_a[...]
    other = recv_a[...]
    left = jnp.where(is_first, own, other)
    right = jnp.where(is_first, other, own)
    high_l, high_r = left[D : D + HEADS], right[D : D + HEADS]
    highest = jnp.maximum(high_l, high_r)
    fade_l = jnp.exp2(high_l - highest)
    fade_r = jnp.exp2(high_r - highest)
    total = left[D + HEADS :] * fade_l + right[D + HEADS :] * fade_r
    mixed_t = left[:D] * per_channel(fade_l / total) + right[:D] * per_channel(fade_r / total)
    log_total = head_line(highest + jnp.log2(total))
    factor_s[...] = jnp.exp2(shifts_s[...] - log_total)
    attended_c = (mixed_t.T + bias[4:5]).astype(bf16)

    second_normed, second_rstd = norm_forward(first + dot(attended_c, attn_out[1]) + bias[5:6])
    second = second_normed * gain[1:2] + shift[1:2]
    ffn_input = second.astype(bf16)
    load_ffn[0].wait()
    load_ffn[1].wait()
    blocks = [(j // 4, slice(D * j, D * j + D), slice(j % 4 * D, j % 4 * D + D)) for j in range(FF // D)]
    hidden_bias = ffn_in_bias[...].astype(f32).reshape(1, FF)
    def feed_forward(gate_s):
        for k, cols, part in blocks:
            hidden = dot(ffn_input, ffn_in_s[k][:, part]) + hidden_bias[:, cols]
            half_gate = 0.5 + 0.5 * lax.erf(hidden * math.sqrt(0.5))
            active_s[k][:, part] = (hidden * half_gate).astype(bf16)
            gate_s[:, cols] = half_gate + hidden * jnp.exp(hidden * hidden * -0.5) * (
                1.0 / math.sqrt(2.0 * math.pi)
            )
        load_ffn[2].wait()
        third_normed, third_rstd = norm_forward(
            second
            + dot(active_s[0][...], ffn_out_s[:half])
            + dot(active_s[1][...], ffn_out_s[half:])
            + ffn_out_bias[...].astype(f32).reshape(1, D)
        )
        result_out[...] = (third_normed * gain[2:3] + shift[2:3])[:NQ].astype(bf16)
        grad_third, gain_grad_2, shift_grad_2 = norm_backward(
            pad_s[2], third_normed, third_rstd, gain[2:3]
        )
        grad_branch_f = grad_third.astype(bf16)
        for k, cols, part in blocks:
            grad_hidden = dot_nt(grad_branch_f, ffn_out_s[cols]) * gate_s[:, cols]
            slope_s[k][:, part] = grad_hidden.astype(bf16)
        return grad_third, gain_grad_2, shift_grad_2, grad_branch_f

    grad_third, gain_grad_2, shift_grad_2, grad_branch_f = pl.run_scoped(
        feed_forward, pltpu.VMEM((NP, FF), f32)
    )
    grad_second = grad_third + dot_nt(slope_s[0][...], ffn_in_s[0][...])
    grad_second += dot_nt(slope_s[1][...], ffn_in_s[1][...])
    grad_second_in, gain_grad_1, shift_grad_1 = norm_backward(
        grad_second, second_normed, second_rstd, gain[1:2]
    )
    grad_branch_c = grad_second_in.astype(bf16)
    ffn_input_t = second.T.astype(bf16)

    def ffn_rows(target, k):
        @pl.when(member == 0)
        def _():
            for j in range(4):
                part = slice(D * j, D * j + D)
                target[part] = dot(ffn_input_t, slope_s[k][:, part]).astype(bf16)

        @pl.when(member == 1)
        def _():
            for j in range(4):
                part = slice(D * j, D * j + D)
                target[part] = dot_tn(active_s[k][:, part], grad_branch_f).astype(bf16)

    ffn_rows(rows_f, 0)
    sum_f.phases[0]()
    ffn_rows(rows_g, 1)

    is_first = member == 0
    out_grad_c = dot_tn(attended_c, grad_branch_c)
    rows_k[2 * D : 3 * D] = jnp.where(is_first, out_grad_c, 0.0).astype(bf16)

    clear_rest(rows_f, ROWS_F)
    clear_rest(rows_g, ROWS_F)
    clear_rest(rows_t, ROWS_T)
    clear_rest(rows_k, ROWS_K)
    sum_g.phases[0]()
    grad_attended_c = dot_nt(grad_branch_c, attn_out[1]).astype(bf16).astype(f32)
    small_s[:16] = jnp.concatenate(
        [row_total(slope_s[k][:, part]) for k, _, part in blocks]
        + [
            row_total(grad_branch_f),
            row_total(grad_branch_c),
            gain_grad_2,
            shift_grad_2,
            gain_grad_1,
            shift_grad_1,
            row_total(grad_attended_c),
            jnp.zeros((1, D), f32),
        ],
        axis=0,
    )

    grad_attended_t = grad_attended_c.T
    grad_x = spread_rows(grad_attended_c)
    grad_vt[...] = dot(attn_in[1, 2], spread_cols(grad_attended_t)).astype(bf16)
    back_s[HQ:] = dot_nt(grad_x, attn_in[1, 2]).astype(bf16)
    inner = head_line(head_sums(grad_attended_t * mixed_t))
    own_share = jnp.exp2(total_s[0:1] - log_total)
    rows_k[D : 2 * D] = dot((mixed_s[...] * own_share).astype(bf16), grad_x).astype(bf16)
    mixed_s[...] = jnp.zeros_like(mixed_s)

    def in_turn(i, phases):
        for k, phase in enumerate(phases):
            pl.when(i == chunks * (k + 1) // (len(phases) + 1))(phase)

    mixed_phases = [phase for pair in zip(sum_f.phases[1:], sum_g.phases[1:]) for phase in pair]

    @pl.loop(0, chunks)
    def _(i):
        rows = pl.ds(pl.multiple_of(i * CHUNK, CHUNK), CHUNK)
        key_ct = key_in_s[rows].T
        memory_c = memory_s[rows]
        for p in range(4):
            cols = pair_cols(p)
            grad_probs = dot(memory_c, grad_vt[:, cols])
            probs = probs_s[rows, cols].astype(f32) * factor_s[pl.ds(i, 1), cols]
            probs_s[rows, cols] = probs.astype(bf16)
            grad_scores_s[rows, cols] = (probs * (grad_probs - inner[:, cols])).astype(bf16)
            mixed_s[:, cols] += dot(key_ct, grad_scores_s[rows, cols])
        in_turn(i, mixed_phases[:4])

    send_b[...] = project_heads(key_wt, mixed_s[...]) * scale
    swap_b = pltpu.make_async_remote_copy(
        src_ref=send_b,
        dst_ref=recv_b,
        send_sem=link_sem.at[2],
        recv_sem=link_sem.at[3],
        device_id=partner,
        device_id_type=pl.DeviceIdType.MESH,
    )
    swap_b.start()
    query_x = spread_rows(query_c.astype(f32))
    rows_k[:D] = (dot(mixed_s[...].astype(bf16), query_x) * scale).astype(bf16)
    sum_k.phases[0]()
    mixed_phases[4]()
    mixed_phases[5]()
    swap_b.wait()
    grad_query_c = (send_b[...] + recv_b[...]).T.astype(bf16)

    cross_pos_grad = dot_nt(grad_query_c, attn_in[1, 0])
    grad_first_in, gain_grad_0, shift_grad_0 = norm_backward(
        grad_second_in + cross_pos_grad, first_normed, first_rstd, gain[0:1]
    )
    grad_branch = grad_first_in.astype(bf16)
    grad_attended = dot_nt(grad_branch, attn_out[0]).astype(bf16).astype(f32)
    grad_probs = dot(value_self, spread_cols(grad_attended.T))
    inner_self = jnp.sum(probs_self * grad_probs, axis=0, keepdims=True)
    grad_scores = (probs_self * (grad_probs - inner_self)).astype(bf16)
    key_t = key_self.astype(f32).T.astype(bf16)
    grad_query_s = (
        own_blocks([dot(key_t[pair_rows(p)], grad_scores[:, pair_cols(p)]) for p in range(4)]) * scale
    ).T.astype(bf16)
    grad_key_s = (dot(grad_scores, spread_rows(query_self.astype(f32))) * scale).astype(bf16)
    grad_value_s = dot(probs_self_b, spread_rows(grad_attended)).astype(bf16)
    grad_mixed_q = dot_nt(grad_query_s, attn_in[0, 0]) + dot_nt(grad_key_s, attn_in[0, 1])
    queries_grad_out[...] = (grad_first_in + grad_mixed_q + dot_nt(grad_value_s, attn_in[0, 2]))[
        :NQ
    ].astype(bf16)
    small_s[16:] = jnp.concatenate(
        [
            row_total(grad_query_s),
            row_total(grad_value_s),
            row_total(grad_branch),
            row_total(grad_query_c),
            gain_grad_0,
            shift_grad_0,
            jnp.zeros((10, D), f32),
        ],
        axis=0,
    )
    @pl.when(member == 0)
    def _():
        rows_t[:D] = dot_tn(mixed_q, grad_query_s).astype(bf16)
        rows_t[D : 2 * D] = dot_tn(mixed_q, grad_key_s).astype(bf16)
        rows_t[2 * D : 3 * D] = dot_tn(queries_b, grad_value_s).astype(bf16)

    @pl.when(member == 1)
    def _():
        rows_t[:D] = dot_tn(cross_q, grad_query_c).astype(bf16)
        rows_t[D : 2 * D] = dot_tn(attended, grad_branch).astype(bf16)
        rows_t[ROW_POS:ROW_SMALL] = (grad_mixed_q + cross_pos_grad).astype(bf16)
        rows_t[ROW_SMALL : ROW_SMALL + 32] = small_s[...].astype(bf16)
        rows_t[ROW_SMALL + 32 : ROWS_T] = jnp.zeros((ROWS_T - ROW_SMALL - 32, D), bf16)

    sum_t.phases[0]()
    sum_k.phases[1]()
    mixed_phases[6]()
    mixed_phases[7]()

    @pl.loop(0, chunks)
    def _(i):
        rows = pl.ds(pl.multiple_of(i * CHUNK, CHUNK), CHUNK)
        both = jnp.concatenate([grad_scores_s[rows], probs_s[rows]], axis=1)
        memory_s[rows] = dot(both, back_s[...]).astype(bf16)
        pltpu.make_async_copy(memory_s.at[rows], memory_grad_hbm.at[0, rows], store_sem.at[i]).start()
        in_turn(
            i,
            [
                sum_t.phases[1],
                sum_k.phases[2],
                *mixed_phases[8:10],
                sum_t.phases[2],
                *mixed_phases[10:-2],
            ],
        )

    sum_k.phases[3]()
    sum_t.phases[3]()
    mixed_phases[-2]()
    mixed_phases[-1]()
    stores = [
        pltpu.make_async_copy(whole, target, load_sem.at[4 + k])
        for k, (whole, target) in enumerate(
            (
                (whole_f, whole_f_hbm),
                (whole_g, whole_g_hbm),
                (whole_t, whole_t_hbm),
                (whole_k, whole_k_hbm),
            )
        )
    ]
    stores[0].start()
    stores[1].start()
    for k in range(4, max(len(sum_k.phases), len(sum_t.phases))):
        if k < len(sum_t.phases):
            sum_t.phases[k]()
        if k < len(sum_k.phases):
            sum_k.phases[k]()
    stores[2].start()
    stores[3].start()

    @pl.loop(0, chunks)
    def _(i):
        rows = pl.ds(pl.multiple_of(i * CHUNK, CHUNK), CHUNK)
        pltpu.make_async_copy(memory_s.at[rows], memory_grad_hbm.at[0, rows], store_sem.at[i]).wait()

    for store in stores:
        store.wait()


def finish_kernel(
    result_in,
    queries_grad_in,
    memory_grad_in,
    whole_f,
    whole_g,
    whole_t,
    whole_k,
    result,
    queries_grad,
    memory_grad,
    attn_in_grad,
    attn_out_grad,
    attn_bias_grad,
    ffn_in_grad,
    ffn_in_bias_grad,
    ffn_out_grad,
    ffn_out_bias_grad,
    norm_gain_grad,
    norm_bias_grad,
    query_pos_grad,
    moved,
    in_sem,
    out_sem,
):
    pieces = in_sem.shape[0]
    piece = moved.shape[0] // pieces

    def fetch(j):
        rows = pl.ds(piece * j, piece)
        return pltpu.make_async_copy(memory_grad_in.at[0, rows], moved.at[rows], in_sem.at[j])

    def write(j):
        rows = pl.ds(piece * j, piece)
        return pltpu.make_async_copy(moved.at[rows], memory_grad.at[0, rows], out_sem.at[j])

    for j in range(pieces):
        fetch(j).start()
    result[0] = result_in[...]
    queries_grad[0] = queries_grad_in[...]
    for j in range(FF // D):
        piece_at = j % (FF // D // 2) * D
        sums = whole_f if j < FF // D // 2 else whole_g
        ffn_in_grad[:, D * j : D * j + D] = sums[0, piece_at : piece_at + D].astype(f32)
        ffn_out_grad[D * j : D * j + D] = sums[1, piece_at : piece_at + D].astype(f32)
    for j in range(pieces):
        fetch(j).wait()
        write(j).start()
    attn_out_grad[0] = whole_t[1, D : 2 * D].astype(f32)
    attn_out_grad[1] = whole_k[2 * D : 3 * D].astype(f32)
    for j in range(3):
        attn_in_grad[0, j] = whole_t[0, D * j : D * j + D].astype(f32)
    attn_in_grad[1, 0] = whole_t[1, :D].astype(f32)
    attn_in_grad[1, 1] = whole_k[:D].astype(f32)
    attn_in_grad[1, 2] = whole_k[D : 2 * D].astype(f32)
    query_pos_grad[...] = whole_t[1, ROW_POS:ROW_SMALL].astype(f32)[:NQ]
    small = whole_t[1, ROW_SMALL : ROW_SMALL + 32].astype(f32)
    ffn_in_bias_grad[...] = jnp.concatenate([small[j : j + 1] for j in range(FF // D)], axis=1)
    ffn_out_bias_grad[...] = small[8:9]
    for j, (own, cross) in enumerate(((16, 19), (17, 14), (18, 9))):
        attn_bias_grad[j, 0:1] = small[own : own + 1]
        attn_bias_grad[j, 1:2] = small[cross : cross + 1]
    norm_gain_grad[0:1] = small[20:21]
    norm_gain_grad[1:2] = small[12:13]
    norm_gain_grad[2:3] = small[10:11]
    norm_bias_grad[0:1] = small[21:22]
    norm_bias_grad[1:2] = small[13:14]
    norm_bias_grad[2:3] = small[11:12]
    for j in range(pieces):
        write(j).wait()


def body(
    pages,
    queries,
    memory,
    quarter_turns,
    token_order,
    lengths,
    attn_in,
    attn_out,
    attn_bias,
    ffn_in,
    ffn_in_bias,
    ffn_out,
    ffn_out_bias,
    norm_gain,
    norm_bias,
    query_pos,
    out_grad,
):
    tokens = memory.shape[1]
    chunks = tokens // CHUNK
    groups_f, groups_t, groups_k = sum_groups(pages)
    summed = [
        (padded(ROWS_F, pages), groups_f),
        (padded(ROWS_F, pages), groups_f),
        (padded(ROWS_T, pages), groups_t),
        (padded(ROWS_K, 2 * pages), groups_k),
    ]
    whole_shapes = [(2, rows, D) for rows, _ in summed[:3]] + [(summed[3][0], D)]
    sum_buffers = []
    for (rows, groups), shape in zip(summed, whole_shapes):
        landing = PageSum.landing_rows(pages, groups, rows)
        sum_buffers += [pltpu.VMEM(each, bf16) for each in ((rows, D), (landing, D), shape)]
    copies = 32
    vmem = pl.BlockSpec(memory_space=pltpu.VMEM)
    smem = pl.BlockSpec(memory_space=pltpu.SMEM)
    anywhere = pl.BlockSpec(memory_space=pl.ANY)
    parts = pl.pallas_call(
        functools.partial(layer_kernel, tokens, pages),
        out_shape=[
            jax.ShapeDtypeStruct((NQ, D), bf16),
            jax.ShapeDtypeStruct((NQ, D), bf16),
            jax.ShapeDtypeStruct((1, tokens, D), bf16),
            *(jax.ShapeDtypeStruct(shape, bf16) for shape in whole_shapes),
        ],
        in_specs=[
            vmem,
            anywhere,
            smem,
            vmem,
            smem,
            vmem,
            vmem,
            vmem,
            anywhere,
            vmem,
            anywhere,
            vmem,
            vmem,
            vmem,
            vmem,
            vmem,
            vmem,
        ],
        out_specs=[vmem, vmem, anywhere, anywhere, anywhere, anywhere, anywhere],
        scratch_shapes=[
            pltpu.VMEM((tokens, D), bf16),
            pltpu.VMEM((tokens, D), bf16),
            pltpu.VMEM((tokens, HQ), bf16),
            pltpu.VMEM((tokens, HQ), bf16),
            pltpu.VMEM((1, tokens), f32),
            pltpu.VMEM((D, HQ), bf16),
            pltpu.VMEM((D, HQ), bf16),
            pltpu.VMEM((2 * HQ, D), bf16),
            pltpu.VMEM((2, 2 * SIDE, D), bf16),
            pltpu.VMEM((chunks, HQ), f32),
            pltpu.VMEM((chunks, HQ), f32),
            pltpu.VMEM((8, HQ), f32),
            pltpu.VMEM((D, HQ), f32),
            pltpu.VMEM((3, NP, D), f32),
            pltpu.VMEM((D + 2 * HEADS, NP), f32),
            pltpu.VMEM((D + 2 * HEADS, NP), f32),
            pltpu.VMEM((D, NP), f32),
            pltpu.VMEM((D, NP), f32),
            pltpu.VMEM((32, D), f32),
            *sum_buffers,
            pltpu.SemaphoreType.DMA((8,)),
            pltpu.SemaphoreType.DMA((chunks,)),
            pltpu.SemaphoreType.DMA((4,)),
            *[pltpu.SemaphoreType.DMA((copies,))] * 8,
        ],
        compiler_params=pltpu.CompilerParams(
            collective_id=0, has_side_effects=True, vmem_limit_bytes=62 * 1024 * 1024
        ),
        cost_estimate=pl.CostEstimate(
            flops=2 * 8 * tokens * HQ * D, bytes_accessed=20 << 20, transcendentals=tokens * HQ
        ),
        name="decoder_layer",
    )(
        queries,
        memory,
        quarter_turns,
        token_order,
        lengths,
        attn_in,
        attn_out,
        attn_bias.transpose(1, 0, 2),
        ffn_in,
        ffn_in_bias,
        ffn_out,
        ffn_out_bias,
        norm_gain,
        norm_bias,
        query_pos,
        out_grad,
        jnp.asarray(position_table()),
    )
    outs = pl.pallas_call(
        finish_kernel,
        out_shape=[
            jax.ShapeDtypeStruct((1, NQ, D), bf16),
            jax.ShapeDtypeStruct((1, NQ, D), bf16),
            jax.ShapeDtypeStruct((1, tokens, D), bf16),
            jax.ShapeDtypeStruct((2, 3, D, D), f32),
            jax.ShapeDtypeStruct((2, D, D), f32),
            jax.ShapeDtypeStruct((3, 2, D), f32),
            jax.ShapeDtypeStruct((D, FF), f32),
            jax.ShapeDtypeStruct((1, FF), f32),
            jax.ShapeDtypeStruct((FF, D), f32),
            jax.ShapeDtypeStruct((1, D), f32),
            jax.ShapeDtypeStruct((3, D), f32),
            jax.ShapeDtypeStruct((3, D), f32),
            jax.ShapeDtypeStruct((NQ, D), f32),
        ],
        in_specs=[vmem, vmem, anywhere, vmem, vmem, vmem, vmem],
        out_specs=[vmem, vmem, anywhere] + [vmem] * 10,
        scratch_shapes=[
            pltpu.VMEM((tokens, D), bf16),
            pltpu.SemaphoreType.DMA((8,)),
            pltpu.SemaphoreType.DMA((8,)),
        ],
        compiler_params=pltpu.CompilerParams(vmem_limit_bytes=62 * 1024 * 1024),
        name="write_outputs",
    )(*parts)
    return (
        *outs[:5],
        outs[5].transpose(1, 0, 2),
        outs[6],
        outs[7].reshape(FF),
        outs[8],
        outs[9].reshape(D),
        *outs[10:],
    )


def solution(mesh):
    in_specs = (
        P("dp", None, None),
        P("dp", "blk", None),
        P("dp"),
        P("dp", "blk"),
        P("dp"),
        P(),
        P(),
        P(),
        P(),
        P(),
        P(),
        P(),
        P(),
        P(),
        P(),
        P("dp", None, None),
    )
    out_specs = (
        P("dp", None, None),
        P("dp", None, None),
        P("dp", "blk", None),
        P(),
        P(),
        P(),
        P(),
        P(),
        P(),
        P(),
        P(),
        P(),
        P(),
    )
    layer = functools.partial(body, mesh.shape["dp"])
    return jax.shard_map(layer, mesh=mesh, in_specs=in_specs, out_specs=out_specs, check_vma=False)
```

```python
import functools
import math

import jax
import jax.numpy as jnp
import numpy as np
from jax import lax
from jax.experimental import pallas as pl
from jax.experimental.pallas import tpu as pltpu
from jax.sharding import PartitionSpec as P

D = 256
HEADS = 8
HD = D // HEADS
SIDE = 128
NQ = 125
NP = 128
HQ = HEADS * NP
PAIR = 2 * NP
FF = 2048
CHUNK = 512

masked_score = -1e30
norm_eps = 1e-05
scale = 1.0 / math.sqrt(HD)
log2e = math.log2(math.e)

bf16 = jnp.bfloat16
f32 = jnp.float32

ROWS_F = FF // 2
ROW_POS = 2 * D
ROW_SMALL = 2 * D + NP
ROWS_T = 3 * D
ROWS_K = 3 * D
TILE = 16


def axes_of(pages):
    axes = {"core": (2, 1), "y": (2, 2)}
    stride = 4
    while stride < pages:
        radix = 4 if pages // stride % 4 == 0 else 2
        axes["z%d" % (len(axes) - 2)] = (radix, stride)
        stride *= radix
    axes["x"] = (2, 0)
    return axes


def far_axes(pages):
    return [(name,) for name in axes_of(pages) if name.startswith("z")]


def sum_groups(pages):
    far = far_axes(pages)
    return [("core",), ("y",), *far], [("core", "y"), *far], [("core",), ("x",), ("y",), *far]


def padded(rows, pages):
    unit = TILE * pages
    return (rows + unit - 1) // unit * unit


def position_table():
    half = D // 2
    channel = np.arange(half)
    inverse = np.exp((channel // 2).astype(np.float32) * np.float32(-2.0 * math.log(10000.0) / half))
    angle = (np.arange(SIDE, dtype=np.float32) + 1.0) * np.float32(2.0 * math.pi / SIDE)
    angle = angle[:, None] * inverse
    return np.where(channel % 2 == 0, np.sin(angle), np.cos(angle)).astype(np.float32)


def dot(a, b):
    return jnp.dot(a, b, preferred_element_type=f32)


def dot_nt(a, b):
    return lax.dot_general(a, b, (((1,), (1,)), ((), ())), preferred_element_type=f32)


def dot_tn(a, b):
    return lax.dot_general(a, b, (((0,), (0,)), ((), ())), preferred_element_type=f32)


def row_total(values):
    return jnp.sum(values.astype(f32), axis=0, keepdims=True)


def norm_forward(values):
    average = jnp.mean(values, axis=-1, keepdims=True)
    centred = values - average
    variance = jnp.mean(centred * centred, axis=-1, keepdims=True)
    rstd = lax.rsqrt(variance + norm_eps)
    return centred * rstd, rstd


def norm_backward(grad, normed, rstd, gain):
    grad_normed = grad * gain
    first = jnp.mean(grad_normed, axis=-1, keepdims=True)
    second = jnp.mean(grad_normed * normed, axis=-1, keepdims=True)
    grad_in = rstd * (grad_normed - first - normed * second)
    return grad_in, row_total(grad * normed), row_total(grad)


def spread_rows(rows):
    head = lax.broadcasted_iota(jnp.int32, (NP, D), 1) // HD
    return jnp.concatenate(
        [jnp.where(head == h, rows, 0.0) for h in range(HEADS)], axis=0
    ).astype(bf16)


def spread_cols(cols):
    head = lax.broadcasted_iota(jnp.int32, (D, NP), 0) // HD
    return jnp.concatenate(
        [jnp.where(head == h, cols, 0.0) for h in range(HEADS)], axis=1
    ).astype(bf16)


def own_heads(full):
    return jnp.concatenate(
        [full[HD * h : HD * h + HD, NP * h : NP * h + NP] for h in range(HEADS)], axis=0
    )


def project_heads(weight_t, sums):
    high = sums.astype(bf16)
    low = (sums - high.astype(f32)).astype(bf16)
    return own_heads(dot(weight_t, high) + dot(weight_t, low))


def own_blocks(pairs):
    parts = []
    for pair in pairs:
        parts += [pair[:HD, :NP], pair[HD:, NP:]]
    return jnp.concatenate(parts, axis=0)


def head_rows(row):
    return jnp.concatenate([row[:, NP * h : NP * h + NP] for h in range(HEADS)], axis=0)


def head_line(rows):
    return jnp.concatenate([rows[h : h + 1] for h in range(HEADS)], axis=1)


def per_channel(rows):
    return jnp.concatenate(
        [jnp.broadcast_to(rows[h : h + 1], (HD, NP)) for h in range(HEADS)], axis=0
    )


def head_sums(cols):
    return jnp.concatenate(
        [jnp.sum(cols[HD * h : HD * h + HD], axis=0, keepdims=True) for h in range(HEADS)], axis=0
    )


def pair_cols(p):
    return slice(PAIR * p, PAIR * p + PAIR)


def pair_rows(p):
    return slice(2 * HD * p, 2 * HD * p + 2 * HD)


class Place:
    def __init__(self, pages):
        self.axes = axes_of(pages)
        self.page = lax.axis_index("dp")
        self.member = lax.axis_index("blk")
        self.digit = {
            name: self.member if name == "x" else lax.rem(self.page // stride, radix)
            for name, (radix, stride) in self.axes.items()
        }

    def size(self, group):
        return math.prod(self.axes[name][0] for name in group)

    def index(self, group):
        index = 0
        for name in group:
            index = index * self.axes[name][0] + self.digit[name]
        return index

    def peer(self, group, hop):
        index = lax.rem(self.index(group) + hop, self.size(group))
        page, member, rest = self.page, self.member, index
        for name in reversed(group):
            radix, stride = self.axes[name]
            digit = lax.rem(rest, radix)
            rest = rest // radix
            if name == "x":
                member = digit
            else:
                page = page + (digit - self.digit[name]) * stride
        return (page, member), index


class PageSum:
    def __init__(self, place, groups, back, rows, landing, whole, sent, arrived):
        self.place, self.groups, self.back = place, groups, back
        self.rows, self.landing, self.whole = rows, landing, whole
        self.sent, self.arrived = sent, arrived
        self.slots = 0
        self.extents = [rows.shape[0]]
        self.bases = [0]
        self.landings = []
        at = 0
        for group in groups:
            size = place.size(group)
            extent = self.extents[-1] // size
            self.landings.append(at)
            at += (size - 1) * extent
            self.bases.append(pl.multiple_of(self.bases[-1] + place.index(group) * extent, TILE))
            self.extents.append(extent)
        last = len(groups)
        moves = [self.scatter_moves(s) for s in range(last)]
        near = {"all": 0, "across": 1, "sides": 2}[back]
        moves += [self.gather_moves(s) for s in range(last - 1, near - 1, -1)]
        if back == "sides":
            moves += [self.side_moves(), self.corner_moves(), self.core_moves()]
        elif back == "across":
            moves += [self.across_moves(), self.core_moves()]
        self.phases = [functools.partial(self.step, moves, k) for k in range(len(moves) + 1)]

    @staticmethod
    def landing_rows(pages, groups, rows):
        axes = axes_of(pages)
        total, extent = 0, rows
        for group in groups:
            size = math.prod(axes[name][0] for name in group)
            extent //= size
            total += (size - 1) * extent
        return total

    def step(self, moves, k):
        last = len(self.groups)
        if k > 0:
            for move in moves[k - 1]:
                self.copy(*move).wait()
        if 0 < k <= last:
            total = self.scatter_sum(k - 1)
            region = pl.ds(self.bases[k], self.extents[k])
            if k < last:
                self.rows[region] = total
            elif len(self.whole.shape) == 3:
                self.whole[self.place.member, region] = total
            else:
                self.whole[region] = total
        if k < len(moves):
            for move in moves[k]:
                self.copy(*move).start()

    def copy(self, slot, source, target, device):
        return pltpu.make_async_remote_copy(
            src_ref=source(),
            dst_ref=target(),
            send_sem=self.sent.at[slot],
            recv_sem=self.arrived.at[slot],
            device_id=device,
            device_id_type=pl.DeviceIdType.MESH,
        )

    def new_slot(self):
        self.slots += 1
        return self.slots - 1

    def same(self, device, view):
        return (self.new_slot(), view, view, device)

    def scatter_moves(self, step):
        group = self.groups[step]
        extent = self.extents[step + 1]
        moves = []
        for hop in range(1, self.place.size(group)):
            device, other = self.place.peer(group, hop)
            start = pl.multiple_of(self.bases[step] + other * extent, TILE)
            landing = self.landings[step] + (hop - 1) * extent
            moves.append(
                (
                    self.new_slot(),
                    functools.partial(self.part, self.rows, start, extent),
                    functools.partial(self.part, self.landing, landing, extent),
                    device,
                )
            )
        return moves

    @staticmethod
    def part(ref, start, extent):
        return ref.at[pl.ds(start, extent)]

    def half(self, member, start, extent):
        if len(self.whole.shape) == 3:
            return self.whole.at[member, pl.ds(start, extent)]
        return self.whole.at[pl.ds(start, extent)]

    def scatter_sum(self, step):
        extent = self.extents[step + 1]
        total = self.rows[pl.ds(self.bases[step + 1], extent)].astype(f32)
        for hop in range(1, self.place.size(self.groups[step])):
            landing = self.landings[step] + (hop - 1) * extent
            total = total + self.landing[pl.ds(landing, extent)].astype(f32)
        return total.astype(bf16)

    def gather_moves(self, step):
        group = self.groups[step]
        view = functools.partial(self.half, self.place.member, self.bases[step + 1], self.extents[step + 1])
        return [
            self.same(self.place.peer(group, hop)[0], view) for hop in range(1, self.place.size(group))
        ]

    def own_quarter(self):
        step = 2 if len(self.groups[0]) == 1 else 1
        return self.bases[step], self.extents[step]

    def side_moves(self):
        view = functools.partial(self.half, self.place.member, *self.own_quarter())
        return [self.same(self.place.peer((name,), 1)[0], view) for name in ("y", "x")]

    def corner_moves(self):
        base, extent = self.own_quarter()
        other = pl.multiple_of(base + (1 - 2 * self.place.digit["y"]) * extent, TILE)
        view = functools.partial(self.half, self.place.member, other, extent)
        return [self.same(self.place.peer(("x",), 1)[0], view)]

    def across_moves(self):
        view = functools.partial(self.half, self.place.member, *self.own_quarter())
        return [self.same(self.place.peer(("x", "y"), hop)[0], view) for hop in range(1, 4)]

    def core_moves(self):
        extent = self.extents[0] // 2
        start = pl.multiple_of(self.place.digit["core"] * extent, TILE)
        device, _ = self.place.peer(("core",), 1)
        return [self.same(device, functools.partial(self.half, m, start, extent)) for m in range(2)]


def clear_rest(ref, used):
    if ref.shape[0] > used:
        ref[used:] = jnp.zeros((ref.shape[0] - used, D), ref.dtype)


def layer_kernel(
    tokens,
    pages,
    queries_in,
    memory_hbm,
    turns_in,
    order_in,
    lengths_in,
    attn_in,
    attn_out,
    attn_bias,
    ffn_in_hbm,
    ffn_in_bias,
    ffn_out_hbm,
    ffn_out_bias,
    norm_gain,
    norm_bias,
    pos_in,
    out_grad_in,
    table_in,
    result_out,
    queries_grad_out,
    memory_grad_hbm,
    whole_f_hbm,
    whole_g_hbm,
    whole_t_hbm,
    whole_k_hbm,
    memory_s,
    key_in_s,
    probs_s,
    grad_scores_s,
    code_s,
    query_kt,
    grad_vt,
    back_s,
    table_s,
    shifts_s,
    factor_s,
    total_s,
    mixed_s,
    pad_s,
    send_a,
    recv_a,
    send_t,
    recv_t,
    send_b,
    recv_b,
    small_s,
    rows_f,
    landing_f,
    whole_f,
    rows_g,
    landing_g,
    whole_g,
    rows_t,
    landing_t,
    whole_t,
    rows_k,
    landing_k,
    whole_k,
    load_sem,
    store_sem,
    link_sem,
    sent_f,
    arrived_f,
    sent_g,
    arrived_g,
    sent_t,
    arrived_t,
    sent_k,
    arrived_k,
):
    member = lax.axis_index("blk")
    partner = (lax.axis_index("dp"), 1 - member)
    chunks = tokens // CHUNK

    place = Place(pages)
    groups_f, groups_t, groups_k = sum_groups(pages)
    sum_f = PageSum(place, groups_f, "sides", rows_f, landing_f, whole_f, sent_f, arrived_f)
    sum_g = PageSum(place, groups_f, "sides", rows_g, landing_g, whole_g, sent_g, arrived_g)
    sum_t = PageSum(place, groups_t, "across", rows_t, landing_t, whole_t, sent_t, arrived_t)
    sum_k = PageSum(place, groups_k, "all", rows_k, landing_k, whole_k, sent_k, arrived_k)

    barrier = pltpu.get_barrier_semaphore()
    peers = [
        place.peer(group, hop)[0]
        for group in [("x", "core", "y"), *far_axes(pages)]
        for hop in range(1, place.size(group))
    ]
    for peer in peers:
        pl.semaphore_signal(barrier, inc=1, device_id=peer, device_id_type=pl.DeviceIdType.MESH)

    load_memory = pltpu.make_async_copy(memory_hbm.at[0], memory_s, load_sem.at[0])
    half = FF // 2
    ffn_in_s = [grad_scores_s.at[D * k : D * k + D] for k in range(2)]
    ffn_out_s = grad_scores_s.at[2 * D : 2 * D + FF, :D]
    free = 2 * D + FF
    active_s = [grad_scores_s.at[free + NP * k : free + NP * k + NP] for k in range(2)]
    slope_s = [grad_scores_s.at[free + NP * k : free + NP * k + NP] for k in range(2, 4)]
    load_ffn = [
        pltpu.make_async_copy(ffn_in_hbm.at[:, half * k : half * k + half], ffn_in_s[k], load_sem.at[1 + k])
        for k in range(2)
    ]
    load_ffn.append(pltpu.make_async_copy(ffn_out_hbm, ffn_out_s, load_sem.at[3]))
    load_memory.start()
    for load in load_ffn:
        load.start()

    pairs = [attn_bias[j].astype(f32) for j in range(3)]
    bias = jnp.concatenate([pair[k : k + 1] for k in range(2) for pair in pairs], axis=0)
    gain = norm_gain[...].astype(f32)
    shift = norm_bias[...].astype(f32)

    order = order_in[...]
    turn = turns_in[0]
    row_at = order >> 7
    col_at = order & 127
    top = SIDE - 1
    row_new = jnp.where(
        turn == 0, row_at, jnp.where(turn == 1, col_at, jnp.where(turn == 2, top - row_at, top - col_at))
    )
    col_new = jnp.where(
        turn == 0, col_at, jnp.where(turn == 1, top - row_at, jnp.where(turn == 2, top - col_at, row_at))
    )
    past = jnp.where(order < lengths_in[0], 0, SIDE * SIDE)
    code_s[...] = (row_new * SIDE + col_new + past).astype(f32)

    pad_s[...] = jnp.zeros_like(pad_s)
    pad_s[0, :NQ] = queries_in[0].astype(f32)
    pad_s[1, :NQ] = pos_in[...].astype(f32)
    pad_s[2, :NQ] = out_grad_in[0].astype(f32)
    queries_f = pad_s[0]
    pos_f = pad_s[1]
    queries_b = queries_f.astype(bf16)
    mixed_q = (queries_f + pos_f).astype(bf16)
    query_self = (dot(mixed_q, attn_in[0, 0]) + bias[0:1]).astype(bf16)
    key_self = dot(mixed_q, attn_in[0, 1]).astype(bf16)
    value_self = (dot(queries_b, attn_in[0, 2]) + bias[1:2]).astype(bf16)
    scores = dot(key_self, spread_cols(query_self.astype(f32).T)) * scale
    own_key = lax.broadcasted_iota(jnp.int32, (NP, HQ), 0) < NQ
    scores = jnp.where(own_key, scores, masked_score)
    raised = jnp.exp(scores - jnp.max(scores, axis=0, keepdims=True))
    probs_self = raised / jnp.sum(raised, axis=0, keepdims=True)
    probs_self_b = probs_self.astype(bf16)
    value_t = value_self.astype(f32).T.astype(bf16)
    attended = own_blocks(
        [dot(value_t[pair_rows(p)], probs_self_b[:, pair_cols(p)]) for p in range(4)]
    ).T.astype(bf16)
    first_normed, first_rstd = norm_forward(queries_f + dot(attended, attn_out[0]) + bias[2:3])
    first = first_normed * gain[0:1] + shift[0:1]
    cross_q = (first + pos_f).astype(bf16)
    query_c = (dot(cross_q, attn_in[1, 0]) + bias[3:4]).astype(bf16)
    query_x = spread_rows(query_c.astype(f32))
    query_k = dot(attn_in[1, 1], spread_cols(query_c.astype(f32).T))
    query_kt[...] = (query_k * (scale * log2e)).astype(bf16)
    back_s[:HQ] = (dot_nt(query_x, attn_in[1, 1]) * scale).astype(bf16)
    table = table_in[...]
    nothing = jnp.zeros((SIDE, D // 2), f32)
    table = jnp.concatenate(
        [jnp.concatenate([table, nothing], axis=1), jnp.concatenate([nothing, table], axis=1)], axis=0
    )
    table_high = table.astype(bf16)
    table_s[0] = table_high
    table_s[1] = (table - table_high.astype(f32)).astype(bf16)

    load_memory.wait()
    lane = lax.broadcasted_iota(jnp.int32, (CHUNK, NP), 1)

    @pl.loop(0, chunks)
    def _(i):
        rows = pl.ds(pl.multiple_of(i * CHUNK, CHUNK), CHUNK)
        line = code_s[:, rows]
        code = jnp.concatenate(
            [
                jnp.broadcast_to(line[:, NP * j : NP * j + NP], (NP, NP)).T
                for j in range(CHUNK // NP)
            ],
            axis=0,
        ).astype(jnp.int32)
        row_hot = jnp.where(((code >> 7) & 127) == lane, 1.0, 0.0)
        col_hot = jnp.where((code & 127) == lane, 1.0, 0.0)
        hot = jnp.concatenate([row_hot, col_hot], axis=1).astype(bf16)
        block = memory_s[rows].astype(f32)
        key_in_s[rows] = (block + dot(hot, table_s[0]) + dot(hot, table_s[1])).astype(bf16)

    def score_chunk(i, out, top):
        rows = pl.ds(pl.multiple_of(i * CHUNK, CHUNK), CHUNK)
        line = code_s[:, rows]
        code = jnp.concatenate(
            [
                jnp.broadcast_to(line[:, NP * j : NP * j + NP], (NP, NP)).T
                for j in range(CHUNK // NP)
            ],
            axis=0,
        )
        allowed = code < SIDE * SIDE
        allowed = jnp.concatenate([allowed, allowed], axis=1)
        key_in = key_in_s[rows]
        for p in range(4):
            cols = pair_cols(p)
            part = jnp.where(allowed, dot(key_in, query_kt[:, cols]), masked_score)
            out[:, cols] = part
            top[0:1, cols] = jnp.max(part, axis=0, keepdims=True)

    def attend_chunk(i, scored, top):
        rows = pl.ds(pl.multiple_of(i * CHUNK, CHUNK), CHUNK)
        memory_ct = memory_s[rows].T
        for p in range(4):
            cols = pair_cols(p)
            before = total_s[0:1, cols]
            highest = jnp.maximum(before, top[0:1, cols])
            raised = jnp.exp2(scored[:, cols] - highest)
            fade = jnp.exp2(before - highest)
            total_s[0:1, cols] = highest
            total_s[1:2, cols] = total_s[1:2, cols] * fade + jnp.sum(raised, axis=0, keepdims=True)
            shifts_s[pl.ds(i, 1), cols] = highest
            probs_s[rows, cols] = raised.astype(bf16)
            mixed_s[:, cols] = mixed_s[:, cols] * fade + dot(memory_ct, probs_s[rows, cols])

    total_s[0:1] = jnp.full((1, HQ), -3e38, f32)
    total_s[1:2] = jnp.zeros((1, HQ), f32)
    mixed_s[...] = jnp.zeros_like(mixed_s)
    def attend_all(score_a, score_b, top_a, top_b):
        score_chunk(0, score_a, top_a)

        @pl.loop(0, chunks // 2)
        def _(j):
            i = j * 2
            score_chunk(i + 1, score_b, top_b)
            attend_chunk(i, score_a, top_a)
            score_chunk(jnp.minimum(i + 2, chunks - 1), score_a, top_a)
            attend_chunk(i + 1, score_b, top_b)

    score_buffer = pltpu.VMEM((CHUNK, HQ), f32)
    top_buffer = pltpu.VMEM((8, HQ), f32)
    pl.run_scoped(attend_all, score_buffer, score_buffer, top_buffer, top_buffer)

    value_wt = attn_in[1, 2].astype(f32).T.astype(bf16)
    key_wt = attn_in[1, 1].astype(f32).T.astype(bf16)
    send_a[...] = project_heads(value_wt, mixed_s[...]).astype(bf16)
    send_t[:HEADS] = head_rows(total_s[0:1])
    send_t[HEADS:] = head_rows(total_s[1:2])
    pl.semaphore_wait(barrier, len(peers))
    swap_a = pltpu.make_async_remote_copy(
        src_ref=send_a,
        dst_ref=recv_a,
        send_sem=link_sem.at[0],
        recv_sem=link_sem.at[1],
        device_id=partner,
        device_id_type=pl.DeviceIdType.MESH,
    )
    swap_t = pltpu.make_async_remote_copy(
        src_ref=send_t,
        dst_ref=recv_t,
        send_sem=link_sem.at[4],
        recv_sem=link_sem.at[5],
        device_id=partner,
        device_id_type=pl.DeviceIdType.MESH,
    )
    swap_a.start()
    swap_t.start()
    swap_a.wait()
    swap_t.wait()
    is_first = member == 0
    own, other = send_a[...].astype(f32), recv_a[...].astype(f32)
    left = jnp.where(is_first, own, other)
    right = jnp.where(is_first, other, own)
    own, other = send_t[...], recv_t[...]
    left_t = jnp.where(is_first, own, other)
    right_t = jnp.where(is_first, other, own)
    highest = jnp.maximum(left_t[:HEADS], right_t[:HEADS])
    fade_l = jnp.exp2(left_t[:HEADS] - highest)
    fade_r = jnp.exp2(right_t[:HEADS] - highest)
    total = left_t[HEADS:] * fade_l + right_t[HEADS:] * fade_r
    mixed_t = left * per_channel(fade_l / total) + right * per_channel(fade_r / total)
    log_total = head_line(highest + jnp.log2(total))
    factor_s[...] = jnp.exp2(shifts_s[...] - log_total)
    attended_c = (mixed_t.T + bias[4:5]).astype(bf16)

    second_normed, second_rstd = norm_forward(first + dot(attended_c, attn_out[1]) + bias[5:6])
    second = second_normed * gain[1:2] + shift[1:2]
    ffn_input = second.astype(bf16)
    load_ffn[0].wait()
    load_ffn[1].wait()
    blocks = [(j // 4, slice(D * j, D * j + D), slice(j % 4 * D, j % 4 * D + D)) for j in range(FF // D)]
    hidden_bias = ffn_in_bias[...].astype(f32).reshape(1, FF)
    def feed_forward(gate_s):
        for k, cols, part in blocks:
            hidden = dot(ffn_input, ffn_in_s[k][:, part]) + hidden_bias[:, cols]
            half_gate = 0.5 + 0.5 * lax.erf(hidden * math.sqrt(0.5))
            active_s[k][:, part] = (hidden * half_gate).astype(bf16)
            gate_s[:, cols] = half_gate + hidden * jnp.exp(hidden * hidden * -0.5) * (
                1.0 / math.sqrt(2.0 * math.pi)
            )
        load_ffn[2].wait()
        third_normed, third_rstd = norm_forward(
            second
            + dot(active_s[0][...], ffn_out_s[:half])
            + dot(active_s[1][...], ffn_out_s[half:])
            + ffn_out_bias[...].astype(f32).reshape(1, D)
        )
        result_out[...] = (third_normed * gain[2:3] + shift[2:3])[:NQ].astype(bf16)
        grad_third, gain_grad_2, shift_grad_2 = norm_backward(
            pad_s[2], third_normed, third_rstd, gain[2:3]
        )
        grad_branch_f = grad_third.astype(bf16)
        for k, cols, part in blocks:
            grad_hidden = dot_nt(grad_branch_f, ffn_out_s[cols]) * gate_s[:, cols]
            slope_s[k][:, part] = grad_hidden.astype(bf16)
        return grad_third, gain_grad_2, shift_grad_2, grad_branch_f

    grad_third, gain_grad_2, shift_grad_2, grad_branch_f = pl.run_scoped(
        feed_forward, pltpu.VMEM((NP, FF), f32)
    )
    grad_second = grad_third + dot_nt(slope_s[0][...], ffn_in_s[0][...])
    grad_second += dot_nt(slope_s[1][...], ffn_in_s[1][...])
    grad_second_in, gain_grad_1, shift_grad_1 = norm_backward(
        grad_second, second_normed, second_rstd, gain[1:2]
    )
    grad_branch_c = grad_second_in.astype(bf16)
    ffn_input_t = second.T.astype(bf16)

    def ffn_rows(target, k):
        @pl.when(member == 0)
        def _():
            for j in range(4):
                part = slice(D * j, D * j + D)
                target[part] = dot(ffn_input_t, slope_s[k][:, part]).astype(bf16)

        @pl.when(member == 1)
        def _():
            for j in range(4):
                part = slice(D * j, D * j + D)
                target[part] = dot_tn(active_s[k][:, part], grad_branch_f).astype(bf16)

    ffn_rows(rows_f, 0)
    sum_f.phases[0]()
    ffn_rows(rows_g, 1)

    is_first = member == 0
    out_grad_c = dot_tn(attended_c, grad_branch_c)
    rows_k[2 * D : 3 * D] = jnp.where(is_first, out_grad_c, 0.0).astype(bf16)

    clear_rest(rows_f, ROWS_F)
    clear_rest(rows_g, ROWS_F)
    clear_rest(rows_t, ROWS_T)
    clear_rest(rows_k, ROWS_K)
    sum_g.phases[0]()
    grad_attended_c = dot_nt(grad_branch_c, attn_out[1]).astype(bf16).astype(f32)
    small_s[:16] = jnp.concatenate(
        [row_total(slope_s[k][:, part]) for k, _, part in blocks]
        + [
            row_total(grad_branch_f),
            row_total(grad_branch_c),
            gain_grad_2,
            shift_grad_2,
            gain_grad_1,
            shift_grad_1,
            row_total(grad_attended_c),
            jnp.zeros((1, D), f32),
        ],
        axis=0,
    )

    grad_attended_t = grad_attended_c.T
    grad_x = spread_rows(grad_attended_c)
    grad_vt[...] = dot(attn_in[1, 2], spread_cols(grad_attended_t)).astype(bf16)
    back_s[HQ:] = dot_nt(grad_x, attn_in[1, 2]).astype(bf16)
    inner = head_line(head_sums(grad_attended_t * mixed_t))
    own_share = jnp.exp2(total_s[0:1] - log_total)
    rows_k[D : 2 * D] = dot((mixed_s[...] * own_share).astype(bf16), grad_x).astype(bf16)
    mixed_s[...] = jnp.zeros_like(mixed_s)

    queue_f = [phase for pair in zip(sum_f.phases[1:], sum_g.phases[1:]) for phase in pair]
    queue_t = list(sum_t.phases)
    queue_k = list(sum_k.phases)

    def take(queue):
        if queue:
            queue.pop(0)()

    def at(i, steps):
        for step, queue in steps:
            pl.when(i == (step * chunks) // 16)(queue.pop(0))

    @pl.loop(0, chunks)
    def _(i):
        rows = pl.ds(pl.multiple_of(i * CHUNK, CHUNK), CHUNK)
        key_ct = key_in_s[rows].T
        memory_c = memory_s[rows]
        for p in range(4):
            cols = pair_cols(p)
            grad_probs = dot(memory_c, grad_vt[:, cols])
            probs = probs_s[rows, cols].astype(f32) * factor_s[pl.ds(i, 1), cols]
            probs_s[rows, cols] = probs.astype(bf16)
            grad_scores_s[rows, cols] = (probs * (grad_probs - inner[:, cols])).astype(bf16)
            mixed_s[:, cols] += dot(key_ct, grad_scores_s[rows, cols])
        at(i, [(3, queue_f), (4, queue_f), (8, queue_f), (9, queue_f), (13, queue_f), (14, queue_f)])

    send_b[...] = (project_heads(key_wt, mixed_s[...]) * scale).astype(bf16)
    swap_b = pltpu.make_async_remote_copy(
        src_ref=send_b,
        dst_ref=recv_b,
        send_sem=link_sem.at[2],
        recv_sem=link_sem.at[3],
        device_id=partner,
        device_id_type=pl.DeviceIdType.MESH,
    )
    swap_b.start()
    query_x = spread_rows(query_c.astype(f32))
    rows_k[:D] = (dot(mixed_s[...].astype(bf16), query_x) * scale).astype(bf16)
    take(queue_k)
    take(queue_f)
    take(queue_f)
    swap_b.wait()
    take(queue_k)
    grad_query_c = (send_b[...].astype(f32) + recv_b[...].astype(f32)).T.astype(bf16)

    cross_pos_grad = dot_nt(grad_query_c, attn_in[1, 0])
    grad_first_in, gain_grad_0, shift_grad_0 = norm_backward(
        grad_second_in + cross_pos_grad, first_normed, first_rstd, gain[0:1]
    )
    grad_branch = grad_first_in.astype(bf16)
    grad_attended = dot_nt(grad_branch, attn_out[0]).astype(bf16).astype(f32)
    take(queue_k)
    grad_probs = dot(value_self, spread_cols(grad_attended.T))
    inner_self = jnp.sum(probs_self * grad_probs, axis=0, keepdims=True)
    grad_scores = (probs_self * (grad_probs - inner_self)).astype(bf16)
    key_t = key_self.astype(f32).T.astype(bf16)
    grad_query_s = (
        own_blocks([dot(key_t[pair_rows(p)], grad_scores[:, pair_cols(p)]) for p in range(4)]) * scale
    ).T.astype(bf16)
    grad_key_s = (dot(grad_scores, spread_rows(query_self.astype(f32))) * scale).astype(bf16)
    grad_value_s = dot(probs_self_b, spread_rows(grad_attended)).astype(bf16)
    grad_mixed_q = dot_nt(grad_query_s, attn_in[0, 0]) + dot_nt(grad_key_s, attn_in[0, 1])
    queries_grad_out[...] = (grad_first_in + grad_mixed_q + dot_nt(grad_value_s, attn_in[0, 2]))[
        :NQ
    ].astype(bf16)
    small_s[16:] = jnp.concatenate(
        [
            row_total(grad_query_s),
            row_total(grad_value_s),
            row_total(grad_branch),
            row_total(grad_query_c),
            gain_grad_0,
            shift_grad_0,
            jnp.zeros((10, D), f32),
        ],
        axis=0,
    )
    @pl.when(member == 0)
    def _():
        rows_t[:D] = dot_tn(mixed_q, grad_query_s).astype(bf16)
        rows_t[D : 2 * D] = dot_tn(mixed_q, grad_key_s).astype(bf16)
        rows_t[2 * D : 3 * D] = dot_tn(queries_b, grad_value_s).astype(bf16)

    @pl.when(member == 1)
    def _():
        rows_t[:D] = dot_tn(cross_q, grad_query_c).astype(bf16)
        rows_t[D : 2 * D] = dot_tn(attended, grad_branch).astype(bf16)
        rows_t[ROW_POS:ROW_SMALL] = (grad_mixed_q + cross_pos_grad).astype(bf16)
        rows_t[ROW_SMALL : ROW_SMALL + 32] = small_s[...].astype(bf16)
        rows_t[ROW_SMALL + 32 : ROWS_T] = jnp.zeros((ROWS_T - ROW_SMALL - 32, D), bf16)

    take(queue_t)
    take(queue_k)
    take(queue_f)
    take(queue_f)

    @pl.loop(0, chunks)
    def _(i):
        rows = pl.ds(pl.multiple_of(i * CHUNK, CHUNK), CHUNK)
        both = jnp.concatenate([grad_scores_s[rows], probs_s[rows]], axis=1)
        memory_s[rows] = dot(both, back_s[...]).astype(bf16)
        pltpu.make_async_copy(memory_s.at[rows], memory_grad_hbm.at[0, rows], store_sem.at[i]).start()
        at(
            i,
            [
                (3, queue_k),
                (5, queue_t),
                (6, queue_f),
                (7, queue_f),
                (8, queue_k),
                (9, queue_t),
                (11, queue_k),
                (13, queue_t),
                (14, queue_k),
            ],
        )

    while queue_f:
        take(queue_f)
    stores = [
        pltpu.make_async_copy(whole, target, load_sem.at[4 + k])
        for k, (whole, target) in enumerate(
            (
                (whole_f, whole_f_hbm),
                (whole_g, whole_g_hbm),
                (whole_t, whole_t_hbm),
                (whole_k, whole_k_hbm),
            )
        )
    ]
    stores[0].start()
    stores[1].start()
    while queue_t or queue_k:
        take(queue_t)
        take(queue_k)
    stores[2].start()
    stores[3].start()

    @pl.loop(0, chunks)
    def _(i):
        rows = pl.ds(pl.multiple_of(i * CHUNK, CHUNK), CHUNK)
        pltpu.make_async_copy(memory_s.at[rows], memory_grad_hbm.at[0, rows], store_sem.at[i]).wait()

    for store in stores:
        store.wait()


def finish_kernel(
    result_in,
    queries_grad_in,
    memory_grad_in,
    whole_f,
    whole_g,
    whole_t,
    whole_k,
    result,
    queries_grad,
    memory_grad,
    attn_in_grad,
    attn_out_grad,
    attn_bias_grad,
    ffn_in_grad,
    ffn_in_bias_grad,
    ffn_out_grad,
    ffn_out_bias_grad,
    norm_gain_grad,
    norm_bias_grad,
    query_pos_grad,
    moved,
    in_sem,
    out_sem,
):
    pieces = in_sem.shape[0]
    piece = moved.shape[0] // pieces

    def fetch(j):
        rows = pl.ds(piece * j, piece)
        return pltpu.make_async_copy(memory_grad_in.at[0, rows], moved.at[rows], in_sem.at[j])

    def write(j):
        rows = pl.ds(piece * j, piece)
        return pltpu.make_async_copy(moved.at[rows], memory_grad.at[0, rows], out_sem.at[j])

    for j in range(pieces):
        fetch(j).start()
    result[0] = result_in[...]
    queries_grad[0] = queries_grad_in[...]
    for j in range(FF // D):
        piece_at = j % (FF // D // 2) * D
        sums = whole_f if j < FF // D // 2 else whole_g
        ffn_in_grad[:, D * j : D * j + D] = sums[0, piece_at : piece_at + D].astype(f32)
        ffn_out_grad[D * j : D * j + D] = sums[1, piece_at : piece_at + D].astype(f32)
    for j in range(pieces):
        fetch(j).wait()
        write(j).start()
    attn_out_grad[0] = whole_t[1, D : 2 * D].astype(f32)
    attn_out_grad[1] = whole_k[2 * D : 3 * D].astype(f32)
    for j in range(3):
        attn_in_grad[0, j] = whole_t[0, D * j : D * j + D].astype(f32)
    attn_in_grad[1, 0] = whole_t[1, :D].astype(f32)
    attn_in_grad[1, 1] = whole_k[:D].astype(f32)
    attn_in_grad[1, 2] = whole_k[D : 2 * D].astype(f32)
    query_pos_grad[...] = whole_t[1, ROW_POS:ROW_SMALL].astype(f32)[:NQ]
    small = whole_t[1, ROW_SMALL : ROW_SMALL + 32].astype(f32)
    ffn_in_bias_grad[...] = jnp.concatenate([small[j : j + 1] for j in range(FF // D)], axis=1)
    ffn_out_bias_grad[...] = small[8:9]
    for j, (own, cross) in enumerate(((16, 19), (17, 14), (18, 9))):
        attn_bias_grad[j, 0:1] = small[own : own + 1]
        attn_bias_grad[j, 1:2] = small[cross : cross + 1]
    norm_gain_grad[0:1] = small[20:21]
    norm_gain_grad[1:2] = small[12:13]
    norm_gain_grad[2:3] = small[10:11]
    norm_bias_grad[0:1] = small[21:22]
    norm_bias_grad[1:2] = small[13:14]
    norm_bias_grad[2:3] = small[11:12]
    for j in range(pieces):
        write(j).wait()


def body(
    pages,
    queries,
    memory,
    quarter_turns,
    token_order,
    lengths,
    attn_in,
    attn_out,
    attn_bias,
    ffn_in,
    ffn_in_bias,
    ffn_out,
    ffn_out_bias,
    norm_gain,
    norm_bias,
    query_pos,
    out_grad,
):
    tokens = memory.shape[1]
    chunks = tokens // CHUNK
    groups_f, groups_t, groups_k = sum_groups(pages)
    summed = [
        (padded(ROWS_F, pages), groups_f),
        (padded(ROWS_F, pages), groups_f),
        (padded(ROWS_T, pages), groups_t),
        (padded(ROWS_K, 2 * pages), groups_k),
    ]
    whole_shapes = [(2, rows, D) for rows, _ in summed[:3]] + [(summed[3][0], D)]
    sum_buffers = []
    for (rows, groups), shape in zip(summed, whole_shapes):
        landing = PageSum.landing_rows(pages, groups, rows)
        sum_buffers += [pltpu.VMEM(each, bf16) for each in ((rows, D), (landing, D), shape)]
    copies = 32
    vmem = pl.BlockSpec(memory_space=pltpu.VMEM)
    smem = pl.BlockSpec(memory_space=pltpu.SMEM)
    anywhere = pl.BlockSpec(memory_space=pl.ANY)
    parts = pl.pallas_call(
        functools.partial(layer_kernel, tokens, pages),
        out_shape=[
            jax.ShapeDtypeStruct((NQ, D), bf16),
            jax.ShapeDtypeStruct((NQ, D), bf16),
            jax.ShapeDtypeStruct((1, tokens, D), bf16),
            *(jax.ShapeDtypeStruct(shape, bf16) for shape in whole_shapes),
        ],
        in_specs=[
            vmem,
            anywhere,
            smem,
            vmem,
            smem,
            vmem,
            vmem,
            vmem,
            anywhere,
            vmem,
            anywhere,
            vmem,
            vmem,
            vmem,
            vmem,
            vmem,
            vmem,
        ],
        out_specs=[vmem, vmem, anywhere, anywhere, anywhere, anywhere, anywhere],
        scratch_shapes=[
            pltpu.VMEM((tokens, D), bf16),
            pltpu.VMEM((tokens, D), bf16),
            pltpu.VMEM((tokens, HQ), bf16),
            pltpu.VMEM((tokens, HQ), bf16),
            pltpu.VMEM((1, tokens), f32),
            pltpu.VMEM((D, HQ), bf16),
            pltpu.VMEM((D, HQ), bf16),
            pltpu.VMEM((2 * HQ, D), bf16),
            pltpu.VMEM((2, 2 * SIDE, D), bf16),
            pltpu.VMEM((chunks, HQ), f32),
            pltpu.VMEM((chunks, HQ), f32),
            pltpu.VMEM((8, HQ), f32),
            pltpu.VMEM((D, HQ), f32),
            pltpu.VMEM((3, NP, D), f32),
            pltpu.VMEM((D, NP), bf16),
            pltpu.VMEM((D, NP), bf16),
            pltpu.VMEM((2 * HEADS, NP), f32),
            pltpu.VMEM((2 * HEADS, NP), f32),
            pltpu.VMEM((D, NP), bf16),
            pltpu.VMEM((D, NP), bf16),
            pltpu.VMEM((32, D), f32),
            *sum_buffers,
            pltpu.SemaphoreType.DMA((8,)),
            pltpu.SemaphoreType.DMA((chunks,)),
            pltpu.SemaphoreType.DMA((6,)),
            *[pltpu.SemaphoreType.DMA((copies,))] * 8,
        ],
        compiler_params=pltpu.CompilerParams(
            collective_id=0, has_side_effects=True, vmem_limit_bytes=63 * 1024 * 1024
        ),
        cost_estimate=pl.CostEstimate(
            flops=2 * 8 * tokens * HQ * D, bytes_accessed=20 << 20, transcendentals=tokens * HQ
        ),
        name="decoder_layer",
    )(
        queries,
        memory,
        quarter_turns,
        token_order,
        lengths,
        attn_in,
        attn_out,
        attn_bias.transpose(1, 0, 2),
        ffn_in,
        ffn_in_bias,
        ffn_out,
        ffn_out_bias,
        norm_gain,
        norm_bias,
        query_pos,
        out_grad,
        jnp.asarray(position_table()),
    )
    outs = pl.pallas_call(
        finish_kernel,
        out_shape=[
            jax.ShapeDtypeStruct((1, NQ, D), bf16),
            jax.ShapeDtypeStruct((1, NQ, D), bf16),
            jax.ShapeDtypeStruct((1, tokens, D), bf16),
            jax.ShapeDtypeStruct((2, 3, D, D), f32),
            jax.ShapeDtypeStruct((2, D, D), f32),
            jax.ShapeDtypeStruct((3, 2, D), f32),
            jax.ShapeDtypeStruct((D, FF), f32),
            jax.ShapeDtypeStruct((1, FF), f32),
            jax.ShapeDtypeStruct((FF, D), f32),
            jax.ShapeDtypeStruct((1, D), f32),
            jax.ShapeDtypeStruct((3, D), f32),
            jax.ShapeDtypeStruct((3, D), f32),
            jax.ShapeDtypeStruct((NQ, D), f32),
        ],
        in_specs=[vmem, vmem, anywhere, vmem, vmem, vmem, vmem],
        out_specs=[vmem, vmem, anywhere] + [vmem] * 10,
        scratch_shapes=[
            pltpu.VMEM((tokens, D), bf16),
            pltpu.SemaphoreType.DMA((8,)),
            pltpu.SemaphoreType.DMA((8,)),
        ],
        compiler_params=pltpu.CompilerParams(vmem_limit_bytes=62 * 1024 * 1024),
        name="write_outputs",
    )(*parts)
    return (
        *outs[:5],
        outs[5].transpose(1, 0, 2),
        outs[6],
        outs[7].reshape(FF),
        outs[8],
        outs[9].reshape(D),
        *outs[10:],
    )


def solution(mesh):
    in_specs = (
        P("dp", None, None),
        P("dp", "blk", None),
        P("dp"),
        P("dp", "blk"),
        P("dp"),
        P(),
        P(),
        P(),
        P(),
        P(),
        P(),
        P(),
        P(),
        P(),
        P(),
        P("dp", None, None),
    )
    out_specs = (
        P("dp", None, None),
        P("dp", None, None),
        P("dp", "blk", None),
        P(),
        P(),
        P(),
        P(),
        P(),
        P(),
        P(),
        P(),
        P(),
        P(),
    )
    layer = functools.partial(body, mesh.shape["dp"])
    return jax.shard_map(layer, mesh=mesh, in_specs=in_specs, out_specs=out_specs, check_vma=False)
```

```python
import functools
import math

import jax
import jax.numpy as jnp
import numpy as np
from jax import lax
from jax.experimental import pallas as pl
from jax.experimental.pallas import tpu as pltpu
from jax.sharding import PartitionSpec as P

D = 256
HEADS = 8
HD = D // HEADS
SIDE = 128
NQ = 125
NP = 128
HQ = HEADS * NP
PAIR = 2 * NP
FF = 2048
CHUNK = 512

masked_score = -1e30
norm_eps = 1e-05
scale = 1.0 / math.sqrt(HD)
log2e = math.log2(math.e)

bf16 = jnp.bfloat16
f32 = jnp.float32

ROWS_F = FF // 2
ROW_POS = 2 * D
ROW_SMALL = 2 * D + NP
ROWS_T = 3 * D
ROWS_K = 3 * D
TILE = 16


def axes_of(pages):
    axes = {"core": (2, 1), "y": (2, 2)}
    stride = 4
    while stride < pages:
        radix = 4 if pages // stride % 4 == 0 else 2
        axes["z%d" % (len(axes) - 2)] = (radix, stride)
        stride *= radix
    axes["x"] = (2, 0)
    return axes


def far_axes(pages):
    return [(name,) for name in axes_of(pages) if name.startswith("z")]


def sum_groups(pages):
    far = far_axes(pages)
    return [("core",), ("y",), *far], [("core", "y"), *far], [("core",), ("x",), ("y",), *far]


def padded(rows, pages):
    unit = TILE * pages
    return (rows + unit - 1) // unit * unit


def position_table():
    half = D // 2
    channel = np.arange(half)
    inverse = np.exp((channel // 2).astype(np.float32) * np.float32(-2.0 * math.log(10000.0) / half))
    angle = (np.arange(SIDE, dtype=np.float32) + 1.0) * np.float32(2.0 * math.pi / SIDE)
    angle = angle[:, None] * inverse
    return np.where(channel % 2 == 0, np.sin(angle), np.cos(angle)).astype(np.float32)


def dot(a, b):
    return jnp.dot(a, b, preferred_element_type=f32)


def dot_nt(a, b):
    return lax.dot_general(a, b, (((1,), (1,)), ((), ())), preferred_element_type=f32)


def dot_tn(a, b):
    return lax.dot_general(a, b, (((0,), (0,)), ((), ())), preferred_element_type=f32)


def row_total(values):
    return jnp.sum(values.astype(f32), axis=0, keepdims=True)


def norm_forward(values):
    average = jnp.mean(values, axis=-1, keepdims=True)
    centred = values - average
    variance = jnp.mean(centred * centred, axis=-1, keepdims=True)
    rstd = lax.rsqrt(variance + norm_eps)
    return centred * rstd, rstd


def norm_backward(grad, normed, rstd, gain):
    grad_normed = grad * gain
    first = jnp.mean(grad_normed, axis=-1, keepdims=True)
    second = jnp.mean(grad_normed * normed, axis=-1, keepdims=True)
    grad_in = rstd * (grad_normed - first - normed * second)
    return grad_in, row_total(grad * normed), row_total(grad)


def spread_rows(rows):
    head = lax.broadcasted_iota(jnp.int32, (NP, D), 1) // HD
    return jnp.concatenate(
        [jnp.where(head == h, rows, 0.0) for h in range(HEADS)], axis=0
    ).astype(bf16)


def spread_cols(cols):
    head = lax.broadcasted_iota(jnp.int32, (D, NP), 0) // HD
    return jnp.concatenate(
        [jnp.where(head == h, cols, 0.0) for h in range(HEADS)], axis=1
    ).astype(bf16)


def own_heads(full):
    return jnp.concatenate(
        [full[HD * h : HD * h + HD, NP * h : NP * h + NP] for h in range(HEADS)], axis=0
    )


def project_heads(weight_t, sums):
    high = sums.astype(bf16)
    low = (sums - high.astype(f32)).astype(bf16)
    return own_heads(dot(weight_t, high) + dot(weight_t, low))


def own_blocks(pairs):
    parts = []
    for pair in pairs:
        parts += [pair[:HD, :NP], pair[HD:, NP:]]
    return jnp.concatenate(parts, axis=0)


def head_rows(row):
    return jnp.concatenate([row[:, NP * h : NP * h + NP] for h in range(HEADS)], axis=0)


def head_line(rows):
    return jnp.concatenate([rows[h : h + 1] for h in range(HEADS)], axis=1)


def per_channel(rows):
    return jnp.concatenate(
        [jnp.broadcast_to(rows[h : h + 1], (HD, NP)) for h in range(HEADS)], axis=0
    )


def head_sums(cols):
    return jnp.concatenate(
        [jnp.sum(cols[HD * h : HD * h + HD], axis=0, keepdims=True) for h in range(HEADS)], axis=0
    )


def pair_cols(p):
    return slice(PAIR * p, PAIR * p + PAIR)


def pair_rows(p):
    return slice(2 * HD * p, 2 * HD * p + 2 * HD)


class Place:
    def __init__(self, pages):
        self.axes = axes_of(pages)
        self.page = lax.axis_index("dp")
        self.member = lax.axis_index("blk")
        self.digit = {
            name: self.member if name == "x" else lax.rem(self.page // stride, radix)
            for name, (radix, stride) in self.axes.items()
        }

    def size(self, group):
        return math.prod(self.axes[name][0] for name in group)

    def index(self, group):
        index = 0
        for name in group:
            index = index * self.axes[name][0] + self.digit[name]
        return index

    def peer(self, group, hop):
        index = lax.rem(self.index(group) + hop, self.size(group))
        page, member, rest = self.page, self.member, index
        for name in reversed(group):
            radix, stride = self.axes[name]
            digit = lax.rem(rest, radix)
            rest = rest // radix
            if name == "x":
                member = digit
            else:
                page = page + (digit - self.digit[name]) * stride
        return (page, member), index


class PageSum:
    def __init__(self, place, groups, back, rows, landing, whole, sent, arrived):
        self.place, self.groups, self.back = place, groups, back
        self.rows, self.landing, self.whole = rows, landing, whole
        self.sent, self.arrived = sent, arrived
        self.slots = 0
        self.extents = [rows.shape[0]]
        self.bases = [0]
        self.landings = []
        at = 0
        for group in groups:
            size = place.size(group)
            extent = self.extents[-1] // size
            self.landings.append(at)
            at += (size - 1) * extent
            self.bases.append(pl.multiple_of(self.bases[-1] + place.index(group) * extent, TILE))
            self.extents.append(extent)
        last = len(groups)
        moves = [self.scatter_moves(s) for s in range(last)]
        near = {"all": 0, "across": 1, "sides": 2}[back]
        moves += [self.gather_moves(s) for s in range(last - 1, near - 1, -1)]
        if back == "sides":
            moves += [self.side_moves(), self.corner_moves(), self.core_moves()]
        elif back == "across":
            moves += [self.across_moves(), self.core_moves()]
        self.phases = [functools.partial(self.step, moves, k) for k in range(len(moves) + 1)]

    @staticmethod
    def landing_rows(pages, groups, rows):
        axes = axes_of(pages)
        total, extent = 0, rows
        for group in groups:
            size = math.prod(axes[name][0] for name in group)
            extent //= size
            total += (size - 1) * extent
        return total

    def step(self, moves, k):
        last = len(self.groups)
        if k > 0:
            for move in moves[k - 1]:
                self.copy(*move).wait()
        if 0 < k <= last:
            total = self.scatter_sum(k - 1)
            region = pl.ds(self.bases[k], self.extents[k])
            if k < last:
                self.rows[region] = total
            elif len(self.whole.shape) == 3:
                self.whole[self.place.member, region] = total
            else:
                self.whole[region] = total
        if k < len(moves):
            for move in moves[k]:
                self.copy(*move).start()

    def copy(self, slot, source, target, device):
        return pltpu.make_async_remote_copy(
            src_ref=source(),
            dst_ref=target(),
            send_sem=self.sent.at[slot],
            recv_sem=self.arrived.at[slot],
            device_id=device,
            device_id_type=pl.DeviceIdType.MESH,
        )

    def new_slot(self):
        self.slots += 1
        return self.slots - 1

    def same(self, device, view):
        return (self.new_slot(), view, view, device)

    def scatter_moves(self, step):
        group = self.groups[step]
        extent = self.extents[step + 1]
        moves = []
        for hop in range(1, self.place.size(group)):
            device, other = self.place.peer(group, hop)
            start = pl.multiple_of(self.bases[step] + other * extent, TILE)
            landing = self.landings[step] + (hop - 1) * extent
            moves.append(
                (
                    self.new_slot(),
                    functools.partial(self.part, self.rows, start, extent),
                    functools.partial(self.part, self.landing, landing, extent),
                    device,
                )
            )
        return moves

    @staticmethod
    def part(ref, start, extent):
        return ref.at[pl.ds(start, extent)]

    def half(self, member, start, extent):
        if len(self.whole.shape) == 3:
            return self.whole.at[member, pl.ds(start, extent)]
        return self.whole.at[pl.ds(start, extent)]

    def scatter_sum(self, step):
        extent = self.extents[step + 1]
        total = self.rows[pl.ds(self.bases[step + 1], extent)].astype(f32)
        for hop in range(1, self.place.size(self.groups[step])):
            landing = self.landings[step] + (hop - 1) * extent
            total = total + self.landing[pl.ds(landing, extent)].astype(f32)
        return total.astype(bf16)

    def gather_moves(self, step):
        group = self.groups[step]
        view = functools.partial(self.half, self.place.member, self.bases[step + 1], self.extents[step + 1])
        return [
            self.same(self.place.peer(group, hop)[0], view) for hop in range(1, self.place.size(group))
        ]

    def own_quarter(self):
        step = 2 if len(self.groups[0]) == 1 else 1
        return self.bases[step], self.extents[step]

    def side_moves(self):
        view = functools.partial(self.half, self.place.member, *self.own_quarter())
        return [self.same(self.place.peer((name,), 1)[0], view) for name in ("y", "x")]

    def corner_moves(self):
        base, extent = self.own_quarter()
        other = pl.multiple_of(base + (1 - 2 * self.place.digit["y"]) * extent, TILE)
        view = functools.partial(self.half, self.place.member, other, extent)
        return [self.same(self.place.peer(("x",), 1)[0], view)]

    def across_moves(self):
        view = functools.partial(self.half, self.place.member, *self.own_quarter())
        return [self.same(self.place.peer(("x", "y"), hop)[0], view) for hop in range(1, 4)]

    def core_moves(self):
        extent = self.extents[0] // 2
        start = pl.multiple_of(self.place.digit["core"] * extent, TILE)
        device, _ = self.place.peer(("core",), 1)
        return [self.same(device, functools.partial(self.half, m, start, extent)) for m in range(2)]


def clear_rest(ref, used):
    if ref.shape[0] > used:
        ref[used:] = jnp.zeros((ref.shape[0] - used, D), ref.dtype)


def layer_kernel(
    tokens,
    pages,
    queries_in,
    memory_hbm,
    turns_in,
    order_in,
    lengths_in,
    attn_in,
    attn_out,
    attn_bias,
    ffn_in_hbm,
    ffn_in_bias,
    ffn_out_hbm,
    ffn_out_bias,
    norm_gain,
    norm_bias,
    pos_in,
    out_grad_in,
    table_in,
    result_out,
    queries_grad_out,
    memory_grad_hbm,
    whole_f_hbm,
    whole_g_hbm,
    whole_t_hbm,
    whole_k_hbm,
    memory_s,
    key_in_s,
    probs_s,
    grad_scores_s,
    code_s,
    query_kt,
    grad_vt,
    back_s,
    table_s,
    shifts_s,
    factor_s,
    total_s,
    mixed_s,
    pad_s,
    send_a,
    recv_a,
    send_t,
    recv_t,
    send_b,
    recv_b,
    small_s,
    rows_f,
    landing_f,
    whole_f,
    rows_g,
    landing_g,
    whole_g,
    rows_t,
    landing_t,
    whole_t,
    rows_k,
    landing_k,
    whole_k,
    load_sem,
    store_sem,
    link_sem,
    sent_f,
    arrived_f,
    sent_g,
    arrived_g,
    sent_t,
    arrived_t,
    sent_k,
    arrived_k,
):
    member = lax.axis_index("blk")
    partner = (lax.axis_index("dp"), 1 - member)
    chunks = tokens // CHUNK

    place = Place(pages)
    groups_f, groups_t, groups_k = sum_groups(pages)
    sum_f = PageSum(place, groups_f, "sides", rows_f, landing_f, whole_f, sent_f, arrived_f)
    sum_g = PageSum(place, groups_f, "sides", rows_g, landing_g, whole_g, sent_g, arrived_g)
    sum_t = PageSum(place, groups_t, "across", rows_t, landing_t, whole_t, sent_t, arrived_t)
    sum_k = PageSum(place, groups_k, "all", rows_k, landing_k, whole_k, sent_k, arrived_k)

    barrier = pltpu.get_barrier_semaphore()
    peers = [
        place.peer(group, hop)[0]
        for group in [("x", "core", "y"), *far_axes(pages)]
        for hop in range(1, place.size(group))
    ]
    for peer in peers:
        pl.semaphore_signal(barrier, inc=1, device_id=peer, device_id_type=pl.DeviceIdType.MESH)

    load_memory = pltpu.make_async_copy(memory_hbm.at[0], memory_s, load_sem.at[0])
    half = FF // 2
    ffn_in_s = [grad_scores_s.at[D * k : D * k + D] for k in range(2)]
    ffn_out_s = grad_scores_s.at[2 * D : 2 * D + FF, :D]
    free = 2 * D + FF
    active_s = [grad_scores_s.at[free + NP * k : free + NP * k + NP] for k in range(2)]
    slope_s = [grad_scores_s.at[free + NP * k : free + NP * k + NP] for k in range(2, 4)]
    load_ffn = [
        pltpu.make_async_copy(ffn_in_hbm.at[:, half * k : half * k + half], ffn_in_s[k], load_sem.at[1 + k])
        for k in range(2)
    ]
    load_ffn.append(pltpu.make_async_copy(ffn_out_hbm, ffn_out_s, load_sem.at[3]))
    load_memory.start()
    for load in load_ffn:
        load.start()

    pairs = [attn_bias[j].astype(f32) for j in range(3)]
    bias = jnp.concatenate([pair[k : k + 1] for k in range(2) for pair in pairs], axis=0)
    gain = norm_gain[...].astype(f32)
    shift = norm_bias[...].astype(f32)

    order = order_in[...]
    turn = turns_in[0]
    row_at = order >> 7
    col_at = order & 127
    top = SIDE - 1
    row_new = jnp.where(
        turn == 0, row_at, jnp.where(turn == 1, col_at, jnp.where(turn == 2, top - row_at, top - col_at))
    )
    col_new = jnp.where(
        turn == 0, col_at, jnp.where(turn == 1, top - row_at, jnp.where(turn == 2, top - col_at, row_at))
    )
    past = jnp.where(order < lengths_in[0], 0, SIDE * SIDE)
    code_s[...] = (row_new * SIDE + col_new + past).astype(f32)

    pad_s[...] = jnp.zeros_like(pad_s)
    pad_s[0, :NQ] = queries_in[0].astype(f32)
    pad_s[1, :NQ] = pos_in[...].astype(f32)
    pad_s[2, :NQ] = out_grad_in[0].astype(f32)
    queries_f = pad_s[0]
    pos_f = pad_s[1]
    queries_b = queries_f.astype(bf16)
    mixed_q = (queries_f + pos_f).astype(bf16)
    query_self = (dot(mixed_q, attn_in[0, 0]) + bias[0:1]).astype(bf16)
    key_self = dot(mixed_q, attn_in[0, 1]).astype(bf16)
    value_self = (dot(queries_b, attn_in[0, 2]) + bias[1:2]).astype(bf16)
    scores = dot(key_self, spread_cols(query_self.astype(f32).T)) * scale
    own_key = lax.broadcasted_iota(jnp.int32, (NP, HQ), 0) < NQ
    scores = jnp.where(own_key, scores, masked_score)
    raised = jnp.exp(scores - jnp.max(scores, axis=0, keepdims=True))
    probs_self = raised / jnp.sum(raised, axis=0, keepdims=True)
    probs_self_b = probs_self.astype(bf16)
    value_t = value_self.astype(f32).T.astype(bf16)
    attended = own_blocks(
        [dot(value_t[pair_rows(p)], probs_self_b[:, pair_cols(p)]) for p in range(4)]
    ).T.astype(bf16)
    first_normed, first_rstd = norm_forward(queries_f + dot(attended, attn_out[0]) + bias[2:3])
    first = first_normed * gain[0:1] + shift[0:1]
    cross_q = (first + pos_f).astype(bf16)
    query_c = (dot(cross_q, attn_in[1, 0]) + bias[3:4]).astype(bf16)
    query_x = spread_rows(query_c.astype(f32))
    query_k = dot(attn_in[1, 1], spread_cols(query_c.astype(f32).T))
    query_kt[...] = (query_k * (scale * log2e)).astype(bf16)
    back_s[:HQ] = (dot_nt(query_x, attn_in[1, 1]) * scale).astype(bf16)
    table = table_in[...]
    nothing = jnp.zeros((SIDE, D // 2), f32)
    table = jnp.concatenate(
        [jnp.concatenate([table, nothing], axis=1), jnp.concatenate([nothing, table], axis=1)], axis=0
    )
    table_high = table.astype(bf16)
    table_s[0] = table_high
    table_s[1] = (table - table_high.astype(f32)).astype(bf16)

    load_memory.wait()
    lane = lax.broadcasted_iota(jnp.int32, (CHUNK, NP), 1)

    def place_chunk(i):
        rows = pl.ds(pl.multiple_of(i * CHUNK, CHUNK), CHUNK)
        line = code_s[:, rows]
        code = jnp.concatenate(
            [
                jnp.broadcast_to(line[:, NP * j : NP * j + NP], (NP, NP)).T
                for j in range(CHUNK // NP)
            ],
            axis=0,
        ).astype(jnp.int32)
        row_hot = jnp.where(((code >> 7) & 127) == lane, 1.0, 0.0)
        col_hot = jnp.where((code & 127) == lane, 1.0, 0.0)
        hot = jnp.concatenate([row_hot, col_hot], axis=1).astype(bf16)
        block = memory_s[rows].astype(f32)
        key_in_s[rows] = (block + dot(hot, table_s[0]) + dot(hot, table_s[1])).astype(bf16)

    @pl.loop(0, chunks // 4)
    def _(j):
        for k in range(4):
            place_chunk(j * 4 + k)

    def score_chunk(i, out, top):
        rows = pl.ds(pl.multiple_of(i * CHUNK, CHUNK), CHUNK)
        line = code_s[:, rows]
        code = jnp.concatenate(
            [
                jnp.broadcast_to(line[:, NP * j : NP * j + NP], (NP, NP)).T
                for j in range(CHUNK // NP)
            ],
            axis=0,
        )
        allowed = code < SIDE * SIDE
        allowed = jnp.concatenate([allowed, allowed], axis=1)
        key_in = key_in_s[rows]
        for p in range(4):
            cols = pair_cols(p)
            part = jnp.where(allowed, dot(key_in, query_kt[:, cols]), masked_score)
            out[:, cols] = part
            top[0:1, cols] = jnp.max(part, axis=0, keepdims=True)

    def attend_chunk(i, scored, top):
        rows = pl.ds(pl.multiple_of(i * CHUNK, CHUNK), CHUNK)
        memory_ct = memory_s[rows].T
        for p in range(4):
            cols = pair_cols(p)
            before = total_s[0:1, cols]
            highest = jnp.maximum(before, top[0:1, cols])
            raised = jnp.exp2(scored[:, cols] - highest)
            fade = jnp.exp2(before - highest)
            total_s[0:1, cols] = highest
            total_s[1:2, cols] = total_s[1:2, cols] * fade + jnp.sum(raised, axis=0, keepdims=True)
            shifts_s[pl.ds(i, 1), cols] = highest
            probs_s[rows, cols] = raised.astype(bf16)
            mixed_s[:, cols] = mixed_s[:, cols] * fade + dot(memory_ct, probs_s[rows, cols])

    total_s[0:1] = jnp.full((1, HQ), -3e38, f32)
    total_s[1:2] = jnp.zeros((1, HQ), f32)
    mixed_s[...] = jnp.zeros_like(mixed_s)
    def attend_all(score_a, score_b, top_a, top_b):
        score_chunk(0, score_a, top_a)

        @pl.loop(0, chunks // 2)
        def _(j):
            i = j * 2
            score_chunk(i + 1, score_b, top_b)
            attend_chunk(i, score_a, top_a)
            score_chunk(jnp.minimum(i + 2, chunks - 1), score_a, top_a)
            attend_chunk(i + 1, score_b, top_b)

    score_buffer = pltpu.VMEM((CHUNK, HQ), f32)
    top_buffer = pltpu.VMEM((8, HQ), f32)
    pl.run_scoped(attend_all, score_buffer, score_buffer, top_buffer, top_buffer)

    value_wt = attn_in[1, 2].astype(f32).T.astype(bf16)
    key_wt = attn_in[1, 1].astype(f32).T.astype(bf16)
    send_a[...] = project_heads(value_wt, mixed_s[...]).astype(bf16)
    send_t[:HEADS] = head_rows(total_s[0:1])
    send_t[HEADS:] = head_rows(total_s[1:2])
    pl.semaphore_wait(barrier, len(peers))
    swap_a = pltpu.make_async_remote_copy(
        src_ref=send_a,
        dst_ref=recv_a,
        send_sem=link_sem.at[0],
        recv_sem=link_sem.at[1],
        device_id=partner,
        device_id_type=pl.DeviceIdType.MESH,
    )
    swap_t = pltpu.make_async_remote_copy(
        src_ref=send_t,
        dst_ref=recv_t,
        send_sem=link_sem.at[4],
        recv_sem=link_sem.at[5],
        device_id=partner,
        device_id_type=pl.DeviceIdType.MESH,
    )
    swap_a.start()
    swap_t.start()
    swap_a.wait()
    swap_t.wait()
    is_first = member == 0
    own, other = send_a[...].astype(f32), recv_a[...].astype(f32)
    left = jnp.where(is_first, own, other)
    right = jnp.where(is_first, other, own)
    own, other = send_t[...], recv_t[...]
    left_t = jnp.where(is_first, own, other)
    right_t = jnp.where(is_first, other, own)
    highest = jnp.maximum(left_t[:HEADS], right_t[:HEADS])
    fade_l = jnp.exp2(left_t[:HEADS] - highest)
    fade_r = jnp.exp2(right_t[:HEADS] - highest)
    total = left_t[HEADS:] * fade_l + right_t[HEADS:] * fade_r
    mixed_t = left * per_channel(fade_l / total) + right * per_channel(fade_r / total)
    log_total = head_line(highest + jnp.log2(total))
    factor_s[...] = jnp.exp2(shifts_s[...] - log_total)
    attended_c = (mixed_t.T + bias[4:5]).astype(bf16)

    second_normed, second_rstd = norm_forward(first + dot(attended_c, attn_out[1]) + bias[5:6])
    second = second_normed * gain[1:2] + shift[1:2]
    ffn_input = second.astype(bf16)
    load_ffn[0].wait()
    load_ffn[1].wait()
    blocks = [(j // 4, slice(D * j, D * j + D), slice(j % 4 * D, j % 4 * D + D)) for j in range(FF // D)]
    hidden_bias = ffn_in_bias[...].astype(f32).reshape(1, FF)
    def feed_forward(gate_s):
        for k, cols, part in blocks:
            hidden = dot(ffn_input, ffn_in_s[k][:, part]) + hidden_bias[:, cols]
            half_gate = 0.5 + 0.5 * lax.erf(hidden * math.sqrt(0.5))
            active_s[k][:, part] = (hidden * half_gate).astype(bf16)
            gate_s[:, cols] = half_gate + hidden * jnp.exp(hidden * hidden * -0.5) * (
                1.0 / math.sqrt(2.0 * math.pi)
            )
        load_ffn[2].wait()
        third_normed, third_rstd = norm_forward(
            second
            + dot(active_s[0][...], ffn_out_s[:half])
            + dot(active_s[1][...], ffn_out_s[half:])
            + ffn_out_bias[...].astype(f32).reshape(1, D)
        )
        result_out[...] = (third_normed * gain[2:3] + shift[2:3])[:NQ].astype(bf16)
        grad_third, gain_grad_2, shift_grad_2 = norm_backward(
            pad_s[2], third_normed, third_rstd, gain[2:3]
        )
        grad_branch_f = grad_third.astype(bf16)
        for k, cols, part in blocks:
            grad_hidden = dot_nt(grad_branch_f, ffn_out_s[cols]) * gate_s[:, cols]
            slope_s[k][:, part] = grad_hidden.astype(bf16)
        return grad_third, gain_grad_2, shift_grad_2, grad_branch_f

    grad_third, gain_grad_2, shift_grad_2, grad_branch_f = pl.run_scoped(
        feed_forward, pltpu.VMEM((NP, FF), f32)
    )
    grad_second = grad_third + dot_nt(slope_s[0][...], ffn_in_s[0][...])
    grad_second += dot_nt(slope_s[1][...], ffn_in_s[1][...])
    grad_second_in, gain_grad_1, shift_grad_1 = norm_backward(
        grad_second, second_normed, second_rstd, gain[1:2]
    )
    grad_branch_c = grad_second_in.astype(bf16)
    ffn_input_t = second.T.astype(bf16)

    def ffn_rows(target, k):
        @pl.when(member == 0)
        def _():
            for j in range(4):
                part = slice(D * j, D * j + D)
                target[part] = dot(ffn_input_t, slope_s[k][:, part]).astype(bf16)

        @pl.when(member == 1)
        def _():
            for j in range(4):
                part = slice(D * j, D * j + D)
                target[part] = dot_tn(active_s[k][:, part], grad_branch_f).astype(bf16)

    ffn_rows(rows_f, 0)
    sum_f.phases[0]()
    ffn_rows(rows_g, 1)

    is_first = member == 0
    out_grad_c = dot_tn(attended_c, grad_branch_c)
    rows_k[2 * D : 3 * D] = jnp.where(is_first, out_grad_c, 0.0).astype(bf16)

    clear_rest(rows_f, ROWS_F)
    clear_rest(rows_g, ROWS_F)
    clear_rest(rows_t, ROWS_T)
    clear_rest(rows_k, ROWS_K)
    sum_g.phases[0]()
    grad_attended_c = dot_nt(grad_branch_c, attn_out[1]).astype(bf16).astype(f32)
    small_s[:16] = jnp.concatenate(
        [row_total(slope_s[k][:, part]) for k, _, part in blocks]
        + [
            row_total(grad_branch_f),
            row_total(grad_branch_c),
            gain_grad_2,
            shift_grad_2,
            gain_grad_1,
            shift_grad_1,
            row_total(grad_attended_c),
            jnp.zeros((1, D), f32),
        ],
        axis=0,
    )

    grad_attended_t = grad_attended_c.T
    grad_x = spread_rows(grad_attended_c)
    grad_vt[...] = dot(attn_in[1, 2], spread_cols(grad_attended_t)).astype(bf16)
    back_s[HQ:] = dot_nt(grad_x, attn_in[1, 2]).astype(bf16)
    inner = head_line(head_sums(grad_attended_t * mixed_t))
    own_share = jnp.exp2(total_s[0:1] - log_total)
    rows_k[D : 2 * D] = dot((mixed_s[...] * own_share).astype(bf16), grad_x).astype(bf16)
    mixed_s[...] = jnp.zeros_like(mixed_s)

    queue_f = [phase for pair in zip(sum_f.phases[1:], sum_g.phases[1:]) for phase in pair]
    queue_t = list(sum_t.phases)
    queue_k = list(sum_k.phases)

    def take(queue):
        if queue:
            queue.pop(0)()

    def at(i, steps):
        for step, queue in steps:
            pl.when(i == (step * chunks) // 32)(queue.pop(0))

    @pl.loop(0, chunks // 2)
    def _(i):
        rows = pl.ds(pl.multiple_of(i * 2 * CHUNK, 2 * CHUNK), 2 * CHUNK)
        key_ct = key_in_s[rows].T
        memory_c = memory_s[rows]
        for p in range(4):
            cols = pair_cols(p)
            grad_probs = dot(memory_c, grad_vt[:, cols])
            for k in range(2):
                part = pl.ds(pl.multiple_of((i * 2 + k) * CHUNK, CHUNK), CHUNK)
                probs = probs_s[part, cols].astype(f32) * factor_s[pl.ds(i * 2 + k, 1), cols]
                slopes = probs * (grad_probs[CHUNK * k : CHUNK * k + CHUNK] - inner[:, cols])
                probs_s[part, cols] = probs.astype(bf16)
                grad_scores_s[part, cols] = slopes.astype(bf16)
            mixed_s[:, cols] += dot(key_ct, grad_scores_s[rows, cols])
        at(i, [(3, queue_f), (4, queue_f), (8, queue_f), (9, queue_f), (13, queue_f), (14, queue_f)])

    send_b[...] = (project_heads(key_wt, mixed_s[...]) * scale).astype(bf16)
    swap_b = pltpu.make_async_remote_copy(
        src_ref=send_b,
        dst_ref=recv_b,
        send_sem=link_sem.at[2],
        recv_sem=link_sem.at[3],
        device_id=partner,
        device_id_type=pl.DeviceIdType.MESH,
    )
    swap_b.start()
    query_x = spread_rows(query_c.astype(f32))
    rows_k[:D] = (dot(mixed_s[...].astype(bf16), query_x) * scale).astype(bf16)
    take(queue_k)
    take(queue_f)
    take(queue_f)
    swap_b.wait()
    take(queue_k)
    grad_query_c = (send_b[...].astype(f32) + recv_b[...].astype(f32)).T.astype(bf16)

    cross_pos_grad = dot_nt(grad_query_c, attn_in[1, 0])
    grad_first_in, gain_grad_0, shift_grad_0 = norm_backward(
        grad_second_in + cross_pos_grad, first_normed, first_rstd, gain[0:1]
    )
    grad_branch = grad_first_in.astype(bf16)
    grad_attended = dot_nt(grad_branch, attn_out[0]).astype(bf16).astype(f32)
    take(queue_k)
    grad_probs = dot(value_self, spread_cols(grad_attended.T))
    inner_self = jnp.sum(probs_self * grad_probs, axis=0, keepdims=True)
    grad_scores = (probs_self * (grad_probs - inner_self)).astype(bf16)
    key_t = key_self.astype(f32).T.astype(bf16)
    grad_query_s = (
        own_blocks([dot(key_t[pair_rows(p)], grad_scores[:, pair_cols(p)]) for p in range(4)]) * scale
    ).T.astype(bf16)
    grad_key_s = (dot(grad_scores, spread_rows(query_self.astype(f32))) * scale).astype(bf16)
    grad_value_s = dot(probs_self_b, spread_rows(grad_attended)).astype(bf16)
    grad_mixed_q = dot_nt(grad_query_s, attn_in[0, 0]) + dot_nt(grad_key_s, attn_in[0, 1])
    queries_grad_out[...] = (grad_first_in + grad_mixed_q + dot_nt(grad_value_s, attn_in[0, 2]))[
        :NQ
    ].astype(bf16)
    small_s[16:] = jnp.concatenate(
        [
            row_total(grad_query_s),
            row_total(grad_value_s),
            row_total(grad_branch),
            row_total(grad_query_c),
            gain_grad_0,
            shift_grad_0,
            jnp.zeros((10, D), f32),
        ],
        axis=0,
    )
    @pl.when(member == 0)
    def _():
        rows_t[:D] = dot_tn(mixed_q, grad_query_s).astype(bf16)
        rows_t[D : 2 * D] = dot_tn(mixed_q, grad_key_s).astype(bf16)
        rows_t[2 * D : 3 * D] = dot_tn(queries_b, grad_value_s).astype(bf16)

    @pl.when(member == 1)
    def _():
        rows_t[:D] = dot_tn(cross_q, grad_query_c).astype(bf16)
        rows_t[D : 2 * D] = dot_tn(attended, grad_branch).astype(bf16)
        rows_t[ROW_POS:ROW_SMALL] = (grad_mixed_q + cross_pos_grad).astype(bf16)
        rows_t[ROW_SMALL : ROW_SMALL + 32] = small_s[...].astype(bf16)
        rows_t[ROW_SMALL + 32 : ROWS_T] = jnp.zeros((ROWS_T - ROW_SMALL - 32, D), bf16)

    take(queue_t)
    take(queue_k)
    take(queue_f)
    take(queue_f)

    @pl.loop(0, chunks // 2)
    def _(i):
        rows = pl.ds(pl.multiple_of(i * 2 * CHUNK, 2 * CHUNK), 2 * CHUNK)
        both = jnp.concatenate([grad_scores_s[rows], probs_s[rows]], axis=1)
        memory_s[rows] = dot(both, back_s[...]).astype(bf16)
        pltpu.make_async_copy(memory_s.at[rows], memory_grad_hbm.at[0, rows], store_sem.at[i]).start()
        at(
            i,
            [
                (3, queue_k),
                (5, queue_t),
                (6, queue_f),
                (7, queue_f),
                (8, queue_k),
                (9, queue_t),
                (11, queue_k),
                (13, queue_t),
                (14, queue_k),
            ],
        )

    while queue_f:
        take(queue_f)
    stores = [
        pltpu.make_async_copy(whole, target, load_sem.at[4 + k])
        for k, (whole, target) in enumerate(
            (
                (whole_f, whole_f_hbm),
                (whole_g, whole_g_hbm),
                (whole_t, whole_t_hbm),
                (whole_k, whole_k_hbm),
            )
        )
    ]
    stores[0].start()
    stores[1].start()
    while queue_t or queue_k:
        take(queue_t)
        take(queue_k)
    stores[2].start()
    stores[3].start()

    @pl.loop(0, chunks // 2)
    def _(i):
        rows = pl.ds(pl.multiple_of(i * 2 * CHUNK, 2 * CHUNK), 2 * CHUNK)
        pltpu.make_async_copy(memory_s.at[rows], memory_grad_hbm.at[0, rows], store_sem.at[i]).wait()

    for store in stores:
        store.wait()


def finish_kernel(
    result_in,
    queries_grad_in,
    memory_grad_in,
    whole_f,
    whole_g,
    whole_t,
    whole_k,
    result,
    queries_grad,
    memory_grad,
    attn_in_grad,
    attn_out_grad,
    attn_bias_grad,
    ffn_in_grad,
    ffn_in_bias_grad,
    ffn_out_grad,
    ffn_out_bias_grad,
    norm_gain_grad,
    norm_bias_grad,
    query_pos_grad,
    moved,
    in_sem,
    out_sem,
):
    pieces = in_sem.shape[0]
    piece = moved.shape[0] // pieces

    def fetch(j):
        rows = pl.ds(piece * j, piece)
        return pltpu.make_async_copy(memory_grad_in.at[0, rows], moved.at[rows], in_sem.at[j])

    def write(j):
        rows = pl.ds(piece * j, piece)
        return pltpu.make_async_copy(moved.at[rows], memory_grad.at[0, rows], out_sem.at[j])

    for j in range(pieces):
        fetch(j).start()
    result[0] = result_in[...]
    queries_grad[0] = queries_grad_in[...]
    for j in range(FF // D):
        piece_at = j % (FF // D // 2) * D
        sums = whole_f if j < FF // D // 2 else whole_g
        ffn_in_grad[:, D * j : D * j + D] = sums[0, piece_at : piece_at + D].astype(f32)
        ffn_out_grad[D * j : D * j + D] = sums[1, piece_at : piece_at + D].astype(f32)
    for j in range(pieces):
        fetch(j).wait()
        write(j).start()
    attn_out_grad[0] = whole_t[1, D : 2 * D].astype(f32)
    attn_out_grad[1] = whole_k[2 * D : 3 * D].astype(f32)
    for j in range(3):
        attn_in_grad[0, j] = whole_t[0, D * j : D * j + D].astype(f32)
    attn_in_grad[1, 0] = whole_t[1, :D].astype(f32)
    attn_in_grad[1, 1] = whole_k[:D].astype(f32)
    attn_in_grad[1, 2] = whole_k[D : 2 * D].astype(f32)
    query_pos_grad[...] = whole_t[1, ROW_POS:ROW_SMALL].astype(f32)[:NQ]
    small = whole_t[1, ROW_SMALL : ROW_SMALL + 32].astype(f32)
    ffn_in_bias_grad[...] = jnp.concatenate([small[j : j + 1] for j in range(FF // D)], axis=1)
    ffn_out_bias_grad[...] = small[8:9]
    for j, (own, cross) in enumerate(((16, 19), (17, 14), (18, 9))):
        attn_bias_grad[j, 0:1] = small[own : own + 1]
        attn_bias_grad[j, 1:2] = small[cross : cross + 1]
    norm_gain_grad[0:1] = small[20:21]
    norm_gain_grad[1:2] = small[12:13]
    norm_gain_grad[2:3] = small[10:11]
    norm_bias_grad[0:1] = small[21:22]
    norm_bias_grad[1:2] = small[13:14]
    norm_bias_grad[2:3] = small[11:12]
    for j in range(pieces):
        write(j).wait()


def body(
    pages,
    queries,
    memory,
    quarter_turns,
    token_order,
    lengths,
    attn_in,
    attn_out,
    attn_bias,
    ffn_in,
    ffn_in_bias,
    ffn_out,
    ffn_out_bias,
    norm_gain,
    norm_bias,
    query_pos,
    out_grad,
):
    tokens = memory.shape[1]
    chunks = tokens // CHUNK
    groups_f, groups_t, groups_k = sum_groups(pages)
    summed = [
        (padded(ROWS_F, pages), groups_f),
        (padded(ROWS_F, pages), groups_f),
        (padded(ROWS_T, pages), groups_t),
        (padded(ROWS_K, 2 * pages), groups_k),
    ]
    whole_shapes = [(2, rows, D) for rows, _ in summed[:3]] + [(summed[3][0], D)]
    sum_buffers = []
    for (rows, groups), shape in zip(summed, whole_shapes):
        landing = PageSum.landing_rows(pages, groups, rows)
        sum_buffers += [pltpu.VMEM(each, bf16) for each in ((rows, D), (landing, D), shape)]
    copies = 32
    vmem = pl.BlockSpec(memory_space=pltpu.VMEM)
    smem = pl.BlockSpec(memory_space=pltpu.SMEM)
    anywhere = pl.BlockSpec(memory_space=pl.ANY)
    parts = pl.pallas_call(
        functools.partial(layer_kernel, tokens, pages),
        out_shape=[
            jax.ShapeDtypeStruct((NQ, D), bf16),
            jax.ShapeDtypeStruct((NQ, D), bf16),
            jax.ShapeDtypeStruct((1, tokens, D), bf16),
            *(jax.ShapeDtypeStruct(shape, bf16) for shape in whole_shapes),
        ],
        in_specs=[
            vmem,
            anywhere,
            smem,
            vmem,
            smem,
            vmem,
            vmem,
            vmem,
            anywhere,
            vmem,
            anywhere,
            vmem,
            vmem,
            vmem,
            vmem,
            vmem,
            vmem,
        ],
        out_specs=[vmem, vmem, anywhere, anywhere, anywhere, anywhere, anywhere],
        scratch_shapes=[
            pltpu.VMEM((tokens, D), bf16),
            pltpu.VMEM((tokens, D), bf16),
            pltpu.VMEM((tokens, HQ), bf16),
            pltpu.VMEM((tokens, HQ), bf16),
            pltpu.VMEM((1, tokens), f32),
            pltpu.VMEM((D, HQ), bf16),
            pltpu.VMEM((D, HQ), bf16),
            pltpu.VMEM((2 * HQ, D), bf16),
            pltpu.VMEM((2, 2 * SIDE, D), bf16),
            pltpu.VMEM((chunks, HQ), f32),
            pltpu.VMEM((chunks, HQ), f32),
            pltpu.VMEM((8, HQ), f32),
            pltpu.VMEM((D, HQ), f32),
            pltpu.VMEM((3, NP, D), f32),
            pltpu.VMEM((D, NP), bf16),
            pltpu.VMEM((D, NP), bf16),
            pltpu.VMEM((2 * HEADS, NP), f32),
            pltpu.VMEM((2 * HEADS, NP), f32),
            pltpu.VMEM((D, NP), bf16),
            pltpu.VMEM((D, NP), bf16),
            pltpu.VMEM((32, D), f32),
            *sum_buffers,
            pltpu.SemaphoreType.DMA((8,)),
            pltpu.SemaphoreType.DMA((chunks,)),
            pltpu.SemaphoreType.DMA((6,)),
            *[pltpu.SemaphoreType.DMA((copies,))] * 8,
        ],
        compiler_params=pltpu.CompilerParams(
            collective_id=0, has_side_effects=True, vmem_limit_bytes=63 * 1024 * 1024
        ),
        cost_estimate=pl.CostEstimate(
            flops=2 * 8 * tokens * HQ * D, bytes_accessed=20 << 20, transcendentals=tokens * HQ
        ),
        name="decoder_layer",
    )(
        queries,
        memory,
        quarter_turns,
        token_order,
        lengths,
        attn_in,
        attn_out,
        attn_bias.transpose(1, 0, 2),
        ffn_in,
        ffn_in_bias,
        ffn_out,
        ffn_out_bias,
        norm_gain,
        norm_bias,
        query_pos,
        out_grad,
        jnp.asarray(position_table()),
    )
    outs = pl.pallas_call(
        finish_kernel,
        out_shape=[
            jax.ShapeDtypeStruct((1, NQ, D), bf16),
            jax.ShapeDtypeStruct((1, NQ, D), bf16),
            jax.ShapeDtypeStruct((1, tokens, D), bf16),
            jax.ShapeDtypeStruct((2, 3, D, D), f32),
            jax.ShapeDtypeStruct((2, D, D), f32),
            jax.ShapeDtypeStruct((3, 2, D), f32),
            jax.ShapeDtypeStruct((D, FF), f32),
            jax.ShapeDtypeStruct((1, FF), f32),
            jax.ShapeDtypeStruct((FF, D), f32),
            jax.ShapeDtypeStruct((1, D), f32),
            jax.ShapeDtypeStruct((3, D), f32),
            jax.ShapeDtypeStruct((3, D), f32),
            jax.ShapeDtypeStruct((NQ, D), f32),
        ],
        in_specs=[vmem, vmem, anywhere, vmem, vmem, vmem, vmem],
        out_specs=[vmem, vmem, anywhere] + [vmem] * 10,
        scratch_shapes=[
            pltpu.VMEM((tokens, D), bf16),
            pltpu.SemaphoreType.DMA((8,)),
            pltpu.SemaphoreType.DMA((8,)),
        ],
        compiler_params=pltpu.CompilerParams(vmem_limit_bytes=62 * 1024 * 1024),
        name="write_outputs",
    )(*parts)
    return (
        *outs[:5],
        outs[5].transpose(1, 0, 2),
        outs[6],
        outs[7].reshape(FF),
        outs[8],
        outs[9].reshape(D),
        *outs[10:],
    )


def solution(mesh):
    in_specs = (
        P("dp", None, None),
        P("dp", "blk", None),
        P("dp"),
        P("dp", "blk"),
        P("dp"),
        P(),
        P(),
        P(),
        P(),
        P(),
        P(),
        P(),
        P(),
        P(),
        P(),
        P("dp", None, None),
    )
    out_specs = (
        P("dp", None, None),
        P("dp", None, None),
        P("dp", "blk", None),
        P(),
        P(),
        P(),
        P(),
        P(),
        P(),
        P(),
        P(),
        P(),
        P(),
    )
    layer = functools.partial(body, mesh.shape["dp"])
    return jax.shard_map(layer, mesh=mesh, in_specs=in_specs, out_specs=out_specs, check_vma=False)
```

```python
import functools
import math

import jax
import jax.numpy as jnp
import numpy as np
from jax import lax
from jax.experimental import pallas as pl
from jax.experimental.pallas import tpu as pltpu
from jax.sharding import PartitionSpec as P

D = 256
HEADS = 8
HD = D // HEADS
SIDE = 128
NQ = 125
NP = 128
HQ = HEADS * NP
PAIR = 2 * NP
FF = 2048
CHUNK = 512

masked_score = -1e30
norm_eps = 1e-05
scale = 1.0 / math.sqrt(HD)
log2e = math.log2(math.e)

bf16 = jnp.bfloat16
f32 = jnp.float32

ROWS_F = FF // 2
ROW_POS = 2 * D
ROW_SMALL = 2 * D + NP
ROWS_T = 3 * D
ROWS_K = 3 * D
TILE = 16


def axes_of(pages):
    axes = {"core": (2, 1), "y": (2, 2)}
    stride = 4
    while stride < pages:
        radix = 4 if pages // stride % 4 == 0 else 2
        axes["z%d" % (len(axes) - 2)] = (radix, stride)
        stride *= radix
    axes["x"] = (2, 0)
    return axes


def far_axes(pages):
    return [(name,) for name in axes_of(pages) if name.startswith("z")]


def sum_groups(pages):
    far = far_axes(pages)
    return [("core",), ("y",), *far], [("core", "y"), *far], [("core",), ("x",), ("y",), *far]


def padded(rows, pages):
    unit = TILE * pages
    return (rows + unit - 1) // unit * unit


def position_table():
    half = D // 2
    channel = np.arange(half)
    inverse = np.exp((channel // 2).astype(np.float32) * np.float32(-2.0 * math.log(10000.0) / half))
    angle = (np.arange(SIDE, dtype=np.float32) + 1.0) * np.float32(2.0 * math.pi / SIDE)
    angle = angle[:, None] * inverse
    return np.where(channel % 2 == 0, np.sin(angle), np.cos(angle)).astype(np.float32)


def dot(a, b):
    return jnp.dot(a, b, preferred_element_type=f32)


def dot_nt(a, b):
    return lax.dot_general(a, b, (((1,), (1,)), ((), ())), preferred_element_type=f32)


def dot_tn(a, b):
    return lax.dot_general(a, b, (((0,), (0,)), ((), ())), preferred_element_type=f32)


def row_total(values):
    return jnp.sum(values.astype(f32), axis=0, keepdims=True)


def norm_forward(values):
    average = jnp.mean(values, axis=-1, keepdims=True)
    centred = values - average
    variance = jnp.mean(centred * centred, axis=-1, keepdims=True)
    rstd = lax.rsqrt(variance + norm_eps)
    return centred * rstd, rstd


def norm_backward(grad, normed, rstd, gain):
    grad_normed = grad * gain
    first = jnp.mean(grad_normed, axis=-1, keepdims=True)
    second = jnp.mean(grad_normed * normed, axis=-1, keepdims=True)
    grad_in = rstd * (grad_normed - first - normed * second)
    return grad_in, row_total(grad * normed), row_total(grad)


def spread_rows(rows):
    head = lax.broadcasted_iota(jnp.int32, (NP, D), 1) // HD
    return jnp.concatenate(
        [jnp.where(head == h, rows, 0.0) for h in range(HEADS)], axis=0
    ).astype(bf16)


def spread_cols(cols):
    head = lax.broadcasted_iota(jnp.int32, (D, NP), 0) // HD
    return jnp.concatenate(
        [jnp.where(head == h, cols, 0.0) for h in range(HEADS)], axis=1
    ).astype(bf16)


def own_heads(full):
    return jnp.concatenate(
        [full[HD * h : HD * h + HD, NP * h : NP * h + NP] for h in range(HEADS)], axis=0
    )


def project_heads(weight_t, sums):
    high = sums.astype(bf16)
    low = (sums - high.astype(f32)).astype(bf16)
    return own_heads(dot(weight_t, high) + dot(weight_t, low))


def own_blocks(pairs):
    parts = []
    for pair in pairs:
        parts += [pair[:HD, :NP], pair[HD:, NP:]]
    return jnp.concatenate(parts, axis=0)


def head_rows(row):
    return jnp.concatenate([row[:, NP * h : NP * h + NP] for h in range(HEADS)], axis=0)


def head_line(rows):
    return jnp.concatenate([rows[h : h + 1] for h in range(HEADS)], axis=1)


def per_channel(rows):
    return jnp.concatenate(
        [jnp.broadcast_to(rows[h : h + 1], (HD, NP)) for h in range(HEADS)], axis=0
    )


def head_sums(cols):
    return jnp.concatenate(
        [jnp.sum(cols[HD * h : HD * h + HD], axis=0, keepdims=True) for h in range(HEADS)], axis=0
    )


def pair_cols(p):
    return slice(PAIR * p, PAIR * p + PAIR)


def pair_rows(p):
    return slice(2 * HD * p, 2 * HD * p + 2 * HD)


class Place:
    def __init__(self, pages):
        self.axes = axes_of(pages)
        self.page = lax.axis_index("dp")
        self.member = lax.axis_index("blk")
        self.digit = {
            name: self.member if name == "x" else lax.rem(self.page // stride, radix)
            for name, (radix, stride) in self.axes.items()
        }

    def size(self, group):
        return math.prod(self.axes[name][0] for name in group)

    def index(self, group):
        index = 0
        for name in group:
            index = index * self.axes[name][0] + self.digit[name]
        return index

    def peer(self, group, hop):
        index = lax.rem(self.index(group) + hop, self.size(group))
        page, member, rest = self.page, self.member, index
        for name in reversed(group):
            radix, stride = self.axes[name]
            digit = lax.rem(rest, radix)
            rest = rest // radix
            if name == "x":
                member = digit
            else:
                page = page + (digit - self.digit[name]) * stride
        return (page, member), index


class PageSum:
    def __init__(self, place, groups, back, rows, landing, whole, sent, arrived):
        self.place, self.groups, self.back = place, groups, back
        self.rows, self.landing, self.whole = rows, landing, whole
        self.sent, self.arrived = sent, arrived
        self.slots = 0
        self.extents = [rows.shape[0]]
        self.bases = [0]
        self.landings = []
        at = 0
        for group in groups:
            size = place.size(group)
            extent = self.extents[-1] // size
            self.landings.append(at)
            at += (size - 1) * extent
            self.bases.append(pl.multiple_of(self.bases[-1] + place.index(group) * extent, TILE))
            self.extents.append(extent)
        last = len(groups)
        moves = [self.scatter_moves(s) for s in range(last)]
        near = {"all": 0, "across": 1, "sides": 2}[back]
        moves += [self.gather_moves(s) for s in range(last - 1, near - 1, -1)]
        if back == "sides":
            moves += [self.side_moves(), self.corner_moves(), self.core_moves()]
        elif back == "across":
            moves += [self.across_moves(), self.core_moves()]
        self.phases = [functools.partial(self.step, moves, k) for k in range(len(moves) + 1)]

    @staticmethod
    def landing_rows(pages, groups, rows):
        axes = axes_of(pages)
        total, extent = 0, rows
        for group in groups:
            size = math.prod(axes[name][0] for name in group)
            extent //= size
            total += (size - 1) * extent
        return total

    def step(self, moves, k):
        last = len(self.groups)
        if k > 0:
            for move in moves[k - 1]:
                self.copy(*move).wait()
        if 0 < k <= last:
            total = self.scatter_sum(k - 1)
            region = pl.ds(self.bases[k], self.extents[k])
            if k < last:
                self.rows[region] = total
            elif len(self.whole.shape) == 3:
                self.whole[self.place.member, region] = total
            else:
                self.whole[region] = total
        if k < len(moves):
            for move in moves[k]:
                self.copy(*move).start()

    def copy(self, slot, source, target, device):
        return pltpu.make_async_remote_copy(
            src_ref=source(),
            dst_ref=target(),
            send_sem=self.sent.at[slot],
            recv_sem=self.arrived.at[slot],
            device_id=device,
            device_id_type=pl.DeviceIdType.MESH,
        )

    def new_slot(self):
        self.slots += 1
        return self.slots - 1

    def same(self, device, view):
        return (self.new_slot(), view, view, device)

    def scatter_moves(self, step):
        group = self.groups[step]
        extent = self.extents[step + 1]
        moves = []
        for hop in range(1, self.place.size(group)):
            device, other = self.place.peer(group, hop)
            start = pl.multiple_of(self.bases[step] + other * extent, TILE)
            landing = self.landings[step] + (hop - 1) * extent
            moves.append(
                (
                    self.new_slot(),
                    functools.partial(self.part, self.rows, start, extent),
                    functools.partial(self.part, self.landing, landing, extent),
                    device,
                )
            )
        return moves

    @staticmethod
    def part(ref, start, extent):
        return ref.at[pl.ds(start, extent)]

    def half(self, member, start, extent):
        if len(self.whole.shape) == 3:
            return self.whole.at[member, pl.ds(start, extent)]
        return self.whole.at[pl.ds(start, extent)]

    def scatter_sum(self, step):
        extent = self.extents[step + 1]
        total = self.rows[pl.ds(self.bases[step + 1], extent)].astype(f32)
        for hop in range(1, self.place.size(self.groups[step])):
            landing = self.landings[step] + (hop - 1) * extent
            total = total + self.landing[pl.ds(landing, extent)].astype(f32)
        return total.astype(bf16)

    def gather_moves(self, step):
        group = self.groups[step]
        view = functools.partial(self.half, self.place.member, self.bases[step + 1], self.extents[step + 1])
        return [
            self.same(self.place.peer(group, hop)[0], view) for hop in range(1, self.place.size(group))
        ]

    def own_quarter(self):
        step = 2 if len(self.groups[0]) == 1 else 1
        return self.bases[step], self.extents[step]

    def side_moves(self):
        view = functools.partial(self.half, self.place.member, *self.own_quarter())
        return [self.same(self.place.peer((name,), 1)[0], view) for name in ("y", "x")]

    def corner_moves(self):
        base, extent = self.own_quarter()
        other = pl.multiple_of(base + (1 - 2 * self.place.digit["y"]) * extent, TILE)
        view = functools.partial(self.half, self.place.member, other, extent)
        return [self.same(self.place.peer(("x",), 1)[0], view)]

    def across_moves(self):
        view = functools.partial(self.half, self.place.member, *self.own_quarter())
        return [self.same(self.place.peer(("x", "y"), hop)[0], view) for hop in range(1, 4)]

    def core_moves(self):
        extent = self.extents[0] // 2
        start = pl.multiple_of(self.place.digit["core"] * extent, TILE)
        device, _ = self.place.peer(("core",), 1)
        return [self.same(device, functools.partial(self.half, m, start, extent)) for m in range(2)]


def clear_rest(ref, used):
    if ref.shape[0] > used:
        ref[used:] = jnp.zeros((ref.shape[0] - used, D), ref.dtype)


def layer_kernel(
    tokens,
    pages,
    queries_in,
    memory_hbm,
    turns_in,
    order_in,
    lengths_in,
    attn_in,
    attn_out,
    attn_bias,
    ffn_in_hbm,
    ffn_in_bias,
    ffn_out_hbm,
    ffn_out_bias,
    norm_gain,
    norm_bias,
    pos_in,
    out_grad_in,
    table_in,
    result_out,
    queries_grad_out,
    memory_grad_hbm,
    whole_f_hbm,
    whole_g_hbm,
    whole_t_hbm,
    whole_k_hbm,
    memory_s,
    key_in_s,
    probs_s,
    grad_scores_s,
    code_s,
    query_kt,
    grad_vt,
    back_s,
    table_s,
    mask_s,
    top_s,
    total_s,
    mixed_s,
    pad_s,
    send_a,
    recv_a,
    send_t,
    recv_t,
    send_b,
    recv_b,
    small_s,
    rows_f,
    landing_f,
    whole_f,
    rows_g,
    landing_g,
    whole_g,
    rows_t,
    landing_t,
    whole_t,
    rows_k,
    landing_k,
    whole_k,
    load_sem,
    store_sem,
    link_sem,
    sent_f,
    arrived_f,
    sent_g,
    arrived_g,
    sent_t,
    arrived_t,
    sent_k,
    arrived_k,
):
    member = lax.axis_index("blk")
    partner = (lax.axis_index("dp"), 1 - member)
    chunks = tokens // CHUNK

    place = Place(pages)
    groups_f, groups_t, groups_k = sum_groups(pages)
    sum_f = PageSum(place, groups_f, "sides", rows_f, landing_f, whole_f, sent_f, arrived_f)
    sum_g = PageSum(place, groups_f, "sides", rows_g, landing_g, whole_g, sent_g, arrived_g)
    sum_t = PageSum(place, groups_t, "across", rows_t, landing_t, whole_t, sent_t, arrived_t)
    sum_k = PageSum(place, groups_k, "all", rows_k, landing_k, whole_k, sent_k, arrived_k)

    barrier = pltpu.get_barrier_semaphore()
    peers = [
        place.peer(group, hop)[0]
        for group in [("x", "core", "y"), *far_axes(pages)]
        for hop in range(1, place.size(group))
    ]
    for peer in peers:
        pl.semaphore_signal(barrier, inc=1, device_id=peer, device_id_type=pl.DeviceIdType.MESH)

    load_memory = pltpu.make_async_copy(memory_hbm.at[0], memory_s, load_sem.at[0])
    half = FF // 2
    ffn_in_s = [grad_scores_s.at[D * k : D * k + D] for k in range(2)]
    ffn_out_s = grad_scores_s.at[2 * D : 2 * D + FF, :D]
    free = 2 * D + FF
    active_s = [grad_scores_s.at[free + NP * k : free + NP * k + NP] for k in range(2)]
    slope_s = [grad_scores_s.at[free + NP * k : free + NP * k + NP] for k in range(2, 4)]
    load_ffn = [
        pltpu.make_async_copy(ffn_in_hbm.at[:, half * k : half * k + half], ffn_in_s[k], load_sem.at[1 + k])
        for k in range(2)
    ]
    load_ffn.append(pltpu.make_async_copy(ffn_out_hbm, ffn_out_s, load_sem.at[3]))
    load_memory.start()
    for load in load_ffn:
        load.start()

    pairs = [attn_bias[j].astype(f32) for j in range(3)]
    bias = jnp.concatenate([pair[k : k + 1] for k in range(2) for pair in pairs], axis=0)
    gain = norm_gain[...].astype(f32)
    shift = norm_bias[...].astype(f32)

    order = order_in[...]
    turn = turns_in[0]
    row_at = order >> 7
    col_at = order & 127
    top = SIDE - 1
    row_new = jnp.where(
        turn == 0, row_at, jnp.where(turn == 1, col_at, jnp.where(turn == 2, top - row_at, top - col_at))
    )
    col_new = jnp.where(
        turn == 0, col_at, jnp.where(turn == 1, top - row_at, jnp.where(turn == 2, top - col_at, row_at))
    )
    past = jnp.where(order < lengths_in[0], 0, SIDE * SIDE)
    code_s[...] = (row_new * SIDE + col_new + past).astype(f32)

    pad_s[...] = jnp.zeros_like(pad_s)
    pad_s[0, :NQ] = queries_in[0].astype(f32)
    pad_s[1, :NQ] = pos_in[...].astype(f32)
    pad_s[2, :NQ] = out_grad_in[0].astype(f32)
    queries_f = pad_s[0]
    pos_f = pad_s[1]
    queries_b = queries_f.astype(bf16)
    mixed_q = (queries_f + pos_f).astype(bf16)
    query_self = (dot(mixed_q, attn_in[0, 0]) + bias[0:1]).astype(bf16)
    key_self = dot(mixed_q, attn_in[0, 1]).astype(bf16)
    value_self = (dot(queries_b, attn_in[0, 2]) + bias[1:2]).astype(bf16)
    scores = dot(key_self, spread_cols(query_self.astype(f32).T)) * scale
    own_key = lax.broadcasted_iota(jnp.int32, (NP, HQ), 0) < NQ
    scores = jnp.where(own_key, scores, masked_score)
    raised = jnp.exp(scores - jnp.max(scores, axis=0, keepdims=True))
    probs_self = raised / jnp.sum(raised, axis=0, keepdims=True)
    probs_self_b = probs_self.astype(bf16)
    value_t = value_self.astype(f32).T.astype(bf16)
    attended = own_blocks(
        [dot(value_t[pair_rows(p)], probs_self_b[:, pair_cols(p)]) for p in range(4)]
    ).T.astype(bf16)
    first_normed, first_rstd = norm_forward(queries_f + dot(attended, attn_out[0]) + bias[2:3])
    first = first_normed * gain[0:1] + shift[0:1]
    cross_q = (first + pos_f).astype(bf16)
    query_c = (dot(cross_q, attn_in[1, 0]) + bias[3:4]).astype(bf16)
    query_x = spread_rows(query_c.astype(f32))
    query_k = dot(attn_in[1, 1], spread_cols(query_c.astype(f32).T))
    query_kt[...] = (query_k * (scale * log2e)).astype(bf16)
    back_s[:HQ] = (dot_nt(query_x, attn_in[1, 1]) * scale).astype(bf16)
    table = table_in[...]
    nothing = jnp.zeros((SIDE, D // 2), f32)
    table = jnp.concatenate(
        [jnp.concatenate([table, nothing], axis=1), jnp.concatenate([nothing, table], axis=1)], axis=0
    )
    table_high = table.astype(bf16)
    table_s[0] = table_high
    table_s[1] = (table - table_high.astype(f32)).astype(bf16)

    load_memory.wait()
    lane = lax.broadcasted_iota(jnp.int32, (CHUNK, NP), 1)

    def place_chunk(i):
        rows = pl.ds(pl.multiple_of(i * CHUNK, CHUNK), CHUNK)
        line = code_s[:, rows]
        code = jnp.concatenate(
            [
                jnp.broadcast_to(line[:, NP * j : NP * j + NP], (NP, NP)).T
                for j in range(CHUNK // NP)
            ],
            axis=0,
        ).astype(jnp.int32)
        row_hot = jnp.where(((code >> 7) & 127) == lane, 1.0, 0.0)
        col_hot = jnp.where((code & 127) == lane, 1.0, 0.0)
        hot = jnp.concatenate([row_hot, col_hot], axis=1).astype(bf16)
        mask = jnp.where(code < SIDE * SIDE, 0.0, masked_score)
        mask_s[rows] = mask
        block = memory_s[rows].astype(f32)
        key_in = (block + dot(hot, table_s[0]) + dot(hot, table_s[1])).astype(bf16)
        key_in_s[rows] = key_in
        mask = jnp.concatenate([mask, mask], axis=1)
        for p in range(4):
            cols = pair_cols(p)
            part = dot(key_in, query_kt[:, cols]) + mask
            part = jnp.max(part.reshape(CHUNK // 8, 8, PAIR), axis=0)
            top_s[:, cols] = jnp.maximum(top_s[:, cols], part)

    top_s[...] = jnp.full((8, HQ), -3e38, f32)

    @pl.loop(0, chunks // 2)
    def _(j):
        for k in range(2):
            place_chunk(j * 2 + k)

    highest_own = jnp.max(top_s[...], axis=0, keepdims=True)
    total_s[...] = jnp.zeros_like(total_s)
    mixed_s[...] = jnp.zeros_like(mixed_s)

    @pl.loop(0, chunks // 2)
    def _(i):
        rows = pl.ds(pl.multiple_of(i * 2 * CHUNK, 2 * CHUNK), 2 * CHUNK)
        memory_ct = memory_s[rows].T
        key_in = key_in_s[rows]
        mask = jnp.concatenate([mask_s[rows], mask_s[rows]], axis=1)
        for p in range(4):
            cols = pair_cols(p)
            part = dot(key_in, query_kt[:, cols]) + mask
            raised = jnp.exp2(part - highest_own[:, cols])
            total_s[:, cols] += jnp.sum(raised.reshape(CHUNK // 4, 8, PAIR), axis=0)
            probs_s[rows, cols] = raised.astype(bf16)
            mixed_s[:, cols] += dot(memory_ct, probs_s[rows, cols])

    total_own = jnp.sum(total_s[...], axis=0, keepdims=True)

    value_wt = attn_in[1, 2].astype(f32).T.astype(bf16)
    key_wt = attn_in[1, 1].astype(f32).T.astype(bf16)
    send_a[...] = project_heads(value_wt, mixed_s[...]).astype(bf16)
    send_t[:HEADS] = head_rows(highest_own)
    send_t[HEADS:] = head_rows(total_own)
    pl.semaphore_wait(barrier, len(peers))
    swap_a = pltpu.make_async_remote_copy(
        src_ref=send_a,
        dst_ref=recv_a,
        send_sem=link_sem.at[0],
        recv_sem=link_sem.at[1],
        device_id=partner,
        device_id_type=pl.DeviceIdType.MESH,
    )
    swap_t = pltpu.make_async_remote_copy(
        src_ref=send_t,
        dst_ref=recv_t,
        send_sem=link_sem.at[4],
        recv_sem=link_sem.at[5],
        device_id=partner,
        device_id_type=pl.DeviceIdType.MESH,
    )
    swap_a.start()
    swap_t.start()
    swap_a.wait()
    swap_t.wait()
    is_first = member == 0
    own, other = send_a[...].astype(f32), recv_a[...].astype(f32)
    left = jnp.where(is_first, own, other)
    right = jnp.where(is_first, other, own)
    own, other = send_t[...], recv_t[...]
    left_t = jnp.where(is_first, own, other)
    right_t = jnp.where(is_first, other, own)
    highest = jnp.maximum(left_t[:HEADS], right_t[:HEADS])
    fade_l = jnp.exp2(left_t[:HEADS] - highest)
    fade_r = jnp.exp2(right_t[:HEADS] - highest)
    total = left_t[HEADS:] * fade_l + right_t[HEADS:] * fade_r
    mixed_t = left * per_channel(fade_l / total) + right * per_channel(fade_r / total)
    own_share = jnp.exp2(highest_own - head_line(highest + jnp.log2(total)))
    attended_c = (mixed_t.T + bias[4:5]).astype(bf16)

    second_normed, second_rstd = norm_forward(first + dot(attended_c, attn_out[1]) + bias[5:6])
    second = second_normed * gain[1:2] + shift[1:2]
    ffn_input = second.astype(bf16)
    load_ffn[0].wait()
    load_ffn[1].wait()
    blocks = [(j // 4, slice(D * j, D * j + D), slice(j % 4 * D, j % 4 * D + D)) for j in range(FF // D)]
    hidden_bias = ffn_in_bias[...].astype(f32).reshape(1, FF)
    def feed_forward(gate_s):
        for k, cols, part in blocks:
            hidden = dot(ffn_input, ffn_in_s[k][:, part]) + hidden_bias[:, cols]
            half_gate = 0.5 + 0.5 * lax.erf(hidden * math.sqrt(0.5))
            active_s[k][:, part] = (hidden * half_gate).astype(bf16)
            gate_s[:, cols] = half_gate + hidden * jnp.exp(hidden * hidden * -0.5) * (
                1.0 / math.sqrt(2.0 * math.pi)
            )
        load_ffn[2].wait()
        third_normed, third_rstd = norm_forward(
            second
            + dot(active_s[0][...], ffn_out_s[:half])
            + dot(active_s[1][...], ffn_out_s[half:])
            + ffn_out_bias[...].astype(f32).reshape(1, D)
        )
        result_out[...] = (third_normed * gain[2:3] + shift[2:3])[:NQ].astype(bf16)
        grad_third, gain_grad_2, shift_grad_2 = norm_backward(
            pad_s[2], third_normed, third_rstd, gain[2:3]
        )
        grad_branch_f = grad_third.astype(bf16)
        for k, cols, part in blocks:
            grad_hidden = dot_nt(grad_branch_f, ffn_out_s[cols]) * gate_s[:, cols]
            slope_s[k][:, part] = grad_hidden.astype(bf16)
        return grad_third, gain_grad_2, shift_grad_2, grad_branch_f

    grad_third, gain_grad_2, shift_grad_2, grad_branch_f = pl.run_scoped(
        feed_forward, pltpu.VMEM((NP, FF), f32)
    )
    grad_second = grad_third + dot_nt(slope_s[0][...], ffn_in_s[0][...])
    grad_second += dot_nt(slope_s[1][...], ffn_in_s[1][...])
    grad_second_in, gain_grad_1, shift_grad_1 = norm_backward(
        grad_second, second_normed, second_rstd, gain[1:2]
    )
    grad_branch_c = grad_second_in.astype(bf16)
    ffn_input_t = second.T.astype(bf16)

    def ffn_rows(target, k):
        @pl.when(member == 0)
        def _():
            for j in range(4):
                part = slice(D * j, D * j + D)
                target[part] = dot(ffn_input_t, slope_s[k][:, part]).astype(bf16)

        @pl.when(member == 1)
        def _():
            for j in range(4):
                part = slice(D * j, D * j + D)
                target[part] = dot_tn(active_s[k][:, part], grad_branch_f).astype(bf16)

    ffn_rows(rows_f, 0)
    sum_f.phases[0]()
    ffn_rows(rows_g, 1)

    is_first = member == 0
    out_grad_c = dot_tn(attended_c, grad_branch_c)
    rows_k[2 * D : 3 * D] = jnp.where(is_first, out_grad_c, 0.0).astype(bf16)

    clear_rest(rows_f, ROWS_F)
    clear_rest(rows_g, ROWS_F)
    clear_rest(rows_t, ROWS_T)
    clear_rest(rows_k, ROWS_K)
    sum_g.phases[0]()
    grad_attended_c = dot_nt(grad_branch_c, attn_out[1]).astype(bf16).astype(f32)
    small_s[:16] = jnp.concatenate(
        [row_total(slope_s[k][:, part]) for k, _, part in blocks]
        + [
            row_total(grad_branch_f),
            row_total(grad_branch_c),
            gain_grad_2,
            shift_grad_2,
            gain_grad_1,
            shift_grad_1,
            row_total(grad_attended_c),
            jnp.zeros((1, D), f32),
        ],
        axis=0,
    )

    grad_attended_t = grad_attended_c.T
    grad_x = spread_rows(grad_attended_c)
    grad_v = dot(attn_in[1, 2], spread_cols(grad_attended_t)) * own_share
    grad_vt[...] = grad_v.astype(bf16)
    back_s[HQ:] = grad_v.T.astype(bf16)
    inner = head_line(head_sums(grad_attended_t * mixed_t)) * own_share
    rows_k[D : 2 * D] = dot((mixed_s[...] * own_share).astype(bf16), grad_x).astype(bf16)
    mixed_s[...] = jnp.zeros_like(mixed_s)

    queue_f = [phase for pair in zip(sum_f.phases[1:], sum_g.phases[1:]) for phase in pair]
    queue_t = list(sum_t.phases)
    queue_k = list(sum_k.phases)

    def take(queue):
        if queue:
            queue.pop(0)()

    def at(i, steps):
        for step, queue in steps:
            pl.when(i == (step * chunks) // 32)(queue.pop(0))

    @pl.loop(0, chunks // 2)
    def _(i):
        rows = pl.ds(pl.multiple_of(i * 2 * CHUNK, 2 * CHUNK), 2 * CHUNK)
        key_ct = key_in_s[rows].T
        memory_c = memory_s[rows]
        for p in range(4):
            cols = pair_cols(p)
            grad_probs = dot(memory_c, grad_vt[:, cols])
            slopes = probs_s[rows, cols].astype(f32) * (grad_probs - inner[:, cols])
            grad_scores_s[rows, cols] = slopes.astype(bf16)
            mixed_s[:, cols] += dot(key_ct, grad_scores_s[rows, cols])
        at(i, [(3, queue_f), (4, queue_f), (8, queue_f), (9, queue_f), (13, queue_f), (14, queue_f)])

    send_b[...] = (project_heads(key_wt, mixed_s[...]) * scale).astype(bf16)
    swap_b = pltpu.make_async_remote_copy(
        src_ref=send_b,
        dst_ref=recv_b,
        send_sem=link_sem.at[2],
        recv_sem=link_sem.at[3],
        device_id=partner,
        device_id_type=pl.DeviceIdType.MESH,
    )
    swap_b.start()
    query_x = spread_rows(query_c.astype(f32))
    rows_k[:D] = (dot(mixed_s[...].astype(bf16), query_x) * scale).astype(bf16)
    take(queue_k)
    take(queue_f)
    take(queue_f)
    swap_b.wait()
    take(queue_k)
    grad_query_c = (send_b[...].astype(f32) + recv_b[...].astype(f32)).T.astype(bf16)

    cross_pos_grad = dot_nt(grad_query_c, attn_in[1, 0])
    grad_first_in, gain_grad_0, shift_grad_0 = norm_backward(
        grad_second_in + cross_pos_grad, first_normed, first_rstd, gain[0:1]
    )
    grad_branch = grad_first_in.astype(bf16)
    grad_attended = dot_nt(grad_branch, attn_out[0]).astype(bf16).astype(f32)
    take(queue_k)
    grad_probs = dot(value_self, spread_cols(grad_attended.T))
    inner_self = jnp.sum(probs_self * grad_probs, axis=0, keepdims=True)
    grad_scores = (probs_self * (grad_probs - inner_self)).astype(bf16)
    key_t = key_self.astype(f32).T.astype(bf16)
    grad_query_s = (
        own_blocks([dot(key_t[pair_rows(p)], grad_scores[:, pair_cols(p)]) for p in range(4)]) * scale
    ).T.astype(bf16)
    grad_key_s = (dot(grad_scores, spread_rows(query_self.astype(f32))) * scale).astype(bf16)
    grad_value_s = dot(probs_self_b, spread_rows(grad_attended)).astype(bf16)
    grad_mixed_q = dot_nt(grad_query_s, attn_in[0, 0]) + dot_nt(grad_key_s, attn_in[0, 1])
    queries_grad_out[...] = (grad_first_in + grad_mixed_q + dot_nt(grad_value_s, attn_in[0, 2]))[
        :NQ
    ].astype(bf16)
    small_s[16:] = jnp.concatenate(
        [
            row_total(grad_query_s),
            row_total(grad_value_s),
            row_total(grad_branch),
            row_total(grad_query_c),
            gain_grad_0,
            shift_grad_0,
            jnp.zeros((10, D), f32),
        ],
        axis=0,
    )
    @pl.when(member == 0)
    def _():
        rows_t[:D] = dot_tn(mixed_q, grad_query_s).astype(bf16)
        rows_t[D : 2 * D] = dot_tn(mixed_q, grad_key_s).astype(bf16)
        rows_t[2 * D : 3 * D] = dot_tn(queries_b, grad_value_s).astype(bf16)

    @pl.when(member == 1)
    def _():
        rows_t[:D] = dot_tn(cross_q, grad_query_c).astype(bf16)
        rows_t[D : 2 * D] = dot_tn(attended, grad_branch).astype(bf16)
        rows_t[ROW_POS:ROW_SMALL] = (grad_mixed_q + cross_pos_grad).astype(bf16)
        rows_t[ROW_SMALL : ROW_SMALL + 32] = small_s[...].astype(bf16)
        rows_t[ROW_SMALL + 32 : ROWS_T] = jnp.zeros((ROWS_T - ROW_SMALL - 32, D), bf16)

    take(queue_t)
    take(queue_k)
    take(queue_f)
    take(queue_f)

    @pl.loop(0, chunks // 2)
    def _(i):
        rows = pl.ds(pl.multiple_of(i * 2 * CHUNK, 2 * CHUNK), 2 * CHUNK)
        both = jnp.concatenate([grad_scores_s[rows], probs_s[rows]], axis=1)
        memory_s[rows] = dot(both, back_s[...]).astype(bf16)
        pltpu.make_async_copy(memory_s.at[rows], memory_grad_hbm.at[0, rows], store_sem.at[i]).start()
        at(
            i,
            [
                (3, queue_k),
                (5, queue_t),
                (6, queue_f),
                (7, queue_f),
                (8, queue_k),
                (9, queue_t),
                (11, queue_k),
                (13, queue_t),
                (14, queue_k),
            ],
        )

    while queue_f:
        take(queue_f)
    stores = [
        pltpu.make_async_copy(whole, target, load_sem.at[4 + k])
        for k, (whole, target) in enumerate(
            (
                (whole_f, whole_f_hbm),
                (whole_g, whole_g_hbm),
                (whole_t, whole_t_hbm),
                (whole_k, whole_k_hbm),
            )
        )
    ]
    stores[0].start()
    stores[1].start()
    while queue_t or queue_k:
        take(queue_t)
        take(queue_k)
    stores[2].start()
    stores[3].start()

    @pl.loop(0, chunks // 2)
    def _(i):
        rows = pl.ds(pl.multiple_of(i * 2 * CHUNK, 2 * CHUNK), 2 * CHUNK)
        pltpu.make_async_copy(memory_s.at[rows], memory_grad_hbm.at[0, rows], store_sem.at[i]).wait()

    for store in stores:
        store.wait()


def finish_kernel(
    result_in,
    queries_grad_in,
    memory_grad_in,
    whole_f,
    whole_g,
    whole_t,
    whole_k,
    result,
    queries_grad,
    memory_grad,
    attn_in_grad,
    attn_out_grad,
    attn_bias_grad,
    ffn_in_grad,
    ffn_in_bias_grad,
    ffn_out_grad,
    ffn_out_bias_grad,
    norm_gain_grad,
    norm_bias_grad,
    query_pos_grad,
    moved,
    in_sem,
    out_sem,
):
    pieces = in_sem.shape[0]
    piece = moved.shape[0] // pieces

    def fetch(j):
        rows = pl.ds(piece * j, piece)
        return pltpu.make_async_copy(memory_grad_in.at[0, rows], moved.at[rows], in_sem.at[j])

    def write(j):
        rows = pl.ds(piece * j, piece)
        return pltpu.make_async_copy(moved.at[rows], memory_grad.at[0, rows], out_sem.at[j])

    for j in range(pieces):
        fetch(j).start()
    result[0] = result_in[...]
    queries_grad[0] = queries_grad_in[...]
    for j in range(FF // D):
        piece_at = j % (FF // D // 2) * D
        sums = whole_f if j < FF // D // 2 else whole_g
        ffn_in_grad[:, D * j : D * j + D] = sums[0, piece_at : piece_at + D].astype(f32)
        ffn_out_grad[D * j : D * j + D] = sums[1, piece_at : piece_at + D].astype(f32)
    for j in range(pieces):
        fetch(j).wait()
        write(j).start()
    attn_out_grad[0] = whole_t[1, D : 2 * D].astype(f32)
    attn_out_grad[1] = whole_k[2 * D : 3 * D].astype(f32)
    for j in range(3):
        attn_in_grad[0, j] = whole_t[0, D * j : D * j + D].astype(f32)
    attn_in_grad[1, 0] = whole_t[1, :D].astype(f32)
    attn_in_grad[1, 1] = whole_k[:D].astype(f32)
    attn_in_grad[1, 2] = whole_k[D : 2 * D].astype(f32)
    query_pos_grad[...] = whole_t[1, ROW_POS:ROW_SMALL].astype(f32)[:NQ]
    small = whole_t[1, ROW_SMALL : ROW_SMALL + 32].astype(f32)
    ffn_in_bias_grad[...] = jnp.concatenate([small[j : j + 1] for j in range(FF // D)], axis=1)
    ffn_out_bias_grad[...] = small[8:9]
    for j, (own, cross) in enumerate(((16, 19), (17, 14), (18, 9))):
        attn_bias_grad[j, 0:1] = small[own : own + 1]
        attn_bias_grad[j, 1:2] = small[cross : cross + 1]
    norm_gain_grad[0:1] = small[20:21]
    norm_gain_grad[1:2] = small[12:13]
    norm_gain_grad[2:3] = small[10:11]
    norm_bias_grad[0:1] = small[21:22]
    norm_bias_grad[1:2] = small[13:14]
    norm_bias_grad[2:3] = small[11:12]
    for j in range(pieces):
        write(j).wait()


def body(
    pages,
    queries,
    memory,
    quarter_turns,
    token_order,
    lengths,
    attn_in,
    attn_out,
    attn_bias,
    ffn_in,
    ffn_in_bias,
    ffn_out,
    ffn_out_bias,
    norm_gain,
    norm_bias,
    query_pos,
    out_grad,
):
    tokens = memory.shape[1]
    chunks = tokens // CHUNK
    groups_f, groups_t, groups_k = sum_groups(pages)
    summed = [
        (padded(ROWS_F, pages), groups_f),
        (padded(ROWS_F, pages), groups_f),
        (padded(ROWS_T, pages), groups_t),
        (padded(ROWS_K, 2 * pages), groups_k),
    ]
    whole_shapes = [(2, rows, D) for rows, _ in summed[:3]] + [(summed[3][0], D)]
    sum_buffers = []
    for (rows, groups), shape in zip(summed, whole_shapes):
        landing = PageSum.landing_rows(pages, groups, rows)
        sum_buffers += [pltpu.VMEM(each, bf16) for each in ((rows, D), (landing, D), shape)]
    copies = 32
    vmem = pl.BlockSpec(memory_space=pltpu.VMEM)
    smem = pl.BlockSpec(memory_space=pltpu.SMEM)
    anywhere = pl.BlockSpec(memory_space=pl.ANY)
    parts = pl.pallas_call(
        functools.partial(layer_kernel, tokens, pages),
        out_shape=[
            jax.ShapeDtypeStruct((NQ, D), bf16),
            jax.ShapeDtypeStruct((NQ, D), bf16),
            jax.ShapeDtypeStruct((1, tokens, D), bf16),
            *(jax.ShapeDtypeStruct(shape, bf16) for shape in whole_shapes),
        ],
        in_specs=[
            vmem,
            anywhere,
            smem,
            vmem,
            smem,
            vmem,
            vmem,
            vmem,
            anywhere,
            vmem,
            anywhere,
            vmem,
            vmem,
            vmem,
            vmem,
            vmem,
            vmem,
        ],
        out_specs=[vmem, vmem, anywhere, anywhere, anywhere, anywhere, anywhere],
        scratch_shapes=[
            pltpu.VMEM((tokens, D), bf16),
            pltpu.VMEM((tokens, D), bf16),
            pltpu.VMEM((tokens, HQ), bf16),
            pltpu.VMEM((tokens, HQ), bf16),
            pltpu.VMEM((1, tokens), f32),
            pltpu.VMEM((D, HQ), bf16),
            pltpu.VMEM((D, HQ), bf16),
            pltpu.VMEM((2 * HQ, D), bf16),
            pltpu.VMEM((2, 2 * SIDE, D), bf16),
            pltpu.VMEM((tokens, NP), f32),
            pltpu.VMEM((8, HQ), f32),
            pltpu.VMEM((8, HQ), f32),
            pltpu.VMEM((D, HQ), f32),
            pltpu.VMEM((3, NP, D), f32),
            pltpu.VMEM((D, NP), bf16),
            pltpu.VMEM((D, NP), bf16),
            pltpu.VMEM((2 * HEADS, NP), f32),
            pltpu.VMEM((2 * HEADS, NP), f32),
            pltpu.VMEM((D, NP), bf16),
            pltpu.VMEM((D, NP), bf16),
            pltpu.VMEM((32, D), f32),
            *sum_buffers,
            pltpu.SemaphoreType.DMA((8,)),
            pltpu.SemaphoreType.DMA((chunks,)),
            pltpu.SemaphoreType.DMA((6,)),
            *[pltpu.SemaphoreType.DMA((copies,))] * 8,
        ],
        compiler_params=pltpu.CompilerParams(
            collective_id=0, has_side_effects=True, vmem_limit_bytes=63 * 1024 * 1024
        ),
        cost_estimate=pl.CostEstimate(
            flops=2 * 8 * tokens * HQ * D, bytes_accessed=20 << 20, transcendentals=tokens * HQ
        ),
        name="decoder_layer",
    )(
        queries,
        memory,
        quarter_turns,
        token_order,
        lengths,
        attn_in,
        attn_out,
        attn_bias.transpose(1, 0, 2),
        ffn_in,
        ffn_in_bias,
        ffn_out,
        ffn_out_bias,
        norm_gain,
        norm_bias,
        query_pos,
        out_grad,
        jnp.asarray(position_table()),
    )
    outs = pl.pallas_call(
        finish_kernel,
        out_shape=[
            jax.ShapeDtypeStruct((1, NQ, D), bf16),
            jax.ShapeDtypeStruct((1, NQ, D), bf16),
            jax.ShapeDtypeStruct((1, tokens, D), bf16),
            jax.ShapeDtypeStruct((2, 3, D, D), f32),
            jax.ShapeDtypeStruct((2, D, D), f32),
            jax.ShapeDtypeStruct((3, 2, D), f32),
            jax.ShapeDtypeStruct((D, FF), f32),
            jax.ShapeDtypeStruct((1, FF), f32),
            jax.ShapeDtypeStruct((FF, D), f32),
            jax.ShapeDtypeStruct((1, D), f32),
            jax.ShapeDtypeStruct((3, D), f32),
            jax.ShapeDtypeStruct((3, D), f32),
            jax.ShapeDtypeStruct((NQ, D), f32),
        ],
        in_specs=[vmem, vmem, anywhere, vmem, vmem, vmem, vmem],
        out_specs=[vmem, vmem, anywhere] + [vmem] * 10,
        scratch_shapes=[
            pltpu.VMEM((tokens, D), bf16),
            pltpu.SemaphoreType.DMA((8,)),
            pltpu.SemaphoreType.DMA((8,)),
        ],
        compiler_params=pltpu.CompilerParams(vmem_limit_bytes=62 * 1024 * 1024),
        name="write_outputs",
    )(*parts)
    return (
        *outs[:5],
        outs[5].transpose(1, 0, 2),
        outs[6],
        outs[7].reshape(FF),
        outs[8],
        outs[9].reshape(D),
        *outs[10:],
    )


def solution(mesh):
    in_specs = (
        P("dp", None, None),
        P("dp", "blk", None),
        P("dp"),
        P("dp", "blk"),
        P("dp"),
        P(),
        P(),
        P(),
        P(),
        P(),
        P(),
        P(),
        P(),
        P(),
        P(),
        P("dp", None, None),
    )
    out_specs = (
        P("dp", None, None),
        P("dp", None, None),
        P("dp", "blk", None),
        P(),
        P(),
        P(),
        P(),
        P(),
        P(),
        P(),
        P(),
        P(),
        P(),
    )
    layer = functools.partial(body, mesh.shape["dp"])
    return jax.shard_map(layer, mesh=mesh, in_specs=in_specs, out_specs=out_specs, check_vma=False)
```

```python
import functools
import math

import jax
import jax.numpy as jnp
import numpy as np
from jax import lax
from jax.experimental import pallas as pl
from jax.experimental.pallas import tpu as pltpu
from jax.sharding import PartitionSpec as P

D = 256
HEADS = 8
HD = D // HEADS
SIDE = 128
NQ = 125
NP = 128
HQ = HEADS * NP
PAIR = 2 * NP
FF = 2048
CHUNK = 1024

masked_score = -1e30
norm_eps = 1e-05
scale = 1.0 / math.sqrt(HD)
log2e = math.log2(math.e)

bf16 = jnp.bfloat16
f32 = jnp.float32

ROWS_F = FF // 2
ROW_POS = 2 * D
ROW_SMALL = 2 * D + NP
ROWS_T = 3 * D
ROWS_K = 3 * D
TILE = 16


def axes_of(pages):
    axes = {"core": (2, 1), "y": (2, 2)}
    stride = 4
    while stride < pages:
        radix = 4 if pages // stride % 4 == 0 else 2
        axes["z%d" % (len(axes) - 2)] = (radix, stride)
        stride *= radix
    axes["x"] = (2, 0)
    return axes


def far_axes(pages):
    return [(name,) for name in axes_of(pages) if name.startswith("z")]


def sum_groups(pages):
    far = far_axes(pages)
    return [("core",), ("y",), *far], [("core", "y"), *far], [("core",), ("x",), ("y",), *far]


def padded(rows, pages):
    unit = TILE * pages
    return (rows + unit - 1) // unit * unit


def position_table():
    half = D // 2
    channel = np.arange(half)
    inverse = np.exp((channel // 2).astype(np.float32) * np.float32(-2.0 * math.log(10000.0) / half))
    angle = (np.arange(SIDE, dtype=np.float32) + 1.0) * np.float32(2.0 * math.pi / SIDE)
    angle = angle[:, None] * inverse
    return np.where(channel % 2 == 0, np.sin(angle), np.cos(angle)).astype(np.float32)


def dot(a, b):
    return jnp.dot(a, b, preferred_element_type=f32)


def dot_nt(a, b):
    return lax.dot_general(a, b, (((1,), (1,)), ((), ())), preferred_element_type=f32)


def dot_tn(a, b):
    return lax.dot_general(a, b, (((0,), (0,)), ((), ())), preferred_element_type=f32)


def row_total(values):
    return jnp.sum(values.astype(f32), axis=0, keepdims=True)


def norm_forward(values):
    average = jnp.mean(values, axis=-1, keepdims=True)
    centred = values - average
    variance = jnp.mean(centred * centred, axis=-1, keepdims=True)
    rstd = lax.rsqrt(variance + norm_eps)
    return centred * rstd, rstd


def norm_backward(grad, normed, rstd, gain):
    grad_normed = grad * gain
    first = jnp.mean(grad_normed, axis=-1, keepdims=True)
    second = jnp.mean(grad_normed * normed, axis=-1, keepdims=True)
    grad_in = rstd * (grad_normed - first - normed * second)
    return grad_in, row_total(grad * normed), row_total(grad)


def spread_rows(rows):
    head = lax.broadcasted_iota(jnp.int32, (NP, D), 1) // HD
    return jnp.concatenate(
        [jnp.where(head == h, rows, 0.0) for h in range(HEADS)], axis=0
    ).astype(bf16)


def spread_cols(cols):
    head = lax.broadcasted_iota(jnp.int32, (D, NP), 0) // HD
    return jnp.concatenate(
        [jnp.where(head == h, cols, 0.0) for h in range(HEADS)], axis=1
    ).astype(bf16)


def own_heads(full):
    return jnp.concatenate(
        [full[HD * h : HD * h + HD, NP * h : NP * h + NP] for h in range(HEADS)], axis=0
    )


def project_heads(weight_t, sums):
    high = sums.astype(bf16)
    low = (sums - high.astype(f32)).astype(bf16)
    return own_heads(dot(weight_t, high) + dot(weight_t, low))


def own_blocks(pairs):
    parts = []
    for pair in pairs:
        parts += [pair[:HD, :NP], pair[HD:, NP:]]
    return jnp.concatenate(parts, axis=0)


def head_rows(row):
    return jnp.concatenate([row[:, NP * h : NP * h + NP] for h in range(HEADS)], axis=0)


def head_line(rows):
    return jnp.concatenate([rows[h : h + 1] for h in range(HEADS)], axis=1)


def per_channel(rows):
    return jnp.concatenate(
        [jnp.broadcast_to(rows[h : h + 1], (HD, NP)) for h in range(HEADS)], axis=0
    )


def head_sums(cols):
    return jnp.concatenate(
        [jnp.sum(cols[HD * h : HD * h + HD], axis=0, keepdims=True) for h in range(HEADS)], axis=0
    )


def pair_cols(p):
    return slice(PAIR * p, PAIR * p + PAIR)


def pair_rows(p):
    return slice(2 * HD * p, 2 * HD * p + 2 * HD)


class Place:
    def __init__(self, pages):
        self.axes = axes_of(pages)
        self.page = lax.axis_index("dp")
        self.member = lax.axis_index("blk")
        self.digit = {
            name: self.member if name == "x" else lax.rem(self.page // stride, radix)
            for name, (radix, stride) in self.axes.items()
        }

    def size(self, group):
        return math.prod(self.axes[name][0] for name in group)

    def index(self, group):
        index = 0
        for name in group:
            index = index * self.axes[name][0] + self.digit[name]
        return index

    def peer(self, group, hop):
        index = lax.rem(self.index(group) + hop, self.size(group))
        page, member, rest = self.page, self.member, index
        for name in reversed(group):
            radix, stride = self.axes[name]
            digit = lax.rem(rest, radix)
            rest = rest // radix
            if name == "x":
                member = digit
            else:
                page = page + (digit - self.digit[name]) * stride
        return (page, member), index


class PageSum:
    def __init__(self, place, groups, back, rows, landing, whole, sent, arrived):
        self.place, self.groups, self.back = place, groups, back
        self.rows, self.landing, self.whole = rows, landing, whole
        self.sent, self.arrived = sent, arrived
        self.slots = 0
        self.extents = [rows.shape[0]]
        self.bases = [0]
        self.landings = []
        at = 0
        for group in groups:
            size = place.size(group)
            extent = self.extents[-1] // size
            self.landings.append(at)
            at += (size - 1) * extent
            self.bases.append(pl.multiple_of(self.bases[-1] + place.index(group) * extent, TILE))
            self.extents.append(extent)
        last = len(groups)
        moves = [self.scatter_moves(s) for s in range(last)]
        near = {"all": 0, "across": 1, "sides": 2}[back]
        moves += [self.gather_moves(s) for s in range(last - 1, near - 1, -1)]
        if back == "sides":
            moves += [self.side_moves(), self.corner_moves(), self.core_moves()]
        elif back == "across":
            moves += [self.across_moves(), self.core_moves()]
        self.phases = [functools.partial(self.step, moves, k) for k in range(len(moves) + 1)]

    @staticmethod
    def landing_rows(pages, groups, rows):
        axes = axes_of(pages)
        total, extent = 0, rows
        for group in groups:
            size = math.prod(axes[name][0] for name in group)
            extent //= size
            total += (size - 1) * extent
        return total

    def step(self, moves, k):
        last = len(self.groups)
        if k > 0:
            for move in moves[k - 1]:
                self.copy(*move).wait()
        if 0 < k <= last:
            total = self.scatter_sum(k - 1)
            region = pl.ds(self.bases[k], self.extents[k])
            if k < last:
                self.rows[region] = total
            elif len(self.whole.shape) == 3:
                self.whole[self.place.member, region] = total
            else:
                self.whole[region] = total
        if k < len(moves):
            for move in moves[k]:
                self.copy(*move).start()

    def copy(self, slot, source, target, device):
        return pltpu.make_async_remote_copy(
            src_ref=source(),
            dst_ref=target(),
            send_sem=self.sent.at[slot],
            recv_sem=self.arrived.at[slot],
            device_id=device,
            device_id_type=pl.DeviceIdType.MESH,
        )

    def new_slot(self):
        self.slots += 1
        return self.slots - 1

    def same(self, device, view):
        return (self.new_slot(), view, view, device)

    def scatter_moves(self, step):
        group = self.groups[step]
        extent = self.extents[step + 1]
        moves = []
        for hop in range(1, self.place.size(group)):
            device, other = self.place.peer(group, hop)
            start = pl.multiple_of(self.bases[step] + other * extent, TILE)
            landing = self.landings[step] + (hop - 1) * extent
            moves.append(
                (
                    self.new_slot(),
                    functools.partial(self.part, self.rows, start, extent),
                    functools.partial(self.part, self.landing, landing, extent),
                    device,
                )
            )
        return moves

    @staticmethod
    def part(ref, start, extent):
        return ref.at[pl.ds(start, extent)]

    def half(self, member, start, extent):
        if len(self.whole.shape) == 3:
            return self.whole.at[member, pl.ds(start, extent)]
        return self.whole.at[pl.ds(start, extent)]

    def scatter_sum(self, step):
        extent = self.extents[step + 1]
        total = self.rows[pl.ds(self.bases[step + 1], extent)].astype(f32)
        for hop in range(1, self.place.size(self.groups[step])):
            landing = self.landings[step] + (hop - 1) * extent
            total = total + self.landing[pl.ds(landing, extent)].astype(f32)
        return total.astype(bf16)

    def gather_moves(self, step):
        group = self.groups[step]
        view = functools.partial(self.half, self.place.member, self.bases[step + 1], self.extents[step + 1])
        return [
            self.same(self.place.peer(group, hop)[0], view) for hop in range(1, self.place.size(group))
        ]

    def own_quarter(self):
        step = 2 if len(self.groups[0]) == 1 else 1
        return self.bases[step], self.extents[step]

    def side_moves(self):
        view = functools.partial(self.half, self.place.member, *self.own_quarter())
        return [self.same(self.place.peer((name,), 1)[0], view) for name in ("y", "x")]

    def corner_moves(self):
        base, extent = self.own_quarter()
        other = pl.multiple_of(base + (1 - 2 * self.place.digit["y"]) * extent, TILE)
        view = functools.partial(self.half, self.place.member, other, extent)
        return [self.same(self.place.peer(("x",), 1)[0], view)]

    def across_moves(self):
        view = functools.partial(self.half, self.place.member, *self.own_quarter())
        return [self.same(self.place.peer(("x", "y"), hop)[0], view) for hop in range(1, 4)]

    def core_moves(self):
        extent = self.extents[0] // 2
        start = pl.multiple_of(self.place.digit["core"] * extent, TILE)
        device, _ = self.place.peer(("core",), 1)
        return [self.same(device, functools.partial(self.half, m, start, extent)) for m in range(2)]


def clear_rest(ref, used):
    if ref.shape[0] > used:
        ref[used:] = jnp.zeros((ref.shape[0] - used, D), ref.dtype)


def layer_kernel(
    tokens,
    pages,
    queries_in,
    memory_hbm,
    turns_in,
    order_in,
    lengths_in,
    attn_in,
    attn_out,
    attn_bias,
    ffn_in_hbm,
    ffn_in_bias,
    ffn_out_hbm,
    ffn_out_bias,
    norm_gain,
    norm_bias,
    pos_in,
    out_grad_in,
    table_in,
    result_out,
    queries_grad_out,
    memory_grad_hbm,
    whole_f_hbm,
    whole_g_hbm,
    whole_t_hbm,
    whole_k_hbm,
    memory_s,
    key_in_s,
    probs_s,
    grad_scores_s,
    code_s,
    query_kt,
    grad_vt,
    back_s,
    table_s,
    top_s,
    highest_s,
    shifts_s,
    factor_s,
    total_s,
    mixed_s,
    pad_s,
    send_a,
    recv_a,
    send_t,
    recv_t,
    send_b,
    recv_b,
    small_s,
    rows_f,
    landing_f,
    whole_f,
    rows_g,
    landing_g,
    whole_g,
    rows_t,
    landing_t,
    whole_t,
    rows_k,
    landing_k,
    whole_k,
    load_sem,
    store_sem,
    link_sem,
    sent_f,
    arrived_f,
    sent_g,
    arrived_g,
    sent_t,
    arrived_t,
    sent_k,
    arrived_k,
):
    member = lax.axis_index("blk")
    partner = (lax.axis_index("dp"), 1 - member)
    chunks = tokens // CHUNK

    place = Place(pages)
    groups_f, groups_t, groups_k = sum_groups(pages)
    sum_f = PageSum(place, groups_f, "sides", rows_f, landing_f, whole_f, sent_f, arrived_f)
    sum_g = PageSum(place, groups_f, "sides", rows_g, landing_g, whole_g, sent_g, arrived_g)
    sum_t = PageSum(place, groups_t, "across", rows_t, landing_t, whole_t, sent_t, arrived_t)
    sum_k = PageSum(place, groups_k, "all", rows_k, landing_k, whole_k, sent_k, arrived_k)

    barrier = pltpu.get_barrier_semaphore()
    peers = [
        place.peer(group, hop)[0]
        for group in [("x", "core", "y"), *far_axes(pages)]
        for hop in range(1, place.size(group))
    ]
    for peer in peers:
        pl.semaphore_signal(barrier, inc=1, device_id=peer, device_id_type=pl.DeviceIdType.MESH)

    load_memory = pltpu.make_async_copy(memory_hbm.at[0], memory_s, load_sem.at[0])
    half = FF // 2
    ffn_in_s = [grad_scores_s.at[D * k : D * k + D] for k in range(2)]
    ffn_out_s = grad_scores_s.at[2 * D : 2 * D + FF, :D]
    free = 2 * D + FF
    active_s = [grad_scores_s.at[free + NP * k : free + NP * k + NP] for k in range(2)]
    slope_s = [grad_scores_s.at[free + NP * k : free + NP * k + NP] for k in range(2, 4)]
    load_ffn = [
        pltpu.make_async_copy(ffn_in_hbm.at[:, half * k : half * k + half], ffn_in_s[k], load_sem.at[1 + k])
        for k in range(2)
    ]
    load_ffn.append(pltpu.make_async_copy(ffn_out_hbm, ffn_out_s, load_sem.at[3]))
    load_memory.start()
    for load in load_ffn:
        load.start()

    pairs = [attn_bias[j].astype(f32) for j in range(3)]
    bias = jnp.concatenate([pair[k : k + 1] for k in range(2) for pair in pairs], axis=0)
    gain = norm_gain[...].astype(f32)
    shift = norm_bias[...].astype(f32)

    order = order_in[...]
    turn = turns_in[0]
    row_at = order >> 7
    col_at = order & 127
    top = SIDE - 1
    row_new = jnp.where(
        turn == 0, row_at, jnp.where(turn == 1, col_at, jnp.where(turn == 2, top - row_at, top - col_at))
    )
    col_new = jnp.where(
        turn == 0, col_at, jnp.where(turn == 1, top - row_at, jnp.where(turn == 2, top - col_at, row_at))
    )
    past = jnp.where(order < lengths_in[0], 0, SIDE * SIDE)
    code_s[...] = (row_new * SIDE + col_new + past).astype(f32)

    pad_s[...] = jnp.zeros_like(pad_s)
    pad_s[0, :NQ] = queries_in[0].astype(f32)
    pad_s[1, :NQ] = pos_in[...].astype(f32)
    pad_s[2, :NQ] = out_grad_in[0].astype(f32)
    queries_f = pad_s[0]
    pos_f = pad_s[1]
    queries_b = queries_f.astype(bf16)
    mixed_q = (queries_f + pos_f).astype(bf16)
    query_self = (dot(mixed_q, attn_in[0, 0]) + bias[0:1]).astype(bf16)
    key_self = dot(mixed_q, attn_in[0, 1]).astype(bf16)
    value_self = (dot(queries_b, attn_in[0, 2]) + bias[1:2]).astype(bf16)
    scores = dot(key_self, spread_cols(query_self.astype(f32).T)) * scale
    own_key = lax.broadcasted_iota(jnp.int32, (NP, HQ), 0) < NQ
    scores = jnp.where(own_key, scores, masked_score)
    raised = jnp.exp(scores - jnp.max(scores, axis=0, keepdims=True))
    probs_self = raised / jnp.sum(raised, axis=0, keepdims=True)
    probs_self_b = probs_self.astype(bf16)
    value_t = value_self.astype(f32).T.astype(bf16)
    attended = own_blocks(
        [dot(value_t[pair_rows(p)], probs_self_b[:, pair_cols(p)]) for p in range(4)]
    ).T.astype(bf16)
    first_normed, first_rstd = norm_forward(queries_f + dot(attended, attn_out[0]) + bias[2:3])
    first = first_normed * gain[0:1] + shift[0:1]
    cross_q = (first + pos_f).astype(bf16)
    query_c = (dot(cross_q, attn_in[1, 0]) + bias[3:4]).astype(bf16)
    query_x = spread_rows(query_c.astype(f32))
    query_k = dot(attn_in[1, 1], spread_cols(query_c.astype(f32).T))
    query_kt[...] = (query_k * (scale * log2e)).astype(bf16)
    back_s[:HQ] = (dot_nt(query_x, attn_in[1, 1]) * scale).astype(bf16)
    table = table_in[...]
    nothing = jnp.zeros((SIDE, D // 2), f32)
    table = jnp.concatenate(
        [jnp.concatenate([table, nothing], axis=1), jnp.concatenate([nothing, table], axis=1)], axis=0
    )
    table_high = table.astype(bf16)
    table_s[: 2 * SIDE] = table_high
    table_s[2 * SIDE :] = (table - table_high.astype(f32)).astype(bf16)

    load_memory.wait()
    def mask_view(i):
        side, place = i // (chunks // 2), lax.rem(i, chunks // 2)
        return grad_scores_s.at[
            pl.ds(pl.multiple_of(tokens // 2 + place * CHUNK, CHUNK), CHUNK),
            pl.ds(pl.multiple_of(side * NP, NP), NP),
        ]

    lane = lax.broadcasted_iota(jnp.int32, (CHUNK, NP), 1)

    @pl.loop(0, chunks)
    def _(i):
        rows = pl.ds(pl.multiple_of(i * CHUNK, CHUNK), CHUNK)
        line = code_s[:, rows]
        code = jnp.concatenate(
            [
                jnp.broadcast_to(line[:, NP * j : NP * j + NP], (NP, NP)).T
                for j in range(CHUNK // NP)
            ],
            axis=0,
        ).astype(jnp.int32)
        row_hot = jnp.where(((code >> 7) & 127) == lane, 1.0, 0.0).astype(bf16)
        col_hot = jnp.where((code & 127) == lane, 1.0, 0.0).astype(bf16)
        hot = jnp.concatenate([row_hot, col_hot, row_hot, col_hot], axis=1)
        masked = jnp.where(code < SIDE * SIDE, 0.0, masked_score)
        mask_view(i)[...] = masked.astype(bf16)
        key_in_s[rows] = (memory_s[rows].astype(f32) + dot(hot, table_s[...])).astype(bf16)

    def score_pair(p, key_in, mask, score_s):
        cols = pair_cols(p)
        part = dot(key_in, query_kt[:, cols]) + mask
        score_s[:, cols] = part
        top_s[:, cols] = jnp.max(part.reshape(CHUNK // 8, 8, PAIR), axis=0)

    def score_operands(i):
        rows = pl.ds(pl.multiple_of(i * CHUNK, CHUNK), CHUNK)
        mask = mask_view(i)[...].astype(f32)
        return key_in_s[rows], jnp.concatenate([mask, mask], axis=1)

    def attend_all(score_s):
        operands = score_operands(0)
        for p in range(4):
            score_pair(p, *operands, score_s)

        @pl.loop(0, chunks)
        def _(i):
            rows = pl.ds(pl.multiple_of(i * CHUNK, CHUNK), CHUNK)
            memory_ct = memory_s[rows].T
            operands = score_operands(jnp.minimum(i + 1, chunks - 1))
            for p in range(4):
                cols = pair_cols(p)
                before = highest_s[0:1, cols]
                highest = jnp.maximum(before, jnp.max(top_s[:, cols], axis=0, keepdims=True))
                highest_s[0:1, cols] = highest
                shifts_s[pl.ds(i, 1), cols] = highest
                fade = jnp.exp2(before - highest)
                raised = jnp.exp2(score_s[:, cols] - highest)
                sums = jnp.sum(raised.reshape(CHUNK // 8, 8, PAIR), axis=0)
                total_s[:, cols] = total_s[:, cols] * fade + sums
                probs_s[rows, cols] = raised.astype(bf16)
                mixed_s[:, cols] = mixed_s[:, cols] * fade + dot(memory_ct, probs_s[rows, cols])
                score_pair(p, *operands, score_s)

    highest_s[0:1] = jnp.full((1, HQ), -3e38, f32)
    total_s[...] = jnp.zeros_like(total_s)
    mixed_s[...] = jnp.zeros_like(mixed_s)
    pl.run_scoped(attend_all, pltpu.VMEM((CHUNK, HQ), f32))
    highest_own = highest_s[0:1]
    total_own = jnp.sum(total_s[...], axis=0, keepdims=True)

    value_wt = attn_in[1, 2].astype(f32).T.astype(bf16)
    key_wt = attn_in[1, 1].astype(f32).T.astype(bf16)
    send_a[...] = project_heads(value_wt, mixed_s[...]).astype(bf16)
    send_t[:HEADS] = head_rows(highest_own)
    send_t[HEADS:] = head_rows(total_own)
    pl.semaphore_wait(barrier, len(peers))
    swap_a = pltpu.make_async_remote_copy(
        src_ref=send_a,
        dst_ref=recv_a,
        send_sem=link_sem.at[0],
        recv_sem=link_sem.at[1],
        device_id=partner,
        device_id_type=pl.DeviceIdType.MESH,
    )
    swap_t = pltpu.make_async_remote_copy(
        src_ref=send_t,
        dst_ref=recv_t,
        send_sem=link_sem.at[4],
        recv_sem=link_sem.at[5],
        device_id=partner,
        device_id_type=pl.DeviceIdType.MESH,
    )
    swap_a.start()
    swap_t.start()
    swap_a.wait()
    swap_t.wait()
    is_first = member == 0
    own, other = send_a[...].astype(f32), recv_a[...].astype(f32)
    left = jnp.where(is_first, own, other)
    right = jnp.where(is_first, other, own)
    own, other = send_t[...], recv_t[...]
    left_t = jnp.where(is_first, own, other)
    right_t = jnp.where(is_first, other, own)
    highest = jnp.maximum(left_t[:HEADS], right_t[:HEADS])
    fade_l = jnp.exp2(left_t[:HEADS] - highest)
    fade_r = jnp.exp2(right_t[:HEADS] - highest)
    total = left_t[HEADS:] * fade_l + right_t[HEADS:] * fade_r
    mixed_t = left * per_channel(fade_l / total) + right * per_channel(fade_r / total)
    log_total = head_line(highest + jnp.log2(total))
    own_share = jnp.exp2(highest_own - log_total)
    factor_s[...] = jnp.exp2(shifts_s[...] - log_total)
    attended_c = (mixed_t.T + bias[4:5]).astype(bf16)

    second_normed, second_rstd = norm_forward(first + dot(attended_c, attn_out[1]) + bias[5:6])
    second = second_normed * gain[1:2] + shift[1:2]
    ffn_input = second.astype(bf16)
    load_ffn[0].wait()
    load_ffn[1].wait()
    blocks = [(j // 4, slice(D * j, D * j + D), slice(j % 4 * D, j % 4 * D + D)) for j in range(FF // D)]
    hidden_bias = ffn_in_bias[...].astype(f32).reshape(1, FF)
    def feed_forward(gate_s):
        for k, cols, part in blocks:
            hidden = dot(ffn_input, ffn_in_s[k][:, part]) + hidden_bias[:, cols]
            half_gate = 0.5 + 0.5 * lax.erf(hidden * math.sqrt(0.5))
            active_s[k][:, part] = (hidden * half_gate).astype(bf16)
            gate_s[:, cols] = half_gate + hidden * jnp.exp(hidden * hidden * -0.5) * (
                1.0 / math.sqrt(2.0 * math.pi)
            )
        load_ffn[2].wait()
        third_normed, third_rstd = norm_forward(
            second
            + dot(active_s[0][...], ffn_out_s[:half])
            + dot(active_s[1][...], ffn_out_s[half:])
            + ffn_out_bias[...].astype(f32).reshape(1, D)
        )
        result_out[...] = (third_normed * gain[2:3] + shift[2:3])[:NQ].astype(bf16)
        grad_third, gain_grad_2, shift_grad_2 = norm_backward(
            pad_s[2], third_normed, third_rstd, gain[2:3]
        )
        grad_branch_f = grad_third.astype(bf16)
        for k, cols, part in blocks:
            grad_hidden = dot_nt(grad_branch_f, ffn_out_s[cols]) * gate_s[:, cols]
            slope_s[k][:, part] = grad_hidden.astype(bf16)
        return grad_third, gain_grad_2, shift_grad_2, grad_branch_f

    grad_third, gain_grad_2, shift_grad_2, grad_branch_f = pl.run_scoped(
        feed_forward, pltpu.VMEM((NP, FF), f32)
    )
    grad_second = grad_third + dot_nt(slope_s[0][...], ffn_in_s[0][...])
    grad_second += dot_nt(slope_s[1][...], ffn_in_s[1][...])
    grad_second_in, gain_grad_1, shift_grad_1 = norm_backward(
        grad_second, second_normed, second_rstd, gain[1:2]
    )
    grad_branch_c = grad_second_in.astype(bf16)
    ffn_input_t = second.T.astype(bf16)

    def ffn_rows(target, k):
        @pl.when(member == 0)
        def _():
            for j in range(4):
                part = slice(D * j, D * j + D)
                target[part] = dot(ffn_input_t, slope_s[k][:, part]).astype(bf16)

        @pl.when(member == 1)
        def _():
            for j in range(4):
                part = slice(D * j, D * j + D)
                target[part] = dot_tn(active_s[k][:, part], grad_branch_f).astype(bf16)

    ffn_rows(rows_f, 0)
    sum_f.phases[0]()
    ffn_rows(rows_g, 1)

    is_first = member == 0
    out_grad_c = dot_tn(attended_c, grad_branch_c)
    rows_k[2 * D : 3 * D] = jnp.where(is_first, out_grad_c, 0.0).astype(bf16)

    clear_rest(rows_f, ROWS_F)
    clear_rest(rows_g, ROWS_F)
    clear_rest(rows_t, ROWS_T)
    clear_rest(rows_k, ROWS_K)
    sum_g.phases[0]()
    grad_attended_c = dot_nt(grad_branch_c, attn_out[1]).astype(bf16).astype(f32)
    small_s[:16] = jnp.concatenate(
        [row_total(slope_s[k][:, part]) for k, _, part in blocks]
        + [
            row_total(grad_branch_f),
            row_total(grad_branch_c),
            gain_grad_2,
            shift_grad_2,
            gain_grad_1,
            shift_grad_1,
            row_total(grad_attended_c),
            jnp.zeros((1, D), f32),
        ],
        axis=0,
    )

    grad_attended_t = grad_attended_c.T
    grad_x = spread_rows(grad_attended_c)
    grad_v = dot(attn_in[1, 2], spread_cols(grad_attended_t))
    grad_vt[...] = grad_v.astype(bf16)
    back_s[HQ:] = grad_v.T.astype(bf16)
    inner = head_line(head_sums(grad_attended_t * mixed_t))
    rows_k[D : 2 * D] = dot((mixed_s[...] * own_share).astype(bf16), grad_x).astype(bf16)
    mixed_s[...] = jnp.zeros_like(mixed_s)

    queue_f = [phase for pair in zip(sum_f.phases[1:], sum_g.phases[1:]) for phase in pair]
    queue_t = list(sum_t.phases)
    queue_k = list(sum_k.phases)

    def take(queue):
        if queue:
            queue.pop(0)()

    def at(i, steps):
        for step, queue in steps:
            pl.when(i == (step * chunks) // 16)(queue.pop(0))

    @pl.loop(0, chunks)
    def _(i):
        rows = pl.ds(pl.multiple_of(i * CHUNK, CHUNK), CHUNK)
        key_ct = key_in_s[rows].T
        memory_c = memory_s[rows]
        for p in range(4):
            cols = pair_cols(p)
            grad_probs = dot(memory_c, grad_vt[:, cols])
            probs = probs_s[rows, cols].astype(f32) * factor_s[pl.ds(i, 1), cols]
            probs_s[rows, cols] = probs.astype(bf16)
            grad_scores_s[rows, cols] = (probs * (grad_probs - inner[:, cols])).astype(bf16)
            mixed_s[:, cols] += dot(key_ct, grad_scores_s[rows, cols])
        at(i, [(3, queue_f), (4, queue_f), (8, queue_f), (9, queue_f), (13, queue_f), (14, queue_f)])

    send_b[...] = (project_heads(key_wt, mixed_s[...]) * scale).astype(bf16)
    swap_b = pltpu.make_async_remote_copy(
        src_ref=send_b,
        dst_ref=recv_b,
        send_sem=link_sem.at[2],
        recv_sem=link_sem.at[3],
        device_id=partner,
        device_id_type=pl.DeviceIdType.MESH,
    )
    swap_b.start()
    query_x = spread_rows(query_c.astype(f32))
    rows_k[:D] = (dot(mixed_s[...].astype(bf16), query_x) * scale).astype(bf16)
    take(queue_k)
    take(queue_f)
    take(queue_f)
    swap_b.wait()
    take(queue_k)
    grad_query_c = (send_b[...].astype(f32) + recv_b[...].astype(f32)).T.astype(bf16)

    cross_pos_grad = dot_nt(grad_query_c, attn_in[1, 0])
    grad_first_in, gain_grad_0, shift_grad_0 = norm_backward(
        grad_second_in + cross_pos_grad, first_normed, first_rstd, gain[0:1]
    )
    grad_branch = grad_first_in.astype(bf16)
    grad_attended = dot_nt(grad_branch, attn_out[0]).astype(bf16).astype(f32)
    take(queue_k)
    grad_probs = dot(value_self, spread_cols(grad_attended.T))
    inner_self = jnp.sum(probs_self * grad_probs, axis=0, keepdims=True)
    grad_scores = (probs_self * (grad_probs - inner_self)).astype(bf16)
    key_t = key_self.astype(f32).T.astype(bf16)
    grad_query_s = (
        own_blocks([dot(key_t[pair_rows(p)], grad_scores[:, pair_cols(p)]) for p in range(4)]) * scale
    ).T.astype(bf16)
    grad_key_s = (dot(grad_scores, spread_rows(query_self.astype(f32))) * scale).astype(bf16)
    grad_value_s = dot(probs_self_b, spread_rows(grad_attended)).astype(bf16)
    grad_mixed_q = dot_nt(grad_query_s, attn_in[0, 0]) + dot_nt(grad_key_s, attn_in[0, 1])
    queries_grad_out[...] = (grad_first_in + grad_mixed_q + dot_nt(grad_value_s, attn_in[0, 2]))[
        :NQ
    ].astype(bf16)
    small_s[16:] = jnp.concatenate(
        [
            row_total(grad_query_s),
            row_total(grad_value_s),
            row_total(grad_branch),
            row_total(grad_query_c),
            gain_grad_0,
            shift_grad_0,
            jnp.zeros((10, D), f32),
        ],
        axis=0,
    )
    @pl.when(member == 0)
    def _():
        rows_t[:D] = dot_tn(mixed_q, grad_query_s).astype(bf16)
        rows_t[D : 2 * D] = dot_tn(mixed_q, grad_key_s).astype(bf16)
        rows_t[2 * D : 3 * D] = dot_tn(queries_b, grad_value_s).astype(bf16)

    @pl.when(member == 1)
    def _():
        rows_t[:D] = dot_tn(cross_q, grad_query_c).astype(bf16)
        rows_t[D : 2 * D] = dot_tn(attended, grad_branch).astype(bf16)
        rows_t[ROW_POS:ROW_SMALL] = (grad_mixed_q + cross_pos_grad).astype(bf16)
        rows_t[ROW_SMALL : ROW_SMALL + 32] = small_s[...].astype(bf16)
        rows_t[ROW_SMALL + 32 : ROWS_T] = jnp.zeros((ROWS_T - ROW_SMALL - 32, D), bf16)

    take(queue_t)
    take(queue_k)
    take(queue_f)
    take(queue_f)

    @pl.loop(0, chunks)
    def _(i):
        rows = pl.ds(pl.multiple_of(i * CHUNK, CHUNK), CHUNK)
        both = jnp.concatenate([grad_scores_s[rows], probs_s[rows]], axis=1)
        memory_s[rows] = dot(both, back_s[...]).astype(bf16)
        pltpu.make_async_copy(memory_s.at[rows], memory_grad_hbm.at[0, rows], store_sem.at[i]).start()
        at(
            i,
            [
                (3, queue_t),
                (4, queue_k),
                (7, queue_t),
                (8, queue_k),
                (9, queue_f),
                (10, queue_f),
                (11, queue_t),
                (12, queue_k),
                (15, queue_t),
            ],
        )

    while queue_f:
        take(queue_f)
    stores = [
        pltpu.make_async_copy(whole, target, load_sem.at[4 + k])
        for k, (whole, target) in enumerate(
            (
                (whole_f, whole_f_hbm),
                (whole_g, whole_g_hbm),
                (whole_t, whole_t_hbm),
                (whole_k, whole_k_hbm),
            )
        )
    ]
    stores[0].start()
    stores[1].start()
    while queue_t or queue_k:
        take(queue_t)
        take(queue_k)
    stores[2].start()
    stores[3].start()

    @pl.loop(0, chunks)
    def _(i):
        rows = pl.ds(pl.multiple_of(i * CHUNK, CHUNK), CHUNK)
        pltpu.make_async_copy(memory_s.at[rows], memory_grad_hbm.at[0, rows], store_sem.at[i]).wait()

    for store in stores:
        store.wait()


def finish_kernel(
    result_in,
    queries_grad_in,
    memory_grad_in,
    whole_f,
    whole_g,
    whole_t,
    whole_k,
    result,
    queries_grad,
    memory_grad,
    attn_in_grad,
    attn_out_grad,
    attn_bias_grad,
    ffn_in_grad,
    ffn_in_bias_grad,
    ffn_out_grad,
    ffn_out_bias_grad,
    norm_gain_grad,
    norm_bias_grad,
    query_pos_grad,
    moved,
    in_sem,
    out_sem,
):
    pieces = in_sem.shape[0]
    piece = moved.shape[0] // pieces

    def fetch(j):
        rows = pl.ds(piece * j, piece)
        return pltpu.make_async_copy(memory_grad_in.at[0, rows], moved.at[rows], in_sem.at[j])

    def write(j):
        rows = pl.ds(piece * j, piece)
        return pltpu.make_async_copy(moved.at[rows], memory_grad.at[0, rows], out_sem.at[j])

    for j in range(pieces):
        fetch(j).start()
    result[0] = result_in[...]
    queries_grad[0] = queries_grad_in[...]
    for j in range(FF // D):
        piece_at = j % (FF // D // 2) * D
        sums = whole_f if j < FF // D // 2 else whole_g
        ffn_in_grad[:, D * j : D * j + D] = sums[0, piece_at : piece_at + D].astype(f32)
        ffn_out_grad[D * j : D * j + D] = sums[1, piece_at : piece_at + D].astype(f32)
    for j in range(pieces):
        fetch(j).wait()
        write(j).start()
    attn_out_grad[0] = whole_t[1, D : 2 * D].astype(f32)
    attn_out_grad[1] = whole_k[2 * D : 3 * D].astype(f32)
    for j in range(3):
        attn_in_grad[0, j] = whole_t[0, D * j : D * j + D].astype(f32)
    attn_in_grad[1, 0] = whole_t[1, :D].astype(f32)
    attn_in_grad[1, 1] = whole_k[:D].astype(f32)
    attn_in_grad[1, 2] = whole_k[D : 2 * D].astype(f32)
    query_pos_grad[...] = whole_t[1, ROW_POS:ROW_SMALL].astype(f32)[:NQ]
    small = whole_t[1, ROW_SMALL : ROW_SMALL + 32].astype(f32)
    ffn_in_bias_grad[...] = jnp.concatenate([small[j : j + 1] for j in range(FF // D)], axis=1)
    ffn_out_bias_grad[...] = small[8:9]
    for j, (own, cross) in enumerate(((16, 19), (17, 14), (18, 9))):
        attn_bias_grad[j, 0:1] = small[own : own + 1]
        attn_bias_grad[j, 1:2] = small[cross : cross + 1]
    norm_gain_grad[0:1] = small[20:21]
    norm_gain_grad[1:2] = small[12:13]
    norm_gain_grad[2:3] = small[10:11]
    norm_bias_grad[0:1] = small[21:22]
    norm_bias_grad[1:2] = small[13:14]
    norm_bias_grad[2:3] = small[11:12]
    for j in range(pieces):
        write(j).wait()


def body(
    pages,
    queries,
    memory,
    quarter_turns,
    token_order,
    lengths,
    attn_in,
    attn_out,
    attn_bias,
    ffn_in,
    ffn_in_bias,
    ffn_out,
    ffn_out_bias,
    norm_gain,
    norm_bias,
    query_pos,
    out_grad,
):
    tokens = memory.shape[1]
    chunks = tokens // CHUNK
    groups_f, groups_t, groups_k = sum_groups(pages)
    summed = [
        (padded(ROWS_F, pages), groups_f),
        (padded(ROWS_F, pages), groups_f),
        (padded(ROWS_T, pages), groups_t),
        (padded(ROWS_K, 2 * pages), groups_k),
    ]
    whole_shapes = [(2, rows, D) for rows, _ in summed[:3]] + [(summed[3][0], D)]
    sum_buffers = []
    for (rows, groups), shape in zip(summed, whole_shapes):
        landing = PageSum.landing_rows(pages, groups, rows)
        sum_buffers += [pltpu.VMEM(each, bf16) for each in ((rows, D), (landing, D), shape)]
    copies = 32
    vmem = pl.BlockSpec(memory_space=pltpu.VMEM)
    smem = pl.BlockSpec(memory_space=pltpu.SMEM)
    anywhere = pl.BlockSpec(memory_space=pl.ANY)
    parts = pl.pallas_call(
        functools.partial(layer_kernel, tokens, pages),
        out_shape=[
            jax.ShapeDtypeStruct((NQ, D), bf16),
            jax.ShapeDtypeStruct((NQ, D), bf16),
            jax.ShapeDtypeStruct((1, tokens, D), bf16),
            *(jax.ShapeDtypeStruct(shape, bf16) for shape in whole_shapes),
        ],
        in_specs=[
            vmem,
            anywhere,
            smem,
            vmem,
            smem,
            vmem,
            vmem,
            vmem,
            anywhere,
            vmem,
            anywhere,
            vmem,
            vmem,
            vmem,
            vmem,
            vmem,
            vmem,
        ],
        out_specs=[vmem, vmem, anywhere, anywhere, anywhere, anywhere, anywhere],
        scratch_shapes=[
            pltpu.VMEM((tokens, D), bf16),
            pltpu.VMEM((tokens, D), bf16),
            pltpu.VMEM((tokens, HQ), bf16),
            pltpu.VMEM((tokens, HQ), bf16),
            pltpu.VMEM((1, tokens), f32),
            pltpu.VMEM((D, HQ), bf16),
            pltpu.VMEM((D, HQ), bf16),
            pltpu.VMEM((2 * HQ, D), bf16),
            pltpu.VMEM((4 * SIDE, D), bf16),
            pltpu.VMEM((8, HQ), f32),
            pltpu.VMEM((8, HQ), f32),
            pltpu.VMEM((chunks, HQ), f32),
            pltpu.VMEM((chunks, HQ), f32),
            pltpu.VMEM((8, HQ), f32),
            pltpu.VMEM((D, HQ), f32),
            pltpu.VMEM((3, NP, D), f32),
            pltpu.VMEM((D, NP), bf16),
            pltpu.VMEM((D, NP), bf16),
            pltpu.VMEM((2 * HEADS, NP), f32),
            pltpu.VMEM((2 * HEADS, NP), f32),
            pltpu.VMEM((D, NP), bf16),
            pltpu.VMEM((D, NP), bf16),
            pltpu.VMEM((32, D), f32),
            *sum_buffers,
            pltpu.SemaphoreType.DMA((8,)),
            pltpu.SemaphoreType.DMA((chunks,)),
            pltpu.SemaphoreType.DMA((6,)),
            *[pltpu.SemaphoreType.DMA((copies,))] * 8,
        ],
        compiler_params=pltpu.CompilerParams(
            collective_id=0, has_side_effects=True, vmem_limit_bytes=127 * 512 * 1024
        ),
        cost_estimate=pl.CostEstimate(
            flops=2 * 8 * tokens * HQ * D, bytes_accessed=20 << 20, transcendentals=tokens * HQ
        ),
        name="decoder_layer",
    )(
        queries,
        memory,
        quarter_turns,
        token_order,
        lengths,
        attn_in,
        attn_out,
        attn_bias.transpose(1, 0, 2),
        ffn_in,
        ffn_in_bias,
        ffn_out,
        ffn_out_bias,
        norm_gain,
        norm_bias,
        query_pos,
        out_grad,
        jnp.asarray(position_table()),
    )
    outs = pl.pallas_call(
        finish_kernel,
        out_shape=[
            jax.ShapeDtypeStruct((1, NQ, D), bf16),
            jax.ShapeDtypeStruct((1, NQ, D), bf16),
            jax.ShapeDtypeStruct((1, tokens, D), bf16),
            jax.ShapeDtypeStruct((2, 3, D, D), f32),
            jax.ShapeDtypeStruct((2, D, D), f32),
            jax.ShapeDtypeStruct((3, 2, D), f32),
            jax.ShapeDtypeStruct((D, FF), f32),
            jax.ShapeDtypeStruct((1, FF), f32),
            jax.ShapeDtypeStruct((FF, D), f32),
            jax.ShapeDtypeStruct((1, D), f32),
            jax.ShapeDtypeStruct((3, D), f32),
            jax.ShapeDtypeStruct((3, D), f32),
            jax.ShapeDtypeStruct((NQ, D), f32),
        ],
        in_specs=[vmem, vmem, anywhere, vmem, vmem, vmem, vmem],
        out_specs=[vmem, vmem, anywhere] + [vmem] * 10,
        scratch_shapes=[
            pltpu.VMEM((tokens, D), bf16),
            pltpu.SemaphoreType.DMA((8,)),
            pltpu.SemaphoreType.DMA((8,)),
        ],
        compiler_params=pltpu.CompilerParams(vmem_limit_bytes=62 * 1024 * 1024),
        name="write_outputs",
    )(*parts)
    return (
        *outs[:5],
        outs[5].transpose(1, 0, 2),
        outs[6],
        outs[7].reshape(FF),
        outs[8],
        outs[9].reshape(D),
        *outs[10:],
    )


def solution(mesh):
    in_specs = (
        P("dp", None, None),
        P("dp", "blk", None),
        P("dp"),
        P("dp", "blk"),
        P("dp"),
        P(),
        P(),
        P(),
        P(),
        P(),
        P(),
        P(),
        P(),
        P(),
        P(),
        P("dp", None, None),
    )
    out_specs = (
        P("dp", None, None),
        P("dp", None, None),
        P("dp", "blk", None),
        P(),
        P(),
        P(),
        P(),
        P(),
        P(),
        P(),
        P(),
        P(),
        P(),
    )
    layer = functools.partial(body, mesh.shape["dp"])
    return jax.shard_map(layer, mesh=mesh, in_specs=in_specs, out_specs=out_specs, check_vma=False)
```

```python
import functools
import math

import jax
import jax.numpy as jnp
import numpy as np
from jax import lax
from jax.experimental import pallas as pl
from jax.experimental.pallas import tpu as pltpu
from jax.sharding import PartitionSpec as P

D = 256
HEADS = 8
HD = D // HEADS
SIDE = 128
NQ = 125
NP = 128
HQ = HEADS * NP
PAIR = 2 * NP
FF = 2048
CHUNK = 1024

masked_score = -1e30
norm_eps = 1e-05
scale = 1.0 / math.sqrt(HD)
log2e = math.log2(math.e)

bf16 = jnp.bfloat16
f32 = jnp.float32

ROWS_F = FF // 2
ROW_POS = D
ROW_SMALL = D + NP
ROWS_T = 2 * D
ROWS_K = 3 * D
ROWS_U = D
TILE = 16


def axes_of(pages):
    axes = {"core": (2, 1), "y": (2, 2)}
    stride = 4
    while stride < pages:
        radix = 4 if pages // stride % 4 == 0 else 2
        axes["z%d" % (len(axes) - 2)] = (radix, stride)
        stride *= radix
    axes["x"] = (2, 0)
    return axes


def far_axes(pages):
    return [(name,) for name in axes_of(pages) if name.startswith("z")]


def sum_groups(pages):
    far = far_axes(pages)
    return [("core",), ("y",), *far], [("core", "y"), *far], [("core",), ("x",), ("y",), *far]


def fourth_joins(pages):
    return padded(ROWS_T + ROWS_U, pages) < padded(ROWS_T, pages) + padded(ROWS_U, pages)


def padded(rows, pages):
    unit = TILE * pages
    return (rows + unit - 1) // unit * unit


def position_table():
    half = D // 2
    channel = np.arange(half)
    inverse = np.exp((channel // 2).astype(np.float32) * np.float32(-2.0 * math.log(10000.0) / half))
    angle = (np.arange(SIDE, dtype=np.float32) + 1.0) * np.float32(2.0 * math.pi / SIDE)
    angle = angle[:, None] * inverse
    return np.where(channel % 2 == 0, np.sin(angle), np.cos(angle)).astype(np.float32)


def dot(a, b):
    return jnp.dot(a, b, preferred_element_type=f32)


def dot_nt(a, b):
    return lax.dot_general(a, b, (((1,), (1,)), ((), ())), preferred_element_type=f32)


def dot_tn(a, b):
    return lax.dot_general(a, b, (((0,), (0,)), ((), ())), preferred_element_type=f32)


def row_total(values):
    return jnp.sum(values.astype(f32), axis=0, keepdims=True)


def norm_forward(values):
    average = jnp.mean(values, axis=-1, keepdims=True)
    centred = values - average
    variance = jnp.mean(centred * centred, axis=-1, keepdims=True)
    rstd = lax.rsqrt(variance + norm_eps)
    return centred * rstd, rstd


def norm_backward(grad, normed, rstd, gain):
    grad_normed = grad * gain
    first = jnp.mean(grad_normed, axis=-1, keepdims=True)
    second = jnp.mean(grad_normed * normed, axis=-1, keepdims=True)
    grad_in = rstd * (grad_normed - first - normed * second)
    return grad_in, row_total(grad * normed), row_total(grad)


def spread_rows(rows):
    head = lax.broadcasted_iota(jnp.int32, (NP, D), 1) // HD
    return jnp.concatenate(
        [jnp.where(head == h, rows, 0.0) for h in range(HEADS)], axis=0
    ).astype(bf16)


def spread_cols(cols):
    head = lax.broadcasted_iota(jnp.int32, (D, NP), 0) // HD
    return jnp.concatenate(
        [jnp.where(head == h, cols, 0.0) for h in range(HEADS)], axis=1
    ).astype(bf16)


def own_heads(full):
    return jnp.concatenate(
        [full[HD * h : HD * h + HD, NP * h : NP * h + NP] for h in range(HEADS)], axis=0
    )


def project_heads(weight_t, sums):
    high = sums.astype(bf16)
    low = (sums - high.astype(f32)).astype(bf16)
    return own_heads(dot(weight_t, high) + dot(weight_t, low))


def own_blocks(pairs):
    parts = []
    for pair in pairs:
        parts += [pair[:HD, :NP], pair[HD:, NP:]]
    return jnp.concatenate(parts, axis=0)


def head_rows(row):
    return jnp.concatenate([row[:, NP * h : NP * h + NP] for h in range(HEADS)], axis=0)


def head_line(rows):
    return jnp.concatenate([rows[h : h + 1] for h in range(HEADS)], axis=1)


def per_channel(rows):
    return jnp.concatenate(
        [jnp.broadcast_to(rows[h : h + 1], (HD, NP)) for h in range(HEADS)], axis=0
    )


def head_sums(cols):
    return jnp.concatenate(
        [jnp.sum(cols[HD * h : HD * h + HD], axis=0, keepdims=True) for h in range(HEADS)], axis=0
    )


def pair_cols(p):
    return slice(PAIR * p, PAIR * p + PAIR)


def pair_rows(p):
    return slice(2 * HD * p, 2 * HD * p + 2 * HD)


class Place:
    def __init__(self, pages):
        self.axes = axes_of(pages)
        self.page = lax.axis_index("dp")
        self.member = lax.axis_index("blk")
        self.digit = {
            name: self.member if name == "x" else lax.rem(self.page // stride, radix)
            for name, (radix, stride) in self.axes.items()
        }

    def size(self, group):
        return math.prod(self.axes[name][0] for name in group)

    def index(self, group):
        index = 0
        for name in group:
            index = index * self.axes[name][0] + self.digit[name]
        return index

    def peer(self, group, hop):
        index = lax.rem(self.index(group) + hop, self.size(group))
        page, member, rest = self.page, self.member, index
        for name in reversed(group):
            radix, stride = self.axes[name]
            digit = lax.rem(rest, radix)
            rest = rest // radix
            if name == "x":
                member = digit
            else:
                page = page + (digit - self.digit[name]) * stride
        return (page, member), index


class PageSum:
    def __init__(self, place, groups, back, rows, landing, whole, sent, arrived):
        self.place, self.groups, self.back = place, groups, back
        self.rows, self.landing, self.whole = rows, landing, whole
        self.sent, self.arrived = sent, arrived
        self.slots = 0
        self.extents = [rows.shape[0]]
        self.bases = [0]
        self.landings = []
        at = 0
        for group in groups:
            size = place.size(group)
            extent = self.extents[-1] // size
            self.landings.append(at)
            at += (size - 1) * extent
            self.bases.append(pl.multiple_of(self.bases[-1] + place.index(group) * extent, TILE))
            self.extents.append(extent)
        last = len(groups)
        moves = [self.scatter_moves(s) for s in range(last)]
        near = {"all": 0, "across": 1, "sides": 2}[back]
        moves += [self.gather_moves(s) for s in range(last - 1, near - 1, -1)]
        if back == "sides":
            moves += [self.side_moves(), self.corner_moves(), self.core_moves()]
        elif back == "across":
            moves += [self.across_moves(), self.core_moves()]
        self.phases = [functools.partial(self.step, moves, k) for k in range(len(moves) + 1)]

    @staticmethod
    def landing_rows(pages, groups, rows):
        axes = axes_of(pages)
        total, extent = 0, rows
        for group in groups:
            size = math.prod(axes[name][0] for name in group)
            extent //= size
            total += (size - 1) * extent
        return total

    def step(self, moves, k):
        last = len(self.groups)
        if k > 0:
            for move in moves[k - 1]:
                self.copy(*move).wait()
        if 0 < k <= last:
            total = self.scatter_sum(k - 1)
            region = pl.ds(self.bases[k], self.extents[k])
            if k < last:
                self.rows[region] = total
            elif len(self.whole.shape) == 3:
                self.whole[self.place.member, region] = total
            else:
                self.whole[region] = total
        if k < len(moves):
            for move in moves[k]:
                self.copy(*move).start()

    def copy(self, slot, source, target, device):
        return pltpu.make_async_remote_copy(
            src_ref=source(),
            dst_ref=target(),
            send_sem=self.sent.at[slot],
            recv_sem=self.arrived.at[slot],
            device_id=device,
            device_id_type=pl.DeviceIdType.MESH,
        )

    def new_slot(self):
        self.slots += 1
        return self.slots - 1

    def same(self, device, view):
        return (self.new_slot(), view, view, device)

    def scatter_moves(self, step):
        group = self.groups[step]
        extent = self.extents[step + 1]
        moves = []
        for hop in range(1, self.place.size(group)):
            device, other = self.place.peer(group, hop)
            start = pl.multiple_of(self.bases[step] + other * extent, TILE)
            landing = self.landings[step] + (hop - 1) * extent
            moves.append(
                (
                    self.new_slot(),
                    functools.partial(self.part, self.rows, start, extent),
                    functools.partial(self.part, self.landing, landing, extent),
                    device,
                )
            )
        return moves

    @staticmethod
    def part(ref, start, extent):
        return ref.at[pl.ds(start, extent)]

    def half(self, member, start, extent):
        if len(self.whole.shape) == 3:
            return self.whole.at[member, pl.ds(start, extent)]
        return self.whole.at[pl.ds(start, extent)]

    def scatter_sum(self, step):
        extent = self.extents[step + 1]
        total = self.rows[pl.ds(self.bases[step + 1], extent)].astype(f32)
        for hop in range(1, self.place.size(self.groups[step])):
            landing = self.landings[step] + (hop - 1) * extent
            total = total + self.landing[pl.ds(landing, extent)].astype(f32)
        return total.astype(bf16)

    def gather_moves(self, step):
        group = self.groups[step]
        view = functools.partial(self.half, self.place.member, self.bases[step + 1], self.extents[step + 1])
        return [
            self.same(self.place.peer(group, hop)[0], view) for hop in range(1, self.place.size(group))
        ]

    def own_quarter(self):
        step = 2 if len(self.groups[0]) == 1 else 1
        return self.bases[step], self.extents[step]

    def side_moves(self):
        view = functools.partial(self.half, self.place.member, *self.own_quarter())
        return [self.same(self.place.peer((name,), 1)[0], view) for name in ("y", "x")]

    def corner_moves(self):
        base, extent = self.own_quarter()
        other = pl.multiple_of(base + (1 - 2 * self.place.digit["y"]) * extent, TILE)
        view = functools.partial(self.half, self.place.member, other, extent)
        return [self.same(self.place.peer(("x",), 1)[0], view)]

    def across_moves(self):
        view = functools.partial(self.half, self.place.member, *self.own_quarter())
        return [self.same(self.place.peer(("x", "y"), hop)[0], view) for hop in range(1, 4)]

    def core_moves(self):
        extent = self.extents[0] // 2
        start = pl.multiple_of(self.place.digit["core"] * extent, TILE)
        device, _ = self.place.peer(("core",), 1)
        return [self.same(device, functools.partial(self.half, m, start, extent)) for m in range(2)]


def clear_rest(ref, used):
    if ref.shape[0] > used:
        ref[used:] = jnp.zeros((ref.shape[0] - used, D), ref.dtype)


def layer_kernel(
    tokens,
    pages,
    queries_in,
    memory_hbm,
    turns_in,
    order_in,
    lengths_in,
    attn_in,
    attn_out,
    attn_bias,
    ffn_in_hbm,
    ffn_in_bias,
    ffn_out_hbm,
    ffn_out_bias,
    norm_gain,
    norm_bias,
    pos_in,
    out_grad_in,
    table_in,
    result_out,
    queries_grad_out,
    memory_grad_hbm,
    whole_f_hbm,
    whole_g_hbm,
    whole_t_hbm,
    whole_k_hbm,
    whole_u_hbm,
    memory_s,
    key_in_s,
    probs_s,
    grad_scores_s,
    code_s,
    query_kt,
    grad_vt,
    back_s,
    table_s,
    top_s,
    highest_s,
    shifts_s,
    factor_s,
    total_s,
    mixed_s,
    pad_s,
    send_a,
    recv_a,
    send_t,
    recv_t,
    send_b,
    recv_b,
    small_s,
    rows_f,
    landing_f,
    whole_f,
    rows_g,
    landing_g,
    whole_g,
    rows_t,
    landing_t,
    whole_t,
    rows_k,
    landing_k,
    whole_k,
    rows_u,
    landing_u,
    whole_u,
    load_sem,
    store_sem,
    link_sem,
    sent_f,
    arrived_f,
    sent_g,
    arrived_g,
    sent_t,
    arrived_t,
    sent_k,
    arrived_k,
    sent_u,
    arrived_u,
):
    member = lax.axis_index("blk")
    partner = (lax.axis_index("dp"), 1 - member)
    chunks = tokens // CHUNK

    place = Place(pages)
    groups_f, groups_t, groups_k = sum_groups(pages)
    sum_f = PageSum(place, groups_f, "sides", rows_f, landing_f, whole_f, sent_f, arrived_f)
    sum_g = PageSum(place, groups_f, "sides", rows_g, landing_g, whole_g, sent_g, arrived_g)
    sum_t = PageSum(place, groups_t, "across", rows_t, landing_t, whole_t, sent_t, arrived_t)
    sum_k = PageSum(place, groups_k, "all", rows_k, landing_k, whole_k, sent_k, arrived_k)
    joined = fourth_joins(pages)
    if joined:
        rows_u = rows_t.at[ROWS_T : ROWS_T + ROWS_U]
    else:
        sum_u = PageSum(place, groups_t, "across", rows_u, landing_u, whole_u, sent_u, arrived_u)

    barrier = pltpu.get_barrier_semaphore()
    peers = [
        place.peer(group, hop)[0]
        for group in [("x", "core", "y"), *far_axes(pages)]
        for hop in range(1, place.size(group))
    ]
    for peer in peers:
        pl.semaphore_signal(barrier, inc=1, device_id=peer, device_id_type=pl.DeviceIdType.MESH)

    load_memory = [
        pltpu.make_async_copy(
            memory_hbm.at[0, CHUNK * k : CHUNK * k + CHUNK],
            memory_s.at[CHUNK * k : CHUNK * k + CHUNK],
            store_sem.at[k],
        )
        for k in range(chunks)
    ]
    half = FF // 2
    ffn_in_s = [grad_scores_s.at[D * k : D * k + D] for k in range(2)]
    ffn_out_s = grad_scores_s.at[2 * D : 2 * D + FF, :D]
    free = 2 * D + FF
    active_s = [grad_scores_s.at[free + NP * k : free + NP * k + NP] for k in range(2)]
    slope_s = [grad_scores_s.at[free + NP * k : free + NP * k + NP] for k in range(2, 4)]
    load_ffn = [
        pltpu.make_async_copy(ffn_in_hbm.at[:, half * k : half * k + half], ffn_in_s[k], load_sem.at[k])
        for k in range(2)
    ]
    load_ffn.append(pltpu.make_async_copy(ffn_out_hbm, ffn_out_s, load_sem.at[2]))
    for load in load_memory + load_ffn:
        load.start()

    pairs = [attn_bias[j].astype(f32) for j in range(3)]
    bias = jnp.concatenate([pair[k : k + 1] for k in range(2) for pair in pairs], axis=0)
    gain = norm_gain[...].astype(f32)
    shift = norm_bias[...].astype(f32)

    order = order_in[...]
    turn = turns_in[0]
    row_at = order >> 7
    col_at = order & 127
    top = SIDE - 1
    row_new = jnp.where(
        turn == 0, row_at, jnp.where(turn == 1, col_at, jnp.where(turn == 2, top - row_at, top - col_at))
    )
    col_new = jnp.where(
        turn == 0, col_at, jnp.where(turn == 1, top - row_at, jnp.where(turn == 2, top - col_at, row_at))
    )
    past = jnp.where(order < lengths_in[0], 0, SIDE * SIDE)
    code_s[...] = (row_new * SIDE + col_new + past).astype(f32)

    pad_s[...] = jnp.zeros_like(pad_s)
    pad_s[0, :NQ] = queries_in[0].astype(f32)
    pad_s[1, :NQ] = pos_in[...].astype(f32)
    pad_s[2, :NQ] = out_grad_in[0].astype(f32)
    queries_f = pad_s[0]
    pos_f = pad_s[1]
    queries_b = queries_f.astype(bf16)
    mixed_q = (queries_f + pos_f).astype(bf16)
    query_self = (dot(mixed_q, attn_in[0, 0]) + bias[0:1]).astype(bf16)
    key_self = dot(mixed_q, attn_in[0, 1]).astype(bf16)
    value_self = (dot(queries_b, attn_in[0, 2]) + bias[1:2]).astype(bf16)
    scores = dot(key_self, spread_cols(query_self.astype(f32).T)) * scale
    own_key = lax.broadcasted_iota(jnp.int32, (NP, HQ), 0) < NQ
    scores = jnp.where(own_key, scores, masked_score)
    raised = jnp.exp(scores - jnp.max(scores, axis=0, keepdims=True))
    probs_self = raised / jnp.sum(raised, axis=0, keepdims=True)
    probs_self_b = probs_self.astype(bf16)
    value_t = value_self.astype(f32).T.astype(bf16)
    table = table_in[...]
    nothing = jnp.zeros((SIDE, D // 2), f32)
    table = jnp.concatenate(
        [jnp.concatenate([table, nothing], axis=1), jnp.concatenate([nothing, table], axis=1)], axis=0
    )
    table_high = table.astype(bf16)
    table_s[: 2 * SIDE] = table_high
    table_s[2 * SIDE :] = (table - table_high.astype(f32)).astype(bf16)

    def mask_view(i):
        side, place = i // (chunks // 2), lax.rem(i, chunks // 2)
        return grad_scores_s.at[
            pl.ds(pl.multiple_of(tokens // 2 + place * CHUNK, CHUNK), CHUNK),
            pl.ds(pl.multiple_of(side * NP, NP), NP),
        ]

    lane = lax.broadcasted_iota(jnp.int32, (CHUNK, NP), 1)

    def place_chunk(i):
        rows = pl.ds(pl.multiple_of(i * CHUNK, CHUNK), CHUNK)
        line = code_s[:, rows]
        code = jnp.concatenate(
            [
                jnp.broadcast_to(line[:, NP * j : NP * j + NP], (NP, NP)).T
                for j in range(CHUNK // NP)
            ],
            axis=0,
        ).astype(jnp.int32)
        row_hot = jnp.where(((code >> 7) & 127) == lane, 1.0, 0.0).astype(bf16)
        col_hot = jnp.where((code & 127) == lane, 1.0, 0.0).astype(bf16)
        hot = jnp.concatenate([row_hot, col_hot, row_hot, col_hot], axis=1)
        masked = jnp.where(code < SIDE * SIDE, 0.0, masked_score)
        mask_view(i)[...] = masked.astype(bf16)
        key_in_s[rows] = (memory_s[rows].astype(f32) + dot(hot, table_s[...])).astype(bf16)

    for load in load_memory[:4]:
        load.wait()
    attended = own_blocks(
        [dot(value_t[pair_rows(p)], probs_self_b[:, pair_cols(p)]) for p in range(4)]
    ).T.astype(bf16)
    place_chunk(0)
    first_normed, first_rstd = norm_forward(queries_f + dot(attended, attn_out[0]) + bias[2:3])
    place_chunk(1)
    first = first_normed * gain[0:1] + shift[0:1]
    cross_q = (first + pos_f).astype(bf16)
    query_c = (dot(cross_q, attn_in[1, 0]) + bias[3:4]).astype(bf16)
    place_chunk(2)
    query_k = dot(attn_in[1, 1], spread_cols(query_c.astype(f32).T))
    query_kt[...] = (query_k * (scale * log2e)).astype(bf16)
    place_chunk(3)
    for load in load_memory[4:]:
        load.wait()
    pl.loop(4, chunks)(place_chunk)

    def score_pair(p, key_in, mask, score_s):
        cols = pair_cols(p)
        part = dot(key_in, query_kt[:, cols]) + mask
        score_s[:, cols] = part
        top_s[:, cols] = jnp.max(part.reshape(CHUNK // 8, 8, PAIR), axis=0)

    def score_operands(i):
        rows = pl.ds(pl.multiple_of(i * CHUNK, CHUNK), CHUNK)
        mask = mask_view(i)[...].astype(f32)
        return key_in_s[rows], jnp.concatenate([mask, mask], axis=1)

    def attend_all(score_s):
        operands = score_operands(0)
        for p in range(4):
            score_pair(p, *operands, score_s)

        @pl.loop(0, chunks)
        def _(i):
            rows = pl.ds(pl.multiple_of(i * CHUNK, CHUNK), CHUNK)
            memory_ct = memory_s[rows].T
            operands = score_operands(jnp.minimum(i + 1, chunks - 1))
            for p in range(4):
                cols = pair_cols(p)
                before = highest_s[0:1, cols]
                highest = jnp.maximum(before, jnp.max(top_s[:, cols], axis=0, keepdims=True))
                highest_s[0:1, cols] = highest
                shifts_s[pl.ds(i, 1), cols] = highest
                fade = jnp.exp2(before - highest)
                raised = jnp.exp2(score_s[:, cols] - highest)
                sums = jnp.sum(raised.reshape(CHUNK // 8, 8, PAIR), axis=0)
                total_s[:, cols] = total_s[:, cols] * fade + sums
                probs_s[rows, cols] = raised.astype(bf16)
                mixed_s[:, cols] = mixed_s[:, cols] * fade + dot(memory_ct, probs_s[rows, cols])
                score_pair(p, *operands, score_s)

    highest_s[0:1] = jnp.full((1, HQ), -3e38, f32)
    total_s[...] = jnp.zeros_like(total_s)
    mixed_s[...] = jnp.zeros_like(mixed_s)
    pl.run_scoped(attend_all, pltpu.VMEM((CHUNK, HQ), f32))
    highest_own = highest_s[0:1]
    total_own = jnp.sum(total_s[...], axis=0, keepdims=True)

    value_wt = attn_in[1, 2].astype(f32).T.astype(bf16)
    key_wt = attn_in[1, 1].astype(f32).T.astype(bf16)
    send_a[...] = project_heads(value_wt, mixed_s[...]).astype(bf16)
    send_t[:HEADS] = head_rows(highest_own)
    send_t[HEADS:] = head_rows(total_own)
    pl.semaphore_wait(barrier, len(peers))
    swap_a = pltpu.make_async_remote_copy(
        src_ref=send_a,
        dst_ref=recv_a,
        send_sem=link_sem.at[0],
        recv_sem=link_sem.at[1],
        device_id=partner,
        device_id_type=pl.DeviceIdType.MESH,
    )
    swap_t = pltpu.make_async_remote_copy(
        src_ref=send_t,
        dst_ref=recv_t,
        send_sem=link_sem.at[4],
        recv_sem=link_sem.at[5],
        device_id=partner,
        device_id_type=pl.DeviceIdType.MESH,
    )
    swap_a.start()
    swap_t.start()
    swap_a.wait()
    swap_t.wait()
    is_first = member == 0
    own, other = send_a[...].astype(f32), recv_a[...].astype(f32)
    left = jnp.where(is_first, own, other)
    right = jnp.where(is_first, other, own)
    own, other = send_t[...], recv_t[...]
    left_t = jnp.where(is_first, own, other)
    right_t = jnp.where(is_first, other, own)
    highest = jnp.maximum(left_t[:HEADS], right_t[:HEADS])
    fade_l = jnp.exp2(left_t[:HEADS] - highest)
    fade_r = jnp.exp2(right_t[:HEADS] - highest)
    total = left_t[HEADS:] * fade_l + right_t[HEADS:] * fade_r
    mixed_t = left * per_channel(fade_l / total) + right * per_channel(fade_r / total)
    log_total = head_line(highest + jnp.log2(total))
    own_share = jnp.exp2(highest_own - log_total)
    factor_s[...] = jnp.exp2(shifts_s[...] - log_total)
    attended_c = (mixed_t.T + bias[4:5]).astype(bf16)

    second_normed, second_rstd = norm_forward(first + dot(attended_c, attn_out[1]) + bias[5:6])
    second = second_normed * gain[1:2] + shift[1:2]
    ffn_input = second.astype(bf16)
    load_ffn[0].wait()
    load_ffn[1].wait()
    blocks = [(j // 4, slice(D * j, D * j + D), slice(j % 4 * D, j % 4 * D + D)) for j in range(FF // D)]
    hidden_bias = ffn_in_bias[...].astype(f32).reshape(1, FF)
    def feed_forward(gate_s):
        for k, cols, part in blocks:
            hidden = dot(ffn_input, ffn_in_s[k][:, part]) + hidden_bias[:, cols]
            half_gate = 0.5 + 0.5 * lax.erf(hidden * math.sqrt(0.5))
            active_s[k][:, part] = (hidden * half_gate).astype(bf16)
            gate_s[:, cols] = half_gate + hidden * jnp.exp(hidden * hidden * -0.5) * (
                1.0 / math.sqrt(2.0 * math.pi)
            )
        load_ffn[2].wait()
        third_normed, third_rstd = norm_forward(
            second
            + dot(active_s[0][...], ffn_out_s[:half])
            + dot(active_s[1][...], ffn_out_s[half:])
            + ffn_out_bias[...].astype(f32).reshape(1, D)
        )
        result_out[...] = (third_normed * gain[2:3] + shift[2:3])[:NQ].astype(bf16)
        grad_third, gain_grad_2, shift_grad_2 = norm_backward(
            pad_s[2], third_normed, third_rstd, gain[2:3]
        )
        grad_branch_f = grad_third.astype(bf16)
        for k, cols, part in blocks:
            grad_hidden = dot_nt(grad_branch_f, ffn_out_s[cols]) * gate_s[:, cols]
            slope_s[k][:, part] = grad_hidden.astype(bf16)
        return grad_third, gain_grad_2, shift_grad_2, grad_branch_f

    grad_third, gain_grad_2, shift_grad_2, grad_branch_f = pl.run_scoped(
        feed_forward, pltpu.VMEM((NP, FF), f32)
    )
    grad_second = grad_third + dot_nt(slope_s[0][...], ffn_in_s[0][...])
    grad_second += dot_nt(slope_s[1][...], ffn_in_s[1][...])
    grad_second_in, gain_grad_1, shift_grad_1 = norm_backward(
        grad_second, second_normed, second_rstd, gain[1:2]
    )
    grad_branch_c = grad_second_in.astype(bf16)
    ffn_input_t = second.T.astype(bf16)

    def ffn_rows(target, k):
        @pl.when(member == 0)
        def _():
            for j in range(4):
                part = slice(D * j, D * j + D)
                target[part] = dot(ffn_input_t, slope_s[k][:, part]).astype(bf16)

        @pl.when(member == 1)
        def _():
            for j in range(4):
                part = slice(D * j, D * j + D)
                target[part] = dot_tn(active_s[k][:, part], grad_branch_f).astype(bf16)

    ffn_rows(rows_f, 0)
    sum_f.phases[0]()
    ffn_rows(rows_g, 1)

    is_first = member == 0
    clear_rest(rows_f, ROWS_F)
    clear_rest(rows_g, ROWS_F)
    clear_rest(rows_t, ROWS_T + (ROWS_U if joined else 0))
    clear_rest(rows_k, ROWS_K)
    if not joined:
        clear_rest(rows_u, ROWS_U)
    sum_g.phases[0]()
    grad_attended_c = dot_nt(grad_branch_c, attn_out[1]).astype(bf16).astype(f32)
    hidden_sums = [row_total(slope_s[k][:, part]) for k, _, part in blocks]

    grad_attended_t = grad_attended_c.T
    grad_v = dot(attn_in[1, 2], spread_cols(grad_attended_t))
    grad_vt[...] = grad_v.astype(bf16)
    inner = head_line(head_sums(grad_attended_t * mixed_t))
    shares = query_kt
    shares[...] = (mixed_s[...] * own_share).astype(bf16)
    mixed_s[...] = jnp.zeros_like(mixed_s)

    queue_f = [phase for pair in zip(sum_f.phases[1:], sum_g.phases[1:]) for phase in pair]
    queue_t = list(sum_t.phases)
    queue_k = list(sum_k.phases)
    queue_u = [] if joined else list(sum_u.phases)

    def take(queue):
        if queue:
            queue.pop(0)()

    def at(i, steps):
        for step, queue in steps:
            if queue:
                pl.when(i == (step * chunks) // 16)(queue.pop(0))

    @pl.loop(0, chunks)
    def _(i):
        rows = pl.ds(pl.multiple_of(i * CHUNK, CHUNK), CHUNK)
        key_ct = key_in_s[rows].T
        memory_c = memory_s[rows]
        for p in range(4):
            cols = pair_cols(p)
            grad_probs = dot(memory_c, grad_vt[:, cols])
            probs = probs_s[rows, cols].astype(f32) * factor_s[pl.ds(i, 1), cols]
            probs_s[rows, cols] = probs.astype(bf16)
            grad_scores_s[rows, cols] = (probs * (grad_probs - inner[:, cols])).astype(bf16)
            mixed_s[:, cols] += dot(key_ct, grad_scores_s[rows, cols])
        at(i, [(3, queue_f), (4, queue_f), (8, queue_f), (9, queue_f), (13, queue_f), (14, queue_f)])

    send_b[...] = (project_heads(key_wt, mixed_s[...]) * scale).astype(bf16)
    swap_b = pltpu.make_async_remote_copy(
        src_ref=send_b,
        dst_ref=recv_b,
        send_sem=link_sem.at[2],
        recv_sem=link_sem.at[3],
        device_id=partner,
        device_id_type=pl.DeviceIdType.MESH,
    )
    swap_b.start()
    query_x = spread_rows(query_c.astype(f32))
    grad_x = spread_rows(grad_attended_c)
    rows_k[:D] = (dot(mixed_s[...].astype(bf16), query_x) * scale).astype(bf16)
    rows_k[D : 2 * D] = dot(shares[...], grad_x).astype(bf16)
    out_grad_c = dot_tn(attended_c, grad_branch_c)
    rows_k[2 * D : 3 * D] = jnp.where(is_first, out_grad_c, 0.0).astype(bf16)
    take(queue_k)
    small_s[:16] = jnp.concatenate(
        hidden_sums
        + [
            row_total(grad_branch_f),
            row_total(grad_branch_c),
            gain_grad_2,
            shift_grad_2,
            gain_grad_1,
            shift_grad_1,
            row_total(grad_attended_c),
            jnp.zeros((1, D), f32),
        ],
        axis=0,
    )
    take(queue_f)
    take(queue_f)
    swap_b.wait()
    take(queue_k)
    grad_query_c = (send_b[...].astype(f32) + recv_b[...].astype(f32)).T.astype(bf16)

    cross_pos_grad = dot_nt(grad_query_c, attn_in[1, 0])
    grad_first_in, gain_grad_0, shift_grad_0 = norm_backward(
        grad_second_in + cross_pos_grad, first_normed, first_rstd, gain[0:1]
    )
    grad_branch = grad_first_in.astype(bf16)
    grad_attended = dot_nt(grad_branch, attn_out[0]).astype(bf16).astype(f32)

    @pl.when(member == 0)
    def _():
        rows_u[:ROWS_U] = dot_tn(cross_q, grad_query_c).astype(bf16)

    @pl.when(member == 1)
    def _():
        rows_u[:ROWS_U] = dot_tn(attended, grad_branch).astype(bf16)

    take(queue_u)
    take(queue_k)
    grad_probs = dot(value_self, spread_cols(grad_attended.T))
    inner_self = jnp.sum(probs_self * grad_probs, axis=0, keepdims=True)
    grad_scores = (probs_self * (grad_probs - inner_self)).astype(bf16)
    key_t = key_self.astype(f32).T.astype(bf16)
    grad_query_s = (
        own_blocks([dot(key_t[pair_rows(p)], grad_scores[:, pair_cols(p)]) for p in range(4)]) * scale
    ).T.astype(bf16)
    grad_key_s = (dot(grad_scores, spread_rows(query_self.astype(f32))) * scale).astype(bf16)
    grad_value_s = dot(probs_self_b, spread_rows(grad_attended)).astype(bf16)
    grad_mixed_q = dot_nt(grad_query_s, attn_in[0, 0]) + dot_nt(grad_key_s, attn_in[0, 1])
    small_s[16:] = jnp.concatenate(
        [
            row_total(grad_query_s),
            row_total(grad_value_s),
            row_total(grad_branch),
            row_total(grad_query_c),
            gain_grad_0,
            shift_grad_0,
            jnp.zeros((10, D), f32),
        ],
        axis=0,
    )
    @pl.when(member == 0)
    def _():
        rows_t[:D] = dot_tn(mixed_q, grad_query_s).astype(bf16)
        rows_t[D : 2 * D] = dot_tn(mixed_q, grad_key_s).astype(bf16)

    @pl.when(member == 1)
    def _():
        rows_t[:D] = dot_tn(queries_b, grad_value_s).astype(bf16)
        rows_t[ROW_POS:ROW_SMALL] = (grad_mixed_q + cross_pos_grad).astype(bf16)
        rows_t[ROW_SMALL : ROW_SMALL + 32] = small_s[...].astype(bf16)
        rows_t[ROW_SMALL + 32 : ROWS_T] = jnp.zeros((ROWS_T - ROW_SMALL - 32, D), bf16)

    take(queue_u)
    take(queue_t)
    take(queue_k)
    take(queue_f)
    take(queue_f)
    queries_grad_out[...] = (grad_first_in + grad_mixed_q + dot_nt(grad_value_s, attn_in[0, 2]))[
        :NQ
    ].astype(bf16)
    back_s[:HQ] = (dot_nt(query_x, attn_in[1, 1]) * scale).astype(bf16)
    back_s[HQ:] = dot_nt(grad_x, attn_in[1, 2]).astype(bf16)

    @pl.loop(0, chunks)
    def _(i):
        rows = pl.ds(pl.multiple_of(i * CHUNK, CHUNK), CHUNK)
        both = jnp.concatenate([grad_scores_s[rows], probs_s[rows]], axis=1)
        memory_s[rows] = dot(both, back_s[...]).astype(bf16)
        pltpu.make_async_copy(memory_s.at[rows], memory_grad_hbm.at[0, rows], store_sem.at[i]).start()
        at(
            i,
            [
                (1, queue_t),
                (2, queue_u),
                (3, queue_k),
                (5, queue_t),
                (6, queue_u),
                (7, queue_f),
                (8, queue_f),
                (9, queue_t),
                (10, queue_u),
                (11, queue_k),
                (13, queue_t),
                (14, queue_u),
                (15, queue_k),
            ],
        )

    stores = [
        pltpu.make_async_copy(whole, target, load_sem.at[3 + k])
        for k, (whole, target) in enumerate(
            (
                (whole_f, whole_f_hbm),
                (whole_g, whole_g_hbm),
                (whole_t, whole_t_hbm),
                (whole_k, whole_k_hbm),
                *([] if joined else [(whole_u, whole_u_hbm)]),
            )
        )
    ]
    while queue_f:
        take(queue_f)
    stores[0].start()
    stores[1].start()
    while queue_t or queue_k or queue_u:
        take(queue_t)
        take(queue_u)
        take(queue_k)
    for store in stores[2:]:
        store.start()

    @pl.loop(0, chunks)
    def _(i):
        rows = pl.ds(pl.multiple_of(i * CHUNK, CHUNK), CHUNK)
        pltpu.make_async_copy(memory_s.at[rows], memory_grad_hbm.at[0, rows], store_sem.at[i]).wait()

    for store in stores:
        store.wait()


def finish_kernel(
    joined,
    result_in,
    queries_grad_in,
    memory_grad_in,
    whole_f_hbm,
    whole_g_hbm,
    whole_t_hbm,
    whole_k_hbm,
    whole_u_hbm,
    result,
    queries_grad,
    memory_grad,
    attn_in_hbm,
    attn_out_hbm,
    attn_bias_grad,
    ffn_in_hbm,
    ffn_in_bias_grad,
    ffn_out_hbm,
    ffn_out_bias_grad,
    norm_gain_grad,
    norm_bias_grad,
    query_pos_grad,
    moved,
    whole_f,
    whole_g,
    whole_t,
    whole_k,
    whole_u,
    attn_in_grad,
    attn_out_grad,
    ffn_in_grad,
    ffn_out_grad,
    in_sem,
    out_sem,
    sum_sem,
    grad_sem,
):
    pieces = in_sem.shape[0]
    piece = moved.shape[0] // pieces

    def fetch(j):
        rows = pl.ds(piece * j, piece)
        return pltpu.make_async_copy(memory_grad_in.at[0, rows], moved.at[rows], in_sem.at[j])

    def write(j):
        rows = pl.ds(piece * j, piece)
        return pltpu.make_async_copy(moved.at[rows], memory_grad.at[0, rows], out_sem.at[j])

    sums = [(whole_f_hbm, whole_f), (whole_g_hbm, whole_g), (whole_t_hbm, whole_t), (whole_k_hbm, whole_k)]
    if not joined:
        sums.append((whole_u_hbm, whole_u))
    loads = [pltpu.make_async_copy(*pair, sum_sem.at[j]) for j, pair in enumerate(sums)]
    for load in loads:
        load.start()
    for j in range(pieces):
        fetch(j).start()
    blocks = FF // D
    stores = []

    def store(source, target):
        stores.append(pltpu.make_async_copy(source, target, grad_sem.at[len(stores)]))
        stores[-1].start()

    result[0] = result_in[...]
    queries_grad[0] = queries_grad_in[...]
    for load, whole, first in ((loads[0], whole_f, 0), (loads[1], whole_g, blocks // 2)):
        load.wait()
        for j in range(blocks // 2):
            at = slice(D * (first + j), D * (first + j) + D)
            ffn_out_grad[at] = whole[1, D * j : D * j + D].astype(f32)
        half = slice(D * first, D * first + FF // 2)
        store(ffn_out_grad.at[half], ffn_out_hbm.at[half])
        for j in range(blocks // 2):
            at = slice(D * (first + j), D * (first + j) + D)
            ffn_in_grad[:, at] = whole[0, D * j : D * j + D].astype(f32)
        store(ffn_in_grad.at[:, half], ffn_in_hbm.at[:, half])
    for load in loads[2:]:
        load.wait()
    fourth, at = (whole_t, ROWS_T) if joined else (whole_u, 0)
    for j in range(2):
        attn_in_grad[0, j] = whole_t[0, D * j : D * j + D].astype(f32)
    attn_in_grad[0, 2] = whole_t[1, :D].astype(f32)
    attn_in_grad[1, 0] = fourth[0, at : at + D].astype(f32)
    attn_in_grad[1, 1] = whole_k[:D].astype(f32)
    attn_in_grad[1, 2] = whole_k[D : 2 * D].astype(f32)
    store(attn_in_grad, attn_in_hbm)
    attn_out_grad[0] = fourth[1, at : at + D].astype(f32)
    attn_out_grad[1] = whole_k[2 * D : 3 * D].astype(f32)
    store(attn_out_grad, attn_out_hbm)
    for j in range(pieces):
        fetch(j).wait()
        write(j).start()
    query_pos_grad[...] = whole_t[1, ROW_POS:ROW_SMALL].astype(f32)[:NQ]
    small = whole_t[1, ROW_SMALL : ROW_SMALL + 32].astype(f32)
    ffn_in_bias_grad[...] = jnp.concatenate([small[j : j + 1] for j in range(blocks)], axis=1)
    ffn_out_bias_grad[...] = small[8:9]
    for j, (own, cross) in enumerate(((16, 19), (17, 14), (18, 9))):
        attn_bias_grad[j, 0:1] = small[own : own + 1]
        attn_bias_grad[j, 1:2] = small[cross : cross + 1]
    for j, (gain, shift) in enumerate(((20, 21), (12, 13), (10, 11))):
        norm_gain_grad[j : j + 1] = small[gain : gain + 1]
        norm_bias_grad[j : j + 1] = small[shift : shift + 1]
    for j in range(pieces):
        write(j).wait()
    for copy in stores:
        copy.wait()


def body(
    pages,
    queries,
    memory,
    quarter_turns,
    token_order,
    lengths,
    attn_in,
    attn_out,
    attn_bias,
    ffn_in,
    ffn_in_bias,
    ffn_out,
    ffn_out_bias,
    norm_gain,
    norm_bias,
    query_pos,
    out_grad,
):
    tokens = memory.shape[1]
    chunks = tokens // CHUNK
    groups_f, groups_t, groups_k = sum_groups(pages)
    joined = fourth_joins(pages)
    summed = [
        (padded(ROWS_F, pages), groups_f),
        (padded(ROWS_F, pages), groups_f),
        (padded(ROWS_T + (ROWS_U if joined else 0), pages), groups_t),
        (padded(ROWS_K, 2 * pages), groups_k),
        (TILE if joined else padded(ROWS_U, pages), groups_t),
    ]
    whole_shapes = [(rows, D) if groups is groups_k else (2, rows, D) for rows, groups in summed]
    sum_buffers = []
    for (rows, groups), shape in zip(summed, whole_shapes):
        landing = max(TILE, PageSum.landing_rows(pages, groups, rows))
        sum_buffers += [pltpu.VMEM(each, bf16) for each in ((rows, D), (landing, D), shape)]
    copies = 32
    vmem = pl.BlockSpec(memory_space=pltpu.VMEM)
    smem = pl.BlockSpec(memory_space=pltpu.SMEM)
    anywhere = pl.BlockSpec(memory_space=pl.ANY)
    parts = pl.pallas_call(
        functools.partial(layer_kernel, tokens, pages),
        out_shape=[
            jax.ShapeDtypeStruct((NQ, D), bf16),
            jax.ShapeDtypeStruct((NQ, D), bf16),
            jax.ShapeDtypeStruct((1, tokens, D), bf16),
            *(jax.ShapeDtypeStruct(shape, bf16) for shape in whole_shapes),
        ],
        in_specs=[
            vmem,
            anywhere,
            smem,
            vmem,
            smem,
            vmem,
            vmem,
            vmem,
            anywhere,
            vmem,
            anywhere,
            vmem,
            vmem,
            vmem,
            vmem,
            vmem,
            vmem,
        ],
        out_specs=[vmem, vmem] + [anywhere] * 6,
        scratch_shapes=[
            pltpu.VMEM((tokens, D), bf16),
            pltpu.VMEM((tokens, D), bf16),
            pltpu.VMEM((tokens, HQ), bf16),
            pltpu.VMEM((tokens, HQ), bf16),
            pltpu.VMEM((1, tokens), f32),
            pltpu.VMEM((D, HQ), bf16),
            pltpu.VMEM((D, HQ), bf16),
            pltpu.VMEM((2 * HQ, D), bf16),
            pltpu.VMEM((4 * SIDE, D), bf16),
            pltpu.VMEM((8, HQ), f32),
            pltpu.VMEM((8, HQ), f32),
            pltpu.VMEM((chunks, HQ), f32),
            pltpu.VMEM((chunks, HQ), f32),
            pltpu.VMEM((8, HQ), f32),
            pltpu.VMEM((D, HQ), f32),
            pltpu.VMEM((3, NP, D), f32),
            pltpu.VMEM((D, NP), bf16),
            pltpu.VMEM((D, NP), bf16),
            pltpu.VMEM((2 * HEADS, NP), f32),
            pltpu.VMEM((2 * HEADS, NP), f32),
            pltpu.VMEM((D, NP), bf16),
            pltpu.VMEM((D, NP), bf16),
            pltpu.VMEM((32, D), f32),
            *sum_buffers,
            pltpu.SemaphoreType.DMA((8,)),
            pltpu.SemaphoreType.DMA((chunks,)),
            pltpu.SemaphoreType.DMA((6,)),
            *[pltpu.SemaphoreType.DMA((copies,))] * 10,
        ],
        compiler_params=pltpu.CompilerParams(
            collective_id=0, has_side_effects=True, vmem_limit_bytes=127 * 512 * 1024
        ),
        cost_estimate=pl.CostEstimate(
            flops=2 * 8 * tokens * HQ * D, bytes_accessed=20 << 20, transcendentals=tokens * HQ
        ),
        name="decoder_layer",
    )(
        queries,
        memory,
        quarter_turns,
        token_order,
        lengths,
        attn_in,
        attn_out,
        attn_bias.transpose(1, 0, 2),
        ffn_in,
        ffn_in_bias,
        ffn_out,
        ffn_out_bias,
        norm_gain,
        norm_bias,
        query_pos,
        out_grad,
        jnp.asarray(position_table()),
    )
    outs = pl.pallas_call(
        functools.partial(finish_kernel, joined),
        out_shape=[
            jax.ShapeDtypeStruct((1, NQ, D), bf16),
            jax.ShapeDtypeStruct((1, NQ, D), bf16),
            jax.ShapeDtypeStruct((1, tokens, D), bf16),
            jax.ShapeDtypeStruct((2, 3, D, D), f32),
            jax.ShapeDtypeStruct((2, D, D), f32),
            jax.ShapeDtypeStruct((3, 2, D), f32),
            jax.ShapeDtypeStruct((D, FF), f32),
            jax.ShapeDtypeStruct((1, FF), f32),
            jax.ShapeDtypeStruct((FF, D), f32),
            jax.ShapeDtypeStruct((1, D), f32),
            jax.ShapeDtypeStruct((3, D), f32),
            jax.ShapeDtypeStruct((3, D), f32),
            jax.ShapeDtypeStruct((NQ, D), f32),
        ],
        in_specs=[vmem, vmem] + [anywhere] * 6,
        out_specs=[vmem, vmem, anywhere, anywhere, anywhere, vmem, anywhere, vmem, anywhere] + [vmem] * 4,
        scratch_shapes=[
            pltpu.VMEM((tokens, D), bf16),
            *(pltpu.VMEM(shape, bf16) for shape in whole_shapes),
            pltpu.VMEM((2, 3, D, D), f32),
            pltpu.VMEM((2, D, D), f32),
            pltpu.VMEM((D, FF), f32),
            pltpu.VMEM((FF, D), f32),
            pltpu.SemaphoreType.DMA((8,)),
            pltpu.SemaphoreType.DMA((8,)),
            pltpu.SemaphoreType.DMA((5,)),
            pltpu.SemaphoreType.DMA((6,)),
        ],
        compiler_params=pltpu.CompilerParams(vmem_limit_bytes=62 * 1024 * 1024),
        name="write_outputs",
    )(*parts)
    return (
        *outs[:5],
        outs[5].transpose(1, 0, 2),
        outs[6],
        outs[7].reshape(FF),
        outs[8],
        outs[9].reshape(D),
        *outs[10:],
    )


def solution(mesh):
    in_specs = (
        P("dp", None, None),
        P("dp", "blk", None),
        P("dp"),
        P("dp", "blk"),
        P("dp"),
        P(),
        P(),
        P(),
        P(),
        P(),
        P(),
        P(),
        P(),
        P(),
        P(),
        P("dp", None, None),
    )
    out_specs = (
        P("dp", None, None),
        P("dp", None, None),
        P("dp", "blk", None),
        P(),
        P(),
        P(),
        P(),
        P(),
        P(),
        P(),
        P(),
        P(),
        P(),
    )
    layer = functools.partial(body, mesh.shape["dp"])
    return jax.shard_map(layer, mesh=mesh, in_specs=in_specs, out_specs=out_specs, check_vma=False)
```

```python
import functools
import math

import jax
import jax.numpy as jnp
import numpy as np
from jax import lax
from jax.experimental import pallas as pl
from jax.experimental.pallas import tpu as pltpu
from jax.sharding import PartitionSpec as P

D = 256
HEADS = 8
HD = D // HEADS
SIDE = 128
NQ = 125
NP = 128
HQ = HEADS * NP
PAIR = 2 * NP
FF = 2048
CHUNK = 1024

masked_score = -1e30
norm_eps = 1e-05
scale = 1.0 / math.sqrt(HD)
log2e = math.log2(math.e)

bf16 = jnp.bfloat16
f32 = jnp.float32

ROWS_F = FF // 2
ROW_POS = D
ROW_SMALL = D + NP
ROWS_T = 2 * D
ROWS_K = 3 * D
ROWS_U = D
TILE = 16


def axes_of(pages):
    axes = {"core": (2, 1), "y": (2, 2)}
    stride = 4
    while stride < pages:
        radix = 4 if pages // stride % 4 == 0 else 2
        axes["z%d" % (len(axes) - 2)] = (radix, stride)
        stride *= radix
    axes["x"] = (2, 0)
    return axes


def far_axes(pages):
    return [(name,) for name in axes_of(pages) if name.startswith("z")]


def sum_groups(pages):
    far = far_axes(pages)
    return [("core",), ("y",), *far], [("core", "y"), *far], [("core",), ("x",), ("y",), *far]


def fourth_joins(pages):
    return padded(ROWS_T + ROWS_U, pages) <= padded(ROWS_T, pages) + padded(ROWS_U, pages)


def padded(rows, pages):
    unit = TILE * pages
    return (rows + unit - 1) // unit * unit


def position_table():
    half = D // 2
    channel = np.arange(half)
    inverse = np.exp((channel // 2).astype(np.float32) * np.float32(-2.0 * math.log(10000.0) / half))
    angle = (np.arange(SIDE, dtype=np.float32) + 1.0) * np.float32(2.0 * math.pi / SIDE)
    angle = angle[:, None] * inverse
    return np.where(channel % 2 == 0, np.sin(angle), np.cos(angle)).astype(np.float32)


def dot(a, b):
    return jnp.dot(a, b, preferred_element_type=f32)


def dot_nt(a, b):
    return lax.dot_general(a, b, (((1,), (1,)), ((), ())), preferred_element_type=f32)


def dot_tn(a, b):
    return lax.dot_general(a, b, (((0,), (0,)), ((), ())), preferred_element_type=f32)


def row_total(values):
    return jnp.sum(values.astype(f32), axis=0, keepdims=True)


def norm_forward(values):
    average = jnp.mean(values, axis=-1, keepdims=True)
    centred = values - average
    variance = jnp.mean(centred * centred, axis=-1, keepdims=True)
    rstd = lax.rsqrt(variance + norm_eps)
    return centred * rstd, rstd


def norm_backward(grad, normed, rstd, gain):
    grad_normed = grad * gain
    first = jnp.mean(grad_normed, axis=-1, keepdims=True)
    second = jnp.mean(grad_normed * normed, axis=-1, keepdims=True)
    grad_in = rstd * (grad_normed - first - normed * second)
    return grad_in, row_total(grad * normed), row_total(grad)


def spread_rows(rows):
    head = lax.broadcasted_iota(jnp.int32, (NP, D), 1) // HD
    return jnp.concatenate(
        [jnp.where(head == h, rows, 0.0) for h in range(HEADS)], axis=0
    ).astype(bf16)


def spread_cols(cols):
    head = lax.broadcasted_iota(jnp.int32, (D, NP), 0) // HD
    return jnp.concatenate(
        [jnp.where(head == h, cols, 0.0) for h in range(HEADS)], axis=1
    ).astype(bf16)


def own_heads(full):
    return jnp.concatenate(
        [full[HD * h : HD * h + HD, NP * h : NP * h + NP] for h in range(HEADS)], axis=0
    )


def project_heads(weight_t, sums):
    high = sums.astype(bf16)
    low = (sums - high.astype(f32)).astype(bf16)
    return own_heads(dot(weight_t, high) + dot(weight_t, low))


def own_blocks(pairs):
    parts = []
    for pair in pairs:
        parts += [pair[:HD, :NP], pair[HD:, NP:]]
    return jnp.concatenate(parts, axis=0)


def head_rows(row):
    return jnp.concatenate([row[:, NP * h : NP * h + NP] for h in range(HEADS)], axis=0)


def head_line(rows):
    return jnp.concatenate([rows[h : h + 1] for h in range(HEADS)], axis=1)


def per_channel(rows):
    return jnp.concatenate(
        [jnp.broadcast_to(rows[h : h + 1], (HD, NP)) for h in range(HEADS)], axis=0
    )


def head_sums(cols):
    return jnp.concatenate(
        [jnp.sum(cols[HD * h : HD * h + HD], axis=0, keepdims=True) for h in range(HEADS)], axis=0
    )


def pair_cols(p):
    return slice(PAIR * p, PAIR * p + PAIR)


def pair_rows(p):
    return slice(2 * HD * p, 2 * HD * p + 2 * HD)


class Place:
    def __init__(self, pages):
        self.axes = axes_of(pages)
        self.page = lax.axis_index("dp")
        self.member = lax.axis_index("blk")
        self.digit = {
            name: self.member if name == "x" else lax.rem(self.page // stride, radix)
            for name, (radix, stride) in self.axes.items()
        }

    def size(self, group):
        return math.prod(self.axes[name][0] for name in group)

    def index(self, group):
        index = 0
        for name in group:
            index = index * self.axes[name][0] + self.digit[name]
        return index

    def peer(self, group, hop):
        index = lax.rem(self.index(group) + hop, self.size(group))
        page, member, rest = self.page, self.member, index
        for name in reversed(group):
            radix, stride = self.axes[name]
            digit = lax.rem(rest, radix)
            rest = rest // radix
            if name == "x":
                member = digit
            else:
                page = page + (digit - self.digit[name]) * stride
        return (page, member), index


class PageSum:
    def __init__(self, place, groups, back, rows, landing, whole, sent, arrived):
        self.place, self.groups, self.back = place, groups, back
        self.rows, self.landing, self.whole = rows, landing, whole
        self.sent, self.arrived = sent, arrived
        self.slots = 0
        self.extents = [rows.shape[0]]
        self.bases = [0]
        self.landings = []
        at = 0
        for group in groups:
            size = place.size(group)
            extent = self.extents[-1] // size
            self.landings.append(at)
            at += (size - 1) * extent
            self.bases.append(pl.multiple_of(self.bases[-1] + place.index(group) * extent, TILE))
            self.extents.append(extent)
        last = len(groups)
        moves = [self.scatter_moves(s) for s in range(last)]
        near = {"all": 0, "across": 1, "sides": 2}[back]
        moves += [self.gather_moves(s) for s in range(last - 1, near - 1, -1)]
        if back == "sides":
            moves += [self.side_moves(), self.corner_moves(), self.core_moves()]
        elif back == "across":
            moves += [self.across_moves(), self.core_moves()]
        self.phases = [functools.partial(self.step, moves, k) for k in range(len(moves) + 1)]

    @staticmethod
    def landing_rows(pages, groups, rows):
        axes = axes_of(pages)
        total, extent = 0, rows
        for group in groups:
            size = math.prod(axes[name][0] for name in group)
            extent //= size
            total += (size - 1) * extent
        return total

    def step(self, moves, k):
        last = len(self.groups)
        if k > 0:
            for move in moves[k - 1]:
                self.copy(*move).wait()
        if 0 < k <= last:
            if k < last:
                target = self.rows
            else:
                target = self.whole.at[self.place.member] if len(self.whole.shape) == 3 else self.whole
            self.scatter_sum(k - 1, target)
        if k < len(moves):
            for move in moves[k]:
                self.copy(*move).start()

    def copy(self, slot, source, target, device):
        return pltpu.make_async_remote_copy(
            src_ref=source(),
            dst_ref=target(),
            send_sem=self.sent.at[slot],
            recv_sem=self.arrived.at[slot],
            device_id=device,
            device_id_type=pl.DeviceIdType.MESH,
        )

    def new_slot(self):
        self.slots += 1
        return self.slots - 1

    def same(self, device, view):
        return (self.new_slot(), view, view, device)

    def scatter_moves(self, step):
        group = self.groups[step]
        extent = self.extents[step + 1]
        moves = []
        for hop in range(1, self.place.size(group)):
            device, other = self.place.peer(group, hop)
            start = pl.multiple_of(self.bases[step] + other * extent, TILE)
            landing = self.landings[step] + (hop - 1) * extent
            moves.append(
                (
                    self.new_slot(),
                    functools.partial(self.part, self.rows, start, extent),
                    functools.partial(self.part, self.landing, landing, extent),
                    device,
                )
            )
        return moves

    @staticmethod
    def part(ref, start, extent):
        return ref.at[pl.ds(start, extent)]

    def half(self, member, start, extent):
        if len(self.whole.shape) == 3:
            return self.whole.at[member, pl.ds(start, extent)]
        return self.whole.at[pl.ds(start, extent)]

    def scatter_sum(self, step, target):
        extent = self.extents[step + 1]
        block = math.gcd(extent, 64)

        def add(i):
            start = pl.multiple_of(i * block, block)
            own = pl.ds(pl.multiple_of(self.bases[step + 1] + start, TILE), block)
            total = self.rows[own].astype(f32)
            for hop in range(1, self.place.size(self.groups[step])):
                landing = self.landings[step] + (hop - 1) * extent
                total = total + self.landing[pl.ds(landing + start, block)].astype(f32)
            target[own] = total.astype(bf16)

        if extent == block:
            add(0)
        else:
            pl.loop(0, extent // block)(add)

    def gather_moves(self, step):
        group = self.groups[step]
        view = functools.partial(self.half, self.place.member, self.bases[step + 1], self.extents[step + 1])
        return [
            self.same(self.place.peer(group, hop)[0], view) for hop in range(1, self.place.size(group))
        ]

    def own_quarter(self):
        step = 2 if len(self.groups[0]) == 1 else 1
        return self.bases[step], self.extents[step]

    def side_moves(self):
        view = functools.partial(self.half, self.place.member, *self.own_quarter())
        return [self.same(self.place.peer((name,), 1)[0], view) for name in ("y", "x")]

    def corner_moves(self):
        base, extent = self.own_quarter()
        other = pl.multiple_of(base + (1 - 2 * self.place.digit["y"]) * extent, TILE)
        view = functools.partial(self.half, self.place.member, other, extent)
        return [self.same(self.place.peer(("x",), 1)[0], view)]

    def across_moves(self):
        view = functools.partial(self.half, self.place.member, *self.own_quarter())
        return [self.same(self.place.peer(("x", "y"), hop)[0], view) for hop in range(1, 4)]

    def core_moves(self):
        extent = self.extents[0] // 2
        start = pl.multiple_of(self.place.digit["core"] * extent, TILE)
        device, _ = self.place.peer(("core",), 1)
        return [self.same(device, functools.partial(self.half, m, start, extent)) for m in range(2)]


def clear_rest(ref, used):
    if ref.shape[0] > used:
        ref[used:] = jnp.zeros((ref.shape[0] - used, D), ref.dtype)


def layer_kernel(
    tokens,
    pages,
    queries_in,
    memory_hbm,
    turns_in,
    order_in,
    lengths_in,
    attn_in,
    attn_out,
    attn_bias,
    ffn_in_hbm,
    ffn_in_bias,
    ffn_out_hbm,
    ffn_out_bias,
    norm_gain,
    norm_bias,
    pos_in,
    out_grad_in,
    table_in,
    result_out,
    queries_grad_out,
    memory_grad_hbm,
    whole_f_hbm,
    whole_g_hbm,
    whole_t_hbm,
    whole_k_hbm,
    whole_u_hbm,
    memory_s,
    key_in_s,
    probs_s,
    grad_scores_s,
    code_s,
    query_kt,
    grad_vt,
    back_s,
    table_s,
    top_s,
    highest_s,
    shifts_s,
    factor_s,
    total_s,
    mixed_s,
    pad_s,
    send_a,
    recv_a,
    send_t,
    recv_t,
    send_b,
    recv_b,
    small_s,
    rows_f,
    landing_f,
    whole_f,
    rows_g,
    landing_g,
    whole_g,
    rows_t,
    landing_t,
    whole_t,
    rows_k,
    landing_k,
    whole_k,
    rows_u,
    landing_u,
    whole_u,
    load_sem,
    store_sem,
    link_sem,
    sent_f,
    arrived_f,
    sent_g,
    arrived_g,
    sent_t,
    arrived_t,
    sent_k,
    arrived_k,
    sent_u,
    arrived_u,
):
    member = lax.axis_index("blk")
    partner = (lax.axis_index("dp"), 1 - member)
    chunks = tokens // CHUNK

    place = Place(pages)
    groups_f, groups_t, groups_k = sum_groups(pages)
    sum_f = PageSum(place, groups_f, "sides", rows_f, landing_f, whole_f, sent_f, arrived_f)
    sum_g = PageSum(place, groups_f, "sides", rows_g, landing_g, whole_g, sent_g, arrived_g)
    sum_t = PageSum(place, groups_t, "across", rows_t, landing_t, whole_t, sent_t, arrived_t)
    sum_k = PageSum(place, groups_k, "all", rows_k, landing_k, whole_k, sent_k, arrived_k)
    joined = fourth_joins(pages)
    if joined:
        rows_u = rows_t.at[ROWS_T : ROWS_T + ROWS_U]
    else:
        sum_u = PageSum(place, groups_t, "across", rows_u, landing_u, whole_u, sent_u, arrived_u)

    barrier = pltpu.get_barrier_semaphore()
    peers = [
        place.peer(group, hop)[0]
        for group in [("x", "core", "y"), *far_axes(pages)]
        for hop in range(1, place.size(group))
    ]
    for peer in peers:
        pl.semaphore_signal(barrier, inc=1, device_id=peer, device_id_type=pl.DeviceIdType.MESH)

    def load_memory(i):
        rows = pl.ds(pl.multiple_of(i * CHUNK, CHUNK), CHUNK)
        return pltpu.make_async_copy(memory_hbm.at[0, rows], memory_s.at[rows], store_sem.at[i])

    half = FF // 2
    ffn_in_s = [grad_scores_s.at[D * k : D * k + D] for k in range(2)]
    ffn_out_s = grad_scores_s.at[2 * D : 2 * D + FF, :D]
    free = 2 * D + FF
    active_s = [grad_scores_s.at[free + NP * k : free + NP * k + NP] for k in range(2)]
    slope_s = [grad_scores_s.at[free + NP * k : free + NP * k + NP] for k in range(2, 4)]
    load_ffn = [
        pltpu.make_async_copy(ffn_in_hbm.at[:, half * k : half * k + half], ffn_in_s[k], load_sem.at[k])
        for k in range(2)
    ]
    load_ffn.append(pltpu.make_async_copy(ffn_out_hbm, ffn_out_s, load_sem.at[2]))
    for k in range(chunks):
        load_memory(k).start()
    for load in load_ffn:
        load.start()

    pairs = [attn_bias[j].astype(f32) for j in range(3)]
    bias = jnp.concatenate([pair[k : k + 1] for k in range(2) for pair in pairs], axis=0)
    gain = norm_gain[...].astype(f32)
    shift = norm_bias[...].astype(f32)

    order = order_in[...]
    turn = turns_in[0]
    row_at = order >> 7
    col_at = order & 127
    top = SIDE - 1
    row_new = jnp.where(
        turn == 0, row_at, jnp.where(turn == 1, col_at, jnp.where(turn == 2, top - row_at, top - col_at))
    )
    col_new = jnp.where(
        turn == 0, col_at, jnp.where(turn == 1, top - row_at, jnp.where(turn == 2, top - col_at, row_at))
    )
    past = jnp.where(order < lengths_in[0], 0, SIDE * SIDE)
    code_s[...] = (row_new * SIDE + col_new + past).astype(f32)

    pad_s[...] = jnp.zeros_like(pad_s)
    pad_s[0, :NQ] = queries_in[0].astype(f32)
    pad_s[1, :NQ] = pos_in[...].astype(f32)
    pad_s[2, :NQ] = out_grad_in[0].astype(f32)
    queries_f = pad_s[0]
    pos_f = pad_s[1]
    queries_b = queries_f.astype(bf16)
    mixed_q = (queries_f + pos_f).astype(bf16)
    query_self = (dot(mixed_q, attn_in[0, 0]) + bias[0:1]).astype(bf16)
    key_self = dot(mixed_q, attn_in[0, 1]).astype(bf16)
    value_self = (dot(queries_b, attn_in[0, 2]) + bias[1:2]).astype(bf16)
    scores = dot(key_self, spread_cols(query_self.astype(f32).T)) * scale
    own_key = lax.broadcasted_iota(jnp.int32, (NP, HQ), 0) < NQ
    scores = jnp.where(own_key, scores, masked_score)
    raised = jnp.exp(scores - jnp.max(scores, axis=0, keepdims=True))
    probs_self = raised / jnp.sum(raised, axis=0, keepdims=True)
    probs_self_b = probs_self.astype(bf16)
    value_t = value_self.astype(f32).T.astype(bf16)
    table = table_in[...]
    nothing = jnp.zeros((SIDE, D // 2), f32)
    table = jnp.concatenate(
        [jnp.concatenate([table, nothing], axis=1), jnp.concatenate([nothing, table], axis=1)], axis=0
    )
    table_high = table.astype(bf16)
    table_s[: 2 * SIDE] = table_high
    table_s[2 * SIDE :] = (table - table_high.astype(f32)).astype(bf16)

    def mask_view(i):
        side, place = i // (chunks // 2), lax.rem(i, chunks // 2)
        return grad_scores_s.at[
            pl.ds(pl.multiple_of(tokens // 2 + place * CHUNK, CHUNK), CHUNK),
            pl.ds(pl.multiple_of(side * NP, NP), NP),
        ]

    lane = lax.broadcasted_iota(jnp.int32, (CHUNK, NP), 1)

    def place_chunk(i):
        rows = pl.ds(pl.multiple_of(i * CHUNK, CHUNK), CHUNK)
        line = code_s[:, rows]
        code = jnp.concatenate(
            [
                jnp.broadcast_to(line[:, NP * j : NP * j + NP], (NP, NP)).T
                for j in range(CHUNK // NP)
            ],
            axis=0,
        ).astype(jnp.int32)
        row_hot = jnp.where(((code >> 7) & 127) == lane, 1.0, 0.0).astype(bf16)
        col_hot = jnp.where((code & 127) == lane, 1.0, 0.0).astype(bf16)
        hot = jnp.concatenate([row_hot, col_hot, row_hot, col_hot], axis=1)
        masked = jnp.where(code < SIDE * SIDE, 0.0, masked_score)
        mask_view(i)[...] = masked.astype(bf16)
        load_memory(i).wait()
        key_in_s[rows] = (memory_s[rows].astype(f32) + dot(hot, table_s[...])).astype(bf16)

    attended = own_blocks(
        [dot(value_t[pair_rows(p)], probs_self_b[:, pair_cols(p)]) for p in range(4)]
    ).T.astype(bf16)
    first_normed, first_rstd = norm_forward(queries_f + dot(attended, attn_out[0]) + bias[2:3])
    first = first_normed * gain[0:1] + shift[0:1]
    cross_q = (first + pos_f).astype(bf16)
    query_c = (dot(cross_q, attn_in[1, 0]) + bias[3:4]).astype(bf16)
    query_k = dot(attn_in[1, 1], spread_cols(query_c.astype(f32).T))
    query_kt[...] = (query_k * (scale * log2e)).astype(bf16)
    pl.loop(0, chunks)(place_chunk)

    def score_pair(p, key_in, mask, score_s):
        cols = pair_cols(p)
        part = dot(key_in, query_kt[:, cols]) + mask
        score_s[:, cols] = part
        top_s[:, cols] = jnp.max(part.reshape(CHUNK // 8, 8, PAIR), axis=0)

    def score_operands(i):
        rows = pl.ds(pl.multiple_of(i * CHUNK, CHUNK), CHUNK)
        mask = mask_view(i)[...].astype(f32)
        return key_in_s[rows], jnp.concatenate([mask, mask], axis=1)

    def attend_all(score_s):
        operands = score_operands(0)
        for p in range(4):
            score_pair(p, *operands, score_s)

        @pl.loop(0, chunks)
        def _(i):
            rows = pl.ds(pl.multiple_of(i * CHUNK, CHUNK), CHUNK)
            memory_ct = memory_s[rows].T
            operands = score_operands(jnp.minimum(i + 1, chunks - 1))
            for p in range(4):
                cols = pair_cols(p)
                before = highest_s[0:1, cols]
                highest = jnp.maximum(before, jnp.max(top_s[:, cols], axis=0, keepdims=True))
                highest_s[0:1, cols] = highest
                shifts_s[pl.ds(i, 1), cols] = highest
                fade = jnp.exp2(before - highest)
                raised = jnp.exp2(score_s[:, cols] - highest)
                sums = jnp.sum(raised.reshape(CHUNK // 8, 8, PAIR), axis=0)
                total_s[:, cols] = total_s[:, cols] * fade + sums
                probs_s[rows, cols] = raised.astype(bf16)
                mixed_s[:, cols] = mixed_s[:, cols] * fade + dot(memory_ct, probs_s[rows, cols])
                score_pair(p, *operands, score_s)

    highest_s[0:1] = jnp.full((1, HQ), -3e38, f32)
    total_s[...] = jnp.zeros_like(total_s)
    mixed_s[...] = jnp.zeros_like(mixed_s)
    pl.run_scoped(attend_all, pltpu.VMEM((CHUNK, HQ), f32))
    highest_own = highest_s[0:1]
    total_own = jnp.sum(total_s[...], axis=0, keepdims=True)

    value_wt = attn_in[1, 2].astype(f32).T.astype(bf16)
    key_wt = attn_in[1, 1].astype(f32).T.astype(bf16)
    send_a[...] = project_heads(value_wt, mixed_s[...]).astype(bf16)
    send_t[:HEADS] = head_rows(highest_own)
    send_t[HEADS:] = head_rows(total_own)
    pl.semaphore_wait(barrier, len(peers))
    swap_a = pltpu.make_async_remote_copy(
        src_ref=send_a,
        dst_ref=recv_a,
        send_sem=link_sem.at[0],
        recv_sem=link_sem.at[1],
        device_id=partner,
        device_id_type=pl.DeviceIdType.MESH,
    )
    swap_t = pltpu.make_async_remote_copy(
        src_ref=send_t,
        dst_ref=recv_t,
        send_sem=link_sem.at[4],
        recv_sem=link_sem.at[5],
        device_id=partner,
        device_id_type=pl.DeviceIdType.MESH,
    )
    swap_a.start()
    swap_t.start()
    swap_a.wait()
    swap_t.wait()
    is_first = member == 0
    own, other = send_a[...].astype(f32), recv_a[...].astype(f32)
    left = jnp.where(is_first, own, other)
    right = jnp.where(is_first, other, own)
    own, other = send_t[...], recv_t[...]
    left_t = jnp.where(is_first, own, other)
    right_t = jnp.where(is_first, other, own)
    highest = jnp.maximum(left_t[:HEADS], right_t[:HEADS])
    fade_l = jnp.exp2(left_t[:HEADS] - highest)
    fade_r = jnp.exp2(right_t[:HEADS] - highest)
    total = left_t[HEADS:] * fade_l + right_t[HEADS:] * fade_r
    mixed_t = left * per_channel(fade_l / total) + right * per_channel(fade_r / total)
    log_total = head_line(highest + jnp.log2(total))
    own_share = jnp.exp2(highest_own - log_total)
    factor_s[...] = jnp.exp2(shifts_s[...] - log_total)
    attended_c = (mixed_t.T + bias[4:5]).astype(bf16)

    second_normed, second_rstd = norm_forward(first + dot(attended_c, attn_out[1]) + bias[5:6])
    second = second_normed * gain[1:2] + shift[1:2]
    ffn_input = second.astype(bf16)
    load_ffn[0].wait()
    load_ffn[1].wait()
    blocks = [(j // 4, slice(D * j, D * j + D), slice(j % 4 * D, j % 4 * D + D)) for j in range(FF // D)]
    hidden_bias = ffn_in_bias[...].astype(f32).reshape(1, FF)
    def feed_forward(gate_s):
        for k, cols, part in blocks:
            hidden = dot(ffn_input, ffn_in_s[k][:, part]) + hidden_bias[:, cols]
            half_gate = 0.5 + 0.5 * lax.erf(hidden * math.sqrt(0.5))
            active_s[k][:, part] = (hidden * half_gate).astype(bf16)
            gate_s[:, cols] = half_gate + hidden * jnp.exp(hidden * hidden * -0.5) * (
                1.0 / math.sqrt(2.0 * math.pi)
            )
        load_ffn[2].wait()
        third_normed, third_rstd = norm_forward(
            second
            + dot(active_s[0][...], ffn_out_s[:half])
            + dot(active_s[1][...], ffn_out_s[half:])
            + ffn_out_bias[...].astype(f32).reshape(1, D)
        )
        result_out[...] = (third_normed * gain[2:3] + shift[2:3])[:NQ].astype(bf16)
        grad_third, gain_grad_2, shift_grad_2 = norm_backward(
            pad_s[2], third_normed, third_rstd, gain[2:3]
        )
        grad_branch_f = grad_third.astype(bf16)
        for k, cols, part in blocks:
            grad_hidden = dot_nt(grad_branch_f, ffn_out_s[cols]) * gate_s[:, cols]
            slope_s[k][:, part] = grad_hidden.astype(bf16)
        return grad_third, gain_grad_2, shift_grad_2, grad_branch_f

    grad_third, gain_grad_2, shift_grad_2, grad_branch_f = pl.run_scoped(
        feed_forward, pltpu.VMEM((NP, FF), f32)
    )
    grad_second = grad_third + dot_nt(slope_s[0][...], ffn_in_s[0][...])
    grad_second += dot_nt(slope_s[1][...], ffn_in_s[1][...])
    grad_second_in, gain_grad_1, shift_grad_1 = norm_backward(
        grad_second, second_normed, second_rstd, gain[1:2]
    )
    grad_branch_c = grad_second_in.astype(bf16)
    ffn_input_t = second.T.astype(bf16)

    def ffn_rows(target, k):
        @pl.when(member == 0)
        def _():
            @pl.loop(0, FF // D // 2)
            def _(j):
                part = pl.ds(pl.multiple_of(D * j, D), D)
                target[part] = dot(ffn_input_t, slope_s[k][:, part]).astype(bf16)

        @pl.when(member == 1)
        def _():
            @pl.loop(0, FF // D // 2)
            def _(j):
                part = pl.ds(pl.multiple_of(D * j, D), D)
                target[part] = dot_tn(active_s[k][:, part], grad_branch_f).astype(bf16)

    ffn_rows(rows_f, 0)
    sum_f.phases[0]()
    ffn_rows(rows_g, 1)

    is_first = member == 0
    clear_rest(rows_f, ROWS_F)
    clear_rest(rows_g, ROWS_F)
    clear_rest(rows_t, ROWS_T + (ROWS_U if joined else 0))
    clear_rest(rows_k, ROWS_K)
    if not joined:
        clear_rest(rows_u, ROWS_U)
    sum_g.phases[0]()
    grad_attended_c = dot_nt(grad_branch_c, attn_out[1]).astype(bf16).astype(f32)
    hidden_sums = [row_total(slope_s[k][:, part]) for k, _, part in blocks]

    grad_attended_t = grad_attended_c.T
    grad_v = dot(attn_in[1, 2], spread_cols(grad_attended_t))
    grad_vt[...] = grad_v.astype(bf16)
    inner = head_line(head_sums(grad_attended_t * mixed_t))
    shares = query_kt
    shares[...] = (mixed_s[...] * own_share).astype(bf16)
    mixed_s[...] = jnp.zeros_like(mixed_s)

    queue_f = [phase for pair in zip(sum_f.phases[1:], sum_g.phases[1:]) for phase in pair]
    queue_t = list(sum_t.phases)
    queue_k = list(sum_k.phases)
    queue_u = [] if joined else list(sum_u.phases)

    def take(queue):
        if queue:
            queue.pop(0)()

    def at(i, steps):
        for step, queue in steps:
            if queue:
                pl.when(i == (step * chunks) // 16)(queue.pop(0))

    @pl.loop(0, chunks)
    def _(i):
        rows = pl.ds(pl.multiple_of(i * CHUNK, CHUNK), CHUNK)
        key_ct = key_in_s[rows].T
        memory_c = memory_s[rows]
        for p in range(4):
            cols = pair_cols(p)
            grad_probs = dot(memory_c, grad_vt[:, cols])
            probs = probs_s[rows, cols].astype(f32) * factor_s[pl.ds(i, 1), cols]
            probs_s[rows, cols] = probs.astype(bf16)
            grad_scores_s[rows, cols] = (probs * (grad_probs - inner[:, cols])).astype(bf16)
            mixed_s[:, cols] += dot(key_ct, grad_scores_s[rows, cols])
        at(i, [(3, queue_f), (4, queue_f), (8, queue_f), (9, queue_f), (13, queue_f), (14, queue_f)])

    send_b[...] = (project_heads(key_wt, mixed_s[...]) * scale).astype(bf16)
    swap_b = pltpu.make_async_remote_copy(
        src_ref=send_b,
        dst_ref=recv_b,
        send_sem=link_sem.at[2],
        recv_sem=link_sem.at[3],
        device_id=partner,
        device_id_type=pl.DeviceIdType.MESH,
    )
    swap_b.start()
    query_x = spread_rows(query_c.astype(f32))
    grad_x = spread_rows(grad_attended_c)
    rows_k[:D] = (dot(mixed_s[...].astype(bf16), query_x) * scale).astype(bf16)
    rows_k[D : 2 * D] = dot(shares[...], grad_x).astype(bf16)
    out_grad_c = dot_tn(attended_c, grad_branch_c)
    rows_k[2 * D : 3 * D] = jnp.where(is_first, out_grad_c, 0.0).astype(bf16)
    take(queue_k)
    small_s[:16] = jnp.concatenate(
        hidden_sums
        + [
            row_total(grad_branch_f),
            row_total(grad_branch_c),
            gain_grad_2,
            shift_grad_2,
            gain_grad_1,
            shift_grad_1,
            row_total(grad_attended_c),
            jnp.zeros((1, D), f32),
        ],
        axis=0,
    )
    take(queue_f)
    take(queue_f)
    swap_b.wait()
    take(queue_k)
    grad_query_c = (send_b[...].astype(f32) + recv_b[...].astype(f32)).T.astype(bf16)

    cross_pos_grad = dot_nt(grad_query_c, attn_in[1, 0])
    grad_first_in, gain_grad_0, shift_grad_0 = norm_backward(
        grad_second_in + cross_pos_grad, first_normed, first_rstd, gain[0:1]
    )
    grad_branch = grad_first_in.astype(bf16)
    grad_attended = dot_nt(grad_branch, attn_out[0]).astype(bf16).astype(f32)

    @pl.when(member == 0)
    def _():
        rows_u[:ROWS_U] = dot_tn(cross_q, grad_query_c).astype(bf16)

    @pl.when(member == 1)
    def _():
        rows_u[:ROWS_U] = dot_tn(attended, grad_branch).astype(bf16)

    take(queue_u)
    take(queue_k)
    grad_probs = dot(value_self, spread_cols(grad_attended.T))
    inner_self = jnp.sum(probs_self * grad_probs, axis=0, keepdims=True)
    grad_scores = (probs_self * (grad_probs - inner_self)).astype(bf16)
    key_t = key_self.astype(f32).T.astype(bf16)
    grad_query_s = (
        own_blocks([dot(key_t[pair_rows(p)], grad_scores[:, pair_cols(p)]) for p in range(4)]) * scale
    ).T.astype(bf16)
    grad_key_s = (dot(grad_scores, spread_rows(query_self.astype(f32))) * scale).astype(bf16)
    grad_value_s = dot(probs_self_b, spread_rows(grad_attended)).astype(bf16)
    grad_mixed_q = dot_nt(grad_query_s, attn_in[0, 0]) + dot_nt(grad_key_s, attn_in[0, 1])
    small_s[16:] = jnp.concatenate(
        [
            row_total(grad_query_s),
            row_total(grad_value_s),
            row_total(grad_branch),
            row_total(grad_query_c),
            gain_grad_0,
            shift_grad_0,
            jnp.zeros((10, D), f32),
        ],
        axis=0,
    )
    @pl.when(member == 0)
    def _():
        rows_t[:D] = dot_tn(mixed_q, grad_query_s).astype(bf16)
        rows_t[D : 2 * D] = dot_tn(mixed_q, grad_key_s).astype(bf16)

    @pl.when(member == 1)
    def _():
        rows_t[:D] = dot_tn(queries_b, grad_value_s).astype(bf16)
        rows_t[ROW_POS:ROW_SMALL] = (grad_mixed_q + cross_pos_grad).astype(bf16)
        rows_t[ROW_SMALL : ROW_SMALL + 32] = small_s[...].astype(bf16)
        rows_t[ROW_SMALL + 32 : ROWS_T] = jnp.zeros((ROWS_T - ROW_SMALL - 32, D), bf16)

    take(queue_u)
    take(queue_t)
    take(queue_k)
    take(queue_f)
    take(queue_f)
    queries_grad_out[...] = (grad_first_in + grad_mixed_q + dot_nt(grad_value_s, attn_in[0, 2]))[
        :NQ
    ].astype(bf16)
    back_s[:HQ] = (dot_nt(query_x, attn_in[1, 1]) * scale).astype(bf16)
    back_s[HQ:] = dot_nt(grad_x, attn_in[1, 2]).astype(bf16)

    @pl.loop(0, chunks)
    def _(i):
        rows = pl.ds(pl.multiple_of(i * CHUNK, CHUNK), CHUNK)
        both = jnp.concatenate([grad_scores_s[rows], probs_s[rows]], axis=1)
        memory_s[rows] = dot(both, back_s[...]).astype(bf16)
        pltpu.make_async_copy(memory_s.at[rows], memory_grad_hbm.at[0, rows], store_sem.at[i]).start()
        at(
            i,
            [
                (1, queue_t),
                (2, queue_u),
                (3, queue_k),
                (5, queue_t),
                (6, queue_u),
                (7, queue_f),
                (8, queue_f),
                (9, queue_t),
                (10, queue_u),
                (11, queue_k),
                (13, queue_t),
                (14, queue_u),
                (15, queue_k),
            ],
        )

    stores = [
        pltpu.make_async_copy(whole, target, load_sem.at[3 + k])
        for k, (whole, target) in enumerate(
            (
                (whole_f, whole_f_hbm),
                (whole_g, whole_g_hbm),
                (whole_t, whole_t_hbm),
                (whole_k, whole_k_hbm),
                *([] if joined else [(whole_u, whole_u_hbm)]),
            )
        )
    ]
    while queue_f:
        take(queue_f)
    stores[0].start()
    stores[1].start()
    while queue_t or queue_k or queue_u:
        take(queue_t)
        take(queue_u)
        take(queue_k)
    for store in stores[2:]:
        store.start()

    @pl.loop(0, chunks)
    def _(i):
        rows = pl.ds(pl.multiple_of(i * CHUNK, CHUNK), CHUNK)
        pltpu.make_async_copy(memory_s.at[rows], memory_grad_hbm.at[0, rows], store_sem.at[i]).wait()

    for store in stores:
        store.wait()


def finish_kernel(
    joined,
    result_in,
    queries_grad_in,
    memory_grad_in,
    whole_f_hbm,
    whole_g_hbm,
    whole_t_hbm,
    whole_k_hbm,
    whole_u_hbm,
    result,
    queries_grad,
    memory_grad,
    attn_in_hbm,
    attn_out_hbm,
    attn_bias_grad,
    ffn_in_hbm,
    ffn_in_bias_grad,
    ffn_out_hbm,
    ffn_out_bias_grad,
    norm_gain_grad,
    norm_bias_grad,
    query_pos_grad,
    moved,
    whole_f,
    whole_g,
    whole_t,
    whole_k,
    whole_u,
    attn_in_grad,
    attn_out_grad,
    ffn_in_grad,
    ffn_out_grad,
    in_sem,
    out_sem,
    sum_sem,
    grad_sem,
):
    pieces = in_sem.shape[0]
    piece = moved.shape[0] // pieces

    def fetch(j):
        rows = pl.ds(piece * j, piece)
        return pltpu.make_async_copy(memory_grad_in.at[0, rows], moved.at[rows], in_sem.at[j])

    def write(j):
        rows = pl.ds(piece * j, piece)
        return pltpu.make_async_copy(moved.at[rows], memory_grad.at[0, rows], out_sem.at[j])

    sums = [(whole_f_hbm, whole_f), (whole_g_hbm, whole_g), (whole_t_hbm, whole_t), (whole_k_hbm, whole_k)]
    if not joined:
        sums.append((whole_u_hbm, whole_u))
    loads = [pltpu.make_async_copy(*pair, sum_sem.at[j]) for j, pair in enumerate(sums)]
    for load in loads:
        load.start()
    for j in range(pieces):
        fetch(j).start()
    blocks = FF // D
    stores = []

    def store(source, target):
        stores.append(pltpu.make_async_copy(source, target, grad_sem.at[len(stores)]))
        stores[-1].start()

    result[0] = result_in[...]
    queries_grad[0] = queries_grad_in[...]
    for load, whole, first in ((loads[0], whole_f, 0), (loads[1], whole_g, blocks // 2)):
        load.wait()
        for j in range(blocks // 2):
            at = slice(D * (first + j), D * (first + j) + D)
            ffn_out_grad[at] = whole[1, D * j : D * j + D].astype(f32)
        half = slice(D * first, D * first + FF // 2)
        store(ffn_out_grad.at[half], ffn_out_hbm.at[half])
        for j in range(blocks // 2):
            at = slice(D * (first + j), D * (first + j) + D)
            ffn_in_grad[:, at] = whole[0, D * j : D * j + D].astype(f32)
        store(ffn_in_grad.at[:, half], ffn_in_hbm.at[:, half])
    for load in loads[2:]:
        load.wait()
    fourth, at = (whole_t, ROWS_T) if joined else (whole_u, 0)
    for j in range(2):
        attn_in_grad[0, j] = whole_t[0, D * j : D * j + D].astype(f32)
    attn_in_grad[0, 2] = whole_t[1, :D].astype(f32)
    attn_in_grad[1, 0] = fourth[0, at : at + D].astype(f32)
    attn_in_grad[1, 1] = whole_k[:D].astype(f32)
    attn_in_grad[1, 2] = whole_k[D : 2 * D].astype(f32)
    store(attn_in_grad, attn_in_hbm)
    attn_out_grad[0] = fourth[1, at : at + D].astype(f32)
    attn_out_grad[1] = whole_k[2 * D : 3 * D].astype(f32)
    store(attn_out_grad, attn_out_hbm)
    for j in range(pieces):
        fetch(j).wait()
        write(j).start()
    query_pos_grad[...] = whole_t[1, ROW_POS:ROW_SMALL].astype(f32)[:NQ]
    small = whole_t[1, ROW_SMALL : ROW_SMALL + 32].astype(f32)
    ffn_in_bias_grad[...] = jnp.concatenate([small[j : j + 1] for j in range(blocks)], axis=1)
    ffn_out_bias_grad[...] = small[8:9]
    for j, (own, cross) in enumerate(((16, 19), (17, 14), (18, 9))):
        attn_bias_grad[j, 0:1] = small[own : own + 1]
        attn_bias_grad[j, 1:2] = small[cross : cross + 1]
    for j, (gain, shift) in enumerate(((20, 21), (12, 13), (10, 11))):
        norm_gain_grad[j : j + 1] = small[gain : gain + 1]
        norm_bias_grad[j : j + 1] = small[shift : shift + 1]
    for j in range(pieces):
        write(j).wait()
    for copy in stores:
        copy.wait()


def body(
    pages,
    queries,
    memory,
    quarter_turns,
    token_order,
    lengths,
    attn_in,
    attn_out,
    attn_bias,
    ffn_in,
    ffn_in_bias,
    ffn_out,
    ffn_out_bias,
    norm_gain,
    norm_bias,
    query_pos,
    out_grad,
):
    tokens = memory.shape[1]
    chunks = tokens // CHUNK
    groups_f, groups_t, groups_k = sum_groups(pages)
    joined = fourth_joins(pages)
    summed = [
        (padded(ROWS_F, pages), groups_f),
        (padded(ROWS_F, pages), groups_f),
        (padded(ROWS_T + (ROWS_U if joined else 0), pages), groups_t),
        (padded(ROWS_K, 2 * pages), groups_k),
        (TILE if joined else padded(ROWS_U, pages), groups_t),
    ]
    whole_shapes = [(rows, D) if groups is groups_k else (2, rows, D) for rows, groups in summed]
    sum_buffers = []
    for (rows, groups), shape in zip(summed, whole_shapes):
        landing = max(TILE, PageSum.landing_rows(pages, groups, rows))
        sum_buffers += [pltpu.VMEM(each, bf16) for each in ((rows, D), (landing, D), shape)]
    copies = 32
    vmem = pl.BlockSpec(memory_space=pltpu.VMEM)
    smem = pl.BlockSpec(memory_space=pltpu.SMEM)
    anywhere = pl.BlockSpec(memory_space=pl.ANY)
    parts = pl.pallas_call(
        functools.partial(layer_kernel, tokens, pages),
        out_shape=[
            jax.ShapeDtypeStruct((NQ, D), bf16),
            jax.ShapeDtypeStruct((NQ, D), bf16),
            jax.ShapeDtypeStruct((1, tokens, D), bf16),
            *(jax.ShapeDtypeStruct(shape, bf16) for shape in whole_shapes),
        ],
        in_specs=[
            vmem,
            anywhere,
            smem,
            vmem,
            smem,
            vmem,
            vmem,
            vmem,
            anywhere,
            vmem,
            anywhere,
            vmem,
            vmem,
            vmem,
            vmem,
            vmem,
            vmem,
        ],
        out_specs=[vmem, vmem] + [anywhere] * 6,
        scratch_shapes=[
            pltpu.VMEM((tokens, D), bf16),
            pltpu.VMEM((tokens, D), bf16),
            pltpu.VMEM((tokens, HQ), bf16),
            pltpu.VMEM((tokens, HQ), bf16),
            pltpu.VMEM((1, tokens), f32),
            pltpu.VMEM((D, HQ), bf16),
            pltpu.VMEM((D, HQ), bf16),
            pltpu.VMEM((2 * HQ, D), bf16),
            pltpu.VMEM((4 * SIDE, D), bf16),
            pltpu.VMEM((8, HQ), f32),
            pltpu.VMEM((8, HQ), f32),
            pltpu.VMEM((chunks, HQ), f32),
            pltpu.VMEM((chunks, HQ), f32),
            pltpu.VMEM((8, HQ), f32),
            pltpu.VMEM((D, HQ), f32),
            pltpu.VMEM((3, NP, D), f32),
            pltpu.VMEM((D, NP), bf16),
            pltpu.VMEM((D, NP), bf16),
            pltpu.VMEM((2 * HEADS, NP), f32),
            pltpu.VMEM((2 * HEADS, NP), f32),
            pltpu.VMEM((D, NP), bf16),
            pltpu.VMEM((D, NP), bf16),
            pltpu.VMEM((32, D), f32),
            *sum_buffers,
            pltpu.SemaphoreType.DMA((8,)),
            pltpu.SemaphoreType.DMA((chunks,)),
            pltpu.SemaphoreType.DMA((6,)),
            *[pltpu.SemaphoreType.DMA((copies,))] * 10,
        ],
        compiler_params=pltpu.CompilerParams(
            collective_id=0, has_side_effects=True, vmem_limit_bytes=127 * 512 * 1024
        ),
        cost_estimate=pl.CostEstimate(
            flops=2 * 8 * tokens * HQ * D, bytes_accessed=20 << 20, transcendentals=tokens * HQ
        ),
        name="decoder_layer",
    )(
        queries,
        memory,
        quarter_turns,
        token_order,
        lengths,
        attn_in,
        attn_out,
        attn_bias.transpose(1, 0, 2),
        ffn_in,
        ffn_in_bias,
        ffn_out,
        ffn_out_bias,
        norm_gain,
        norm_bias,
        query_pos,
        out_grad,
        jnp.asarray(position_table()),
    )
    outs = pl.pallas_call(
        functools.partial(finish_kernel, joined),
        out_shape=[
            jax.ShapeDtypeStruct((1, NQ, D), bf16),
            jax.ShapeDtypeStruct((1, NQ, D), bf16),
            jax.ShapeDtypeStruct((1, tokens, D), bf16),
            jax.ShapeDtypeStruct((2, 3, D, D), f32),
            jax.ShapeDtypeStruct((2, D, D), f32),
            jax.ShapeDtypeStruct((3, 2, D), f32),
            jax.ShapeDtypeStruct((D, FF), f32),
            jax.ShapeDtypeStruct((1, FF), f32),
            jax.ShapeDtypeStruct((FF, D), f32),
            jax.ShapeDtypeStruct((1, D), f32),
            jax.ShapeDtypeStruct((3, D), f32),
            jax.ShapeDtypeStruct((3, D), f32),
            jax.ShapeDtypeStruct((NQ, D), f32),
        ],
        in_specs=[vmem, vmem] + [anywhere] * 6,
        out_specs=[vmem, vmem, anywhere, anywhere, anywhere, vmem, anywhere, vmem, anywhere] + [vmem] * 4,
        scratch_shapes=[
            pltpu.VMEM((tokens, D), bf16),
            *(pltpu.VMEM(shape, bf16) for shape in whole_shapes),
            pltpu.VMEM((2, 3, D, D), f32),
            pltpu.VMEM((2, D, D), f32),
            pltpu.VMEM((D, FF), f32),
            pltpu.VMEM((FF, D), f32),
            pltpu.SemaphoreType.DMA((8,)),
            pltpu.SemaphoreType.DMA((8,)),
            pltpu.SemaphoreType.DMA((5,)),
            pltpu.SemaphoreType.DMA((6,)),
        ],
        compiler_params=pltpu.CompilerParams(vmem_limit_bytes=62 * 1024 * 1024),
        name="write_outputs",
    )(*parts)
    return (
        *outs[:5],
        outs[5].transpose(1, 0, 2),
        outs[6],
        outs[7].reshape(FF),
        outs[8],
        outs[9].reshape(D),
        *outs[10:],
    )


def solution(mesh):
    in_specs = (
        P("dp", None, None),
        P("dp", "blk", None),
        P("dp"),
        P("dp", "blk"),
        P("dp"),
        P(),
        P(),
        P(),
        P(),
        P(),
        P(),
        P(),
        P(),
        P(),
        P(),
        P("dp", None, None),
    )
    out_specs = (
        P("dp", None, None),
        P("dp", None, None),
        P("dp", "blk", None),
        P(),
        P(),
        P(),
        P(),
        P(),
        P(),
        P(),
        P(),
        P(),
        P(),
    )
    layer = functools.partial(body, mesh.shape["dp"])
    return jax.shard_map(layer, mesh=mesh, in_specs=in_specs, out_specs=out_specs, check_vma=False)
```

```python
import functools
import math

import jax
import jax.numpy as jnp
import numpy as np
from jax import lax
from jax.experimental import pallas as pl
from jax.experimental.pallas import tpu as pltpu
from jax.sharding import PartitionSpec as P

D = 256
HEADS = 8
HD = D // HEADS
SIDE = 128
NQ = 125
NP = 128
HQ = HEADS * NP
PAIR = 2 * NP
FF = 2048
CHUNK = 1024

masked_score = -1e30
norm_eps = 1e-05
scale = 1.0 / math.sqrt(HD)
log2e = math.log2(math.e)

bf16 = jnp.bfloat16
f32 = jnp.float32

ROWS_F = FF // 2
ROW_POS = D
ROW_SMALL = D + NP
ROWS_T = 2 * D
ROWS_K = 3 * D
ROWS_U = D
TILE = 16


def axes_of(pages):
    axes = {"core": (2, 1), "y": (2, 2)}
    stride = 4
    while stride < pages:
        radix = 4 if pages // stride % 4 == 0 else 2
        axes["z%d" % (len(axes) - 2)] = (radix, stride)
        stride *= radix
    axes["x"] = (2, 0)
    return axes


def far_axes(pages):
    return [(name,) for name in axes_of(pages) if name.startswith("z")]


def sum_groups(pages):
    far = far_axes(pages)
    return [("core",), ("y",), *far], [("core", "y"), *far], [("core",), ("x",), ("y",), *far]


def fourth_joins(pages):
    return padded(ROWS_T + ROWS_U, pages) < padded(ROWS_T, pages) + padded(ROWS_U, pages)


def padded(rows, pages):
    unit = TILE * pages
    return (rows + unit - 1) // unit * unit


def position_table():
    half = D // 2
    channel = np.arange(half)
    inverse = np.exp((channel // 2).astype(np.float32) * np.float32(-2.0 * math.log(10000.0) / half))
    angle = (np.arange(SIDE, dtype=np.float32) + 1.0) * np.float32(2.0 * math.pi / SIDE)
    angle = angle[:, None] * inverse
    return np.where(channel % 2 == 0, np.sin(angle), np.cos(angle)).astype(np.float32)


def dot(a, b):
    return jnp.dot(a, b, preferred_element_type=f32)


def dot_nt(a, b):
    return lax.dot_general(a, b, (((1,), (1,)), ((), ())), preferred_element_type=f32)


def dot_tn(a, b):
    return lax.dot_general(a, b, (((0,), (0,)), ((), ())), preferred_element_type=f32)


def row_total(values):
    return jnp.sum(values.astype(f32), axis=0, keepdims=True)


def norm_forward(values):
    average = jnp.mean(values, axis=-1, keepdims=True)
    centred = values - average
    variance = jnp.mean(centred * centred, axis=-1, keepdims=True)
    rstd = lax.rsqrt(variance + norm_eps)
    return centred * rstd, rstd


def norm_backward(grad, normed, rstd, gain):
    grad_normed = grad * gain
    first = jnp.mean(grad_normed, axis=-1, keepdims=True)
    second = jnp.mean(grad_normed * normed, axis=-1, keepdims=True)
    grad_in = rstd * (grad_normed - first - normed * second)
    return grad_in, row_total(grad * normed), row_total(grad)


def spread_rows(rows):
    head = lax.broadcasted_iota(jnp.int32, (NP, D), 1) // HD
    return jnp.concatenate(
        [jnp.where(head == h, rows, 0.0) for h in range(HEADS)], axis=0
    ).astype(bf16)


def spread_cols(cols):
    head = lax.broadcasted_iota(jnp.int32, (D, NP), 0) // HD
    return jnp.concatenate(
        [jnp.where(head == h, cols, 0.0) for h in range(HEADS)], axis=1
    ).astype(bf16)


def own_heads(full):
    return jnp.concatenate(
        [full[HD * h : HD * h + HD, NP * h : NP * h + NP] for h in range(HEADS)], axis=0
    )


def project_heads(weight_t, sums):
    high = sums.astype(bf16)
    low = (sums - high.astype(f32)).astype(bf16)
    return own_heads(dot(weight_t, high) + dot(weight_t, low))


def own_blocks(pairs):
    parts = []
    for pair in pairs:
        parts += [pair[:HD, :NP], pair[HD:, NP:]]
    return jnp.concatenate(parts, axis=0)


def head_rows(row):
    return jnp.concatenate([row[:, NP * h : NP * h + NP] for h in range(HEADS)], axis=0)


def head_line(rows):
    return jnp.concatenate([rows[h : h + 1] for h in range(HEADS)], axis=1)


def per_channel(rows):
    return jnp.concatenate(
        [jnp.broadcast_to(rows[h : h + 1], (HD, NP)) for h in range(HEADS)], axis=0
    )


def head_sums(cols):
    return jnp.concatenate(
        [jnp.sum(cols[HD * h : HD * h + HD], axis=0, keepdims=True) for h in range(HEADS)], axis=0
    )


def pair_cols(p):
    return slice(PAIR * p, PAIR * p + PAIR)


def pair_rows(p):
    return slice(2 * HD * p, 2 * HD * p + 2 * HD)


class Place:
    def __init__(self, pages):
        self.axes = axes_of(pages)
        self.page = lax.axis_index("dp")
        self.member = lax.axis_index("blk")
        self.digit = {
            name: self.member if name == "x" else lax.rem(self.page // stride, radix)
            for name, (radix, stride) in self.axes.items()
        }

    def size(self, group):
        return math.prod(self.axes[name][0] for name in group)

    def index(self, group):
        index = 0
        for name in group:
            index = index * self.axes[name][0] + self.digit[name]
        return index

    def peer(self, group, hop):
        index = lax.rem(self.index(group) + hop, self.size(group))
        page, member, rest = self.page, self.member, index
        for name in reversed(group):
            radix, stride = self.axes[name]
            digit = lax.rem(rest, radix)
            rest = rest // radix
            if name == "x":
                member = digit
            else:
                page = page + (digit - self.digit[name]) * stride
        return (page, member), index


class PageSum:
    def __init__(self, place, groups, back, rows, landing, whole, sent, arrived):
        self.place, self.groups, self.back = place, groups, back
        self.rows, self.landing, self.whole = rows, landing, whole
        self.sent, self.arrived = sent, arrived
        self.slots = 0
        self.extents = [rows.shape[0]]
        self.bases = [0]
        self.landings = []
        at = 0
        for group in groups:
            size = place.size(group)
            extent = self.extents[-1] // size
            self.landings.append(at)
            at += (size - 1) * extent
            self.bases.append(pl.multiple_of(self.bases[-1] + place.index(group) * extent, TILE))
            self.extents.append(extent)
        last = len(groups)
        moves = [self.scatter_moves(s) for s in range(last)]
        near = {"all": 0, "across": 1, "sides": 2}[back]
        moves += [self.gather_moves(s) for s in range(last - 1, near - 1, -1)]
        if back == "sides":
            moves += [self.side_moves(), self.corner_moves(), self.core_moves()]
        elif back == "across":
            moves += [self.across_moves(), self.core_moves()]
        self.phases = [functools.partial(self.step, moves, k) for k in range(len(moves) + 1)]

    @staticmethod
    def landing_rows(pages, groups, rows):
        axes = axes_of(pages)
        total, extent = 0, rows
        for group in groups:
            size = math.prod(axes[name][0] for name in group)
            extent //= size
            total += (size - 1) * extent
        return total

    def step(self, moves, k):
        last = len(self.groups)
        if k > 0:
            for move in moves[k - 1]:
                self.copy(*move).wait()
        if 0 < k <= last:
            if k < last:
                target = self.rows
            else:
                target = self.whole.at[self.place.member] if len(self.whole.shape) == 3 else self.whole
            self.scatter_sum(k - 1, target)
        if k < len(moves):
            for move in moves[k]:
                self.copy(*move).start()

    def copy(self, slot, source, target, device):
        return pltpu.make_async_remote_copy(
            src_ref=source(),
            dst_ref=target(),
            send_sem=self.sent.at[slot],
            recv_sem=self.arrived.at[slot],
            device_id=device,
            device_id_type=pl.DeviceIdType.MESH,
        )

    def new_slot(self):
        self.slots += 1
        return self.slots - 1

    def same(self, device, view):
        return (self.new_slot(), view, view, device)

    def scatter_moves(self, step):
        group = self.groups[step]
        extent = self.extents[step + 1]
        moves = []
        for hop in range(1, self.place.size(group)):
            device, other = self.place.peer(group, hop)
            start = pl.multiple_of(self.bases[step] + other * extent, TILE)
            landing = self.landings[step] + (hop - 1) * extent
            moves.append(
                (
                    self.new_slot(),
                    functools.partial(self.part, self.rows, start, extent),
                    functools.partial(self.part, self.landing, landing, extent),
                    device,
                )
            )
        return moves

    @staticmethod
    def part(ref, start, extent):
        return ref.at[pl.ds(start, extent)]

    def half(self, member, start, extent):
        if len(self.whole.shape) == 3:
            return self.whole.at[member, pl.ds(start, extent)]
        return self.whole.at[pl.ds(start, extent)]

    def scatter_sum(self, step, target):
        extent = self.extents[step + 1]
        block = math.gcd(extent, 64)

        def add(i):
            start = pl.multiple_of(i * block, block)
            own = pl.ds(pl.multiple_of(self.bases[step + 1] + start, TILE), block)
            total = self.rows[own].astype(f32)
            for hop in range(1, self.place.size(self.groups[step])):
                landing = self.landings[step] + (hop - 1) * extent
                total = total + self.landing[pl.ds(landing + start, block)].astype(f32)
            target[own] = total.astype(bf16)

        for i in range(extent // block):
            add(i)

    def gather_moves(self, step):
        group = self.groups[step]
        view = functools.partial(self.half, self.place.member, self.bases[step + 1], self.extents[step + 1])
        return [
            self.same(self.place.peer(group, hop)[0], view) for hop in range(1, self.place.size(group))
        ]

    def own_quarter(self):
        step = 2 if len(self.groups[0]) == 1 else 1
        return self.bases[step], self.extents[step]

    def side_moves(self):
        view = functools.partial(self.half, self.place.member, *self.own_quarter())
        return [self.same(self.place.peer((name,), 1)[0], view) for name in ("y", "x")]

    def corner_moves(self):
        base, extent = self.own_quarter()
        other = pl.multiple_of(base + (1 - 2 * self.place.digit["y"]) * extent, TILE)
        view = functools.partial(self.half, self.place.member, other, extent)
        return [self.same(self.place.peer(("x",), 1)[0], view)]

    def across_moves(self):
        view = functools.partial(self.half, self.place.member, *self.own_quarter())
        return [self.same(self.place.peer(("x", "y"), hop)[0], view) for hop in range(1, 4)]

    def core_moves(self):
        extent = self.extents[0] // 2
        start = pl.multiple_of(self.place.digit["core"] * extent, TILE)
        device, _ = self.place.peer(("core",), 1)
        return [self.same(device, functools.partial(self.half, m, start, extent)) for m in range(2)]


def clear_rest(ref, used):
    if ref.shape[0] > used:
        ref[used:] = jnp.zeros((ref.shape[0] - used, D), ref.dtype)


def layer_kernel(
    tokens,
    pages,
    queries_in,
    memory_hbm,
    turns_in,
    order_in,
    lengths_in,
    attn_in,
    attn_out,
    attn_bias,
    ffn_in_hbm,
    ffn_in_bias,
    ffn_out_hbm,
    ffn_out_bias,
    norm_gain,
    norm_bias,
    pos_in,
    out_grad_in,
    table_in,
    result_out,
    queries_grad_out,
    memory_grad_hbm,
    whole_f_hbm,
    whole_g_hbm,
    whole_t_hbm,
    whole_k_hbm,
    whole_u_hbm,
    memory_s,
    key_in_s,
    probs_s,
    grad_scores_s,
    code_s,
    query_kt,
    grad_vt,
    back_s,
    table_s,
    top_s,
    highest_s,
    shifts_s,
    factor_s,
    total_s,
    mixed_s,
    pad_s,
    send_a,
    recv_a,
    send_t,
    recv_t,
    send_b,
    recv_b,
    small_s,
    rows_f,
    landing_f,
    whole_f,
    rows_g,
    landing_g,
    whole_g,
    rows_t,
    landing_t,
    whole_t,
    rows_k,
    landing_k,
    whole_k,
    rows_u,
    landing_u,
    whole_u,
    load_sem,
    store_sem,
    link_sem,
    sent_f,
    arrived_f,
    sent_g,
    arrived_g,
    sent_t,
    arrived_t,
    sent_k,
    arrived_k,
    sent_u,
    arrived_u,
):
    member = lax.axis_index("blk")
    partner = (lax.axis_index("dp"), 1 - member)
    chunks = tokens // CHUNK

    place = Place(pages)
    groups_f, groups_t, groups_k = sum_groups(pages)
    sum_f = PageSum(place, groups_f, "sides", rows_f, landing_f, whole_f, sent_f, arrived_f)
    sum_g = PageSum(place, groups_f, "sides", rows_g, landing_g, whole_g, sent_g, arrived_g)
    sum_t = PageSum(place, groups_t, "across", rows_t, landing_t, whole_t, sent_t, arrived_t)
    sum_k = PageSum(place, groups_k, "all", rows_k, landing_k, whole_k, sent_k, arrived_k)
    joined = fourth_joins(pages)
    if joined:
        rows_u = rows_t.at[ROWS_T : ROWS_T + ROWS_U]
    else:
        sum_u = PageSum(place, groups_t, "across", rows_u, landing_u, whole_u, sent_u, arrived_u)

    barrier = pltpu.get_barrier_semaphore()
    peers = [
        place.peer(group, hop)[0]
        for group in [("x", "core", "y"), *far_axes(pages)]
        for hop in range(1, place.size(group))
    ]
    for peer in peers:
        pl.semaphore_signal(barrier, inc=1, device_id=peer, device_id_type=pl.DeviceIdType.MESH)

    def load_memory(i):
        rows = pl.ds(pl.multiple_of(i * CHUNK, CHUNK), CHUNK)
        return pltpu.make_async_copy(memory_hbm.at[0, rows], memory_s.at[rows], store_sem.at[i])

    half = FF // 2
    ffn_in_s = [grad_scores_s.at[D * k : D * k + D] for k in range(2)]
    ffn_out_s = grad_scores_s.at[2 * D : 2 * D + FF, :D]
    free = 2 * D + FF
    active_s = [grad_scores_s.at[free + NP * k : free + NP * k + NP] for k in range(2)]
    slope_s = [grad_scores_s.at[free + NP * k : free + NP * k + NP] for k in range(2, 4)]
    load_ffn = [
        pltpu.make_async_copy(ffn_in_hbm.at[:, half * k : half * k + half], ffn_in_s[k], load_sem.at[k])
        for k in range(2)
    ]
    load_ffn.append(pltpu.make_async_copy(ffn_out_hbm, ffn_out_s, load_sem.at[2]))
    for k in range(chunks):
        load_memory(k).start()
    for load in load_ffn:
        load.start()

    pairs = [attn_bias[j].astype(f32) for j in range(3)]
    bias = jnp.concatenate([pair[k : k + 1] for k in range(2) for pair in pairs], axis=0)
    gain = norm_gain[...].astype(f32)
    shift = norm_bias[...].astype(f32)

    order = order_in[...]
    turn = turns_in[0]
    row_at = order >> 7
    col_at = order & 127
    top = SIDE - 1
    row_new = jnp.where(
        turn == 0, row_at, jnp.where(turn == 1, col_at, jnp.where(turn == 2, top - row_at, top - col_at))
    )
    col_new = jnp.where(
        turn == 0, col_at, jnp.where(turn == 1, top - row_at, jnp.where(turn == 2, top - col_at, row_at))
    )
    past = jnp.where(order < lengths_in[0], 0, SIDE * SIDE)
    code_s[...] = (row_new * SIDE + col_new + past).astype(f32)

    pad_s[...] = jnp.zeros_like(pad_s)
    pad_s[0, :NQ] = queries_in[0].astype(f32)
    pad_s[1, :NQ] = pos_in[...].astype(f32)
    pad_s[2, :NQ] = out_grad_in[0].astype(f32)
    queries_f = pad_s[0]
    pos_f = pad_s[1]
    queries_b = queries_f.astype(bf16)
    mixed_q = (queries_f + pos_f).astype(bf16)
    query_self = (dot(mixed_q, attn_in[0, 0]) + bias[0:1]).astype(bf16)
    key_self = dot(mixed_q, attn_in[0, 1]).astype(bf16)
    value_self = (dot(queries_b, attn_in[0, 2]) + bias[1:2]).astype(bf16)
    scores = dot(key_self, spread_cols(query_self.astype(f32).T)) * scale
    own_key = lax.broadcasted_iota(jnp.int32, (NP, HQ), 0) < NQ
    scores = jnp.where(own_key, scores, masked_score)
    raised = jnp.exp(scores - jnp.max(scores, axis=0, keepdims=True))
    probs_self = raised / jnp.sum(raised, axis=0, keepdims=True)
    probs_self_b = probs_self.astype(bf16)
    value_t = value_self.astype(f32).T.astype(bf16)
    table = table_in[...]
    nothing = jnp.zeros((SIDE, D // 2), f32)
    table = jnp.concatenate(
        [jnp.concatenate([table, nothing], axis=1), jnp.concatenate([nothing, table], axis=1)], axis=0
    )
    table_high = table.astype(bf16)
    table_s[: 2 * SIDE] = table_high
    table_s[2 * SIDE :] = (table - table_high.astype(f32)).astype(bf16)

    def mask_view(i):
        side, place = i // (chunks // 2), lax.rem(i, chunks // 2)
        return grad_scores_s.at[
            pl.ds(pl.multiple_of(tokens // 2 + place * CHUNK, CHUNK), CHUNK),
            pl.ds(pl.multiple_of(side * NP, NP), NP),
        ]

    lane = lax.broadcasted_iota(jnp.int32, (CHUNK, NP), 1)

    def place_chunk(i):
        rows = pl.ds(pl.multiple_of(i * CHUNK, CHUNK), CHUNK)
        line = code_s[:, rows]
        code = jnp.concatenate(
            [
                jnp.broadcast_to(line[:, NP * j : NP * j + NP], (NP, NP)).T
                for j in range(CHUNK // NP)
            ],
            axis=0,
        ).astype(jnp.int32)
        row_hot = jnp.where(((code >> 7) & 127) == lane, 1.0, 0.0).astype(bf16)
        col_hot = jnp.where((code & 127) == lane, 1.0, 0.0).astype(bf16)
        hot = jnp.concatenate([row_hot, col_hot, row_hot, col_hot], axis=1)
        masked = jnp.where(code < SIDE * SIDE, 0.0, masked_score)
        mask_view(i)[...] = masked.astype(bf16)
        load_memory(i).wait()
        key_in_s[rows] = (memory_s[rows].astype(f32) + dot(hot, table_s[...])).astype(bf16)

    attended = own_blocks(
        [dot(value_t[pair_rows(p)], probs_self_b[:, pair_cols(p)]) for p in range(4)]
    ).T.astype(bf16)
    first_normed, first_rstd = norm_forward(queries_f + dot(attended, attn_out[0]) + bias[2:3])
    first = first_normed * gain[0:1] + shift[0:1]
    cross_q = (first + pos_f).astype(bf16)
    query_c = (dot(cross_q, attn_in[1, 0]) + bias[3:4]).astype(bf16)
    query_k = dot(attn_in[1, 1], spread_cols(query_c.astype(f32).T))
    query_kt[...] = (query_k * (scale * log2e)).astype(bf16)
    pl.loop(0, chunks)(place_chunk)

    def score_pair(p, key_in, mask, score_s):
        cols = pair_cols(p)
        part = dot(key_in, query_kt[:, cols]) + mask
        score_s[:, cols] = part
        top_s[:, cols] = jnp.max(part.reshape(CHUNK // 8, 8, PAIR), axis=0)

    def score_operands(i):
        rows = pl.ds(pl.multiple_of(i * CHUNK, CHUNK), CHUNK)
        mask = mask_view(i)[...].astype(f32)
        return key_in_s[rows], jnp.concatenate([mask, mask], axis=1)

    def attend_all(score_s):
        operands = score_operands(0)
        for p in range(4):
            score_pair(p, *operands, score_s)

        @pl.loop(0, chunks)
        def _(i):
            rows = pl.ds(pl.multiple_of(i * CHUNK, CHUNK), CHUNK)
            memory_ct = memory_s[rows].T
            operands = score_operands(jnp.minimum(i + 1, chunks - 1))
            for p in range(4):
                cols = pair_cols(p)
                before = highest_s[0:1, cols]
                highest = jnp.maximum(before, jnp.max(top_s[:, cols], axis=0, keepdims=True))
                highest_s[0:1, cols] = highest
                shifts_s[pl.ds(i, 1), cols] = highest
                fade = jnp.exp2(before - highest)
                raised = jnp.exp2(score_s[:, cols] - highest)
                sums = jnp.sum(raised.reshape(CHUNK // 8, 8, PAIR), axis=0)
                total_s[:, cols] = total_s[:, cols] * fade + sums
                probs_s[rows, cols] = raised.astype(bf16)
                mixed_s[:, cols] = mixed_s[:, cols] * fade + dot(memory_ct, probs_s[rows, cols])
                score_pair(p, *operands, score_s)

    highest_s[0:1] = jnp.full((1, HQ), -3e38, f32)
    total_s[...] = jnp.zeros_like(total_s)
    mixed_s[...] = jnp.zeros_like(mixed_s)
    pl.run_scoped(attend_all, pltpu.VMEM((CHUNK, HQ), f32))
    highest_own = highest_s[0:1]
    total_own = jnp.sum(total_s[...], axis=0, keepdims=True)

    value_wt = attn_in[1, 2].astype(f32).T.astype(bf16)
    key_wt = attn_in[1, 1].astype(f32).T.astype(bf16)
    send_a[...] = project_heads(value_wt, mixed_s[...]).astype(bf16)
    send_t[:HEADS] = head_rows(highest_own)
    send_t[HEADS:] = head_rows(total_own)
    pl.semaphore_wait(barrier, len(peers))
    swap_a = pltpu.make_async_remote_copy(
        src_ref=send_a,
        dst_ref=recv_a,
        send_sem=link_sem.at[0],
        recv_sem=link_sem.at[1],
        device_id=partner,
        device_id_type=pl.DeviceIdType.MESH,
    )
    swap_t = pltpu.make_async_remote_copy(
        src_ref=send_t,
        dst_ref=recv_t,
        send_sem=link_sem.at[4],
        recv_sem=link_sem.at[5],
        device_id=partner,
        device_id_type=pl.DeviceIdType.MESH,
    )
    swap_a.start()
    swap_t.start()
    swap_a.wait()
    swap_t.wait()
    is_first = member == 0
    own, other = send_a[...].astype(f32), recv_a[...].astype(f32)
    left = jnp.where(is_first, own, other)
    right = jnp.where(is_first, other, own)
    own, other = send_t[...], recv_t[...]
    left_t = jnp.where(is_first, own, other)
    right_t = jnp.where(is_first, other, own)
    highest = jnp.maximum(left_t[:HEADS], right_t[:HEADS])
    fade_l = jnp.exp2(left_t[:HEADS] - highest)
    fade_r = jnp.exp2(right_t[:HEADS] - highest)
    total = left_t[HEADS:] * fade_l + right_t[HEADS:] * fade_r
    mixed_t = left * per_channel(fade_l / total) + right * per_channel(fade_r / total)
    log_total = head_line(highest + jnp.log2(total))
    own_share = jnp.exp2(highest_own - log_total)
    factor_s[...] = jnp.exp2(shifts_s[...] - log_total)
    attended_c = (mixed_t.T + bias[4:5]).astype(bf16)

    second_normed, second_rstd = norm_forward(first + dot(attended_c, attn_out[1]) + bias[5:6])
    second = second_normed * gain[1:2] + shift[1:2]
    ffn_input = second.astype(bf16)
    load_ffn[0].wait()
    load_ffn[1].wait()
    blocks = [(j // 4, slice(D * j, D * j + D), slice(j % 4 * D, j % 4 * D + D)) for j in range(FF // D)]
    hidden_bias = ffn_in_bias[...].astype(f32).reshape(1, FF)
    def feed_forward(gate_s):
        for k, cols, part in blocks:
            hidden = dot(ffn_input, ffn_in_s[k][:, part]) + hidden_bias[:, cols]
            half_gate = 0.5 + 0.5 * lax.erf(hidden * math.sqrt(0.5))
            active_s[k][:, part] = (hidden * half_gate).astype(bf16)
            gate_s[:, cols] = half_gate + hidden * jnp.exp(hidden * hidden * -0.5) * (
                1.0 / math.sqrt(2.0 * math.pi)
            )
        load_ffn[2].wait()
        third_normed, third_rstd = norm_forward(
            second
            + dot(active_s[0][...], ffn_out_s[:half])
            + dot(active_s[1][...], ffn_out_s[half:])
            + ffn_out_bias[...].astype(f32).reshape(1, D)
        )
        result_out[...] = (third_normed * gain[2:3] + shift[2:3])[:NQ].astype(bf16)
        grad_third, gain_grad_2, shift_grad_2 = norm_backward(
            pad_s[2], third_normed, third_rstd, gain[2:3]
        )
        grad_branch_f = grad_third.astype(bf16)
        for k, cols, part in blocks:
            grad_hidden = dot_nt(grad_branch_f, ffn_out_s[cols]) * gate_s[:, cols]
            slope_s[k][:, part] = grad_hidden.astype(bf16)
        return grad_third, gain_grad_2, shift_grad_2, grad_branch_f

    grad_third, gain_grad_2, shift_grad_2, grad_branch_f = pl.run_scoped(
        feed_forward, pltpu.VMEM((NP, FF), f32)
    )
    grad_second = grad_third + dot_nt(slope_s[0][...], ffn_in_s[0][...])
    grad_second += dot_nt(slope_s[1][...], ffn_in_s[1][...])
    grad_second_in, gain_grad_1, shift_grad_1 = norm_backward(
        grad_second, second_normed, second_rstd, gain[1:2]
    )
    grad_branch_c = grad_second_in.astype(bf16)
    ffn_input_t = second.T.astype(bf16)

    def ffn_rows(target, k):
        @pl.when(member == 0)
        def _():
            for j in range(4):
                part = slice(D * j, D * j + D)
                target[part] = dot(ffn_input_t, slope_s[k][:, part]).astype(bf16)

        @pl.when(member == 1)
        def _():
            for j in range(4):
                part = slice(D * j, D * j + D)
                target[part] = dot_tn(active_s[k][:, part], grad_branch_f).astype(bf16)

    ffn_rows(rows_f, 0)
    sum_f.phases[0]()
    ffn_rows(rows_g, 1)

    is_first = member == 0
    clear_rest(rows_f, ROWS_F)
    clear_rest(rows_g, ROWS_F)
    clear_rest(rows_t, ROWS_T + (ROWS_U if joined else 0))
    clear_rest(rows_k, ROWS_K)
    if not joined:
        clear_rest(rows_u, ROWS_U)
    sum_g.phases[0]()
    grad_attended_c = dot_nt(grad_branch_c, attn_out[1]).astype(bf16).astype(f32)
    hidden_sums = [row_total(slope_s[k][:, part]) for k, _, part in blocks]

    grad_attended_t = grad_attended_c.T
    grad_v = dot(attn_in[1, 2], spread_cols(grad_attended_t))
    grad_vt[...] = grad_v.astype(bf16)
    inner = head_line(head_sums(grad_attended_t * mixed_t))
    shares = query_kt
    shares[...] = (mixed_s[...] * own_share).astype(bf16)
    mixed_s[...] = jnp.zeros_like(mixed_s)

    queue_f = [phase for pair in zip(sum_f.phases[1:], sum_g.phases[1:]) for phase in pair]
    queue_t = list(sum_t.phases)
    queue_k = list(sum_k.phases)
    queue_u = [] if joined else list(sum_u.phases)

    def take(queue):
        if queue:
            queue.pop(0)()

    def at(i, steps):
        for step, queue in steps:
            if queue:
                pl.when(i == (step * chunks) // 16)(queue.pop(0))

    @pl.loop(0, chunks)
    def _(i):
        rows = pl.ds(pl.multiple_of(i * CHUNK, CHUNK), CHUNK)
        key_ct = key_in_s[rows].T
        memory_c = memory_s[rows]
        for p in range(4):
            cols = pair_cols(p)
            grad_probs = dot(memory_c, grad_vt[:, cols])
            probs = probs_s[rows, cols].astype(f32) * factor_s[pl.ds(i, 1), cols]
            probs_s[rows, cols] = probs.astype(bf16)
            grad_scores_s[rows, cols] = (probs * (grad_probs - inner[:, cols])).astype(bf16)
            mixed_s[:, cols] += dot(key_ct, grad_scores_s[rows, cols])
        at(i, [(3, queue_f), (4, queue_f), (8, queue_f), (9, queue_f), (13, queue_f), (14, queue_f)])

    send_b[...] = (project_heads(key_wt, mixed_s[...]) * scale).astype(bf16)
    swap_b = pltpu.make_async_remote_copy(
        src_ref=send_b,
        dst_ref=recv_b,
        send_sem=link_sem.at[2],
        recv_sem=link_sem.at[3],
        device_id=partner,
        device_id_type=pl.DeviceIdType.MESH,
    )
    swap_b.start()
    query_x = spread_rows(query_c.astype(f32))
    grad_x = spread_rows(grad_attended_c)
    rows_k[:D] = (dot(mixed_s[...].astype(bf16), query_x) * scale).astype(bf16)
    rows_k[D : 2 * D] = dot(shares[...], grad_x).astype(bf16)
    out_grad_c = dot_tn(attended_c, grad_branch_c)
    rows_k[2 * D : 3 * D] = jnp.where(is_first, out_grad_c, 0.0).astype(bf16)
    take(queue_k)
    small_s[:16] = jnp.concatenate(
        hidden_sums
        + [
            row_total(grad_branch_f),
            row_total(grad_branch_c),
            gain_grad_2,
            shift_grad_2,
            gain_grad_1,
            shift_grad_1,
            row_total(grad_attended_c),
            jnp.zeros((1, D), f32),
        ],
        axis=0,
    )
    take(queue_f)
    take(queue_f)
    swap_b.wait()
    take(queue_k)
    grad_query_c = (send_b[...].astype(f32) + recv_b[...].astype(f32)).T.astype(bf16)

    cross_pos_grad = dot_nt(grad_query_c, attn_in[1, 0])
    grad_first_in, gain_grad_0, shift_grad_0 = norm_backward(
        grad_second_in + cross_pos_grad, first_normed, first_rstd, gain[0:1]
    )
    grad_branch = grad_first_in.astype(bf16)
    grad_attended = dot_nt(grad_branch, attn_out[0]).astype(bf16).astype(f32)

    @pl.when(member == 0)
    def _():
        rows_u[:ROWS_U] = dot_tn(cross_q, grad_query_c).astype(bf16)

    @pl.when(member == 1)
    def _():
        rows_u[:ROWS_U] = dot_tn(attended, grad_branch).astype(bf16)

    take(queue_u)
    take(queue_k)
    grad_probs = dot(value_self, spread_cols(grad_attended.T))
    inner_self = jnp.sum(probs_self * grad_probs, axis=0, keepdims=True)
    grad_scores = (probs_self * (grad_probs - inner_self)).astype(bf16)
    key_t = key_self.astype(f32).T.astype(bf16)
    grad_query_s = (
        own_blocks([dot(key_t[pair_rows(p)], grad_scores[:, pair_cols(p)]) for p in range(4)]) * scale
    ).T.astype(bf16)
    take(queue_k)
    take(queue_f)
    take(queue_f)
    grad_key_s = (dot(grad_scores, spread_rows(query_self.astype(f32))) * scale).astype(bf16)
    grad_value_s = dot(probs_self_b, spread_rows(grad_attended)).astype(bf16)
    grad_mixed_q = dot_nt(grad_query_s, attn_in[0, 0]) + dot_nt(grad_key_s, attn_in[0, 1])
    small_s[16:] = jnp.concatenate(
        [
            row_total(grad_query_s),
            row_total(grad_value_s),
            row_total(grad_branch),
            row_total(grad_query_c),
            gain_grad_0,
            shift_grad_0,
            jnp.zeros((10, D), f32),
        ],
        axis=0,
    )
    @pl.when(member == 0)
    def _():
        rows_t[:D] = dot_tn(mixed_q, grad_query_s).astype(bf16)
        rows_t[D : 2 * D] = dot_tn(mixed_q, grad_key_s).astype(bf16)

    @pl.when(member == 1)
    def _():
        rows_t[:D] = dot_tn(queries_b, grad_value_s).astype(bf16)
        rows_t[ROW_POS:ROW_SMALL] = (grad_mixed_q + cross_pos_grad).astype(bf16)
        rows_t[ROW_SMALL : ROW_SMALL + 32] = small_s[...].astype(bf16)
        rows_t[ROW_SMALL + 32 : ROWS_T] = jnp.zeros((ROWS_T - ROW_SMALL - 32, D), bf16)

    take(queue_t)
    take(queue_u)
    take(queue_k)
    queries_grad_out[...] = (grad_first_in + grad_mixed_q + dot_nt(grad_value_s, attn_in[0, 2]))[
        :NQ
    ].astype(bf16)
    back_s[:HQ] = (dot_nt(query_x, attn_in[1, 1]) * scale).astype(bf16)
    back_s[HQ:] = dot_nt(grad_x, attn_in[1, 2]).astype(bf16)

    @pl.loop(0, chunks)
    def _(i):
        rows = pl.ds(pl.multiple_of(i * CHUNK, CHUNK), CHUNK)
        both = jnp.concatenate([grad_scores_s[rows], probs_s[rows]], axis=1)
        memory_s[rows] = dot(both, back_s[...]).astype(bf16)
        pltpu.make_async_copy(memory_s.at[rows], memory_grad_hbm.at[0, rows], store_sem.at[i]).start()
        at(
            i,
            [
                (2, queue_t),
                (3, queue_u),
                (4, queue_k),
                (5, queue_f),
                (5, queue_f),
                (6, queue_t),
                (7, queue_u),
                (8, queue_k),
                (9, queue_f),
                (9, queue_f),
                (10, queue_t),
                (11, queue_u),
                (12, queue_k),
                (14, queue_t),
                (15, queue_u),
                (15, queue_k),
            ],
        )

    stores = [
        pltpu.make_async_copy(whole, target, load_sem.at[3 + k])
        for k, (whole, target) in enumerate(
            (
                (whole_f, whole_f_hbm),
                (whole_g, whole_g_hbm),
                (whole_t, whole_t_hbm),
                (whole_k, whole_k_hbm),
                *([] if joined else [(whole_u, whole_u_hbm)]),
            )
        )
    ]
    while queue_f:
        take(queue_f)
    stores[0].start()
    stores[1].start()
    while queue_t or queue_k or queue_u:
        take(queue_t)
        take(queue_u)
        take(queue_k)
    for store in stores[2:]:
        store.start()

    @pl.loop(0, chunks)
    def _(i):
        rows = pl.ds(pl.multiple_of(i * CHUNK, CHUNK), CHUNK)
        pltpu.make_async_copy(memory_s.at[rows], memory_grad_hbm.at[0, rows], store_sem.at[i]).wait()

    for store in stores:
        store.wait()


def finish_kernel(
    joined,
    result_in,
    queries_grad_in,
    memory_grad_in,
    whole_f_hbm,
    whole_g_hbm,
    whole_t_hbm,
    whole_k_hbm,
    whole_u_hbm,
    result,
    queries_grad,
    memory_grad,
    attn_in_hbm,
    attn_out_hbm,
    attn_bias_grad,
    ffn_in_hbm,
    ffn_in_bias_grad,
    ffn_out_hbm,
    ffn_out_bias_grad,
    norm_gain_grad,
    norm_bias_grad,
    query_pos_grad,
    moved,
    whole_f,
    whole_g,
    whole_t,
    whole_k,
    whole_u,
    attn_in_grad,
    attn_out_grad,
    ffn_in_grad,
    ffn_out_grad,
    in_sem,
    out_sem,
    sum_sem,
    grad_sem,
):
    pieces = in_sem.shape[0]
    piece = moved.shape[0] // pieces

    def fetch(j):
        rows = pl.ds(piece * j, piece)
        return pltpu.make_async_copy(memory_grad_in.at[0, rows], moved.at[rows], in_sem.at[j])

    def write(j):
        rows = pl.ds(piece * j, piece)
        return pltpu.make_async_copy(moved.at[rows], memory_grad.at[0, rows], out_sem.at[j])

    sums = [(whole_f_hbm, whole_f), (whole_g_hbm, whole_g), (whole_t_hbm, whole_t), (whole_k_hbm, whole_k)]
    if not joined:
        sums.append((whole_u_hbm, whole_u))
    loads = [pltpu.make_async_copy(*pair, sum_sem.at[j]) for j, pair in enumerate(sums)]
    for load in loads:
        load.start()
    for j in range(pieces):
        fetch(j).start()
    blocks = FF // D
    stores = []

    def store(source, target):
        stores.append(pltpu.make_async_copy(source, target, grad_sem.at[len(stores)]))
        stores[-1].start()

    result[0] = result_in[...]
    queries_grad[0] = queries_grad_in[...]
    for load, whole, first in ((loads[0], whole_f, 0), (loads[1], whole_g, blocks // 2)):
        load.wait()
        for j in range(blocks // 2):
            at = slice(D * (first + j), D * (first + j) + D)
            ffn_out_grad[at] = whole[1, D * j : D * j + D].astype(f32)
        half = slice(D * first, D * first + FF // 2)
        store(ffn_out_grad.at[half], ffn_out_hbm.at[half])
        for j in range(blocks // 2):
            at = slice(D * (first + j), D * (first + j) + D)
            ffn_in_grad[:, at] = whole[0, D * j : D * j + D].astype(f32)
        store(ffn_in_grad.at[:, half], ffn_in_hbm.at[:, half])
    for load in loads[2:]:
        load.wait()
    fourth, at = (whole_t, ROWS_T) if joined else (whole_u, 0)
    for j in range(2):
        attn_in_grad[0, j] = whole_t[0, D * j : D * j + D].astype(f32)
    attn_in_grad[0, 2] = whole_t[1, :D].astype(f32)
    attn_in_grad[1, 0] = fourth[0, at : at + D].astype(f32)
    attn_in_grad[1, 1] = whole_k[:D].astype(f32)
    attn_in_grad[1, 2] = whole_k[D : 2 * D].astype(f32)
    store(attn_in_grad, attn_in_hbm)
    attn_out_grad[0] = fourth[1, at : at + D].astype(f32)
    attn_out_grad[1] = whole_k[2 * D : 3 * D].astype(f32)
    store(attn_out_grad, attn_out_hbm)
    for j in range(pieces):
        fetch(j).wait()
        write(j).start()
    query_pos_grad[...] = whole_t[1, ROW_POS:ROW_SMALL].astype(f32)[:NQ]
    small = whole_t[1, ROW_SMALL : ROW_SMALL + 32].astype(f32)
    ffn_in_bias_grad[...] = jnp.concatenate([small[j : j + 1] for j in range(blocks)], axis=1)
    ffn_out_bias_grad[...] = small[8:9]
    for j, (own, cross) in enumerate(((16, 19), (17, 14), (18, 9))):
        attn_bias_grad[j, 0:1] = small[own : own + 1]
        attn_bias_grad[j, 1:2] = small[cross : cross + 1]
    for j, (gain, shift) in enumerate(((20, 21), (12, 13), (10, 11))):
        norm_gain_grad[j : j + 1] = small[gain : gain + 1]
        norm_bias_grad[j : j + 1] = small[shift : shift + 1]
    for j in range(pieces):
        write(j).wait()
    for copy in stores:
        copy.wait()


def body(
    pages,
    queries,
    memory,
    quarter_turns,
    token_order,
    lengths,
    attn_in,
    attn_out,
    attn_bias,
    ffn_in,
    ffn_in_bias,
    ffn_out,
    ffn_out_bias,
    norm_gain,
    norm_bias,
    query_pos,
    out_grad,
):
    tokens = memory.shape[1]
    chunks = tokens // CHUNK
    groups_f, groups_t, groups_k = sum_groups(pages)
    joined = fourth_joins(pages)
    summed = [
        (padded(ROWS_F, pages), groups_f),
        (padded(ROWS_F, pages), groups_f),
        (padded(ROWS_T + (ROWS_U if joined else 0), pages), groups_t),
        (padded(ROWS_K, 2 * pages), groups_k),
        (TILE if joined else padded(ROWS_U, pages), groups_t),
    ]
    whole_shapes = [(rows, D) if groups is groups_k else (2, rows, D) for rows, groups in summed]
    sum_buffers = []
    for (rows, groups), shape in zip(summed, whole_shapes):
        landing = max(TILE, PageSum.landing_rows(pages, groups, rows))
        sum_buffers += [pltpu.VMEM(each, bf16) for each in ((rows, D), (landing, D), shape)]
    copies = 32
    vmem = pl.BlockSpec(memory_space=pltpu.VMEM)
    smem = pl.BlockSpec(memory_space=pltpu.SMEM)
    anywhere = pl.BlockSpec(memory_space=pl.ANY)
    parts = pl.pallas_call(
        functools.partial(layer_kernel, tokens, pages),
        out_shape=[
            jax.ShapeDtypeStruct((NQ, D), bf16),
            jax.ShapeDtypeStruct((NQ, D), bf16),
            jax.ShapeDtypeStruct((1, tokens, D), bf16),
            *(jax.ShapeDtypeStruct(shape, bf16) for shape in whole_shapes),
        ],
        in_specs=[
            vmem,
            anywhere,
            smem,
            vmem,
            smem,
            vmem,
            vmem,
            vmem,
            anywhere,
            vmem,
            anywhere,
            vmem,
            vmem,
            vmem,
            vmem,
            vmem,
            vmem,
        ],
        out_specs=[vmem, vmem] + [anywhere] * 6,
        scratch_shapes=[
            pltpu.VMEM((tokens, D), bf16),
            pltpu.VMEM((tokens, D), bf16),
            pltpu.VMEM((tokens, HQ), bf16),
            pltpu.VMEM((tokens, HQ), bf16),
            pltpu.VMEM((1, tokens), f32),
            pltpu.VMEM((D, HQ), bf16),
            pltpu.VMEM((D, HQ), bf16),
            pltpu.VMEM((2 * HQ, D), bf16),
            pltpu.VMEM((4 * SIDE, D), bf16),
            pltpu.VMEM((8, HQ), f32),
            pltpu.VMEM((8, HQ), f32),
            pltpu.VMEM((chunks, HQ), f32),
            pltpu.VMEM((chunks, HQ), f32),
            pltpu.VMEM((8, HQ), f32),
            pltpu.VMEM((D, HQ), f32),
            pltpu.VMEM((3, NP, D), f32),
            pltpu.VMEM((D, NP), bf16),
            pltpu.VMEM((D, NP), bf16),
            pltpu.VMEM((2 * HEADS, NP), f32),
            pltpu.VMEM((2 * HEADS, NP), f32),
            pltpu.VMEM((D, NP), bf16),
            pltpu.VMEM((D, NP), bf16),
            pltpu.VMEM((32, D), f32),
            *sum_buffers,
            pltpu.SemaphoreType.DMA((8,)),
            pltpu.SemaphoreType.DMA((chunks,)),
            pltpu.SemaphoreType.DMA((6,)),
            *[pltpu.SemaphoreType.DMA((copies,))] * 10,
        ],
        compiler_params=pltpu.CompilerParams(
            collective_id=0, has_side_effects=True, vmem_limit_bytes=127 * 512 * 1024
        ),
        cost_estimate=pl.CostEstimate(
            flops=2 * 8 * tokens * HQ * D, bytes_accessed=20 << 20, transcendentals=tokens * HQ
        ),
        name="decoder_layer",
    )(
        queries,
        memory,
        quarter_turns,
        token_order,
        lengths,
        attn_in,
        attn_out,
        attn_bias.transpose(1, 0, 2),
        ffn_in,
        ffn_in_bias,
        ffn_out,
        ffn_out_bias,
        norm_gain,
        norm_bias,
        query_pos,
        out_grad,
        jnp.asarray(position_table()),
    )
    outs = pl.pallas_call(
        functools.partial(finish_kernel, joined),
        out_shape=[
            jax.ShapeDtypeStruct((1, NQ, D), bf16),
            jax.ShapeDtypeStruct((1, NQ, D), bf16),
            jax.ShapeDtypeStruct((1, tokens, D), bf16),
            jax.ShapeDtypeStruct((2, 3, D, D), f32),
            jax.ShapeDtypeStruct((2, D, D), f32),
            jax.ShapeDtypeStruct((3, 2, D), f32),
            jax.ShapeDtypeStruct((D, FF), f32),
            jax.ShapeDtypeStruct((1, FF), f32),
            jax.ShapeDtypeStruct((FF, D), f32),
            jax.ShapeDtypeStruct((1, D), f32),
            jax.ShapeDtypeStruct((3, D), f32),
            jax.ShapeDtypeStruct((3, D), f32),
            jax.ShapeDtypeStruct((NQ, D), f32),
        ],
        in_specs=[vmem, vmem] + [anywhere] * 6,
        out_specs=[vmem, vmem, anywhere, anywhere, anywhere, vmem, anywhere, vmem, anywhere] + [vmem] * 4,
        scratch_shapes=[
            pltpu.VMEM((tokens, D), bf16),
            *(pltpu.VMEM(shape, bf16) for shape in whole_shapes),
            pltpu.VMEM((2, 3, D, D), f32),
            pltpu.VMEM((2, D, D), f32),
            pltpu.VMEM((D, FF), f32),
            pltpu.VMEM((FF, D), f32),
            pltpu.SemaphoreType.DMA((8,)),
            pltpu.SemaphoreType.DMA((8,)),
            pltpu.SemaphoreType.DMA((5,)),
            pltpu.SemaphoreType.DMA((6,)),
        ],
        compiler_params=pltpu.CompilerParams(vmem_limit_bytes=62 * 1024 * 1024),
        name="write_outputs",
    )(*parts)
    return (
        *outs[:5],
        outs[5].transpose(1, 0, 2),
        outs[6],
        outs[7].reshape(FF),
        outs[8],
        outs[9].reshape(D),
        *outs[10:],
    )


def solution(mesh):
    in_specs = (
        P("dp", None, None),
        P("dp", "blk", None),
        P("dp"),
        P("dp", "blk"),
        P("dp"),
        P(),
        P(),
        P(),
        P(),
        P(),
        P(),
        P(),
        P(),
        P(),
        P(),
        P("dp", None, None),
    )
    out_specs = (
        P("dp", None, None),
        P("dp", None, None),
        P("dp", "blk", None),
        P(),
        P(),
        P(),
        P(),
        P(),
        P(),
        P(),
        P(),
        P(),
        P(),
    )
    layer = functools.partial(body, mesh.shape["dp"])
    return jax.shard_map(layer, mesh=mesh, in_specs=in_specs, out_specs=out_specs, check_vma=False)
```

```python
import functools
import math

import jax
import jax.numpy as jnp
import numpy as np
from jax import lax
from jax.experimental import pallas as pl
from jax.experimental.pallas import tpu as pltpu
from jax.sharding import PartitionSpec as P

D = 256
HEADS = 8
HD = D // HEADS
SIDE = 128
NQ = 125
NP = 128
HQ = HEADS * NP
PAIR = 2 * NP
FF = 2048
CHUNK = 1024

masked_score = -1e30
norm_eps = 1e-05
scale = 1.0 / math.sqrt(HD)
log2e = math.log2(math.e)

bf16 = jnp.bfloat16
f32 = jnp.float32

ROWS_F = FF
ROW_POS = 2 * D
ROW_SMALL = 2 * D + NP
ROWS_T = 3 * D
ROWS_K = 3 * D
TILE = 16


def axes_of(pages):
    axes = {"core": (2, 1), "y": (2, 2)}
    stride = 4
    while stride < pages:
        radix = 4 if pages // stride % 4 == 0 else 2
        axes["z%d" % (len(axes) - 2)] = (radix, stride)
        stride *= radix
    axes["x"] = (2, 0)
    return axes


def far_axes(pages):
    return [(name,) for name in axes_of(pages) if name.startswith("z")]


def sum_groups(pages):
    far = far_axes(pages)
    return [("core",), ("y",), *far], [("core", "y"), *far], [("core",), ("x",), ("y",), *far]


def padded(rows, pages):
    unit = TILE * pages
    return (rows + unit - 1) // unit * unit


def position_table():
    half = D // 2
    channel = np.arange(half)
    inverse = np.exp((channel // 2).astype(np.float32) * np.float32(-2.0 * math.log(10000.0) / half))
    angle = (np.arange(SIDE, dtype=np.float32) + 1.0) * np.float32(2.0 * math.pi / SIDE)
    angle = angle[:, None] * inverse
    return np.where(channel % 2 == 0, np.sin(angle), np.cos(angle)).astype(np.float32)


def dot(a, b):
    return jnp.dot(a, b, preferred_element_type=f32)


def dot_nt(a, b):
    return lax.dot_general(a, b, (((1,), (1,)), ((), ())), preferred_element_type=f32)


def dot_tn(a, b):
    return lax.dot_general(a, b, (((0,), (0,)), ((), ())), preferred_element_type=f32)


def row_total(values):
    return jnp.sum(values.astype(f32), axis=0, keepdims=True)


def norm_forward(values):
    average = jnp.mean(values, axis=-1, keepdims=True)
    centred = values - average
    variance = jnp.mean(centred * centred, axis=-1, keepdims=True)
    rstd = lax.rsqrt(variance + norm_eps)
    return centred * rstd, rstd


def norm_backward(grad, normed, rstd, gain):
    grad_normed = grad * gain
    first = jnp.mean(grad_normed, axis=-1, keepdims=True)
    second = jnp.mean(grad_normed * normed, axis=-1, keepdims=True)
    grad_in = rstd * (grad_normed - first - normed * second)
    return grad_in, row_total(grad * normed), row_total(grad)


def spread_rows(rows):
    head = lax.broadcasted_iota(jnp.int32, (NP, D), 1) // HD
    return jnp.concatenate(
        [jnp.where(head == h, rows, 0.0) for h in range(HEADS)], axis=0
    ).astype(bf16)


def spread_cols(cols):
    head = lax.broadcasted_iota(jnp.int32, (D, NP), 0) // HD
    return jnp.concatenate(
        [jnp.where(head == h, cols, 0.0) for h in range(HEADS)], axis=1
    ).astype(bf16)


def own_heads(full):
    return jnp.concatenate(
        [full[HD * h : HD * h + HD, NP * h : NP * h + NP] for h in range(HEADS)], axis=0
    )


def project_heads(weight_t, sums):
    high = sums.astype(bf16)
    low = (sums - high.astype(f32)).astype(bf16)
    return own_heads(dot(weight_t, high) + dot(weight_t, low))


def own_blocks(pairs):
    parts = []
    for pair in pairs:
        parts += [pair[:HD, :NP], pair[HD:, NP:]]
    return jnp.concatenate(parts, axis=0)


def head_rows(row):
    return jnp.concatenate([row[:, NP * h : NP * h + NP] for h in range(HEADS)], axis=0)


def head_line(rows):
    return jnp.concatenate([rows[h : h + 1] for h in range(HEADS)], axis=1)


def per_channel(rows):
    return jnp.concatenate(
        [jnp.broadcast_to(rows[h : h + 1], (HD, NP)) for h in range(HEADS)], axis=0
    )


def head_sums(cols):
    return jnp.concatenate(
        [jnp.sum(cols[HD * h : HD * h + HD], axis=0, keepdims=True) for h in range(HEADS)], axis=0
    )


def pair_cols(p):
    return slice(PAIR * p, PAIR * p + PAIR)


def pair_rows(p):
    return slice(2 * HD * p, 2 * HD * p + 2 * HD)


class Place:
    def __init__(self, pages):
        self.axes = axes_of(pages)
        self.page = lax.axis_index("dp")
        self.member = lax.axis_index("blk")
        self.digit = {
            name: self.member if name == "x" else lax.rem(self.page // stride, radix)
            for name, (radix, stride) in self.axes.items()
        }

    def size(self, group):
        return math.prod(self.axes[name][0] for name in group)

    def index(self, group):
        index = 0
        for name in group:
            index = index * self.axes[name][0] + self.digit[name]
        return index

    def peer(self, group, hop):
        index = lax.rem(self.index(group) + hop, self.size(group))
        page, member, rest = self.page, self.member, index
        for name in reversed(group):
            radix, stride = self.axes[name]
            digit = lax.rem(rest, radix)
            rest = rest // radix
            if name == "x":
                member = digit
            else:
                page = page + (digit - self.digit[name]) * stride
        return (page, member), index


class PageSum:
    def __init__(self, place, groups, back, rows, landing, whole, sent, arrived):
        self.place, self.groups, self.back = place, groups, back
        self.rows, self.landing, self.whole = rows, landing, whole
        self.sent, self.arrived = sent, arrived
        self.slots = 0
        self.extents = [rows.shape[0]]
        self.bases = [0]
        self.landings = []
        at = 0
        for group in groups:
            size = place.size(group)
            extent = self.extents[-1] // size
            self.landings.append(at)
            at += (size - 1) * extent
            self.bases.append(pl.multiple_of(self.bases[-1] + place.index(group) * extent, TILE))
            self.extents.append(extent)
        last = len(groups)
        moves = [self.scatter_moves(s) for s in range(last)]
        near = {"all": 0, "across": 1, "sides": 2}[back]
        moves += [self.gather_moves(s) for s in range(last - 1, near - 1, -1)]
        if back == "sides":
            moves += [self.side_moves(), self.corner_moves(), self.core_moves()]
        elif back == "across":
            moves += [self.across_moves(), self.core_moves()]
        self.phases = [functools.partial(self.step, moves, k) for k in range(len(moves) + 1)]

    @staticmethod
    def landing_rows(pages, groups, rows):
        axes = axes_of(pages)
        total, extent = 0, rows
        for group in groups:
            size = math.prod(axes[name][0] for name in group)
            extent //= size
            total += (size - 1) * extent
        return total

    def step(self, moves, k):
        last = len(self.groups)
        if k > 0:
            for move in moves[k - 1]:
                self.copy(*move).wait()
        if 0 < k <= last:
            total = self.scatter_sum(k - 1)
            region = pl.ds(self.bases[k], self.extents[k])
            if k < last:
                self.rows[region] = total
            elif len(self.whole.shape) == 3:
                self.whole[self.place.member, region] = total
            else:
                self.whole[region] = total
        if k < len(moves):
            for move in moves[k]:
                self.copy(*move).start()

    def copy(self, slot, source, target, device):
        return pltpu.make_async_remote_copy(
            src_ref=source(),
            dst_ref=target(),
            send_sem=self.sent.at[slot],
            recv_sem=self.arrived.at[slot],
            device_id=device,
            device_id_type=pl.DeviceIdType.MESH,
        )

    def new_slot(self):
        self.slots += 1
        return self.slots - 1

    def same(self, device, view):
        return (self.new_slot(), view, view, device)

    def scatter_moves(self, step):
        group = self.groups[step]
        extent = self.extents[step + 1]
        moves = []
        for hop in range(1, self.place.size(group)):
            device, other = self.place.peer(group, hop)
            start = pl.multiple_of(self.bases[step] + other * extent, TILE)
            landing = self.landings[step] + (hop - 1) * extent
            moves.append(
                (
                    self.new_slot(),
                    functools.partial(self.part, self.rows, start, extent),
                    functools.partial(self.part, self.landing, landing, extent),
                    device,
                )
            )
        return moves

    @staticmethod
    def part(ref, start, extent):
        return ref.at[pl.ds(start, extent)]

    def half(self, member, start, extent):
        if len(self.whole.shape) == 3:
            return self.whole.at[member, pl.ds(start, extent)]
        return self.whole.at[pl.ds(start, extent)]

    def scatter_sum(self, step):
        extent = self.extents[step + 1]
        total = self.rows[pl.ds(self.bases[step + 1], extent)].astype(f32)
        for hop in range(1, self.place.size(self.groups[step])):
            landing = self.landings[step] + (hop - 1) * extent
            total = total + self.landing[pl.ds(landing, extent)].astype(f32)
        return total.astype(bf16)

    def gather_moves(self, step):
        group = self.groups[step]
        view = functools.partial(self.half, self.place.member, self.bases[step + 1], self.extents[step + 1])
        return [
            self.same(self.place.peer(group, hop)[0], view) for hop in range(1, self.place.size(group))
        ]

    def own_quarter(self):
        step = 2 if len(self.groups[0]) == 1 else 1
        return self.bases[step], self.extents[step]

    def side_moves(self):
        view = functools.partial(self.half, self.place.member, *self.own_quarter())
        return [self.same(self.place.peer((name,), 1)[0], view) for name in ("y", "x")]

    def corner_moves(self):
        base, extent = self.own_quarter()
        other = pl.multiple_of(base + (1 - 2 * self.place.digit["y"]) * extent, TILE)
        view = functools.partial(self.half, self.place.member, other, extent)
        return [self.same(self.place.peer(("x",), 1)[0], view)]

    def across_moves(self):
        view = functools.partial(self.half, self.place.member, *self.own_quarter())
        return [self.same(self.place.peer(("x", "y"), hop)[0], view) for hop in range(1, 4)]

    def core_moves(self):
        extent = self.extents[0] // 2
        start = pl.multiple_of(self.place.digit["core"] * extent, TILE)
        device, _ = self.place.peer(("core",), 1)
        return [self.same(device, functools.partial(self.half, m, start, extent)) for m in range(2)]


def clear_rest(ref, used):
    if ref.shape[0] > used:
        ref[used:] = jnp.zeros((ref.shape[0] - used, D), ref.dtype)


def layer_kernel(
    tokens,
    pages,
    queries_in,
    memory_hbm,
    turns_in,
    order_in,
    lengths_in,
    attn_in,
    attn_out,
    attn_bias,
    ffn_in_hbm,
    ffn_in_bias,
    ffn_out_hbm,
    ffn_out_bias,
    norm_gain,
    norm_bias,
    pos_in,
    out_grad_in,
    table_in,
    result_out,
    queries_grad_out,
    memory_grad_hbm,
    whole_f_hbm,
    whole_t_hbm,
    whole_k_hbm,
    memory_s,
    key_in_s,
    probs_s,
    grad_scores_s,
    code_s,
    query_kt,
    grad_vt,
    back_s,
    table_s,
    top_s,
    highest_s,
    shifts_s,
    factor_s,
    total_s,
    mixed_s,
    pad_s,
    send_a,
    recv_a,
    send_t,
    recv_t,
    send_b,
    recv_b,
    small_s,
    rows_f,
    landing_f,
    whole_f,
    rows_t,
    landing_t,
    whole_t,
    rows_k,
    landing_k,
    whole_k,
    load_sem,
    store_sem,
    link_sem,
    sent_f,
    arrived_f,
    sent_t,
    arrived_t,
    sent_k,
    arrived_k,
):
    member = lax.axis_index("blk")
    partner = (lax.axis_index("dp"), 1 - member)
    chunks = tokens // CHUNK

    place = Place(pages)
    groups_f, groups_t, groups_k = sum_groups(pages)
    sum_f = PageSum(place, groups_f, "sides", rows_f, landing_f, whole_f, sent_f, arrived_f)
    sum_t = PageSum(place, groups_t, "across", rows_t, landing_t, whole_t, sent_t, arrived_t)
    sum_k = PageSum(place, groups_k, "all", rows_k, landing_k, whole_k, sent_k, arrived_k)

    barrier = pltpu.get_barrier_semaphore()
    peers = [
        place.peer(group, hop)[0]
        for group in [("x", "core", "y"), *far_axes(pages)]
        for hop in range(1, place.size(group))
    ]
    for peer in peers:
        pl.semaphore_signal(barrier, inc=1, device_id=peer, device_id_type=pl.DeviceIdType.MESH)

    load_memory = pltpu.make_async_copy(memory_hbm.at[0], memory_s, load_sem.at[0])
    half = FF // 2
    ffn_in_s = [grad_scores_s.at[D * k : D * k + D] for k in range(2)]
    ffn_out_s = grad_scores_s.at[2 * D : 2 * D + FF, :D]
    free = 2 * D + FF
    active_s = [grad_scores_s.at[free + NP * k : free + NP * k + NP] for k in range(2)]
    slope_s = [grad_scores_s.at[free + NP * k : free + NP * k + NP] for k in range(2, 4)]
    load_ffn = [
        pltpu.make_async_copy(ffn_in_hbm.at[:, half * k : half * k + half], ffn_in_s[k], load_sem.at[1 + k])
        for k in range(2)
    ]
    load_ffn.append(pltpu.make_async_copy(ffn_out_hbm, ffn_out_s, load_sem.at[3]))
    load_memory.start()
    for load in load_ffn:
        load.start()

    pairs = [attn_bias[j].astype(f32) for j in range(3)]
    bias = jnp.concatenate([pair[k : k + 1] for k in range(2) for pair in pairs], axis=0)
    gain = norm_gain[...].astype(f32)
    shift = norm_bias[...].astype(f32)

    order = order_in[...]
    turn = turns_in[0]
    row_at = order >> 7
    col_at = order & 127
    top = SIDE - 1
    row_new = jnp.where(
        turn == 0, row_at, jnp.where(turn == 1, col_at, jnp.where(turn == 2, top - row_at, top - col_at))
    )
    col_new = jnp.where(
        turn == 0, col_at, jnp.where(turn == 1, top - row_at, jnp.where(turn == 2, top - col_at, row_at))
    )
    past = jnp.where(order < lengths_in[0], 0, SIDE * SIDE)
    code_s[...] = (row_new * SIDE + col_new + past).astype(f32)

    pad_s[...] = jnp.zeros_like(pad_s)
    pad_s[0, :NQ] = queries_in[0].astype(f32)
    pad_s[1, :NQ] = pos_in[...].astype(f32)
    pad_s[2, :NQ] = out_grad_in[0].astype(f32)
    queries_f = pad_s[0]
    pos_f = pad_s[1]
    queries_b = queries_f.astype(bf16)
    mixed_q = (queries_f + pos_f).astype(bf16)
    query_self = (dot(mixed_q, attn_in[0, 0]) + bias[0:1]).astype(bf16)
    key_self = dot(mixed_q, attn_in[0, 1]).astype(bf16)
    value_self = (dot(queries_b, attn_in[0, 2]) + bias[1:2]).astype(bf16)
    scores = dot(key_self, spread_cols(query_self.astype(f32).T)) * scale
    own_key = lax.broadcasted_iota(jnp.int32, (NP, HQ), 0) < NQ
    scores = jnp.where(own_key, scores, masked_score)
    raised = jnp.exp(scores - jnp.max(scores, axis=0, keepdims=True))
    probs_self = raised / jnp.sum(raised, axis=0, keepdims=True)
    probs_self_b = probs_self.astype(bf16)
    value_t = value_self.astype(f32).T.astype(bf16)
    attended = own_blocks(
        [dot(value_t[pair_rows(p)], probs_self_b[:, pair_cols(p)]) for p in range(4)]
    ).T.astype(bf16)
    first_normed, first_rstd = norm_forward(queries_f + dot(attended, attn_out[0]) + bias[2:3])
    first = first_normed * gain[0:1] + shift[0:1]
    cross_q = (first + pos_f).astype(bf16)
    query_c = (dot(cross_q, attn_in[1, 0]) + bias[3:4]).astype(bf16)
    query_x = spread_rows(query_c.astype(f32))
    query_k = dot(attn_in[1, 1], spread_cols(query_c.astype(f32).T))
    query_kt[...] = (query_k * (scale * log2e)).astype(bf16)
    back_s[:HQ] = (dot_nt(query_x, attn_in[1, 1]) * scale).astype(bf16)
    table = table_in[...]
    nothing = jnp.zeros((SIDE, D // 2), f32)
    table = jnp.concatenate(
        [jnp.concatenate([table, nothing], axis=1), jnp.concatenate([nothing, table], axis=1)], axis=0
    )
    table_high = table.astype(bf16)
    table_s[: 2 * SIDE] = table_high
    table_s[2 * SIDE :] = (table - table_high.astype(f32)).astype(bf16)

    load_memory.wait()
    def mask_view(i):
        side, place = i // (chunks // 2), lax.rem(i, chunks // 2)
        return grad_scores_s.at[
            pl.ds(pl.multiple_of(tokens // 2 + place * CHUNK, CHUNK), CHUNK),
            pl.ds(pl.multiple_of(side * NP, NP), NP),
        ]

    lane = lax.broadcasted_iota(jnp.int32, (CHUNK, NP), 1)

    @pl.loop(0, chunks)
    def _(i):
        rows = pl.ds(pl.multiple_of(i * CHUNK, CHUNK), CHUNK)
        line = code_s[:, rows]
        code = jnp.concatenate(
            [
                jnp.broadcast_to(line[:, NP * j : NP * j + NP], (NP, NP)).T
                for j in range(CHUNK // NP)
            ],
            axis=0,
        ).astype(jnp.int32)
        row_hot = jnp.where(((code >> 7) & 127) == lane, 1.0, 0.0).astype(bf16)
        col_hot = jnp.where((code & 127) == lane, 1.0, 0.0).astype(bf16)
        hot = jnp.concatenate([row_hot, col_hot, row_hot, col_hot], axis=1)
        masked = jnp.where(code < SIDE * SIDE, 0.0, masked_score)
        mask_view(i)[...] = masked.astype(bf16)
        key_in_s[rows] = (memory_s[rows].astype(f32) + dot(hot, table_s[...])).astype(bf16)

    def score_pair(p, key_in, mask, score_s):
        cols = pair_cols(p)
        part = dot(key_in, query_kt[:, cols]) + mask
        score_s[:, cols] = part
        top_s[:, cols] = jnp.max(part.reshape(CHUNK // 8, 8, PAIR), axis=0)

    def score_operands(i):
        rows = pl.ds(pl.multiple_of(i * CHUNK, CHUNK), CHUNK)
        mask = mask_view(i)[...].astype(f32)
        return key_in_s[rows], jnp.concatenate([mask, mask], axis=1)

    def attend_all(score_s):
        operands = score_operands(0)
        for p in range(4):
            score_pair(p, *operands, score_s)

        @pl.loop(0, chunks)
        def _(i):
            rows = pl.ds(pl.multiple_of(i * CHUNK, CHUNK), CHUNK)
            memory_ct = memory_s[rows].T
            operands = score_operands(jnp.minimum(i + 1, chunks - 1))
            for p in range(4):
                cols = pair_cols(p)
                before = highest_s[0:1, cols]
                highest = jnp.maximum(before, jnp.max(top_s[:, cols], axis=0, keepdims=True))
                highest_s[0:1, cols] = highest
                shifts_s[pl.ds(i, 1), cols] = highest
                fade = jnp.exp2(before - highest)
                raised = jnp.exp2(score_s[:, cols] - highest)
                sums = jnp.sum(raised.reshape(CHUNK // 8, 8, PAIR), axis=0)
                total_s[:, cols] = total_s[:, cols] * fade + sums
                probs_s[rows, cols] = raised.astype(bf16)
                mixed_s[:, cols] = mixed_s[:, cols] * fade + dot(memory_ct, probs_s[rows, cols])
                score_pair(p, *operands, score_s)

    highest_s[0:1] = jnp.full((1, HQ), -3e38, f32)
    total_s[...] = jnp.zeros_like(total_s)
    mixed_s[...] = jnp.zeros_like(mixed_s)
    pl.run_scoped(attend_all, pltpu.VMEM((CHUNK, HQ), f32))
    highest_own = highest_s[0:1]
    total_own = jnp.sum(total_s[...], axis=0, keepdims=True)

    value_wt = attn_in[1, 2].astype(f32).T.astype(bf16)
    key_wt = attn_in[1, 1].astype(f32).T.astype(bf16)
    send_a[...] = project_heads(value_wt, mixed_s[...]).astype(bf16)
    send_t[:HEADS] = head_rows(highest_own)
    send_t[HEADS:] = head_rows(total_own)
    pl.semaphore_wait(barrier, len(peers))
    swap_a = pltpu.make_async_remote_copy(
        src_ref=send_a,
        dst_ref=recv_a,
        send_sem=link_sem.at[0],
        recv_sem=link_sem.at[1],
        device_id=partner,
        device_id_type=pl.DeviceIdType.MESH,
    )
    swap_t = pltpu.make_async_remote_copy(
        src_ref=send_t,
        dst_ref=recv_t,
        send_sem=link_sem.at[4],
        recv_sem=link_sem.at[5],
        device_id=partner,
        device_id_type=pl.DeviceIdType.MESH,
    )
    swap_a.start()
    swap_t.start()
    swap_a.wait()
    swap_t.wait()
    is_first = member == 0
    own, other = send_a[...].astype(f32), recv_a[...].astype(f32)
    left = jnp.where(is_first, own, other)
    right = jnp.where(is_first, other, own)
    own, other = send_t[...], recv_t[...]
    left_t = jnp.where(is_first, own, other)
    right_t = jnp.where(is_first, other, own)
    highest = jnp.maximum(left_t[:HEADS], right_t[:HEADS])
    fade_l = jnp.exp2(left_t[:HEADS] - highest)
    fade_r = jnp.exp2(right_t[:HEADS] - highest)
    total = left_t[HEADS:] * fade_l + right_t[HEADS:] * fade_r
    mixed_t = left * per_channel(fade_l / total) + right * per_channel(fade_r / total)
    log_total = head_line(highest + jnp.log2(total))
    own_share = jnp.exp2(highest_own - log_total)
    factor_s[...] = jnp.exp2(shifts_s[...] - log_total)
    attended_c = (mixed_t.T + bias[4:5]).astype(bf16)

    second_normed, second_rstd = norm_forward(first + dot(attended_c, attn_out[1]) + bias[5:6])
    second = second_normed * gain[1:2] + shift[1:2]
    ffn_input = second.astype(bf16)
    load_ffn[0].wait()
    load_ffn[1].wait()
    blocks = [(j // 4, slice(D * j, D * j + D), slice(j % 4 * D, j % 4 * D + D)) for j in range(FF // D)]
    hidden_bias = ffn_in_bias[...].astype(f32).reshape(1, FF)
    def feed_forward(gate_s):
        for k, cols, part in blocks:
            hidden = dot(ffn_input, ffn_in_s[k][:, part]) + hidden_bias[:, cols]
            half_gate = 0.5 + 0.5 * lax.erf(hidden * math.sqrt(0.5))
            active_s[k][:, part] = (hidden * half_gate).astype(bf16)
            gate_s[:, cols] = half_gate + hidden * jnp.exp(hidden * hidden * -0.5) * (
                1.0 / math.sqrt(2.0 * math.pi)
            )
        load_ffn[2].wait()
        third_normed, third_rstd = norm_forward(
            second
            + dot(active_s[0][...], ffn_out_s[:half])
            + dot(active_s[1][...], ffn_out_s[half:])
            + ffn_out_bias[...].astype(f32).reshape(1, D)
        )
        result_out[...] = (third_normed * gain[2:3] + shift[2:3])[:NQ].astype(bf16)
        grad_third, gain_grad_2, shift_grad_2 = norm_backward(
            pad_s[2], third_normed, third_rstd, gain[2:3]
        )
        grad_branch_f = grad_third.astype(bf16)
        for k, cols, part in blocks:
            grad_hidden = dot_nt(grad_branch_f, ffn_out_s[cols]) * gate_s[:, cols]
            slope_s[k][:, part] = grad_hidden.astype(bf16)
        return grad_third, gain_grad_2, shift_grad_2, grad_branch_f

    grad_third, gain_grad_2, shift_grad_2, grad_branch_f = pl.run_scoped(
        feed_forward, pltpu.VMEM((NP, FF), f32)
    )
    grad_second = grad_third + dot_nt(slope_s[0][...], ffn_in_s[0][...])
    grad_second += dot_nt(slope_s[1][...], ffn_in_s[1][...])
    grad_second_in, gain_grad_1, shift_grad_1 = norm_backward(
        grad_second, second_normed, second_rstd, gain[1:2]
    )
    grad_branch_c = grad_second_in.astype(bf16)
    ffn_input_t = second.T.astype(bf16)

    @pl.when(member == 0)
    def _():
        for k, cols, part in blocks:
            rows_f[cols] = dot(ffn_input_t, slope_s[k][:, part]).astype(bf16)

    @pl.when(member == 1)
    def _():
        for k, cols, part in blocks:
            rows_f[cols] = dot_tn(active_s[k][:, part], grad_branch_f).astype(bf16)

    is_first = member == 0
    out_grad_c = dot_tn(attended_c, grad_branch_c)
    rows_k[2 * D : 3 * D] = jnp.where(is_first, out_grad_c, 0.0).astype(bf16)

    clear_rest(rows_f, ROWS_F)
    clear_rest(rows_t, ROWS_T)
    clear_rest(rows_k, ROWS_K)
    sum_f.phases[0]()
    grad_attended_c = dot_nt(grad_branch_c, attn_out[1]).astype(bf16).astype(f32)
    small_s[:16] = jnp.concatenate(
        [row_total(slope_s[k][:, part]) for k, _, part in blocks]
        + [
            row_total(grad_branch_f),
            row_total(grad_branch_c),
            gain_grad_2,
            shift_grad_2,
            gain_grad_1,
            shift_grad_1,
            row_total(grad_attended_c),
            jnp.zeros((1, D), f32),
        ],
        axis=0,
    )

    grad_attended_t = grad_attended_c.T
    grad_x = spread_rows(grad_attended_c)
    grad_v = dot(attn_in[1, 2], spread_cols(grad_attended_t))
    grad_vt[...] = grad_v.astype(bf16)
    back_s[HQ:] = grad_v.T.astype(bf16)
    inner = head_line(head_sums(grad_attended_t * mixed_t))
    rows_k[D : 2 * D] = dot((mixed_s[...] * own_share).astype(bf16), grad_x).astype(bf16)
    mixed_s[...] = jnp.zeros_like(mixed_s)

    queue_f = sum_f.phases[1:]
    queue_t = list(sum_t.phases)
    queue_k = list(sum_k.phases)

    def take(queue):
        if queue:
            queue.pop(0)()

    def at(i, steps):
        for step, queue in steps:
            pl.when(i == (step * chunks) // 16)(queue.pop(0))

    @pl.loop(0, chunks)
    def _(i):
        rows = pl.ds(pl.multiple_of(i * CHUNK, CHUNK), CHUNK)
        key_ct = key_in_s[rows].T
        memory_c = memory_s[rows]
        for p in range(4):
            cols = pair_cols(p)
            grad_probs = dot(memory_c, grad_vt[:, cols])
            probs = probs_s[rows, cols].astype(f32) * factor_s[pl.ds(i, 1), cols]
            probs_s[rows, cols] = probs.astype(bf16)
            grad_scores_s[rows, cols] = (probs * (grad_probs - inner[:, cols])).astype(bf16)
            mixed_s[:, cols] += dot(key_ct, grad_scores_s[rows, cols])
        at(i, [(3, queue_f), (9, queue_f), (15, queue_f)])

    send_b[...] = (project_heads(key_wt, mixed_s[...]) * scale).astype(bf16)
    swap_b = pltpu.make_async_remote_copy(
        src_ref=send_b,
        dst_ref=recv_b,
        send_sem=link_sem.at[2],
        recv_sem=link_sem.at[3],
        device_id=partner,
        device_id_type=pl.DeviceIdType.MESH,
    )
    swap_b.start()
    query_x = spread_rows(query_c.astype(f32))
    rows_k[:D] = (dot(mixed_s[...].astype(bf16), query_x) * scale).astype(bf16)
    take(queue_k)
    swap_b.wait()
    take(queue_f)
    take(queue_k)
    grad_query_c = (send_b[...].astype(f32) + recv_b[...].astype(f32)).T.astype(bf16)

    cross_pos_grad = dot_nt(grad_query_c, attn_in[1, 0])
    grad_first_in, gain_grad_0, shift_grad_0 = norm_backward(
        grad_second_in + cross_pos_grad, first_normed, first_rstd, gain[0:1]
    )
    grad_branch = grad_first_in.astype(bf16)
    grad_attended = dot_nt(grad_branch, attn_out[0]).astype(bf16).astype(f32)
    take(queue_k)
    grad_probs = dot(value_self, spread_cols(grad_attended.T))
    inner_self = jnp.sum(probs_self * grad_probs, axis=0, keepdims=True)
    grad_scores = (probs_self * (grad_probs - inner_self)).astype(bf16)
    key_t = key_self.astype(f32).T.astype(bf16)
    grad_query_s = (
        own_blocks([dot(key_t[pair_rows(p)], grad_scores[:, pair_cols(p)]) for p in range(4)]) * scale
    ).T.astype(bf16)
    grad_key_s = (dot(grad_scores, spread_rows(query_self.astype(f32))) * scale).astype(bf16)
    grad_value_s = dot(probs_self_b, spread_rows(grad_attended)).astype(bf16)
    grad_mixed_q = dot_nt(grad_query_s, attn_in[0, 0]) + dot_nt(grad_key_s, attn_in[0, 1])
    queries_grad_out[...] = (grad_first_in + grad_mixed_q + dot_nt(grad_value_s, attn_in[0, 2]))[
        :NQ
    ].astype(bf16)
    small_s[16:] = jnp.concatenate(
        [
            row_total(grad_query_s),
            row_total(grad_value_s),
            row_total(grad_branch),
            row_total(grad_query_c),
            gain_grad_0,
            shift_grad_0,
            jnp.zeros((10, D), f32),
        ],
        axis=0,
    )
    @pl.when(member == 0)
    def _():
        rows_t[:D] = dot_tn(mixed_q, grad_query_s).astype(bf16)
        rows_t[D : 2 * D] = dot_tn(mixed_q, grad_key_s).astype(bf16)
        rows_t[2 * D : 3 * D] = dot_tn(queries_b, grad_value_s).astype(bf16)

    @pl.when(member == 1)
    def _():
        rows_t[:D] = dot_tn(cross_q, grad_query_c).astype(bf16)
        rows_t[D : 2 * D] = dot_tn(attended, grad_branch).astype(bf16)
        rows_t[ROW_POS:ROW_SMALL] = (grad_mixed_q + cross_pos_grad).astype(bf16)
        rows_t[ROW_SMALL : ROW_SMALL + 32] = small_s[...].astype(bf16)
        rows_t[ROW_SMALL + 32 : ROWS_T] = jnp.zeros((ROWS_T - ROW_SMALL - 32, D), bf16)

    take(queue_t)
    take(queue_k)
    take(queue_f)

    @pl.loop(0, chunks)
    def _(i):
        rows = pl.ds(pl.multiple_of(i * CHUNK, CHUNK), CHUNK)
        both = jnp.concatenate([grad_scores_s[rows], probs_s[rows]], axis=1)
        memory_s[rows] = dot(both, back_s[...]).astype(bf16)
        pltpu.make_async_copy(memory_s.at[rows], memory_grad_hbm.at[0, rows], store_sem.at[i]).start()
        at(
            i,
            [
                (3, queue_t),
                (4, queue_k),
                (7, queue_t),
                (8, queue_k),
                (9, queue_f),
                (11, queue_t),
                (12, queue_k),
                (15, queue_t),
            ],
        )

    while queue_f:
        take(queue_f)
    stores = [
        pltpu.make_async_copy(whole, target, load_sem.at[4 + k])
        for k, (whole, target) in enumerate(
            (
                (whole_f, whole_f_hbm),
                (whole_t, whole_t_hbm),
                (whole_k, whole_k_hbm),
            )
        )
    ]
    stores[0].start()
    while queue_t or queue_k:
        take(queue_t)
        take(queue_k)
    for store in stores[1:]:
        store.start()

    @pl.loop(0, chunks)
    def _(i):
        rows = pl.ds(pl.multiple_of(i * CHUNK, CHUNK), CHUNK)
        pltpu.make_async_copy(memory_s.at[rows], memory_grad_hbm.at[0, rows], store_sem.at[i]).wait()

    for store in stores:
        store.wait()


def finish_kernel(
    result_in,
    queries_grad_in,
    memory_grad_in,
    whole_f_hbm,
    whole_t_hbm,
    whole_k_hbm,
    result,
    queries_grad,
    memory_grad,
    attn_in_hbm,
    attn_out_hbm,
    attn_bias_grad,
    ffn_in_hbm,
    ffn_in_bias_grad,
    ffn_out_hbm,
    ffn_out_bias_grad,
    norm_gain_grad,
    norm_bias_grad,
    query_pos_grad,
    moved,
    whole_f,
    whole_t,
    whole_k,
    attn_in_grad,
    attn_out_grad,
    ffn_in_grad,
    ffn_out_grad,
    in_sem,
    out_sem,
    sum_sem,
    grad_sem,
):
    pieces = in_sem.shape[0]
    piece = moved.shape[0] // pieces

    def fetch(j):
        rows = pl.ds(piece * j, piece)
        return pltpu.make_async_copy(memory_grad_in.at[0, rows], moved.at[rows], in_sem.at[j])

    def write(j):
        rows = pl.ds(piece * j, piece)
        return pltpu.make_async_copy(moved.at[rows], memory_grad.at[0, rows], out_sem.at[j])

    sums = [(whole_f_hbm, whole_f), (whole_t_hbm, whole_t), (whole_k_hbm, whole_k)]
    loads = [pltpu.make_async_copy(*pair, sum_sem.at[j]) for j, pair in enumerate(sums)]
    for load in loads:
        load.start()
    for j in range(pieces):
        fetch(j).start()
    blocks = FF // D
    stores = []

    def store(source, target):
        stores.append(pltpu.make_async_copy(source, target, grad_sem.at[len(stores)]))
        stores[-1].start()

    result[0] = result_in[...]
    queries_grad[0] = queries_grad_in[...]
    loads[0].wait()
    for k in range(2):
        half = slice(FF // 2 * k, FF // 2 * (k + 1))
        ffn_out_grad[half] = whole_f[1, half].astype(f32)
        store(ffn_out_grad.at[half], ffn_out_hbm.at[half])
    for k in range(2):
        half = slice(FF // 2 * k, FF // 2 * (k + 1))
        for j in range(blocks // 2 * k, blocks // 2 * (k + 1)):
            at = slice(D * j, D * j + D)
            ffn_in_grad[:, at] = whole_f[0, at].astype(f32)
        store(ffn_in_grad.at[:, half], ffn_in_hbm.at[:, half])
    for load in loads[1:]:
        load.wait()
    for j in range(3):
        attn_in_grad[0, j] = whole_t[0, D * j : D * j + D].astype(f32)
    attn_in_grad[1, 0] = whole_t[1, :D].astype(f32)
    attn_in_grad[1, 1] = whole_k[:D].astype(f32)
    attn_in_grad[1, 2] = whole_k[D : 2 * D].astype(f32)
    store(attn_in_grad, attn_in_hbm)
    attn_out_grad[0] = whole_t[1, D : 2 * D].astype(f32)
    attn_out_grad[1] = whole_k[2 * D : 3 * D].astype(f32)
    store(attn_out_grad, attn_out_hbm)
    for j in range(pieces):
        fetch(j).wait()
        write(j).start()
    query_pos_grad[...] = whole_t[1, ROW_POS:ROW_SMALL].astype(f32)[:NQ]
    small = whole_t[1, ROW_SMALL : ROW_SMALL + 32].astype(f32)
    ffn_in_bias_grad[...] = jnp.concatenate([small[j : j + 1] for j in range(blocks)], axis=1)
    ffn_out_bias_grad[...] = small[8:9]
    for j, (own, cross) in enumerate(((16, 19), (17, 14), (18, 9))):
        attn_bias_grad[j, 0:1] = small[own : own + 1]
        attn_bias_grad[j, 1:2] = small[cross : cross + 1]
    for j, (gain, shift) in enumerate(((20, 21), (12, 13), (10, 11))):
        norm_gain_grad[j : j + 1] = small[gain : gain + 1]
        norm_bias_grad[j : j + 1] = small[shift : shift + 1]
    for j in range(pieces):
        write(j).wait()
    for copy in stores:
        copy.wait()


def body(
    pages,
    queries,
    memory,
    quarter_turns,
    token_order,
    lengths,
    attn_in,
    attn_out,
    attn_bias,
    ffn_in,
    ffn_in_bias,
    ffn_out,
    ffn_out_bias,
    norm_gain,
    norm_bias,
    query_pos,
    out_grad,
):
    tokens = memory.shape[1]
    chunks = tokens // CHUNK
    groups_f, groups_t, groups_k = sum_groups(pages)
    summed = [
        (padded(ROWS_F, pages), groups_f),
        (padded(ROWS_T, pages), groups_t),
        (padded(ROWS_K, 2 * pages), groups_k),
    ]
    whole_shapes = [(2, rows, D) for rows, _ in summed[:2]] + [(summed[2][0], D)]
    sum_buffers = []
    for (rows, groups), shape in zip(summed, whole_shapes):
        landing = PageSum.landing_rows(pages, groups, rows)
        sum_buffers += [pltpu.VMEM(each, bf16) for each in ((rows, D), (landing, D), shape)]
    copies = 32
    vmem = pl.BlockSpec(memory_space=pltpu.VMEM)
    smem = pl.BlockSpec(memory_space=pltpu.SMEM)
    anywhere = pl.BlockSpec(memory_space=pl.ANY)
    parts = pl.pallas_call(
        functools.partial(layer_kernel, tokens, pages),
        out_shape=[
            jax.ShapeDtypeStruct((NQ, D), bf16),
            jax.ShapeDtypeStruct((NQ, D), bf16),
            jax.ShapeDtypeStruct((1, tokens, D), bf16),
            *(jax.ShapeDtypeStruct(shape, bf16) for shape in whole_shapes),
        ],
        in_specs=[
            vmem,
            anywhere,
            smem,
            vmem,
            smem,
            vmem,
            vmem,
            vmem,
            anywhere,
            vmem,
            anywhere,
            vmem,
            vmem,
            vmem,
            vmem,
            vmem,
            vmem,
        ],
        out_specs=[vmem, vmem] + [anywhere] * 4,
        scratch_shapes=[
            pltpu.VMEM((tokens, D), bf16),
            pltpu.VMEM((tokens, D), bf16),
            pltpu.VMEM((tokens, HQ), bf16),
            pltpu.VMEM((tokens, HQ), bf16),
            pltpu.VMEM((1, tokens), f32),
            pltpu.VMEM((D, HQ), bf16),
            pltpu.VMEM((D, HQ), bf16),
            pltpu.VMEM((2 * HQ, D), bf16),
            pltpu.VMEM((4 * SIDE, D), bf16),
            pltpu.VMEM((8, HQ), f32),
            pltpu.VMEM((8, HQ), f32),
            pltpu.VMEM((chunks, HQ), f32),
            pltpu.VMEM((chunks, HQ), f32),
            pltpu.VMEM((8, HQ), f32),
            pltpu.VMEM((D, HQ), f32),
            pltpu.VMEM((3, NP, D), f32),
            pltpu.VMEM((D, NP), bf16),
            pltpu.VMEM((D, NP), bf16),
            pltpu.VMEM((2 * HEADS, NP), f32),
            pltpu.VMEM((2 * HEADS, NP), f32),
            pltpu.VMEM((D, NP), bf16),
            pltpu.VMEM((D, NP), bf16),
            pltpu.VMEM((32, D), f32),
            *sum_buffers,
            pltpu.SemaphoreType.DMA((8,)),
            pltpu.SemaphoreType.DMA((chunks,)),
            pltpu.SemaphoreType.DMA((6,)),
            *[pltpu.SemaphoreType.DMA((copies,))] * 6,
        ],
        compiler_params=pltpu.CompilerParams(
            collective_id=0, has_side_effects=True, vmem_limit_bytes=127 * 512 * 1024
        ),
        cost_estimate=pl.CostEstimate(
            flops=2 * 8 * tokens * HQ * D, bytes_accessed=20 << 20, transcendentals=tokens * HQ
        ),
        name="decoder_layer",
    )(
        queries,
        memory,
        quarter_turns,
        token_order,
        lengths,
        attn_in,
        attn_out,
        attn_bias.transpose(1, 0, 2),
        ffn_in,
        ffn_in_bias,
        ffn_out,
        ffn_out_bias,
        norm_gain,
        norm_bias,
        query_pos,
        out_grad,
        jnp.asarray(position_table()),
    )
    outs = pl.pallas_call(
        finish_kernel,
        out_shape=[
            jax.ShapeDtypeStruct((1, NQ, D), bf16),
            jax.ShapeDtypeStruct((1, NQ, D), bf16),
            jax.ShapeDtypeStruct((1, tokens, D), bf16),
            jax.ShapeDtypeStruct((2, 3, D, D), f32),
            jax.ShapeDtypeStruct((2, D, D), f32),
            jax.ShapeDtypeStruct((3, 2, D), f32),
            jax.ShapeDtypeStruct((D, FF), f32),
            jax.ShapeDtypeStruct((1, FF), f32),
            jax.ShapeDtypeStruct((FF, D), f32),
            jax.ShapeDtypeStruct((1, D), f32),
            jax.ShapeDtypeStruct((3, D), f32),
            jax.ShapeDtypeStruct((3, D), f32),
            jax.ShapeDtypeStruct((NQ, D), f32),
        ],
        in_specs=[vmem, vmem] + [anywhere] * 4,
        out_specs=[vmem, vmem, anywhere, anywhere, anywhere, vmem, anywhere, vmem, anywhere] + [vmem] * 4,
        scratch_shapes=[
            pltpu.VMEM((tokens, D), bf16),
            *(pltpu.VMEM(shape, bf16) for shape in whole_shapes),
            pltpu.VMEM((2, 3, D, D), f32),
            pltpu.VMEM((2, D, D), f32),
            pltpu.VMEM((D, FF), f32),
            pltpu.VMEM((FF, D), f32),
            pltpu.SemaphoreType.DMA((8,)),
            pltpu.SemaphoreType.DMA((8,)),
            pltpu.SemaphoreType.DMA((3,)),
            pltpu.SemaphoreType.DMA((6,)),
        ],
        compiler_params=pltpu.CompilerParams(vmem_limit_bytes=62 * 1024 * 1024),
        name="write_outputs",
    )(*parts)
    return (
        *outs[:5],
        outs[5].transpose(1, 0, 2),
        outs[6],
        outs[7].reshape(FF),
        outs[8],
        outs[9].reshape(D),
        *outs[10:],
    )


def solution(mesh):
    in_specs = (
        P("dp", None, None),
        P("dp", "blk", None),
        P("dp"),
        P("dp", "blk"),
        P("dp"),
        P(),
        P(),
        P(),
        P(),
        P(),
        P(),
        P(),
        P(),
        P(),
        P(),
        P("dp", None, None),
    )
    out_specs = (
        P("dp", None, None),
        P("dp", None, None),
        P("dp", "blk", None),
        P(),
        P(),
        P(),
        P(),
        P(),
        P(),
        P(),
        P(),
        P(),
        P(),
    )
    layer = functools.partial(body, mesh.shape["dp"])
    return jax.shard_map(layer, mesh=mesh, in_specs=in_specs, out_specs=out_specs, check_vma=False)
```

```python
import functools
import math

import jax
import jax.numpy as jnp
import numpy as np
from jax import lax
from jax.experimental import pallas as pl
from jax.experimental.pallas import tpu as pltpu
from jax.sharding import PartitionSpec as P

D = 256
HEADS = 8
HD = D // HEADS
SIDE = 128
NQ = 125
NP = 128
HQ = HEADS * NP
PAIR = 2 * NP
FF = 2048
CHUNK = 1024

masked_score = -1e30
norm_eps = 1e-05
scale = 1.0 / math.sqrt(HD)
log2e = math.log2(math.e)

bf16 = jnp.bfloat16
f32 = jnp.float32

ROWS_F = FF
ROW_POS = 2 * D
ROW_SMALL = 2 * D + NP
ROWS_T = 3 * D
ROWS_K = 3 * D
TILE = 16


def axes_of(pages):
    axes = {"core": (2, 1), "y": (2, 2)}
    stride = 4
    while stride < pages:
        radix = 4 if pages // stride % 4 == 0 else 2
        axes["z%d" % (len(axes) - 2)] = (radix, stride)
        stride *= radix
    axes["x"] = (2, 0)
    return axes


def far_axes(pages):
    return [(name,) for name in axes_of(pages) if name.startswith("z")]


def sum_groups(pages):
    far = far_axes(pages)
    return [("core",), ("y",), *far], [("core", "y"), *far], [("core",), ("x",), ("y",), *far]


def padded(rows, pages):
    unit = TILE * pages
    return (rows + unit - 1) // unit * unit


def position_table():
    half = D // 2
    channel = np.arange(half)
    inverse = np.exp((channel // 2).astype(np.float32) * np.float32(-2.0 * math.log(10000.0) / half))
    angle = (np.arange(SIDE, dtype=np.float32) + 1.0) * np.float32(2.0 * math.pi / SIDE)
    angle = angle[:, None] * inverse
    return np.where(channel % 2 == 0, np.sin(angle), np.cos(angle)).astype(np.float32)


def dot(a, b):
    return jnp.dot(a, b, preferred_element_type=f32)


def dot_nt(a, b):
    return lax.dot_general(a, b, (((1,), (1,)), ((), ())), preferred_element_type=f32)


def dot_tn(a, b):
    return lax.dot_general(a, b, (((0,), (0,)), ((), ())), preferred_element_type=f32)


def row_total(values):
    return jnp.sum(values.astype(f32), axis=0, keepdims=True)


def norm_forward(values):
    average = jnp.mean(values, axis=-1, keepdims=True)
    centred = values - average
    variance = jnp.mean(centred * centred, axis=-1, keepdims=True)
    rstd = lax.rsqrt(variance + norm_eps)
    return centred * rstd, rstd


def norm_backward(grad, normed, rstd, gain):
    grad_normed = grad * gain
    first = jnp.mean(grad_normed, axis=-1, keepdims=True)
    second = jnp.mean(grad_normed * normed, axis=-1, keepdims=True)
    grad_in = rstd * (grad_normed - first - normed * second)
    return grad_in, row_total(grad * normed), row_total(grad)


def spread_rows(rows):
    head = lax.broadcasted_iota(jnp.int32, (NP, D), 1) // HD
    return jnp.concatenate(
        [jnp.where(head == h, rows, 0.0) for h in range(HEADS)], axis=0
    ).astype(bf16)


def spread_cols(cols):
    head = lax.broadcasted_iota(jnp.int32, (D, NP), 0) // HD
    return jnp.concatenate(
        [jnp.where(head == h, cols, 0.0) for h in range(HEADS)], axis=1
    ).astype(bf16)


def project_heads(weight_t, sums):
    high = sums.astype(bf16)
    low = (sums - high.astype(f32)).astype(bf16)
    return own_blocks(
        [
            dot(weight_t[pair_rows(p)], high[:, pair_cols(p)])
            + dot(weight_t[pair_rows(p)], low[:, pair_cols(p)])
            for p in range(4)
        ]
    )


def own_blocks(pairs):
    parts = []
    for pair in pairs:
        parts += [pair[:HD, :NP], pair[HD:, NP:]]
    return jnp.concatenate(parts, axis=0)


def head_rows(row):
    return jnp.concatenate([row[:, NP * h : NP * h + NP] for h in range(HEADS)], axis=0)


def head_line(rows):
    return jnp.concatenate([rows[h : h + 1] for h in range(HEADS)], axis=1)


def per_channel(rows):
    return jnp.concatenate(
        [jnp.broadcast_to(rows[h : h + 1], (HD, NP)) for h in range(HEADS)], axis=0
    )


def head_sums(cols):
    return jnp.concatenate(
        [jnp.sum(cols[HD * h : HD * h + HD], axis=0, keepdims=True) for h in range(HEADS)], axis=0
    )


def pair_cols(p):
    return slice(PAIR * p, PAIR * p + PAIR)


def pair_rows(p):
    return slice(2 * HD * p, 2 * HD * p + 2 * HD)


class Place:
    def __init__(self, pages):
        self.axes = axes_of(pages)
        self.page = lax.axis_index("dp")
        self.member = lax.axis_index("blk")
        self.digit = {
            name: self.member if name == "x" else lax.rem(self.page // stride, radix)
            for name, (radix, stride) in self.axes.items()
        }

    def size(self, group):
        return math.prod(self.axes[name][0] for name in group)

    def index(self, group):
        index = 0
        for name in group:
            index = index * self.axes[name][0] + self.digit[name]
        return index

    def peer(self, group, hop):
        index = lax.rem(self.index(group) + hop, self.size(group))
        page, member, rest = self.page, self.member, index
        for name in reversed(group):
            radix, stride = self.axes[name]
            digit = lax.rem(rest, radix)
            rest = rest // radix
            if name == "x":
                member = digit
            else:
                page = page + (digit - self.digit[name]) * stride
        return (page, member), index


class PageSum:
    def __init__(self, place, groups, back, rows, landing, whole, sent, arrived):
        self.place, self.groups, self.back = place, groups, back
        self.rows, self.landing, self.whole = rows, landing, whole
        self.sent, self.arrived = sent, arrived
        self.slots = 0
        self.extents = [rows.shape[0]]
        self.bases = [0]
        self.landings = []
        at = 0
        for group in groups:
            size = place.size(group)
            extent = self.extents[-1] // size
            self.landings.append(at)
            at += (size - 1) * extent
            self.bases.append(pl.multiple_of(self.bases[-1] + place.index(group) * extent, TILE))
            self.extents.append(extent)
        last = len(groups)
        moves = [self.scatter_moves(s) for s in range(last)]
        near = {"all": 0, "across": 1, "sides": 2}[back]
        moves += [self.gather_moves(s) for s in range(last - 1, near - 1, -1)]
        if back == "sides":
            moves += [self.side_moves(), self.corner_moves(), self.core_moves()]
        elif back == "across":
            moves += [self.across_moves(), self.core_moves()]
        self.phases = [functools.partial(self.step, moves, k) for k in range(len(moves) + 1)]

    @staticmethod
    def landing_rows(pages, groups, rows):
        axes = axes_of(pages)
        total, extent = 0, rows
        for group in groups:
            size = math.prod(axes[name][0] for name in group)
            extent //= size
            total += (size - 1) * extent
        return total

    def step(self, moves, k):
        last = len(self.groups)
        if k > 0:
            for move in moves[k - 1]:
                self.copy(*move).wait()
        if 0 < k <= last:
            total = self.scatter_sum(k - 1)
            region = pl.ds(self.bases[k], self.extents[k])
            if k < last:
                self.rows[region] = total
            elif len(self.whole.shape) == 3:
                self.whole[self.place.member, region] = total
            else:
                self.whole[region] = total
        if k < len(moves):
            for move in moves[k]:
                self.copy(*move).start()

    def copy(self, slot, source, target, device):
        return pltpu.make_async_remote_copy(
            src_ref=source(),
            dst_ref=target(),
            send_sem=self.sent.at[slot],
            recv_sem=self.arrived.at[slot],
            device_id=device,
            device_id_type=pl.DeviceIdType.MESH,
        )

    def new_slot(self):
        self.slots += 1
        return self.slots - 1

    def same(self, device, view):
        return (self.new_slot(), view, view, device)

    def scatter_moves(self, step):
        group = self.groups[step]
        extent = self.extents[step + 1]
        moves = []
        for hop in range(1, self.place.size(group)):
            device, other = self.place.peer(group, hop)
            start = pl.multiple_of(self.bases[step] + other * extent, TILE)
            landing = self.landings[step] + (hop - 1) * extent
            moves.append(
                (
                    self.new_slot(),
                    functools.partial(self.part, self.rows, start, extent),
                    functools.partial(self.part, self.landing, landing, extent),
                    device,
                )
            )
        return moves

    @staticmethod
    def part(ref, start, extent):
        return ref.at[pl.ds(start, extent)]

    def half(self, member, start, extent):
        if len(self.whole.shape) == 3:
            return self.whole.at[member, pl.ds(start, extent)]
        return self.whole.at[pl.ds(start, extent)]

    def scatter_sum(self, step):
        extent = self.extents[step + 1]
        total = self.rows[pl.ds(self.bases[step + 1], extent)].astype(f32)
        for hop in range(1, self.place.size(self.groups[step])):
            landing = self.landings[step] + (hop - 1) * extent
            total = total + self.landing[pl.ds(landing, extent)].astype(f32)
        return total.astype(bf16)

    def gather_moves(self, step):
        group = self.groups[step]
        view = functools.partial(self.half, self.place.member, self.bases[step + 1], self.extents[step + 1])
        return [
            self.same(self.place.peer(group, hop)[0], view) for hop in range(1, self.place.size(group))
        ]

    def own_quarter(self):
        step = 2 if len(self.groups[0]) == 1 else 1
        return self.bases[step], self.extents[step]

    def side_moves(self):
        view = functools.partial(self.half, self.place.member, *self.own_quarter())
        return [self.same(self.place.peer((name,), 1)[0], view) for name in ("y", "x")]

    def corner_moves(self):
        base, extent = self.own_quarter()
        other = pl.multiple_of(base + (1 - 2 * self.place.digit["y"]) * extent, TILE)
        view = functools.partial(self.half, self.place.member, other, extent)
        return [self.same(self.place.peer(("x",), 1)[0], view)]

    def across_moves(self):
        view = functools.partial(self.half, self.place.member, *self.own_quarter())
        return [self.same(self.place.peer(("x", "y"), hop)[0], view) for hop in range(1, 4)]

    def core_moves(self):
        extent = self.extents[0] // 2
        start = pl.multiple_of(self.place.digit["core"] * extent, TILE)
        device, _ = self.place.peer(("core",), 1)
        return [self.same(device, functools.partial(self.half, m, start, extent)) for m in range(2)]


def clear_rest(ref, used):
    if ref.shape[0] > used:
        ref[used:] = jnp.zeros((ref.shape[0] - used, D), ref.dtype)


def layer_kernel(
    tokens,
    pages,
    queries_in,
    memory_hbm,
    turns_in,
    order_in,
    lengths_in,
    attn_in,
    attn_out,
    attn_bias,
    ffn_in_hbm,
    ffn_in_bias,
    ffn_out_hbm,
    ffn_out_bias,
    norm_gain,
    norm_bias,
    pos_in,
    out_grad_in,
    table_in,
    result_hbm,
    queries_grad_hbm,
    memory_grad_hbm,
    whole_f_hbm,
    whole_t_hbm,
    whole_k_hbm,
    memory_s,
    key_in_s,
    probs_s,
    grad_scores_s,
    code_s,
    query_kt,
    grad_vt,
    back_s,
    table_s,
    top_s,
    highest_s,
    shifts_s,
    factor_s,
    total_s,
    mixed_s,
    pad_s,
    result_out,
    queries_grad_out,
    send_a,
    recv_a,
    send_t,
    recv_t,
    send_b,
    recv_b,
    small_s,
    rows_f,
    landing_f,
    whole_f,
    rows_t,
    landing_t,
    whole_t,
    rows_k,
    landing_k,
    whole_k,
    load_sem,
    store_sem,
    link_sem,
    sent_f,
    arrived_f,
    sent_t,
    arrived_t,
    sent_k,
    arrived_k,
):
    member = lax.axis_index("blk")
    partner = (lax.axis_index("dp"), 1 - member)
    chunks = tokens // CHUNK

    place = Place(pages)
    groups_f, groups_t, groups_k = sum_groups(pages)
    sum_f = PageSum(place, groups_f, "sides", rows_f, landing_f, whole_f, sent_f, arrived_f)
    sum_t = PageSum(place, groups_t, "across", rows_t, landing_t, whole_t, sent_t, arrived_t)
    sum_k = PageSum(place, groups_k, "all", rows_k, landing_k, whole_k, sent_k, arrived_k)

    barrier = pltpu.get_barrier_semaphore()
    peers = [
        place.peer(group, hop)[0]
        for group in [("x", "core", "y"), *far_axes(pages)]
        for hop in range(1, place.size(group))
    ]
    for peer in peers:
        pl.semaphore_signal(barrier, inc=1, device_id=peer, device_id_type=pl.DeviceIdType.MESH)

    load_memory = pltpu.make_async_copy(memory_hbm.at[0], memory_s, load_sem.at[0])
    half = FF // 2
    ffn_in_s = [grad_scores_s.at[D * k : D * k + D] for k in range(2)]
    ffn_out_s = grad_scores_s.at[2 * D : 2 * D + FF, :D]
    free = 2 * D + FF
    active_s = [grad_scores_s.at[free + NP * k : free + NP * k + NP] for k in range(2)]
    slope_s = [grad_scores_s.at[free + NP * k : free + NP * k + NP] for k in range(2, 4)]
    load_ffn = [
        pltpu.make_async_copy(ffn_in_hbm.at[:, half * k : half * k + half], ffn_in_s[k], load_sem.at[1 + k])
        for k in range(2)
    ]
    load_ffn.append(pltpu.make_async_copy(ffn_out_hbm, ffn_out_s, load_sem.at[3]))
    load_memory.start()
    for load in load_ffn:
        load.start()

    pairs = [attn_bias[j].astype(f32) for j in range(3)]
    bias = jnp.concatenate([pair[k : k + 1] for k in range(2) for pair in pairs], axis=0)
    gain = norm_gain[...].astype(f32)
    shift = norm_bias[...].astype(f32)

    order = order_in[...]
    turn = turns_in[0]
    row_at = order >> 7
    col_at = order & 127
    top = SIDE - 1
    row_new = jnp.where(
        turn == 0, row_at, jnp.where(turn == 1, col_at, jnp.where(turn == 2, top - row_at, top - col_at))
    )
    col_new = jnp.where(
        turn == 0, col_at, jnp.where(turn == 1, top - row_at, jnp.where(turn == 2, top - col_at, row_at))
    )
    past = jnp.where(order < lengths_in[0], 0, SIDE * SIDE)
    code_s[...] = (row_new * SIDE + col_new + past).astype(f32)

    pad_s[...] = jnp.zeros_like(pad_s)
    pad_s[0, :NQ] = queries_in[0].astype(f32)
    pad_s[1, :NQ] = pos_in[...].astype(f32)
    pad_s[2, :NQ] = out_grad_in[0].astype(f32)
    queries_f = pad_s[0]
    pos_f = pad_s[1]
    queries_b = queries_f.astype(bf16)
    mixed_q = (queries_f + pos_f).astype(bf16)
    query_self = (dot(mixed_q, attn_in[0, 0]) + bias[0:1]).astype(bf16)
    key_self = dot(mixed_q, attn_in[0, 1]).astype(bf16)
    value_self = (dot(queries_b, attn_in[0, 2]) + bias[1:2]).astype(bf16)
    scores = dot(key_self, spread_cols(query_self.astype(f32).T)) * scale
    own_key = lax.broadcasted_iota(jnp.int32, (NP, HQ), 0) < NQ
    scores = jnp.where(own_key, scores, masked_score)
    raised = jnp.exp(scores - jnp.max(scores, axis=0, keepdims=True))
    probs_self = raised / jnp.sum(raised, axis=0, keepdims=True)
    probs_self_b = probs_self.astype(bf16)
    value_t = value_self.astype(f32).T.astype(bf16)
    attended = own_blocks(
        [dot(value_t[pair_rows(p)], probs_self_b[:, pair_cols(p)]) for p in range(4)]
    ).T.astype(bf16)
    first_normed, first_rstd = norm_forward(queries_f + dot(attended, attn_out[0]) + bias[2:3])
    first = first_normed * gain[0:1] + shift[0:1]
    cross_q = (first + pos_f).astype(bf16)
    query_c = (dot(cross_q, attn_in[1, 0]) + bias[3:4]).astype(bf16)
    query_x = spread_rows(query_c.astype(f32))
    query_k = dot(attn_in[1, 1], spread_cols(query_c.astype(f32).T))
    query_kt[...] = (query_k * (scale * log2e)).astype(bf16)
    back_s[:HQ] = (dot_nt(query_x, attn_in[1, 1]) * scale).astype(bf16)
    table = table_in[...]
    nothing = jnp.zeros((SIDE, D // 2), f32)
    table = jnp.concatenate(
        [jnp.concatenate([table, nothing], axis=1), jnp.concatenate([nothing, table], axis=1)], axis=0
    )
    table_high = table.astype(bf16)
    table_s[: 2 * SIDE] = table_high
    table_s[2 * SIDE :] = (table - table_high.astype(f32)).astype(bf16)

    load_memory.wait()
    def mask_view(i):
        side, place = i // (chunks // 2), lax.rem(i, chunks // 2)
        return grad_scores_s.at[
            pl.ds(pl.multiple_of(tokens // 2 + place * CHUNK, CHUNK), CHUNK),
            pl.ds(pl.multiple_of(side * NP, NP), NP),
        ]

    lane = lax.broadcasted_iota(jnp.int32, (CHUNK, NP), 1)

    @pl.loop(0, chunks)
    def _(i):
        rows = pl.ds(pl.multiple_of(i * CHUNK, CHUNK), CHUNK)
        line = code_s[:, rows]
        code = jnp.concatenate(
            [
                jnp.broadcast_to(line[:, NP * j : NP * j + NP], (NP, NP)).T
                for j in range(CHUNK // NP)
            ],
            axis=0,
        ).astype(jnp.int32)
        row_hot = jnp.where(((code >> 7) & 127) == lane, 1.0, 0.0).astype(bf16)
        col_hot = jnp.where((code & 127) == lane, 1.0, 0.0).astype(bf16)
        hot = jnp.concatenate([row_hot, col_hot, row_hot, col_hot], axis=1)
        masked = jnp.where(code < SIDE * SIDE, 0.0, masked_score)
        mask_view(i)[...] = masked.astype(bf16)
        key_in_s[rows] = (memory_s[rows].astype(f32) + dot(hot, table_s[...])).astype(bf16)

    def score_pair(p, key_in, mask, score_s):
        cols = pair_cols(p)
        part = dot(key_in, query_kt[:, cols]) + mask
        score_s[:, cols] = part
        top_s[:, cols] = jnp.max(part.reshape(CHUNK // 8, 8, PAIR), axis=0)

    def score_operands(i):
        rows = pl.ds(pl.multiple_of(i * CHUNK, CHUNK), CHUNK)
        mask = mask_view(i)[...].astype(f32)
        return key_in_s[rows], jnp.concatenate([mask, mask], axis=1)

    def attend_all(score_s):
        operands = score_operands(0)
        for p in range(4):
            score_pair(p, *operands, score_s)

        @pl.loop(0, chunks)
        def _(i):
            rows = pl.ds(pl.multiple_of(i * CHUNK, CHUNK), CHUNK)
            memory_ct = memory_s[rows].T
            operands = score_operands(jnp.minimum(i + 1, chunks - 1))
            for p in range(4):
                cols = pair_cols(p)
                before = highest_s[0:1, cols]
                highest = jnp.maximum(before, jnp.max(top_s[:, cols], axis=0, keepdims=True))
                highest_s[0:1, cols] = highest
                shifts_s[pl.ds(i, 1), cols] = highest
                fade = jnp.exp2(before - highest)
                raised = jnp.exp2(score_s[:, cols] - highest)
                sums = jnp.sum(raised.reshape(CHUNK // 8, 8, PAIR), axis=0)
                total_s[:, cols] = total_s[:, cols] * fade + sums
                probs_s[rows, cols] = raised.astype(bf16)
                mixed_s[:, cols] = mixed_s[:, cols] * fade + dot(memory_ct, probs_s[rows, cols])
                score_pair(p, *operands, score_s)

    highest_s[0:1] = jnp.full((1, HQ), -3e38, f32)
    total_s[...] = jnp.zeros_like(total_s)
    mixed_s[...] = jnp.zeros_like(mixed_s)
    pl.run_scoped(attend_all, pltpu.VMEM((CHUNK, HQ), f32))
    highest_own = highest_s[0:1]
    total_own = jnp.sum(total_s[...], axis=0, keepdims=True)

    value_wt = attn_in[1, 2].astype(f32).T.astype(bf16)
    key_wt = attn_in[1, 1].astype(f32).T.astype(bf16)
    send_a[...] = project_heads(value_wt, mixed_s[...]).astype(bf16)
    send_t[:HEADS] = head_rows(highest_own)
    send_t[HEADS:] = head_rows(total_own)
    pl.semaphore_wait(barrier, len(peers))
    swap_a = pltpu.make_async_remote_copy(
        src_ref=send_a,
        dst_ref=recv_a,
        send_sem=link_sem.at[0],
        recv_sem=link_sem.at[1],
        device_id=partner,
        device_id_type=pl.DeviceIdType.MESH,
    )
    swap_t = pltpu.make_async_remote_copy(
        src_ref=send_t,
        dst_ref=recv_t,
        send_sem=link_sem.at[4],
        recv_sem=link_sem.at[5],
        device_id=partner,
        device_id_type=pl.DeviceIdType.MESH,
    )
    swap_a.start()
    swap_t.start()
    swap_a.wait()
    swap_t.wait()
    is_first = member == 0
    own, other = send_a[...].astype(f32), recv_a[...].astype(f32)
    left = jnp.where(is_first, own, other)
    right = jnp.where(is_first, other, own)
    own, other = send_t[...], recv_t[...]
    left_t = jnp.where(is_first, own, other)
    right_t = jnp.where(is_first, other, own)
    highest = jnp.maximum(left_t[:HEADS], right_t[:HEADS])
    fade_l = jnp.exp2(left_t[:HEADS] - highest)
    fade_r = jnp.exp2(right_t[:HEADS] - highest)
    total = left_t[HEADS:] * fade_l + right_t[HEADS:] * fade_r
    mixed_t = left * per_channel(fade_l / total) + right * per_channel(fade_r / total)
    log_total = head_line(highest + jnp.log2(total))
    own_share = jnp.exp2(highest_own - log_total)
    factor_s[...] = jnp.exp2(shifts_s[...] - log_total)
    attended_c = (mixed_t.T + bias[4:5]).astype(bf16)

    second_normed, second_rstd = norm_forward(first + dot(attended_c, attn_out[1]) + bias[5:6])
    second = second_normed * gain[1:2] + shift[1:2]
    ffn_input = second.astype(bf16)
    load_ffn[0].wait()
    load_ffn[1].wait()
    blocks = [(j // 4, slice(D * j, D * j + D), slice(j % 4 * D, j % 4 * D + D)) for j in range(FF // D)]
    hidden_bias = ffn_in_bias[...].astype(f32).reshape(1, FF)
    def feed_forward(gate_s):
        for k, cols, part in blocks:
            hidden = dot(ffn_input, ffn_in_s[k][:, part]) + hidden_bias[:, cols]
            half_gate = 0.5 + 0.5 * lax.erf(hidden * math.sqrt(0.5))
            active_s[k][:, part] = (hidden * half_gate).astype(bf16)
            gate_s[:, cols] = half_gate + hidden * jnp.exp(hidden * hidden * -0.5) * (
                1.0 / math.sqrt(2.0 * math.pi)
            )
        load_ffn[2].wait()
        third_normed, third_rstd = norm_forward(
            second
            + dot(active_s[0][...], ffn_out_s[:half])
            + dot(active_s[1][...], ffn_out_s[half:])
            + ffn_out_bias[...].astype(f32).reshape(1, D)
        )
        result_out[...] = (third_normed * gain[2:3] + shift[2:3])[:NQ].astype(bf16)
        grad_third, gain_grad_2, shift_grad_2 = norm_backward(
            pad_s[2], third_normed, third_rstd, gain[2:3]
        )
        grad_branch_f = grad_third.astype(bf16)
        for k, cols, part in blocks:
            grad_hidden = dot_nt(grad_branch_f, ffn_out_s[cols]) * gate_s[:, cols]
            slope_s[k][:, part] = grad_hidden.astype(bf16)
        return grad_third, gain_grad_2, shift_grad_2, grad_branch_f

    grad_third, gain_grad_2, shift_grad_2, grad_branch_f = pl.run_scoped(
        feed_forward, pltpu.VMEM((NP, FF), f32)
    )
    grad_second = grad_third + dot_nt(slope_s[0][...], ffn_in_s[0][...])
    grad_second += dot_nt(slope_s[1][...], ffn_in_s[1][...])
    grad_second_in, gain_grad_1, shift_grad_1 = norm_backward(
        grad_second, second_normed, second_rstd, gain[1:2]
    )
    grad_branch_c = grad_second_in.astype(bf16)
    ffn_input_t = second.T.astype(bf16)

    @pl.when(member == 0)
    def _():
        for k, cols, part in blocks:
            rows_f[cols] = dot(ffn_input_t, slope_s[k][:, part]).astype(bf16)

    @pl.when(member == 1)
    def _():
        for k, cols, part in blocks:
            rows_f[cols] = dot_tn(active_s[k][:, part], grad_branch_f).astype(bf16)

    is_first = member == 0
    out_grad_c = dot_tn(attended_c, grad_branch_c)
    rows_k[2 * D : 3 * D] = jnp.where(is_first, out_grad_c, 0.0).astype(bf16)

    clear_rest(rows_f, ROWS_F)
    clear_rest(rows_t, ROWS_T)
    clear_rest(rows_k, ROWS_K)
    sum_f.phases[0]()
    grad_attended_c = dot_nt(grad_branch_c, attn_out[1]).astype(bf16).astype(f32)
    small_s[:16] = jnp.concatenate(
        [row_total(slope_s[k][:, part]) for k, _, part in blocks]
        + [
            row_total(grad_branch_f),
            row_total(grad_branch_c),
            gain_grad_2,
            shift_grad_2,
            gain_grad_1,
            shift_grad_1,
            row_total(grad_attended_c),
            jnp.zeros((1, D), f32),
        ],
        axis=0,
    )

    store_result = pltpu.make_async_copy(result_out, result_hbm, load_sem.at[7])
    store_result.start()

    grad_attended_t = grad_attended_c.T
    grad_x = spread_rows(grad_attended_c)
    grad_v = dot(attn_in[1, 2], spread_cols(grad_attended_t))
    grad_vt[...] = grad_v.astype(bf16)
    back_s[HQ:] = grad_v.T.astype(bf16)
    inner = head_line(head_sums(grad_attended_t * mixed_t))
    rows_k[D : 2 * D] = dot((mixed_s[...] * own_share).astype(bf16), grad_x).astype(bf16)
    mixed_s[...] = jnp.zeros_like(mixed_s)

    queue_f = sum_f.phases[1:]
    queue_t = list(sum_t.phases)
    queue_k = list(sum_k.phases)

    def take(queue):
        if queue:
            queue.pop(0)()

    def at(i, steps):
        for step, queue in steps:
            pl.when(i == (step * chunks) // 16)(queue.pop(0))

    @pl.loop(0, chunks)
    def _(i):
        rows = pl.ds(pl.multiple_of(i * CHUNK, CHUNK), CHUNK)
        key_ct = key_in_s[rows].T
        memory_c = memory_s[rows]
        for p in range(4):
            cols = pair_cols(p)
            grad_probs = dot(memory_c, grad_vt[:, cols])
            probs = probs_s[rows, cols].astype(f32) * factor_s[pl.ds(i, 1), cols]
            probs_s[rows, cols] = probs.astype(bf16)
            grad_scores_s[rows, cols] = (probs * (grad_probs - inner[:, cols])).astype(bf16)
        mixed_s[...] += dot(key_ct, grad_scores_s[rows])
        at(i, [(3, queue_f), (9, queue_f), (15, queue_f)])

    send_b[...] = (project_heads(key_wt, mixed_s[...]) * scale).astype(bf16)
    swap_b = pltpu.make_async_remote_copy(
        src_ref=send_b,
        dst_ref=recv_b,
        send_sem=link_sem.at[2],
        recv_sem=link_sem.at[3],
        device_id=partner,
        device_id_type=pl.DeviceIdType.MESH,
    )
    swap_b.start()
    query_x = spread_rows(query_c.astype(f32))
    rows_k[:D] = (dot(mixed_s[...].astype(bf16), query_x) * scale).astype(bf16)
    take(queue_k)
    swap_b.wait()
    take(queue_f)
    take(queue_k)
    grad_query_c = (send_b[...].astype(f32) + recv_b[...].astype(f32)).T.astype(bf16)

    cross_pos_grad = dot_nt(grad_query_c, attn_in[1, 0])
    grad_first_in, gain_grad_0, shift_grad_0 = norm_backward(
        grad_second_in + cross_pos_grad, first_normed, first_rstd, gain[0:1]
    )
    grad_branch = grad_first_in.astype(bf16)
    grad_attended = dot_nt(grad_branch, attn_out[0]).astype(bf16).astype(f32)
    take(queue_k)
    grad_probs = dot(value_self, spread_cols(grad_attended.T))
    inner_self = jnp.sum(probs_self * grad_probs, axis=0, keepdims=True)
    grad_scores = (probs_self * (grad_probs - inner_self)).astype(bf16)
    key_t = key_self.astype(f32).T.astype(bf16)
    grad_query_s = (
        own_blocks([dot(key_t[pair_rows(p)], grad_scores[:, pair_cols(p)]) for p in range(4)]) * scale
    ).T.astype(bf16)
    grad_key_s = (dot(grad_scores, spread_rows(query_self.astype(f32))) * scale).astype(bf16)
    grad_value_s = dot(probs_self_b, spread_rows(grad_attended)).astype(bf16)
    grad_mixed_q = dot_nt(grad_query_s, attn_in[0, 0]) + dot_nt(grad_key_s, attn_in[0, 1])
    queries_grad_out[...] = (grad_first_in + grad_mixed_q + dot_nt(grad_value_s, attn_in[0, 2]))[
        :NQ
    ].astype(bf16)
    store_queries = pltpu.make_async_copy(queries_grad_out, queries_grad_hbm, load_sem.at[8])
    store_queries.start()
    small_s[16:] = jnp.concatenate(
        [
            row_total(grad_query_s),
            row_total(grad_value_s),
            row_total(grad_branch),
            row_total(grad_query_c),
            gain_grad_0,
            shift_grad_0,
            jnp.zeros((10, D), f32),
        ],
        axis=0,
    )
    @pl.when(member == 0)
    def _():
        rows_t[:D] = dot_tn(mixed_q, grad_query_s).astype(bf16)
        rows_t[D : 2 * D] = dot_tn(mixed_q, grad_key_s).astype(bf16)
        rows_t[2 * D : 3 * D] = dot_tn(queries_b, grad_value_s).astype(bf16)

    @pl.when(member == 1)
    def _():
        rows_t[:D] = dot_tn(cross_q, grad_query_c).astype(bf16)
        rows_t[D : 2 * D] = dot_tn(attended, grad_branch).astype(bf16)
        rows_t[ROW_POS:ROW_SMALL] = (grad_mixed_q + cross_pos_grad).astype(bf16)
        rows_t[ROW_SMALL : ROW_SMALL + 32] = small_s[...].astype(bf16)
        rows_t[ROW_SMALL + 32 : ROWS_T] = jnp.zeros((ROWS_T - ROW_SMALL - 32, D), bf16)

    take(queue_t)
    take(queue_k)
    take(queue_f)

    @pl.loop(0, chunks)
    def _(i):
        rows = pl.ds(pl.multiple_of(i * CHUNK, CHUNK), CHUNK)
        both = jnp.concatenate([grad_scores_s[rows], probs_s[rows]], axis=1)
        memory_s[rows] = dot(both, back_s[...]).astype(bf16)
        pltpu.make_async_copy(memory_s.at[rows], memory_grad_hbm.at[0, rows], store_sem.at[i]).start()
        at(
            i,
            [
                (3, queue_t),
                (4, queue_k),
                (7, queue_t),
                (8, queue_k),
                (9, queue_f),
                (11, queue_t),
                (12, queue_k),
                (15, queue_t),
            ],
        )

    while queue_f:
        take(queue_f)
    stores = [
        pltpu.make_async_copy(whole, target, load_sem.at[4 + k])
        for k, (whole, target) in enumerate(
            (
                (whole_f, whole_f_hbm),
                (whole_t, whole_t_hbm),
                (whole_k, whole_k_hbm),
            )
        )
    ]
    stores[0].start()
    while queue_t or queue_k:
        take(queue_t)
        take(queue_k)
    for store in stores[1:]:
        store.start()

    @pl.loop(0, chunks)
    def _(i):
        rows = pl.ds(pl.multiple_of(i * CHUNK, CHUNK), CHUNK)
        pltpu.make_async_copy(memory_s.at[rows], memory_grad_hbm.at[0, rows], store_sem.at[i]).wait()

    for store in [*stores, store_result, store_queries]:
        store.wait()


def finish_kernel(
    result_in,
    queries_grad_in,
    memory_grad_in,
    whole_f_hbm,
    whole_t_hbm,
    whole_k_hbm,
    result_hbm,
    queries_grad_hbm,
    memory_grad,
    attn_in_hbm,
    attn_out_hbm,
    attn_bias_hbm,
    ffn_in_hbm,
    ffn_in_bias_hbm,
    ffn_out_hbm,
    ffn_out_bias_hbm,
    norm_gain_hbm,
    norm_bias_hbm,
    query_pos_hbm,
    moved,
    whole_f,
    whole_t,
    whole_k,
    result,
    queries_grad,
    attn_in_grad,
    attn_out_grad,
    attn_bias_grad,
    ffn_in_grad,
    ffn_in_bias_grad,
    ffn_out_grad,
    ffn_out_bias_grad,
    norm_gain_grad,
    norm_bias_grad,
    query_pos_grad,
    in_sem,
    out_sem,
    sum_sem,
    grad_sem,
):
    pieces = in_sem.shape[0]
    piece = moved.shape[0] // pieces

    def fetch(j):
        rows = pl.ds(piece * j, piece)
        return pltpu.make_async_copy(memory_grad_in.at[0, rows], moved.at[rows], in_sem.at[j])

    def write(j):
        rows = pl.ds(piece * j, piece)
        return pltpu.make_async_copy(moved.at[rows], memory_grad.at[0, rows], out_sem.at[j])

    sums = [
        (whole_t_hbm, whole_t),
        (whole_k_hbm, whole_k),
        (whole_f_hbm, whole_f),
        (result_in, result),
        (queries_grad_in, queries_grad),
    ]
    loads = [pltpu.make_async_copy(*pair, sum_sem.at[j]) for j, pair in enumerate(sums)]
    for load in loads:
        load.start()
    for j in range(pieces):
        fetch(j).start()
    blocks = FF // D
    stores = []

    def store(source, target):
        stores.append(pltpu.make_async_copy(source, target, grad_sem.at[len(stores)]))
        stores[-1].start()

    loads[0].wait()
    loads[1].wait()
    for j in range(3):
        attn_in_grad[0, j] = whole_t[0, D * j : D * j + D].astype(f32)
    attn_in_grad[1, 0] = whole_t[1, :D].astype(f32)
    attn_in_grad[1, 1] = whole_k[:D].astype(f32)
    attn_in_grad[1, 2] = whole_k[D : 2 * D].astype(f32)
    store(attn_in_grad, attn_in_hbm)
    attn_out_grad[0] = whole_t[1, D : 2 * D].astype(f32)
    attn_out_grad[1] = whole_k[2 * D : 3 * D].astype(f32)
    store(attn_out_grad, attn_out_hbm)
    loads[2].wait()
    for k in range(2):
        half = slice(FF // 2 * k, FF // 2 * (k + 1))
        ffn_out_grad[half] = whole_f[1, half].astype(f32)
        store(ffn_out_grad.at[half], ffn_out_hbm.at[half])
    for k in range(2):
        half = slice(FF // 2 * k, FF // 2 * (k + 1))
        for j in range(blocks // 2 * k, blocks // 2 * (k + 1)):
            at = slice(D * j, D * j + D)
            ffn_in_grad[:, at] = whole_f[0, at].astype(f32)
        store(ffn_in_grad.at[:, half], ffn_in_hbm.at[:, half])
    for j in range(pieces):
        fetch(j).wait()
        write(j).start()
    loads[3].wait()
    store(result, result_hbm.at[0])
    loads[4].wait()
    store(queries_grad, queries_grad_hbm.at[0])
    query_pos_grad[...] = whole_t[1, ROW_POS:ROW_SMALL].astype(f32)[:NQ]
    store(query_pos_grad, query_pos_hbm)
    small = whole_t[1, ROW_SMALL : ROW_SMALL + 32].astype(f32)
    ffn_in_bias_grad[...] = jnp.concatenate([small[j : j + 1] for j in range(blocks)], axis=1)
    store(ffn_in_bias_grad, ffn_in_bias_hbm)
    ffn_out_bias_grad[...] = small[8:9]
    store(ffn_out_bias_grad, ffn_out_bias_hbm)
    for j, (own, cross) in enumerate(((16, 19), (17, 14), (18, 9))):
        attn_bias_grad[j, 0:1] = small[own : own + 1]
        attn_bias_grad[j, 1:2] = small[cross : cross + 1]
    store(attn_bias_grad, attn_bias_hbm)
    for j, (gain, shift) in enumerate(((20, 21), (12, 13), (10, 11))):
        norm_gain_grad[j : j + 1] = small[gain : gain + 1]
        norm_bias_grad[j : j + 1] = small[shift : shift + 1]
    store(norm_gain_grad, norm_gain_hbm)
    store(norm_bias_grad, norm_bias_hbm)
    for j in range(pieces):
        write(j).wait()
    for copy in stores:
        copy.wait()


def body(
    pages,
    queries,
    memory,
    quarter_turns,
    token_order,
    lengths,
    attn_in,
    attn_out,
    attn_bias,
    ffn_in,
    ffn_in_bias,
    ffn_out,
    ffn_out_bias,
    norm_gain,
    norm_bias,
    query_pos,
    out_grad,
):
    tokens = memory.shape[1]
    chunks = tokens // CHUNK
    groups_f, groups_t, groups_k = sum_groups(pages)
    summed = [
        (padded(ROWS_F, pages), groups_f),
        (padded(ROWS_T, pages), groups_t),
        (padded(ROWS_K, 2 * pages), groups_k),
    ]
    whole_shapes = [(2, rows, D) for rows, _ in summed[:2]] + [(summed[2][0], D)]
    sum_buffers = []
    for (rows, groups), shape in zip(summed, whole_shapes):
        landing = PageSum.landing_rows(pages, groups, rows)
        sum_buffers += [pltpu.VMEM(each, bf16) for each in ((rows, D), (landing, D), shape)]
    copies = 32
    vmem = pl.BlockSpec(memory_space=pltpu.VMEM)
    smem = pl.BlockSpec(memory_space=pltpu.SMEM)
    anywhere = pl.BlockSpec(memory_space=pl.ANY)
    parts = pl.pallas_call(
        functools.partial(layer_kernel, tokens, pages),
        out_shape=[
            jax.ShapeDtypeStruct((NQ, D), bf16),
            jax.ShapeDtypeStruct((NQ, D), bf16),
            jax.ShapeDtypeStruct((1, tokens, D), bf16),
            *(jax.ShapeDtypeStruct(shape, bf16) for shape in whole_shapes),
        ],
        in_specs=[
            vmem,
            anywhere,
            smem,
            vmem,
            smem,
            vmem,
            vmem,
            vmem,
            anywhere,
            vmem,
            anywhere,
            vmem,
            vmem,
            vmem,
            vmem,
            vmem,
            vmem,
        ],
        out_specs=[anywhere] * 6,
        scratch_shapes=[
            pltpu.VMEM((tokens, D), bf16),
            pltpu.VMEM((tokens, D), bf16),
            pltpu.VMEM((tokens, HQ), bf16),
            pltpu.VMEM((tokens, HQ), bf16),
            pltpu.VMEM((1, tokens), f32),
            pltpu.VMEM((D, HQ), bf16),
            pltpu.VMEM((D, HQ), bf16),
            pltpu.VMEM((2 * HQ, D), bf16),
            pltpu.VMEM((4 * SIDE, D), bf16),
            pltpu.VMEM((8, HQ), f32),
            pltpu.VMEM((8, HQ), f32),
            pltpu.VMEM((chunks, HQ), f32),
            pltpu.VMEM((chunks, HQ), f32),
            pltpu.VMEM((8, HQ), f32),
            pltpu.VMEM((D, HQ), f32),
            pltpu.VMEM((3, NP, D), f32),
            pltpu.VMEM((NQ, D), bf16),
            pltpu.VMEM((NQ, D), bf16),
            pltpu.VMEM((D, NP), bf16),
            pltpu.VMEM((D, NP), bf16),
            pltpu.VMEM((2 * HEADS, NP), f32),
            pltpu.VMEM((2 * HEADS, NP), f32),
            pltpu.VMEM((D, NP), bf16),
            pltpu.VMEM((D, NP), bf16),
            pltpu.VMEM((32, D), f32),
            *sum_buffers,
            pltpu.SemaphoreType.DMA((9,)),
            pltpu.SemaphoreType.DMA((chunks,)),
            pltpu.SemaphoreType.DMA((6,)),
            *[pltpu.SemaphoreType.DMA((copies,))] * 6,
        ],
        compiler_params=pltpu.CompilerParams(
            collective_id=0, has_side_effects=True, vmem_limit_bytes=127 * 512 * 1024
        ),
        cost_estimate=pl.CostEstimate(
            flops=2 * 8 * tokens * HQ * D, bytes_accessed=20 << 20, transcendentals=tokens * HQ
        ),
        name="decoder_layer",
    )(
        queries,
        memory,
        quarter_turns,
        token_order,
        lengths,
        attn_in,
        attn_out,
        attn_bias.transpose(1, 0, 2),
        ffn_in,
        ffn_in_bias,
        ffn_out,
        ffn_out_bias,
        norm_gain,
        norm_bias,
        query_pos,
        out_grad,
        jnp.asarray(position_table()),
    )
    outs = pl.pallas_call(
        finish_kernel,
        out_shape=[
            jax.ShapeDtypeStruct((1, NQ, D), bf16),
            jax.ShapeDtypeStruct((1, NQ, D), bf16),
            jax.ShapeDtypeStruct((1, tokens, D), bf16),
            jax.ShapeDtypeStruct((2, 3, D, D), f32),
            jax.ShapeDtypeStruct((2, D, D), f32),
            jax.ShapeDtypeStruct((3, 2, D), f32),
            jax.ShapeDtypeStruct((D, FF), f32),
            jax.ShapeDtypeStruct((1, FF), f32),
            jax.ShapeDtypeStruct((FF, D), f32),
            jax.ShapeDtypeStruct((1, D), f32),
            jax.ShapeDtypeStruct((3, D), f32),
            jax.ShapeDtypeStruct((3, D), f32),
            jax.ShapeDtypeStruct((NQ, D), f32),
        ],
        in_specs=[anywhere] * 6,
        out_specs=[anywhere] * 13,
        scratch_shapes=[
            pltpu.VMEM((tokens, D), bf16),
            *(pltpu.VMEM(shape, bf16) for shape in whole_shapes),
            pltpu.VMEM((NQ, D), bf16),
            pltpu.VMEM((NQ, D), bf16),
            pltpu.VMEM((2, 3, D, D), f32),
            pltpu.VMEM((2, D, D), f32),
            pltpu.VMEM((3, 2, D), f32),
            pltpu.VMEM((D, FF), f32),
            pltpu.VMEM((1, FF), f32),
            pltpu.VMEM((FF, D), f32),
            pltpu.VMEM((1, D), f32),
            pltpu.VMEM((3, D), f32),
            pltpu.VMEM((3, D), f32),
            pltpu.VMEM((NQ, D), f32),
            pltpu.SemaphoreType.DMA((8,)),
            pltpu.SemaphoreType.DMA((8,)),
            pltpu.SemaphoreType.DMA((5,)),
            pltpu.SemaphoreType.DMA((14,)),
        ],
        compiler_params=pltpu.CompilerParams(vmem_limit_bytes=62 * 1024 * 1024),
        name="write_outputs",
    )(*parts)
    return (
        *outs[:5],
        outs[5].transpose(1, 0, 2),
        outs[6],
        outs[7].reshape(FF),
        outs[8],
        outs[9].reshape(D),
        *outs[10:],
    )


def solution(mesh):
    in_specs = (
        P("dp", None, None),
        P("dp", "blk", None),
        P("dp"),
        P("dp", "blk"),
        P("dp"),
        P(),
        P(),
        P(),
        P(),
        P(),
        P(),
        P(),
        P(),
        P(),
        P(),
        P("dp", None, None),
    )
    out_specs = (
        P("dp", None, None),
        P("dp", None, None),
        P("dp", "blk", None),
        P(),
        P(),
        P(),
        P(),
        P(),
        P(),
        P(),
        P(),
        P(),
        P(),
    )
    layer = functools.partial(body, mesh.shape["dp"])
    return jax.shard_map(layer, mesh=mesh, in_specs=in_specs, out_specs=out_specs, check_vma=False)
```

```python
import functools
import math

import jax
import jax.numpy as jnp
import numpy as np
from jax import lax
from jax.experimental import pallas as pl
from jax.experimental.pallas import tpu as pltpu
from jax.sharding import PartitionSpec as P

D = 256
HEADS = 8
HD = D // HEADS
SIDE = 128
NQ = 125
NP = 128
HQ = HEADS * NP
PAIR = 2 * NP
FF = 2048
CHUNK = 1024

masked_score = -1e30
norm_eps = 1e-05
scale = 1.0 / math.sqrt(HD)
log2e = math.log2(math.e)

bf16 = jnp.bfloat16
f32 = jnp.float32

ROWS_F = FF
ROW_POS = 2 * D
ROW_SMALL = 2 * D + NP
ROWS_T = 3 * D
ROWS_K = 3 * D
TILE = 16
PIECES = 4


def axes_of(pages):
    axes = {"core": (2, 1), "y": (2, 2)}
    stride = 4
    while stride < pages:
        radix = 4 if pages // stride % 4 == 0 else 2
        axes["z%d" % (len(axes) - 2)] = (radix, stride)
        stride *= radix
    axes["x"] = (2, 0)
    return axes


def far_axes(pages):
    return [(name,) for name in axes_of(pages) if name.startswith("z")]


def sum_groups(pages):
    far = far_axes(pages)
    return [("core",), ("y",), *far], [("core", "y"), *far], [("core",), ("x",), ("y",), *far]


def padded(rows, pages):
    unit = TILE * pages
    return (rows + unit - 1) // unit * unit


def position_table():
    half = D // 2
    channel = np.arange(half)
    inverse = np.exp((channel // 2).astype(np.float32) * np.float32(-2.0 * math.log(10000.0) / half))
    angle = (np.arange(SIDE, dtype=np.float32) + 1.0) * np.float32(2.0 * math.pi / SIDE)
    angle = angle[:, None] * inverse
    return np.where(channel % 2 == 0, np.sin(angle), np.cos(angle)).astype(np.float32)


def dot(a, b):
    return jnp.dot(a, b, preferred_element_type=f32)


def dot_nt(a, b):
    return lax.dot_general(a, b, (((1,), (1,)), ((), ())), preferred_element_type=f32)


def dot_tn(a, b):
    return lax.dot_general(a, b, (((0,), (0,)), ((), ())), preferred_element_type=f32)


def row_total(values):
    return jnp.sum(values.astype(f32), axis=0, keepdims=True)


def norm_forward(values):
    average = jnp.mean(values, axis=-1, keepdims=True)
    centred = values - average
    variance = jnp.mean(centred * centred, axis=-1, keepdims=True)
    rstd = lax.rsqrt(variance + norm_eps)
    return centred * rstd, rstd


def norm_backward(grad, normed, rstd, gain):
    grad_normed = grad * gain
    first = jnp.mean(grad_normed, axis=-1, keepdims=True)
    second = jnp.mean(grad_normed * normed, axis=-1, keepdims=True)
    grad_in = rstd * (grad_normed - first - normed * second)
    return grad_in, row_total(grad * normed), row_total(grad)


def spread_rows(rows):
    head = lax.broadcasted_iota(jnp.int32, (NP, D), 1) // HD
    return jnp.concatenate(
        [jnp.where(head == h, rows, 0.0) for h in range(HEADS)], axis=0
    ).astype(bf16)


def spread_cols(cols):
    head = lax.broadcasted_iota(jnp.int32, (D, NP), 0) // HD
    return jnp.concatenate(
        [jnp.where(head == h, cols, 0.0) for h in range(HEADS)], axis=1
    ).astype(bf16)


def project_heads(weight_t, sums):
    high = sums.astype(bf16)
    low = (sums - high.astype(f32)).astype(bf16)
    return own_blocks(
        [
            dot(weight_t[pair_rows(p)], high[:, pair_cols(p)])
            + dot(weight_t[pair_rows(p)], low[:, pair_cols(p)])
            for p in range(4)
        ]
    )


def own_blocks(pairs):
    parts = []
    for pair in pairs:
        parts += [pair[:HD, :NP], pair[HD:, NP:]]
    return jnp.concatenate(parts, axis=0)


def head_rows(row):
    return jnp.concatenate([row[:, NP * h : NP * h + NP] for h in range(HEADS)], axis=0)


def head_line(rows):
    return jnp.concatenate([rows[h : h + 1] for h in range(HEADS)], axis=1)


def per_channel(rows):
    return jnp.concatenate(
        [jnp.broadcast_to(rows[h : h + 1], (HD, NP)) for h in range(HEADS)], axis=0
    )


def head_sums(cols):
    return jnp.concatenate(
        [jnp.sum(cols[HD * h : HD * h + HD], axis=0, keepdims=True) for h in range(HEADS)], axis=0
    )


def pair_cols(p):
    return slice(PAIR * p, PAIR * p + PAIR)


def pair_rows(p):
    return slice(2 * HD * p, 2 * HD * p + 2 * HD)


class Place:
    def __init__(self, pages):
        self.axes = axes_of(pages)
        self.page = lax.axis_index("dp")
        self.member = lax.axis_index("blk")
        self.digit = {
            name: self.member if name == "x" else lax.rem(self.page // stride, radix)
            for name, (radix, stride) in self.axes.items()
        }

    def size(self, group):
        return math.prod(self.axes[name][0] for name in group)

    def index(self, group):
        index = 0
        for name in group:
            index = index * self.axes[name][0] + self.digit[name]
        return index

    def peer(self, group, hop):
        index = lax.rem(self.index(group) + hop, self.size(group))
        page, member, rest = self.page, self.member, index
        for name in reversed(group):
            radix, stride = self.axes[name]
            digit = lax.rem(rest, radix)
            rest = rest // radix
            if name == "x":
                member = digit
            else:
                page = page + (digit - self.digit[name]) * stride
        return (page, member), index


class PageSum:
    def __init__(self, place, groups, back, rows, landing, whole, sent, arrived):
        self.place, self.groups, self.back = place, groups, back
        self.rows, self.landing, self.whole = rows, landing, whole
        self.sent, self.arrived = sent, arrived
        self.slots = 0
        self.extents = [rows.shape[0]]
        self.bases = [0]
        self.landings = []
        at = 0
        for group in groups:
            size = place.size(group)
            extent = self.extents[-1] // size
            self.landings.append(at)
            at += (size - 1) * extent
            self.bases.append(pl.multiple_of(self.bases[-1] + place.index(group) * extent, TILE))
            self.extents.append(extent)
        last = len(groups)
        moves = [self.scatter_moves(s) for s in range(last)]
        near = {"all": 0, "across": 1, "sides": 2}[back]
        moves += [self.gather_moves(s) for s in range(last - 1, near - 1, -1)]
        if back == "sides":
            moves += [self.side_moves(), self.corner_moves(), self.core_moves()]
        elif back == "across":
            moves += [self.across_moves(), self.core_moves()]
        self.phases = [functools.partial(self.step, moves, k) for k in range(len(moves) + 1)]

    @staticmethod
    def landing_rows(pages, groups, rows):
        axes = axes_of(pages)
        total, extent = 0, rows
        for group in groups:
            size = math.prod(axes[name][0] for name in group)
            extent //= size
            total += (size - 1) * extent
        return total

    def step(self, moves, k):
        last = len(self.groups)
        if k > 0:
            for move in moves[k - 1]:
                for copy in self.copies(*move):
                    copy.wait()
        if 0 < k <= last:
            total = self.scatter_sum(k - 1)
            region = pl.ds(self.bases[k], self.extents[k])
            if k < last:
                self.rows[region] = total
            elif len(self.whole.shape) == 3:
                self.whole[self.place.member, region] = total
            else:
                self.whole[region] = total
        if k < len(moves):
            for move in moves[k]:
                for copy in self.copies(*move):
                    copy.start()

    def copies(self, slot, source, target, device):
        rows = source().shape[0]
        count = PIECES if rows % (PIECES * 32) == 0 else 2 if rows % 64 == 0 else 1
        for k in range(count):
            part = pl.ds(k * (rows // count), rows // count)
            yield pltpu.make_async_remote_copy(
                src_ref=source().at[part],
                dst_ref=target().at[part],
                send_sem=self.sent.at[slot + k],
                recv_sem=self.arrived.at[slot + k],
                device_id=device,
                device_id_type=pl.DeviceIdType.MESH,
            )

    def new_slot(self):
        self.slots += PIECES
        return self.slots - PIECES

    def same(self, device, view):
        return (self.new_slot(), view, view, device)

    def scatter_moves(self, step):
        group = self.groups[step]
        extent = self.extents[step + 1]
        moves = []
        for hop in range(1, self.place.size(group)):
            device, other = self.place.peer(group, hop)
            start = pl.multiple_of(self.bases[step] + other * extent, TILE)
            landing = self.landings[step] + (hop - 1) * extent
            moves.append(
                (
                    self.new_slot(),
                    functools.partial(self.part, self.rows, start, extent),
                    functools.partial(self.part, self.landing, landing, extent),
                    device,
                )
            )
        return moves

    @staticmethod
    def part(ref, start, extent):
        return ref.at[pl.ds(start, extent)]

    def half(self, member, start, extent):
        if len(self.whole.shape) == 3:
            return self.whole.at[member, pl.ds(start, extent)]
        return self.whole.at[pl.ds(start, extent)]

    def scatter_sum(self, step):
        extent = self.extents[step + 1]
        total = self.rows[pl.ds(self.bases[step + 1], extent)].astype(f32)
        for hop in range(1, self.place.size(self.groups[step])):
            landing = self.landings[step] + (hop - 1) * extent
            total = total + self.landing[pl.ds(landing, extent)].astype(f32)
        return total.astype(bf16)

    def gather_moves(self, step):
        group = self.groups[step]
        view = functools.partial(self.half, self.place.member, self.bases[step + 1], self.extents[step + 1])
        return [
            self.same(self.place.peer(group, hop)[0], view) for hop in range(1, self.place.size(group))
        ]

    def own_quarter(self):
        step = 2 if len(self.groups[0]) == 1 else 1
        return self.bases[step], self.extents[step]

    def side_moves(self):
        view = functools.partial(self.half, self.place.member, *self.own_quarter())
        return [self.same(self.place.peer((name,), 1)[0], view) for name in ("y", "x")]

    def corner_moves(self):
        base, extent = self.own_quarter()
        other = pl.multiple_of(base + (1 - 2 * self.place.digit["y"]) * extent, TILE)
        view = functools.partial(self.half, self.place.member, other, extent)
        return [self.same(self.place.peer(("x",), 1)[0], view)]

    def across_moves(self):
        view = functools.partial(self.half, self.place.member, *self.own_quarter())
        return [self.same(self.place.peer(("x", "y"), hop)[0], view) for hop in range(1, 4)]

    def core_moves(self):
        extent = self.extents[0] // 2
        start = pl.multiple_of(self.place.digit["core"] * extent, TILE)
        device, _ = self.place.peer(("core",), 1)
        return [self.same(device, functools.partial(self.half, m, start, extent)) for m in range(2)]


def clear_rest(ref, used):
    if ref.shape[0] > used:
        ref[used:] = jnp.zeros((ref.shape[0] - used, D), ref.dtype)


def layer_kernel(
    tokens,
    pages,
    queries_in,
    memory_hbm,
    turns_in,
    order_in,
    lengths_in,
    attn_in,
    attn_out,
    attn_bias,
    ffn_in_hbm,
    ffn_in_bias,
    ffn_out_hbm,
    ffn_out_bias,
    norm_gain,
    norm_bias,
    pos_in,
    out_grad_in,
    table_in,
    result_hbm,
    queries_grad_hbm,
    memory_grad_hbm,
    whole_f_hbm,
    whole_t_hbm,
    whole_k_hbm,
    memory_s,
    key_in_s,
    probs_s,
    grad_scores_s,
    code_s,
    query_kt,
    grad_vt,
    back_s,
    table_s,
    top_s,
    highest_s,
    shifts_s,
    factor_s,
    total_s,
    mixed_s,
    pad_s,
    result_out,
    queries_grad_out,
    send_a,
    recv_a,
    send_t,
    recv_t,
    send_b,
    recv_b,
    small_s,
    rows_f,
    landing_f,
    whole_f,
    rows_t,
    landing_t,
    whole_t,
    rows_k,
    landing_k,
    whole_k,
    load_sem,
    store_sem,
    link_sem,
    sent_f,
    arrived_f,
    sent_t,
    arrived_t,
    sent_k,
    arrived_k,
):
    member = lax.axis_index("blk")
    partner = (lax.axis_index("dp"), 1 - member)
    chunks = tokens // CHUNK

    place = Place(pages)
    groups_f, groups_t, groups_k = sum_groups(pages)
    sum_f = PageSum(place, groups_f, "sides", rows_f, landing_f, whole_f, sent_f, arrived_f)
    sum_t = PageSum(place, groups_t, "across", rows_t, landing_t, whole_t, sent_t, arrived_t)
    sum_k = PageSum(place, groups_k, "all", rows_k, landing_k, whole_k, sent_k, arrived_k)

    barrier = pltpu.get_barrier_semaphore()
    peers = [
        place.peer(group, hop)[0]
        for group in [("x", "core", "y"), *far_axes(pages)]
        for hop in range(1, place.size(group))
    ]
    for peer in peers:
        pl.semaphore_signal(barrier, inc=1, device_id=peer, device_id_type=pl.DeviceIdType.MESH)

    load_memory = pltpu.make_async_copy(memory_hbm.at[0], memory_s, load_sem.at[0])
    half = FF // 2
    ffn_in_s = [grad_scores_s.at[D * k : D * k + D] for k in range(2)]
    ffn_out_s = grad_scores_s.at[2 * D : 2 * D + FF, :D]
    free = 2 * D + FF
    active_s = [grad_scores_s.at[free + NP * k : free + NP * k + NP] for k in range(2)]
    slope_s = [grad_scores_s.at[free + NP * k : free + NP * k + NP] for k in range(2, 4)]
    load_ffn = [
        pltpu.make_async_copy(ffn_in_hbm.at[:, half * k : half * k + half], ffn_in_s[k], load_sem.at[1 + k])
        for k in range(2)
    ]
    load_ffn.append(pltpu.make_async_copy(ffn_out_hbm, ffn_out_s, load_sem.at[3]))
    load_memory.start()
    for load in load_ffn:
        load.start()

    pairs = [attn_bias[j].astype(f32) for j in range(3)]
    bias = jnp.concatenate([pair[k : k + 1] for k in range(2) for pair in pairs], axis=0)
    gain = norm_gain[...].astype(f32)
    shift = norm_bias[...].astype(f32)

    order = order_in[...]
    turn = turns_in[0]
    row_at = order >> 7
    col_at = order & 127
    top = SIDE - 1
    row_new = jnp.where(
        turn == 0, row_at, jnp.where(turn == 1, col_at, jnp.where(turn == 2, top - row_at, top - col_at))
    )
    col_new = jnp.where(
        turn == 0, col_at, jnp.where(turn == 1, top - row_at, jnp.where(turn == 2, top - col_at, row_at))
    )
    past = jnp.where(order < lengths_in[0], 0, SIDE * SIDE)
    code_s[...] = (row_new * SIDE + col_new + past).astype(f32)

    pad_s[...] = jnp.zeros_like(pad_s)
    pad_s[0, :NQ] = queries_in[0].astype(f32)
    pad_s[1, :NQ] = pos_in[...].astype(f32)
    pad_s[2, :NQ] = out_grad_in[0].astype(f32)
    queries_f = pad_s[0]
    pos_f = pad_s[1]
    queries_b = queries_f.astype(bf16)
    mixed_q = (queries_f + pos_f).astype(bf16)
    query_self = (dot(mixed_q, attn_in[0, 0]) + bias[0:1]).astype(bf16)
    key_self = dot(mixed_q, attn_in[0, 1]).astype(bf16)
    value_self = (dot(queries_b, attn_in[0, 2]) + bias[1:2]).astype(bf16)
    scores = dot(key_self, spread_cols(query_self.astype(f32).T)) * scale
    own_key = lax.broadcasted_iota(jnp.int32, (NP, HQ), 0) < NQ
    scores = jnp.where(own_key, scores, masked_score)
    raised = jnp.exp(scores - jnp.max(scores, axis=0, keepdims=True))
    probs_self = raised / jnp.sum(raised, axis=0, keepdims=True)
    probs_self_b = probs_self.astype(bf16)
    value_t = value_self.astype(f32).T.astype(bf16)
    attended = own_blocks(
        [dot(value_t[pair_rows(p)], probs_self_b[:, pair_cols(p)]) for p in range(4)]
    ).T.astype(bf16)
    first_normed, first_rstd = norm_forward(queries_f + dot(attended, attn_out[0]) + bias[2:3])
    first = first_normed * gain[0:1] + shift[0:1]
    cross_q = (first + pos_f).astype(bf16)
    query_c = (dot(cross_q, attn_in[1, 0]) + bias[3:4]).astype(bf16)
    query_x = spread_rows(query_c.astype(f32))
    query_k = dot(attn_in[1, 1], spread_cols(query_c.astype(f32).T))
    query_kt[...] = (query_k * (scale * log2e)).astype(bf16)
    back_s[:HQ] = (dot_nt(query_x, attn_in[1, 1]) * scale).astype(bf16)
    table = table_in[...]
    nothing = jnp.zeros((SIDE, D // 2), f32)
    table = jnp.concatenate(
        [jnp.concatenate([table, nothing], axis=1), jnp.concatenate([nothing, table], axis=1)], axis=0
    )
    table_high = table.astype(bf16)
    table_s[: 2 * SIDE] = table_high
    table_s[2 * SIDE :] = (table - table_high.astype(f32)).astype(bf16)

    load_memory.wait()
    def mask_view(i):
        side, place = i // (chunks // 2), lax.rem(i, chunks // 2)
        return grad_scores_s.at[
            pl.ds(pl.multiple_of(tokens // 2 + place * CHUNK, CHUNK), CHUNK),
            pl.ds(pl.multiple_of(side * NP, NP), NP),
        ]

    lane = lax.broadcasted_iota(jnp.int32, (CHUNK, NP), 1)

    @pl.loop(0, chunks)
    def _(i):
        rows = pl.ds(pl.multiple_of(i * CHUNK, CHUNK), CHUNK)
        line = code_s[:, rows]
        code = jnp.concatenate(
            [
                jnp.broadcast_to(line[:, NP * j : NP * j + NP], (NP, NP)).T
                for j in range(CHUNK // NP)
            ],
            axis=0,
        ).astype(jnp.int32)
        row_hot = jnp.where(((code >> 7) & 127) == lane, 1.0, 0.0).astype(bf16)
        col_hot = jnp.where((code & 127) == lane, 1.0, 0.0).astype(bf16)
        hot = jnp.concatenate([row_hot, col_hot, row_hot, col_hot], axis=1)
        masked = jnp.where(code < SIDE * SIDE, 0.0, masked_score)
        mask_view(i)[...] = masked.astype(bf16)
        key_in_s[rows] = (memory_s[rows].astype(f32) + dot(hot, table_s[...])).astype(bf16)

    def score_pair(p, key_in, mask, score_s):
        cols = pair_cols(p)
        part = dot(key_in, query_kt[:, cols]) + mask
        score_s[:, cols] = part
        top_s[:, cols] = jnp.max(part.reshape(CHUNK // 8, 8, PAIR), axis=0)

    def score_operands(i):
        rows = pl.ds(pl.multiple_of(i * CHUNK, CHUNK), CHUNK)
        mask = mask_view(i)[...].astype(f32)
        return key_in_s[rows], jnp.concatenate([mask, mask], axis=1)

    def attend_all(score_s):
        operands = score_operands(0)
        for p in range(4):
            score_pair(p, *operands, score_s)

        @pl.loop(0, chunks)
        def _(i):
            rows = pl.ds(pl.multiple_of(i * CHUNK, CHUNK), CHUNK)
            memory_ct = memory_s[rows].T
            operands = score_operands(jnp.minimum(i + 1, chunks - 1))
            for p in range(4):
                cols = pair_cols(p)
                before = highest_s[0:1, cols]
                highest = jnp.maximum(before, jnp.max(top_s[:, cols], axis=0, keepdims=True))
                highest_s[0:1, cols] = highest
                shifts_s[pl.ds(i, 1), cols] = highest
                fade = jnp.exp2(before - highest)
                raised = jnp.exp2(score_s[:, cols] - highest)
                sums = jnp.sum(raised.reshape(CHUNK // 8, 8, PAIR), axis=0)
                total_s[:, cols] = total_s[:, cols] * fade + sums
                probs_s[rows, cols] = raised.astype(bf16)
                mixed_s[:, cols] = mixed_s[:, cols] * fade + dot(memory_ct, probs_s[rows, cols])
                score_pair(p, *operands, score_s)

    highest_s[0:1] = jnp.full((1, HQ), -3e38, f32)
    total_s[...] = jnp.zeros_like(total_s)
    mixed_s[...] = jnp.zeros_like(mixed_s)
    pl.run_scoped(attend_all, pltpu.VMEM((CHUNK, HQ), f32))
    highest_own = highest_s[0:1]
    total_own = jnp.sum(total_s[...], axis=0, keepdims=True)

    value_wt = attn_in[1, 2].astype(f32).T.astype(bf16)
    key_wt = attn_in[1, 1].astype(f32).T.astype(bf16)
    send_a[...] = project_heads(value_wt, mixed_s[...]).astype(bf16)
    send_t[:HEADS] = head_rows(highest_own)
    send_t[HEADS:] = head_rows(total_own)
    pl.semaphore_wait(barrier, len(peers))
    swap_a = pltpu.make_async_remote_copy(
        src_ref=send_a,
        dst_ref=recv_a,
        send_sem=link_sem.at[0],
        recv_sem=link_sem.at[1],
        device_id=partner,
        device_id_type=pl.DeviceIdType.MESH,
    )
    swap_t = pltpu.make_async_remote_copy(
        src_ref=send_t,
        dst_ref=recv_t,
        send_sem=link_sem.at[4],
        recv_sem=link_sem.at[5],
        device_id=partner,
        device_id_type=pl.DeviceIdType.MESH,
    )
    swap_a.start()
    swap_t.start()
    swap_a.wait()
    swap_t.wait()
    is_first = member == 0
    own, other = send_a[...].astype(f32), recv_a[...].astype(f32)
    left = jnp.where(is_first, own, other)
    right = jnp.where(is_first, other, own)
    own, other = send_t[...], recv_t[...]
    left_t = jnp.where(is_first, own, other)
    right_t = jnp.where(is_first, other, own)
    highest = jnp.maximum(left_t[:HEADS], right_t[:HEADS])
    fade_l = jnp.exp2(left_t[:HEADS] - highest)
    fade_r = jnp.exp2(right_t[:HEADS] - highest)
    total = left_t[HEADS:] * fade_l + right_t[HEADS:] * fade_r
    mixed_t = left * per_channel(fade_l / total) + right * per_channel(fade_r / total)
    log_total = head_line(highest + jnp.log2(total))
    own_share = jnp.exp2(highest_own - log_total)
    factor_s[...] = jnp.exp2(shifts_s[...] - log_total)
    attended_c = (mixed_t.T + bias[4:5]).astype(bf16)

    second_normed, second_rstd = norm_forward(first + dot(attended_c, attn_out[1]) + bias[5:6])
    second = second_normed * gain[1:2] + shift[1:2]
    ffn_input = second.astype(bf16)
    load_ffn[0].wait()
    load_ffn[1].wait()
    blocks = [(j // 4, slice(D * j, D * j + D), slice(j % 4 * D, j % 4 * D + D)) for j in range(FF // D)]
    hidden_bias = ffn_in_bias[...].astype(f32).reshape(1, FF)
    def feed_forward(gate_s):
        for k, cols, part in blocks:
            hidden = dot(ffn_input, ffn_in_s[k][:, part]) + hidden_bias[:, cols]
            half_gate = 0.5 + 0.5 * lax.erf(hidden * math.sqrt(0.5))
            active_s[k][:, part] = (hidden * half_gate).astype(bf16)
            gate_s[:, cols] = half_gate + hidden * jnp.exp(hidden * hidden * -0.5) * (
                1.0 / math.sqrt(2.0 * math.pi)
            )
        load_ffn[2].wait()
        third_normed, third_rstd = norm_forward(
            second
            + dot(active_s[0][...], ffn_out_s[:half])
            + dot(active_s[1][...], ffn_out_s[half:])
            + ffn_out_bias[...].astype(f32).reshape(1, D)
        )
        result_out[...] = (third_normed * gain[2:3] + shift[2:3])[:NQ].astype(bf16)
        grad_third, gain_grad_2, shift_grad_2 = norm_backward(
            pad_s[2], third_normed, third_rstd, gain[2:3]
        )
        grad_branch_f = grad_third.astype(bf16)
        for k, cols, part in blocks:
            grad_hidden = dot_nt(grad_branch_f, ffn_out_s[cols]) * gate_s[:, cols]
            slope_s[k][:, part] = grad_hidden.astype(bf16)
        return grad_third, gain_grad_2, shift_grad_2, grad_branch_f

    grad_third, gain_grad_2, shift_grad_2, grad_branch_f = pl.run_scoped(
        feed_forward, pltpu.VMEM((NP, FF), f32)
    )
    grad_second = grad_third + dot_nt(slope_s[0][...], ffn_in_s[0][...])
    grad_second += dot_nt(slope_s[1][...], ffn_in_s[1][...])
    grad_second_in, gain_grad_1, shift_grad_1 = norm_backward(
        grad_second, second_normed, second_rstd, gain[1:2]
    )
    grad_branch_c = grad_second_in.astype(bf16)
    ffn_input_t = second.T.astype(bf16)

    @pl.when(member == 0)
    def _():
        for k, cols, part in blocks:
            rows_f[cols] = dot(ffn_input_t, slope_s[k][:, part]).astype(bf16)

    @pl.when(member == 1)
    def _():
        for k, cols, part in blocks:
            rows_f[cols] = dot_tn(active_s[k][:, part], grad_branch_f).astype(bf16)

    is_first = member == 0
    out_grad_c = dot_tn(attended_c, grad_branch_c)
    rows_k[2 * D : 3 * D] = jnp.where(is_first, out_grad_c, 0.0).astype(bf16)

    clear_rest(rows_f, ROWS_F)
    clear_rest(rows_t, ROWS_T)
    clear_rest(rows_k, ROWS_K)
    sum_f.phases[0]()
    grad_attended_c = dot_nt(grad_branch_c, attn_out[1]).astype(bf16).astype(f32)
    small_s[:16] = jnp.concatenate(
        [row_total(slope_s[k][:, part]) for k, _, part in blocks]
        + [
            row_total(grad_branch_f),
            row_total(grad_branch_c),
            gain_grad_2,
            shift_grad_2,
            gain_grad_1,
            shift_grad_1,
            row_total(grad_attended_c),
            jnp.zeros((1, D), f32),
        ],
        axis=0,
    )

    store_result = pltpu.make_async_copy(result_out, result_hbm, load_sem.at[7])
    store_result.start()

    grad_attended_t = grad_attended_c.T
    grad_x = spread_rows(grad_attended_c)
    grad_v = dot(attn_in[1, 2], spread_cols(grad_attended_t))
    grad_vt[...] = grad_v.astype(bf16)
    back_s[HQ:] = grad_v.T.astype(bf16)
    inner = head_line(head_sums(grad_attended_t * mixed_t))
    rows_k[D : 2 * D] = dot((mixed_s[...] * own_share).astype(bf16), grad_x).astype(bf16)
    mixed_s[...] = jnp.zeros_like(mixed_s)

    queue_f = sum_f.phases[1:]
    queue_t = list(sum_t.phases)
    queue_k = list(sum_k.phases)

    def take(queue):
        if queue:
            queue.pop(0)()

    def at(i, steps):
        for step, queue in steps:
            pl.when(i == (step * chunks) // 16)(queue.pop(0))

    @pl.loop(0, chunks)
    def _(i):
        rows = pl.ds(pl.multiple_of(i * CHUNK, CHUNK), CHUNK)
        key_ct = key_in_s[rows].T
        memory_c = memory_s[rows]
        for p in range(4):
            cols = pair_cols(p)
            grad_probs = dot(memory_c, grad_vt[:, cols])
            probs = probs_s[rows, cols].astype(f32) * factor_s[pl.ds(i, 1), cols]
            probs_s[rows, cols] = probs.astype(bf16)
            grad_scores_s[rows, cols] = (probs * (grad_probs - inner[:, cols])).astype(bf16)
        mixed_s[...] += dot(key_ct, grad_scores_s[rows])
        at(i, [(3, queue_f), (9, queue_f), (15, queue_f)])

    send_b[...] = (project_heads(key_wt, mixed_s[...]) * scale).astype(bf16)
    swap_b = pltpu.make_async_remote_copy(
        src_ref=send_b,
        dst_ref=recv_b,
        send_sem=link_sem.at[2],
        recv_sem=link_sem.at[3],
        device_id=partner,
        device_id_type=pl.DeviceIdType.MESH,
    )
    swap_b.start()
    query_x = spread_rows(query_c.astype(f32))
    rows_k[:D] = (dot(mixed_s[...].astype(bf16), query_x) * scale).astype(bf16)
    take(queue_k)
    swap_b.wait()
    take(queue_f)
    take(queue_k)
    grad_query_c = (send_b[...].astype(f32) + recv_b[...].astype(f32)).T.astype(bf16)

    cross_pos_grad = dot_nt(grad_query_c, attn_in[1, 0])
    grad_first_in, gain_grad_0, shift_grad_0 = norm_backward(
        grad_second_in + cross_pos_grad, first_normed, first_rstd, gain[0:1]
    )
    grad_branch = grad_first_in.astype(bf16)
    grad_attended = dot_nt(grad_branch, attn_out[0]).astype(bf16).astype(f32)
    take(queue_k)
    grad_probs = dot(value_self, spread_cols(grad_attended.T))
    inner_self = jnp.sum(probs_self * grad_probs, axis=0, keepdims=True)
    grad_scores = (probs_self * (grad_probs - inner_self)).astype(bf16)
    key_t = key_self.astype(f32).T.astype(bf16)
    grad_query_s = (
        own_blocks([dot(key_t[pair_rows(p)], grad_scores[:, pair_cols(p)]) for p in range(4)]) * scale
    ).T.astype(bf16)
    grad_key_s = (dot(grad_scores, spread_rows(query_self.astype(f32))) * scale).astype(bf16)
    grad_value_s = dot(probs_self_b, spread_rows(grad_attended)).astype(bf16)
    grad_mixed_q = dot_nt(grad_query_s, attn_in[0, 0]) + dot_nt(grad_key_s, attn_in[0, 1])
    queries_grad_out[...] = (grad_first_in + grad_mixed_q + dot_nt(grad_value_s, attn_in[0, 2]))[
        :NQ
    ].astype(bf16)
    store_queries = pltpu.make_async_copy(queries_grad_out, queries_grad_hbm, load_sem.at[8])
    store_queries.start()
    small_s[16:] = jnp.concatenate(
        [
            row_total(grad_query_s),
            row_total(grad_value_s),
            row_total(grad_branch),
            row_total(grad_query_c),
            gain_grad_0,
            shift_grad_0,
            jnp.zeros((10, D), f32),
        ],
        axis=0,
    )
    @pl.when(member == 0)
    def _():
        rows_t[:D] = dot_tn(mixed_q, grad_query_s).astype(bf16)
        rows_t[D : 2 * D] = dot_tn(mixed_q, grad_key_s).astype(bf16)
        rows_t[2 * D : 3 * D] = dot_tn(queries_b, grad_value_s).astype(bf16)

    @pl.when(member == 1)
    def _():
        rows_t[:D] = dot_tn(cross_q, grad_query_c).astype(bf16)
        rows_t[D : 2 * D] = dot_tn(attended, grad_branch).astype(bf16)
        rows_t[ROW_POS:ROW_SMALL] = (grad_mixed_q + cross_pos_grad).astype(bf16)
        rows_t[ROW_SMALL : ROW_SMALL + 32] = small_s[...].astype(bf16)
        rows_t[ROW_SMALL + 32 : ROWS_T] = jnp.zeros((ROWS_T - ROW_SMALL - 32, D), bf16)

    take(queue_t)
    take(queue_k)
    take(queue_f)

    @pl.loop(0, chunks)
    def _(i):
        rows = pl.ds(pl.multiple_of(i * CHUNK, CHUNK), CHUNK)
        both = jnp.concatenate([grad_scores_s[rows], probs_s[rows]], axis=1)
        memory_s[rows] = dot(both, back_s[...]).astype(bf16)
        pltpu.make_async_copy(memory_s.at[rows], memory_grad_hbm.at[0, rows], store_sem.at[i]).start()
        at(
            i,
            [
                (3, queue_t),
                (4, queue_k),
                (7, queue_t),
                (8, queue_k),
                (9, queue_f),
                (11, queue_t),
                (12, queue_k),
                (15, queue_t),
            ],
        )

    while queue_f:
        take(queue_f)
    stores = [
        pltpu.make_async_copy(whole, target, load_sem.at[4 + k])
        for k, (whole, target) in enumerate(
            (
                (whole_f, whole_f_hbm),
                (whole_t, whole_t_hbm),
                (whole_k, whole_k_hbm),
            )
        )
    ]
    stores[0].start()
    while queue_t or queue_k:
        take(queue_t)
        take(queue_k)
    for store in stores[1:]:
        store.start()

    @pl.loop(0, chunks)
    def _(i):
        rows = pl.ds(pl.multiple_of(i * CHUNK, CHUNK), CHUNK)
        pltpu.make_async_copy(memory_s.at[rows], memory_grad_hbm.at[0, rows], store_sem.at[i]).wait()

    for store in [*stores, store_result, store_queries]:
        store.wait()


def finish_kernel(
    result_in,
    queries_grad_in,
    memory_grad_in,
    whole_f_hbm,
    whole_t_hbm,
    whole_k_hbm,
    result_hbm,
    queries_grad_hbm,
    memory_grad,
    attn_in_hbm,
    attn_out_hbm,
    attn_bias_hbm,
    ffn_in_hbm,
    ffn_in_bias_hbm,
    ffn_out_hbm,
    ffn_out_bias_hbm,
    norm_gain_hbm,
    norm_bias_hbm,
    query_pos_hbm,
    moved,
    whole_f,
    whole_t,
    whole_k,
    result,
    queries_grad,
    attn_in_grad,
    attn_out_grad,
    attn_bias_grad,
    ffn_in_grad,
    ffn_in_bias_grad,
    ffn_out_grad,
    ffn_out_bias_grad,
    norm_gain_grad,
    norm_bias_grad,
    query_pos_grad,
    in_sem,
    out_sem,
    sum_sem,
    grad_sem,
):
    pieces = in_sem.shape[0]
    piece = moved.shape[0] // pieces

    def fetch(j):
        rows = pl.ds(piece * j, piece)
        return pltpu.make_async_copy(memory_grad_in.at[0, rows], moved.at[rows], in_sem.at[j])

    def write(j):
        rows = pl.ds(piece * j, piece)
        return pltpu.make_async_copy(moved.at[rows], memory_grad.at[0, rows], out_sem.at[j])

    sums = [
        (whole_t_hbm, whole_t),
        (whole_k_hbm, whole_k),
        (whole_f_hbm, whole_f),
        (result_in, result),
        (queries_grad_in, queries_grad),
    ]
    loads = [pltpu.make_async_copy(*pair, sum_sem.at[j]) for j, pair in enumerate(sums)]
    for load in loads:
        load.start()
    for j in range(pieces):
        fetch(j).start()
    blocks = FF // D
    stores = []

    def store(source, target):
        stores.append(pltpu.make_async_copy(source, target, grad_sem.at[len(stores)]))
        stores[-1].start()

    loads[0].wait()
    loads[1].wait()
    for j in range(3):
        attn_in_grad[0, j] = whole_t[0, D * j : D * j + D].astype(f32)
    attn_in_grad[1, 0] = whole_t[1, :D].astype(f32)
    attn_in_grad[1, 1] = whole_k[:D].astype(f32)
    attn_in_grad[1, 2] = whole_k[D : 2 * D].astype(f32)
    store(attn_in_grad, attn_in_hbm)
    attn_out_grad[0] = whole_t[1, D : 2 * D].astype(f32)
    attn_out_grad[1] = whole_k[2 * D : 3 * D].astype(f32)
    store(attn_out_grad, attn_out_hbm)
    loads[2].wait()
    for k in range(2):
        half = slice(FF // 2 * k, FF // 2 * (k + 1))
        ffn_out_grad[half] = whole_f[1, half].astype(f32)
        store(ffn_out_grad.at[half], ffn_out_hbm.at[half])
    for k in range(2):
        half = slice(FF // 2 * k, FF // 2 * (k + 1))
        for j in range(blocks // 2 * k, blocks // 2 * (k + 1)):
            at = slice(D * j, D * j + D)
            ffn_in_grad[:, at] = whole_f[0, at].astype(f32)
        store(ffn_in_grad.at[:, half], ffn_in_hbm.at[:, half])
    for j in range(pieces):
        fetch(j).wait()
        write(j).start()
    loads[3].wait()
    store(result, result_hbm.at[0])
    loads[4].wait()
    store(queries_grad, queries_grad_hbm.at[0])
    query_pos_grad[...] = whole_t[1, ROW_POS:ROW_SMALL].astype(f32)[:NQ]
    store(query_pos_grad, query_pos_hbm)
    small = whole_t[1, ROW_SMALL : ROW_SMALL + 32].astype(f32)
    ffn_in_bias_grad[...] = jnp.concatenate([small[j : j + 1] for j in range(blocks)], axis=1)
    store(ffn_in_bias_grad, ffn_in_bias_hbm)
    ffn_out_bias_grad[...] = small[8:9]
    store(ffn_out_bias_grad, ffn_out_bias_hbm)
    for j, (own, cross) in enumerate(((16, 19), (17, 14), (18, 9))):
        attn_bias_grad[j, 0:1] = small[own : own + 1]
        attn_bias_grad[j, 1:2] = small[cross : cross + 1]
    store(attn_bias_grad, attn_bias_hbm)
    for j, (gain, shift) in enumerate(((20, 21), (12, 13), (10, 11))):
        norm_gain_grad[j : j + 1] = small[gain : gain + 1]
        norm_bias_grad[j : j + 1] = small[shift : shift + 1]
    store(norm_gain_grad, norm_gain_hbm)
    store(norm_bias_grad, norm_bias_hbm)
    for j in range(pieces):
        write(j).wait()
    for copy in stores:
        copy.wait()


def body(
    pages,
    queries,
    memory,
    quarter_turns,
    token_order,
    lengths,
    attn_in,
    attn_out,
    attn_bias,
    ffn_in,
    ffn_in_bias,
    ffn_out,
    ffn_out_bias,
    norm_gain,
    norm_bias,
    query_pos,
    out_grad,
):
    tokens = memory.shape[1]
    chunks = tokens // CHUNK
    groups_f, groups_t, groups_k = sum_groups(pages)
    summed = [
        (padded(ROWS_F, pages), groups_f),
        (padded(ROWS_T, pages), groups_t),
        (padded(ROWS_K, 2 * pages), groups_k),
    ]
    whole_shapes = [(2, rows, D) for rows, _ in summed[:2]] + [(summed[2][0], D)]
    sum_buffers = []
    for (rows, groups), shape in zip(summed, whole_shapes):
        landing = PageSum.landing_rows(pages, groups, rows)
        sum_buffers += [pltpu.VMEM(each, bf16) for each in ((rows, D), (landing, D), shape)]
    copies = 32 * PIECES
    vmem = pl.BlockSpec(memory_space=pltpu.VMEM)
    smem = pl.BlockSpec(memory_space=pltpu.SMEM)
    anywhere = pl.BlockSpec(memory_space=pl.ANY)
    parts = pl.pallas_call(
        functools.partial(layer_kernel, tokens, pages),
        out_shape=[
            jax.ShapeDtypeStruct((NQ, D), bf16),
            jax.ShapeDtypeStruct((NQ, D), bf16),
            jax.ShapeDtypeStruct((1, tokens, D), bf16),
            *(jax.ShapeDtypeStruct(shape, bf16) for shape in whole_shapes),
        ],
        in_specs=[
            vmem,
            anywhere,
            smem,
            vmem,
            smem,
            vmem,
            vmem,
            vmem,
            anywhere,
            vmem,
            anywhere,
            vmem,
            vmem,
            vmem,
            vmem,
            vmem,
            vmem,
        ],
        out_specs=[anywhere] * 6,
        scratch_shapes=[
            pltpu.VMEM((tokens, D), bf16),
            pltpu.VMEM((tokens, D), bf16),
            pltpu.VMEM((tokens, HQ), bf16),
            pltpu.VMEM((tokens, HQ), bf16),
            pltpu.VMEM((1, tokens), f32),
            pltpu.VMEM((D, HQ), bf16),
            pltpu.VMEM((D, HQ), bf16),
            pltpu.VMEM((2 * HQ, D), bf16),
            pltpu.VMEM((4 * SIDE, D), bf16),
            pltpu.VMEM((8, HQ), f32),
            pltpu.VMEM((8, HQ), f32),
            pltpu.VMEM((chunks, HQ), f32),
            pltpu.VMEM((chunks, HQ), f32),
            pltpu.VMEM((8, HQ), f32),
            pltpu.VMEM((D, HQ), f32),
            pltpu.VMEM((3, NP, D), f32),
            pltpu.VMEM((NQ, D), bf16),
            pltpu.VMEM((NQ, D), bf16),
            pltpu.VMEM((D, NP), bf16),
            pltpu.VMEM((D, NP), bf16),
            pltpu.VMEM((2 * HEADS, NP), f32),
            pltpu.VMEM((2 * HEADS, NP), f32),
            pltpu.VMEM((D, NP), bf16),
            pltpu.VMEM((D, NP), bf16),
            pltpu.VMEM((32, D), f32),
            *sum_buffers,
            pltpu.SemaphoreType.DMA((9,)),
            pltpu.SemaphoreType.DMA((chunks,)),
            pltpu.SemaphoreType.DMA((6,)),
            *[pltpu.SemaphoreType.DMA((copies,))] * 6,
        ],
        compiler_params=pltpu.CompilerParams(
            collective_id=0, has_side_effects=True, vmem_limit_bytes=127 * 512 * 1024
        ),
        cost_estimate=pl.CostEstimate(
            flops=2 * 8 * tokens * HQ * D, bytes_accessed=20 << 20, transcendentals=tokens * HQ
        ),
        name="decoder_layer",
    )(
        queries,
        memory,
        quarter_turns,
        token_order,
        lengths,
        attn_in,
        attn_out,
        attn_bias.transpose(1, 0, 2),
        ffn_in,
        ffn_in_bias,
        ffn_out,
        ffn_out_bias,
        norm_gain,
        norm_bias,
        query_pos,
        out_grad,
        jnp.asarray(position_table()),
    )
    outs = pl.pallas_call(
        finish_kernel,
        out_shape=[
            jax.ShapeDtypeStruct((1, NQ, D), bf16),
            jax.ShapeDtypeStruct((1, NQ, D), bf16),
            jax.ShapeDtypeStruct((1, tokens, D), bf16),
            jax.ShapeDtypeStruct((2, 3, D, D), f32),
            jax.ShapeDtypeStruct((2, D, D), f32),
            jax.ShapeDtypeStruct((3, 2, D), f32),
            jax.ShapeDtypeStruct((D, FF), f32),
            jax.ShapeDtypeStruct((1, FF), f32),
            jax.ShapeDtypeStruct((FF, D), f32),
            jax.ShapeDtypeStruct((1, D), f32),
            jax.ShapeDtypeStruct((3, D), f32),
            jax.ShapeDtypeStruct((3, D), f32),
            jax.ShapeDtypeStruct((NQ, D), f32),
        ],
        in_specs=[anywhere] * 6,
        out_specs=[anywhere] * 13,
        scratch_shapes=[
            pltpu.VMEM((tokens, D), bf16),
            *(pltpu.VMEM(shape, bf16) for shape in whole_shapes),
            pltpu.VMEM((NQ, D), bf16),
            pltpu.VMEM((NQ, D), bf16),
            pltpu.VMEM((2, 3, D, D), f32),
            pltpu.VMEM((2, D, D), f32),
            pltpu.VMEM((3, 2, D), f32),
            pltpu.VMEM((D, FF), f32),
            pltpu.VMEM((1, FF), f32),
            pltpu.VMEM((FF, D), f32),
            pltpu.VMEM((1, D), f32),
            pltpu.VMEM((3, D), f32),
            pltpu.VMEM((3, D), f32),
            pltpu.VMEM((NQ, D), f32),
            pltpu.SemaphoreType.DMA((8,)),
            pltpu.SemaphoreType.DMA((8,)),
            pltpu.SemaphoreType.DMA((5,)),
            pltpu.SemaphoreType.DMA((14,)),
        ],
        compiler_params=pltpu.CompilerParams(vmem_limit_bytes=62 * 1024 * 1024),
        name="write_outputs",
    )(*parts)
    return (
        *outs[:5],
        outs[5].transpose(1, 0, 2),
        outs[6],
        outs[7].reshape(FF),
        outs[8],
        outs[9].reshape(D),
        *outs[10:],
    )


def solution(mesh):
    in_specs = (
        P("dp", None, None),
        P("dp", "blk", None),
        P("dp"),
        P("dp", "blk"),
        P("dp"),
        P(),
        P(),
        P(),
        P(),
        P(),
        P(),
        P(),
        P(),
        P(),
        P(),
        P("dp", None, None),
    )
    out_specs = (
        P("dp", None, None),
        P("dp", None, None),
        P("dp", "blk", None),
        P(),
        P(),
        P(),
        P(),
        P(),
        P(),
        P(),
        P(),
        P(),
        P(),
    )
    layer = functools.partial(body, mesh.shape["dp"])
    return jax.shard_map(layer, mesh=mesh, in_specs=in_specs, out_specs=out_specs, check_vma=False)
```

```python
import functools
import math

import jax
import jax.numpy as jnp
import numpy as np
from jax import lax
from jax.experimental import pallas as pl
from jax.experimental.pallas import tpu as pltpu
from jax.sharding import PartitionSpec as P

D = 256
HEADS = 8
HD = D // HEADS
SIDE = 128
NQ = 125
NP = 128
HQ = HEADS * NP
PAIR = 2 * NP
FF = 2048
CHUNK = 1024

masked_score = -1e30
norm_eps = 1e-05
scale = 1.0 / math.sqrt(HD)
log2e = math.log2(math.e)

bf16 = jnp.bfloat16
f32 = jnp.float32

ROWS_F = FF
ROW_POS = 2 * D
ROW_SMALL = 2 * D + NP
ROWS_T = 3 * D
ROWS_K = 3 * D
TILE = 16


def axes_of(pages):
    axes = {"core": (2, 1), "y": (2, 2)}
    stride = 4
    while stride < pages:
        radix = 4 if pages // stride % 4 == 0 else 2
        axes["z%d" % (len(axes) - 2)] = (radix, stride)
        stride *= radix
    axes["x"] = (2, 0)
    return axes


def far_axes(pages):
    return [(name,) for name in axes_of(pages) if name.startswith("z")]


def sum_groups(pages):
    far = far_axes(pages)
    return [("core",), ("y",), *far], [("core", "y"), *far], [("core",), ("x",), ("y",), *far]


def padded(rows, pages):
    unit = TILE * pages
    return (rows + unit - 1) // unit * unit


def position_table():
    half = D // 2
    channel = np.arange(half)
    inverse = np.exp((channel // 2).astype(np.float32) * np.float32(-2.0 * math.log(10000.0) / half))
    angle = (np.arange(SIDE, dtype=np.float32) + 1.0) * np.float32(2.0 * math.pi / SIDE)
    angle = angle[:, None] * inverse
    return np.where(channel % 2 == 0, np.sin(angle), np.cos(angle)).astype(np.float32)


def dot(a, b):
    return jnp.dot(a, b, preferred_element_type=f32)


def dot_nt(a, b):
    return lax.dot_general(a, b, (((1,), (1,)), ((), ())), preferred_element_type=f32)


def dot_tn(a, b):
    return lax.dot_general(a, b, (((0,), (0,)), ((), ())), preferred_element_type=f32)


def row_total(values):
    return jnp.sum(values.astype(f32), axis=0, keepdims=True)


def norm_forward(values):
    average = jnp.mean(values, axis=-1, keepdims=True)
    centred = values - average
    variance = jnp.mean(centred * centred, axis=-1, keepdims=True)
    rstd = lax.rsqrt(variance + norm_eps)
    return centred * rstd, rstd


def norm_backward(grad, normed, rstd, gain):
    grad_normed = grad * gain
    first = jnp.mean(grad_normed, axis=-1, keepdims=True)
    second = jnp.mean(grad_normed * normed, axis=-1, keepdims=True)
    grad_in = rstd * (grad_normed - first - normed * second)
    return grad_in, row_total(grad * normed), row_total(grad)


def spread_rows(rows):
    head = lax.broadcasted_iota(jnp.int32, (NP, D), 1) // HD
    return jnp.concatenate(
        [jnp.where(head == h, rows, 0.0) for h in range(HEADS)], axis=0
    ).astype(bf16)


def spread_cols(cols):
    head = lax.broadcasted_iota(jnp.int32, (D, NP), 0) // HD
    return jnp.concatenate(
        [jnp.where(head == h, cols, 0.0) for h in range(HEADS)], axis=1
    ).astype(bf16)


def project_heads(weight_t, sums):
    high = sums.astype(bf16)
    low = (sums - high.astype(f32)).astype(bf16)
    return own_blocks(
        [
            dot(weight_t[pair_rows(p)], high[:, pair_cols(p)])
            + dot(weight_t[pair_rows(p)], low[:, pair_cols(p)])
            for p in range(4)
        ]
    )


def own_blocks(pairs):
    parts = []
    for pair in pairs:
        parts += [pair[:HD, :NP], pair[HD:, NP:]]
    return jnp.concatenate(parts, axis=0)


def head_rows(row):
    return jnp.concatenate([row[:, NP * h : NP * h + NP] for h in range(HEADS)], axis=0)


def head_line(rows):
    return jnp.concatenate([rows[h : h + 1] for h in range(HEADS)], axis=1)


def per_channel(rows):
    return jnp.concatenate(
        [jnp.broadcast_to(rows[h : h + 1], (HD, NP)) for h in range(HEADS)], axis=0
    )


def head_sums(cols):
    return jnp.concatenate(
        [jnp.sum(cols[HD * h : HD * h + HD], axis=0, keepdims=True) for h in range(HEADS)], axis=0
    )


def pair_cols(p):
    return slice(PAIR * p, PAIR * p + PAIR)


def pair_rows(p):
    return slice(2 * HD * p, 2 * HD * p + 2 * HD)


class Place:
    def __init__(self, pages):
        self.axes = axes_of(pages)
        self.page = lax.axis_index("dp")
        self.member = lax.axis_index("blk")
        self.digit = {
            name: self.member if name == "x" else lax.rem(self.page // stride, radix)
            for name, (radix, stride) in self.axes.items()
        }

    def size(self, group):
        return math.prod(self.axes[name][0] for name in group)

    def index(self, group):
        index = 0
        for name in group:
            index = index * self.axes[name][0] + self.digit[name]
        return index

    def peer(self, group, hop):
        index = lax.rem(self.index(group) + hop, self.size(group))
        page, member, rest = self.page, self.member, index
        for name in reversed(group):
            radix, stride = self.axes[name]
            digit = lax.rem(rest, radix)
            rest = rest // radix
            if name == "x":
                member = digit
            else:
                page = page + (digit - self.digit[name]) * stride
        return (page, member), index


class PageSum:
    def __init__(self, place, groups, back, rows, landing, whole, sent, arrived):
        self.place, self.groups, self.back = place, groups, back
        self.rows, self.landing, self.whole = rows, landing, whole
        self.sent, self.arrived = sent, arrived
        self.slots = 0
        self.extents = [rows.shape[0]]
        self.bases = [0]
        self.landings = []
        at = 0
        for group in groups:
            size = place.size(group)
            extent = self.extents[-1] // size
            self.landings.append(at)
            at += (size - 1) * extent
            self.bases.append(pl.multiple_of(self.bases[-1] + place.index(group) * extent, TILE))
            self.extents.append(extent)
        last = len(groups)
        moves = [self.scatter_moves(s) for s in range(last)]
        near = {"all": 0, "across": 1, "sides": 2}[back]
        moves += [self.gather_moves(s) for s in range(last - 1, near - 1, -1)]
        if back == "sides":
            moves += [self.side_moves(), self.corner_moves(), self.core_moves()]
        elif back == "across":
            moves += [self.across_moves(), self.core_moves()]
        self.phases = [functools.partial(self.step, moves, k) for k in range(len(moves) + 1)]

    @staticmethod
    def landing_rows(pages, groups, rows):
        axes = axes_of(pages)
        total, extent = 0, rows
        for group in groups:
            size = math.prod(axes[name][0] for name in group)
            extent //= size
            total += (size - 1) * extent
        return total

    def step(self, moves, k):
        last = len(self.groups)
        if k > 0:
            for move in moves[k - 1]:
                self.copy(*move).wait()
        if 0 < k <= last:
            total = self.scatter_sum(k - 1)
            region = pl.ds(self.bases[k], self.extents[k])
            if k < last:
                self.rows[region] = total
            elif len(self.whole.shape) == 3:
                self.whole[self.place.member, region] = total
            else:
                self.whole[region] = total
        if k < len(moves):
            for move in moves[k]:
                self.copy(*move).start()

    def copy(self, slot, source, target, device):
        return pltpu.make_async_remote_copy(
            src_ref=source(),
            dst_ref=target(),
            send_sem=self.sent.at[slot],
            recv_sem=self.arrived.at[slot],
            device_id=device,
            device_id_type=pl.DeviceIdType.MESH,
        )

    def new_slot(self):
        self.slots += 1
        return self.slots - 1

    def same(self, device, view):
        return (self.new_slot(), view, view, device)

    def scatter_moves(self, step):
        group = self.groups[step]
        extent = self.extents[step + 1]
        moves = []
        for hop in range(1, self.place.size(group)):
            device, other = self.place.peer(group, hop)
            start = pl.multiple_of(self.bases[step] + other * extent, TILE)
            landing = self.landings[step] + (hop - 1) * extent
            moves.append(
                (
                    self.new_slot(),
                    functools.partial(self.part, self.rows, start, extent),
                    functools.partial(self.part, self.landing, landing, extent),
                    device,
                )
            )
        return moves

    @staticmethod
    def part(ref, start, extent):
        return ref.at[pl.ds(start, extent)]

    def half(self, member, start, extent):
        if len(self.whole.shape) == 3:
            return self.whole.at[member, pl.ds(start, extent)]
        return self.whole.at[pl.ds(start, extent)]

    def scatter_sum(self, step):
        extent = self.extents[step + 1]
        total = self.rows[pl.ds(self.bases[step + 1], extent)].astype(f32)
        for hop in range(1, self.place.size(self.groups[step])):
            landing = self.landings[step] + (hop - 1) * extent
            total = total + self.landing[pl.ds(landing, extent)].astype(f32)
        return total.astype(bf16)

    def gather_moves(self, step):
        group = self.groups[step]
        view = functools.partial(self.half, self.place.member, self.bases[step + 1], self.extents[step + 1])
        return [
            self.same(self.place.peer(group, hop)[0], view) for hop in range(1, self.place.size(group))
        ]

    def own_quarter(self):
        step = 2 if len(self.groups[0]) == 1 else 1
        return self.bases[step], self.extents[step]

    def side_moves(self):
        view = functools.partial(self.half, self.place.member, *self.own_quarter())
        return [self.same(self.place.peer((name,), 1)[0], view) for name in ("y", "x")]

    def corner_moves(self):
        base, extent = self.own_quarter()
        other = pl.multiple_of(base + (1 - 2 * self.place.digit["y"]) * extent, TILE)
        view = functools.partial(self.half, self.place.member, other, extent)
        return [self.same(self.place.peer(("x",), 1)[0], view)]

    def across_moves(self):
        view = functools.partial(self.half, self.place.member, *self.own_quarter())
        return [self.same(self.place.peer(("x", "y"), hop)[0], view) for hop in range(1, 4)]

    def core_moves(self):
        extent = self.extents[0] // 2
        start = pl.multiple_of(self.place.digit["core"] * extent, TILE)
        device, _ = self.place.peer(("core",), 1)
        return [self.same(device, functools.partial(self.half, m, start, extent)) for m in range(2)]


def clear_rest(ref, used):
    if ref.shape[0] > used:
        ref[used:] = jnp.zeros((ref.shape[0] - used, D), ref.dtype)


def layer_kernel(
    tokens,
    pages,
    queries_in,
    memory_hbm,
    turns_in,
    order_in,
    lengths_in,
    attn_in,
    attn_out,
    attn_bias,
    ffn_in_hbm,
    ffn_in_bias,
    ffn_out_hbm,
    ffn_out_bias,
    norm_gain,
    norm_bias,
    pos_in,
    out_grad_in,
    table_in,
    result_hbm,
    queries_grad_hbm,
    memory_grad_hbm,
    whole_f_hbm,
    whole_t_hbm,
    whole_k_hbm,
    memory_s,
    key_in_s,
    probs_s,
    grad_scores_s,
    code_s,
    query_kt,
    grad_vt,
    back_s,
    table_s,
    top_s,
    highest_s,
    shifts_s,
    factor_s,
    total_s,
    mixed_s,
    pad_s,
    result_out,
    queries_grad_out,
    send_a,
    recv_a,
    send_t,
    recv_t,
    send_b,
    recv_b,
    small_s,
    rows_f,
    landing_f,
    whole_f,
    rows_t,
    landing_t,
    whole_t,
    rows_k,
    landing_k,
    whole_k,
    load_sem,
    store_sem,
    link_sem,
    sent_f,
    arrived_f,
    sent_t,
    arrived_t,
    sent_k,
    arrived_k,
):
    member = lax.axis_index("blk")
    partner = (lax.axis_index("dp"), 1 - member)
    chunks = tokens // CHUNK

    place = Place(pages)
    groups_f, groups_t, groups_k = sum_groups(pages)
    sum_f = PageSum(place, groups_f, "sides", rows_f, landing_f, whole_f, sent_f, arrived_f)
    sum_t = PageSum(place, groups_t, "across", rows_t, landing_t, whole_t, sent_t, arrived_t)
    sum_k = PageSum(place, groups_k, "all", rows_k, landing_k, whole_k, sent_k, arrived_k)

    barrier = pltpu.get_barrier_semaphore()
    peers = [
        place.peer(group, hop)[0]
        for group in [("x", "core", "y"), *far_axes(pages)]
        for hop in range(1, place.size(group))
    ]
    for peer in peers:
        pl.semaphore_signal(barrier, inc=1, device_id=peer, device_id_type=pl.DeviceIdType.MESH)

    parts = [slice(0, 4 * CHUNK), slice(4 * CHUNK, tokens)]
    load_memory = [
        pltpu.make_async_copy(memory_hbm.at[0, part], memory_s.at[part], load_sem.at[k])
        for part, k in zip(parts, (0, 9))
    ]
    half = FF // 2
    ffn_in_s = [grad_scores_s.at[D * k : D * k + D] for k in range(2)]
    ffn_out_s = grad_scores_s.at[2 * D : 2 * D + FF, :D]
    free = 2 * D + FF
    active_s = [grad_scores_s.at[free + NP * k : free + NP * k + NP] for k in range(2)]
    slope_s = [grad_scores_s.at[free + NP * k : free + NP * k + NP] for k in range(2, 4)]
    load_ffn = [
        pltpu.make_async_copy(ffn_in_hbm.at[:, half * k : half * k + half], ffn_in_s[k], load_sem.at[1 + k])
        for k in range(2)
    ]
    load_ffn.append(pltpu.make_async_copy(ffn_out_hbm, ffn_out_s, load_sem.at[3]))
    for load in load_memory + load_ffn:
        load.start()

    pairs = [attn_bias[j].astype(f32) for j in range(3)]
    bias = jnp.concatenate([pair[k : k + 1] for k in range(2) for pair in pairs], axis=0)
    gain = norm_gain[...].astype(f32)
    shift = norm_bias[...].astype(f32)

    order = order_in[...]
    turn = turns_in[0]
    row_at = order >> 7
    col_at = order & 127
    top = SIDE - 1
    row_new = jnp.where(
        turn == 0, row_at, jnp.where(turn == 1, col_at, jnp.where(turn == 2, top - row_at, top - col_at))
    )
    col_new = jnp.where(
        turn == 0, col_at, jnp.where(turn == 1, top - row_at, jnp.where(turn == 2, top - col_at, row_at))
    )
    past = jnp.where(order < lengths_in[0], 0, SIDE * SIDE)
    code_s[...] = (row_new * SIDE + col_new + past).astype(f32)

    pad_s[...] = jnp.zeros_like(pad_s)
    pad_s[0, :NQ] = queries_in[0].astype(f32)
    pad_s[1, :NQ] = pos_in[...].astype(f32)
    pad_s[2, :NQ] = out_grad_in[0].astype(f32)
    queries_f = pad_s[0]
    pos_f = pad_s[1]
    queries_b = queries_f.astype(bf16)
    mixed_q = (queries_f + pos_f).astype(bf16)
    query_self = (dot(mixed_q, attn_in[0, 0]) + bias[0:1]).astype(bf16)
    key_self = dot(mixed_q, attn_in[0, 1]).astype(bf16)
    value_self = (dot(queries_b, attn_in[0, 2]) + bias[1:2]).astype(bf16)
    scores = dot(key_self, spread_cols(query_self.astype(f32).T)) * scale
    own_key = lax.broadcasted_iota(jnp.int32, (NP, HQ), 0) < NQ
    scores = jnp.where(own_key, scores, masked_score)
    raised = jnp.exp(scores - jnp.max(scores, axis=0, keepdims=True))
    probs_self = raised / jnp.sum(raised, axis=0, keepdims=True)
    probs_self_b = probs_self.astype(bf16)
    value_t = value_self.astype(f32).T.astype(bf16)
    table = table_in[...]
    nothing = jnp.zeros((SIDE, D // 2), f32)
    table = jnp.concatenate(
        [jnp.concatenate([table, nothing], axis=1), jnp.concatenate([nothing, table], axis=1)], axis=0
    )
    table_high = table.astype(bf16)
    table_s[: 2 * SIDE] = table_high
    table_s[2 * SIDE :] = (table - table_high.astype(f32)).astype(bf16)

    def mask_view(i):
        side, place = i // (chunks // 2), lax.rem(i, chunks // 2)
        return grad_scores_s.at[
            pl.ds(pl.multiple_of(tokens // 2 + place * CHUNK, CHUNK), CHUNK),
            pl.ds(pl.multiple_of(side * NP, NP), NP),
        ]

    lane = lax.broadcasted_iota(jnp.int32, (CHUNK, NP), 1)

    def place_chunk(i):
        rows = pl.ds(pl.multiple_of(i * CHUNK, CHUNK), CHUNK)
        line = code_s[:, rows]
        code = jnp.concatenate(
            [
                jnp.broadcast_to(line[:, NP * j : NP * j + NP], (NP, NP)).T
                for j in range(CHUNK // NP)
            ],
            axis=0,
        ).astype(jnp.int32)
        row_hot = jnp.where(((code >> 7) & 127) == lane, 1.0, 0.0).astype(bf16)
        col_hot = jnp.where((code & 127) == lane, 1.0, 0.0).astype(bf16)
        hot = jnp.concatenate([row_hot, col_hot, row_hot, col_hot], axis=1)
        masked = jnp.where(code < SIDE * SIDE, 0.0, masked_score)
        mask_view(i)[...] = masked.astype(bf16)
        key_in_s[rows] = (memory_s[rows].astype(f32) + dot(hot, table_s[...])).astype(bf16)

    load_memory[0].wait()
    attended = own_blocks(
        [dot(value_t[pair_rows(p)], probs_self_b[:, pair_cols(p)]) for p in range(4)]
    ).T.astype(bf16)
    place_chunk(0)
    first_normed, first_rstd = norm_forward(queries_f + dot(attended, attn_out[0]) + bias[2:3])
    place_chunk(1)
    first = first_normed * gain[0:1] + shift[0:1]
    cross_q = (first + pos_f).astype(bf16)
    query_c = (dot(cross_q, attn_in[1, 0]) + bias[3:4]).astype(bf16)
    place_chunk(2)
    query_k = dot(attn_in[1, 1], spread_cols(query_c.astype(f32).T))
    query_kt[...] = (query_k * (scale * log2e)).astype(bf16)
    place_chunk(3)
    back_s[:HQ] = (dot_nt(spread_rows(query_c.astype(f32)), attn_in[1, 1]) * scale).astype(bf16)
    load_memory[1].wait()
    pl.loop(4, chunks)(place_chunk)

    def score_pair(p, key_in, mask, score_s):
        cols = pair_cols(p)
        part = dot(key_in, query_kt[:, cols]) + mask
        score_s[:, cols] = part
        top_s[:, cols] = jnp.max(part.reshape(CHUNK // 8, 8, PAIR), axis=0)

    def score_operands(i):
        rows = pl.ds(pl.multiple_of(i * CHUNK, CHUNK), CHUNK)
        mask = mask_view(i)[...].astype(f32)
        return key_in_s[rows], jnp.concatenate([mask, mask], axis=1)

    def attend_all(score_s):
        operands = score_operands(0)
        for p in range(4):
            score_pair(p, *operands, score_s)

        @pl.loop(0, chunks)
        def _(i):
            rows = pl.ds(pl.multiple_of(i * CHUNK, CHUNK), CHUNK)
            memory_ct = memory_s[rows].T
            operands = score_operands(jnp.minimum(i + 1, chunks - 1))
            for p in range(4):
                cols = pair_cols(p)
                before = highest_s[0:1, cols]
                highest = jnp.maximum(before, jnp.max(top_s[:, cols], axis=0, keepdims=True))
                highest_s[0:1, cols] = highest
                shifts_s[pl.ds(i, 1), cols] = highest
                fade = jnp.exp2(before - highest)
                raised = jnp.exp2(score_s[:, cols] - highest)
                sums = jnp.sum(raised.reshape(CHUNK // 8, 8, PAIR), axis=0)
                total_s[:, cols] = total_s[:, cols] * fade + sums
                probs_s[rows, cols] = raised.astype(bf16)
                mixed_s[:, cols] = mixed_s[:, cols] * fade + dot(memory_ct, probs_s[rows, cols])
                score_pair(p, *operands, score_s)

    highest_s[0:1] = jnp.full((1, HQ), -3e38, f32)
    total_s[...] = jnp.zeros_like(total_s)
    mixed_s[...] = jnp.zeros_like(mixed_s)
    pl.run_scoped(attend_all, pltpu.VMEM((CHUNK, HQ), f32))
    highest_own = highest_s[0:1]
    total_own = jnp.sum(total_s[...], axis=0, keepdims=True)

    value_wt = attn_in[1, 2].astype(f32).T.astype(bf16)
    key_wt = attn_in[1, 1].astype(f32).T.astype(bf16)
    send_a[...] = project_heads(value_wt, mixed_s[...]).astype(bf16)
    send_t[:HEADS] = head_rows(highest_own)
    send_t[HEADS:] = head_rows(total_own)
    pl.semaphore_wait(barrier, len(peers))
    swap_a = pltpu.make_async_remote_copy(
        src_ref=send_a,
        dst_ref=recv_a,
        send_sem=link_sem.at[0],
        recv_sem=link_sem.at[1],
        device_id=partner,
        device_id_type=pl.DeviceIdType.MESH,
    )
    swap_t = pltpu.make_async_remote_copy(
        src_ref=send_t,
        dst_ref=recv_t,
        send_sem=link_sem.at[4],
        recv_sem=link_sem.at[5],
        device_id=partner,
        device_id_type=pl.DeviceIdType.MESH,
    )
    swap_a.start()
    swap_t.start()
    swap_a.wait()
    swap_t.wait()
    is_first = member == 0
    own, other = send_a[...].astype(f32), recv_a[...].astype(f32)
    left = jnp.where(is_first, own, other)
    right = jnp.where(is_first, other, own)
    own, other = send_t[...], recv_t[...]
    left_t = jnp.where(is_first, own, other)
    right_t = jnp.where(is_first, other, own)
    highest = jnp.maximum(left_t[:HEADS], right_t[:HEADS])
    fade_l = jnp.exp2(left_t[:HEADS] - highest)
    fade_r = jnp.exp2(right_t[:HEADS] - highest)
    total = left_t[HEADS:] * fade_l + right_t[HEADS:] * fade_r
    mixed_t = left * per_channel(fade_l / total) + right * per_channel(fade_r / total)
    log_total = head_line(highest + jnp.log2(total))
    own_share = jnp.exp2(highest_own - log_total)
    factor_s[...] = jnp.exp2(shifts_s[...] - log_total)
    attended_c = (mixed_t.T + bias[4:5]).astype(bf16)

    second_normed, second_rstd = norm_forward(first + dot(attended_c, attn_out[1]) + bias[5:6])
    second = second_normed * gain[1:2] + shift[1:2]
    ffn_input = second.astype(bf16)
    load_ffn[0].wait()
    load_ffn[1].wait()
    blocks = [(j // 4, slice(D * j, D * j + D), slice(j % 4 * D, j % 4 * D + D)) for j in range(FF // D)]
    hidden_bias = ffn_in_bias[...].astype(f32).reshape(1, FF)
    def feed_forward(gate_s):
        for k, cols, part in blocks:
            hidden = dot(ffn_input, ffn_in_s[k][:, part]) + hidden_bias[:, cols]
            half_gate = 0.5 + 0.5 * lax.erf(hidden * math.sqrt(0.5))
            active_s[k][:, part] = (hidden * half_gate).astype(bf16)
            gate_s[:, cols] = half_gate + hidden * jnp.exp(hidden * hidden * -0.5) * (
                1.0 / math.sqrt(2.0 * math.pi)
            )
        load_ffn[2].wait()
        third_normed, third_rstd = norm_forward(
            second
            + dot(active_s[0][...], ffn_out_s[:half])
            + dot(active_s[1][...], ffn_out_s[half:])
            + ffn_out_bias[...].astype(f32).reshape(1, D)
        )
        result_out[...] = (third_normed * gain[2:3] + shift[2:3])[:NQ].astype(bf16)
        grad_third, gain_grad_2, shift_grad_2 = norm_backward(
            pad_s[2], third_normed, third_rstd, gain[2:3]
        )
        grad_branch_f = grad_third.astype(bf16)
        for k, cols, part in blocks:
            grad_hidden = dot_nt(grad_branch_f, ffn_out_s[cols]) * gate_s[:, cols]
            slope_s[k][:, part] = grad_hidden.astype(bf16)
        return grad_third, gain_grad_2, shift_grad_2, grad_branch_f

    grad_third, gain_grad_2, shift_grad_2, grad_branch_f = pl.run_scoped(
        feed_forward, pltpu.VMEM((NP, FF), f32)
    )
    grad_second = grad_third + dot_nt(slope_s[0][...], ffn_in_s[0][...])
    grad_second += dot_nt(slope_s[1][...], ffn_in_s[1][...])
    grad_second_in, gain_grad_1, shift_grad_1 = norm_backward(
        grad_second, second_normed, second_rstd, gain[1:2]
    )
    grad_branch_c = grad_second_in.astype(bf16)
    ffn_input_t = second.T.astype(bf16)

    @pl.when(member == 0)
    def _():
        for k, cols, part in blocks:
            rows_f[cols] = dot(ffn_input_t, slope_s[k][:, part]).astype(bf16)

    @pl.when(member == 1)
    def _():
        for k, cols, part in blocks:
            rows_f[cols] = dot_tn(active_s[k][:, part], grad_branch_f).astype(bf16)

    is_first = member == 0
    out_grad_c = dot_tn(attended_c, grad_branch_c)
    rows_k[2 * D : 3 * D] = jnp.where(is_first, out_grad_c, 0.0).astype(bf16)

    clear_rest(rows_f, ROWS_F)
    clear_rest(rows_t, ROWS_T)
    clear_rest(rows_k, ROWS_K)
    sum_f.phases[0]()
    grad_attended_c = dot_nt(grad_branch_c, attn_out[1]).astype(bf16).astype(f32)
    small_s[:16] = jnp.concatenate(
        [row_total(slope_s[k][:, part]) for k, _, part in blocks]
        + [
            row_total(grad_branch_f),
            row_total(grad_branch_c),
            gain_grad_2,
            shift_grad_2,
            gain_grad_1,
            shift_grad_1,
            row_total(grad_attended_c),
            jnp.zeros((1, D), f32),
        ],
        axis=0,
    )

    store_result = pltpu.make_async_copy(result_out, result_hbm, load_sem.at[7])
    store_result.start()

    grad_attended_t = grad_attended_c.T
    grad_x = spread_rows(grad_attended_c)
    grad_v = dot(attn_in[1, 2], spread_cols(grad_attended_t))
    grad_vt[...] = grad_v.astype(bf16)
    back_s[HQ:] = grad_v.T.astype(bf16)
    inner = head_line(head_sums(grad_attended_t * mixed_t))
    rows_k[D : 2 * D] = dot((mixed_s[...] * own_share).astype(bf16), grad_x).astype(bf16)
    mixed_s[...] = jnp.zeros_like(mixed_s)

    queue_f = sum_f.phases[1:]
    queue_t = list(sum_t.phases)
    queue_k = list(sum_k.phases)

    def take(queue):
        if queue:
            queue.pop(0)()

    def at(i, steps):
        for step, queue in steps:
            pl.when(i == (step * chunks) // 16)(queue.pop(0))

    @pl.loop(0, chunks)
    def _(i):
        rows = pl.ds(pl.multiple_of(i * CHUNK, CHUNK), CHUNK)
        key_ct = key_in_s[rows].T
        memory_c = memory_s[rows]
        for p in range(4):
            cols = pair_cols(p)
            grad_probs = dot(memory_c, grad_vt[:, cols])
            probs = probs_s[rows, cols].astype(f32) * factor_s[pl.ds(i, 1), cols]
            probs_s[rows, cols] = probs.astype(bf16)
            grad_scores_s[rows, cols] = (probs * (grad_probs - inner[:, cols])).astype(bf16)
        mixed_s[...] += dot(key_ct, grad_scores_s[rows])
        at(i, [(3, queue_f), (9, queue_f), (15, queue_f)])

    send_b[...] = (project_heads(key_wt, mixed_s[...]) * scale).astype(bf16)
    swap_b = pltpu.make_async_remote_copy(
        src_ref=send_b,
        dst_ref=recv_b,
        send_sem=link_sem.at[2],
        recv_sem=link_sem.at[3],
        device_id=partner,
        device_id_type=pl.DeviceIdType.MESH,
    )
    swap_b.start()
    query_x = spread_rows(query_c.astype(f32))
    rows_k[:D] = (dot(mixed_s[...].astype(bf16), query_x) * scale).astype(bf16)
    take(queue_k)
    swap_b.wait()
    take(queue_f)
    take(queue_k)
    grad_query_c = (send_b[...].astype(f32) + recv_b[...].astype(f32)).T.astype(bf16)

    cross_pos_grad = dot_nt(grad_query_c, attn_in[1, 0])
    grad_first_in, gain_grad_0, shift_grad_0 = norm_backward(
        grad_second_in + cross_pos_grad, first_normed, first_rstd, gain[0:1]
    )
    grad_branch = grad_first_in.astype(bf16)
    grad_attended = dot_nt(grad_branch, attn_out[0]).astype(bf16).astype(f32)
    take(queue_k)
    grad_probs = dot(value_self, spread_cols(grad_attended.T))
    inner_self = jnp.sum(probs_self * grad_probs, axis=0, keepdims=True)
    grad_scores = (probs_self * (grad_probs - inner_self)).astype(bf16)
    key_t = key_self.astype(f32).T.astype(bf16)
    grad_query_s = (
        own_blocks([dot(key_t[pair_rows(p)], grad_scores[:, pair_cols(p)]) for p in range(4)]) * scale
    ).T.astype(bf16)
    take(queue_f)
    grad_key_s = (dot(grad_scores, spread_rows(query_self.astype(f32))) * scale).astype(bf16)
    grad_value_s = dot(probs_self_b, spread_rows(grad_attended)).astype(bf16)
    grad_mixed_q = dot_nt(grad_query_s, attn_in[0, 0]) + dot_nt(grad_key_s, attn_in[0, 1])
    queries_grad_out[...] = (grad_first_in + grad_mixed_q + dot_nt(grad_value_s, attn_in[0, 2]))[
        :NQ
    ].astype(bf16)
    store_queries = pltpu.make_async_copy(queries_grad_out, queries_grad_hbm, load_sem.at[8])
    store_queries.start()
    small_s[16:] = jnp.concatenate(
        [
            row_total(grad_query_s),
            row_total(grad_value_s),
            row_total(grad_branch),
            row_total(grad_query_c),
            gain_grad_0,
            shift_grad_0,
            jnp.zeros((10, D), f32),
        ],
        axis=0,
    )
    @pl.when(member == 0)
    def _():
        rows_t[:D] = dot_tn(mixed_q, grad_query_s).astype(bf16)
        rows_t[D : 2 * D] = dot_tn(mixed_q, grad_key_s).astype(bf16)
        rows_t[2 * D : 3 * D] = dot_tn(queries_b, grad_value_s).astype(bf16)

    @pl.when(member == 1)
    def _():
        rows_t[:D] = dot_tn(cross_q, grad_query_c).astype(bf16)
        rows_t[D : 2 * D] = dot_tn(attended, grad_branch).astype(bf16)
        rows_t[ROW_POS:ROW_SMALL] = (grad_mixed_q + cross_pos_grad).astype(bf16)
        rows_t[ROW_SMALL : ROW_SMALL + 32] = small_s[...].astype(bf16)
        rows_t[ROW_SMALL + 32 : ROWS_T] = jnp.zeros((ROWS_T - ROW_SMALL - 32, D), bf16)

    take(queue_t)
    take(queue_k)

    @pl.loop(0, chunks)
    def _(i):
        rows = pl.ds(pl.multiple_of(i * CHUNK, CHUNK), CHUNK)
        both = jnp.concatenate([grad_scores_s[rows], probs_s[rows]], axis=1)
        memory_s[rows] = dot(both, back_s[...]).astype(bf16)
        pltpu.make_async_copy(memory_s.at[rows], memory_grad_hbm.at[0, rows], store_sem.at[i]).start()
        at(
            i,
            [
                (1, queue_f),
                (3, queue_t),
                (4, queue_k),
                (7, queue_t),
                (8, queue_k),
                (11, queue_t),
                (12, queue_k),
                (15, queue_t),
            ],
        )

    while queue_f:
        take(queue_f)
    stores = [
        pltpu.make_async_copy(whole, target, load_sem.at[4 + k])
        for k, (whole, target) in enumerate(
            (
                (whole_f, whole_f_hbm),
                (whole_t, whole_t_hbm),
                (whole_k, whole_k_hbm),
            )
        )
    ]
    stores[0].start()
    while queue_t or queue_k:
        take(queue_t)
        take(queue_k)
    for store in stores[1:]:
        store.start()

    @pl.loop(0, chunks)
    def _(i):
        rows = pl.ds(pl.multiple_of(i * CHUNK, CHUNK), CHUNK)
        pltpu.make_async_copy(memory_s.at[rows], memory_grad_hbm.at[0, rows], store_sem.at[i]).wait()

    for store in [*stores, store_result, store_queries]:
        store.wait()


def finish_kernel(
    result_in,
    queries_grad_in,
    memory_grad_in,
    whole_f_hbm,
    whole_t_hbm,
    whole_k_hbm,
    result_hbm,
    queries_grad_hbm,
    memory_grad,
    attn_in_hbm,
    attn_out_hbm,
    attn_bias_hbm,
    ffn_in_hbm,
    ffn_in_bias_hbm,
    ffn_out_hbm,
    ffn_out_bias_hbm,
    norm_gain_hbm,
    norm_bias_hbm,
    query_pos_hbm,
    moved,
    whole_f,
    whole_t,
    whole_k,
    result,
    queries_grad,
    attn_in_grad,
    attn_out_grad,
    attn_bias_grad,
    ffn_in_grad,
    ffn_in_bias_grad,
    ffn_out_grad,
    ffn_out_bias_grad,
    norm_gain_grad,
    norm_bias_grad,
    query_pos_grad,
    in_sem,
    out_sem,
    sum_sem,
    grad_sem,
):
    pieces = in_sem.shape[0]
    piece = moved.shape[0] // pieces

    def fetch(j):
        rows = pl.ds(piece * j, piece)
        return pltpu.make_async_copy(memory_grad_in.at[0, rows], moved.at[rows], in_sem.at[j])

    def write(j):
        rows = pl.ds(piece * j, piece)
        return pltpu.make_async_copy(moved.at[rows], memory_grad.at[0, rows], out_sem.at[j])

    sums = [
        (whole_t_hbm, whole_t),
        (whole_k_hbm, whole_k),
        (whole_f_hbm, whole_f),
        (result_in, result),
        (queries_grad_in, queries_grad),
    ]
    loads = [pltpu.make_async_copy(*pair, sum_sem.at[j]) for j, pair in enumerate(sums)]
    for load in loads:
        load.start()
    for j in range(pieces):
        fetch(j).start()
    blocks = FF // D
    stores = []

    def store(source, target):
        stores.append(pltpu.make_async_copy(source, target, grad_sem.at[len(stores)]))
        stores[-1].start()

    loads[0].wait()
    loads[1].wait()
    for j in range(3):
        attn_in_grad[0, j] = whole_t[0, D * j : D * j + D].astype(f32)
    attn_in_grad[1, 0] = whole_t[1, :D].astype(f32)
    attn_in_grad[1, 1] = whole_k[:D].astype(f32)
    attn_in_grad[1, 2] = whole_k[D : 2 * D].astype(f32)
    store(attn_in_grad, attn_in_hbm)
    attn_out_grad[0] = whole_t[1, D : 2 * D].astype(f32)
    attn_out_grad[1] = whole_k[2 * D : 3 * D].astype(f32)
    store(attn_out_grad, attn_out_hbm)
    loads[2].wait()
    for k in range(2):
        half = slice(FF // 2 * k, FF // 2 * (k + 1))
        ffn_out_grad[half] = whole_f[1, half].astype(f32)
        store(ffn_out_grad.at[half], ffn_out_hbm.at[half])
    for k in range(2):
        half = slice(FF // 2 * k, FF // 2 * (k + 1))
        for j in range(blocks // 2 * k, blocks // 2 * (k + 1)):
            at = slice(D * j, D * j + D)
            ffn_in_grad[:, at] = whole_f[0, at].astype(f32)
        store(ffn_in_grad.at[:, half], ffn_in_hbm.at[:, half])
    for j in range(pieces):
        fetch(j).wait()
        write(j).start()
    loads[3].wait()
    store(result, result_hbm.at[0])
    loads[4].wait()
    store(queries_grad, queries_grad_hbm.at[0])
    query_pos_grad[...] = whole_t[1, ROW_POS:ROW_SMALL].astype(f32)[:NQ]
    store(query_pos_grad, query_pos_hbm)
    small = whole_t[1, ROW_SMALL : ROW_SMALL + 32].astype(f32)
    ffn_in_bias_grad[...] = jnp.concatenate([small[j : j + 1] for j in range(blocks)], axis=1)
    store(ffn_in_bias_grad, ffn_in_bias_hbm)
    ffn_out_bias_grad[...] = small[8:9]
    store(ffn_out_bias_grad, ffn_out_bias_hbm)
    for j, (own, cross) in enumerate(((16, 19), (17, 14), (18, 9))):
        attn_bias_grad[j, 0:1] = small[own : own + 1]
        attn_bias_grad[j, 1:2] = small[cross : cross + 1]
    store(attn_bias_grad, attn_bias_hbm)
    for j, (gain, shift) in enumerate(((20, 21), (12, 13), (10, 11))):
        norm_gain_grad[j : j + 1] = small[gain : gain + 1]
        norm_bias_grad[j : j + 1] = small[shift : shift + 1]
    store(norm_gain_grad, norm_gain_hbm)
    store(norm_bias_grad, norm_bias_hbm)
    for j in range(pieces):
        write(j).wait()
    for copy in stores:
        copy.wait()


def body(
    pages,
    queries,
    memory,
    quarter_turns,
    token_order,
    lengths,
    attn_in,
    attn_out,
    attn_bias,
    ffn_in,
    ffn_in_bias,
    ffn_out,
    ffn_out_bias,
    norm_gain,
    norm_bias,
    query_pos,
    out_grad,
):
    tokens = memory.shape[1]
    chunks = tokens // CHUNK
    groups_f, groups_t, groups_k = sum_groups(pages)
    summed = [
        (padded(ROWS_F, pages), groups_f),
        (padded(ROWS_T, pages), groups_t),
        (padded(ROWS_K, 2 * pages), groups_k),
    ]
    whole_shapes = [(2, rows, D) for rows, _ in summed[:2]] + [(summed[2][0], D)]
    sum_buffers = []
    for (rows, groups), shape in zip(summed, whole_shapes):
        landing = PageSum.landing_rows(pages, groups, rows)
        sum_buffers += [pltpu.VMEM(each, bf16) for each in ((rows, D), (landing, D), shape)]
    copies = 32
    vmem = pl.BlockSpec(memory_space=pltpu.VMEM)
    smem = pl.BlockSpec(memory_space=pltpu.SMEM)
    anywhere = pl.BlockSpec(memory_space=pl.ANY)
    parts = pl.pallas_call(
        functools.partial(layer_kernel, tokens, pages),
        out_shape=[
            jax.ShapeDtypeStruct((NQ, D), bf16),
            jax.ShapeDtypeStruct((NQ, D), bf16),
            jax.ShapeDtypeStruct((1, tokens, D), bf16),
            *(jax.ShapeDtypeStruct(shape, bf16) for shape in whole_shapes),
        ],
        in_specs=[
            vmem,
            anywhere,
            smem,
            vmem,
            smem,
            vmem,
            vmem,
            vmem,
            anywhere,
            vmem,
            anywhere,
            vmem,
            vmem,
            vmem,
            vmem,
            vmem,
            vmem,
        ],
        out_specs=[anywhere] * 6,
        scratch_shapes=[
            pltpu.VMEM((tokens, D), bf16),
            pltpu.VMEM((tokens, D), bf16),
            pltpu.VMEM((tokens, HQ), bf16),
            pltpu.VMEM((tokens, HQ), bf16),
            pltpu.VMEM((1, tokens), f32),
            pltpu.VMEM((D, HQ), bf16),
            pltpu.VMEM((D, HQ), bf16),
            pltpu.VMEM((2 * HQ, D), bf16),
            pltpu.VMEM((4 * SIDE, D), bf16),
            pltpu.VMEM((8, HQ), f32),
            pltpu.VMEM((8, HQ), f32),
            pltpu.VMEM((chunks, HQ), f32),
            pltpu.VMEM((chunks, HQ), f32),
            pltpu.VMEM((8, HQ), f32),
            pltpu.VMEM((D, HQ), f32),
            pltpu.VMEM((3, NP, D), f32),
            pltpu.VMEM((NQ, D), bf16),
            pltpu.VMEM((NQ, D), bf16),
            pltpu.VMEM((D, NP), bf16),
            pltpu.VMEM((D, NP), bf16),
            pltpu.VMEM((2 * HEADS, NP), f32),
            pltpu.VMEM((2 * HEADS, NP), f32),
            pltpu.VMEM((D, NP), bf16),
            pltpu.VMEM((D, NP), bf16),
            pltpu.VMEM((32, D), f32),
            *sum_buffers,
            pltpu.SemaphoreType.DMA((10,)),
            pltpu.SemaphoreType.DMA((chunks,)),
            pltpu.SemaphoreType.DMA((6,)),
            *[pltpu.SemaphoreType.DMA((copies,))] * 6,
        ],
        compiler_params=pltpu.CompilerParams(
            collective_id=0, has_side_effects=True, vmem_limit_bytes=127 * 512 * 1024
        ),
        cost_estimate=pl.CostEstimate(
            flops=2 * 8 * tokens * HQ * D, bytes_accessed=20 << 20, transcendentals=tokens * HQ
        ),
        name="decoder_layer",
    )(
        queries,
        memory,
        quarter_turns,
        token_order,
        lengths,
        attn_in,
        attn_out,
        attn_bias.transpose(1, 0, 2),
        ffn_in,
        ffn_in_bias,
        ffn_out,
        ffn_out_bias,
        norm_gain,
        norm_bias,
        query_pos,
        out_grad,
        jnp.asarray(position_table()),
    )
    outs = pl.pallas_call(
        finish_kernel,
        out_shape=[
            jax.ShapeDtypeStruct((1, NQ, D), bf16),
            jax.ShapeDtypeStruct((1, NQ, D), bf16),
            jax.ShapeDtypeStruct((1, tokens, D), bf16),
            jax.ShapeDtypeStruct((2, 3, D, D), f32),
            jax.ShapeDtypeStruct((2, D, D), f32),
            jax.ShapeDtypeStruct((3, 2, D), f32),
            jax.ShapeDtypeStruct((D, FF), f32),
            jax.ShapeDtypeStruct((1, FF), f32),
            jax.ShapeDtypeStruct((FF, D), f32),
            jax.ShapeDtypeStruct((1, D), f32),
            jax.ShapeDtypeStruct((3, D), f32),
            jax.ShapeDtypeStruct((3, D), f32),
            jax.ShapeDtypeStruct((NQ, D), f32),
        ],
        in_specs=[anywhere] * 6,
        out_specs=[anywhere] * 13,
        scratch_shapes=[
            pltpu.VMEM((tokens, D), bf16),
            *(pltpu.VMEM(shape, bf16) for shape in whole_shapes),
            pltpu.VMEM((NQ, D), bf16),
            pltpu.VMEM((NQ, D), bf16),
            pltpu.VMEM((2, 3, D, D), f32),
            pltpu.VMEM((2, D, D), f32),
            pltpu.VMEM((3, 2, D), f32),
            pltpu.VMEM((D, FF), f32),
            pltpu.VMEM((1, FF), f32),
            pltpu.VMEM((FF, D), f32),
            pltpu.VMEM((1, D), f32),
            pltpu.VMEM((3, D), f32),
            pltpu.VMEM((3, D), f32),
            pltpu.VMEM((NQ, D), f32),
            pltpu.SemaphoreType.DMA((8,)),
            pltpu.SemaphoreType.DMA((8,)),
            pltpu.SemaphoreType.DMA((5,)),
            pltpu.SemaphoreType.DMA((14,)),
        ],
        compiler_params=pltpu.CompilerParams(vmem_limit_bytes=62 * 1024 * 1024),
        name="write_outputs",
    )(*parts)
    return (
        *outs[:5],
        outs[5].transpose(1, 0, 2),
        outs[6],
        outs[7].reshape(FF),
        outs[8],
        outs[9].reshape(D),
        *outs[10:],
    )


def solution(mesh):
    in_specs = (
        P("dp", None, None),
        P("dp", "blk", None),
        P("dp"),
        P("dp", "blk"),
        P("dp"),
        P(),
        P(),
        P(),
        P(),
        P(),
        P(),
        P(),
        P(),
        P(),
        P(),
        P("dp", None, None),
    )
    out_specs = (
        P("dp", None, None),
        P("dp", None, None),
        P("dp", "blk", None),
        P(),
        P(),
        P(),
        P(),
        P(),
        P(),
        P(),
        P(),
        P(),
        P(),
    )
    layer = functools.partial(body, mesh.shape["dp"])
    return jax.shard_map(layer, mesh=mesh, in_specs=in_specs, out_specs=out_specs, check_vma=False)
```

```python
import functools
import math

import jax
import jax.numpy as jnp
import numpy as np
from jax import lax
from jax.experimental import pallas as pl
from jax.experimental.pallas import tpu as pltpu
from jax.sharding import PartitionSpec as P

D = 256
HEADS = 8
HD = D // HEADS
SIDE = 128
NQ = 125
NP = 128
HQ = HEADS * NP
PAIR = 2 * NP
FF = 2048
CHUNK = 1024

masked_score = -1e30
norm_eps = 1e-05
scale = 1.0 / math.sqrt(HD)
log2e = math.log2(math.e)

bf16 = jnp.bfloat16
f32 = jnp.float32

ROWS_F = FF
ROW_POS = 2 * D
ROW_SMALL = 2 * D + NP
ROWS_T = 3 * D
ROWS_K = 3 * D
TILE = 16


def axes_of(pages):
    axes = {"core": (2, 1), "y": (2, 2)}
    stride = 4
    while stride < pages:
        radix = 4 if pages // stride % 4 == 0 else 2
        axes["z%d" % (len(axes) - 2)] = (radix, stride)
        stride *= radix
    axes["x"] = (2, 0)
    return axes


def far_axes(pages):
    return [(name,) for name in axes_of(pages) if name.startswith("z")]


def sum_groups(pages):
    far = far_axes(pages)
    return [("core",), ("y",), *far], [("core", "y"), *far], [("core",), ("x",), ("y",), *far]


def padded(rows, pages):
    unit = TILE * pages
    return (rows + unit - 1) // unit * unit


def position_table():
    half = D // 2
    channel = np.arange(half)
    inverse = np.exp((channel // 2).astype(np.float32) * np.float32(-2.0 * math.log(10000.0) / half))
    angle = (np.arange(SIDE, dtype=np.float32) + 1.0) * np.float32(2.0 * math.pi / SIDE)
    angle = angle[:, None] * inverse
    return np.where(channel % 2 == 0, np.sin(angle), np.cos(angle)).astype(np.float32)


def dot(a, b):
    return jnp.dot(a, b, preferred_element_type=f32)


def dot_nt(a, b):
    return lax.dot_general(a, b, (((1,), (1,)), ((), ())), preferred_element_type=f32)


def dot_tn(a, b):
    return lax.dot_general(a, b, (((0,), (0,)), ((), ())), preferred_element_type=f32)


def row_total(values):
    return jnp.sum(values.astype(f32), axis=0, keepdims=True)


def norm_forward(values):
    average = jnp.mean(values, axis=-1, keepdims=True)
    centred = values - average
    variance = jnp.mean(centred * centred, axis=-1, keepdims=True)
    rstd = lax.rsqrt(variance + norm_eps)
    return centred * rstd, rstd


def norm_backward(grad, normed, rstd, gain):
    grad_normed = grad * gain
    first = jnp.mean(grad_normed, axis=-1, keepdims=True)
    second = jnp.mean(grad_normed * normed, axis=-1, keepdims=True)
    grad_in = rstd * (grad_normed - first - normed * second)
    return grad_in, row_total(grad * normed), row_total(grad)


def spread_rows(rows):
    head = lax.broadcasted_iota(jnp.int32, (NP, D), 1) // HD
    return jnp.concatenate(
        [jnp.where(head == h, rows, 0.0) for h in range(HEADS)], axis=0
    ).astype(bf16)


def spread_cols(cols):
    head = lax.broadcasted_iota(jnp.int32, (D, NP), 0) // HD
    return jnp.concatenate(
        [jnp.where(head == h, cols, 0.0) for h in range(HEADS)], axis=1
    ).astype(bf16)


def project_heads(weight_t, sums):
    high = sums.astype(bf16)
    low = (sums - high.astype(f32)).astype(bf16)
    return own_blocks(
        [
            dot(weight_t[pair_rows(p)], high[:, pair_cols(p)])
            + dot(weight_t[pair_rows(p)], low[:, pair_cols(p)])
            for p in range(4)
        ]
    )


def own_blocks(pairs):
    parts = []
    for pair in pairs:
        parts += [pair[:HD, :NP], pair[HD:, NP:]]
    return jnp.concatenate(parts, axis=0)


def head_rows(row):
    return jnp.concatenate([row[:, NP * h : NP * h + NP] for h in range(HEADS)], axis=0)


def head_line(rows):
    return jnp.concatenate([rows[h : h + 1] for h in range(HEADS)], axis=1)


def per_channel(rows):
    return jnp.concatenate(
        [jnp.broadcast_to(rows[h : h + 1], (HD, NP)) for h in range(HEADS)], axis=0
    )


def head_sums(cols):
    return jnp.concatenate(
        [jnp.sum(cols[HD * h : HD * h + HD], axis=0, keepdims=True) for h in range(HEADS)], axis=0
    )


def pair_cols(p):
    return slice(PAIR * p, PAIR * p + PAIR)


def pair_rows(p):
    return slice(2 * HD * p, 2 * HD * p + 2 * HD)


class Place:
    def __init__(self, pages):
        self.axes = axes_of(pages)
        self.page = lax.axis_index("dp")
        self.member = lax.axis_index("blk")
        self.digit = {
            name: self.member if name == "x" else lax.rem(self.page // stride, radix)
            for name, (radix, stride) in self.axes.items()
        }

    def size(self, group):
        return math.prod(self.axes[name][0] for name in group)

    def index(self, group):
        index = 0
        for name in group:
            index = index * self.axes[name][0] + self.digit[name]
        return index

    def peer(self, group, hop):
        index = lax.rem(self.index(group) + hop, self.size(group))
        page, member, rest = self.page, self.member, index
        for name in reversed(group):
            radix, stride = self.axes[name]
            digit = lax.rem(rest, radix)
            rest = rest // radix
            if name == "x":
                member = digit
            else:
                page = page + (digit - self.digit[name]) * stride
        return (page, member), index


class PageSum:
    def __init__(self, place, groups, back, rows, landing, whole, sent, arrived):
        self.place, self.groups, self.back = place, groups, back
        self.rows, self.landing, self.whole = rows, landing, whole
        self.sent, self.arrived = sent, arrived
        self.slots = 0
        self.extents = [rows.shape[0]]
        self.bases = [0]
        self.landings = []
        at = 0
        for group in groups:
            size = place.size(group)
            extent = self.extents[-1] // size
            self.landings.append(at)
            at += (size - 1) * extent
            self.bases.append(pl.multiple_of(self.bases[-1] + place.index(group) * extent, TILE))
            self.extents.append(extent)
        last = len(groups)
        moves = [self.scatter_moves(s) for s in range(last)]
        near = {"all": 0, "across": 1, "sides": 2}[back]
        moves += [self.gather_moves(s) for s in range(last - 1, near - 1, -1)]
        if back == "sides":
            moves += [self.side_moves(), self.corner_moves(), self.core_moves()]
        elif back == "across":
            moves += [self.across_moves(), self.core_moves()]
        self.phases = [functools.partial(self.step, moves, k) for k in range(len(moves) + 1)]

    @staticmethod
    def landing_rows(pages, groups, rows):
        axes = axes_of(pages)
        total, extent = 0, rows
        for group in groups:
            size = math.prod(axes[name][0] for name in group)
            extent //= size
            total += (size - 1) * extent
        return total

    def step(self, moves, k):
        last = len(self.groups)
        if k > 0:
            for move in moves[k - 1]:
                self.copy(*move).wait()
        if 0 < k <= last:
            total = self.scatter_sum(k - 1)
            region = pl.ds(self.bases[k], self.extents[k])
            if k < last:
                self.rows[region] = total
            elif len(self.whole.shape) == 3:
                self.whole[self.place.member, region] = total
            else:
                self.whole[region] = total
        if k < len(moves):
            for move in moves[k]:
                self.copy(*move).start()

    def copy(self, slot, source, target, device):
        return pltpu.make_async_remote_copy(
            src_ref=source(),
            dst_ref=target(),
            send_sem=self.sent.at[slot],
            recv_sem=self.arrived.at[slot],
            device_id=device,
            device_id_type=pl.DeviceIdType.MESH,
        )

    def new_slot(self):
        self.slots += 1
        return self.slots - 1

    def same(self, device, view):
        return (self.new_slot(), view, view, device)

    def scatter_moves(self, step):
        group = self.groups[step]
        extent = self.extents[step + 1]
        moves = []
        for hop in range(1, self.place.size(group)):
            device, other = self.place.peer(group, hop)
            start = pl.multiple_of(self.bases[step] + other * extent, TILE)
            landing = self.landings[step] + (hop - 1) * extent
            moves.append(
                (
                    self.new_slot(),
                    functools.partial(self.part, self.rows, start, extent),
                    functools.partial(self.part, self.landing, landing, extent),
                    device,
                )
            )
        return moves

    @staticmethod
    def part(ref, start, extent):
        return ref.at[pl.ds(start, extent)]

    def half(self, member, start, extent):
        if len(self.whole.shape) == 3:
            return self.whole.at[member, pl.ds(start, extent)]
        return self.whole.at[pl.ds(start, extent)]

    def scatter_sum(self, step):
        extent = self.extents[step + 1]
        total = self.rows[pl.ds(self.bases[step + 1], extent)].astype(f32)
        for hop in range(1, self.place.size(self.groups[step])):
            landing = self.landings[step] + (hop - 1) * extent
            total = total + self.landing[pl.ds(landing, extent)].astype(f32)
        return total.astype(bf16)

    def gather_moves(self, step):
        group = self.groups[step]
        view = functools.partial(self.half, self.place.member, self.bases[step + 1], self.extents[step + 1])
        return [
            self.same(self.place.peer(group, hop)[0], view) for hop in range(1, self.place.size(group))
        ]

    def own_quarter(self):
        step = 2 if len(self.groups[0]) == 1 else 1
        return self.bases[step], self.extents[step]

    def side_moves(self):
        view = functools.partial(self.half, self.place.member, *self.own_quarter())
        return [self.same(self.place.peer((name,), 1)[0], view) for name in ("y", "x")]

    def corner_moves(self):
        base, extent = self.own_quarter()
        other = pl.multiple_of(base + (1 - 2 * self.place.digit["y"]) * extent, TILE)
        view = functools.partial(self.half, self.place.member, other, extent)
        return [self.same(self.place.peer(("x",), 1)[0], view)]

    def across_moves(self):
        view = functools.partial(self.half, self.place.member, *self.own_quarter())
        return [self.same(self.place.peer(("x", "y"), hop)[0], view) for hop in range(1, 4)]

    def core_moves(self):
        extent = self.extents[0] // 2
        start = pl.multiple_of(self.place.digit["core"] * extent, TILE)
        device, _ = self.place.peer(("core",), 1)
        return [self.same(device, functools.partial(self.half, m, start, extent)) for m in range(2)]


def clear_rest(ref, used):
    if ref.shape[0] > used:
        ref[used:] = jnp.zeros((ref.shape[0] - used, D), ref.dtype)


def layer_kernel(
    tokens,
    pages,
    queries_in,
    memory_hbm,
    turns_in,
    order_in,
    lengths_in,
    attn_in,
    attn_out,
    attn_bias,
    ffn_in_hbm,
    ffn_in_bias,
    ffn_out_hbm,
    ffn_out_bias,
    norm_gain,
    norm_bias,
    pos_in,
    out_grad_in,
    table_in,
    result_hbm,
    queries_grad_hbm,
    memory_grad_hbm,
    whole_f_hbm,
    whole_t_hbm,
    whole_k_hbm,
    memory_s,
    key_in_s,
    probs_s,
    grad_scores_s,
    code_s,
    query_kt,
    grad_vt,
    back_s,
    table_s,
    top_s,
    highest_s,
    shifts_s,
    factor_s,
    total_s,
    mixed_s,
    pad_s,
    result_out,
    queries_grad_out,
    send_a,
    recv_a,
    send_t,
    recv_t,
    send_b,
    recv_b,
    small_s,
    rows_f,
    landing_f,
    whole_f,
    rows_t,
    landing_t,
    whole_t,
    rows_k,
    landing_k,
    whole_k,
    load_sem,
    store_sem,
    link_sem,
    sent_f,
    arrived_f,
    sent_t,
    arrived_t,
    sent_k,
    arrived_k,
):
    member = lax.axis_index("blk")
    partner = (lax.axis_index("dp"), 1 - member)
    chunks = tokens // CHUNK

    place = Place(pages)
    groups_f, groups_t, groups_k = sum_groups(pages)
    sum_f = PageSum(place, groups_f, "sides", rows_f, landing_f, whole_f, sent_f, arrived_f)
    sum_t = PageSum(place, groups_t, "across", rows_t, landing_t, whole_t, sent_t, arrived_t)
    sum_k = PageSum(place, groups_k, "all", rows_k, landing_k, whole_k, sent_k, arrived_k)

    barrier = pltpu.get_barrier_semaphore()
    peers = [
        place.peer(group, hop)[0]
        for group in [("x", "core", "y"), *far_axes(pages)]
        for hop in range(1, place.size(group))
    ]
    for peer in peers:
        pl.semaphore_signal(barrier, inc=1, device_id=peer, device_id_type=pl.DeviceIdType.MESH)

    load_memory = pltpu.make_async_copy(memory_hbm.at[0], memory_s, load_sem.at[0])
    half = FF // 2
    ffn_in_s = [grad_scores_s.at[D * k : D * k + D] for k in range(2)]
    ffn_out_s = grad_scores_s.at[2 * D : 2 * D + FF, :D]
    free = 2 * D + FF
    active_s = [grad_scores_s.at[free + NP * k : free + NP * k + NP] for k in range(2)]
    slope_s = [grad_scores_s.at[free + NP * k : free + NP * k + NP] for k in range(2, 4)]
    load_ffn = [
        pltpu.make_async_copy(ffn_in_hbm.at[:, half * k : half * k + half], ffn_in_s[k], load_sem.at[1 + k])
        for k in range(2)
    ]
    load_ffn.append(pltpu.make_async_copy(ffn_out_hbm, ffn_out_s, load_sem.at[3]))
    load_memory.start()
    for load in load_ffn:
        load.start()

    pairs = [attn_bias[j].astype(f32) for j in range(3)]
    bias = jnp.concatenate([pair[k : k + 1] for k in range(2) for pair in pairs], axis=0)
    gain = norm_gain[...].astype(f32)
    shift = norm_bias[...].astype(f32)

    order = order_in[...]
    turn = turns_in[0]
    row_at = order >> 7
    col_at = order & 127
    top = SIDE - 1
    row_new = jnp.where(
        turn == 0, row_at, jnp.where(turn == 1, col_at, jnp.where(turn == 2, top - row_at, top - col_at))
    )
    col_new = jnp.where(
        turn == 0, col_at, jnp.where(turn == 1, top - row_at, jnp.where(turn == 2, top - col_at, row_at))
    )
    past = jnp.where(order < lengths_in[0], 0, SIDE * SIDE)
    code_s[...] = (row_new * SIDE + col_new + past).astype(f32)

    pad_s[...] = jnp.zeros_like(pad_s)
    pad_s[0, :NQ] = queries_in[0].astype(f32)
    pad_s[1, :NQ] = pos_in[...].astype(f32)
    pad_s[2, :NQ] = out_grad_in[0].astype(f32)
    queries_f = pad_s[0]
    pos_f = pad_s[1]
    queries_b = queries_f.astype(bf16)
    mixed_q = (queries_f + pos_f).astype(bf16)
    query_self = (dot(mixed_q, attn_in[0, 0]) + bias[0:1]).astype(bf16)
    key_self = dot(mixed_q, attn_in[0, 1]).astype(bf16)
    value_self = (dot(queries_b, attn_in[0, 2]) + bias[1:2]).astype(bf16)
    scores = dot(key_self, spread_cols(query_self.astype(f32).T)) * scale
    own_key = lax.broadcasted_iota(jnp.int32, (NP, HQ), 0) < NQ
    scores = jnp.where(own_key, scores, masked_score)
    raised = jnp.exp(scores - jnp.max(scores, axis=0, keepdims=True))
    probs_self = raised / jnp.sum(raised, axis=0, keepdims=True)
    probs_self_b = probs_self.astype(bf16)
    value_t = value_self.astype(f32).T.astype(bf16)
    attended = own_blocks(
        [dot(value_t[pair_rows(p)], probs_self_b[:, pair_cols(p)]) for p in range(4)]
    ).T.astype(bf16)
    first_normed, first_rstd = norm_forward(queries_f + dot(attended, attn_out[0]) + bias[2:3])
    first = first_normed * gain[0:1] + shift[0:1]
    cross_q = (first + pos_f).astype(bf16)
    query_c = (dot(cross_q, attn_in[1, 0]) + bias[3:4]).astype(bf16)
    query_x = spread_rows(query_c.astype(f32))
    query_k = dot(attn_in[1, 1], spread_cols(query_c.astype(f32).T))
    query_kt[...] = (query_k * (scale * log2e)).astype(bf16)
    back_s[:HQ] = (dot_nt(query_x, attn_in[1, 1]) * scale).astype(bf16)
    table = table_in[...]
    nothing = jnp.zeros((SIDE, D // 2), f32)
    table = jnp.concatenate(
        [jnp.concatenate([table, nothing], axis=1), jnp.concatenate([nothing, table], axis=1)], axis=0
    )
    table_high = table.astype(bf16)
    table_s[: 2 * SIDE] = table_high
    table_s[2 * SIDE :] = (table - table_high.astype(f32)).astype(bf16)

    load_memory.wait()
    def mask_view(i):
        side, place = i // (chunks // 2), lax.rem(i, chunks // 2)
        return grad_scores_s.at[
            pl.ds(pl.multiple_of(tokens // 2 + place * CHUNK, CHUNK), CHUNK),
            pl.ds(pl.multiple_of(side * NP, NP), NP),
        ]

    lane = lax.broadcasted_iota(jnp.int32, (CHUNK, NP), 1)

    @pl.loop(0, chunks)
    def _(i):
        rows = pl.ds(pl.multiple_of(i * CHUNK, CHUNK), CHUNK)
        line = code_s[:, rows]
        code = jnp.concatenate(
            [
                jnp.broadcast_to(line[:, NP * j : NP * j + NP], (NP, NP)).T
                for j in range(CHUNK // NP)
            ],
            axis=0,
        ).astype(jnp.int32)
        row_hot = jnp.where(((code >> 7) & 127) == lane, 1.0, 0.0).astype(bf16)
        col_hot = jnp.where((code & 127) == lane, 1.0, 0.0).astype(bf16)
        hot = jnp.concatenate([row_hot, col_hot, row_hot, col_hot], axis=1)
        masked = jnp.where(code < SIDE * SIDE, 0.0, masked_score)
        mask_view(i)[...] = masked.astype(bf16)
        key_in_s[rows] = (memory_s[rows].astype(f32) + dot(hot, table_s[...])).astype(bf16)

    def score_pair(p, key_in, mask, score_s):
        cols = pl.ds(pl.multiple_of(p * PAIR, PAIR), PAIR)
        part = dot(key_in, query_kt[:, cols]) + mask
        score_s[:, cols] = part
        top_s[:, cols] = jnp.max(part.reshape(CHUNK // 8, 8, PAIR), axis=0)

    def score_operands(i):
        rows = pl.ds(pl.multiple_of(i * CHUNK, CHUNK), CHUNK)
        mask = mask_view(i)[...].astype(f32)
        return key_in_s[rows], jnp.concatenate([mask, mask], axis=1)

    def attend_all(score_s):
        operands = score_operands(0)
        for p in range(4):
            score_pair(p, *operands, score_s)

        @pl.loop(0, chunks)
        def _(i):
            rows = pl.ds(pl.multiple_of(i * CHUNK, CHUNK), CHUNK)
            memory_ct = memory_s[rows].T
            operands = score_operands(jnp.minimum(i + 1, chunks - 1))
            @pl.loop(0, 4)
            def _(p):
                cols = pl.ds(pl.multiple_of(p * PAIR, PAIR), PAIR)
                before = highest_s[0:1, cols]
                highest = jnp.maximum(before, jnp.max(top_s[:, cols], axis=0, keepdims=True))
                highest_s[0:1, cols] = highest
                shifts_s[pl.ds(i, 1), cols] = highest
                fade = jnp.exp2(before - highest)
                raised = jnp.exp2(score_s[:, cols] - highest)
                sums = jnp.sum(raised.reshape(CHUNK // 8, 8, PAIR), axis=0)
                total_s[:, cols] = total_s[:, cols] * fade + sums
                probs_s[rows, cols] = raised.astype(bf16)
                mixed_s[:, cols] = mixed_s[:, cols] * fade + dot(memory_ct, probs_s[rows, cols])
                score_pair(p, *operands, score_s)

    highest_s[0:1] = jnp.full((1, HQ), -3e38, f32)
    total_s[...] = jnp.zeros_like(total_s)
    mixed_s[...] = jnp.zeros_like(mixed_s)
    pl.run_scoped(attend_all, pltpu.VMEM((CHUNK, HQ), f32))
    highest_own = highest_s[0:1]
    total_own = jnp.sum(total_s[...], axis=0, keepdims=True)

    value_wt = attn_in[1, 2].astype(f32).T.astype(bf16)
    key_wt = attn_in[1, 1].astype(f32).T.astype(bf16)
    send_a[...] = project_heads(value_wt, mixed_s[...]).astype(bf16)
    send_t[:HEADS] = head_rows(highest_own)
    send_t[HEADS:] = head_rows(total_own)
    pl.semaphore_wait(barrier, len(peers))
    swap_a = pltpu.make_async_remote_copy(
        src_ref=send_a,
        dst_ref=recv_a,
        send_sem=link_sem.at[0],
        recv_sem=link_sem.at[1],
        device_id=partner,
        device_id_type=pl.DeviceIdType.MESH,
    )
    swap_t = pltpu.make_async_remote_copy(
        src_ref=send_t,
        dst_ref=recv_t,
        send_sem=link_sem.at[4],
        recv_sem=link_sem.at[5],
        device_id=partner,
        device_id_type=pl.DeviceIdType.MESH,
    )
    swap_a.start()
    swap_t.start()
    swap_a.wait()
    swap_t.wait()
    is_first = member == 0
    own, other = send_a[...].astype(f32), recv_a[...].astype(f32)
    left = jnp.where(is_first, own, other)
    right = jnp.where(is_first, other, own)
    own, other = send_t[...], recv_t[...]
    left_t = jnp.where(is_first, own, other)
    right_t = jnp.where(is_first, other, own)
    highest = jnp.maximum(left_t[:HEADS], right_t[:HEADS])
    fade_l = jnp.exp2(left_t[:HEADS] - highest)
    fade_r = jnp.exp2(right_t[:HEADS] - highest)
    total = left_t[HEADS:] * fade_l + right_t[HEADS:] * fade_r
    mixed_t = left * per_channel(fade_l / total) + right * per_channel(fade_r / total)
    log_total = head_line(highest + jnp.log2(total))
    own_share = jnp.exp2(highest_own - log_total)
    factor_s[...] = jnp.exp2(shifts_s[...] - log_total)
    attended_c = (mixed_t.T + bias[4:5]).astype(bf16)

    second_normed, second_rstd = norm_forward(first + dot(attended_c, attn_out[1]) + bias[5:6])
    second = second_normed * gain[1:2] + shift[1:2]
    ffn_input = second.astype(bf16)
    load_ffn[0].wait()
    load_ffn[1].wait()
    blocks = [(j // 4, slice(D * j, D * j + D), slice(j % 4 * D, j % 4 * D + D)) for j in range(FF // D)]
    hidden_bias = ffn_in_bias[...].astype(f32).reshape(1, FF)
    def feed_forward(gate_s):
        for k, cols, part in blocks:
            hidden = dot(ffn_input, ffn_in_s[k][:, part]) + hidden_bias[:, cols]
            half_gate = 0.5 + 0.5 * lax.erf(hidden * math.sqrt(0.5))
            active_s[k][:, part] = (hidden * half_gate).astype(bf16)
            gate_s[:, cols] = half_gate + hidden * jnp.exp(hidden * hidden * -0.5) * (
                1.0 / math.sqrt(2.0 * math.pi)
            )
        load_ffn[2].wait()
        third_normed, third_rstd = norm_forward(
            second
            + dot(active_s[0][...], ffn_out_s[:half])
            + dot(active_s[1][...], ffn_out_s[half:])
            + ffn_out_bias[...].astype(f32).reshape(1, D)
        )
        result_out[...] = (third_normed * gain[2:3] + shift[2:3])[:NQ].astype(bf16)
        grad_third, gain_grad_2, shift_grad_2 = norm_backward(
            pad_s[2], third_normed, third_rstd, gain[2:3]
        )
        grad_branch_f = grad_third.astype(bf16)
        for k, cols, part in blocks:
            grad_hidden = dot_nt(grad_branch_f, ffn_out_s[cols]) * gate_s[:, cols]
            slope_s[k][:, part] = grad_hidden.astype(bf16)
        return grad_third, gain_grad_2, shift_grad_2, grad_branch_f

    grad_third, gain_grad_2, shift_grad_2, grad_branch_f = pl.run_scoped(
        feed_forward, pltpu.VMEM((NP, FF), f32)
    )
    grad_second = grad_third + dot_nt(slope_s[0][...], ffn_in_s[0][...])
    grad_second += dot_nt(slope_s[1][...], ffn_in_s[1][...])
    grad_second_in, gain_grad_1, shift_grad_1 = norm_backward(
        grad_second, second_normed, second_rstd, gain[1:2]
    )
    grad_branch_c = grad_second_in.astype(bf16)
    ffn_input_t = second.T.astype(bf16)

    @pl.when(member == 0)
    def _():
        for k, cols, part in blocks:
            rows_f[cols] = dot(ffn_input_t, slope_s[k][:, part]).astype(bf16)

    @pl.when(member == 1)
    def _():
        for k, cols, part in blocks:
            rows_f[cols] = dot_tn(active_s[k][:, part], grad_branch_f).astype(bf16)

    is_first = member == 0
    out_grad_c = dot_tn(attended_c, grad_branch_c)
    rows_k[2 * D : 3 * D] = jnp.where(is_first, out_grad_c, 0.0).astype(bf16)

    clear_rest(rows_f, ROWS_F)
    clear_rest(rows_t, ROWS_T)
    clear_rest(rows_k, ROWS_K)
    sum_f.phases[0]()
    grad_attended_c = dot_nt(grad_branch_c, attn_out[1]).astype(bf16).astype(f32)
    small_s[:16] = jnp.concatenate(
        [row_total(slope_s[k][:, part]) for k, _, part in blocks]
        + [
            row_total(grad_branch_f),
            row_total(grad_branch_c),
            gain_grad_2,
            shift_grad_2,
            gain_grad_1,
            shift_grad_1,
            row_total(grad_attended_c),
            jnp.zeros((1, D), f32),
        ],
        axis=0,
    )

    store_result = pltpu.make_async_copy(result_out, result_hbm, load_sem.at[7])
    store_result.start()

    grad_attended_t = grad_attended_c.T
    grad_x = spread_rows(grad_attended_c)
    grad_v = dot(attn_in[1, 2], spread_cols(grad_attended_t))
    grad_vt[...] = grad_v.astype(bf16)
    back_s[HQ:] = grad_v.T.astype(bf16)
    inner = head_line(head_sums(grad_attended_t * mixed_t))
    rows_k[D : 2 * D] = dot((mixed_s[...] * own_share).astype(bf16), grad_x).astype(bf16)
    mixed_s[...] = jnp.zeros_like(mixed_s)

    queue_f = sum_f.phases[1:]
    queue_t = list(sum_t.phases)
    queue_k = list(sum_k.phases)

    def take(queue):
        if queue:
            queue.pop(0)()

    def at(i, steps):
        for step, queue in steps:
            pl.when(i == (step * chunks) // 16)(queue.pop(0))

    @pl.loop(0, chunks)
    def _(i):
        rows = pl.ds(pl.multiple_of(i * CHUNK, CHUNK), CHUNK)
        key_ct = key_in_s[rows].T
        memory_c = memory_s[rows]
        for p in range(4):
            cols = pair_cols(p)
            grad_probs = dot(memory_c, grad_vt[:, cols])
            probs = probs_s[rows, cols].astype(f32) * factor_s[pl.ds(i, 1), cols]
            probs_s[rows, cols] = probs.astype(bf16)
            grad_scores_s[rows, cols] = (probs * (grad_probs - inner[:, cols])).astype(bf16)
        mixed_s[...] += dot(key_ct, grad_scores_s[rows])
        at(i, [(3, queue_f), (9, queue_f), (15, queue_f)])

    send_b[...] = (project_heads(key_wt, mixed_s[...]) * scale).astype(bf16)
    swap_b = pltpu.make_async_remote_copy(
        src_ref=send_b,
        dst_ref=recv_b,
        send_sem=link_sem.at[2],
        recv_sem=link_sem.at[3],
        device_id=partner,
        device_id_type=pl.DeviceIdType.MESH,
    )
    swap_b.start()
    query_x = spread_rows(query_c.astype(f32))
    rows_k[:D] = (dot(mixed_s[...].astype(bf16), query_x) * scale).astype(bf16)
    take(queue_k)
    swap_b.wait()
    take(queue_f)
    take(queue_k)
    grad_query_c = (send_b[...].astype(f32) + recv_b[...].astype(f32)).T.astype(bf16)

    cross_pos_grad = dot_nt(grad_query_c, attn_in[1, 0])
    grad_first_in, gain_grad_0, shift_grad_0 = norm_backward(
        grad_second_in + cross_pos_grad, first_normed, first_rstd, gain[0:1]
    )
    grad_branch = grad_first_in.astype(bf16)
    grad_attended = dot_nt(grad_branch, attn_out[0]).astype(bf16).astype(f32)
    take(queue_k)
    grad_probs = dot(value_self, spread_cols(grad_attended.T))
    inner_self = jnp.sum(probs_self * grad_probs, axis=0, keepdims=True)
    grad_scores = (probs_self * (grad_probs - inner_self)).astype(bf16)
    key_t = key_self.astype(f32).T.astype(bf16)
    grad_query_s = (
        own_blocks([dot(key_t[pair_rows(p)], grad_scores[:, pair_cols(p)]) for p in range(4)]) * scale
    ).T.astype(bf16)
    grad_key_s = (dot(grad_scores, spread_rows(query_self.astype(f32))) * scale).astype(bf16)
    grad_value_s = dot(probs_self_b, spread_rows(grad_attended)).astype(bf16)
    grad_mixed_q = dot_nt(grad_query_s, attn_in[0, 0]) + dot_nt(grad_key_s, attn_in[0, 1])
    queries_grad_out[...] = (grad_first_in + grad_mixed_q + dot_nt(grad_value_s, attn_in[0, 2]))[
        :NQ
    ].astype(bf16)
    store_queries = pltpu.make_async_copy(queries_grad_out, queries_grad_hbm, load_sem.at[8])
    store_queries.start()
    small_s[16:] = jnp.concatenate(
        [
            row_total(grad_query_s),
            row_total(grad_value_s),
            row_total(grad_branch),
            row_total(grad_query_c),
            gain_grad_0,
            shift_grad_0,
            jnp.zeros((10, D), f32),
        ],
        axis=0,
    )
    @pl.when(member == 0)
    def _():
        rows_t[:D] = dot_tn(mixed_q, grad_query_s).astype(bf16)
        rows_t[D : 2 * D] = dot_tn(mixed_q, grad_key_s).astype(bf16)
        rows_t[2 * D : 3 * D] = dot_tn(queries_b, grad_value_s).astype(bf16)

    @pl.when(member == 1)
    def _():
        rows_t[:D] = dot_tn(cross_q, grad_query_c).astype(bf16)
        rows_t[D : 2 * D] = dot_tn(attended, grad_branch).astype(bf16)
        rows_t[ROW_POS:ROW_SMALL] = (grad_mixed_q + cross_pos_grad).astype(bf16)
        rows_t[ROW_SMALL : ROW_SMALL + 32] = small_s[...].astype(bf16)
        rows_t[ROW_SMALL + 32 : ROWS_T] = jnp.zeros((ROWS_T - ROW_SMALL - 32, D), bf16)

    take(queue_t)
    take(queue_k)
    take(queue_f)

    @pl.loop(0, chunks)
    def _(i):
        rows = pl.ds(pl.multiple_of(i * CHUNK, CHUNK), CHUNK)
        both = jnp.concatenate([grad_scores_s[rows], probs_s[rows]], axis=1)
        memory_s[rows] = dot(both, back_s[...]).astype(bf16)
        pltpu.make_async_copy(memory_s.at[rows], memory_grad_hbm.at[0, rows], store_sem.at[i]).start()
        at(
            i,
            [
                (3, queue_t),
                (4, queue_k),
                (7, queue_t),
                (8, queue_k),
                (9, queue_f),
                (11, queue_t),
                (12, queue_k),
                (15, queue_t),
            ],
        )

    while queue_f:
        take(queue_f)
    stores = [
        pltpu.make_async_copy(whole, target, load_sem.at[4 + k])
        for k, (whole, target) in enumerate(
            (
                (whole_f, whole_f_hbm),
                (whole_t, whole_t_hbm),
                (whole_k, whole_k_hbm),
            )
        )
    ]
    stores[0].start()
    while queue_t or queue_k:
        take(queue_t)
        take(queue_k)
    for store in stores[1:]:
        store.start()

    @pl.loop(0, chunks)
    def _(i):
        rows = pl.ds(pl.multiple_of(i * CHUNK, CHUNK), CHUNK)
        pltpu.make_async_copy(memory_s.at[rows], memory_grad_hbm.at[0, rows], store_sem.at[i]).wait()

    for store in [*stores, store_result, store_queries]:
        store.wait()


def finish_kernel(
    result_in,
    queries_grad_in,
    memory_grad_in,
    whole_f_hbm,
    whole_t_hbm,
    whole_k_hbm,
    result_hbm,
    queries_grad_hbm,
    memory_grad,
    attn_in_hbm,
    attn_out_hbm,
    attn_bias_hbm,
    ffn_in_hbm,
    ffn_in_bias_hbm,
    ffn_out_hbm,
    ffn_out_bias_hbm,
    norm_gain_hbm,
    norm_bias_hbm,
    query_pos_hbm,
    moved,
    whole_f,
    whole_t,
    whole_k,
    result,
    queries_grad,
    attn_in_grad,
    attn_out_grad,
    attn_bias_grad,
    ffn_in_grad,
    ffn_in_bias_grad,
    ffn_out_grad,
    ffn_out_bias_grad,
    norm_gain_grad,
    norm_bias_grad,
    query_pos_grad,
    in_sem,
    out_sem,
    sum_sem,
    grad_sem,
):
    pieces = in_sem.shape[0]
    piece = moved.shape[0] // pieces

    def fetch(j):
        rows = pl.ds(piece * j, piece)
        return pltpu.make_async_copy(memory_grad_in.at[0, rows], moved.at[rows], in_sem.at[j])

    def write(j):
        rows = pl.ds(piece * j, piece)
        return pltpu.make_async_copy(moved.at[rows], memory_grad.at[0, rows], out_sem.at[j])

    sums = [
        (whole_t_hbm, whole_t),
        (whole_k_hbm, whole_k),
        (whole_f_hbm, whole_f),
        (result_in, result),
        (queries_grad_in, queries_grad),
    ]
    loads = [pltpu.make_async_copy(*pair, sum_sem.at[j]) for j, pair in enumerate(sums)]
    for load in loads:
        load.start()
    for j in range(pieces):
        fetch(j).start()
    blocks = FF // D
    stores = []

    def store(source, target):
        stores.append(pltpu.make_async_copy(source, target, grad_sem.at[len(stores)]))
        stores[-1].start()

    loads[0].wait()
    loads[1].wait()
    for j in range(3):
        attn_in_grad[0, j] = whole_t[0, D * j : D * j + D].astype(f32)
    attn_in_grad[1, 0] = whole_t[1, :D].astype(f32)
    attn_in_grad[1, 1] = whole_k[:D].astype(f32)
    attn_in_grad[1, 2] = whole_k[D : 2 * D].astype(f32)
    store(attn_in_grad, attn_in_hbm)
    attn_out_grad[0] = whole_t[1, D : 2 * D].astype(f32)
    attn_out_grad[1] = whole_k[2 * D : 3 * D].astype(f32)
    store(attn_out_grad, attn_out_hbm)
    loads[2].wait()
    for k in range(2):
        half = slice(FF // 2 * k, FF // 2 * (k + 1))
        ffn_out_grad[half] = whole_f[1, half].astype(f32)
        store(ffn_out_grad.at[half], ffn_out_hbm.at[half])
    for k in range(2):
        half = slice(FF // 2 * k, FF // 2 * (k + 1))
        for j in range(blocks // 2 * k, blocks // 2 * (k + 1)):
            at = slice(D * j, D * j + D)
            ffn_in_grad[:, at] = whole_f[0, at].astype(f32)
        store(ffn_in_grad.at[:, half], ffn_in_hbm.at[:, half])
    for j in range(pieces):
        fetch(j).wait()
        write(j).start()
    loads[3].wait()
    store(result, result_hbm.at[0])
    loads[4].wait()
    store(queries_grad, queries_grad_hbm.at[0])
    query_pos_grad[...] = whole_t[1, ROW_POS:ROW_SMALL].astype(f32)[:NQ]
    store(query_pos_grad, query_pos_hbm)
    small = whole_t[1, ROW_SMALL : ROW_SMALL + 32].astype(f32)
    ffn_in_bias_grad[...] = jnp.concatenate([small[j : j + 1] for j in range(blocks)], axis=1)
    store(ffn_in_bias_grad, ffn_in_bias_hbm)
    ffn_out_bias_grad[...] = small[8:9]
    store(ffn_out_bias_grad, ffn_out_bias_hbm)
    for j, (own, cross) in enumerate(((16, 19), (17, 14), (18, 9))):
        attn_bias_grad[j, 0:1] = small[own : own + 1]
        attn_bias_grad[j, 1:2] = small[cross : cross + 1]
    store(attn_bias_grad, attn_bias_hbm)
    for j, (gain, shift) in enumerate(((20, 21), (12, 13), (10, 11))):
        norm_gain_grad[j : j + 1] = small[gain : gain + 1]
        norm_bias_grad[j : j + 1] = small[shift : shift + 1]
    store(norm_gain_grad, norm_gain_hbm)
    store(norm_bias_grad, norm_bias_hbm)
    for j in range(pieces):
        write(j).wait()
    for copy in stores:
        copy.wait()


def body(
    pages,
    queries,
    memory,
    quarter_turns,
    token_order,
    lengths,
    attn_in,
    attn_out,
    attn_bias,
    ffn_in,
    ffn_in_bias,
    ffn_out,
    ffn_out_bias,
    norm_gain,
    norm_bias,
    query_pos,
    out_grad,
):
    tokens = memory.shape[1]
    chunks = tokens // CHUNK
    groups_f, groups_t, groups_k = sum_groups(pages)
    summed = [
        (padded(ROWS_F, pages), groups_f),
        (padded(ROWS_T, pages), groups_t),
        (padded(ROWS_K, 2 * pages), groups_k),
    ]
    whole_shapes = [(2, rows, D) for rows, _ in summed[:2]] + [(summed[2][0], D)]
    sum_buffers = []
    for (rows, groups), shape in zip(summed, whole_shapes):
        landing = PageSum.landing_rows(pages, groups, rows)
        sum_buffers += [pltpu.VMEM(each, bf16) for each in ((rows, D), (landing, D), shape)]
    copies = 32
    vmem = pl.BlockSpec(memory_space=pltpu.VMEM)
    smem = pl.BlockSpec(memory_space=pltpu.SMEM)
    anywhere = pl.BlockSpec(memory_space=pl.ANY)
    parts = pl.pallas_call(
        functools.partial(layer_kernel, tokens, pages),
        out_shape=[
            jax.ShapeDtypeStruct((NQ, D), bf16),
            jax.ShapeDtypeStruct((NQ, D), bf16),
            jax.ShapeDtypeStruct((1, tokens, D), bf16),
            *(jax.ShapeDtypeStruct(shape, bf16) for shape in whole_shapes),
        ],
        in_specs=[
            vmem,
            anywhere,
            smem,
            vmem,
            smem,
            vmem,
            vmem,
            vmem,
            anywhere,
            vmem,
            anywhere,
            vmem,
            vmem,
            vmem,
            vmem,
            vmem,
            vmem,
        ],
        out_specs=[anywhere] * 6,
        scratch_shapes=[
            pltpu.VMEM((tokens, D), bf16),
            pltpu.VMEM((tokens, D), bf16),
            pltpu.VMEM((tokens, HQ), bf16),
            pltpu.VMEM((tokens, HQ), bf16),
            pltpu.VMEM((1, tokens), f32),
            pltpu.VMEM((D, HQ), bf16),
            pltpu.VMEM((D, HQ), bf16),
            pltpu.VMEM((2 * HQ, D), bf16),
            pltpu.VMEM((4 * SIDE, D), bf16),
            pltpu.VMEM((8, HQ), f32),
            pltpu.VMEM((8, HQ), f32),
            pltpu.VMEM((chunks, HQ), f32),
            pltpu.VMEM((chunks, HQ), f32),
            pltpu.VMEM((8, HQ), f32),
            pltpu.VMEM((D, HQ), f32),
            pltpu.VMEM((3, NP, D), f32),
            pltpu.VMEM((NQ, D), bf16),
            pltpu.VMEM((NQ, D), bf16),
            pltpu.VMEM((D, NP), bf16),
            pltpu.VMEM((D, NP), bf16),
            pltpu.VMEM((2 * HEADS, NP), f32),
            pltpu.VMEM((2 * HEADS, NP), f32),
            pltpu.VMEM((D, NP), bf16),
            pltpu.VMEM((D, NP), bf16),
            pltpu.VMEM((32, D), f32),
            *sum_buffers,
            pltpu.SemaphoreType.DMA((9,)),
            pltpu.SemaphoreType.DMA((chunks,)),
            pltpu.SemaphoreType.DMA((6,)),
            *[pltpu.SemaphoreType.DMA((copies,))] * 6,
        ],
        compiler_params=pltpu.CompilerParams(
            collective_id=0, has_side_effects=True, vmem_limit_bytes=127 * 512 * 1024
        ),
        cost_estimate=pl.CostEstimate(
            flops=2 * 8 * tokens * HQ * D, bytes_accessed=20 << 20, transcendentals=tokens * HQ
        ),
        name="decoder_layer",
    )(
        queries,
        memory,
        quarter_turns,
        token_order,
        lengths,
        attn_in,
        attn_out,
        attn_bias.transpose(1, 0, 2),
        ffn_in,
        ffn_in_bias,
        ffn_out,
        ffn_out_bias,
        norm_gain,
        norm_bias,
        query_pos,
        out_grad,
        jnp.asarray(position_table()),
    )
    outs = pl.pallas_call(
        finish_kernel,
        out_shape=[
            jax.ShapeDtypeStruct((1, NQ, D), bf16),
            jax.ShapeDtypeStruct((1, NQ, D), bf16),
            jax.ShapeDtypeStruct((1, tokens, D), bf16),
            jax.ShapeDtypeStruct((2, 3, D, D), f32),
            jax.ShapeDtypeStruct((2, D, D), f32),
            jax.ShapeDtypeStruct((3, 2, D), f32),
            jax.ShapeDtypeStruct((D, FF), f32),
            jax.ShapeDtypeStruct((1, FF), f32),
            jax.ShapeDtypeStruct((FF, D), f32),
            jax.ShapeDtypeStruct((1, D), f32),
            jax.ShapeDtypeStruct((3, D), f32),
            jax.ShapeDtypeStruct((3, D), f32),
            jax.ShapeDtypeStruct((NQ, D), f32),
        ],
        in_specs=[anywhere] * 6,
        out_specs=[anywhere] * 13,
        scratch_shapes=[
            pltpu.VMEM((tokens, D), bf16),
            *(pltpu.VMEM(shape, bf16) for shape in whole_shapes),
            pltpu.VMEM((NQ, D), bf16),
            pltpu.VMEM((NQ, D), bf16),
            pltpu.VMEM((2, 3, D, D), f32),
            pltpu.VMEM((2, D, D), f32),
            pltpu.VMEM((3, 2, D), f32),
            pltpu.VMEM((D, FF), f32),
            pltpu.VMEM((1, FF), f32),
            pltpu.VMEM((FF, D), f32),
            pltpu.VMEM((1, D), f32),
            pltpu.VMEM((3, D), f32),
            pltpu.VMEM((3, D), f32),
            pltpu.VMEM((NQ, D), f32),
            pltpu.SemaphoreType.DMA((8,)),
            pltpu.SemaphoreType.DMA((8,)),
            pltpu.SemaphoreType.DMA((5,)),
            pltpu.SemaphoreType.DMA((14,)),
        ],
        compiler_params=pltpu.CompilerParams(vmem_limit_bytes=62 * 1024 * 1024),
        name="write_outputs",
    )(*parts)
    return (
        *outs[:5],
        outs[5].transpose(1, 0, 2),
        outs[6],
        outs[7].reshape(FF),
        outs[8],
        outs[9].reshape(D),
        *outs[10:],
    )


def solution(mesh):
    in_specs = (
        P("dp", None, None),
        P("dp", "blk", None),
        P("dp"),
        P("dp", "blk"),
        P("dp"),
        P(),
        P(),
        P(),
        P(),
        P(),
        P(),
        P(),
        P(),
        P(),
        P(),
        P("dp", None, None),
    )
    out_specs = (
        P("dp", None, None),
        P("dp", None, None),
        P("dp", "blk", None),
        P(),
        P(),
        P(),
        P(),
        P(),
        P(),
        P(),
        P(),
        P(),
        P(),
    )
    layer = functools.partial(body, mesh.shape["dp"])
    return jax.shard_map(layer, mesh=mesh, in_specs=in_specs, out_specs=out_specs, check_vma=False)
```

```python
import functools
import math

import jax
import jax.numpy as jnp
import numpy as np
from jax import lax
from jax.experimental import pallas as pl
from jax.experimental.pallas import tpu as pltpu
from jax.sharding import PartitionSpec as P

D = 256
HEADS = 8
HD = D // HEADS
SIDE = 128
NQ = 125
NP = 128
HQ = HEADS * NP
PAIR = 2 * NP
FF = 2048
CHUNK = 1024

masked_score = -1e30
norm_eps = 1e-05
scale = 1.0 / math.sqrt(HD)
log2e = math.log2(math.e)

bf16 = jnp.bfloat16
f32 = jnp.float32

ROWS_F = FF
ROW_POS = 2 * D
ROW_SMALL = 2 * D + NP
ROWS_T = 3 * D
ROWS_K = 3 * D
TILE = 16


def axes_of(pages):
    axes = {"core": (2, 1), "y": (2, 2)}
    stride = 4
    while stride < pages:
        radix = 4 if pages // stride % 4 == 0 else 2
        axes["z%d" % (len(axes) - 2)] = (radix, stride)
        stride *= radix
    axes["x"] = (2, 0)
    return axes


def far_axes(pages):
    return [(name,) for name in axes_of(pages) if name.startswith("z")]


def sum_groups(pages):
    far = far_axes(pages)
    return [("core",), ("y",), *far], [("core", "y"), *far], [("core",), ("x",), ("y",), *far]


def padded(rows, pages):
    unit = TILE * pages
    return (rows + unit - 1) // unit * unit


def position_table():
    half = D // 2
    channel = np.arange(half)
    inverse = np.exp((channel // 2).astype(np.float32) * np.float32(-2.0 * math.log(10000.0) / half))
    angle = (np.arange(SIDE, dtype=np.float32) + 1.0) * np.float32(2.0 * math.pi / SIDE)
    angle = angle[:, None] * inverse
    return np.where(channel % 2 == 0, np.sin(angle), np.cos(angle)).astype(np.float32)


def dot(a, b):
    return jnp.dot(a, b, preferred_element_type=f32)


def dot_nt(a, b):
    return lax.dot_general(a, b, (((1,), (1,)), ((), ())), preferred_element_type=f32)


def dot_tn(a, b):
    return lax.dot_general(a, b, (((0,), (0,)), ((), ())), preferred_element_type=f32)


def row_total(values):
    return jnp.sum(values.astype(f32), axis=0, keepdims=True)


def norm_forward(values):
    average = jnp.mean(values, axis=-1, keepdims=True)
    centred = values - average
    variance = jnp.mean(centred * centred, axis=-1, keepdims=True)
    rstd = lax.rsqrt(variance + norm_eps)
    return centred * rstd, rstd


def norm_backward(grad, normed, rstd, gain):
    grad_normed = grad * gain
    first = jnp.mean(grad_normed, axis=-1, keepdims=True)
    second = jnp.mean(grad_normed * normed, axis=-1, keepdims=True)
    grad_in = rstd * (grad_normed - first - normed * second)
    return grad_in, row_total(grad * normed), row_total(grad)


def spread_rows(rows):
    head = lax.broadcasted_iota(jnp.int32, (NP, D), 1) // HD
    return jnp.concatenate(
        [jnp.where(head == h, rows, 0.0) for h in range(HEADS)], axis=0
    ).astype(bf16)


def spread_cols(cols):
    head = lax.broadcasted_iota(jnp.int32, (D, NP), 0) // HD
    return jnp.concatenate(
        [jnp.where(head == h, cols, 0.0) for h in range(HEADS)], axis=1
    ).astype(bf16)


def project_heads(weight_t, sums):
    high = sums.astype(bf16)
    low = (sums - high.astype(f32)).astype(bf16)
    return own_blocks(
        [
            dot(weight_t[pair_rows(p)], high[:, pair_cols(p)])
            + dot(weight_t[pair_rows(p)], low[:, pair_cols(p)])
            for p in range(4)
        ]
    )


def own_blocks(pairs):
    parts = []
    for pair in pairs:
        parts += [pair[:HD, :NP], pair[HD:, NP:]]
    return jnp.concatenate(parts, axis=0)


def head_rows(row):
    return jnp.concatenate([row[:, NP * h : NP * h + NP] for h in range(HEADS)], axis=0)


def head_line(rows):
    return jnp.concatenate([rows[h : h + 1] for h in range(HEADS)], axis=1)


def per_channel(rows):
    return jnp.concatenate(
        [jnp.broadcast_to(rows[h : h + 1], (HD, NP)) for h in range(HEADS)], axis=0
    )


def head_sums(cols):
    return jnp.concatenate(
        [jnp.sum(cols[HD * h : HD * h + HD], axis=0, keepdims=True) for h in range(HEADS)], axis=0
    )


def pair_cols(p):
    return slice(PAIR * p, PAIR * p + PAIR)


def pair_rows(p):
    return slice(2 * HD * p, 2 * HD * p + 2 * HD)


class Place:
    def __init__(self, pages):
        self.axes = axes_of(pages)
        self.page = lax.axis_index("dp")
        self.member = lax.axis_index("blk")
        self.digit = {
            name: self.member if name == "x" else lax.rem(self.page // stride, radix)
            for name, (radix, stride) in self.axes.items()
        }

    def size(self, group):
        return math.prod(self.axes[name][0] for name in group)

    def index(self, group):
        index = 0
        for name in group:
            index = index * self.axes[name][0] + self.digit[name]
        return index

    def peer(self, group, hop):
        index = lax.rem(self.index(group) + hop, self.size(group))
        page, member, rest = self.page, self.member, index
        for name in reversed(group):
            radix, stride = self.axes[name]
            digit = lax.rem(rest, radix)
            rest = rest // radix
            if name == "x":
                member = digit
            else:
                page = page + (digit - self.digit[name]) * stride
        return (page, member), index


class PageSum:
    def __init__(self, place, groups, back, rows, landing, whole, sent, arrived):
        self.place, self.groups, self.back = place, groups, back
        self.rows, self.landing, self.whole = rows, landing, whole
        self.sent, self.arrived = sent, arrived
        self.slots = 0
        self.extents = [rows.shape[0]]
        self.bases = [0]
        self.landings = []
        at = 0
        for group in groups:
            size = place.size(group)
            extent = self.extents[-1] // size
            self.landings.append(at)
            at += (size - 1) * extent
            self.bases.append(pl.multiple_of(self.bases[-1] + place.index(group) * extent, TILE))
            self.extents.append(extent)
        last = len(groups)
        moves = [self.scatter_moves(s) for s in range(last)]
        near = {"all": 0, "across": 1, "sides": 2}[back]
        moves += [self.gather_moves(s) for s in range(last - 1, near - 1, -1)]
        if back == "sides":
            moves += [self.side_moves(), self.corner_moves(), self.core_moves()]
        elif back == "across":
            moves += [self.across_moves(), self.core_moves()]
        self.phases = [functools.partial(self.step, moves, k) for k in range(len(moves) + 1)]

    @staticmethod
    def landing_rows(pages, groups, rows):
        axes = axes_of(pages)
        total, extent = 0, rows
        for group in groups:
            size = math.prod(axes[name][0] for name in group)
            extent //= size
            total += (size - 1) * extent
        return total

    def step(self, moves, k):
        last = len(self.groups)
        if k > 0:
            for move in moves[k - 1]:
                self.copy(*move).wait()
        if 0 < k <= last:
            total = self.scatter_sum(k - 1)
            region = pl.ds(self.bases[k], self.extents[k])
            if k < last:
                self.rows[region] = total
            elif len(self.whole.shape) == 3:
                self.whole[self.place.member, region] = total
            else:
                self.whole[region] = total
        if k < len(moves):
            for move in moves[k]:
                self.copy(*move).start()

    def copy(self, slot, source, target, device):
        return pltpu.make_async_remote_copy(
            src_ref=source(),
            dst_ref=target(),
            send_sem=self.sent.at[slot],
            recv_sem=self.arrived.at[slot],
            device_id=device,
            device_id_type=pl.DeviceIdType.MESH,
        )

    def new_slot(self):
        self.slots += 1
        return self.slots - 1

    def same(self, device, view):
        return (self.new_slot(), view, view, device)

    def scatter_moves(self, step):
        group = self.groups[step]
        extent = self.extents[step + 1]
        moves = []
        for hop in range(1, self.place.size(group)):
            device, other = self.place.peer(group, hop)
            start = pl.multiple_of(self.bases[step] + other * extent, TILE)
            landing = self.landings[step] + (hop - 1) * extent
            moves.append(
                (
                    self.new_slot(),
                    functools.partial(self.part, self.rows, start, extent),
                    functools.partial(self.part, self.landing, landing, extent),
                    device,
                )
            )
        return moves

    @staticmethod
    def part(ref, start, extent):
        return ref.at[pl.ds(start, extent)]

    def half(self, member, start, extent):
        if len(self.whole.shape) == 3:
            return self.whole.at[member, pl.ds(start, extent)]
        return self.whole.at[pl.ds(start, extent)]

    def scatter_sum(self, step):
        extent = self.extents[step + 1]
        total = self.rows[pl.ds(self.bases[step + 1], extent)].astype(f32)
        for hop in range(1, self.place.size(self.groups[step])):
            landing = self.landings[step] + (hop - 1) * extent
            total = total + self.landing[pl.ds(landing, extent)].astype(f32)
        return total.astype(bf16)

    def gather_moves(self, step):
        group = self.groups[step]
        view = functools.partial(self.half, self.place.member, self.bases[step + 1], self.extents[step + 1])
        return [
            self.same(self.place.peer(group, hop)[0], view) for hop in range(1, self.place.size(group))
        ]

    def own_quarter(self):
        step = 2 if len(self.groups[0]) == 1 else 1
        return self.bases[step], self.extents[step]

    def side_moves(self):
        view = functools.partial(self.half, self.place.member, *self.own_quarter())
        return [self.same(self.place.peer((name,), 1)[0], view) for name in ("y", "x")]

    def corner_moves(self):
        base, extent = self.own_quarter()
        other = pl.multiple_of(base + (1 - 2 * self.place.digit["y"]) * extent, TILE)
        view = functools.partial(self.half, self.place.member, other, extent)
        return [self.same(self.place.peer(("x",), 1)[0], view)]

    def across_moves(self):
        view = functools.partial(self.half, self.place.member, *self.own_quarter())
        return [self.same(self.place.peer(("x", "y"), hop)[0], view) for hop in range(1, 4)]

    def core_moves(self):
        extent = self.extents[0] // 2
        start = pl.multiple_of(self.place.digit["core"] * extent, TILE)
        device, _ = self.place.peer(("core",), 1)
        return [self.same(device, functools.partial(self.half, m, start, extent)) for m in range(2)]


def clear_rest(ref, used):
    if ref.shape[0] > used:
        ref[used:] = jnp.zeros((ref.shape[0] - used, D), ref.dtype)


def layer_kernel(
    tokens,
    pages,
    queries_in,
    memory_hbm,
    turns_in,
    order_in,
    lengths_in,
    attn_in,
    attn_out,
    attn_bias,
    ffn_in_hbm,
    ffn_in_bias,
    ffn_out_hbm,
    ffn_out_bias,
    norm_gain,
    norm_bias,
    pos_in,
    out_grad_in,
    table_in,
    result_hbm,
    queries_grad_hbm,
    memory_grad_hbm,
    whole_f_hbm,
    whole_t_hbm,
    whole_k_hbm,
    memory_s,
    key_in_s,
    probs_s,
    grad_scores_s,
    code_s,
    query_kt,
    grad_vt,
    back_s,
    table_s,
    top_s,
    highest_s,
    shifts_s,
    factor_s,
    total_s,
    mixed_s,
    pad_s,
    result_out,
    queries_grad_out,
    send_a,
    recv_a,
    send_t,
    recv_t,
    send_b,
    recv_b,
    small_s,
    rows_f,
    landing_f,
    whole_f,
    rows_t,
    landing_t,
    whole_t,
    rows_k,
    landing_k,
    whole_k,
    load_sem,
    store_sem,
    link_sem,
    sent_f,
    arrived_f,
    sent_t,
    arrived_t,
    sent_k,
    arrived_k,
):
    member = lax.axis_index("blk")
    partner = (lax.axis_index("dp"), 1 - member)
    chunks = tokens // CHUNK

    place = Place(pages)
    groups_f, groups_t, groups_k = sum_groups(pages)
    sum_f = PageSum(place, groups_f, "sides", rows_f, landing_f, whole_f, sent_f, arrived_f)
    sum_t = PageSum(place, groups_t, "across", rows_t, landing_t, whole_t, sent_t, arrived_t)
    sum_k = PageSum(place, groups_k, "all", rows_k, landing_k, whole_k, sent_k, arrived_k)

    barrier = pltpu.get_barrier_semaphore()
    peers = [
        place.peer(group, hop)[0]
        for group in [("x", "core", "y"), *far_axes(pages)]
        for hop in range(1, place.size(group))
    ]
    for peer in peers:
        pl.semaphore_signal(barrier, inc=1, device_id=peer, device_id_type=pl.DeviceIdType.MESH)

    load_memory = pltpu.make_async_copy(memory_hbm.at[0], memory_s, load_sem.at[0])
    half = FF // 2
    ffn_in_s = [grad_scores_s.at[D * k : D * k + D] for k in range(2)]
    ffn_out_s = grad_scores_s.at[2 * D : 2 * D + FF, :D]
    free = 2 * D + FF
    active_s = [grad_scores_s.at[free + NP * k : free + NP * k + NP] for k in range(2)]
    slope_s = [grad_scores_s.at[free + NP * k : free + NP * k + NP] for k in range(2, 4)]
    load_ffn = [
        pltpu.make_async_copy(ffn_in_hbm.at[:, half * k : half * k + half], ffn_in_s[k], load_sem.at[1 + k])
        for k in range(2)
    ]
    load_ffn.append(pltpu.make_async_copy(ffn_out_hbm, ffn_out_s, load_sem.at[3]))
    load_memory.start()
    for load in load_ffn:
        load.start()

    pairs = [attn_bias[j].astype(f32) for j in range(3)]
    bias = jnp.concatenate([pair[k : k + 1] for k in range(2) for pair in pairs], axis=0)
    gain = norm_gain[...].astype(f32)
    shift = norm_bias[...].astype(f32)

    def each_two(block):
        @pl.loop(0, chunks // 2)
        def _(j):
            block(j * 2)
            block(j * 2 + 1)

    order = order_in[...]
    turn = turns_in[0]
    row_at = order >> 7
    col_at = order & 127
    top = SIDE - 1
    row_new = jnp.where(
        turn == 0, row_at, jnp.where(turn == 1, col_at, jnp.where(turn == 2, top - row_at, top - col_at))
    )
    col_new = jnp.where(
        turn == 0, col_at, jnp.where(turn == 1, top - row_at, jnp.where(turn == 2, top - col_at, row_at))
    )
    past = jnp.where(order < lengths_in[0], 0, SIDE * SIDE)
    code_s[...] = (row_new * SIDE + col_new + past).astype(f32)

    pad_s[...] = jnp.zeros_like(pad_s)
    pad_s[0, :NQ] = queries_in[0].astype(f32)
    pad_s[1, :NQ] = pos_in[...].astype(f32)
    pad_s[2, :NQ] = out_grad_in[0].astype(f32)
    queries_f = pad_s[0]
    pos_f = pad_s[1]
    queries_b = queries_f.astype(bf16)
    mixed_q = (queries_f + pos_f).astype(bf16)
    query_self = (dot(mixed_q, attn_in[0, 0]) + bias[0:1]).astype(bf16)
    key_self = dot(mixed_q, attn_in[0, 1]).astype(bf16)
    value_self = (dot(queries_b, attn_in[0, 2]) + bias[1:2]).astype(bf16)
    scores = dot(key_self, spread_cols(query_self.astype(f32).T)) * scale
    own_key = lax.broadcasted_iota(jnp.int32, (NP, HQ), 0) < NQ
    scores = jnp.where(own_key, scores, masked_score)
    raised = jnp.exp(scores - jnp.max(scores, axis=0, keepdims=True))
    probs_self = raised / jnp.sum(raised, axis=0, keepdims=True)
    probs_self_b = probs_self.astype(bf16)
    value_t = value_self.astype(f32).T.astype(bf16)
    attended = own_blocks(
        [dot(value_t[pair_rows(p)], probs_self_b[:, pair_cols(p)]) for p in range(4)]
    ).T.astype(bf16)
    first_normed, first_rstd = norm_forward(queries_f + dot(attended, attn_out[0]) + bias[2:3])
    first = first_normed * gain[0:1] + shift[0:1]
    cross_q = (first + pos_f).astype(bf16)
    query_c = (dot(cross_q, attn_in[1, 0]) + bias[3:4]).astype(bf16)
    query_x = spread_rows(query_c.astype(f32))
    query_k = dot(attn_in[1, 1], spread_cols(query_c.astype(f32).T))
    query_kt[...] = (query_k * (scale * log2e)).astype(bf16)
    back_s[:HQ] = (dot_nt(query_x, attn_in[1, 1]) * scale).astype(bf16)
    table = table_in[...]
    nothing = jnp.zeros((SIDE, D // 2), f32)
    table = jnp.concatenate(
        [jnp.concatenate([table, nothing], axis=1), jnp.concatenate([nothing, table], axis=1)], axis=0
    )
    table_high = table.astype(bf16)
    table_s[: 2 * SIDE] = table_high
    table_s[2 * SIDE :] = (table - table_high.astype(f32)).astype(bf16)

    load_memory.wait()
    def mask_view(i):
        side, place = i // (chunks // 2), lax.rem(i, chunks // 2)
        return grad_scores_s.at[
            pl.ds(pl.multiple_of(tokens // 2 + place * CHUNK, CHUNK), CHUNK),
            pl.ds(pl.multiple_of(side * NP, NP), NP),
        ]

    lane = lax.broadcasted_iota(jnp.int32, (CHUNK, NP), 1)

    @each_two
    def _(i):
        rows = pl.ds(pl.multiple_of(i * CHUNK, CHUNK), CHUNK)
        line = code_s[:, rows]
        code = jnp.concatenate(
            [
                jnp.broadcast_to(line[:, NP * j : NP * j + NP], (NP, NP)).T
                for j in range(CHUNK // NP)
            ],
            axis=0,
        ).astype(jnp.int32)
        row_hot = jnp.where(((code >> 7) & 127) == lane, 1.0, 0.0).astype(bf16)
        col_hot = jnp.where((code & 127) == lane, 1.0, 0.0).astype(bf16)
        hot = jnp.concatenate([row_hot, col_hot, row_hot, col_hot], axis=1)
        masked = jnp.where(code < SIDE * SIDE, 0.0, masked_score)
        mask_view(i)[...] = masked.astype(bf16)
        key_in_s[rows] = (memory_s[rows].astype(f32) + dot(hot, table_s[...])).astype(bf16)

    def score_pair(p, key_in, mask, score_s):
        cols = pair_cols(p)
        part = dot(key_in, query_kt[:, cols]) + mask
        score_s[:, cols] = part
        top_s[:, cols] = jnp.max(part.reshape(CHUNK // 8, 8, PAIR), axis=0)

    def score_operands(i):
        rows = pl.ds(pl.multiple_of(i * CHUNK, CHUNK), CHUNK)
        mask = mask_view(i)[...].astype(f32)
        return key_in_s[rows], jnp.concatenate([mask, mask], axis=1)

    def attend_all(score_s):
        operands = score_operands(0)
        for p in range(4):
            score_pair(p, *operands, score_s)

        @pl.loop(0, chunks)
        def _(i):
            rows = pl.ds(pl.multiple_of(i * CHUNK, CHUNK), CHUNK)
            memory_ct = memory_s[rows].T
            operands = score_operands(jnp.minimum(i + 1, chunks - 1))
            for p in range(4):
                cols = pair_cols(p)
                before = highest_s[0:1, cols]
                highest = jnp.maximum(before, jnp.max(top_s[:, cols], axis=0, keepdims=True))
                highest_s[0:1, cols] = highest
                shifts_s[pl.ds(i, 1), cols] = highest
                fade = jnp.exp2(before - highest)
                raised = jnp.exp2(score_s[:, cols] - highest)
                sums = jnp.sum(raised.reshape(CHUNK // 8, 8, PAIR), axis=0)
                total_s[:, cols] = total_s[:, cols] * fade + sums
                probs_s[rows, cols] = raised.astype(bf16)
                mixed_s[:, cols] = mixed_s[:, cols] * fade + dot(memory_ct, probs_s[rows, cols])
                score_pair(p, *operands, score_s)

    highest_s[0:1] = jnp.full((1, HQ), -3e38, f32)
    total_s[...] = jnp.zeros_like(total_s)
    mixed_s[...] = jnp.zeros_like(mixed_s)
    pl.run_scoped(attend_all, pltpu.VMEM((CHUNK, HQ), f32))
    highest_own = highest_s[0:1]
    total_own = jnp.sum(total_s[...], axis=0, keepdims=True)

    value_wt = attn_in[1, 2].astype(f32).T.astype(bf16)
    key_wt = attn_in[1, 1].astype(f32).T.astype(bf16)
    send_a[...] = project_heads(value_wt, mixed_s[...]).astype(bf16)
    send_t[:HEADS] = head_rows(highest_own)
    send_t[HEADS:] = head_rows(total_own)
    pl.semaphore_wait(barrier, len(peers))
    swap_a = pltpu.make_async_remote_copy(
        src_ref=send_a,
        dst_ref=recv_a,
        send_sem=link_sem.at[0],
        recv_sem=link_sem.at[1],
        device_id=partner,
        device_id_type=pl.DeviceIdType.MESH,
    )
    swap_t = pltpu.make_async_remote_copy(
        src_ref=send_t,
        dst_ref=recv_t,
        send_sem=link_sem.at[4],
        recv_sem=link_sem.at[5],
        device_id=partner,
        device_id_type=pl.DeviceIdType.MESH,
    )
    swap_a.start()
    swap_t.start()
    swap_a.wait()
    swap_t.wait()
    is_first = member == 0
    own, other = send_a[...].astype(f32), recv_a[...].astype(f32)
    left = jnp.where(is_first, own, other)
    right = jnp.where(is_first, other, own)
    own, other = send_t[...], recv_t[...]
    left_t = jnp.where(is_first, own, other)
    right_t = jnp.where(is_first, other, own)
    highest = jnp.maximum(left_t[:HEADS], right_t[:HEADS])
    fade_l = jnp.exp2(left_t[:HEADS] - highest)
    fade_r = jnp.exp2(right_t[:HEADS] - highest)
    total = left_t[HEADS:] * fade_l + right_t[HEADS:] * fade_r
    mixed_t = left * per_channel(fade_l / total) + right * per_channel(fade_r / total)
    log_total = head_line(highest + jnp.log2(total))
    own_share = jnp.exp2(highest_own - log_total)
    factor_s[...] = jnp.exp2(shifts_s[...] - log_total)
    attended_c = (mixed_t.T + bias[4:5]).astype(bf16)

    second_normed, second_rstd = norm_forward(first + dot(attended_c, attn_out[1]) + bias[5:6])
    second = second_normed * gain[1:2] + shift[1:2]
    ffn_input = second.astype(bf16)
    load_ffn[0].wait()
    load_ffn[1].wait()
    blocks = [(j // 4, slice(D * j, D * j + D), slice(j % 4 * D, j % 4 * D + D)) for j in range(FF // D)]
    hidden_bias = ffn_in_bias[...].astype(f32).reshape(1, FF)
    def feed_forward(gate_s):
        for k, cols, part in blocks:
            hidden = dot(ffn_input, ffn_in_s[k][:, part]) + hidden_bias[:, cols]
            half_gate = 0.5 + 0.5 * lax.erf(hidden * math.sqrt(0.5))
            active_s[k][:, part] = (hidden * half_gate).astype(bf16)
            gate_s[:, cols] = half_gate + hidden * jnp.exp(hidden * hidden * -0.5) * (
                1.0 / math.sqrt(2.0 * math.pi)
            )
        load_ffn[2].wait()
        third_normed, third_rstd = norm_forward(
            second
            + dot(active_s[0][...], ffn_out_s[:half])
            + dot(active_s[1][...], ffn_out_s[half:])
            + ffn_out_bias[...].astype(f32).reshape(1, D)
        )
        result_out[...] = (third_normed * gain[2:3] + shift[2:3])[:NQ].astype(bf16)
        grad_third, gain_grad_2, shift_grad_2 = norm_backward(
            pad_s[2], third_normed, third_rstd, gain[2:3]
        )
        grad_branch_f = grad_third.astype(bf16)
        for k, cols, part in blocks:
            grad_hidden = dot_nt(grad_branch_f, ffn_out_s[cols]) * gate_s[:, cols]
            slope_s[k][:, part] = grad_hidden.astype(bf16)
        return grad_third, gain_grad_2, shift_grad_2, grad_branch_f

    grad_third, gain_grad_2, shift_grad_2, grad_branch_f = pl.run_scoped(
        feed_forward, pltpu.VMEM((NP, FF), f32)
    )
    grad_second = grad_third + dot_nt(slope_s[0][...], ffn_in_s[0][...])
    grad_second += dot_nt(slope_s[1][...], ffn_in_s[1][...])
    grad_second_in, gain_grad_1, shift_grad_1 = norm_backward(
        grad_second, second_normed, second_rstd, gain[1:2]
    )
    grad_branch_c = grad_second_in.astype(bf16)
    ffn_input_t = second.T.astype(bf16)

    @pl.when(member == 0)
    def _():
        for k, cols, part in blocks:
            rows_f[cols] = dot(ffn_input_t, slope_s[k][:, part]).astype(bf16)

    @pl.when(member == 1)
    def _():
        for k, cols, part in blocks:
            rows_f[cols] = dot_tn(active_s[k][:, part], grad_branch_f).astype(bf16)

    is_first = member == 0
    out_grad_c = dot_tn(attended_c, grad_branch_c)
    rows_k[2 * D : 3 * D] = jnp.where(is_first, out_grad_c, 0.0).astype(bf16)

    clear_rest(rows_f, ROWS_F)
    clear_rest(rows_t, ROWS_T)
    clear_rest(rows_k, ROWS_K)
    sum_f.phases[0]()
    grad_attended_c = dot_nt(grad_branch_c, attn_out[1]).astype(bf16).astype(f32)
    small_s[:16] = jnp.concatenate(
        [row_total(slope_s[k][:, part]) for k, _, part in blocks]
        + [
            row_total(grad_branch_f),
            row_total(grad_branch_c),
            gain_grad_2,
            shift_grad_2,
            gain_grad_1,
            shift_grad_1,
            row_total(grad_attended_c),
            jnp.zeros((1, D), f32),
        ],
        axis=0,
    )

    store_result = pltpu.make_async_copy(result_out, result_hbm, load_sem.at[7])
    store_result.start()

    grad_attended_t = grad_attended_c.T
    grad_x = spread_rows(grad_attended_c)
    grad_v = dot(attn_in[1, 2], spread_cols(grad_attended_t))
    grad_vt[...] = grad_v.astype(bf16)
    back_s[HQ:] = grad_v.T.astype(bf16)
    inner = head_line(head_sums(grad_attended_t * mixed_t))
    rows_k[D : 2 * D] = dot((mixed_s[...] * own_share).astype(bf16), grad_x).astype(bf16)
    mixed_s[...] = jnp.zeros_like(mixed_s)

    queue_f = sum_f.phases[1:]
    queue_t = list(sum_t.phases)
    queue_k = list(sum_k.phases)

    def take(queue):
        if queue:
            queue.pop(0)()

    def at(i, steps):
        for step, queue in steps:
            pl.when(i == (step * chunks) // 32)(queue.pop(0))

    def slope_block(i):
        rows = pl.ds(pl.multiple_of(i * CHUNK, CHUNK), CHUNK)
        key_ct = key_in_s[rows].T
        memory_c = memory_s[rows]
        for p in range(4):
            cols = pair_cols(p)
            grad_probs = dot(memory_c, grad_vt[:, cols])
            probs = probs_s[rows, cols].astype(f32) * factor_s[pl.ds(i, 1), cols]
            probs_s[rows, cols] = probs.astype(bf16)
            grad_scores_s[rows, cols] = (probs * (grad_probs - inner[:, cols])).astype(bf16)
        mixed_s[...] += dot(key_ct, grad_scores_s[rows])

    @pl.loop(0, chunks // 2)
    def _(i):
        slope_block(i * 2)
        slope_block(i * 2 + 1)
        at(i, [(3, queue_f), (9, queue_f), (15, queue_f)])

    send_b[...] = (project_heads(key_wt, mixed_s[...]) * scale).astype(bf16)
    swap_b = pltpu.make_async_remote_copy(
        src_ref=send_b,
        dst_ref=recv_b,
        send_sem=link_sem.at[2],
        recv_sem=link_sem.at[3],
        device_id=partner,
        device_id_type=pl.DeviceIdType.MESH,
    )
    swap_b.start()
    query_x = spread_rows(query_c.astype(f32))
    rows_k[:D] = (dot(mixed_s[...].astype(bf16), query_x) * scale).astype(bf16)
    take(queue_k)
    swap_b.wait()
    take(queue_f)
    take(queue_k)
    grad_query_c = (send_b[...].astype(f32) + recv_b[...].astype(f32)).T.astype(bf16)

    cross_pos_grad = dot_nt(grad_query_c, attn_in[1, 0])
    grad_first_in, gain_grad_0, shift_grad_0 = norm_backward(
        grad_second_in + cross_pos_grad, first_normed, first_rstd, gain[0:1]
    )
    grad_branch = grad_first_in.astype(bf16)
    grad_attended = dot_nt(grad_branch, attn_out[0]).astype(bf16).astype(f32)
    take(queue_k)
    grad_probs = dot(value_self, spread_cols(grad_attended.T))
    inner_self = jnp.sum(probs_self * grad_probs, axis=0, keepdims=True)
    grad_scores = (probs_self * (grad_probs - inner_self)).astype(bf16)
    key_t = key_self.astype(f32).T.astype(bf16)
    grad_query_s = (
        own_blocks([dot(key_t[pair_rows(p)], grad_scores[:, pair_cols(p)]) for p in range(4)]) * scale
    ).T.astype(bf16)
    grad_key_s = (dot(grad_scores, spread_rows(query_self.astype(f32))) * scale).astype(bf16)
    grad_value_s = dot(probs_self_b, spread_rows(grad_attended)).astype(bf16)
    grad_mixed_q = dot_nt(grad_query_s, attn_in[0, 0]) + dot_nt(grad_key_s, attn_in[0, 1])
    queries_grad_out[...] = (grad_first_in + grad_mixed_q + dot_nt(grad_value_s, attn_in[0, 2]))[
        :NQ
    ].astype(bf16)
    store_queries = pltpu.make_async_copy(queries_grad_out, queries_grad_hbm, load_sem.at[8])
    store_queries.start()
    small_s[16:] = jnp.concatenate(
        [
            row_total(grad_query_s),
            row_total(grad_value_s),
            row_total(grad_branch),
            row_total(grad_query_c),
            gain_grad_0,
            shift_grad_0,
            jnp.zeros((10, D), f32),
        ],
        axis=0,
    )
    @pl.when(member == 0)
    def _():
        rows_t[:D] = dot_tn(mixed_q, grad_query_s).astype(bf16)
        rows_t[D : 2 * D] = dot_tn(mixed_q, grad_key_s).astype(bf16)
        rows_t[2 * D : 3 * D] = dot_tn(queries_b, grad_value_s).astype(bf16)

    @pl.when(member == 1)
    def _():
        rows_t[:D] = dot_tn(cross_q, grad_query_c).astype(bf16)
        rows_t[D : 2 * D] = dot_tn(attended, grad_branch).astype(bf16)
        rows_t[ROW_POS:ROW_SMALL] = (grad_mixed_q + cross_pos_grad).astype(bf16)
        rows_t[ROW_SMALL : ROW_SMALL + 32] = small_s[...].astype(bf16)
        rows_t[ROW_SMALL + 32 : ROWS_T] = jnp.zeros((ROWS_T - ROW_SMALL - 32, D), bf16)

    take(queue_t)
    take(queue_k)
    take(queue_f)

    def memory_block(i):
        rows = pl.ds(pl.multiple_of(i * CHUNK, CHUNK), CHUNK)
        both = jnp.concatenate([grad_scores_s[rows], probs_s[rows]], axis=1)
        memory_s[rows] = dot(both, back_s[...]).astype(bf16)
        pltpu.make_async_copy(memory_s.at[rows], memory_grad_hbm.at[0, rows], store_sem.at[i]).start()

    @pl.loop(0, chunks // 2)
    def _(i):
        memory_block(i * 2)
        memory_block(i * 2 + 1)
        at(
            i,
            [
                (3, queue_t),
                (4, queue_k),
                (7, queue_t),
                (8, queue_k),
                (9, queue_f),
                (11, queue_t),
                (12, queue_k),
                (15, queue_t),
            ],
        )

    while queue_f:
        take(queue_f)
    stores = [
        pltpu.make_async_copy(whole, target, load_sem.at[4 + k])
        for k, (whole, target) in enumerate(
            (
                (whole_f, whole_f_hbm),
                (whole_t, whole_t_hbm),
                (whole_k, whole_k_hbm),
            )
        )
    ]
    stores[0].start()
    while queue_t or queue_k:
        take(queue_t)
        take(queue_k)
    for store in stores[1:]:
        store.start()

    @pl.loop(0, chunks)
    def _(i):
        rows = pl.ds(pl.multiple_of(i * CHUNK, CHUNK), CHUNK)
        pltpu.make_async_copy(memory_s.at[rows], memory_grad_hbm.at[0, rows], store_sem.at[i]).wait()

    for store in [*stores, store_result, store_queries]:
        store.wait()


def finish_kernel(
    result_in,
    queries_grad_in,
    memory_grad_in,
    whole_f_hbm,
    whole_t_hbm,
    whole_k_hbm,
    result_hbm,
    queries_grad_hbm,
    memory_grad,
    attn_in_hbm,
    attn_out_hbm,
    attn_bias_hbm,
    ffn_in_hbm,
    ffn_in_bias_hbm,
    ffn_out_hbm,
    ffn_out_bias_hbm,
    norm_gain_hbm,
    norm_bias_hbm,
    query_pos_hbm,
    moved,
    whole_f,
    whole_t,
    whole_k,
    result,
    queries_grad,
    attn_in_grad,
    attn_out_grad,
    attn_bias_grad,
    ffn_in_grad,
    ffn_in_bias_grad,
    ffn_out_grad,
    ffn_out_bias_grad,
    norm_gain_grad,
    norm_bias_grad,
    query_pos_grad,
    in_sem,
    out_sem,
    sum_sem,
    grad_sem,
):
    pieces = in_sem.shape[0]
    piece = moved.shape[0] // pieces

    def fetch(j):
        rows = pl.ds(piece * j, piece)
        return pltpu.make_async_copy(memory_grad_in.at[0, rows], moved.at[rows], in_sem.at[j])

    def write(j):
        rows = pl.ds(piece * j, piece)
        return pltpu.make_async_copy(moved.at[rows], memory_grad.at[0, rows], out_sem.at[j])

    sums = [
        (whole_t_hbm, whole_t),
        (whole_k_hbm, whole_k),
        (whole_f_hbm, whole_f),
        (result_in, result),
        (queries_grad_in, queries_grad),
    ]
    loads = [pltpu.make_async_copy(*pair, sum_sem.at[j]) for j, pair in enumerate(sums)]
    for load in loads:
        load.start()
    for j in range(pieces):
        fetch(j).start()
    blocks = FF // D
    stores = []

    def store(source, target):
        stores.append(pltpu.make_async_copy(source, target, grad_sem.at[len(stores)]))
        stores[-1].start()

    loads[0].wait()
    loads[1].wait()
    for j in range(3):
        attn_in_grad[0, j] = whole_t[0, D * j : D * j + D].astype(f32)
    attn_in_grad[1, 0] = whole_t[1, :D].astype(f32)
    attn_in_grad[1, 1] = whole_k[:D].astype(f32)
    attn_in_grad[1, 2] = whole_k[D : 2 * D].astype(f32)
    store(attn_in_grad, attn_in_hbm)
    attn_out_grad[0] = whole_t[1, D : 2 * D].astype(f32)
    attn_out_grad[1] = whole_k[2 * D : 3 * D].astype(f32)
    store(attn_out_grad, attn_out_hbm)
    loads[2].wait()
    for k in range(2):
        half = slice(FF // 2 * k, FF // 2 * (k + 1))
        ffn_out_grad[half] = whole_f[1, half].astype(f32)
        store(ffn_out_grad.at[half], ffn_out_hbm.at[half])
    for k in range(2):
        half = slice(FF // 2 * k, FF // 2 * (k + 1))
        for j in range(blocks // 2 * k, blocks // 2 * (k + 1)):
            at = slice(D * j, D * j + D)
            ffn_in_grad[:, at] = whole_f[0, at].astype(f32)
        store(ffn_in_grad.at[:, half], ffn_in_hbm.at[:, half])
    for j in range(pieces):
        fetch(j).wait()
        write(j).start()
    loads[3].wait()
    store(result, result_hbm.at[0])
    loads[4].wait()
    store(queries_grad, queries_grad_hbm.at[0])
    query_pos_grad[...] = whole_t[1, ROW_POS:ROW_SMALL].astype(f32)[:NQ]
    store(query_pos_grad, query_pos_hbm)
    small = whole_t[1, ROW_SMALL : ROW_SMALL + 32].astype(f32)
    ffn_in_bias_grad[...] = jnp.concatenate([small[j : j + 1] for j in range(blocks)], axis=1)
    store(ffn_in_bias_grad, ffn_in_bias_hbm)
    ffn_out_bias_grad[...] = small[8:9]
    store(ffn_out_bias_grad, ffn_out_bias_hbm)
    for j, (own, cross) in enumerate(((16, 19), (17, 14), (18, 9))):
        attn_bias_grad[j, 0:1] = small[own : own + 1]
        attn_bias_grad[j, 1:2] = small[cross : cross + 1]
    store(attn_bias_grad, attn_bias_hbm)
    for j, (gain, shift) in enumerate(((20, 21), (12, 13), (10, 11))):
        norm_gain_grad[j : j + 1] = small[gain : gain + 1]
        norm_bias_grad[j : j + 1] = small[shift : shift + 1]
    store(norm_gain_grad, norm_gain_hbm)
    store(norm_bias_grad, norm_bias_hbm)
    for j in range(pieces):
        write(j).wait()
    for copy in stores:
        copy.wait()


def body(
    pages,
    queries,
    memory,
    quarter_turns,
    token_order,
    lengths,
    attn_in,
    attn_out,
    attn_bias,
    ffn_in,
    ffn_in_bias,
    ffn_out,
    ffn_out_bias,
    norm_gain,
    norm_bias,
    query_pos,
    out_grad,
):
    tokens = memory.shape[1]
    chunks = tokens // CHUNK
    groups_f, groups_t, groups_k = sum_groups(pages)
    summed = [
        (padded(ROWS_F, pages), groups_f),
        (padded(ROWS_T, pages), groups_t),
        (padded(ROWS_K, 2 * pages), groups_k),
    ]
    whole_shapes = [(2, rows, D) for rows, _ in summed[:2]] + [(summed[2][0], D)]
    sum_buffers = []
    for (rows, groups), shape in zip(summed, whole_shapes):
        landing = PageSum.landing_rows(pages, groups, rows)
        sum_buffers += [pltpu.VMEM(each, bf16) for each in ((rows, D), (landing, D), shape)]
    copies = 32
    vmem = pl.BlockSpec(memory_space=pltpu.VMEM)
    smem = pl.BlockSpec(memory_space=pltpu.SMEM)
    anywhere = pl.BlockSpec(memory_space=pl.ANY)
    parts = pl.pallas_call(
        functools.partial(layer_kernel, tokens, pages),
        out_shape=[
            jax.ShapeDtypeStruct((NQ, D), bf16),
            jax.ShapeDtypeStruct((NQ, D), bf16),
            jax.ShapeDtypeStruct((1, tokens, D), bf16),
            *(jax.ShapeDtypeStruct(shape, bf16) for shape in whole_shapes),
        ],
        in_specs=[
            vmem,
            anywhere,
            smem,
            vmem,
            smem,
            vmem,
            vmem,
            vmem,
            anywhere,
            vmem,
            anywhere,
            vmem,
            vmem,
            vmem,
            vmem,
            vmem,
            vmem,
        ],
        out_specs=[anywhere] * 6,
        scratch_shapes=[
            pltpu.VMEM((tokens, D), bf16),
            pltpu.VMEM((tokens, D), bf16),
            pltpu.VMEM((tokens, HQ), bf16),
            pltpu.VMEM((tokens, HQ), bf16),
            pltpu.VMEM((1, tokens), f32),
            pltpu.VMEM((D, HQ), bf16),
            pltpu.VMEM((D, HQ), bf16),
            pltpu.VMEM((2 * HQ, D), bf16),
            pltpu.VMEM((4 * SIDE, D), bf16),
            pltpu.VMEM((8, HQ), f32),
            pltpu.VMEM((8, HQ), f32),
            pltpu.VMEM((chunks, HQ), f32),
            pltpu.VMEM((chunks, HQ), f32),
            pltpu.VMEM((8, HQ), f32),
            pltpu.VMEM((D, HQ), f32),
            pltpu.VMEM((3, NP, D), f32),
            pltpu.VMEM((NQ, D), bf16),
            pltpu.VMEM((NQ, D), bf16),
            pltpu.VMEM((D, NP), bf16),
            pltpu.VMEM((D, NP), bf16),
            pltpu.VMEM((2 * HEADS, NP), f32),
            pltpu.VMEM((2 * HEADS, NP), f32),
            pltpu.VMEM((D, NP), bf16),
            pltpu.VMEM((D, NP), bf16),
            pltpu.VMEM((32, D), f32),
            *sum_buffers,
            pltpu.SemaphoreType.DMA((9,)),
            pltpu.SemaphoreType.DMA((chunks,)),
            pltpu.SemaphoreType.DMA((6,)),
            *[pltpu.SemaphoreType.DMA((copies,))] * 6,
        ],
        compiler_params=pltpu.CompilerParams(
            collective_id=0, has_side_effects=True, vmem_limit_bytes=127 * 512 * 1024
        ),
        cost_estimate=pl.CostEstimate(
            flops=2 * 8 * tokens * HQ * D, bytes_accessed=20 << 20, transcendentals=tokens * HQ
        ),
        name="decoder_layer",
    )(
        queries,
        memory,
        quarter_turns,
        token_order,
        lengths,
        attn_in,
        attn_out,
        attn_bias.transpose(1, 0, 2),
        ffn_in,
        ffn_in_bias,
        ffn_out,
        ffn_out_bias,
        norm_gain,
        norm_bias,
        query_pos,
        out_grad,
        jnp.asarray(position_table()),
    )
    outs = pl.pallas_call(
        finish_kernel,
        out_shape=[
            jax.ShapeDtypeStruct((1, NQ, D), bf16),
            jax.ShapeDtypeStruct((1, NQ, D), bf16),
            jax.ShapeDtypeStruct((1, tokens, D), bf16),
            jax.ShapeDtypeStruct((2, 3, D, D), f32),
            jax.ShapeDtypeStruct((2, D, D), f32),
            jax.ShapeDtypeStruct((3, 2, D), f32),
            jax.ShapeDtypeStruct((D, FF), f32),
            jax.ShapeDtypeStruct((1, FF), f32),
            jax.ShapeDtypeStruct((FF, D), f32),
            jax.ShapeDtypeStruct((1, D), f32),
            jax.ShapeDtypeStruct((3, D), f32),
            jax.ShapeDtypeStruct((3, D), f32),
            jax.ShapeDtypeStruct((NQ, D), f32),
        ],
        in_specs=[anywhere] * 6,
        out_specs=[anywhere] * 13,
        scratch_shapes=[
            pltpu.VMEM((tokens, D), bf16),
            *(pltpu.VMEM(shape, bf16) for shape in whole_shapes),
            pltpu.VMEM((NQ, D), bf16),
            pltpu.VMEM((NQ, D), bf16),
            pltpu.VMEM((2, 3, D, D), f32),
            pltpu.VMEM((2, D, D), f32),
            pltpu.VMEM((3, 2, D), f32),
            pltpu.VMEM((D, FF), f32),
            pltpu.VMEM((1, FF), f32),
            pltpu.VMEM((FF, D), f32),
            pltpu.VMEM((1, D), f32),
            pltpu.VMEM((3, D), f32),
            pltpu.VMEM((3, D), f32),
            pltpu.VMEM((NQ, D), f32),
            pltpu.SemaphoreType.DMA((8,)),
            pltpu.SemaphoreType.DMA((8,)),
            pltpu.SemaphoreType.DMA((5,)),
            pltpu.SemaphoreType.DMA((14,)),
        ],
        compiler_params=pltpu.CompilerParams(vmem_limit_bytes=62 * 1024 * 1024),
        name="write_outputs",
    )(*parts)
    return (
        *outs[:5],
        outs[5].transpose(1, 0, 2),
        outs[6],
        outs[7].reshape(FF),
        outs[8],
        outs[9].reshape(D),
        *outs[10:],
    )


def solution(mesh):
    in_specs = (
        P("dp", None, None),
        P("dp", "blk", None),
        P("dp"),
        P("dp", "blk"),
        P("dp"),
        P(),
        P(),
        P(),
        P(),
        P(),
        P(),
        P(),
        P(),
        P(),
        P(),
        P("dp", None, None),
    )
    out_specs = (
        P("dp", None, None),
        P("dp", None, None),
        P("dp", "blk", None),
        P(),
        P(),
        P(),
        P(),
        P(),
        P(),
        P(),
        P(),
        P(),
        P(),
    )
    layer = functools.partial(body, mesh.shape["dp"])
    return jax.shard_map(layer, mesh=mesh, in_specs=in_specs, out_specs=out_specs, check_vma=False)
```

```python
import functools
import math

import jax
import jax.numpy as jnp
import numpy as np
from jax import lax
from jax.experimental import pallas as pl
from jax.experimental.pallas import tpu as pltpu
from jax.sharding import PartitionSpec as P

D = 256
HEADS = 8
HD = D // HEADS
SIDE = 128
NQ = 125
NP = 128
HQ = HEADS * NP
PAIR = 2 * NP
FF = 2048
CHUNK = 1024

masked_score = -1e30
norm_eps = 1e-05
scale = 1.0 / math.sqrt(HD)
log2e = math.log2(math.e)

bf16 = jnp.bfloat16
f32 = jnp.float32

ROWS_F = FF
ROW_POS = 2 * D
ROW_SMALL = 2 * D + NP
ROWS_T = 3 * D
ROWS_K = 3 * D
TILE = 16


def axes_of(pages):
    axes = {"core": (2, 1), "y": (2, 2)}
    stride = 4
    while stride < pages:
        radix = 4 if pages // stride % 4 == 0 else 2
        axes["z%d" % (len(axes) - 2)] = (radix, stride)
        stride *= radix
    axes["x"] = (2, 0)
    return axes


def far_axes(pages):
    return [(name,) for name in axes_of(pages) if name.startswith("z")]


def sum_groups(pages):
    far = far_axes(pages)
    return [("core",), ("y",), *far], [("core", "y"), *far], [("core",), ("x",), ("y",), *far]


def padded(rows, pages):
    unit = TILE * pages
    return (rows + unit - 1) // unit * unit


def position_table():
    half = D // 2
    channel = np.arange(half)
    inverse = np.exp((channel // 2).astype(np.float32) * np.float32(-2.0 * math.log(10000.0) / half))
    angle = (np.arange(SIDE, dtype=np.float32) + 1.0) * np.float32(2.0 * math.pi / SIDE)
    angle = angle[:, None] * inverse
    return np.where(channel % 2 == 0, np.sin(angle), np.cos(angle)).astype(np.float32)


def dot(a, b):
    return jnp.dot(a, b, preferred_element_type=f32)


def dot_nt(a, b):
    return lax.dot_general(a, b, (((1,), (1,)), ((), ())), preferred_element_type=f32)


def dot_tn(a, b):
    return lax.dot_general(a, b, (((0,), (0,)), ((), ())), preferred_element_type=f32)


def row_total(values):
    return jnp.sum(values.astype(f32), axis=0, keepdims=True)


def norm_forward(values):
    average = jnp.mean(values, axis=-1, keepdims=True)
    centred = values - average
    variance = jnp.mean(centred * centred, axis=-1, keepdims=True)
    rstd = lax.rsqrt(variance + norm_eps)
    return centred * rstd, rstd


def norm_backward(grad, normed, rstd, gain):
    grad_normed = grad * gain
    first = jnp.mean(grad_normed, axis=-1, keepdims=True)
    second = jnp.mean(grad_normed * normed, axis=-1, keepdims=True)
    grad_in = rstd * (grad_normed - first - normed * second)
    return grad_in, row_total(grad * normed), row_total(grad)


def spread_rows(rows):
    head = lax.broadcasted_iota(jnp.int32, (NP, D), 1) // HD
    return jnp.concatenate(
        [jnp.where(head == h, rows, 0.0) for h in range(HEADS)], axis=0
    ).astype(bf16)


def spread_cols(cols):
    head = lax.broadcasted_iota(jnp.int32, (D, NP), 0) // HD
    return jnp.concatenate(
        [jnp.where(head == h, cols, 0.0) for h in range(HEADS)], axis=1
    ).astype(bf16)


def project_heads(weight_t, sums):
    high = sums.astype(bf16)
    low = (sums - high.astype(f32)).astype(bf16)
    return own_blocks(
        [
            dot(weight_t[pair_rows(p)], high[:, pair_cols(p)])
            + dot(weight_t[pair_rows(p)], low[:, pair_cols(p)])
            for p in range(4)
        ]
    )


def own_blocks(pairs):
    parts = []
    for pair in pairs:
        parts += [pair[:HD, :NP], pair[HD:, NP:]]
    return jnp.concatenate(parts, axis=0)


def head_rows(row):
    return jnp.concatenate([row[:, NP * h : NP * h + NP] for h in range(HEADS)], axis=0)


def head_line(rows):
    return jnp.concatenate([rows[h : h + 1] for h in range(HEADS)], axis=1)


def per_channel(rows):
    return jnp.concatenate(
        [jnp.broadcast_to(rows[h : h + 1], (HD, NP)) for h in range(HEADS)], axis=0
    )


def head_sums(cols):
    return jnp.concatenate(
        [jnp.sum(cols[HD * h : HD * h + HD], axis=0, keepdims=True) for h in range(HEADS)], axis=0
    )


def pair_cols(p):
    return slice(PAIR * p, PAIR * p + PAIR)


def pair_rows(p):
    return slice(2 * HD * p, 2 * HD * p + 2 * HD)


class Place:
    def __init__(self, pages):
        self.axes = axes_of(pages)
        self.page = lax.axis_index("dp")
        self.member = lax.axis_index("blk")
        self.digit = {
            name: self.member if name == "x" else lax.rem(self.page // stride, radix)
            for name, (radix, stride) in self.axes.items()
        }

    def size(self, group):
        return math.prod(self.axes[name][0] for name in group)

    def index(self, group):
        index = 0
        for name in group:
            index = index * self.axes[name][0] + self.digit[name]
        return index

    def peer(self, group, hop):
        index = lax.rem(self.index(group) + hop, self.size(group))
        page, member, rest = self.page, self.member, index
        for name in reversed(group):
            radix, stride = self.axes[name]
            digit = lax.rem(rest, radix)
            rest = rest // radix
            if name == "x":
                member = digit
            else:
                page = page + (digit - self.digit[name]) * stride
        return (page, member), index


class PageSum:
    def __init__(self, place, groups, back, rows, landing, whole, sent, arrived):
        self.place, self.groups, self.back = place, groups, back
        self.rows, self.landing, self.whole = rows, landing, whole
        self.sent, self.arrived = sent, arrived
        self.slots = 0
        self.extents = [rows.shape[0]]
        self.bases = [0]
        self.landings = []
        at = 0
        for group in groups:
            size = place.size(group)
            extent = self.extents[-1] // size
            self.landings.append(at)
            at += (size - 1) * extent
            self.bases.append(pl.multiple_of(self.bases[-1] + place.index(group) * extent, TILE))
            self.extents.append(extent)
        last = len(groups)
        moves = [self.scatter_moves(s) for s in range(last)]
        near = {"all": 0, "across": 1, "sides": 2}[back]
        moves += [self.gather_moves(s) for s in range(last - 1, near - 1, -1)]
        if back == "sides":
            moves += [self.side_moves(), self.corner_moves(), self.core_moves()]
        elif back == "across":
            moves += [self.across_moves(), self.core_moves()]
        self.phases = [functools.partial(self.step, moves, k) for k in range(len(moves) + 1)]

    @staticmethod
    def landing_rows(pages, groups, rows):
        axes = axes_of(pages)
        total, extent = 0, rows
        for group in groups:
            size = math.prod(axes[name][0] for name in group)
            extent //= size
            total += (size - 1) * extent
        return total

    def step(self, moves, k):
        last = len(self.groups)
        if k > 0:
            for move in moves[k - 1]:
                self.copy(*move).wait()
        if 0 < k <= last:
            total = self.scatter_sum(k - 1)
            region = pl.ds(self.bases[k], self.extents[k])
            if k < last:
                self.rows[region] = total
            elif len(self.whole.shape) == 3:
                self.whole[self.place.member, region] = total
            else:
                self.whole[region] = total
        if k < len(moves):
            for move in moves[k]:
                self.copy(*move).start()

    def copy(self, slot, source, target, device):
        return pltpu.make_async_remote_copy(
            src_ref=source(),
            dst_ref=target(),
            send_sem=self.sent.at[slot],
            recv_sem=self.arrived.at[slot],
            device_id=device,
            device_id_type=pl.DeviceIdType.MESH,
        )

    def new_slot(self):
        self.slots += 1
        return self.slots - 1

    def same(self, device, view):
        return (self.new_slot(), view, view, device)

    def scatter_moves(self, step):
        group = self.groups[step]
        extent = self.extents[step + 1]
        moves = []
        for hop in range(1, self.place.size(group)):
            device, other = self.place.peer(group, hop)
            start = pl.multiple_of(self.bases[step] + other * extent, TILE)
            landing = self.landings[step] + (hop - 1) * extent
            moves.append(
                (
                    self.new_slot(),
                    functools.partial(self.part, self.rows, start, extent),
                    functools.partial(self.part, self.landing, landing, extent),
                    device,
                )
            )
        return moves

    @staticmethod
    def part(ref, start, extent):
        return ref.at[pl.ds(start, extent)]

    def half(self, member, start, extent):
        if len(self.whole.shape) == 3:
            return self.whole.at[member, pl.ds(start, extent)]
        return self.whole.at[pl.ds(start, extent)]

    def scatter_sum(self, step):
        extent = self.extents[step + 1]
        total = self.rows[pl.ds(self.bases[step + 1], extent)].astype(f32)
        for hop in range(1, self.place.size(self.groups[step])):
            landing = self.landings[step] + (hop - 1) * extent
            total = total + self.landing[pl.ds(landing, extent)].astype(f32)
        return total.astype(bf16)

    def gather_moves(self, step):
        group = self.groups[step]
        view = functools.partial(self.half, self.place.member, self.bases[step + 1], self.extents[step + 1])
        return [
            self.same(self.place.peer(group, hop)[0], view) for hop in range(1, self.place.size(group))
        ]

    def own_quarter(self):
        step = 2 if len(self.groups[0]) == 1 else 1
        return self.bases[step], self.extents[step]

    def side_moves(self):
        view = functools.partial(self.half, self.place.member, *self.own_quarter())
        return [self.same(self.place.peer((name,), 1)[0], view) for name in ("y", "x")]

    def corner_moves(self):
        base, extent = self.own_quarter()
        other = pl.multiple_of(base + (1 - 2 * self.place.digit["y"]) * extent, TILE)
        view = functools.partial(self.half, self.place.member, other, extent)
        return [self.same(self.place.peer(("x",), 1)[0], view)]

    def across_moves(self):
        view = functools.partial(self.half, self.place.member, *self.own_quarter())
        return [self.same(self.place.peer(("x", "y"), hop)[0], view) for hop in range(1, 4)]

    def core_moves(self):
        extent = self.extents[0] // 2
        start = pl.multiple_of(self.place.digit["core"] * extent, TILE)
        device, _ = self.place.peer(("core",), 1)
        return [self.same(device, functools.partial(self.half, m, start, extent)) for m in range(2)]


def clear_rest(ref, used):
    if ref.shape[0] > used:
        ref[used:] = jnp.zeros((ref.shape[0] - used, D), ref.dtype)


def layer_kernel(
    tokens,
    pages,
    queries_in,
    memory_hbm,
    turns_in,
    order_in,
    lengths_in,
    attn_in,
    attn_out,
    attn_bias,
    ffn_in_hbm,
    ffn_in_bias,
    ffn_out_hbm,
    ffn_out_bias,
    norm_gain,
    norm_bias,
    pos_in,
    out_grad_in,
    table_in,
    result_hbm,
    queries_grad_hbm,
    memory_grad_hbm,
    whole_f_hbm,
    whole_t_hbm,
    whole_k_hbm,
    memory_s,
    key_in_s,
    probs_s,
    grad_scores_s,
    code_s,
    query_kt,
    value_rows,
    table_s,
    top_s,
    highest_s,
    shifts_s,
    factor_s,
    total_s,
    mixed_s,
    pad_s,
    result_out,
    queries_grad_out,
    send_a,
    recv_a,
    send_t,
    recv_t,
    send_b,
    recv_b,
    small_s,
    rows_f,
    landing_f,
    whole_f,
    landing_t,
    whole_t,
    landing_k,
    whole_k,
    load_sem,
    store_sem,
    link_sem,
    sent_f,
    arrived_f,
    sent_t,
    arrived_t,
    sent_k,
    arrived_k,
):
    member = lax.axis_index("blk")
    partner = (lax.axis_index("dp"), 1 - member)
    chunks = tokens // CHUNK

    place = Place(pages)
    grad_vt = query_kt
    back_s = key_in_s.at[: 2 * HQ]
    first_t = 2 * HQ + padded(ROWS_K, 2 * pages)
    rows_k = key_in_s.at[2 * HQ : first_t]
    rows_t = key_in_s.at[first_t : first_t + padded(ROWS_T, pages)]
    groups_f, groups_t, groups_k = sum_groups(pages)
    sum_f = PageSum(place, groups_f, "sides", rows_f, landing_f, whole_f, sent_f, arrived_f)
    sum_t = PageSum(place, groups_t, "across", rows_t, landing_t, whole_t, sent_t, arrived_t)
    sum_k = PageSum(place, groups_k, "all", rows_k, landing_k, whole_k, sent_k, arrived_k)

    barrier = pltpu.get_barrier_semaphore()
    peers = [
        place.peer(group, hop)[0]
        for group in [("x", "core", "y"), *far_axes(pages)]
        for hop in range(1, place.size(group))
    ]
    for peer in peers:
        pl.semaphore_signal(barrier, inc=1, device_id=peer, device_id_type=pl.DeviceIdType.MESH)

    load_memory = pltpu.make_async_copy(memory_hbm.at[0], memory_s, load_sem.at[0])
    half = FF // 2
    ffn_in_s = [grad_scores_s.at[D * k : D * k + D] for k in range(2)]
    ffn_out_s = grad_scores_s.at[2 * D : 2 * D + FF, :D]
    free = 2 * D + FF
    active_s = [grad_scores_s.at[free + NP * k : free + NP * k + NP] for k in range(2)]
    slope_s = [grad_scores_s.at[free + NP * k : free + NP * k + NP] for k in range(2, 4)]
    load_ffn = [
        pltpu.make_async_copy(ffn_in_hbm.at[:, half * k : half * k + half], ffn_in_s[k], load_sem.at[1 + k])
        for k in range(2)
    ]
    load_ffn.append(pltpu.make_async_copy(ffn_out_hbm, ffn_out_s, load_sem.at[3]))
    load_memory.start()
    for load in load_ffn:
        load.start()

    pairs = [attn_bias[j].astype(f32) for j in range(3)]
    bias = jnp.concatenate([pair[k : k + 1] for k in range(2) for pair in pairs], axis=0)
    gain = norm_gain[...].astype(f32)
    shift = norm_bias[...].astype(f32)

    def each_two(block):
        @pl.loop(0, chunks // 2)
        def _(j):
            block(j * 2)
            block(j * 2 + 1)

    order = order_in[...]
    turn = turns_in[0]
    row_at = order >> 7
    col_at = order & 127
    top = SIDE - 1
    row_new = jnp.where(
        turn == 0, row_at, jnp.where(turn == 1, col_at, jnp.where(turn == 2, top - row_at, top - col_at))
    )
    col_new = jnp.where(
        turn == 0, col_at, jnp.where(turn == 1, top - row_at, jnp.where(turn == 2, top - col_at, row_at))
    )
    past = jnp.where(order < lengths_in[0], 0, SIDE * SIDE)
    code_s[...] = (row_new * SIDE + col_new + past).astype(f32)

    pad_s[...] = jnp.zeros_like(pad_s)
    pad_s[0, :NQ] = queries_in[0].astype(f32)
    pad_s[1, :NQ] = pos_in[...].astype(f32)
    pad_s[2, :NQ] = out_grad_in[0].astype(f32)
    queries_f = pad_s[0]
    pos_f = pad_s[1]
    queries_b = queries_f.astype(bf16)
    mixed_q = (queries_f + pos_f).astype(bf16)
    query_self = (dot(mixed_q, attn_in[0, 0]) + bias[0:1]).astype(bf16)
    key_self = dot(mixed_q, attn_in[0, 1]).astype(bf16)
    value_self = (dot(queries_b, attn_in[0, 2]) + bias[1:2]).astype(bf16)
    scores = dot(key_self, spread_cols(query_self.astype(f32).T)) * scale
    own_key = lax.broadcasted_iota(jnp.int32, (NP, HQ), 0) < NQ
    scores = jnp.where(own_key, scores, masked_score)
    raised = jnp.exp(scores - jnp.max(scores, axis=0, keepdims=True))
    probs_self = raised / jnp.sum(raised, axis=0, keepdims=True)
    probs_self_b = probs_self.astype(bf16)
    value_t = value_self.astype(f32).T.astype(bf16)
    attended = own_blocks(
        [dot(value_t[pair_rows(p)], probs_self_b[:, pair_cols(p)]) for p in range(4)]
    ).T.astype(bf16)
    first_normed, first_rstd = norm_forward(queries_f + dot(attended, attn_out[0]) + bias[2:3])
    first = first_normed * gain[0:1] + shift[0:1]
    cross_q = (first + pos_f).astype(bf16)
    query_c = (dot(cross_q, attn_in[1, 0]) + bias[3:4]).astype(bf16)
    query_k = dot(attn_in[1, 1], spread_cols(query_c.astype(f32).T))
    query_kt[...] = (query_k * (scale * log2e)).astype(bf16)
    table = table_in[...]
    nothing = jnp.zeros((SIDE, D // 2), f32)
    table = jnp.concatenate(
        [jnp.concatenate([table, nothing], axis=1), jnp.concatenate([nothing, table], axis=1)], axis=0
    )
    table_high = table.astype(bf16)
    table_s[: 2 * SIDE] = table_high
    table_s[2 * SIDE :] = (table - table_high.astype(f32)).astype(bf16)

    load_memory.wait()
    def mask_view(i):
        side, place = i // (chunks // 2), lax.rem(i, chunks // 2)
        return grad_scores_s.at[
            pl.ds(pl.multiple_of(tokens // 2 + place * CHUNK, CHUNK), CHUNK),
            pl.ds(pl.multiple_of(side * NP, NP), NP),
        ]

    lane = lax.broadcasted_iota(jnp.int32, (CHUNK, NP), 1)

    @each_two
    def _(i):
        rows = pl.ds(pl.multiple_of(i * CHUNK, CHUNK), CHUNK)
        line = code_s[:, rows]
        code = jnp.concatenate(
            [
                jnp.broadcast_to(line[:, NP * j : NP * j + NP], (NP, NP)).T
                for j in range(CHUNK // NP)
            ],
            axis=0,
        ).astype(jnp.int32)
        row_hot = jnp.where(((code >> 7) & 127) == lane, 1.0, 0.0).astype(bf16)
        col_hot = jnp.where((code & 127) == lane, 1.0, 0.0).astype(bf16)
        hot = jnp.concatenate([row_hot, col_hot, row_hot, col_hot], axis=1)
        masked = jnp.where(code < SIDE * SIDE, 0.0, masked_score)
        mask_view(i)[...] = masked.astype(bf16)
        key_in_s[rows] = (memory_s[rows].astype(f32) + dot(hot, table_s[...])).astype(bf16)

    def score_pair(p, key_in, mask, score_s):
        cols = pair_cols(p)
        part = dot(key_in, query_kt[:, cols]) + mask
        score_s[:, cols] = part
        top_s[:, cols] = jnp.max(part.reshape(CHUNK // 8, 8, PAIR), axis=0)

    def score_operands(i):
        rows = pl.ds(pl.multiple_of(i * CHUNK, CHUNK), CHUNK)
        mask = mask_view(i)[...].astype(f32)
        return key_in_s[rows], jnp.concatenate([mask, mask], axis=1)

    def attend_all(score_s):
        operands = score_operands(0)
        for p in range(4):
            score_pair(p, *operands, score_s)

        @(each_two if pages <= 16 else pl.loop(0, chunks))
        def _(i):
            rows = pl.ds(pl.multiple_of(i * CHUNK, CHUNK), CHUNK)
            memory_ct = memory_s[rows].T
            operands = score_operands(jnp.minimum(i + 1, chunks - 1))
            for p in range(4):
                cols = pair_cols(p)
                before = highest_s[0:1, cols]
                highest = jnp.maximum(before, jnp.max(top_s[:, cols], axis=0, keepdims=True))
                highest_s[0:1, cols] = highest
                shifts_s[pl.ds(i, 1), cols] = highest
                fade = jnp.exp2(before - highest)
                raised = jnp.exp2(score_s[:, cols] - highest)
                sums = jnp.sum(raised.reshape(CHUNK // 8, 8, PAIR), axis=0)
                total_s[:, cols] = total_s[:, cols] * fade + sums
                probs_s[rows, cols] = raised.astype(bf16)
                mixed_s[:, cols] = mixed_s[:, cols] * fade + dot(memory_ct, probs_s[rows, cols])
                score_pair(p, *operands, score_s)

    highest_s[0:1] = jnp.full((1, HQ), -3e38, f32)
    total_s[...] = jnp.zeros_like(total_s)
    mixed_s[...] = jnp.zeros_like(mixed_s)
    pl.run_scoped(attend_all, pltpu.VMEM((CHUNK, HQ), f32))
    highest_own = highest_s[0:1]
    total_own = jnp.sum(total_s[...], axis=0, keepdims=True)

    value_wt = attn_in[1, 2].astype(f32).T.astype(bf16)
    key_wt = attn_in[1, 1].astype(f32).T.astype(bf16)
    send_a[...] = project_heads(value_wt, mixed_s[...]).astype(bf16)
    send_t[:HEADS] = head_rows(highest_own)
    send_t[HEADS:] = head_rows(total_own)
    pl.semaphore_wait(barrier, len(peers))
    swap_a = pltpu.make_async_remote_copy(
        src_ref=send_a,
        dst_ref=recv_a,
        send_sem=link_sem.at[0],
        recv_sem=link_sem.at[1],
        device_id=partner,
        device_id_type=pl.DeviceIdType.MESH,
    )
    swap_t = pltpu.make_async_remote_copy(
        src_ref=send_t,
        dst_ref=recv_t,
        send_sem=link_sem.at[4],
        recv_sem=link_sem.at[5],
        device_id=partner,
        device_id_type=pl.DeviceIdType.MESH,
    )
    swap_a.start()
    swap_t.start()
    swap_a.wait()
    swap_t.wait()
    is_first = member == 0
    own, other = send_a[...].astype(f32), recv_a[...].astype(f32)
    left = jnp.where(is_first, own, other)
    right = jnp.where(is_first, other, own)
    own, other = send_t[...], recv_t[...]
    left_t = jnp.where(is_first, own, other)
    right_t = jnp.where(is_first, other, own)
    highest = jnp.maximum(left_t[:HEADS], right_t[:HEADS])
    fade_l = jnp.exp2(left_t[:HEADS] - highest)
    fade_r = jnp.exp2(right_t[:HEADS] - highest)
    total = left_t[HEADS:] * fade_l + right_t[HEADS:] * fade_r
    mixed_t = left * per_channel(fade_l / total) + right * per_channel(fade_r / total)
    log_total = head_line(highest + jnp.log2(total))
    own_share = jnp.exp2(highest_own - log_total)
    factor_s[...] = jnp.exp2(shifts_s[...] - log_total)
    attended_c = (mixed_t.T + bias[4:5]).astype(bf16)

    second_normed, second_rstd = norm_forward(first + dot(attended_c, attn_out[1]) + bias[5:6])
    second = second_normed * gain[1:2] + shift[1:2]
    ffn_input = second.astype(bf16)
    load_ffn[0].wait()
    load_ffn[1].wait()
    blocks = [(j // 4, slice(D * j, D * j + D), slice(j % 4 * D, j % 4 * D + D)) for j in range(FF // D)]
    hidden_bias = ffn_in_bias[...].astype(f32).reshape(1, FF)
    def feed_forward(gate_s):
        for k, cols, part in blocks:
            hidden = dot(ffn_input, ffn_in_s[k][:, part]) + hidden_bias[:, cols]
            half_gate = 0.5 + 0.5 * lax.erf(hidden * math.sqrt(0.5))
            active_s[k][:, part] = (hidden * half_gate).astype(bf16)
            gate_s[:, cols] = half_gate + hidden * jnp.exp(hidden * hidden * -0.5) * (
                1.0 / math.sqrt(2.0 * math.pi)
            )
        load_ffn[2].wait()
        third_normed, third_rstd = norm_forward(
            second
            + dot(active_s[0][...], ffn_out_s[:half])
            + dot(active_s[1][...], ffn_out_s[half:])
            + ffn_out_bias[...].astype(f32).reshape(1, D)
        )
        result_out[...] = (third_normed * gain[2:3] + shift[2:3])[:NQ].astype(bf16)
        grad_third, gain_grad_2, shift_grad_2 = norm_backward(
            pad_s[2], third_normed, third_rstd, gain[2:3]
        )
        grad_branch_f = grad_third.astype(bf16)
        for k, cols, part in blocks:
            grad_hidden = dot_nt(grad_branch_f, ffn_out_s[cols]) * gate_s[:, cols]
            slope_s[k][:, part] = grad_hidden.astype(bf16)
        return grad_third, gain_grad_2, shift_grad_2, grad_branch_f

    grad_third, gain_grad_2, shift_grad_2, grad_branch_f = pl.run_scoped(
        feed_forward, pltpu.VMEM((NP, FF), f32)
    )
    grad_second = grad_third + dot_nt(slope_s[0][...], ffn_in_s[0][...])
    grad_second += dot_nt(slope_s[1][...], ffn_in_s[1][...])
    grad_second_in, gain_grad_1, shift_grad_1 = norm_backward(
        grad_second, second_normed, second_rstd, gain[1:2]
    )
    grad_branch_c = grad_second_in.astype(bf16)
    ffn_input_t = second.T.astype(bf16)

    @pl.when(member == 0)
    def _():
        for k, cols, part in blocks:
            rows_f[cols] = dot(ffn_input_t, slope_s[k][:, part]).astype(bf16)

    @pl.when(member == 1)
    def _():
        for k, cols, part in blocks:
            rows_f[cols] = dot_tn(active_s[k][:, part], grad_branch_f).astype(bf16)

    is_first = member == 0

    clear_rest(rows_f, ROWS_F)
    sum_f.phases[0]()
    grad_attended_c = dot_nt(grad_branch_c, attn_out[1]).astype(bf16).astype(f32)
    small_s[:16] = jnp.concatenate(
        [row_total(slope_s[k][:, part]) for k, _, part in blocks]
        + [
            row_total(grad_branch_f),
            row_total(grad_branch_c),
            gain_grad_2,
            shift_grad_2,
            gain_grad_1,
            shift_grad_1,
            row_total(grad_attended_c),
            jnp.zeros((1, D), f32),
        ],
        axis=0,
    )

    store_result = pltpu.make_async_copy(result_out, result_hbm, load_sem.at[7])
    store_result.start()

    grad_attended_t = grad_attended_c.T
    grad_x = spread_rows(grad_attended_c)
    grad_v = dot(attn_in[1, 2], spread_cols(grad_attended_t))
    grad_vt[...] = grad_v.astype(bf16)
    inner = head_line(head_sums(grad_attended_t * mixed_t))
    value_rows[...] = dot((mixed_s[...] * own_share).astype(bf16), grad_x).astype(bf16)
    mixed_s[...] = jnp.zeros_like(mixed_s)

    queue_f = sum_f.phases[1:]
    queue_t = list(sum_t.phases)
    queue_k = list(sum_k.phases)

    def take(queue):
        if queue:
            queue.pop(0)()

    def at(i, steps):
        for step, queue in steps:
            pl.when(i == (step * chunks) // 32)(queue.pop(0))

    def slope_block(i):
        rows = pl.ds(pl.multiple_of(i * CHUNK, CHUNK), CHUNK)
        key_ct = key_in_s[rows].T
        memory_c = memory_s[rows]
        for p in range(4):
            cols = pair_cols(p)
            grad_probs = dot(memory_c, grad_vt[:, cols])
            probs = probs_s[rows, cols].astype(f32) * factor_s[pl.ds(i, 1), cols]
            probs_s[rows, cols] = probs.astype(bf16)
            grad_scores_s[rows, cols] = (probs * (grad_probs - inner[:, cols])).astype(bf16)
        mixed_s[...] += dot(key_ct, grad_scores_s[rows])

    @pl.loop(0, chunks // 2)
    def _(i):
        slope_block(i * 2)
        slope_block(i * 2 + 1)
        at(i, [(3, queue_f), (9, queue_f), (15, queue_f)])

    send_b[...] = (project_heads(key_wt, mixed_s[...]) * scale).astype(bf16)
    swap_b = pltpu.make_async_remote_copy(
        src_ref=send_b,
        dst_ref=recv_b,
        send_sem=link_sem.at[2],
        recv_sem=link_sem.at[3],
        device_id=partner,
        device_id_type=pl.DeviceIdType.MESH,
    )
    swap_b.start()
    query_x = spread_rows(query_c.astype(f32))
    rows_k[:D] = (dot(mixed_s[...].astype(bf16), query_x) * scale).astype(bf16)
    rows_k[D : 2 * D] = value_rows[...]
    out_grad_c = dot_tn(attended_c, grad_branch_c)
    rows_k[2 * D : 3 * D] = jnp.where(is_first, out_grad_c, 0.0).astype(bf16)
    clear_rest(rows_k, ROWS_K)
    clear_rest(rows_t, ROWS_T)
    take(queue_k)
    swap_b.wait()
    take(queue_f)
    take(queue_k)
    grad_query_c = (send_b[...].astype(f32) + recv_b[...].astype(f32)).T.astype(bf16)

    cross_pos_grad = dot_nt(grad_query_c, attn_in[1, 0])
    grad_first_in, gain_grad_0, shift_grad_0 = norm_backward(
        grad_second_in + cross_pos_grad, first_normed, first_rstd, gain[0:1]
    )
    grad_branch = grad_first_in.astype(bf16)
    grad_attended = dot_nt(grad_branch, attn_out[0]).astype(bf16).astype(f32)
    take(queue_k)
    grad_probs = dot(value_self, spread_cols(grad_attended.T))
    inner_self = jnp.sum(probs_self * grad_probs, axis=0, keepdims=True)
    grad_scores = (probs_self * (grad_probs - inner_self)).astype(bf16)
    key_t = key_self.astype(f32).T.astype(bf16)
    grad_query_s = (
        own_blocks([dot(key_t[pair_rows(p)], grad_scores[:, pair_cols(p)]) for p in range(4)]) * scale
    ).T.astype(bf16)
    grad_key_s = (dot(grad_scores, spread_rows(query_self.astype(f32))) * scale).astype(bf16)
    grad_value_s = dot(probs_self_b, spread_rows(grad_attended)).astype(bf16)
    grad_mixed_q = dot_nt(grad_query_s, attn_in[0, 0]) + dot_nt(grad_key_s, attn_in[0, 1])
    queries_grad_out[...] = (grad_first_in + grad_mixed_q + dot_nt(grad_value_s, attn_in[0, 2]))[
        :NQ
    ].astype(bf16)
    store_queries = pltpu.make_async_copy(queries_grad_out, queries_grad_hbm, load_sem.at[8])
    store_queries.start()
    small_s[16:] = jnp.concatenate(
        [
            row_total(grad_query_s),
            row_total(grad_value_s),
            row_total(grad_branch),
            row_total(grad_query_c),
            gain_grad_0,
            shift_grad_0,
            jnp.zeros((10, D), f32),
        ],
        axis=0,
    )
    @pl.when(member == 0)
    def _():
        rows_t[:D] = dot_tn(mixed_q, grad_query_s).astype(bf16)
        rows_t[D : 2 * D] = dot_tn(mixed_q, grad_key_s).astype(bf16)
        rows_t[2 * D : 3 * D] = dot_tn(queries_b, grad_value_s).astype(bf16)

    @pl.when(member == 1)
    def _():
        rows_t[:D] = dot_tn(cross_q, grad_query_c).astype(bf16)
        rows_t[D : 2 * D] = dot_tn(attended, grad_branch).astype(bf16)
        rows_t[ROW_POS:ROW_SMALL] = (grad_mixed_q + cross_pos_grad).astype(bf16)
        rows_t[ROW_SMALL : ROW_SMALL + 32] = small_s[...].astype(bf16)
        rows_t[ROW_SMALL + 32 : ROWS_T] = jnp.zeros((ROWS_T - ROW_SMALL - 32, D), bf16)

    take(queue_t)
    take(queue_k)
    take(queue_f)
    back_s[:HQ] = (dot_nt(query_x, attn_in[1, 1]) * scale).astype(bf16)
    back_s[HQ:] = dot_nt(spread_rows(grad_attended_c), attn_in[1, 2]).astype(bf16)

    def memory_block(i):
        rows = pl.ds(pl.multiple_of(i * CHUNK, CHUNK), CHUNK)
        both = jnp.concatenate([grad_scores_s[rows], probs_s[rows]], axis=1)
        memory_s[rows] = dot(both, back_s[...]).astype(bf16)
        pltpu.make_async_copy(memory_s.at[rows], memory_grad_hbm.at[0, rows], store_sem.at[i]).start()

    @pl.loop(0, chunks // 2)
    def _(i):
        memory_block(i * 2)
        memory_block(i * 2 + 1)
        at(
            i,
            [
                (3, queue_t),
                (4, queue_k),
                (7, queue_t),
                (8, queue_k),
                (9, queue_f),
                (11, queue_t),
                (12, queue_k),
                (15, queue_t),
            ],
        )

    while queue_f:
        take(queue_f)
    stores = [
        pltpu.make_async_copy(whole, target, load_sem.at[4 + k])
        for k, (whole, target) in enumerate(
            (
                (whole_f, whole_f_hbm),
                (whole_t, whole_t_hbm),
                (whole_k, whole_k_hbm),
            )
        )
    ]
    stores[0].start()
    while queue_t or queue_k:
        take(queue_t)
        take(queue_k)
    for store in stores[1:]:
        store.start()

    @pl.loop(0, chunks)
    def _(i):
        rows = pl.ds(pl.multiple_of(i * CHUNK, CHUNK), CHUNK)
        pltpu.make_async_copy(memory_s.at[rows], memory_grad_hbm.at[0, rows], store_sem.at[i]).wait()

    for store in [*stores, store_result, store_queries]:
        store.wait()


def finish_kernel(
    result_in,
    queries_grad_in,
    memory_grad_in,
    whole_f_hbm,
    whole_t_hbm,
    whole_k_hbm,
    result_hbm,
    queries_grad_hbm,
    memory_grad,
    attn_in_hbm,
    attn_out_hbm,
    attn_bias_hbm,
    ffn_in_hbm,
    ffn_in_bias_hbm,
    ffn_out_hbm,
    ffn_out_bias_hbm,
    norm_gain_hbm,
    norm_bias_hbm,
    query_pos_hbm,
    moved,
    whole_f,
    whole_t,
    whole_k,
    result,
    queries_grad,
    attn_in_grad,
    attn_out_grad,
    attn_bias_grad,
    ffn_in_grad,
    ffn_in_bias_grad,
    ffn_out_grad,
    ffn_out_bias_grad,
    norm_gain_grad,
    norm_bias_grad,
    query_pos_grad,
    in_sem,
    out_sem,
    sum_sem,
    grad_sem,
):
    pieces = in_sem.shape[0]
    piece = moved.shape[0] // pieces

    def fetch(j):
        rows = pl.ds(piece * j, piece)
        return pltpu.make_async_copy(memory_grad_in.at[0, rows], moved.at[rows], in_sem.at[j])

    def write(j):
        rows = pl.ds(piece * j, piece)
        return pltpu.make_async_copy(moved.at[rows], memory_grad.at[0, rows], out_sem.at[j])

    sums = [
        (whole_t_hbm, whole_t),
        (whole_k_hbm, whole_k),
        (whole_f_hbm, whole_f),
        (result_in, result),
        (queries_grad_in, queries_grad),
    ]
    loads = [pltpu.make_async_copy(*pair, sum_sem.at[j]) for j, pair in enumerate(sums)]
    for load in loads:
        load.start()
    for j in range(pieces):
        fetch(j).start()
    blocks = FF // D
    stores = []

    def store(source, target):
        stores.append(pltpu.make_async_copy(source, target, grad_sem.at[len(stores)]))
        stores[-1].start()

    loads[0].wait()
    loads[1].wait()
    for j in range(3):
        attn_in_grad[0, j] = whole_t[0, D * j : D * j + D].astype(f32)
    attn_in_grad[1, 0] = whole_t[1, :D].astype(f32)
    attn_in_grad[1, 1] = whole_k[:D].astype(f32)
    attn_in_grad[1, 2] = whole_k[D : 2 * D].astype(f32)
    store(attn_in_grad, attn_in_hbm)
    attn_out_grad[0] = whole_t[1, D : 2 * D].astype(f32)
    attn_out_grad[1] = whole_k[2 * D : 3 * D].astype(f32)
    store(attn_out_grad, attn_out_hbm)
    loads[2].wait()
    for k in range(2):
        half = slice(FF // 2 * k, FF // 2 * (k + 1))
        ffn_out_grad[half] = whole_f[1, half].astype(f32)
        store(ffn_out_grad.at[half], ffn_out_hbm.at[half])
    for k in range(2):
        half = slice(FF // 2 * k, FF // 2 * (k + 1))
        for j in range(blocks // 2 * k, blocks // 2 * (k + 1)):
            at = slice(D * j, D * j + D)
            ffn_in_grad[:, at] = whole_f[0, at].astype(f32)
        store(ffn_in_grad.at[:, half], ffn_in_hbm.at[:, half])
    for j in range(pieces):
        fetch(j).wait()
        write(j).start()
    loads[3].wait()
    store(result, result_hbm.at[0])
    loads[4].wait()
    store(queries_grad, queries_grad_hbm.at[0])
    query_pos_grad[...] = whole_t[1, ROW_POS:ROW_SMALL].astype(f32)[:NQ]
    store(query_pos_grad, query_pos_hbm)
    small = whole_t[1, ROW_SMALL : ROW_SMALL + 32].astype(f32)
    ffn_in_bias_grad[...] = jnp.concatenate([small[j : j + 1] for j in range(blocks)], axis=1)
    store(ffn_in_bias_grad, ffn_in_bias_hbm)
    ffn_out_bias_grad[...] = small[8:9]
    store(ffn_out_bias_grad, ffn_out_bias_hbm)
    for j, (own, cross) in enumerate(((16, 19), (17, 14), (18, 9))):
        attn_bias_grad[j, 0:1] = small[own : own + 1]
        attn_bias_grad[j, 1:2] = small[cross : cross + 1]
    store(attn_bias_grad, attn_bias_hbm)
    for j, (gain, shift) in enumerate(((20, 21), (12, 13), (10, 11))):
        norm_gain_grad[j : j + 1] = small[gain : gain + 1]
        norm_bias_grad[j : j + 1] = small[shift : shift + 1]
    store(norm_gain_grad, norm_gain_hbm)
    store(norm_bias_grad, norm_bias_hbm)
    for j in range(pieces):
        write(j).wait()
    for copy in stores:
        copy.wait()


def body(
    pages,
    queries,
    memory,
    quarter_turns,
    token_order,
    lengths,
    attn_in,
    attn_out,
    attn_bias,
    ffn_in,
    ffn_in_bias,
    ffn_out,
    ffn_out_bias,
    norm_gain,
    norm_bias,
    query_pos,
    out_grad,
):
    tokens = memory.shape[1]
    chunks = tokens // CHUNK
    groups_f, groups_t, groups_k = sum_groups(pages)
    summed = [
        (padded(ROWS_F, pages), groups_f),
        (padded(ROWS_T, pages), groups_t),
        (padded(ROWS_K, 2 * pages), groups_k),
    ]
    whole_shapes = [(2, rows, D) for rows, _ in summed[:2]] + [(summed[2][0], D)]
    sum_buffers = []
    for (rows, groups), shape in zip(summed, whole_shapes):
        landing = PageSum.landing_rows(pages, groups, rows)
        own_rows = [(rows, D)] if groups is groups_f else []
        sum_buffers += [pltpu.VMEM(each, bf16) for each in (*own_rows, (landing, D), shape)]
    copies = 32
    vmem = pl.BlockSpec(memory_space=pltpu.VMEM)
    smem = pl.BlockSpec(memory_space=pltpu.SMEM)
    anywhere = pl.BlockSpec(memory_space=pl.ANY)
    parts = pl.pallas_call(
        functools.partial(layer_kernel, tokens, pages),
        out_shape=[
            jax.ShapeDtypeStruct((NQ, D), bf16),
            jax.ShapeDtypeStruct((NQ, D), bf16),
            jax.ShapeDtypeStruct((1, tokens, D), bf16),
            *(jax.ShapeDtypeStruct(shape, bf16) for shape in whole_shapes),
        ],
        in_specs=[
            vmem,
            anywhere,
            smem,
            vmem,
            smem,
            vmem,
            vmem,
            vmem,
            anywhere,
            vmem,
            anywhere,
            vmem,
            vmem,
            vmem,
            vmem,
            vmem,
            vmem,
        ],
        out_specs=[anywhere] * 6,
        scratch_shapes=[
            pltpu.VMEM((tokens, D), bf16),
            pltpu.VMEM((tokens, D), bf16),
            pltpu.VMEM((tokens, HQ), bf16),
            pltpu.VMEM((tokens, HQ), bf16),
            pltpu.VMEM((1, tokens), f32),
            pltpu.VMEM((D, HQ), bf16),
            pltpu.VMEM((D, D), bf16),
            pltpu.VMEM((4 * SIDE, D), bf16),
            pltpu.VMEM((8, HQ), f32),
            pltpu.VMEM((8, HQ), f32),
            pltpu.VMEM((chunks, HQ), f32),
            pltpu.VMEM((chunks, HQ), f32),
            pltpu.VMEM((8, HQ), f32),
            pltpu.VMEM((D, HQ), f32),
            pltpu.VMEM((3, NP, D), f32),
            pltpu.VMEM((NQ, D), bf16),
            pltpu.VMEM((NQ, D), bf16),
            pltpu.VMEM((D, NP), bf16),
            pltpu.VMEM((D, NP), bf16),
            pltpu.VMEM((2 * HEADS, NP), f32),
            pltpu.VMEM((2 * HEADS, NP), f32),
            pltpu.VMEM((D, NP), bf16),
            pltpu.VMEM((D, NP), bf16),
            pltpu.VMEM((32, D), f32),
            *sum_buffers,
            pltpu.SemaphoreType.DMA((9,)),
            pltpu.SemaphoreType.DMA((chunks,)),
            pltpu.SemaphoreType.DMA((6,)),
            *[pltpu.SemaphoreType.DMA((copies,))] * 6,
        ],
        compiler_params=pltpu.CompilerParams(
            collective_id=0, has_side_effects=True, vmem_limit_bytes=127 * 512 * 1024
        ),
        cost_estimate=pl.CostEstimate(
            flops=2 * 8 * tokens * HQ * D, bytes_accessed=20 << 20, transcendentals=tokens * HQ
        ),
        name="decoder_layer",
    )(
        queries,
        memory,
        quarter_turns,
        token_order,
        lengths,
        attn_in,
        attn_out,
        attn_bias.transpose(1, 0, 2),
        ffn_in,
        ffn_in_bias,
        ffn_out,
        ffn_out_bias,
        norm_gain,
        norm_bias,
        query_pos,
        out_grad,
        jnp.asarray(position_table()),
    )
    outs = pl.pallas_call(
        finish_kernel,
        out_shape=[
            jax.ShapeDtypeStruct((1, NQ, D), bf16),
            jax.ShapeDtypeStruct((1, NQ, D), bf16),
            jax.ShapeDtypeStruct((1, tokens, D), bf16),
            jax.ShapeDtypeStruct((2, 3, D, D), f32),
            jax.ShapeDtypeStruct((2, D, D), f32),
            jax.ShapeDtypeStruct((3, 2, D), f32),
            jax.ShapeDtypeStruct((D, FF), f32),
            jax.ShapeDtypeStruct((1, FF), f32),
            jax.ShapeDtypeStruct((FF, D), f32),
            jax.ShapeDtypeStruct((1, D), f32),
            jax.ShapeDtypeStruct((3, D), f32),
            jax.ShapeDtypeStruct((3, D), f32),
            jax.ShapeDtypeStruct((NQ, D), f32),
        ],
        in_specs=[anywhere] * 6,
        out_specs=[anywhere] * 13,
        scratch_shapes=[
            pltpu.VMEM((tokens, D), bf16),
            *(pltpu.VMEM(shape, bf16) for shape in whole_shapes),
            pltpu.VMEM((NQ, D), bf16),
            pltpu.VMEM((NQ, D), bf16),
            pltpu.VMEM((2, 3, D, D), f32),
            pltpu.VMEM((2, D, D), f32),
            pltpu.VMEM((3, 2, D), f32),
            pltpu.VMEM((D, FF), f32),
            pltpu.VMEM((1, FF), f32),
            pltpu.VMEM((FF, D), f32),
            pltpu.VMEM((1, D), f32),
            pltpu.VMEM((3, D), f32),
            pltpu.VMEM((3, D), f32),
            pltpu.VMEM((NQ, D), f32),
            pltpu.SemaphoreType.DMA((8,)),
            pltpu.SemaphoreType.DMA((8,)),
            pltpu.SemaphoreType.DMA((5,)),
            pltpu.SemaphoreType.DMA((14,)),
        ],
        compiler_params=pltpu.CompilerParams(vmem_limit_bytes=62 * 1024 * 1024),
        name="write_outputs",
    )(*parts)
    return (
        *outs[:5],
        outs[5].transpose(1, 0, 2),
        outs[6],
        outs[7].reshape(FF),
        outs[8],
        outs[9].reshape(D),
        *outs[10:],
    )


def solution(mesh):
    in_specs = (
        P("dp", None, None),
        P("dp", "blk", None),
        P("dp"),
        P("dp", "blk"),
        P("dp"),
        P(),
        P(),
        P(),
        P(),
        P(),
        P(),
        P(),
        P(),
        P(),
        P(),
        P("dp", None, None),
    )
    out_specs = (
        P("dp", None, None),
        P("dp", None, None),
        P("dp", "blk", None),
        P(),
        P(),
        P(),
        P(),
        P(),
        P(),
        P(),
        P(),
        P(),
        P(),
    )
    layer = functools.partial(body, mesh.shape["dp"])
    return jax.shard_map(layer, mesh=mesh, in_specs=in_specs, out_specs=out_specs, check_vma=False)
```

```python
import functools
import math

import jax
import jax.numpy as jnp
import numpy as np
from jax import lax
from jax.experimental import pallas as pl
from jax.experimental.pallas import tpu as pltpu
from jax.sharding import PartitionSpec as P

D = 256
HEADS = 8
HD = D // HEADS
SIDE = 128
NQ = 125
NP = 128
HQ = HEADS * NP
PAIR = 2 * NP
FF = 2048
CHUNK = 1024

masked_score = -1e30
norm_eps = 1e-05
scale = 1.0 / math.sqrt(HD)
log2e = math.log2(math.e)

bf16 = jnp.bfloat16
f32 = jnp.float32

ROWS_F = FF
ROW_POS = 2 * D
ROW_SMALL = 2 * D + NP
ROWS_T = 3 * D
ROWS_K = 3 * D
TILE = 16


def axes_of(pages):
    axes = {"core": (2, 1), "y": (2, 2)}
    stride = 4
    while stride < pages:
        radix = 4 if pages // stride % 4 == 0 else 2
        axes["z%d" % (len(axes) - 2)] = (radix, stride)
        stride *= radix
    axes["x"] = (2, 0)
    return axes


def far_axes(pages):
    return [(name,) for name in axes_of(pages) if name.startswith("z")]


def sum_groups(pages):
    far = far_axes(pages)
    return [("core",), ("y",), *far], [("core", "y"), *far], [("core",), ("x",), ("y",), *far]


def padded(rows, pages):
    unit = TILE * pages
    return (rows + unit - 1) // unit * unit


def position_table():
    half = D // 2
    channel = np.arange(half)
    inverse = np.exp((channel // 2).astype(np.float32) * np.float32(-2.0 * math.log(10000.0) / half))
    angle = (np.arange(SIDE, dtype=np.float32) + 1.0) * np.float32(2.0 * math.pi / SIDE)
    angle = angle[:, None] * inverse
    return np.where(channel % 2 == 0, np.sin(angle), np.cos(angle)).astype(np.float32)


def dot(a, b):
    return jnp.dot(a, b, preferred_element_type=f32)


def dot_nt(a, b):
    return lax.dot_general(a, b, (((1,), (1,)), ((), ())), preferred_element_type=f32)


def dot_tn(a, b):
    return lax.dot_general(a, b, (((0,), (0,)), ((), ())), preferred_element_type=f32)


def row_total(values):
    return jnp.sum(values.astype(f32), axis=0, keepdims=True)


def norm_forward(values):
    average = jnp.mean(values, axis=-1, keepdims=True)
    centred = values - average
    variance = jnp.mean(centred * centred, axis=-1, keepdims=True)
    rstd = lax.rsqrt(variance + norm_eps)
    return centred * rstd, rstd


def norm_backward(grad, normed, rstd, gain):
    grad_normed = grad * gain
    first = jnp.mean(grad_normed, axis=-1, keepdims=True)
    second = jnp.mean(grad_normed * normed, axis=-1, keepdims=True)
    grad_in = rstd * (grad_normed - first - normed * second)
    return grad_in, row_total(grad * normed), row_total(grad)


def spread_rows(rows):
    head = lax.broadcasted_iota(jnp.int32, (NP, D), 1) // HD
    return jnp.concatenate(
        [jnp.where(head == h, rows, 0.0) for h in range(HEADS)], axis=0
    ).astype(bf16)


def spread_cols(cols):
    head = lax.broadcasted_iota(jnp.int32, (D, NP), 0) // HD
    return jnp.concatenate(
        [jnp.where(head == h, cols, 0.0) for h in range(HEADS)], axis=1
    ).astype(bf16)


def project_heads(weight_t, sums):
    high = sums.astype(bf16)
    low = (sums - high.astype(f32)).astype(bf16)
    return own_blocks(
        [
            dot(weight_t[pair_rows(p)], high[:, pair_cols(p)])
            + dot(weight_t[pair_rows(p)], low[:, pair_cols(p)])
            for p in range(4)
        ]
    )


def own_blocks(pairs):
    parts = []
    for pair in pairs:
        parts += [pair[:HD, :NP], pair[HD:, NP:]]
    return jnp.concatenate(parts, axis=0)


def head_rows(row):
    return jnp.concatenate([row[:, NP * h : NP * h + NP] for h in range(HEADS)], axis=0)


def head_line(rows):
    return jnp.concatenate([rows[h : h + 1] for h in range(HEADS)], axis=1)


def per_channel(rows):
    return jnp.concatenate(
        [jnp.broadcast_to(rows[h : h + 1], (HD, NP)) for h in range(HEADS)], axis=0
    )


def head_sums(cols):
    return jnp.concatenate(
        [jnp.sum(cols[HD * h : HD * h + HD], axis=0, keepdims=True) for h in range(HEADS)], axis=0
    )


def pair_cols(p):
    return slice(PAIR * p, PAIR * p + PAIR)


def pair_rows(p):
    return slice(2 * HD * p, 2 * HD * p + 2 * HD)


class Place:
    def __init__(self, pages):
        self.axes = axes_of(pages)
        self.page = lax.axis_index("dp")
        self.member = lax.axis_index("blk")
        self.digit = {
            name: self.member if name == "x" else lax.rem(self.page // stride, radix)
            for name, (radix, stride) in self.axes.items()
        }

    def size(self, group):
        return math.prod(self.axes[name][0] for name in group)

    def index(self, group):
        index = 0
        for name in group:
            index = index * self.axes[name][0] + self.digit[name]
        return index

    def peer(self, group, hop):
        index = lax.rem(self.index(group) + hop, self.size(group))
        page, member, rest = self.page, self.member, index
        for name in reversed(group):
            radix, stride = self.axes[name]
            digit = lax.rem(rest, radix)
            rest = rest // radix
            if name == "x":
                member = digit
            else:
                page = page + (digit - self.digit[name]) * stride
        return (page, member), index


class PageSum:
    def __init__(self, place, groups, back, rows, landing, whole, sent, arrived):
        self.place, self.groups, self.back = place, groups, back
        self.rows, self.landing, self.whole = rows, landing, whole
        self.sent, self.arrived = sent, arrived
        self.slots = 0
        self.extents = [rows.shape[0]]
        self.bases = [0]
        self.landings = []
        at = 0
        for group in groups:
            size = place.size(group)
            extent = self.extents[-1] // size
            self.landings.append(at)
            at += (size - 1) * extent
            self.bases.append(pl.multiple_of(self.bases[-1] + place.index(group) * extent, TILE))
            self.extents.append(extent)
        last = len(groups)
        moves = [self.scatter_moves(s) for s in range(last)]
        near = {"all": 0, "across": 1, "sides": 2}[back]
        moves += [self.gather_moves(s) for s in range(last - 1, near - 1, -1)]
        if back == "sides":
            moves += [self.side_moves(), self.corner_moves(), self.core_moves()]
        elif back == "across":
            moves += [self.across_moves(), self.core_moves()]
        self.phases = [functools.partial(self.step, moves, k) for k in range(len(moves) + 1)]

    @staticmethod
    def landing_rows(pages, groups, rows):
        axes = axes_of(pages)
        total, extent = 0, rows
        for group in groups:
            size = math.prod(axes[name][0] for name in group)
            extent //= size
            total += (size - 1) * extent
        return total

    def step(self, moves, k):
        last = len(self.groups)
        if k > 0:
            for move in moves[k - 1]:
                self.copy(*move).wait()
        if 0 < k <= last:
            total = self.scatter_sum(k - 1)
            region = pl.ds(self.bases[k], self.extents[k])
            if k < last:
                self.rows[region] = total
            elif len(self.whole.shape) == 3:
                self.whole[self.place.member, region] = total
            else:
                self.whole[region] = total
        if k < len(moves):
            for move in moves[k]:
                self.copy(*move).start()

    def copy(self, slot, source, target, device):
        return pltpu.make_async_remote_copy(
            src_ref=source(),
            dst_ref=target(),
            send_sem=self.sent.at[slot],
            recv_sem=self.arrived.at[slot],
            device_id=device,
            device_id_type=pl.DeviceIdType.MESH,
        )

    def new_slot(self):
        self.slots += 1
        return self.slots - 1

    def same(self, device, view):
        return (self.new_slot(), view, view, device)

    def scatter_moves(self, step):
        group = self.groups[step]
        extent = self.extents[step + 1]
        moves = []
        for hop in range(1, self.place.size(group)):
            device, other = self.place.peer(group, hop)
            start = pl.multiple_of(self.bases[step] + other * extent, TILE)
            landing = self.landings[step] + (hop - 1) * extent
            moves.append(
                (
                    self.new_slot(),
                    functools.partial(self.part, self.rows, start, extent),
                    functools.partial(self.part, self.landing, landing, extent),
                    device,
                )
            )
        return moves

    @staticmethod
    def part(ref, start, extent):
        return ref.at[pl.ds(start, extent)]

    def half(self, member, start, extent):
        if len(self.whole.shape) == 3:
            return self.whole.at[member, pl.ds(start, extent)]
        return self.whole.at[pl.ds(start, extent)]

    def scatter_sum(self, step):
        extent = self.extents[step + 1]
        total = self.rows[pl.ds(self.bases[step + 1], extent)].astype(f32)
        for hop in range(1, self.place.size(self.groups[step])):
            landing = self.landings[step] + (hop - 1) * extent
            total = total + self.landing[pl.ds(landing, extent)].astype(f32)
        return total.astype(bf16)

    def gather_moves(self, step):
        group = self.groups[step]
        view = functools.partial(self.half, self.place.member, self.bases[step + 1], self.extents[step + 1])
        return [
            self.same(self.place.peer(group, hop)[0], view) for hop in range(1, self.place.size(group))
        ]

    def own_quarter(self):
        step = 2 if len(self.groups[0]) == 1 else 1
        return self.bases[step], self.extents[step]

    def side_moves(self):
        view = functools.partial(self.half, self.place.member, *self.own_quarter())
        return [self.same(self.place.peer((name,), 1)[0], view) for name in ("y", "x")]

    def corner_moves(self):
        base, extent = self.own_quarter()
        other = pl.multiple_of(base + (1 - 2 * self.place.digit["y"]) * extent, TILE)
        view = functools.partial(self.half, self.place.member, other, extent)
        return [self.same(self.place.peer(("x",), 1)[0], view)]

    def across_moves(self):
        view = functools.partial(self.half, self.place.member, *self.own_quarter())
        return [self.same(self.place.peer(("x", "y"), hop)[0], view) for hop in range(1, 4)]

    def core_moves(self):
        extent = self.extents[0] // 2
        start = pl.multiple_of(self.place.digit["core"] * extent, TILE)
        device, _ = self.place.peer(("core",), 1)
        return [self.same(device, functools.partial(self.half, m, start, extent)) for m in range(2)]


def clear_rest(ref, used):
    if ref.shape[0] > used:
        ref[used:] = jnp.zeros((ref.shape[0] - used, D), ref.dtype)


def layer_kernel(
    tokens,
    pages,
    queries_in,
    memory_hbm,
    turns_in,
    order_in,
    lengths_in,
    attn_in,
    attn_out,
    attn_bias,
    ffn_in_hbm,
    ffn_in_bias,
    ffn_out_hbm,
    ffn_out_bias,
    norm_gain,
    norm_bias,
    pos_in,
    out_grad_in,
    table_in,
    result_hbm,
    queries_grad_hbm,
    memory_grad_hbm,
    whole_f_hbm,
    whole_t_hbm,
    whole_k_hbm,
    memory_s,
    key_in_s,
    probs_s,
    grad_scores_s,
    code_s,
    query_kt,
    value_rows,
    table_s,
    top_s,
    highest_s,
    shifts_s,
    factor_s,
    total_s,
    mixed_s,
    pad_s,
    result_out,
    queries_grad_out,
    send_a,
    recv_a,
    send_t,
    recv_t,
    send_b,
    recv_b,
    small_s,
    rows_f,
    landing_f,
    whole_f,
    landing_t,
    whole_t,
    landing_k,
    whole_k,
    load_sem,
    store_sem,
    link_sem,
    sent_f,
    arrived_f,
    sent_t,
    arrived_t,
    sent_k,
    arrived_k,
):
    member = lax.axis_index("blk")
    partner = (lax.axis_index("dp"), 1 - member)
    chunks = tokens // CHUNK

    place = Place(pages)
    grad_vt = query_kt
    back_s = key_in_s.at[: 2 * HQ]
    first_t = 2 * HQ + padded(ROWS_K, 2 * pages)
    rows_k = key_in_s.at[2 * HQ : first_t]
    rows_t = key_in_s.at[first_t : first_t + padded(ROWS_T, pages)]
    groups_f, groups_t, groups_k = sum_groups(pages)
    sum_f = PageSum(place, groups_f, "sides", rows_f, landing_f, whole_f, sent_f, arrived_f)
    sum_t = PageSum(place, groups_t, "across", rows_t, landing_t, whole_t, sent_t, arrived_t)
    sum_k = PageSum(place, groups_k, "all", rows_k, landing_k, whole_k, sent_k, arrived_k)

    barrier = pltpu.get_barrier_semaphore()
    peers = [
        place.peer(group, hop)[0]
        for group in [("x", "core", "y"), *far_axes(pages)]
        for hop in range(1, place.size(group))
    ]
    for peer in peers:
        pl.semaphore_signal(barrier, inc=1, device_id=peer, device_id_type=pl.DeviceIdType.MESH)

    load_memory = pltpu.make_async_copy(memory_hbm.at[0], memory_s, load_sem.at[0])
    half = FF // 2
    ffn_in_s = [grad_scores_s.at[D * k : D * k + D] for k in range(2)]
    ffn_out_s = grad_scores_s.at[2 * D : 2 * D + FF, :D]
    free = 2 * D + FF
    active_s = [grad_scores_s.at[free + NP * k : free + NP * k + NP] for k in range(2)]
    slope_s = [grad_scores_s.at[free + NP * k : free + NP * k + NP] for k in range(2, 4)]
    load_ffn = [
        pltpu.make_async_copy(ffn_in_hbm.at[:, half * k : half * k + half], ffn_in_s[k], load_sem.at[1 + k])
        for k in range(2)
    ]
    load_ffn.append(pltpu.make_async_copy(ffn_out_hbm, ffn_out_s, load_sem.at[3]))
    load_memory.start()
    for load in load_ffn:
        load.start()

    pairs = [attn_bias[j].astype(f32) for j in range(3)]
    bias = jnp.concatenate([pair[k : k + 1] for k in range(2) for pair in pairs], axis=0)
    gain = norm_gain[...].astype(f32)
    shift = norm_bias[...].astype(f32)

    def each_two(block):
        @pl.loop(0, chunks // 2)
        def _(j):
            block(j * 2)
            block(j * 2 + 1)

    order = order_in[...]
    turn = turns_in[0]
    row_at = order >> 7
    col_at = order & 127
    top = SIDE - 1
    row_new = jnp.where(
        turn == 0, row_at, jnp.where(turn == 1, col_at, jnp.where(turn == 2, top - row_at, top - col_at))
    )
    col_new = jnp.where(
        turn == 0, col_at, jnp.where(turn == 1, top - row_at, jnp.where(turn == 2, top - col_at, row_at))
    )
    past = jnp.where(order < lengths_in[0], 0, SIDE * SIDE)
    code_s[...] = (row_new * SIDE + col_new + past).astype(f32)

    pad_s[...] = jnp.zeros_like(pad_s)
    pad_s[0, :NQ] = queries_in[0].astype(f32)
    pad_s[1, :NQ] = pos_in[...].astype(f32)
    pad_s[2, :NQ] = out_grad_in[0].astype(f32)
    queries_f = pad_s[0]
    pos_f = pad_s[1]
    queries_b = queries_f.astype(bf16)
    mixed_q = (queries_f + pos_f).astype(bf16)
    query_self = (dot(mixed_q, attn_in[0, 0]) + bias[0:1]).astype(bf16)
    key_self = dot(mixed_q, attn_in[0, 1]).astype(bf16)
    value_self = (dot(queries_b, attn_in[0, 2]) + bias[1:2]).astype(bf16)
    scores = dot(key_self, spread_cols(query_self.astype(f32).T)) * scale
    own_key = lax.broadcasted_iota(jnp.int32, (NP, HQ), 0) < NQ
    scores = jnp.where(own_key, scores, masked_score)
    raised = jnp.exp(scores - jnp.max(scores, axis=0, keepdims=True))
    probs_self = raised / jnp.sum(raised, axis=0, keepdims=True)
    probs_self_b = probs_self.astype(bf16)
    value_t = value_self.astype(f32).T.astype(bf16)
    attended = own_blocks(
        [dot(value_t[pair_rows(p)], probs_self_b[:, pair_cols(p)]) for p in range(4)]
    ).T.astype(bf16)
    first_normed, first_rstd = norm_forward(queries_f + dot(attended, attn_out[0]) + bias[2:3])
    first = first_normed * gain[0:1] + shift[0:1]
    cross_q = (first + pos_f).astype(bf16)
    query_c = (dot(cross_q, attn_in[1, 0]) + bias[3:4]).astype(bf16)
    query_k = dot(attn_in[1, 1], spread_cols(query_c.astype(f32).T))
    query_kt[...] = (query_k * (scale * log2e)).astype(bf16)
    table = table_in[...]
    nothing = jnp.zeros((SIDE, D // 2), f32)
    table = jnp.concatenate(
        [jnp.concatenate([table, nothing], axis=1), jnp.concatenate([nothing, table], axis=1)], axis=0
    )
    table_high = table.astype(bf16)
    table_s[: 2 * SIDE] = table_high
    table_s[2 * SIDE :] = (table - table_high.astype(f32)).astype(bf16)

    load_memory.wait()
    def mask_view(i):
        side, place = i // (chunks // 2), lax.rem(i, chunks // 2)
        return grad_scores_s.at[
            pl.ds(pl.multiple_of(tokens // 2 + place * CHUNK, CHUNK), CHUNK),
            pl.ds(pl.multiple_of(side * NP, NP), NP),
        ]

    lane = lax.broadcasted_iota(jnp.int32, (CHUNK, NP), 1)

    @each_two
    def _(i):
        rows = pl.ds(pl.multiple_of(i * CHUNK, CHUNK), CHUNK)
        line = code_s[:, rows]
        code = jnp.concatenate(
            [
                jnp.broadcast_to(line[:, NP * j : NP * j + NP], (NP, NP)).T
                for j in range(CHUNK // NP)
            ],
            axis=0,
        ).astype(jnp.int32)
        row_hot = jnp.where(((code >> 7) & 127) == lane, 1.0, 0.0).astype(bf16)
        col_hot = jnp.where((code & 127) == lane, 1.0, 0.0).astype(bf16)
        hot = jnp.concatenate([row_hot, col_hot, row_hot, col_hot], axis=1)
        masked = jnp.where(code < SIDE * SIDE, 0.0, masked_score)
        mask_view(i)[...] = masked.astype(bf16)
        key_in_s[rows] = (memory_s[rows].astype(f32) + dot(hot, table_s[...])).astype(bf16)

    def score_pair(p, key_in, mask, score_s):
        cols = pair_cols(p)
        part = dot(key_in, query_kt[:, cols]) + mask
        score_s[:, cols] = part
        top_s[:, cols] = jnp.max(part.reshape(CHUNK // 8, 8, PAIR), axis=0)

    def score_operands(i):
        rows = pl.ds(pl.multiple_of(i * CHUNK, CHUNK), CHUNK)
        mask = mask_view(i)[...].astype(f32)
        return key_in_s[rows], jnp.concatenate([mask, mask], axis=1)

    def attend_all(score_s):
        operands = score_operands(0)
        for p in range(4):
            score_pair(p, *operands, score_s)

        @pl.loop(0, chunks)
        def _(i):
            rows = pl.ds(pl.multiple_of(i * CHUNK, CHUNK), CHUNK)
            memory_ct = memory_s[rows].T
            operands = score_operands(jnp.minimum(i + 1, chunks - 1))
            for p in range(4):
                cols = pair_cols(p)
                before = highest_s[0:1, cols]
                highest = jnp.maximum(before, jnp.max(top_s[:, cols], axis=0, keepdims=True))
                highest_s[0:1, cols] = highest
                shifts_s[pl.ds(i, 1), cols] = highest
                fade = jnp.exp2(before - highest)
                raised = jnp.exp2(score_s[:, cols] - highest)
                sums = jnp.sum(raised.reshape(CHUNK // 8, 8, PAIR), axis=0)
                total_s[:, cols] = total_s[:, cols] * fade + sums
                probs_s[rows, cols] = raised.astype(bf16)
                mixed_s[:, cols] = mixed_s[:, cols] * fade + dot(memory_ct, probs_s[rows, cols])
                score_pair(p, *operands, score_s)

    highest_s[0:1] = jnp.full((1, HQ), -3e38, f32)
    total_s[...] = jnp.zeros_like(total_s)
    mixed_s[...] = jnp.zeros_like(mixed_s)
    pl.run_scoped(attend_all, pltpu.VMEM((CHUNK, HQ), f32))
    highest_own = highest_s[0:1]
    total_own = jnp.sum(total_s[...], axis=0, keepdims=True)

    value_wt = attn_in[1, 2].astype(f32).T.astype(bf16)
    key_wt = attn_in[1, 1].astype(f32).T.astype(bf16)
    send_a[...] = project_heads(value_wt, mixed_s[...]).astype(bf16)
    send_t[:HEADS] = head_rows(highest_own)
    send_t[HEADS:] = head_rows(total_own)
    pl.semaphore_wait(barrier, len(peers))
    swap_a = pltpu.make_async_remote_copy(
        src_ref=send_a,
        dst_ref=recv_a,
        send_sem=link_sem.at[0],
        recv_sem=link_sem.at[1],
        device_id=partner,
        device_id_type=pl.DeviceIdType.MESH,
    )
    swap_t = pltpu.make_async_remote_copy(
        src_ref=send_t,
        dst_ref=recv_t,
        send_sem=link_sem.at[4],
        recv_sem=link_sem.at[5],
        device_id=partner,
        device_id_type=pl.DeviceIdType.MESH,
    )
    swap_a.start()
    swap_t.start()
    swap_a.wait()
    swap_t.wait()
    is_first = member == 0
    own, other = send_a[...].astype(f32), recv_a[...].astype(f32)
    left = jnp.where(is_first, own, other)
    right = jnp.where(is_first, other, own)
    own, other = send_t[...], recv_t[...]
    left_t = jnp.where(is_first, own, other)
    right_t = jnp.where(is_first, other, own)
    highest = jnp.maximum(left_t[:HEADS], right_t[:HEADS])
    fade_l = jnp.exp2(left_t[:HEADS] - highest)
    fade_r = jnp.exp2(right_t[:HEADS] - highest)
    total = left_t[HEADS:] * fade_l + right_t[HEADS:] * fade_r
    mixed_t = left * per_channel(fade_l / total) + right * per_channel(fade_r / total)
    log_total = head_line(highest + jnp.log2(total))
    own_share = jnp.exp2(highest_own - log_total)
    factor_s[...] = jnp.exp2(shifts_s[...] - log_total)
    attended_c = (mixed_t.T + bias[4:5]).astype(bf16)

    second_normed, second_rstd = norm_forward(first + dot(attended_c, attn_out[1]) + bias[5:6])
    second = second_normed * gain[1:2] + shift[1:2]
    ffn_input = second.astype(bf16)
    load_ffn[0].wait()
    load_ffn[1].wait()
    blocks = [(j // 4, slice(D * j, D * j + D), slice(j % 4 * D, j % 4 * D + D)) for j in range(FF // D)]
    hidden_bias = ffn_in_bias[...].astype(f32).reshape(1, FF)
    def feed_forward(gate_s):
        for k, cols, part in blocks:
            hidden = dot(ffn_input, ffn_in_s[k][:, part]) + hidden_bias[:, cols]
            half_gate = 0.5 + 0.5 * lax.erf(hidden * math.sqrt(0.5))
            active_s[k][:, part] = (hidden * half_gate).astype(bf16)
            gate_s[:, cols] = half_gate + hidden * jnp.exp(hidden * hidden * -0.5) * (
                1.0 / math.sqrt(2.0 * math.pi)
            )
        load_ffn[2].wait()
        third_normed, third_rstd = norm_forward(
            second
            + dot(active_s[0][...], ffn_out_s[:half])
            + dot(active_s[1][...], ffn_out_s[half:])
            + ffn_out_bias[...].astype(f32).reshape(1, D)
        )
        result_out[...] = (third_normed * gain[2:3] + shift[2:3])[:NQ].astype(bf16)
        grad_third, gain_grad_2, shift_grad_2 = norm_backward(
            pad_s[2], third_normed, third_rstd, gain[2:3]
        )
        grad_branch_f = grad_third.astype(bf16)
        for k, cols, part in blocks:
            grad_hidden = dot_nt(grad_branch_f, ffn_out_s[cols]) * gate_s[:, cols]
            slope_s[k][:, part] = grad_hidden.astype(bf16)
        return grad_third, gain_grad_2, shift_grad_2, grad_branch_f

    grad_third, gain_grad_2, shift_grad_2, grad_branch_f = pl.run_scoped(
        feed_forward, pltpu.VMEM((NP, FF), f32)
    )
    grad_second = grad_third + dot_nt(slope_s[0][...], ffn_in_s[0][...])
    grad_second += dot_nt(slope_s[1][...], ffn_in_s[1][...])
    grad_second_in, gain_grad_1, shift_grad_1 = norm_backward(
        grad_second, second_normed, second_rstd, gain[1:2]
    )
    grad_branch_c = grad_second_in.astype(bf16)
    ffn_input_t = second.T.astype(bf16)

    @pl.when(member == 0)
    def _():
        for k, cols, part in blocks:
            rows_f[cols] = dot(ffn_input_t, slope_s[k][:, part]).astype(bf16)

    @pl.when(member == 1)
    def _():
        for k, cols, part in blocks:
            rows_f[cols] = dot_tn(active_s[k][:, part], grad_branch_f).astype(bf16)

    is_first = member == 0

    clear_rest(rows_f, ROWS_F)
    sum_f.phases[0]()
    grad_attended_c = dot_nt(grad_branch_c, attn_out[1]).astype(bf16).astype(f32)
    small_s[:16] = jnp.concatenate(
        [row_total(slope_s[k][:, part]) for k, _, part in blocks]
        + [
            row_total(grad_branch_f),
            row_total(grad_branch_c),
            gain_grad_2,
            shift_grad_2,
            gain_grad_1,
            shift_grad_1,
            row_total(grad_attended_c),
            jnp.zeros((1, D), f32),
        ],
        axis=0,
    )

    store_result = pltpu.make_async_copy(result_out, result_hbm, load_sem.at[7])
    store_result.start()

    grad_attended_t = grad_attended_c.T
    grad_x = spread_rows(grad_attended_c)
    grad_v = dot(attn_in[1, 2], spread_cols(grad_attended_t))
    grad_vt[...] = grad_v.astype(bf16)
    inner = head_line(head_sums(grad_attended_t * mixed_t))
    value_rows[...] = dot((mixed_s[...] * own_share).astype(bf16), grad_x).astype(bf16)
    mixed_s[...] = jnp.zeros_like(mixed_s)

    queue_f = sum_f.phases[1:]
    queue_t = list(sum_t.phases)
    queue_k = list(sum_k.phases)

    def take(queue):
        if queue:
            queue.pop(0)()

    def at(i, steps):
        for step, queue in steps:
            pl.when(i == (step * chunks) // 32)(queue.pop(0))

    def slope_block(i):
        rows = pl.ds(pl.multiple_of(i * CHUNK, CHUNK), CHUNK)
        key_ct = key_in_s[rows].T
        memory_c = memory_s[rows]
        for p in range(4):
            cols = pair_cols(p)
            grad_probs = dot(memory_c, grad_vt[:, cols])
            probs = probs_s[rows, cols].astype(f32) * factor_s[pl.ds(i, 1), cols]
            probs_s[rows, cols] = probs.astype(bf16)
            grad_scores_s[rows, cols] = (probs * (grad_probs - inner[:, cols])).astype(bf16)
        mixed_s[...] += dot(key_ct, grad_scores_s[rows])

    @pl.loop(0, chunks // 2)
    def _(i):
        slope_block(i * 2)
        slope_block(i * 2 + 1)
        at(i, [(3, queue_f), (9, queue_f), (15, queue_f)])

    send_b[...] = (project_heads(key_wt, mixed_s[...]) * scale).astype(bf16)
    swap_b = pltpu.make_async_remote_copy(
        src_ref=send_b,
        dst_ref=recv_b,
        send_sem=link_sem.at[2],
        recv_sem=link_sem.at[3],
        device_id=partner,
        device_id_type=pl.DeviceIdType.MESH,
    )
    swap_b.start()
    query_x = spread_rows(query_c.astype(f32))
    rows_k[:D] = (dot(mixed_s[...].astype(bf16), query_x) * scale).astype(bf16)
    rows_k[D : 2 * D] = value_rows[...]
    out_grad_c = dot_tn(attended_c, grad_branch_c)
    rows_k[2 * D : 3 * D] = jnp.where(is_first, out_grad_c, 0.0).astype(bf16)
    clear_rest(rows_k, ROWS_K)
    clear_rest(rows_t, ROWS_T)
    take(queue_k)
    swap_b.wait()
    take(queue_f)
    take(queue_k)
    grad_query_c = (send_b[...].astype(f32) + recv_b[...].astype(f32)).T.astype(bf16)

    cross_pos_grad = dot_nt(grad_query_c, attn_in[1, 0])
    grad_first_in, gain_grad_0, shift_grad_0 = norm_backward(
        grad_second_in + cross_pos_grad, first_normed, first_rstd, gain[0:1]
    )
    grad_branch = grad_first_in.astype(bf16)
    grad_attended = dot_nt(grad_branch, attn_out[0]).astype(bf16).astype(f32)
    take(queue_k)
    grad_probs = dot(value_self, spread_cols(grad_attended.T))
    inner_self = jnp.sum(probs_self * grad_probs, axis=0, keepdims=True)
    grad_scores = (probs_self * (grad_probs - inner_self)).astype(bf16)
    key_t = key_self.astype(f32).T.astype(bf16)
    grad_query_s = (
        own_blocks([dot(key_t[pair_rows(p)], grad_scores[:, pair_cols(p)]) for p in range(4)]) * scale
    ).T.astype(bf16)
    grad_key_s = (dot(grad_scores, spread_rows(query_self.astype(f32))) * scale).astype(bf16)
    grad_value_s = dot(probs_self_b, spread_rows(grad_attended)).astype(bf16)
    grad_mixed_q = dot_nt(grad_query_s, attn_in[0, 0]) + dot_nt(grad_key_s, attn_in[0, 1])
    queries_grad_out[...] = (grad_first_in + grad_mixed_q + dot_nt(grad_value_s, attn_in[0, 2]))[
        :NQ
    ].astype(bf16)
    store_queries = pltpu.make_async_copy(queries_grad_out, queries_grad_hbm, load_sem.at[8])
    store_queries.start()
    small_s[16:] = jnp.concatenate(
        [
            row_total(grad_query_s),
            row_total(grad_value_s),
            row_total(grad_branch),
            row_total(grad_query_c),
            gain_grad_0,
            shift_grad_0,
            jnp.zeros((10, D), f32),
        ],
        axis=0,
    )
    @pl.when(member == 0)
    def _():
        rows_t[:D] = dot_tn(mixed_q, grad_query_s).astype(bf16)
        rows_t[D : 2 * D] = dot_tn(mixed_q, grad_key_s).astype(bf16)
        rows_t[2 * D : 3 * D] = dot_tn(queries_b, grad_value_s).astype(bf16)

    @pl.when(member == 1)
    def _():
        rows_t[:D] = dot_tn(cross_q, grad_query_c).astype(bf16)
        rows_t[D : 2 * D] = dot_tn(attended, grad_branch).astype(bf16)
        rows_t[ROW_POS:ROW_SMALL] = (grad_mixed_q + cross_pos_grad).astype(bf16)
        rows_t[ROW_SMALL : ROW_SMALL + 32] = small_s[...].astype(bf16)
        rows_t[ROW_SMALL + 32 : ROWS_T] = jnp.zeros((ROWS_T - ROW_SMALL - 32, D), bf16)

    take(queue_t)
    take(queue_k)
    take(queue_f)
    back_s[:HQ] = (dot_nt(query_x, attn_in[1, 1]) * scale).astype(bf16)
    back_s[HQ:] = dot_nt(spread_rows(grad_attended_c), attn_in[1, 2]).astype(bf16)

    def memory_block(i):
        rows = pl.ds(pl.multiple_of(i * CHUNK, CHUNK), CHUNK)
        both = jnp.concatenate([grad_scores_s[rows], probs_s[rows]], axis=1)
        memory_s[rows] = dot(both, back_s[...]).astype(bf16)
        pltpu.make_async_copy(memory_s.at[rows], memory_grad_hbm.at[0, rows], store_sem.at[i]).start()

    @pl.loop(0, chunks // 2)
    def _(i):
        memory_block(i * 2)
        memory_block(i * 2 + 1)
        at(
            i,
            [
                (3, queue_t),
                (4, queue_k),
                (7, queue_t),
                (8, queue_k),
                (9, queue_f),
                (11, queue_t),
                (12, queue_k),
                (15, queue_t),
            ],
        )

    while queue_f:
        take(queue_f)
    stores = [
        pltpu.make_async_copy(whole, target, load_sem.at[4 + k])
        for k, (whole, target) in enumerate(
            (
                (whole_f, whole_f_hbm),
                (whole_t, whole_t_hbm),
                (whole_k, whole_k_hbm),
            )
        )
    ]
    stores[0].start()
    while queue_t or queue_k:
        take(queue_t)
        take(queue_k)
    for store in stores[1:]:
        store.start()

    @pl.loop(0, chunks)
    def _(i):
        rows = pl.ds(pl.multiple_of(i * CHUNK, CHUNK), CHUNK)
        pltpu.make_async_copy(memory_s.at[rows], memory_grad_hbm.at[0, rows], store_sem.at[i]).wait()

    for store in [*stores, store_result, store_queries]:
        store.wait()


def finish_kernel(
    result_in,
    queries_grad_in,
    memory_grad_in,
    whole_f_hbm,
    whole_t_hbm,
    whole_k_hbm,
    result_hbm,
    queries_grad_hbm,
    memory_grad,
    attn_in_hbm,
    attn_out_hbm,
    attn_bias_hbm,
    ffn_in_hbm,
    ffn_in_bias_hbm,
    ffn_out_hbm,
    ffn_out_bias_hbm,
    norm_gain_hbm,
    norm_bias_hbm,
    query_pos_hbm,
    moved,
    whole_f,
    whole_t,
    whole_k,
    result,
    queries_grad,
    attn_in_grad,
    attn_out_grad,
    attn_bias_grad,
    ffn_in_grad,
    ffn_in_bias_grad,
    ffn_out_grad,
    ffn_out_bias_grad,
    norm_gain_grad,
    norm_bias_grad,
    query_pos_grad,
    in_sem,
    out_sem,
    sum_sem,
    grad_sem,
):
    pieces = in_sem.shape[0]
    piece = moved.shape[0] // pieces

    def fetch(j):
        rows = pl.ds(piece * j, piece)
        return pltpu.make_async_copy(memory_grad_in.at[0, rows], moved.at[rows], in_sem.at[j])

    def write(j):
        rows = pl.ds(piece * j, piece)
        return pltpu.make_async_copy(moved.at[rows], memory_grad.at[0, rows], out_sem.at[j])

    sums = [
        (whole_t_hbm, whole_t),
        (whole_k_hbm, whole_k),
        (whole_f_hbm, whole_f),
        (result_in, result),
        (queries_grad_in, queries_grad),
    ]
    loads = [pltpu.make_async_copy(*pair, sum_sem.at[j]) for j, pair in enumerate(sums)]
    for load in loads:
        load.start()
    for j in range(pieces):
        fetch(j).start()
    blocks = FF // D
    stores = []

    def store(source, target):
        stores.append(pltpu.make_async_copy(source, target, grad_sem.at[len(stores)]))
        stores[-1].start()

    loads[0].wait()
    loads[1].wait()
    for j in range(3):
        attn_in_grad[0, j] = whole_t[0, D * j : D * j + D].astype(f32)
    attn_in_grad[1, 0] = whole_t[1, :D].astype(f32)
    attn_in_grad[1, 1] = whole_k[:D].astype(f32)
    attn_in_grad[1, 2] = whole_k[D : 2 * D].astype(f32)
    store(attn_in_grad, attn_in_hbm)
    attn_out_grad[0] = whole_t[1, D : 2 * D].astype(f32)
    attn_out_grad[1] = whole_k[2 * D : 3 * D].astype(f32)
    store(attn_out_grad, attn_out_hbm)
    loads[2].wait()
    for k in range(2):
        half = slice(FF // 2 * k, FF // 2 * (k + 1))
        ffn_out_grad[half] = whole_f[1, half].astype(f32)
        store(ffn_out_grad.at[half], ffn_out_hbm.at[half])
    for k in range(2):
        half = slice(FF // 2 * k, FF // 2 * (k + 1))
        for j in range(blocks // 2 * k, blocks // 2 * (k + 1)):
            at = slice(D * j, D * j + D)
            ffn_in_grad[:, at] = whole_f[0, at].astype(f32)
        store(ffn_in_grad.at[:, half], ffn_in_hbm.at[:, half])
    for j in range(pieces):
        fetch(j).wait()
        write(j).start()
    loads[3].wait()
    store(result, result_hbm.at[0])
    loads[4].wait()
    store(queries_grad, queries_grad_hbm.at[0])
    query_pos_grad[...] = whole_t[1, ROW_POS:ROW_SMALL].astype(f32)[:NQ]
    store(query_pos_grad, query_pos_hbm)
    small = whole_t[1, ROW_SMALL : ROW_SMALL + 32].astype(f32)
    ffn_in_bias_grad[...] = jnp.concatenate([small[j : j + 1] for j in range(blocks)], axis=1)
    store(ffn_in_bias_grad, ffn_in_bias_hbm)
    ffn_out_bias_grad[...] = small[8:9]
    store(ffn_out_bias_grad, ffn_out_bias_hbm)
    for j, (own, cross) in enumerate(((16, 19), (17, 14), (18, 9))):
        attn_bias_grad[j, 0:1] = small[own : own + 1]
        attn_bias_grad[j, 1:2] = small[cross : cross + 1]
    store(attn_bias_grad, attn_bias_hbm)
    for j, (gain, shift) in enumerate(((20, 21), (12, 13), (10, 11))):
        norm_gain_grad[j : j + 1] = small[gain : gain + 1]
        norm_bias_grad[j : j + 1] = small[shift : shift + 1]
    store(norm_gain_grad, norm_gain_hbm)
    store(norm_bias_grad, norm_bias_hbm)
    for j in range(pieces):
        write(j).wait()
    for copy in stores:
        copy.wait()


def body(
    pages,
    queries,
    memory,
    quarter_turns,
    token_order,
    lengths,
    attn_in,
    attn_out,
    attn_bias,
    ffn_in,
    ffn_in_bias,
    ffn_out,
    ffn_out_bias,
    norm_gain,
    norm_bias,
    query_pos,
    out_grad,
):
    tokens = memory.shape[1]
    chunks = tokens // CHUNK
    groups_f, groups_t, groups_k = sum_groups(pages)
    summed = [
        (padded(ROWS_F, pages), groups_f),
        (padded(ROWS_T, pages), groups_t),
        (padded(ROWS_K, 2 * pages), groups_k),
    ]
    whole_shapes = [(2, rows, D) for rows, _ in summed[:2]] + [(summed[2][0], D)]
    sum_buffers = []
    for (rows, groups), shape in zip(summed, whole_shapes):
        landing = PageSum.landing_rows(pages, groups, rows)
        own_rows = [(rows, D)] if groups is groups_f else []
        sum_buffers += [pltpu.VMEM(each, bf16) for each in (*own_rows, (landing, D), shape)]
    copies = 32
    vmem = pl.BlockSpec(memory_space=pltpu.VMEM)
    smem = pl.BlockSpec(memory_space=pltpu.SMEM)
    anywhere = pl.BlockSpec(memory_space=pl.ANY)
    parts = pl.pallas_call(
        functools.partial(layer_kernel, tokens, pages),
        out_shape=[
            jax.ShapeDtypeStruct((NQ, D), bf16),
            jax.ShapeDtypeStruct((NQ, D), bf16),
            jax.ShapeDtypeStruct((1, tokens, D), bf16),
            *(jax.ShapeDtypeStruct(shape, bf16) for shape in whole_shapes),
        ],
        in_specs=[
            vmem,
            anywhere,
            smem,
            vmem,
            smem,
            vmem,
            vmem,
            vmem,
            anywhere,
            vmem,
            anywhere,
            vmem,
            vmem,
            vmem,
            vmem,
            vmem,
            vmem,
        ],
        out_specs=[anywhere] * 6,
        scratch_shapes=[
            pltpu.VMEM((tokens, D), bf16),
            pltpu.VMEM((tokens, D), bf16),
            pltpu.VMEM((tokens, HQ), bf16),
            pltpu.VMEM((tokens, HQ), bf16),
            pltpu.VMEM((1, tokens), f32),
            pltpu.VMEM((D, HQ), bf16),
            pltpu.VMEM((D, D), bf16),
            pltpu.VMEM((4 * SIDE, D), bf16),
            pltpu.VMEM((8, HQ), f32),
            pltpu.VMEM((8, HQ), f32),
            pltpu.VMEM((chunks, HQ), f32),
            pltpu.VMEM((chunks, HQ), f32),
            pltpu.VMEM((8, HQ), f32),
            pltpu.VMEM((D, HQ), f32),
            pltpu.VMEM((3, NP, D), f32),
            pltpu.VMEM((NQ, D), bf16),
            pltpu.VMEM((NQ, D), bf16),
            pltpu.VMEM((D, NP), bf16),
            pltpu.VMEM((D, NP), bf16),
            pltpu.VMEM((2 * HEADS, NP), f32),
            pltpu.VMEM((2 * HEADS, NP), f32),
            pltpu.VMEM((D, NP), bf16),
            pltpu.VMEM((D, NP), bf16),
            pltpu.VMEM((32, D), f32),
            *sum_buffers,
            pltpu.SemaphoreType.DMA((9,)),
            pltpu.SemaphoreType.DMA((chunks,)),
            pltpu.SemaphoreType.DMA((6,)),
            *[pltpu.SemaphoreType.DMA((copies,))] * 6,
        ],
        compiler_params=pltpu.CompilerParams(
            collective_id=0, has_side_effects=True, vmem_limit_bytes=127 * 512 * 1024
        ),
        cost_estimate=pl.CostEstimate(
            flops=2 * 8 * tokens * HQ * D, bytes_accessed=20 << 20, transcendentals=tokens * HQ
        ),
        name="decoder_layer",
    )(
        queries,
        memory,
        quarter_turns,
        token_order,
        lengths,
        attn_in,
        attn_out,
        attn_bias.transpose(1, 0, 2),
        ffn_in,
        ffn_in_bias,
        ffn_out,
        ffn_out_bias,
        norm_gain,
        norm_bias,
        query_pos,
        out_grad,
        jnp.asarray(position_table()),
    )
    outs = pl.pallas_call(
        finish_kernel,
        out_shape=[
            jax.ShapeDtypeStruct((1, NQ, D), bf16),
            jax.ShapeDtypeStruct((1, NQ, D), bf16),
            jax.ShapeDtypeStruct((1, tokens, D), bf16),
            jax.ShapeDtypeStruct((2, 3, D, D), f32),
            jax.ShapeDtypeStruct((2, D, D), f32),
            jax.ShapeDtypeStruct((3, 2, D), f32),
            jax.ShapeDtypeStruct((D, FF), f32),
            jax.ShapeDtypeStruct((1, FF), f32),
            jax.ShapeDtypeStruct((FF, D), f32),
            jax.ShapeDtypeStruct((1, D), f32),
            jax.ShapeDtypeStruct((3, D), f32),
            jax.ShapeDtypeStruct((3, D), f32),
            jax.ShapeDtypeStruct((NQ, D), f32),
        ],
        in_specs=[anywhere] * 6,
        out_specs=[anywhere] * 13,
        scratch_shapes=[
            pltpu.VMEM((tokens, D), bf16),
            *(pltpu.VMEM(shape, bf16) for shape in whole_shapes),
            pltpu.VMEM((NQ, D), bf16),
            pltpu.VMEM((NQ, D), bf16),
            pltpu.VMEM((2, 3, D, D), f32),
            pltpu.VMEM((2, D, D), f32),
            pltpu.VMEM((3, 2, D), f32),
            pltpu.VMEM((D, FF), f32),
            pltpu.VMEM((1, FF), f32),
            pltpu.VMEM((FF, D), f32),
            pltpu.VMEM((1, D), f32),
            pltpu.VMEM((3, D), f32),
            pltpu.VMEM((3, D), f32),
            pltpu.VMEM((NQ, D), f32),
            pltpu.SemaphoreType.DMA((8,)),
            pltpu.SemaphoreType.DMA((8,)),
            pltpu.SemaphoreType.DMA((5,)),
            pltpu.SemaphoreType.DMA((14,)),
        ],
        compiler_params=pltpu.CompilerParams(vmem_limit_bytes=62 * 1024 * 1024),
        name="write_outputs",
    )(*parts)
    return (
        *outs[:5],
        outs[5].transpose(1, 0, 2),
        outs[6],
        outs[7].reshape(FF),
        outs[8],
        outs[9].reshape(D),
        *outs[10:],
    )


def solution(mesh):
    in_specs = (
        P("dp", None, None),
        P("dp", "blk", None),
        P("dp"),
        P("dp", "blk"),
        P("dp"),
        P(),
        P(),
        P(),
        P(),
        P(),
        P(),
        P(),
        P(),
        P(),
        P(),
        P("dp", None, None),
    )
    out_specs = (
        P("dp", None, None),
        P("dp", None, None),
        P("dp", "blk", None),
        P(),
        P(),
        P(),
        P(),
        P(),
        P(),
        P(),
        P(),
        P(),
        P(),
    )
    layer = functools.partial(body, mesh.shape["dp"])
    return jax.shard_map(layer, mesh=mesh, in_specs=in_specs, out_specs=out_specs, check_vma=False)
```

```python
import functools
import math

import jax
import jax.numpy as jnp
import numpy as np
from jax import lax
from jax.experimental import pallas as pl
from jax.experimental.pallas import tpu as pltpu
from jax.sharding import PartitionSpec as P

D = 256
HEADS = 8
HD = D // HEADS
SIDE = 128
NQ = 125
NP = 128
HQ = HEADS * NP
PAIR = 2 * NP
FF = 2048
CHUNK = 1024

masked_score = -1e30
norm_eps = 1e-05
scale = 1.0 / math.sqrt(HD)
log2e = math.log2(math.e)

bf16 = jnp.bfloat16
f32 = jnp.float32

ROWS_F = FF
ROW_POS = 2 * D
ROW_SMALL = 2 * D + NP
ROWS_T = 3 * D
ROWS_K = 3 * D
TILE = 16


def axes_of(pages):
    axes = {"core": (2, 1), "y": (2, 2)}
    stride = 4
    while stride < pages:
        radix = 4 if pages // stride % 4 == 0 else 2
        axes["z%d" % (len(axes) - 2)] = (radix, stride)
        stride *= radix
    axes["x"] = (2, 0)
    return axes


def far_axes(pages):
    return [(name,) for name in axes_of(pages) if name.startswith("z")]


def sum_groups(pages):
    far = far_axes(pages)
    return [("core",), ("y",), *far], [("core", "y"), *far], [("core",), ("x",), ("y",), *far]


def padded(rows, pages):
    unit = TILE * pages
    return (rows + unit - 1) // unit * unit


def position_table():
    half = D // 2
    channel = np.arange(half)
    inverse = np.exp((channel // 2).astype(np.float32) * np.float32(-2.0 * math.log(10000.0) / half))
    angle = (np.arange(SIDE, dtype=np.float32) + 1.0) * np.float32(2.0 * math.pi / SIDE)
    angle = angle[:, None] * inverse
    return np.where(channel % 2 == 0, np.sin(angle), np.cos(angle)).astype(np.float32)


def dot(a, b):
    return jnp.dot(a, b, preferred_element_type=f32)


def dot_nt(a, b):
    return lax.dot_general(a, b, (((1,), (1,)), ((), ())), preferred_element_type=f32)


def dot_tn(a, b):
    return lax.dot_general(a, b, (((0,), (0,)), ((), ())), preferred_element_type=f32)


def row_total(values):
    return jnp.sum(values.astype(f32), axis=0, keepdims=True)


def norm_forward(values):
    average = jnp.mean(values, axis=-1, keepdims=True)
    centred = values - average
    variance = jnp.mean(centred * centred, axis=-1, keepdims=True)
    rstd = lax.rsqrt(variance + norm_eps)
    return centred * rstd, rstd


def norm_backward(grad, normed, rstd, gain):
    grad_normed = grad * gain
    first = jnp.mean(grad_normed, axis=-1, keepdims=True)
    second = jnp.mean(grad_normed * normed, axis=-1, keepdims=True)
    grad_in = rstd * (grad_normed - first - normed * second)
    return grad_in, row_total(grad * normed), row_total(grad)


def spread_rows(rows):
    head = lax.broadcasted_iota(jnp.int32, (NP, D), 1) // HD
    return jnp.concatenate(
        [jnp.where(head == h, rows, 0.0) for h in range(HEADS)], axis=0
    ).astype(bf16)


def spread_cols(cols):
    head = lax.broadcasted_iota(jnp.int32, (D, NP), 0) // HD
    return jnp.concatenate(
        [jnp.where(head == h, cols, 0.0) for h in range(HEADS)], axis=1
    ).astype(bf16)


def project_heads(weight_t, sums):
    high = sums.astype(bf16)
    low = (sums - high.astype(f32)).astype(bf16)
    return own_blocks(
        [
            dot(weight_t[pair_rows(p)], high[:, pair_cols(p)])
            + dot(weight_t[pair_rows(p)], low[:, pair_cols(p)])
            for p in range(4)
        ]
    )


def own_blocks(pairs):
    parts = []
    for pair in pairs:
        parts += [pair[:HD, :NP], pair[HD:, NP:]]
    return jnp.concatenate(parts, axis=0)


def head_rows(row):
    return jnp.concatenate([row[:, NP * h : NP * h + NP] for h in range(HEADS)], axis=0)


def head_line(rows):
    return jnp.concatenate([rows[h : h + 1] for h in range(HEADS)], axis=1)


def per_channel(rows):
    return jnp.concatenate(
        [jnp.broadcast_to(rows[h : h + 1], (HD, NP)) for h in range(HEADS)], axis=0
    )


def head_sums(cols):
    return jnp.concatenate(
        [jnp.sum(cols[HD * h : HD * h + HD], axis=0, keepdims=True) for h in range(HEADS)], axis=0
    )


def pair_cols(p):
    return slice(PAIR * p, PAIR * p + PAIR)


def pair_rows(p):
    return slice(2 * HD * p, 2 * HD * p + 2 * HD)


class Place:
    def __init__(self, pages):
        self.axes = axes_of(pages)
        self.page = lax.axis_index("dp")
        self.member = lax.axis_index("blk")
        self.digit = {
            name: self.member if name == "x" else lax.rem(self.page // stride, radix)
            for name, (radix, stride) in self.axes.items()
        }

    def size(self, group):
        return math.prod(self.axes[name][0] for name in group)

    def index(self, group):
        index = 0
        for name in group:
            index = index * self.axes[name][0] + self.digit[name]
        return index

    def peer(self, group, hop):
        index = lax.rem(self.index(group) + hop, self.size(group))
        page, member, rest = self.page, self.member, index
        for name in reversed(group):
            radix, stride = self.axes[name]
            digit = lax.rem(rest, radix)
            rest = rest // radix
            if name == "x":
                member = digit
            else:
                page = page + (digit - self.digit[name]) * stride
        return (page, member), index


class PageSum:
    def __init__(self, place, groups, back, rows, landing, whole, sent, arrived):
        self.place, self.groups, self.back = place, groups, back
        self.rows, self.landing, self.whole = rows, landing, whole
        self.sent, self.arrived = sent, arrived
        self.slots = 0
        self.extents = [rows.shape[0]]
        self.bases = [0]
        self.landings = []
        at = 0
        for group in groups:
            size = place.size(group)
            extent = self.extents[-1] // size
            self.landings.append(at)
            at += (size - 1) * extent
            self.bases.append(pl.multiple_of(self.bases[-1] + place.index(group) * extent, TILE))
            self.extents.append(extent)
        last = len(groups)
        moves = [self.scatter_moves(s) for s in range(last)]
        near = {"all": 0, "across": 1, "sides": 2}[back]
        moves += [self.gather_moves(s) for s in range(last - 1, near - 1, -1)]
        if back == "sides":
            moves += [self.side_moves(), self.corner_moves(), self.core_moves()]
        elif back == "across":
            moves += [self.across_moves(), self.core_moves()]
        self.phases = [functools.partial(self.step, moves, k) for k in range(len(moves) + 1)]

    @staticmethod
    def landing_rows(pages, groups, rows):
        axes = axes_of(pages)
        total, extent = 0, rows
        for group in groups:
            size = math.prod(axes[name][0] for name in group)
            extent //= size
            total += (size - 1) * extent
        return total

    def step(self, moves, k):
        last = len(self.groups)
        if k > 0:
            for move in moves[k - 1]:
                self.copy(*move).wait()
        if 0 < k <= last:
            total = self.scatter_sum(k - 1)
            region = pl.ds(self.bases[k], self.extents[k])
            if k < last:
                self.rows[region] = total
            elif len(self.whole.shape) == 3:
                self.whole[self.place.member, region] = total
            else:
                self.whole[region] = total
        if k < len(moves):
            for move in moves[k]:
                self.copy(*move).start()

    def copy(self, slot, source, target, device):
        return pltpu.make_async_remote_copy(
            src_ref=source(),
            dst_ref=target(),
            send_sem=self.sent.at[slot],
            recv_sem=self.arrived.at[slot],
            device_id=device,
            device_id_type=pl.DeviceIdType.MESH,
        )

    def new_slot(self):
        self.slots += 1
        return self.slots - 1

    def same(self, device, view):
        return (self.new_slot(), view, view, device)

    def scatter_moves(self, step):
        group = self.groups[step]
        extent = self.extents[step + 1]
        moves = []
        for hop in range(1, self.place.size(group)):
            device, other = self.place.peer(group, hop)
            start = pl.multiple_of(self.bases[step] + other * extent, TILE)
            landing = self.landings[step] + (hop - 1) * extent
            moves.append(
                (
                    self.new_slot(),
                    functools.partial(self.part, self.rows, start, extent),
                    functools.partial(self.part, self.landing, landing, extent),
                    device,
                )
            )
        return moves

    @staticmethod
    def part(ref, start, extent):
        return ref.at[pl.ds(start, extent)]

    def half(self, member, start, extent):
        if len(self.whole.shape) == 3:
            return self.whole.at[member, pl.ds(start, extent)]
        return self.whole.at[pl.ds(start, extent)]

    def scatter_sum(self, step):
        extent = self.extents[step + 1]
        total = self.rows[pl.ds(self.bases[step + 1], extent)].astype(f32)
        for hop in range(1, self.place.size(self.groups[step])):
            landing = self.landings[step] + (hop - 1) * extent
            total = total + self.landing[pl.ds(landing, extent)].astype(f32)
        return total.astype(bf16)

    def gather_moves(self, step):
        group = self.groups[step]
        view = functools.partial(self.half, self.place.member, self.bases[step + 1], self.extents[step + 1])
        return [
            self.same(self.place.peer(group, hop)[0], view) for hop in range(1, self.place.size(group))
        ]

    def own_quarter(self):
        step = 2 if len(self.groups[0]) == 1 else 1
        return self.bases[step], self.extents[step]

    def side_moves(self):
        view = functools.partial(self.half, self.place.member, *self.own_quarter())
        return [self.same(self.place.peer((name,), 1)[0], view) for name in ("y", "x")]

    def corner_moves(self):
        base, extent = self.own_quarter()
        other = pl.multiple_of(base + (1 - 2 * self.place.digit["y"]) * extent, TILE)
        view = functools.partial(self.half, self.place.member, other, extent)
        return [self.same(self.place.peer(("x",), 1)[0], view)]

    def across_moves(self):
        view = functools.partial(self.half, self.place.member, *self.own_quarter())
        return [self.same(self.place.peer(("x", "y"), hop)[0], view) for hop in range(1, 4)]

    def core_moves(self):
        extent = self.extents[0] // 2
        start = pl.multiple_of(self.place.digit["core"] * extent, TILE)
        device, _ = self.place.peer(("core",), 1)
        return [self.same(device, functools.partial(self.half, m, start, extent)) for m in range(2)]


def clear_rest(ref, used):
    if ref.shape[0] > used:
        ref[used:] = jnp.zeros((ref.shape[0] - used, D), ref.dtype)


def layer_kernel(
    tokens,
    pages,
    queries_in,
    memory_hbm,
    turns_in,
    order_in,
    lengths_in,
    attn_in,
    attn_out,
    attn_bias,
    ffn_in_hbm,
    ffn_in_bias,
    ffn_out_hbm,
    ffn_out_bias,
    norm_gain,
    norm_bias,
    pos_in,
    out_grad_in,
    table_in,
    result_hbm,
    queries_grad_hbm,
    memory_grad_hbm,
    whole_f_hbm,
    whole_t_hbm,
    whole_k_hbm,
    memory_s,
    key_in_s,
    probs_s,
    grad_scores_s,
    code_s,
    query_kt,
    grad_vt,
    back_s,
    table_s,
    top_s,
    highest_s,
    shifts_s,
    factor_s,
    total_s,
    mixed_s,
    pad_s,
    result_out,
    queries_grad_out,
    send_a,
    recv_a,
    send_t,
    recv_t,
    send_b,
    recv_b,
    small_s,
    rows_f,
    landing_f,
    whole_f,
    rows_t,
    landing_t,
    whole_t,
    rows_k,
    landing_k,
    whole_k,
    load_sem,
    store_sem,
    link_sem,
    sent_f,
    arrived_f,
    sent_t,
    arrived_t,
    sent_k,
    arrived_k,
):
    member = lax.axis_index("blk")
    partner = (lax.axis_index("dp"), 1 - member)
    chunks = tokens // CHUNK

    place = Place(pages)
    groups_f, groups_t, groups_k = sum_groups(pages)
    sum_f = PageSum(place, groups_f, "sides", rows_f, landing_f, whole_f, sent_f, arrived_f)
    sum_t = PageSum(place, groups_t, "across", rows_t, landing_t, whole_t, sent_t, arrived_t)
    sum_k = PageSum(place, groups_k, "all", rows_k, landing_k, whole_k, sent_k, arrived_k)

    barrier = pltpu.get_barrier_semaphore()
    peers = [
        place.peer(group, hop)[0]
        for group in [("x", "core", "y"), *far_axes(pages)]
        for hop in range(1, place.size(group))
    ]
    for peer in peers:
        pl.semaphore_signal(barrier, inc=1, device_id=peer, device_id_type=pl.DeviceIdType.MESH)

    load_memory = pltpu.make_async_copy(memory_hbm.at[0], memory_s, load_sem.at[0])
    half = FF // 2
    ffn_in_s = [grad_scores_s.at[D * k : D * k + D] for k in range(2)]
    ffn_out_s = grad_scores_s.at[2 * D : 2 * D + FF, :D]
    free = 2 * D + FF
    active_s = [grad_scores_s.at[free + NP * k : free + NP * k + NP] for k in range(2)]
    slope_s = [grad_scores_s.at[free + NP * k : free + NP * k + NP] for k in range(2, 4)]
    load_ffn = [
        pltpu.make_async_copy(ffn_in_hbm.at[:, half * k : half * k + half], ffn_in_s[k], load_sem.at[1 + k])
        for k in range(2)
    ]
    load_ffn.append(pltpu.make_async_copy(ffn_out_hbm, ffn_out_s, load_sem.at[3]))
    load_memory.start()
    for load in load_ffn:
        load.start()

    pairs = [attn_bias[j].astype(f32) for j in range(3)]
    bias = jnp.concatenate([pair[k : k + 1] for k in range(2) for pair in pairs], axis=0)
    gain = norm_gain[...].astype(f32)
    shift = norm_bias[...].astype(f32)

    def each_two(block):
        @pl.loop(0, chunks // 2)
        def _(j):
            block(j * 2)
            block(j * 2 + 1)

    order = order_in[...]
    turn = turns_in[0]
    row_at = order >> 7
    col_at = order & 127
    top = SIDE - 1
    row_new = jnp.where(
        turn == 0, row_at, jnp.where(turn == 1, col_at, jnp.where(turn == 2, top - row_at, top - col_at))
    )
    col_new = jnp.where(
        turn == 0, col_at, jnp.where(turn == 1, top - row_at, jnp.where(turn == 2, top - col_at, row_at))
    )
    past = jnp.where(order < lengths_in[0], 0, SIDE * SIDE)
    code_s[...] = (row_new * SIDE + col_new + past).astype(f32)

    pad_s[...] = jnp.zeros_like(pad_s)
    pad_s[0, :NQ] = queries_in[0].astype(f32)
    pad_s[1, :NQ] = pos_in[...].astype(f32)
    pad_s[2, :NQ] = out_grad_in[0].astype(f32)
    queries_f = pad_s[0]
    pos_f = pad_s[1]
    queries_b = queries_f.astype(bf16)
    mixed_q = (queries_f + pos_f).astype(bf16)
    query_self = (dot(mixed_q, attn_in[0, 0]) + bias[0:1]).astype(bf16)
    key_self = dot(mixed_q, attn_in[0, 1]).astype(bf16)
    value_self = (dot(queries_b, attn_in[0, 2]) + bias[1:2]).astype(bf16)
    scores = dot(key_self, spread_cols(query_self.astype(f32).T)) * scale
    own_key = lax.broadcasted_iota(jnp.int32, (NP, HQ), 0) < NQ
    scores = jnp.where(own_key, scores, masked_score)
    raised = jnp.exp(scores - jnp.max(scores, axis=0, keepdims=True))
    probs_self = raised / jnp.sum(raised, axis=0, keepdims=True)
    probs_self_b = probs_self.astype(bf16)
    value_t = value_self.astype(f32).T.astype(bf16)
    attended = own_blocks(
        [dot(value_t[pair_rows(p)], probs_self_b[:, pair_cols(p)]) for p in range(4)]
    ).T.astype(bf16)
    first_normed, first_rstd = norm_forward(queries_f + dot(attended, attn_out[0]) + bias[2:3])
    first = first_normed * gain[0:1] + shift[0:1]
    cross_q = (first + pos_f).astype(bf16)
    query_c = (dot(cross_q, attn_in[1, 0]) + bias[3:4]).astype(bf16)
    query_x = spread_rows(query_c.astype(f32))
    query_k = dot(attn_in[1, 1], spread_cols(query_c.astype(f32).T))
    query_kt[...] = (query_k * (scale * log2e)).astype(bf16)
    back_s[:HQ] = (dot_nt(query_x, attn_in[1, 1]) * scale).astype(bf16)
    table = table_in[...]
    nothing = jnp.zeros((SIDE, D // 2), f32)
    table = jnp.concatenate(
        [jnp.concatenate([table, nothing], axis=1), jnp.concatenate([nothing, table], axis=1)], axis=0
    )
    table_high = table.astype(bf16)
    table_s[: 2 * SIDE] = table_high
    table_s[2 * SIDE :] = (table - table_high.astype(f32)).astype(bf16)

    load_memory.wait()
    def mask_view(i):
        side, place = i // (chunks // 2), lax.rem(i, chunks // 2)
        return grad_scores_s.at[
            pl.ds(pl.multiple_of(tokens // 2 + place * CHUNK, CHUNK), CHUNK),
            pl.ds(pl.multiple_of(side * NP, NP), NP),
        ]

    lane = lax.broadcasted_iota(jnp.int32, (CHUNK, NP), 1)

    @each_two
    def _(i):
        rows = pl.ds(pl.multiple_of(i * CHUNK, CHUNK), CHUNK)
        line = code_s[:, rows]
        code = jnp.concatenate(
            [
                jnp.broadcast_to(line[:, NP * j : NP * j + NP], (NP, NP)).T
                for j in range(CHUNK // NP)
            ],
            axis=0,
        ).astype(jnp.int32)
        row_hot = jnp.where(((code >> 7) & 127) == lane, 1.0, 0.0).astype(bf16)
        col_hot = jnp.where((code & 127) == lane, 1.0, 0.0).astype(bf16)
        hot = jnp.concatenate([row_hot, col_hot, row_hot, col_hot], axis=1)
        masked = jnp.where(code < SIDE * SIDE, 0.0, masked_score)
        mask_view(i)[...] = masked.astype(bf16)
        key_in_s[rows] = (memory_s[rows].astype(f32) + dot(hot, table_s[...])).astype(bf16)

    def score_pair(p, key_in, mask, score_s):
        cols = pair_cols(p)
        part = dot(key_in, query_kt[:, cols]) + mask
        score_s[:, cols] = part
        top_s[:, cols] = jnp.max(part.reshape(CHUNK // 8, 8, PAIR), axis=0)

    def score_operands(i):
        rows = pl.ds(pl.multiple_of(i * CHUNK, CHUNK), CHUNK)
        mask = mask_view(i)[...].astype(f32)
        return key_in_s[rows], jnp.concatenate([mask, mask], axis=1)

    def attend_all(score_s):
        operands = score_operands(0)
        for p in range(4):
            score_pair(p, *operands, score_s)

        @pl.loop(0, chunks)
        def _(i):
            rows = pl.ds(pl.multiple_of(i * CHUNK, CHUNK), CHUNK)
            memory_ct = memory_s[rows].T
            operands = score_operands(jnp.minimum(i + 1, chunks - 1))
            for p in range(4):
                cols = pair_cols(p)
                before = highest_s[0:1, cols]
                highest = jnp.maximum(before, jnp.max(top_s[:, cols], axis=0, keepdims=True))
                if p >= 2:
                    earlier = jnp.minimum(top_s[0:1, pair_cols(p - 2)], -3.3e38)
                    highest = jnp.maximum(highest, earlier)
                highest_s[0:1, cols] = highest
                shifts_s[pl.ds(i, 1), cols] = highest
                fade = jnp.exp2(before - highest)
                raised = jnp.exp2(score_s[:, cols] - highest)
                sums = jnp.sum(raised.reshape(CHUNK // 8, 8, PAIR), axis=0)
                total_s[:, cols] = total_s[:, cols] * fade + sums
                probs_s[rows, cols] = raised.astype(bf16)
                mixed_s[:, cols] = mixed_s[:, cols] * fade + dot(memory_ct, probs_s[rows, cols])
                score_pair(p, *operands, score_s)

    highest_s[0:1] = jnp.full((1, HQ), -3e38, f32)
    total_s[...] = jnp.zeros_like(total_s)
    mixed_s[...] = jnp.zeros_like(mixed_s)
    pl.run_scoped(attend_all, pltpu.VMEM((CHUNK, HQ), f32))
    highest_own = highest_s[0:1]
    total_own = jnp.sum(total_s[...], axis=0, keepdims=True)

    value_wt = attn_in[1, 2].astype(f32).T.astype(bf16)
    key_wt = attn_in[1, 1].astype(f32).T.astype(bf16)
    send_a[...] = project_heads(value_wt, mixed_s[...]).astype(bf16)
    send_t[:HEADS] = head_rows(highest_own)
    send_t[HEADS:] = head_rows(total_own)
    pl.semaphore_wait(barrier, len(peers))
    swap_a = pltpu.make_async_remote_copy(
        src_ref=send_a,
        dst_ref=recv_a,
        send_sem=link_sem.at[0],
        recv_sem=link_sem.at[1],
        device_id=partner,
        device_id_type=pl.DeviceIdType.MESH,
    )
    swap_t = pltpu.make_async_remote_copy(
        src_ref=send_t,
        dst_ref=recv_t,
        send_sem=link_sem.at[4],
        recv_sem=link_sem.at[5],
        device_id=partner,
        device_id_type=pl.DeviceIdType.MESH,
    )
    swap_a.start()
    swap_t.start()
    swap_a.wait()
    swap_t.wait()
    is_first = member == 0
    own, other = send_a[...].astype(f32), recv_a[...].astype(f32)
    left = jnp.where(is_first, own, other)
    right = jnp.where(is_first, other, own)
    own, other = send_t[...], recv_t[...]
    left_t = jnp.where(is_first, own, other)
    right_t = jnp.where(is_first, other, own)
    highest = jnp.maximum(left_t[:HEADS], right_t[:HEADS])
    fade_l = jnp.exp2(left_t[:HEADS] - highest)
    fade_r = jnp.exp2(right_t[:HEADS] - highest)
    total = left_t[HEADS:] * fade_l + right_t[HEADS:] * fade_r
    mixed_t = left * per_channel(fade_l / total) + right * per_channel(fade_r / total)
    log_total = head_line(highest + jnp.log2(total))
    own_share = jnp.exp2(highest_own - log_total)
    factor_s[...] = jnp.exp2(shifts_s[...] - log_total)
    attended_c = (mixed_t.T + bias[4:5]).astype(bf16)

    second_normed, second_rstd = norm_forward(first + dot(attended_c, attn_out[1]) + bias[5:6])
    second = second_normed * gain[1:2] + shift[1:2]
    ffn_input = second.astype(bf16)
    load_ffn[0].wait()
    load_ffn[1].wait()
    blocks = [(j // 4, slice(D * j, D * j + D), slice(j % 4 * D, j % 4 * D + D)) for j in range(FF // D)]
    hidden_bias = ffn_in_bias[...].astype(f32).reshape(1, FF)
    def feed_forward(gate_s):
        for k, cols, part in blocks:
            hidden = dot(ffn_input, ffn_in_s[k][:, part]) + hidden_bias[:, cols]
            half_gate = 0.5 + 0.5 * lax.erf(hidden * math.sqrt(0.5))
            active_s[k][:, part] = (hidden * half_gate).astype(bf16)
            gate_s[:, cols] = half_gate + hidden * jnp.exp(hidden * hidden * -0.5) * (
                1.0 / math.sqrt(2.0 * math.pi)
            )
        load_ffn[2].wait()
        third_normed, third_rstd = norm_forward(
            second
            + dot(active_s[0][...], ffn_out_s[:half])
            + dot(active_s[1][...], ffn_out_s[half:])
            + ffn_out_bias[...].astype(f32).reshape(1, D)
        )
        result_out[...] = (third_normed * gain[2:3] + shift[2:3])[:NQ].astype(bf16)
        grad_third, gain_grad_2, shift_grad_2 = norm_backward(
            pad_s[2], third_normed, third_rstd, gain[2:3]
        )
        grad_branch_f = grad_third.astype(bf16)
        for k, cols, part in blocks:
            grad_hidden = dot_nt(grad_branch_f, ffn_out_s[cols]) * gate_s[:, cols]
            slope_s[k][:, part] = grad_hidden.astype(bf16)
        return grad_third, gain_grad_2, shift_grad_2, grad_branch_f

    grad_third, gain_grad_2, shift_grad_2, grad_branch_f = pl.run_scoped(
        feed_forward, pltpu.VMEM((NP, FF), f32)
    )
    grad_second = grad_third + dot_nt(slope_s[0][...], ffn_in_s[0][...])
    grad_second += dot_nt(slope_s[1][...], ffn_in_s[1][...])
    grad_second_in, gain_grad_1, shift_grad_1 = norm_backward(
        grad_second, second_normed, second_rstd, gain[1:2]
    )
    grad_branch_c = grad_second_in.astype(bf16)
    ffn_input_t = second.T.astype(bf16)

    @pl.when(member == 0)
    def _():
        for k, cols, part in blocks:
            rows_f[cols] = dot(ffn_input_t, slope_s[k][:, part]).astype(bf16)

    @pl.when(member == 1)
    def _():
        for k, cols, part in blocks:
            rows_f[cols] = dot_tn(active_s[k][:, part], grad_branch_f).astype(bf16)

    is_first = member == 0
    out_grad_c = dot_tn(attended_c, grad_branch_c)
    rows_k[2 * D : 3 * D] = jnp.where(is_first, out_grad_c, 0.0).astype(bf16)

    clear_rest(rows_f, ROWS_F)
    clear_rest(rows_t, ROWS_T)
    clear_rest(rows_k, ROWS_K)
    sum_f.phases[0]()
    grad_attended_c = dot_nt(grad_branch_c, attn_out[1]).astype(bf16).astype(f32)
    small_s[:16] = jnp.concatenate(
        [row_total(slope_s[k][:, part]) for k, _, part in blocks]
        + [
            row_total(grad_branch_f),
            row_total(grad_branch_c),
            gain_grad_2,
            shift_grad_2,
            gain_grad_1,
            shift_grad_1,
            row_total(grad_attended_c),
            jnp.zeros((1, D), f32),
        ],
        axis=0,
    )

    store_result = pltpu.make_async_copy(result_out, result_hbm, load_sem.at[7])
    store_result.start()

    grad_attended_t = grad_attended_c.T
    grad_x = spread_rows(grad_attended_c)
    grad_v = dot(attn_in[1, 2], spread_cols(grad_attended_t))
    grad_vt[...] = grad_v.astype(bf16)
    back_s[HQ:] = grad_v.T.astype(bf16)
    inner = head_line(head_sums(grad_attended_t * mixed_t))
    rows_k[D : 2 * D] = dot((mixed_s[...] * own_share).astype(bf16), grad_x).astype(bf16)
    mixed_s[...] = jnp.zeros_like(mixed_s)

    queue_f = sum_f.phases[1:]
    queue_t = list(sum_t.phases)
    queue_k = list(sum_k.phases)

    def take(queue):
        if queue:
            queue.pop(0)()

    def at(i, steps):
        for step, queue in steps:
            pl.when(i == (step * chunks) // 32)(queue.pop(0))

    def slope_block(i):
        rows = pl.ds(pl.multiple_of(i * CHUNK, CHUNK), CHUNK)
        key_ct = key_in_s[rows].T
        memory_c = memory_s[rows]
        for p in range(4):
            cols = pair_cols(p)
            grad_probs = dot(memory_c, grad_vt[:, cols])
            probs = probs_s[rows, cols].astype(f32) * factor_s[pl.ds(i, 1), cols]
            probs_s[rows, cols] = probs.astype(bf16)
            grad_scores_s[rows, cols] = (probs * (grad_probs - inner[:, cols])).astype(bf16)
        mixed_s[...] += dot(key_ct, grad_scores_s[rows])

    @pl.loop(0, chunks // 2)
    def _(i):
        slope_block(i * 2)
        slope_block(i * 2 + 1)
        at(i, [(3, queue_f), (9, queue_f), (15, queue_f)])

    send_b[...] = (project_heads(key_wt, mixed_s[...]) * scale).astype(bf16)
    swap_b = pltpu.make_async_remote_copy(
        src_ref=send_b,
        dst_ref=recv_b,
        send_sem=link_sem.at[2],
        recv_sem=link_sem.at[3],
        device_id=partner,
        device_id_type=pl.DeviceIdType.MESH,
    )
    swap_b.start()
    query_x = spread_rows(query_c.astype(f32))
    rows_k[:D] = (dot(mixed_s[...].astype(bf16), query_x) * scale).astype(bf16)
    take(queue_k)
    swap_b.wait()
    take(queue_f)
    take(queue_k)
    grad_query_c = (send_b[...].astype(f32) + recv_b[...].astype(f32)).T.astype(bf16)

    cross_pos_grad = dot_nt(grad_query_c, attn_in[1, 0])
    grad_first_in, gain_grad_0, shift_grad_0 = norm_backward(
        grad_second_in + cross_pos_grad, first_normed, first_rstd, gain[0:1]
    )
    grad_branch = grad_first_in.astype(bf16)
    grad_attended = dot_nt(grad_branch, attn_out[0]).astype(bf16).astype(f32)
    take(queue_k)
    grad_probs = dot(value_self, spread_cols(grad_attended.T))
    inner_self = jnp.sum(probs_self * grad_probs, axis=0, keepdims=True)
    grad_scores = (probs_self * (grad_probs - inner_self)).astype(bf16)
    key_t = key_self.astype(f32).T.astype(bf16)
    grad_query_s = (
        own_blocks([dot(key_t[pair_rows(p)], grad_scores[:, pair_cols(p)]) for p in range(4)]) * scale
    ).T.astype(bf16)
    grad_key_s = (dot(grad_scores, spread_rows(query_self.astype(f32))) * scale).astype(bf16)
    grad_value_s = dot(probs_self_b, spread_rows(grad_attended)).astype(bf16)
    grad_mixed_q = dot_nt(grad_query_s, attn_in[0, 0]) + dot_nt(grad_key_s, attn_in[0, 1])
    queries_grad_out[...] = (grad_first_in + grad_mixed_q + dot_nt(grad_value_s, attn_in[0, 2]))[
        :NQ
    ].astype(bf16)
    store_queries = pltpu.make_async_copy(queries_grad_out, queries_grad_hbm, load_sem.at[8])
    store_queries.start()
    small_s[16:] = jnp.concatenate(
        [
            row_total(grad_query_s),
            row_total(grad_value_s),
            row_total(grad_branch),
            row_total(grad_query_c),
            gain_grad_0,
            shift_grad_0,
            jnp.zeros((10, D), f32),
        ],
        axis=0,
    )
    @pl.when(member == 0)
    def _():
        rows_t[:D] = dot_tn(mixed_q, grad_query_s).astype(bf16)
        rows_t[D : 2 * D] = dot_tn(mixed_q, grad_key_s).astype(bf16)
        rows_t[2 * D : 3 * D] = dot_tn(queries_b, grad_value_s).astype(bf16)

    @pl.when(member == 1)
    def _():
        rows_t[:D] = dot_tn(cross_q, grad_query_c).astype(bf16)
        rows_t[D : 2 * D] = dot_tn(attended, grad_branch).astype(bf16)
        rows_t[ROW_POS:ROW_SMALL] = (grad_mixed_q + cross_pos_grad).astype(bf16)
        rows_t[ROW_SMALL : ROW_SMALL + 32] = small_s[...].astype(bf16)
        rows_t[ROW_SMALL + 32 : ROWS_T] = jnp.zeros((ROWS_T - ROW_SMALL - 32, D), bf16)

    take(queue_t)
    take(queue_k)
    take(queue_f)

    def memory_block(i):
        rows = pl.ds(pl.multiple_of(i * CHUNK, CHUNK), CHUNK)
        both = jnp.concatenate([grad_scores_s[rows], probs_s[rows]], axis=1)
        memory_s[rows] = dot(both, back_s[...]).astype(bf16)
        pltpu.make_async_copy(memory_s.at[rows], memory_grad_hbm.at[0, rows], store_sem.at[i]).start()

    @pl.loop(0, chunks // 2)
    def _(i):
        memory_block(i * 2)
        memory_block(i * 2 + 1)
        at(
            i,
            [
                (3, queue_t),
                (4, queue_k),
                (7, queue_t),
                (8, queue_k),
                (9, queue_f),
                (11, queue_t),
                (12, queue_k),
                (15, queue_t),
            ],
        )

    while queue_f:
        take(queue_f)
    stores = [
        pltpu.make_async_copy(whole, target, load_sem.at[4 + k])
        for k, (whole, target) in enumerate(
            (
                (whole_f, whole_f_hbm),
                (whole_t, whole_t_hbm),
                (whole_k, whole_k_hbm),
            )
        )
    ]
    stores[0].start()
    while queue_t or queue_k:
        take(queue_t)
        take(queue_k)
    for store in stores[1:]:
        store.start()

    @pl.loop(0, chunks)
    def _(i):
        rows = pl.ds(pl.multiple_of(i * CHUNK, CHUNK), CHUNK)
        pltpu.make_async_copy(memory_s.at[rows], memory_grad_hbm.at[0, rows], store_sem.at[i]).wait()

    for store in [*stores, store_result, store_queries]:
        store.wait()


def finish_kernel(
    result_in,
    queries_grad_in,
    memory_grad_in,
    whole_f_hbm,
    whole_t_hbm,
    whole_k_hbm,
    result_hbm,
    queries_grad_hbm,
    memory_grad,
    attn_in_hbm,
    attn_out_hbm,
    attn_bias_hbm,
    ffn_in_hbm,
    ffn_in_bias_hbm,
    ffn_out_hbm,
    ffn_out_bias_hbm,
    norm_gain_hbm,
    norm_bias_hbm,
    query_pos_hbm,
    moved,
    whole_f,
    whole_t,
    whole_k,
    result,
    queries_grad,
    attn_in_grad,
    attn_out_grad,
    attn_bias_grad,
    ffn_in_grad,
    ffn_in_bias_grad,
    ffn_out_grad,
    ffn_out_bias_grad,
    norm_gain_grad,
    norm_bias_grad,
    query_pos_grad,
    in_sem,
    out_sem,
    sum_sem,
    grad_sem,
):
    pieces = in_sem.shape[0]
    piece = moved.shape[0] // pieces

    def fetch(j):
        rows = pl.ds(piece * j, piece)
        return pltpu.make_async_copy(memory_grad_in.at[0, rows], moved.at[rows], in_sem.at[j])

    def write(j):
        rows = pl.ds(piece * j, piece)
        return pltpu.make_async_copy(moved.at[rows], memory_grad.at[0, rows], out_sem.at[j])

    sums = [
        (whole_t_hbm, whole_t),
        (whole_k_hbm, whole_k),
        (whole_f_hbm, whole_f),
        (result_in, result),
        (queries_grad_in, queries_grad),
    ]
    loads = [pltpu.make_async_copy(*pair, sum_sem.at[j]) for j, pair in enumerate(sums)]
    for load in loads:
        load.start()
    for j in range(pieces):
        fetch(j).start()
    blocks = FF // D
    stores = []

    def store(source, target):
        stores.append(pltpu.make_async_copy(source, target, grad_sem.at[len(stores)]))
        stores[-1].start()

    loads[0].wait()
    loads[1].wait()
    for j in range(3):
        attn_in_grad[0, j] = whole_t[0, D * j : D * j + D].astype(f32)
    attn_in_grad[1, 0] = whole_t[1, :D].astype(f32)
    attn_in_grad[1, 1] = whole_k[:D].astype(f32)
    attn_in_grad[1, 2] = whole_k[D : 2 * D].astype(f32)
    store(attn_in_grad, attn_in_hbm)
    attn_out_grad[0] = whole_t[1, D : 2 * D].astype(f32)
    attn_out_grad[1] = whole_k[2 * D : 3 * D].astype(f32)
    store(attn_out_grad, attn_out_hbm)
    loads[2].wait()
    for k in range(2):
        half = slice(FF // 2 * k, FF // 2 * (k + 1))
        ffn_out_grad[half] = whole_f[1, half].astype(f32)
        store(ffn_out_grad.at[half], ffn_out_hbm.at[half])
    for k in range(2):
        half = slice(FF // 2 * k, FF // 2 * (k + 1))
        for j in range(blocks // 2 * k, blocks // 2 * (k + 1)):
            at = slice(D * j, D * j + D)
            ffn_in_grad[:, at] = whole_f[0, at].astype(f32)
        store(ffn_in_grad.at[:, half], ffn_in_hbm.at[:, half])
    for j in range(pieces):
        fetch(j).wait()
        write(j).start()
    loads[3].wait()
    store(result, result_hbm.at[0])
    loads[4].wait()
    store(queries_grad, queries_grad_hbm.at[0])
    query_pos_grad[...] = whole_t[1, ROW_POS:ROW_SMALL].astype(f32)[:NQ]
    store(query_pos_grad, query_pos_hbm)
    small = whole_t[1, ROW_SMALL : ROW_SMALL + 32].astype(f32)
    ffn_in_bias_grad[...] = jnp.concatenate([small[j : j + 1] for j in range(blocks)], axis=1)
    store(ffn_in_bias_grad, ffn_in_bias_hbm)
    ffn_out_bias_grad[...] = small[8:9]
    store(ffn_out_bias_grad, ffn_out_bias_hbm)
    for j, (own, cross) in enumerate(((16, 19), (17, 14), (18, 9))):
        attn_bias_grad[j, 0:1] = small[own : own + 1]
        attn_bias_grad[j, 1:2] = small[cross : cross + 1]
    store(attn_bias_grad, attn_bias_hbm)
    for j, (gain, shift) in enumerate(((20, 21), (12, 13), (10, 11))):
        norm_gain_grad[j : j + 1] = small[gain : gain + 1]
        norm_bias_grad[j : j + 1] = small[shift : shift + 1]
    store(norm_gain_grad, norm_gain_hbm)
    store(norm_bias_grad, norm_bias_hbm)
    for j in range(pieces):
        write(j).wait()
    for copy in stores:
        copy.wait()


def body(
    pages,
    queries,
    memory,
    quarter_turns,
    token_order,
    lengths,
    attn_in,
    attn_out,
    attn_bias,
    ffn_in,
    ffn_in_bias,
    ffn_out,
    ffn_out_bias,
    norm_gain,
    norm_bias,
    query_pos,
    out_grad,
):
    tokens = memory.shape[1]
    chunks = tokens // CHUNK
    groups_f, groups_t, groups_k = sum_groups(pages)
    summed = [
        (padded(ROWS_F, pages), groups_f),
        (padded(ROWS_T, pages), groups_t),
        (padded(ROWS_K, 2 * pages), groups_k),
    ]
    whole_shapes = [(2, rows, D) for rows, _ in summed[:2]] + [(summed[2][0], D)]
    sum_buffers = []
    for (rows, groups), shape in zip(summed, whole_shapes):
        landing = PageSum.landing_rows(pages, groups, rows)
        sum_buffers += [pltpu.VMEM(each, bf16) for each in ((rows, D), (landing, D), shape)]
    copies = 32
    vmem = pl.BlockSpec(memory_space=pltpu.VMEM)
    smem = pl.BlockSpec(memory_space=pltpu.SMEM)
    anywhere = pl.BlockSpec(memory_space=pl.ANY)
    parts = pl.pallas_call(
        functools.partial(layer_kernel, tokens, pages),
        out_shape=[
            jax.ShapeDtypeStruct((NQ, D), bf16),
            jax.ShapeDtypeStruct((NQ, D), bf16),
            jax.ShapeDtypeStruct((1, tokens, D), bf16),
            *(jax.ShapeDtypeStruct(shape, bf16) for shape in whole_shapes),
        ],
        in_specs=[
            vmem,
            anywhere,
            smem,
            vmem,
            smem,
            vmem,
            vmem,
            vmem,
            anywhere,
            vmem,
            anywhere,
            vmem,
            vmem,
            vmem,
            vmem,
            vmem,
            vmem,
        ],
        out_specs=[anywhere] * 6,
        scratch_shapes=[
            pltpu.VMEM((tokens, D), bf16),
            pltpu.VMEM((tokens, D), bf16),
            pltpu.VMEM((tokens, HQ), bf16),
            pltpu.VMEM((tokens, HQ), bf16),
            pltpu.VMEM((1, tokens), f32),
            pltpu.VMEM((D, HQ), bf16),
            pltpu.VMEM((D, HQ), bf16),
            pltpu.VMEM((2 * HQ, D), bf16),
            pltpu.VMEM((4 * SIDE, D), bf16),
            pltpu.VMEM((8, HQ), f32),
            pltpu.VMEM((8, HQ), f32),
            pltpu.VMEM((chunks, HQ), f32),
            pltpu.VMEM((chunks, HQ), f32),
            pltpu.VMEM((8, HQ), f32),
            pltpu.VMEM((D, HQ), f32),
            pltpu.VMEM((3, NP, D), f32),
            pltpu.VMEM((NQ, D), bf16),
            pltpu.VMEM((NQ, D), bf16),
            pltpu.VMEM((D, NP), bf16),
            pltpu.VMEM((D, NP), bf16),
            pltpu.VMEM((2 * HEADS, NP), f32),
            pltpu.VMEM((2 * HEADS, NP), f32),
            pltpu.VMEM((D, NP), bf16),
            pltpu.VMEM((D, NP), bf16),
            pltpu.VMEM((32, D), f32),
            *sum_buffers,
            pltpu.SemaphoreType.DMA((9,)),
            pltpu.SemaphoreType.DMA((chunks,)),
            pltpu.SemaphoreType.DMA((6,)),
            *[pltpu.SemaphoreType.DMA((copies,))] * 6,
        ],
        compiler_params=pltpu.CompilerParams(
            collective_id=0, has_side_effects=True, vmem_limit_bytes=127 * 512 * 1024
        ),
        cost_estimate=pl.CostEstimate(
            flops=2 * 8 * tokens * HQ * D, bytes_accessed=20 << 20, transcendentals=tokens * HQ
        ),
        name="decoder_layer",
    )(
        queries,
        memory,
        quarter_turns,
        token_order,
        lengths,
        attn_in,
        attn_out,
        attn_bias.transpose(1, 0, 2),
        ffn_in,
        ffn_in_bias,
        ffn_out,
        ffn_out_bias,
        norm_gain,
        norm_bias,
        query_pos,
        out_grad,
        jnp.asarray(position_table()),
    )
    outs = pl.pallas_call(
        finish_kernel,
        out_shape=[
            jax.ShapeDtypeStruct((1, NQ, D), bf16),
            jax.ShapeDtypeStruct((1, NQ, D), bf16),
            jax.ShapeDtypeStruct((1, tokens, D), bf16),
            jax.ShapeDtypeStruct((2, 3, D, D), f32),
            jax.ShapeDtypeStruct((2, D, D), f32),
            jax.ShapeDtypeStruct((3, 2, D), f32),
            jax.ShapeDtypeStruct((D, FF), f32),
            jax.ShapeDtypeStruct((1, FF), f32),
            jax.ShapeDtypeStruct((FF, D), f32),
            jax.ShapeDtypeStruct((1, D), f32),
            jax.ShapeDtypeStruct((3, D), f32),
            jax.ShapeDtypeStruct((3, D), f32),
            jax.ShapeDtypeStruct((NQ, D), f32),
        ],
        in_specs=[anywhere] * 6,
        out_specs=[anywhere] * 13,
        scratch_shapes=[
            pltpu.VMEM((tokens, D), bf16),
            *(pltpu.VMEM(shape, bf16) for shape in whole_shapes),
            pltpu.VMEM((NQ, D), bf16),
            pltpu.VMEM((NQ, D), bf16),
            pltpu.VMEM((2, 3, D, D), f32),
            pltpu.VMEM((2, D, D), f32),
            pltpu.VMEM((3, 2, D), f32),
            pltpu.VMEM((D, FF), f32),
            pltpu.VMEM((1, FF), f32),
            pltpu.VMEM((FF, D), f32),
            pltpu.VMEM((1, D), f32),
            pltpu.VMEM((3, D), f32),
            pltpu.VMEM((3, D), f32),
            pltpu.VMEM((NQ, D), f32),
            pltpu.SemaphoreType.DMA((8,)),
            pltpu.SemaphoreType.DMA((8,)),
            pltpu.SemaphoreType.DMA((5,)),
            pltpu.SemaphoreType.DMA((14,)),
        ],
        compiler_params=pltpu.CompilerParams(vmem_limit_bytes=62 * 1024 * 1024),
        name="write_outputs",
    )(*parts)
    return (
        *outs[:5],
        outs[5].transpose(1, 0, 2),
        outs[6],
        outs[7].reshape(FF),
        outs[8],
        outs[9].reshape(D),
        *outs[10:],
    )


def solution(mesh):
    in_specs = (
        P("dp", None, None),
        P("dp", "blk", None),
        P("dp"),
        P("dp", "blk"),
        P("dp"),
        P(),
        P(),
        P(),
        P(),
        P(),
        P(),
        P(),
        P(),
        P(),
        P(),
        P("dp", None, None),
    )
    out_specs = (
        P("dp", None, None),
        P("dp", None, None),
        P("dp", "blk", None),
        P(),
        P(),
        P(),
        P(),
        P(),
        P(),
        P(),
        P(),
        P(),
        P(),
    )
    layer = functools.partial(body, mesh.shape["dp"])
    return jax.shard_map(layer, mesh=mesh, in_specs=in_specs, out_specs=out_specs, check_vma=False)
```

```python
import functools
import math

import jax
import jax.numpy as jnp
import numpy as np
from jax import lax
from jax.experimental import pallas as pl
from jax.experimental.pallas import tpu as pltpu
from jax.sharding import PartitionSpec as P

D = 256
HEADS = 8
HD = D // HEADS
SIDE = 128
NQ = 125
NP = 128
HQ = HEADS * NP
PAIR = 2 * NP
FF = 2048
CHUNK = 1024

masked_score = -1e30
norm_eps = 1e-05
scale = 1.0 / math.sqrt(HD)
log2e = math.log2(math.e)

bf16 = jnp.bfloat16
f32 = jnp.float32

ROWS_F = FF
ROW_POS = 2 * D
ROW_SMALL = 2 * D + NP
ROWS_T = 3 * D
ROWS_K = 3 * D
TILE = 16


def axes_of(pages):
    axes = {"core": (2, 1), "y": (2, 2)}
    stride = 4
    while stride < pages:
        radix = 4 if pages // stride % 4 == 0 else 2
        axes["z%d" % (len(axes) - 2)] = (radix, stride)
        stride *= radix
    axes["x"] = (2, 0)
    return axes


def far_axes(pages):
    return [(name,) for name in axes_of(pages) if name.startswith("z")]


def sum_groups(pages):
    far = far_axes(pages)
    return [("core",), ("y",), *far], [("core", "y"), *far], [("core",), ("x",), ("y",), *far]


def padded(rows, pages):
    unit = TILE * pages
    return (rows + unit - 1) // unit * unit


def position_table():
    half = D // 2
    channel = np.arange(half)
    inverse = np.exp((channel // 2).astype(np.float32) * np.float32(-2.0 * math.log(10000.0) / half))
    angle = (np.arange(SIDE, dtype=np.float32) + 1.0) * np.float32(2.0 * math.pi / SIDE)
    angle = angle[:, None] * inverse
    return np.where(channel % 2 == 0, np.sin(angle), np.cos(angle)).astype(np.float32)


def dot(a, b):
    return jnp.dot(a, b, preferred_element_type=f32)


def dot_nt(a, b):
    return lax.dot_general(a, b, (((1,), (1,)), ((), ())), preferred_element_type=f32)


def dot_tn(a, b):
    return lax.dot_general(a, b, (((0,), (0,)), ((), ())), preferred_element_type=f32)


def row_total(values):
    return jnp.sum(values.astype(f32), axis=0, keepdims=True)


def norm_forward(values):
    average = jnp.mean(values, axis=-1, keepdims=True)
    centred = values - average
    variance = jnp.mean(centred * centred, axis=-1, keepdims=True)
    rstd = lax.rsqrt(variance + norm_eps)
    return centred * rstd, rstd


def norm_backward(grad, normed, rstd, gain):
    grad_normed = grad * gain
    first = jnp.mean(grad_normed, axis=-1, keepdims=True)
    second = jnp.mean(grad_normed * normed, axis=-1, keepdims=True)
    grad_in = rstd * (grad_normed - first - normed * second)
    return grad_in, row_total(grad * normed), row_total(grad)


def spread_rows(rows):
    head = lax.broadcasted_iota(jnp.int32, (NP, D), 1) // HD
    return jnp.concatenate(
        [jnp.where(head == h, rows, 0.0) for h in range(HEADS)], axis=0
    ).astype(bf16)


def spread_cols(cols):
    head = lax.broadcasted_iota(jnp.int32, (D, NP), 0) // HD
    return jnp.concatenate(
        [jnp.where(head == h, cols, 0.0) for h in range(HEADS)], axis=1
    ).astype(bf16)


def project_heads(weight_t, sums):
    high = sums.astype(bf16)
    low = (sums - high.astype(f32)).astype(bf16)
    return own_blocks(
        [
            dot(weight_t[pair_rows(p)], high[:, pair_cols(p)])
            + dot(weight_t[pair_rows(p)], low[:, pair_cols(p)])
            for p in range(4)
        ]
    )


def own_blocks(pairs):
    parts = []
    for pair in pairs:
        parts += [pair[:HD, :NP], pair[HD:, NP:]]
    return jnp.concatenate(parts, axis=0)


def head_rows(row):
    return jnp.concatenate([row[:, NP * h : NP * h + NP] for h in range(HEADS)], axis=0)


def head_line(rows):
    return jnp.concatenate([rows[h : h + 1] for h in range(HEADS)], axis=1)


def per_channel(rows):
    return jnp.concatenate(
        [jnp.broadcast_to(rows[h : h + 1], (HD, NP)) for h in range(HEADS)], axis=0
    )


def head_sums(cols):
    return jnp.concatenate(
        [jnp.sum(cols[HD * h : HD * h + HD], axis=0, keepdims=True) for h in range(HEADS)], axis=0
    )


def pair_cols(p):
    return slice(PAIR * p, PAIR * p + PAIR)


def pair_rows(p):
    return slice(2 * HD * p, 2 * HD * p + 2 * HD)


class Place:
    def __init__(self, pages):
        self.axes = axes_of(pages)
        self.page = lax.axis_index("dp")
        self.member = lax.axis_index("blk")
        self.digit = {
            name: self.member if name == "x" else lax.rem(self.page // stride, radix)
            for name, (radix, stride) in self.axes.items()
        }

    def size(self, group):
        return math.prod(self.axes[name][0] for name in group)

    def index(self, group):
        index = 0
        for name in group:
            index = index * self.axes[name][0] + self.digit[name]
        return index

    def peer(self, group, hop):
        index = lax.rem(self.index(group) + hop, self.size(group))
        page, member, rest = self.page, self.member, index
        for name in reversed(group):
            radix, stride = self.axes[name]
            digit = lax.rem(rest, radix)
            rest = rest // radix
            if name == "x":
                member = digit
            else:
                page = page + (digit - self.digit[name]) * stride
        return (page, member), index


class PageSum:
    def __init__(self, place, groups, back, rows, landing, whole, sent, arrived):
        self.place, self.groups, self.back = place, groups, back
        self.rows, self.landing, self.whole = rows, landing, whole
        self.sent, self.arrived = sent, arrived
        self.slots = 0
        self.extents = [rows.shape[0]]
        self.bases = [0]
        self.landings = []
        at = 0
        for group in groups:
            size = place.size(group)
            extent = self.extents[-1] // size
            self.landings.append(at)
            at += (size - 1) * extent
            self.bases.append(pl.multiple_of(self.bases[-1] + place.index(group) * extent, TILE))
            self.extents.append(extent)
        last = len(groups)
        moves = [self.scatter_moves(s) for s in range(last)]
        near = {"all": 0, "across": 1, "sides": 2}[back]
        moves += [self.gather_moves(s) for s in range(last - 1, near - 1, -1)]
        if back == "sides":
            moves += [self.side_moves(), self.corner_moves(), self.core_moves()]
        elif back == "across":
            moves += [self.across_moves(), self.core_moves()]
        self.phases = [functools.partial(self.step, moves, k) for k in range(len(moves) + 1)]

    @staticmethod
    def landing_rows(pages, groups, rows):
        axes = axes_of(pages)
        total, extent = 0, rows
        for group in groups:
            size = math.prod(axes[name][0] for name in group)
            extent //= size
            total += (size - 1) * extent
        return total

    def step(self, moves, k):
        last = len(self.groups)
        if k > 0:
            for move in moves[k - 1]:
                self.copy(*move).wait()
        if 0 < k <= last:
            total = self.scatter_sum(k - 1)
            region = pl.ds(self.bases[k], self.extents[k])
            if k < last:
                self.rows[region] = total
            elif len(self.whole.shape) == 3:
                self.whole[self.place.member, region] = total
            else:
                self.whole[region] = total
        if k < len(moves):
            for move in moves[k]:
                self.copy(*move).start()

    def copy(self, slot, source, target, device):
        return pltpu.make_async_remote_copy(
            src_ref=source(),
            dst_ref=target(),
            send_sem=self.sent.at[slot],
            recv_sem=self.arrived.at[slot],
            device_id=device,
            device_id_type=pl.DeviceIdType.MESH,
        )

    def new_slot(self):
        self.slots += 1
        return self.slots - 1

    def same(self, device, view):
        return (self.new_slot(), view, view, device)

    def scatter_moves(self, step):
        group = self.groups[step]
        extent = self.extents[step + 1]
        moves = []
        for hop in range(1, self.place.size(group)):
            device, other = self.place.peer(group, hop)
            start = pl.multiple_of(self.bases[step] + other * extent, TILE)
            landing = self.landings[step] + (hop - 1) * extent
            moves.append(
                (
                    self.new_slot(),
                    functools.partial(self.part, self.rows, start, extent),
                    functools.partial(self.part, self.landing, landing, extent),
                    device,
                )
            )
        return moves

    @staticmethod
    def part(ref, start, extent):
        return ref.at[pl.ds(start, extent)]

    def half(self, member, start, extent):
        if len(self.whole.shape) == 3:
            return self.whole.at[member, pl.ds(start, extent)]
        return self.whole.at[pl.ds(start, extent)]

    def scatter_sum(self, step):
        extent = self.extents[step + 1]
        total = self.rows[pl.ds(self.bases[step + 1], extent)].astype(f32)
        for hop in range(1, self.place.size(self.groups[step])):
            landing = self.landings[step] + (hop - 1) * extent
            total = total + self.landing[pl.ds(landing, extent)].astype(f32)
        return total.astype(bf16)

    def gather_moves(self, step):
        group = self.groups[step]
        view = functools.partial(self.half, self.place.member, self.bases[step + 1], self.extents[step + 1])
        return [
            self.same(self.place.peer(group, hop)[0], view) for hop in range(1, self.place.size(group))
        ]

    def own_quarter(self):
        step = 2 if len(self.groups[0]) == 1 else 1
        return self.bases[step], self.extents[step]

    def side_moves(self):
        view = functools.partial(self.half, self.place.member, *self.own_quarter())
        return [self.same(self.place.peer((name,), 1)[0], view) for name in ("y", "x")]

    def corner_moves(self):
        base, extent = self.own_quarter()
        other = pl.multiple_of(base + (1 - 2 * self.place.digit["y"]) * extent, TILE)
        view = functools.partial(self.half, self.place.member, other, extent)
        return [self.same(self.place.peer(("x",), 1)[0], view)]

    def across_moves(self):
        view = functools.partial(self.half, self.place.member, *self.own_quarter())
        return [self.same(self.place.peer(("x", "y"), hop)[0], view) for hop in range(1, 4)]

    def core_moves(self):
        extent = self.extents[0] // 2
        start = pl.multiple_of(self.place.digit["core"] * extent, TILE)
        device, _ = self.place.peer(("core",), 1)
        return [self.same(device, functools.partial(self.half, m, start, extent)) for m in range(2)]


def clear_rest(ref, used):
    if ref.shape[0] > used:
        ref[used:] = jnp.zeros((ref.shape[0] - used, D), ref.dtype)


def layer_kernel(
    tokens,
    pages,
    queries_in,
    memory_hbm,
    turns_in,
    order_in,
    lengths_in,
    attn_in,
    attn_out,
    attn_bias,
    ffn_in_hbm,
    ffn_in_bias,
    ffn_out_hbm,
    ffn_out_bias,
    norm_gain,
    norm_bias,
    pos_in,
    out_grad_in,
    table_in,
    result_hbm,
    queries_grad_hbm,
    memory_grad_hbm,
    whole_f_hbm,
    whole_t_hbm,
    whole_k_hbm,
    memory_s,
    key_in_s,
    probs_s,
    grad_scores_s,
    code_s,
    query_kt,
    grad_vt,
    back_s,
    table_s,
    top_s,
    highest_s,
    shifts_s,
    factor_s,
    total_s,
    mixed_s,
    pad_s,
    result_out,
    queries_grad_out,
    send_a,
    recv_a,
    send_t,
    recv_t,
    send_b,
    recv_b,
    small_s,
    rows_f,
    landing_f,
    whole_f,
    rows_t,
    landing_t,
    whole_t,
    rows_k,
    landing_k,
    whole_k,
    load_sem,
    store_sem,
    link_sem,
    sent_f,
    arrived_f,
    sent_t,
    arrived_t,
    sent_k,
    arrived_k,
):
    member = lax.axis_index("blk")
    partner = (lax.axis_index("dp"), 1 - member)
    chunks = tokens // CHUNK

    place = Place(pages)
    groups_f, groups_t, groups_k = sum_groups(pages)
    sum_f = PageSum(place, groups_f, "sides", rows_f, landing_f, whole_f, sent_f, arrived_f)
    sum_t = PageSum(place, groups_t, "across", rows_t, landing_t, whole_t, sent_t, arrived_t)
    sum_k = PageSum(place, groups_k, "all", rows_k, landing_k, whole_k, sent_k, arrived_k)

    barrier = pltpu.get_barrier_semaphore()
    peers = [
        place.peer(group, hop)[0]
        for group in [("x", "core", "y"), *far_axes(pages)]
        for hop in range(1, place.size(group))
    ]
    for peer in peers:
        pl.semaphore_signal(barrier, inc=1, device_id=peer, device_id_type=pl.DeviceIdType.MESH)

    load_memory = pltpu.make_async_copy(memory_hbm.at[0], memory_s, load_sem.at[0])
    half = FF // 2
    ffn_in_s = [grad_scores_s.at[D * k : D * k + D] for k in range(2)]
    ffn_out_s = grad_scores_s.at[2 * D : 2 * D + FF, :D]
    free = 2 * D + FF
    active_s = [grad_scores_s.at[free + NP * k : free + NP * k + NP] for k in range(2)]
    slope_s = [grad_scores_s.at[free + NP * k : free + NP * k + NP] for k in range(2, 4)]
    load_ffn = [
        pltpu.make_async_copy(ffn_in_hbm.at[:, half * k : half * k + half], ffn_in_s[k], load_sem.at[1 + k])
        for k in range(2)
    ]
    load_ffn.append(pltpu.make_async_copy(ffn_out_hbm, ffn_out_s, load_sem.at[3]))
    load_memory.start()
    for load in load_ffn:
        load.start()

    pairs = [attn_bias[j].astype(f32) for j in range(3)]
    bias = jnp.concatenate([pair[k : k + 1] for k in range(2) for pair in pairs], axis=0)
    gain = norm_gain[...].astype(f32)
    shift = norm_bias[...].astype(f32)

    order = order_in[...]
    turn = turns_in[0]
    row_at = order >> 7
    col_at = order & 127
    top = SIDE - 1
    row_new = jnp.where(
        turn == 0, row_at, jnp.where(turn == 1, col_at, jnp.where(turn == 2, top - row_at, top - col_at))
    )
    col_new = jnp.where(
        turn == 0, col_at, jnp.where(turn == 1, top - row_at, jnp.where(turn == 2, top - col_at, row_at))
    )
    past = jnp.where(order < lengths_in[0], 0, SIDE * SIDE)
    code_s[...] = (row_new * SIDE + col_new + past).astype(f32)

    pad_s[...] = jnp.zeros_like(pad_s)
    pad_s[0, :NQ] = queries_in[0].astype(f32)
    pad_s[1, :NQ] = pos_in[...].astype(f32)
    pad_s[2, :NQ] = out_grad_in[0].astype(f32)
    queries_f = pad_s[0]
    pos_f = pad_s[1]
    queries_b = queries_f.astype(bf16)
    mixed_q = (queries_f + pos_f).astype(bf16)
    query_self = (dot(mixed_q, attn_in[0, 0]) + bias[0:1]).astype(bf16)
    key_self = dot(mixed_q, attn_in[0, 1]).astype(bf16)
    value_self = (dot(queries_b, attn_in[0, 2]) + bias[1:2]).astype(bf16)
    scores = dot(key_self, spread_cols(query_self.astype(f32).T)) * scale
    own_key = lax.broadcasted_iota(jnp.int32, (NP, HQ), 0) < NQ
    scores = jnp.where(own_key, scores, masked_score)
    raised = jnp.exp(scores - jnp.max(scores, axis=0, keepdims=True))
    probs_self = raised / jnp.sum(raised, axis=0, keepdims=True)
    probs_self_b = probs_self.astype(bf16)
    value_t = value_self.astype(f32).T.astype(bf16)
    attended = own_blocks(
        [dot(value_t[pair_rows(p)], probs_self_b[:, pair_cols(p)]) for p in range(4)]
    ).T.astype(bf16)
    first_normed, first_rstd = norm_forward(queries_f + dot(attended, attn_out[0]) + bias[2:3])
    first = first_normed * gain[0:1] + shift[0:1]
    cross_q = (first + pos_f).astype(bf16)
    query_c = (dot(cross_q, attn_in[1, 0]) + bias[3:4]).astype(bf16)
    query_x = spread_rows(query_c.astype(f32))
    query_k = dot(attn_in[1, 1], spread_cols(query_c.astype(f32).T))
    query_kt[...] = (query_k * (scale * log2e)).astype(bf16)
    back_s[:HQ] = (dot_nt(query_x, attn_in[1, 1]) * scale).astype(bf16)
    table = table_in[...]
    nothing = jnp.zeros((SIDE, D // 2), f32)
    table = jnp.concatenate(
        [jnp.concatenate([table, nothing], axis=1), jnp.concatenate([nothing, table], axis=1)], axis=0
    )
    table_high = table.astype(bf16)
    table_s[: 2 * SIDE] = table_high
    table_s[2 * SIDE :] = (table - table_high.astype(f32)).astype(bf16)

    load_memory.wait()
    def mask_view(i):
        side, place = i // (chunks // 2), lax.rem(i, chunks // 2)
        return grad_scores_s.at[
            pl.ds(pl.multiple_of(tokens // 2 + place * CHUNK, CHUNK), CHUNK),
            pl.ds(pl.multiple_of(side * NP, NP), NP),
        ]

    lane = lax.broadcasted_iota(jnp.int32, (CHUNK, NP), 1)

    def place_block(i):
        rows = pl.ds(pl.multiple_of(i * CHUNK, CHUNK), CHUNK)
        line = code_s[:, rows]
        code = jnp.concatenate(
            [
                jnp.broadcast_to(line[:, NP * j : NP * j + NP], (NP, NP)).T
                for j in range(CHUNK // NP)
            ],
            axis=0,
        ).astype(jnp.int32)
        row_hot = jnp.where(((code >> 7) & 127) == lane, 1.0, 0.0).astype(bf16)
        col_hot = jnp.where((code & 127) == lane, 1.0, 0.0).astype(bf16)
        hot = jnp.concatenate([row_hot, col_hot, row_hot, col_hot], axis=1)
        masked = jnp.where(code < SIDE * SIDE, 0.0, masked_score)
        mask_view(i)[...] = masked.astype(bf16)
        key_in_s[rows] = (memory_s[rows].astype(f32) + dot(hot, table_s[...])).astype(bf16)

    @pl.loop(0, chunks // 4)
    def _(j):
        for k in range(4):
            place_block(j * 4 + k)

    def score_pair(p, key_in, mask, score_s):
        cols = pair_cols(p)
        part = dot(key_in, query_kt[:, cols]) + mask
        score_s[:, cols] = part
        top_s[:, cols] = jnp.max(part.reshape(CHUNK // 8, 8, PAIR), axis=0)

    def score_operands(i):
        rows = pl.ds(pl.multiple_of(i * CHUNK, CHUNK), CHUNK)
        mask = mask_view(i)[...].astype(f32)
        return key_in_s[rows], jnp.concatenate([mask, mask], axis=1)

    def attend_all(score_s):
        operands = score_operands(0)
        for p in range(4):
            score_pair(p, *operands, score_s)

        @pl.loop(0, chunks)
        def _(i):
            rows = pl.ds(pl.multiple_of(i * CHUNK, CHUNK), CHUNK)
            memory_ct = memory_s[rows].T
            operands = score_operands(jnp.minimum(i + 1, chunks - 1))
            for p in range(4):
                cols = pair_cols(p)
                before = highest_s[0:1, cols]
                highest = jnp.maximum(before, jnp.max(top_s[:, cols], axis=0, keepdims=True))
                highest_s[0:1, cols] = highest
                shifts_s[pl.ds(i, 1), cols] = highest
                fade = jnp.exp2(before - highest)
                raised = jnp.exp2(score_s[:, cols] - highest)
                sums = jnp.sum(raised.reshape(CHUNK // 8, 8, PAIR), axis=0)
                total_s[:, cols] = total_s[:, cols] * fade + sums
                probs_s[rows, cols] = raised.astype(bf16)
                mixed_s[:, cols] = mixed_s[:, cols] * fade + dot(memory_ct, probs_s[rows, cols])
                score_pair(p, *operands, score_s)

    highest_s[0:1] = jnp.full((1, HQ), -3e38, f32)
    total_s[...] = jnp.zeros_like(total_s)
    mixed_s[...] = jnp.zeros_like(mixed_s)
    pl.run_scoped(attend_all, pltpu.VMEM((CHUNK, HQ), f32))
    highest_own = highest_s[0:1]
    total_own = jnp.sum(total_s[...], axis=0, keepdims=True)

    value_wt = attn_in[1, 2].astype(f32).T.astype(bf16)
    key_wt = attn_in[1, 1].astype(f32).T.astype(bf16)
    send_a[...] = project_heads(value_wt, mixed_s[...]).astype(bf16)
    send_t[:HEADS] = head_rows(highest_own)
    send_t[HEADS:] = head_rows(total_own)
    pl.semaphore_wait(barrier, len(peers))
    swap_a = pltpu.make_async_remote_copy(
        src_ref=send_a,
        dst_ref=recv_a,
        send_sem=link_sem.at[0],
        recv_sem=link_sem.at[1],
        device_id=partner,
        device_id_type=pl.DeviceIdType.MESH,
    )
    swap_t = pltpu.make_async_remote_copy(
        src_ref=send_t,
        dst_ref=recv_t,
        send_sem=link_sem.at[4],
        recv_sem=link_sem.at[5],
        device_id=partner,
        device_id_type=pl.DeviceIdType.MESH,
    )
    swap_a.start()
    swap_t.start()
    swap_a.wait()
    swap_t.wait()
    is_first = member == 0
    own, other = send_a[...].astype(f32), recv_a[...].astype(f32)
    left = jnp.where(is_first, own, other)
    right = jnp.where(is_first, other, own)
    own, other = send_t[...], recv_t[...]
    left_t = jnp.where(is_first, own, other)
    right_t = jnp.where(is_first, other, own)
    highest = jnp.maximum(left_t[:HEADS], right_t[:HEADS])
    fade_l = jnp.exp2(left_t[:HEADS] - highest)
    fade_r = jnp.exp2(right_t[:HEADS] - highest)
    total = left_t[HEADS:] * fade_l + right_t[HEADS:] * fade_r
    mixed_t = left * per_channel(fade_l / total) + right * per_channel(fade_r / total)
    log_total = head_line(highest + jnp.log2(total))
    own_share = jnp.exp2(highest_own - log_total)
    factor_s[...] = jnp.exp2(shifts_s[...] - log_total)
    attended_c = (mixed_t.T + bias[4:5]).astype(bf16)

    second_normed, second_rstd = norm_forward(first + dot(attended_c, attn_out[1]) + bias[5:6])
    second = second_normed * gain[1:2] + shift[1:2]
    ffn_input = second.astype(bf16)
    load_ffn[0].wait()
    load_ffn[1].wait()
    blocks = [(j // 4, slice(D * j, D * j + D), slice(j % 4 * D, j % 4 * D + D)) for j in range(FF // D)]
    hidden_bias = ffn_in_bias[...].astype(f32).reshape(1, FF)
    def feed_forward(gate_s):
        for k, cols, part in blocks:
            hidden = dot(ffn_input, ffn_in_s[k][:, part]) + hidden_bias[:, cols]
            half_gate = 0.5 + 0.5 * lax.erf(hidden * math.sqrt(0.5))
            active_s[k][:, part] = (hidden * half_gate).astype(bf16)
            gate_s[:, cols] = half_gate + hidden * jnp.exp(hidden * hidden * -0.5) * (
                1.0 / math.sqrt(2.0 * math.pi)
            )
        load_ffn[2].wait()
        third_normed, third_rstd = norm_forward(
            second
            + dot(active_s[0][...], ffn_out_s[:half])
            + dot(active_s[1][...], ffn_out_s[half:])
            + ffn_out_bias[...].astype(f32).reshape(1, D)
        )
        result_out[...] = (third_normed * gain[2:3] + shift[2:3])[:NQ].astype(bf16)
        grad_third, gain_grad_2, shift_grad_2 = norm_backward(
            pad_s[2], third_normed, third_rstd, gain[2:3]
        )
        grad_branch_f = grad_third.astype(bf16)
        for k, cols, part in blocks:
            grad_hidden = dot_nt(grad_branch_f, ffn_out_s[cols]) * gate_s[:, cols]
            slope_s[k][:, part] = grad_hidden.astype(bf16)
        return grad_third, gain_grad_2, shift_grad_2, grad_branch_f

    grad_third, gain_grad_2, shift_grad_2, grad_branch_f = pl.run_scoped(
        feed_forward, pltpu.VMEM((NP, FF), f32)
    )
    grad_second = grad_third + dot_nt(slope_s[0][...], ffn_in_s[0][...])
    grad_second += dot_nt(slope_s[1][...], ffn_in_s[1][...])
    grad_second_in, gain_grad_1, shift_grad_1 = norm_backward(
        grad_second, second_normed, second_rstd, gain[1:2]
    )
    grad_branch_c = grad_second_in.astype(bf16)
    ffn_input_t = second.T.astype(bf16)

    @pl.when(member == 0)
    def _():
        for k, cols, part in blocks:
            rows_f[cols] = dot(ffn_input_t, slope_s[k][:, part]).astype(bf16)

    @pl.when(member == 1)
    def _():
        for k, cols, part in blocks:
            rows_f[cols] = dot_tn(active_s[k][:, part], grad_branch_f).astype(bf16)

    is_first = member == 0
    out_grad_c = dot_tn(attended_c, grad_branch_c)
    rows_k[2 * D : 3 * D] = jnp.where(is_first, out_grad_c, 0.0).astype(bf16)

    clear_rest(rows_f, ROWS_F)
    clear_rest(rows_t, ROWS_T)
    clear_rest(rows_k, ROWS_K)
    sum_f.phases[0]()
    grad_attended_c = dot_nt(grad_branch_c, attn_out[1]).astype(bf16).astype(f32)
    small_s[:16] = jnp.concatenate(
        [row_total(slope_s[k][:, part]) for k, _, part in blocks]
        + [
            row_total(grad_branch_f),
            row_total(grad_branch_c),
            gain_grad_2,
            shift_grad_2,
            gain_grad_1,
            shift_grad_1,
            row_total(grad_attended_c),
            jnp.zeros((1, D), f32),
        ],
        axis=0,
    )

    store_result = pltpu.make_async_copy(result_out, result_hbm, load_sem.at[7])
    store_result.start()

    grad_attended_t = grad_attended_c.T
    grad_x = spread_rows(grad_attended_c)
    grad_v = dot(attn_in[1, 2], spread_cols(grad_attended_t))
    grad_vt[...] = grad_v.astype(bf16)
    back_s[HQ:] = grad_v.T.astype(bf16)
    inner = head_line(head_sums(grad_attended_t * mixed_t))
    rows_k[D : 2 * D] = dot((mixed_s[...] * own_share).astype(bf16), grad_x).astype(bf16)
    mixed_s[...] = jnp.zeros_like(mixed_s)

    queue_f = sum_f.phases[1:]
    queue_t = list(sum_t.phases)
    queue_k = list(sum_k.phases)

    def take(queue):
        if queue:
            queue.pop(0)()

    def at(i, steps):
        for step, queue in steps:
            pl.when(i == (step * chunks) // 32)(queue.pop(0))

    def slope_block(i):
        rows = pl.ds(pl.multiple_of(i * CHUNK, CHUNK), CHUNK)
        key_ct = key_in_s[rows].T
        memory_c = memory_s[rows]
        for p in range(4):
            cols = pair_cols(p)
            grad_probs = dot(memory_c, grad_vt[:, cols])
            probs = probs_s[rows, cols].astype(f32) * factor_s[pl.ds(i, 1), cols]
            probs_s[rows, cols] = probs.astype(bf16)
            grad_scores_s[rows, cols] = (probs * (grad_probs - inner[:, cols])).astype(bf16)
        mixed_s[...] += dot(key_ct, grad_scores_s[rows])

    @pl.loop(0, chunks // 2)
    def _(i):
        slope_block(i * 2)
        slope_block(i * 2 + 1)
        at(i, [(3, queue_f), (9, queue_f), (15, queue_f)])

    send_b[...] = (project_heads(key_wt, mixed_s[...]) * scale).astype(bf16)
    swap_b = pltpu.make_async_remote_copy(
        src_ref=send_b,
        dst_ref=recv_b,
        send_sem=link_sem.at[2],
        recv_sem=link_sem.at[3],
        device_id=partner,
        device_id_type=pl.DeviceIdType.MESH,
    )
    swap_b.start()
    query_x = spread_rows(query_c.astype(f32))
    rows_k[:D] = (dot(mixed_s[...].astype(bf16), query_x) * scale).astype(bf16)
    take(queue_k)
    swap_b.wait()
    take(queue_f)
    take(queue_k)
    grad_query_c = (send_b[...].astype(f32) + recv_b[...].astype(f32)).T.astype(bf16)

    cross_pos_grad = dot_nt(grad_query_c, attn_in[1, 0])
    grad_first_in, gain_grad_0, shift_grad_0 = norm_backward(
        grad_second_in + cross_pos_grad, first_normed, first_rstd, gain[0:1]
    )
    grad_branch = grad_first_in.astype(bf16)
    grad_attended = dot_nt(grad_branch, attn_out[0]).astype(bf16).astype(f32)
    take(queue_k)
    grad_probs = dot(value_self, spread_cols(grad_attended.T))
    inner_self = jnp.sum(probs_self * grad_probs, axis=0, keepdims=True)
    grad_scores = (probs_self * (grad_probs - inner_self)).astype(bf16)
    key_t = key_self.astype(f32).T.astype(bf16)
    grad_query_s = (
        own_blocks([dot(key_t[pair_rows(p)], grad_scores[:, pair_cols(p)]) for p in range(4)]) * scale
    ).T.astype(bf16)
    grad_key_s = (dot(grad_scores, spread_rows(query_self.astype(f32))) * scale).astype(bf16)
    grad_value_s = dot(probs_self_b, spread_rows(grad_attended)).astype(bf16)
    grad_mixed_q = dot_nt(grad_query_s, attn_in[0, 0]) + dot_nt(grad_key_s, attn_in[0, 1])
    queries_grad_out[...] = (grad_first_in + grad_mixed_q + dot_nt(grad_value_s, attn_in[0, 2]))[
        :NQ
    ].astype(bf16)
    store_queries = pltpu.make_async_copy(queries_grad_out, queries_grad_hbm, load_sem.at[8])
    store_queries.start()
    small_s[16:] = jnp.concatenate(
        [
            row_total(grad_query_s),
            row_total(grad_value_s),
            row_total(grad_branch),
            row_total(grad_query_c),
            gain_grad_0,
            shift_grad_0,
            jnp.zeros((10, D), f32),
        ],
        axis=0,
    )
    @pl.when(member == 0)
    def _():
        rows_t[:D] = dot_tn(mixed_q, grad_query_s).astype(bf16)
        rows_t[D : 2 * D] = dot_tn(mixed_q, grad_key_s).astype(bf16)
        rows_t[2 * D : 3 * D] = dot_tn(queries_b, grad_value_s).astype(bf16)

    @pl.when(member == 1)
    def _():
        rows_t[:D] = dot_tn(cross_q, grad_query_c).astype(bf16)
        rows_t[D : 2 * D] = dot_tn(attended, grad_branch).astype(bf16)
        rows_t[ROW_POS:ROW_SMALL] = (grad_mixed_q + cross_pos_grad).astype(bf16)
        rows_t[ROW_SMALL : ROW_SMALL + 32] = small_s[...].astype(bf16)
        rows_t[ROW_SMALL + 32 : ROWS_T] = jnp.zeros((ROWS_T - ROW_SMALL - 32, D), bf16)

    take(queue_t)
    take(queue_k)
    take(queue_f)

    def memory_block(i):
        rows = pl.ds(pl.multiple_of(i * CHUNK, CHUNK), CHUNK)
        both = jnp.concatenate([grad_scores_s[rows], probs_s[rows]], axis=1)
        memory_s[rows] = dot(both, back_s[...]).astype(bf16)
        pltpu.make_async_copy(memory_s.at[rows], memory_grad_hbm.at[0, rows], store_sem.at[i]).start()

    @pl.loop(0, chunks // 2)
    def _(i):
        memory_block(i * 2)
        memory_block(i * 2 + 1)
        at(
            i,
            [
                (3, queue_t),
                (4, queue_k),
                (7, queue_t),
                (8, queue_k),
                (9, queue_f),
                (11, queue_t),
                (12, queue_k),
                (15, queue_t),
            ],
        )

    while queue_f:
        take(queue_f)
    stores = [
        pltpu.make_async_copy(whole, target, load_sem.at[4 + k])
        for k, (whole, target) in enumerate(
            (
                (whole_f, whole_f_hbm),
                (whole_t, whole_t_hbm),
                (whole_k, whole_k_hbm),
            )
        )
    ]
    stores[0].start()
    while queue_t or queue_k:
        take(queue_t)
        take(queue_k)
    for store in stores[1:]:
        store.start()

    @pl.loop(0, chunks)
    def _(i):
        rows = pl.ds(pl.multiple_of(i * CHUNK, CHUNK), CHUNK)
        pltpu.make_async_copy(memory_s.at[rows], memory_grad_hbm.at[0, rows], store_sem.at[i]).wait()

    for store in [*stores, store_result, store_queries]:
        store.wait()


def finish_kernel(
    result_in,
    queries_grad_in,
    memory_grad_in,
    whole_f_hbm,
    whole_t_hbm,
    whole_k_hbm,
    result_hbm,
    queries_grad_hbm,
    memory_grad,
    attn_in_hbm,
    attn_out_hbm,
    attn_bias_hbm,
    ffn_in_hbm,
    ffn_in_bias_hbm,
    ffn_out_hbm,
    ffn_out_bias_hbm,
    norm_gain_hbm,
    norm_bias_hbm,
    query_pos_hbm,
    moved,
    whole_f,
    whole_t,
    whole_k,
    result,
    queries_grad,
    attn_in_grad,
    attn_out_grad,
    attn_bias_grad,
    ffn_in_grad,
    ffn_in_bias_grad,
    ffn_out_grad,
    ffn_out_bias_grad,
    norm_gain_grad,
    norm_bias_grad,
    query_pos_grad,
    in_sem,
    out_sem,
    sum_sem,
    grad_sem,
):
    pieces = in_sem.shape[0]
    piece = moved.shape[0] // pieces

    def fetch(j):
        rows = pl.ds(piece * j, piece)
        return pltpu.make_async_copy(memory_grad_in.at[0, rows], moved.at[rows], in_sem.at[j])

    def write(j):
        rows = pl.ds(piece * j, piece)
        return pltpu.make_async_copy(moved.at[rows], memory_grad.at[0, rows], out_sem.at[j])

    sums = [
        (whole_t_hbm, whole_t),
        (whole_k_hbm, whole_k),
        (whole_f_hbm, whole_f),
        (result_in, result),
        (queries_grad_in, queries_grad),
    ]
    loads = [pltpu.make_async_copy(*pair, sum_sem.at[j]) for j, pair in enumerate(sums)]
    for load in loads:
        load.start()
    for j in range(pieces):
        fetch(j).start()
    blocks = FF // D
    stores = []

    def store(source, target):
        stores.append(pltpu.make_async_copy(source, target, grad_sem.at[len(stores)]))
        stores[-1].start()

    loads[0].wait()
    loads[1].wait()
    for j in range(3):
        attn_in_grad[0, j] = whole_t[0, D * j : D * j + D].astype(f32)
    attn_in_grad[1, 0] = whole_t[1, :D].astype(f32)
    attn_in_grad[1, 1] = whole_k[:D].astype(f32)
    attn_in_grad[1, 2] = whole_k[D : 2 * D].astype(f32)
    store(attn_in_grad, attn_in_hbm)
    attn_out_grad[0] = whole_t[1, D : 2 * D].astype(f32)
    attn_out_grad[1] = whole_k[2 * D : 3 * D].astype(f32)
    store(attn_out_grad, attn_out_hbm)
    loads[2].wait()
    for k in range(2):
        half = slice(FF // 2 * k, FF // 2 * (k + 1))
        ffn_out_grad[half] = whole_f[1, half].astype(f32)
        store(ffn_out_grad.at[half], ffn_out_hbm.at[half])
    for k in range(2):
        half = slice(FF // 2 * k, FF // 2 * (k + 1))
        for j in range(blocks // 2 * k, blocks // 2 * (k + 1)):
            at = slice(D * j, D * j + D)
            ffn_in_grad[:, at] = whole_f[0, at].astype(f32)
        store(ffn_in_grad.at[:, half], ffn_in_hbm.at[:, half])
    for j in range(pieces):
        fetch(j).wait()
        write(j).start()
    loads[3].wait()
    store(result, result_hbm.at[0])
    loads[4].wait()
    store(queries_grad, queries_grad_hbm.at[0])
    query_pos_grad[...] = whole_t[1, ROW_POS:ROW_SMALL].astype(f32)[:NQ]
    store(query_pos_grad, query_pos_hbm)
    small = whole_t[1, ROW_SMALL : ROW_SMALL + 32].astype(f32)
    ffn_in_bias_grad[...] = jnp.concatenate([small[j : j + 1] for j in range(blocks)], axis=1)
    store(ffn_in_bias_grad, ffn_in_bias_hbm)
    ffn_out_bias_grad[...] = small[8:9]
    store(ffn_out_bias_grad, ffn_out_bias_hbm)
    for j, (own, cross) in enumerate(((16, 19), (17, 14), (18, 9))):
        attn_bias_grad[j, 0:1] = small[own : own + 1]
        attn_bias_grad[j, 1:2] = small[cross : cross + 1]
    store(attn_bias_grad, attn_bias_hbm)
    for j, (gain, shift) in enumerate(((20, 21), (12, 13), (10, 11))):
        norm_gain_grad[j : j + 1] = small[gain : gain + 1]
        norm_bias_grad[j : j + 1] = small[shift : shift + 1]
    store(norm_gain_grad, norm_gain_hbm)
    store(norm_bias_grad, norm_bias_hbm)
    for j in range(pieces):
        write(j).wait()
    for copy in stores:
        copy.wait()


def body(
    pages,
    queries,
    memory,
    quarter_turns,
    token_order,
    lengths,
    attn_in,
    attn_out,
    attn_bias,
    ffn_in,
    ffn_in_bias,
    ffn_out,
    ffn_out_bias,
    norm_gain,
    norm_bias,
    query_pos,
    out_grad,
):
    tokens = memory.shape[1]
    chunks = tokens // CHUNK
    groups_f, groups_t, groups_k = sum_groups(pages)
    summed = [
        (padded(ROWS_F, pages), groups_f),
        (padded(ROWS_T, pages), groups_t),
        (padded(ROWS_K, 2 * pages), groups_k),
    ]
    whole_shapes = [(2, rows, D) for rows, _ in summed[:2]] + [(summed[2][0], D)]
    sum_buffers = []
    for (rows, groups), shape in zip(summed, whole_shapes):
        landing = PageSum.landing_rows(pages, groups, rows)
        sum_buffers += [pltpu.VMEM(each, bf16) for each in ((rows, D), (landing, D), shape)]
    copies = 32
    vmem = pl.BlockSpec(memory_space=pltpu.VMEM)
    smem = pl.BlockSpec(memory_space=pltpu.SMEM)
    anywhere = pl.BlockSpec(memory_space=pl.ANY)
    parts = pl.pallas_call(
        functools.partial(layer_kernel, tokens, pages),
        out_shape=[
            jax.ShapeDtypeStruct((NQ, D), bf16),
            jax.ShapeDtypeStruct((NQ, D), bf16),
            jax.ShapeDtypeStruct((1, tokens, D), bf16),
            *(jax.ShapeDtypeStruct(shape, bf16) for shape in whole_shapes),
        ],
        in_specs=[
            vmem,
            anywhere,
            smem,
            vmem,
            smem,
            vmem,
            vmem,
            vmem,
            anywhere,
            vmem,
            anywhere,
            vmem,
            vmem,
            vmem,
            vmem,
            vmem,
            vmem,
        ],
        out_specs=[anywhere] * 6,
        scratch_shapes=[
            pltpu.VMEM((tokens, D), bf16),
            pltpu.VMEM((tokens, D), bf16),
            pltpu.VMEM((tokens, HQ), bf16),
            pltpu.VMEM((tokens, HQ), bf16),
            pltpu.VMEM((1, tokens), f32),
            pltpu.VMEM((D, HQ), bf16),
            pltpu.VMEM((D, HQ), bf16),
            pltpu.VMEM((2 * HQ, D), bf16),
            pltpu.VMEM((4 * SIDE, D), bf16),
            pltpu.VMEM((8, HQ), f32),
            pltpu.VMEM((8, HQ), f32),
            pltpu.VMEM((chunks, HQ), f32),
            pltpu.VMEM((chunks, HQ), f32),
            pltpu.VMEM((8, HQ), f32),
            pltpu.VMEM((D, HQ), f32),
            pltpu.VMEM((3, NP, D), f32),
            pltpu.VMEM((NQ, D), bf16),
            pltpu.VMEM((NQ, D), bf16),
            pltpu.VMEM((D, NP), bf16),
            pltpu.VMEM((D, NP), bf16),
            pltpu.VMEM((2 * HEADS, NP), f32),
            pltpu.VMEM((2 * HEADS, NP), f32),
            pltpu.VMEM((D, NP), bf16),
            pltpu.VMEM((D, NP), bf16),
            pltpu.VMEM((32, D), f32),
            *sum_buffers,
            pltpu.SemaphoreType.DMA((9,)),
            pltpu.SemaphoreType.DMA((chunks,)),
            pltpu.SemaphoreType.DMA((6,)),
            *[pltpu.SemaphoreType.DMA((copies,))] * 6,
        ],
        compiler_params=pltpu.CompilerParams(
            collective_id=0, has_side_effects=True, vmem_limit_bytes=127 * 512 * 1024
        ),
        cost_estimate=pl.CostEstimate(
            flops=2 * 8 * tokens * HQ * D, bytes_accessed=20 << 20, transcendentals=tokens * HQ
        ),
        name="decoder_layer",
    )(
        queries,
        memory,
        quarter_turns,
        token_order,
        lengths,
        attn_in,
        attn_out,
        attn_bias.transpose(1, 0, 2),
        ffn_in,
        ffn_in_bias,
        ffn_out,
        ffn_out_bias,
        norm_gain,
        norm_bias,
        query_pos,
        out_grad,
        jnp.asarray(position_table()),
    )
    outs = pl.pallas_call(
        finish_kernel,
        out_shape=[
            jax.ShapeDtypeStruct((1, NQ, D), bf16),
            jax.ShapeDtypeStruct((1, NQ, D), bf16),
            jax.ShapeDtypeStruct((1, tokens, D), bf16),
            jax.ShapeDtypeStruct((2, 3, D, D), f32),
            jax.ShapeDtypeStruct((2, D, D), f32),
            jax.ShapeDtypeStruct((3, 2, D), f32),
            jax.ShapeDtypeStruct((D, FF), f32),
            jax.ShapeDtypeStruct((1, FF), f32),
            jax.ShapeDtypeStruct((FF, D), f32),
            jax.ShapeDtypeStruct((1, D), f32),
            jax.ShapeDtypeStruct((3, D), f32),
            jax.ShapeDtypeStruct((3, D), f32),
            jax.ShapeDtypeStruct((NQ, D), f32),
        ],
        in_specs=[anywhere] * 6,
        out_specs=[anywhere] * 13,
        scratch_shapes=[
            pltpu.VMEM((tokens, D), bf16),
            *(pltpu.VMEM(shape, bf16) for shape in whole_shapes),
            pltpu.VMEM((NQ, D), bf16),
            pltpu.VMEM((NQ, D), bf16),
            pltpu.VMEM((2, 3, D, D), f32),
            pltpu.VMEM((2, D, D), f32),
            pltpu.VMEM((3, 2, D), f32),
            pltpu.VMEM((D, FF), f32),
            pltpu.VMEM((1, FF), f32),
            pltpu.VMEM((FF, D), f32),
            pltpu.VMEM((1, D), f32),
            pltpu.VMEM((3, D), f32),
            pltpu.VMEM((3, D), f32),
            pltpu.VMEM((NQ, D), f32),
            pltpu.SemaphoreType.DMA((8,)),
            pltpu.SemaphoreType.DMA((8,)),
            pltpu.SemaphoreType.DMA((5,)),
            pltpu.SemaphoreType.DMA((14,)),
        ],
        compiler_params=pltpu.CompilerParams(vmem_limit_bytes=62 * 1024 * 1024),
        name="write_outputs",
    )(*parts)
    return (
        *outs[:5],
        outs[5].transpose(1, 0, 2),
        outs[6],
        outs[7].reshape(FF),
        outs[8],
        outs[9].reshape(D),
        *outs[10:],
    )


def solution(mesh):
    in_specs = (
        P("dp", None, None),
        P("dp", "blk", None),
        P("dp"),
        P("dp", "blk"),
        P("dp"),
        P(),
        P(),
        P(),
        P(),
        P(),
        P(),
        P(),
        P(),
        P(),
        P(),
        P("dp", None, None),
    )
    out_specs = (
        P("dp", None, None),
        P("dp", None, None),
        P("dp", "blk", None),
        P(),
        P(),
        P(),
        P(),
        P(),
        P(),
        P(),
        P(),
        P(),
        P(),
    )
    layer = functools.partial(body, mesh.shape["dp"])
    return jax.shard_map(layer, mesh=mesh, in_specs=in_specs, out_specs=out_specs, check_vma=False)
```

```python
import functools
import math

import jax
import jax.numpy as jnp
import numpy as np
from jax import lax
from jax.experimental import pallas as pl
from jax.experimental.pallas import tpu as pltpu
from jax.sharding import PartitionSpec as P

D = 256
HEADS = 8
HD = D // HEADS
SIDE = 128
NQ = 125
NP = 128
HQ = HEADS * NP
PAIR = 2 * NP
FF = 2048
CHUNK = 1024

masked_score = -1e30
norm_eps = 1e-05
scale = 1.0 / math.sqrt(HD)
log2e = math.log2(math.e)

bf16 = jnp.bfloat16
f32 = jnp.float32

ROWS_F = FF
ROW_POS = 2 * D
ROW_SMALL = 2 * D + NP
ROWS_T = 3 * D
ROWS_K = 3 * D
TILE = 16


def axes_of(pages):
    axes = {"core": (2, 1), "y": (2, 2)}
    stride = 4
    while stride < pages:
        radix = 4 if pages // stride % 4 == 0 else 2
        axes["z%d" % (len(axes) - 2)] = (radix, stride)
        stride *= radix
    axes["x"] = (2, 0)
    return axes


def far_axes(pages):
    return [(name,) for name in axes_of(pages) if name.startswith("z")]


def sum_groups(pages):
    far = far_axes(pages)
    return [("core",), ("y",), *far], [("core", "y"), *far], [("core",), ("x",), ("y",), *far]


def padded(rows, pages):
    unit = TILE * pages
    return (rows + unit - 1) // unit * unit


def position_table():
    half = D // 2
    channel = np.arange(half)
    inverse = np.exp((channel // 2).astype(np.float32) * np.float32(-2.0 * math.log(10000.0) / half))
    angle = (np.arange(SIDE, dtype=np.float32) + 1.0) * np.float32(2.0 * math.pi / SIDE)
    angle = angle[:, None] * inverse
    return np.where(channel % 2 == 0, np.sin(angle), np.cos(angle)).astype(np.float32)


def dot(a, b):
    return jnp.dot(a, b, preferred_element_type=f32)


def dot_nt(a, b):
    return lax.dot_general(a, b, (((1,), (1,)), ((), ())), preferred_element_type=f32)


def dot_tn(a, b):
    return lax.dot_general(a, b, (((0,), (0,)), ((), ())), preferred_element_type=f32)


def row_total(values):
    return jnp.sum(values.astype(f32), axis=0, keepdims=True)


def norm_forward(values):
    average = jnp.mean(values, axis=-1, keepdims=True)
    centred = values - average
    variance = jnp.mean(centred * centred, axis=-1, keepdims=True)
    rstd = lax.rsqrt(variance + norm_eps)
    return centred * rstd, rstd


def norm_backward(grad, normed, rstd, gain):
    grad_normed = grad * gain
    first = jnp.mean(grad_normed, axis=-1, keepdims=True)
    second = jnp.mean(grad_normed * normed, axis=-1, keepdims=True)
    grad_in = rstd * (grad_normed - first - normed * second)
    return grad_in, row_total(grad * normed), row_total(grad)


def spread_rows(rows):
    head = lax.broadcasted_iota(jnp.int32, (NP, D), 1) // HD
    return jnp.concatenate(
        [jnp.where(head == h, rows, 0.0) for h in range(HEADS)], axis=0
    ).astype(bf16)


def spread_cols(cols):
    head = lax.broadcasted_iota(jnp.int32, (D, NP), 0) // HD
    return jnp.concatenate(
        [jnp.where(head == h, cols, 0.0) for h in range(HEADS)], axis=1
    ).astype(bf16)


def project_heads(weight_t, sums):
    high = sums.astype(bf16)
    low = (sums - high.astype(f32)).astype(bf16)
    return own_blocks(
        [
            dot(weight_t[pair_rows(p)], high[:, pair_cols(p)])
            + dot(weight_t[pair_rows(p)], low[:, pair_cols(p)])
            for p in range(4)
        ]
    )


def own_blocks(pairs):
    parts = []
    for pair in pairs:
        parts += [pair[:HD, :NP], pair[HD:, NP:]]
    return jnp.concatenate(parts, axis=0)


def head_rows(row):
    return jnp.concatenate([row[:, NP * h : NP * h + NP] for h in range(HEADS)], axis=0)


def head_line(rows):
    return jnp.concatenate([rows[h : h + 1] for h in range(HEADS)], axis=1)


def per_channel(rows):
    return jnp.concatenate(
        [jnp.broadcast_to(rows[h : h + 1], (HD, NP)) for h in range(HEADS)], axis=0
    )


def head_sums(cols):
    return jnp.concatenate(
        [jnp.sum(cols[HD * h : HD * h + HD], axis=0, keepdims=True) for h in range(HEADS)], axis=0
    )


def pair_cols(p):
    return slice(PAIR * p, PAIR * p + PAIR)


def pair_rows(p):
    return slice(2 * HD * p, 2 * HD * p + 2 * HD)


class Place:
    def __init__(self, pages):
        self.axes = axes_of(pages)
        self.page = lax.axis_index("dp")
        self.member = lax.axis_index("blk")
        self.digit = {
            name: self.member if name == "x" else lax.rem(self.page // stride, radix)
            for name, (radix, stride) in self.axes.items()
        }

    def size(self, group):
        return math.prod(self.axes[name][0] for name in group)

    def index(self, group):
        index = 0
        for name in group:
            index = index * self.axes[name][0] + self.digit[name]
        return index

    def peer(self, group, hop):
        index = lax.rem(self.index(group) + hop, self.size(group))
        page, member, rest = self.page, self.member, index
        for name in reversed(group):
            radix, stride = self.axes[name]
            digit = lax.rem(rest, radix)
            rest = rest // radix
            if name == "x":
                member = digit
            else:
                page = page + (digit - self.digit[name]) * stride
        return (page, member), index


class PageSum:
    def __init__(self, place, groups, back, rows, landing, whole, sent, arrived):
        self.place, self.groups, self.back = place, groups, back
        self.rows, self.landing, self.whole = rows, landing, whole
        self.sent, self.arrived = sent, arrived
        self.slots = 0
        self.extents = [rows.shape[0]]
        self.bases = [0]
        self.landings = []
        at = 0
        for group in groups:
            size = place.size(group)
            extent = self.extents[-1] // size
            self.landings.append(at)
            at += (size - 1) * extent
            self.bases.append(pl.multiple_of(self.bases[-1] + place.index(group) * extent, TILE))
            self.extents.append(extent)
        last = len(groups)
        moves = [self.scatter_moves(s) for s in range(last)]
        near = {"all": 0, "across": 1, "sides": 2}[back]
        moves += [self.gather_moves(s) for s in range(last - 1, near - 1, -1)]
        if back == "sides":
            moves += [self.side_moves(), self.corner_moves(), self.core_moves()]
        elif back == "across":
            moves += [self.across_moves(), self.core_moves()]
        self.phases = [functools.partial(self.step, moves, k) for k in range(len(moves) + 1)]

    @staticmethod
    def landing_rows(pages, groups, rows):
        axes = axes_of(pages)
        total, extent = 0, rows
        for group in groups:
            size = math.prod(axes[name][0] for name in group)
            extent //= size
            total += (size - 1) * extent
        return total

    def step(self, moves, k):
        last = len(self.groups)
        if k > 0:
            for move in moves[k - 1]:
                self.copy(*move).wait()
        if 0 < k <= last:
            total = self.scatter_sum(k - 1)
            region = pl.ds(self.bases[k], self.extents[k])
            if k < last:
                self.rows[region] = total
            elif len(self.whole.shape) == 3:
                self.whole[self.place.member, region] = total
            else:
                self.whole[region] = total
        if k < len(moves):
            for move in moves[k]:
                self.copy(*move).start()

    def copy(self, slot, source, target, device):
        return pltpu.make_async_remote_copy(
            src_ref=source(),
            dst_ref=target(),
            send_sem=self.sent.at[slot],
            recv_sem=self.arrived.at[slot],
            device_id=device,
            device_id_type=pl.DeviceIdType.MESH,
        )

    def new_slot(self):
        self.slots += 1
        return self.slots - 1

    def same(self, device, view):
        return (self.new_slot(), view, view, device)

    def scatter_moves(self, step):
        group = self.groups[step]
        extent = self.extents[step + 1]
        moves = []
        for hop in range(1, self.place.size(group)):
            device, other = self.place.peer(group, hop)
            start = pl.multiple_of(self.bases[step] + other * extent, TILE)
            landing = self.landings[step] + (hop - 1) * extent
            moves.append(
                (
                    self.new_slot(),
                    functools.partial(self.part, self.rows, start, extent),
                    functools.partial(self.part, self.landing, landing, extent),
                    device,
                )
            )
        return moves

    @staticmethod
    def part(ref, start, extent):
        return ref.at[pl.ds(start, extent)]

    def half(self, member, start, extent):
        if len(self.whole.shape) == 3:
            return self.whole.at[member, pl.ds(start, extent)]
        return self.whole.at[pl.ds(start, extent)]

    def scatter_sum(self, step):
        extent = self.extents[step + 1]
        total = self.rows[pl.ds(self.bases[step + 1], extent)].astype(f32)
        for hop in range(1, self.place.size(self.groups[step])):
            landing = self.landings[step] + (hop - 1) * extent
            total = total + self.landing[pl.ds(landing, extent)].astype(f32)
        return total.astype(bf16)

    def gather_moves(self, step):
        group = self.groups[step]
        view = functools.partial(self.half, self.place.member, self.bases[step + 1], self.extents[step + 1])
        return [
            self.same(self.place.peer(group, hop)[0], view) for hop in range(1, self.place.size(group))
        ]

    def own_quarter(self):
        step = 2 if len(self.groups[0]) == 1 else 1
        return self.bases[step], self.extents[step]

    def side_moves(self):
        view = functools.partial(self.half, self.place.member, *self.own_quarter())
        return [self.same(self.place.peer((name,), 1)[0], view) for name in ("y", "x")]

    def corner_moves(self):
        base, extent = self.own_quarter()
        other = pl.multiple_of(base + (1 - 2 * self.place.digit["y"]) * extent, TILE)
        view = functools.partial(self.half, self.place.member, other, extent)
        return [self.same(self.place.peer(("x",), 1)[0], view)]

    def across_moves(self):
        view = functools.partial(self.half, self.place.member, *self.own_quarter())
        return [self.same(self.place.peer(("x", "y"), hop)[0], view) for hop in range(1, 4)]

    def core_moves(self):
        extent = self.extents[0] // 2
        start = pl.multiple_of(self.place.digit["core"] * extent, TILE)
        device, _ = self.place.peer(("core",), 1)
        return [self.same(device, functools.partial(self.half, m, start, extent)) for m in range(2)]


def clear_rest(ref, used):
    if ref.shape[0] > used:
        ref[used:] = jnp.zeros((ref.shape[0] - used, D), ref.dtype)


def layer_kernel(
    tokens,
    pages,
    queries_in,
    memory_hbm,
    turns_in,
    order_in,
    lengths_in,
    attn_in,
    attn_out,
    attn_bias,
    ffn_in_hbm,
    ffn_in_bias,
    ffn_out_hbm,
    ffn_out_bias,
    norm_gain,
    norm_bias,
    pos_in,
    out_grad_in,
    table_in,
    result_hbm,
    queries_grad_hbm,
    memory_grad_hbm,
    whole_f_hbm,
    whole_t_hbm,
    whole_k_hbm,
    memory_s,
    key_in_s,
    probs_s,
    grad_scores_s,
    code_s,
    query_kt,
    grad_vt,
    back_s,
    table_s,
    top_s,
    highest_s,
    shifts_s,
    factor_s,
    total_s,
    mixed_s,
    pad_s,
    result_out,
    queries_grad_out,
    send_a,
    recv_a,
    send_t,
    recv_t,
    send_b,
    recv_b,
    small_s,
    rows_f,
    landing_f,
    whole_f,
    rows_t,
    landing_t,
    whole_t,
    rows_k,
    landing_k,
    whole_k,
    load_sem,
    store_sem,
    link_sem,
    sent_f,
    arrived_f,
    sent_t,
    arrived_t,
    sent_k,
    arrived_k,
):
    member = lax.axis_index("blk")
    partner = (lax.axis_index("dp"), 1 - member)
    chunks = tokens // CHUNK

    place = Place(pages)
    groups_f, groups_t, groups_k = sum_groups(pages)
    sum_f = PageSum(place, groups_f, "sides", rows_f, landing_f, whole_f, sent_f, arrived_f)
    sum_t = PageSum(place, groups_t, "across", rows_t, landing_t, whole_t, sent_t, arrived_t)
    sum_k = PageSum(place, groups_k, "all", rows_k, landing_k, whole_k, sent_k, arrived_k)

    barrier = pltpu.get_barrier_semaphore()
    peers = [
        place.peer(group, hop)[0]
        for group in [("x", "core", "y"), *far_axes(pages)]
        for hop in range(1, place.size(group))
    ]
    for peer in peers:
        pl.semaphore_signal(barrier, inc=1, device_id=peer, device_id_type=pl.DeviceIdType.MESH)

    load_memory = pltpu.make_async_copy(memory_hbm.at[0], memory_s, load_sem.at[0])
    half = FF // 2
    ffn_in_s = [grad_scores_s.at[D * k : D * k + D] for k in range(2)]
    ffn_out_s = grad_scores_s.at[2 * D : 2 * D + FF, :D]
    free = 2 * D + FF
    active_s = [grad_scores_s.at[free + NP * k : free + NP * k + NP] for k in range(2)]
    slope_s = [grad_scores_s.at[free + NP * k : free + NP * k + NP] for k in range(2, 4)]
    load_ffn = [
        pltpu.make_async_copy(ffn_in_hbm.at[:, half * k : half * k + half], ffn_in_s[k], load_sem.at[1 + k])
        for k in range(2)
    ]
    load_ffn.append(pltpu.make_async_copy(ffn_out_hbm, ffn_out_s, load_sem.at[3]))
    load_memory.start()
    for load in load_ffn:
        load.start()

    pairs = [attn_bias[j].astype(f32) for j in range(3)]
    bias = jnp.concatenate([pair[k : k + 1] for k in range(2) for pair in pairs], axis=0)
    gain = norm_gain[...].astype(f32)
    shift = norm_bias[...].astype(f32)

    order = order_in[...]
    turn = turns_in[0]
    row_at = order >> 7
    col_at = order & 127
    top = SIDE - 1
    row_new = jnp.where(
        turn == 0, row_at, jnp.where(turn == 1, col_at, jnp.where(turn == 2, top - row_at, top - col_at))
    )
    col_new = jnp.where(
        turn == 0, col_at, jnp.where(turn == 1, top - row_at, jnp.where(turn == 2, top - col_at, row_at))
    )
    past = jnp.where(order < lengths_in[0], 0, SIDE * SIDE)
    code_s[...] = (row_new * SIDE + col_new + past).astype(f32)

    pad_s[...] = jnp.zeros_like(pad_s)
    pad_s[0, :NQ] = queries_in[0].astype(f32)
    pad_s[1, :NQ] = pos_in[...].astype(f32)
    pad_s[2, :NQ] = out_grad_in[0].astype(f32)
    queries_f = pad_s[0]
    pos_f = pad_s[1]
    queries_b = queries_f.astype(bf16)
    mixed_q = (queries_f + pos_f).astype(bf16)
    query_self = (dot(mixed_q, attn_in[0, 0]) + bias[0:1]).astype(bf16)
    key_self = dot(mixed_q, attn_in[0, 1]).astype(bf16)
    value_self = (dot(queries_b, attn_in[0, 2]) + bias[1:2]).astype(bf16)
    scores = dot(key_self, spread_cols(query_self.astype(f32).T)) * scale
    own_key = lax.broadcasted_iota(jnp.int32, (NP, HQ), 0) < NQ
    scores = jnp.where(own_key, scores, masked_score)
    raised = jnp.exp(scores - jnp.max(scores, axis=0, keepdims=True))
    probs_self = raised / jnp.sum(raised, axis=0, keepdims=True)
    probs_self_b = probs_self.astype(bf16)
    value_t = value_self.astype(f32).T.astype(bf16)
    attended = own_blocks(
        [dot(value_t[pair_rows(p)], probs_self_b[:, pair_cols(p)]) for p in range(4)]
    ).T.astype(bf16)
    first_normed, first_rstd = norm_forward(queries_f + dot(attended, attn_out[0]) + bias[2:3])
    first = first_normed * gain[0:1] + shift[0:1]
    cross_q = (first + pos_f).astype(bf16)
    query_c = (dot(cross_q, attn_in[1, 0]) + bias[3:4]).astype(bf16)
    query_x = spread_rows(query_c.astype(f32))
    query_k = dot(attn_in[1, 1], spread_cols(query_c.astype(f32).T))
    query_kt[...] = (query_k * (scale * log2e)).astype(bf16)
    back_s[:HQ] = (dot_nt(query_x, attn_in[1, 1]) * scale).astype(bf16)
    table = table_in[...]
    nothing = jnp.zeros((SIDE, D // 2), f32)
    table = jnp.concatenate(
        [jnp.concatenate([table, nothing], axis=1), jnp.concatenate([nothing, table], axis=1)], axis=0
    )
    table_high = table.astype(bf16)
    table_s[: 2 * SIDE] = table_high
    table_s[2 * SIDE :] = (table - table_high.astype(f32)).astype(bf16)

    load_memory.wait()
    def mask_view(i):
        side, place = i // (chunks // 2), lax.rem(i, chunks // 2)
        return grad_scores_s.at[
            pl.ds(pl.multiple_of(tokens // 2 + place * CHUNK, CHUNK), CHUNK),
            pl.ds(pl.multiple_of(side * NP, NP), NP),
        ]

    lane = lax.broadcasted_iota(jnp.int32, (CHUNK, NP), 1)

    def place_block(i):
        rows = pl.ds(pl.multiple_of(i * CHUNK, CHUNK), CHUNK)
        line = code_s[:, rows]
        code = jnp.concatenate(
            [
                jnp.broadcast_to(line[:, NP * j : NP * j + NP], (NP, NP)).T
                for j in range(CHUNK // NP)
            ],
            axis=0,
        ).astype(jnp.int32)
        row_hot = jnp.where(((code >> 7) & 127) == lane, 1.0, 0.0).astype(bf16)
        col_hot = jnp.where((code & 127) == lane, 1.0, 0.0).astype(bf16)
        hot = jnp.concatenate([row_hot, col_hot, row_hot, col_hot], axis=1)
        masked = jnp.where(code < SIDE * SIDE, 0.0, masked_score)
        mask_view(i)[...] = masked.astype(bf16)
        key_in_s[rows] = (memory_s[rows].astype(f32) + dot(hot, table_s[...])).astype(bf16)

    @pl.loop(0, chunks // 4)
    def _(j):
        for k in range(4):
            place_block(j * 4 + k)

    def score_pair(p, key_in, mask, score_s):
        cols = pair_cols(p)
        part = dot(key_in, query_kt[:, cols]) + mask
        score_s[:, cols] = part
        top_s[:, cols] = jnp.max(part.reshape(CHUNK // 8, 8, PAIR), axis=0)

    def score_operands(i):
        rows = pl.ds(pl.multiple_of(i * CHUNK, CHUNK), CHUNK)
        mask = mask_view(i)[...].astype(f32)
        return key_in_s[rows], jnp.concatenate([mask, mask], axis=1)

    def attend_all(score_s):
        operands = score_operands(0)
        for p in range(4):
            score_pair(p, *operands, score_s)

        @pl.loop(0, chunks)
        def _(i):
            rows = pl.ds(pl.multiple_of(i * CHUNK, CHUNK), CHUNK)
            memory_ct = memory_s[rows].T
            operands = score_operands(jnp.minimum(i + 1, chunks - 1))
            for p in range(4):
                cols = pair_cols(p)
                before = highest_s[0:1, cols]
                highest = jnp.maximum(before, jnp.max(top_s[:, cols], axis=0, keepdims=True))
                highest_s[0:1, cols] = highest
                shifts_s[pl.ds(i, 1), cols] = highest
                fade = jnp.exp2(before - highest)
                raised = jnp.exp2(score_s[:, cols] - highest)
                sums = jnp.sum(raised.reshape(CHUNK // 8, 8, PAIR), axis=0)
                total_s[:, cols] = total_s[:, cols] * fade + sums
                probs_s[rows, cols] = raised.astype(bf16)
                mixed_s[:, cols] = mixed_s[:, cols] * fade + dot(memory_ct, probs_s[rows, cols])
                score_pair(p, *operands, score_s)

    highest_s[0:1] = jnp.full((1, HQ), -3e38, f32)
    total_s[...] = jnp.zeros_like(total_s)
    mixed_s[...] = jnp.zeros_like(mixed_s)
    pl.run_scoped(attend_all, pltpu.VMEM((CHUNK, HQ), f32))
    highest_own = highest_s[0:1]
    total_own = jnp.sum(total_s[...], axis=0, keepdims=True)

    value_wt = attn_in[1, 2].astype(f32).T.astype(bf16)
    key_wt = attn_in[1, 1].astype(f32).T.astype(bf16)
    send_a[...] = project_heads(value_wt, mixed_s[...]).astype(bf16)
    send_t[:HEADS] = head_rows(highest_own)
    send_t[HEADS:] = head_rows(total_own)
    pl.semaphore_wait(barrier, len(peers))
    swap_a = pltpu.make_async_remote_copy(
        src_ref=send_a,
        dst_ref=recv_a,
        send_sem=link_sem.at[0],
        recv_sem=link_sem.at[1],
        device_id=partner,
        device_id_type=pl.DeviceIdType.MESH,
    )
    swap_t = pltpu.make_async_remote_copy(
        src_ref=send_t,
        dst_ref=recv_t,
        send_sem=link_sem.at[4],
        recv_sem=link_sem.at[5],
        device_id=partner,
        device_id_type=pl.DeviceIdType.MESH,
    )
    swap_a.start()
    swap_t.start()
    swap_a.wait()
    swap_t.wait()
    is_first = member == 0
    own, other = send_a[...].astype(f32), recv_a[...].astype(f32)
    left = jnp.where(is_first, own, other)
    right = jnp.where(is_first, other, own)
    own, other = send_t[...], recv_t[...]
    left_t = jnp.where(is_first, own, other)
    right_t = jnp.where(is_first, other, own)
    highest = jnp.maximum(left_t[:HEADS], right_t[:HEADS])
    fade_l = jnp.exp2(left_t[:HEADS] - highest)
    fade_r = jnp.exp2(right_t[:HEADS] - highest)
    total = left_t[HEADS:] * fade_l + right_t[HEADS:] * fade_r
    mixed_t = left * per_channel(fade_l / total) + right * per_channel(fade_r / total)
    log_total = head_line(highest + jnp.log2(total))
    own_share = jnp.exp2(highest_own - log_total)
    factor_s[...] = jnp.exp2(shifts_s[...] - log_total)
    attended_c = (mixed_t.T + bias[4:5]).astype(bf16)

    second_normed, second_rstd = norm_forward(first + dot(attended_c, attn_out[1]) + bias[5:6])
    second = second_normed * gain[1:2] + shift[1:2]
    ffn_input = second.astype(bf16)
    load_ffn[0].wait()
    load_ffn[1].wait()
    blocks = [(j // 4, slice(D * j, D * j + D), slice(j % 4 * D, j % 4 * D + D)) for j in range(FF // D)]
    hidden_bias = ffn_in_bias[...].astype(f32).reshape(1, FF)
    def feed_forward(gate_s):
        for k, cols, part in blocks:
            hidden = dot(ffn_input, ffn_in_s[k][:, part]) + hidden_bias[:, cols]
            half_gate = 0.5 + 0.5 * lax.erf(hidden * math.sqrt(0.5))
            active_s[k][:, part] = (hidden * half_gate).astype(bf16)
            gate_s[:, cols] = half_gate + hidden * jnp.exp(hidden * hidden * -0.5) * (
                1.0 / math.sqrt(2.0 * math.pi)
            )
        load_ffn[2].wait()
        third_normed, third_rstd = norm_forward(
            second
            + dot(active_s[0][...], ffn_out_s[:half])
            + dot(active_s[1][...], ffn_out_s[half:])
            + ffn_out_bias[...].astype(f32).reshape(1, D)
        )
        result_out[...] = (third_normed * gain[2:3] + shift[2:3])[:NQ].astype(bf16)
        grad_third, gain_grad_2, shift_grad_2 = norm_backward(
            pad_s[2], third_normed, third_rstd, gain[2:3]
        )
        grad_branch_f = grad_third.astype(bf16)
        for k, cols, part in blocks:
            grad_hidden = dot_nt(grad_branch_f, ffn_out_s[cols]) * gate_s[:, cols]
            slope_s[k][:, part] = grad_hidden.astype(bf16)
        return grad_third, gain_grad_2, shift_grad_2, grad_branch_f

    grad_third, gain_grad_2, shift_grad_2, grad_branch_f = pl.run_scoped(
        feed_forward, pltpu.VMEM((NP, FF), f32)
    )
    grad_second = grad_third + dot_nt(slope_s[0][...], ffn_in_s[0][...])
    grad_second += dot_nt(slope_s[1][...], ffn_in_s[1][...])
    grad_second_in, gain_grad_1, shift_grad_1 = norm_backward(
        grad_second, second_normed, second_rstd, gain[1:2]
    )
    grad_branch_c = grad_second_in.astype(bf16)
    ffn_input_t = second.T.astype(bf16)

    @pl.when(member == 0)
    def _():
        for k, cols, part in blocks:
            rows_f[cols] = dot(ffn_input_t, slope_s[k][:, part]).astype(bf16)

    @pl.when(member == 1)
    def _():
        for k, cols, part in blocks:
            rows_f[cols] = dot_tn(active_s[k][:, part], grad_branch_f).astype(bf16)

    is_first = member == 0
    out_grad_c = dot_tn(attended_c, grad_branch_c)
    rows_k[2 * D : 3 * D] = jnp.where(is_first, out_grad_c, 0.0).astype(bf16)

    clear_rest(rows_f, ROWS_F)
    clear_rest(rows_t, ROWS_T)
    clear_rest(rows_k, ROWS_K)
    sum_f.phases[0]()
    grad_attended_c = dot_nt(grad_branch_c, attn_out[1]).astype(bf16).astype(f32)
    small_s[:16] = jnp.concatenate(
        [row_total(slope_s[k][:, part]) for k, _, part in blocks]
        + [
            row_total(grad_branch_f),
            row_total(grad_branch_c),
            gain_grad_2,
            shift_grad_2,
            gain_grad_1,
            shift_grad_1,
            row_total(grad_attended_c),
            jnp.zeros((1, D), f32),
        ],
        axis=0,
    )

    store_result = pltpu.make_async_copy(result_out, result_hbm, load_sem.at[7])
    store_result.start()

    grad_attended_t = grad_attended_c.T
    grad_x = spread_rows(grad_attended_c)
    grad_v = dot(attn_in[1, 2], spread_cols(grad_attended_t))
    grad_vt[...] = grad_v.astype(bf16)
    back_s[HQ:] = grad_v.T.astype(bf16)
    inner = head_line(head_sums(grad_attended_t * mixed_t))
    rows_k[D : 2 * D] = dot((mixed_s[...] * own_share).astype(bf16), grad_x).astype(bf16)
    mixed_s[...] = jnp.zeros_like(mixed_s)

    queue_f = sum_f.phases[1:]
    queue_t = list(sum_t.phases)
    queue_k = list(sum_k.phases)

    def take(queue):
        if queue:
            queue.pop(0)()

    def at(i, steps):
        for step, queue in steps:
            pl.when(i == (step * chunks) // 32)(queue.pop(0))

    def slope_block(i):
        rows = pl.ds(pl.multiple_of(i * CHUNK, CHUNK), CHUNK)
        key_ct = key_in_s[rows].T
        memory_c = memory_s[rows]
        for p in range(4):
            cols = pair_cols(p)
            grad_probs = dot(memory_c, grad_vt[:, cols])
            probs = probs_s[rows, cols].astype(f32) * factor_s[pl.ds(i, 1), cols]
            probs_s[rows, cols] = probs.astype(bf16)
            grad_scores_s[rows, cols] = (probs * (grad_probs - inner[:, cols])).astype(bf16)
            mixed_s[:, cols] += dot(key_ct, grad_scores_s[rows, cols])

    @pl.loop(0, chunks // 2)
    def _(i):
        slope_block(i * 2)
        slope_block(i * 2 + 1)
        at(i, [(3, queue_f), (9, queue_f), (15, queue_f)])

    send_b[...] = (project_heads(key_wt, mixed_s[...]) * scale).astype(bf16)
    swap_b = pltpu.make_async_remote_copy(
        src_ref=send_b,
        dst_ref=recv_b,
        send_sem=link_sem.at[2],
        recv_sem=link_sem.at[3],
        device_id=partner,
        device_id_type=pl.DeviceIdType.MESH,
    )
    swap_b.start()
    query_x = spread_rows(query_c.astype(f32))
    rows_k[:D] = (dot(mixed_s[...].astype(bf16), query_x) * scale).astype(bf16)
    take(queue_k)
    swap_b.wait()
    take(queue_f)
    take(queue_k)
    grad_query_c = (send_b[...].astype(f32) + recv_b[...].astype(f32)).T.astype(bf16)

    cross_pos_grad = dot_nt(grad_query_c, attn_in[1, 0])
    grad_first_in, gain_grad_0, shift_grad_0 = norm_backward(
        grad_second_in + cross_pos_grad, first_normed, first_rstd, gain[0:1]
    )
    grad_branch = grad_first_in.astype(bf16)
    grad_attended = dot_nt(grad_branch, attn_out[0]).astype(bf16).astype(f32)
    take(queue_k)
    grad_probs = dot(value_self, spread_cols(grad_attended.T))
    inner_self = jnp.sum(probs_self * grad_probs, axis=0, keepdims=True)
    grad_scores = (probs_self * (grad_probs - inner_self)).astype(bf16)
    key_t = key_self.astype(f32).T.astype(bf16)
    grad_query_s = (
        own_blocks([dot(key_t[pair_rows(p)], grad_scores[:, pair_cols(p)]) for p in range(4)]) * scale
    ).T.astype(bf16)
    grad_key_s = (dot(grad_scores, spread_rows(query_self.astype(f32))) * scale).astype(bf16)
    grad_value_s = dot(probs_self_b, spread_rows(grad_attended)).astype(bf16)
    grad_mixed_q = dot_nt(grad_query_s, attn_in[0, 0]) + dot_nt(grad_key_s, attn_in[0, 1])
    queries_grad_out[...] = (grad_first_in + grad_mixed_q + dot_nt(grad_value_s, attn_in[0, 2]))[
        :NQ
    ].astype(bf16)
    store_queries = pltpu.make_async_copy(queries_grad_out, queries_grad_hbm, load_sem.at[8])
    store_queries.start()
    small_s[16:] = jnp.concatenate(
        [
            row_total(grad_query_s),
            row_total(grad_value_s),
            row_total(grad_branch),
            row_total(grad_query_c),
            gain_grad_0,
            shift_grad_0,
            jnp.zeros((10, D), f32),
        ],
        axis=0,
    )
    @pl.when(member == 0)
    def _():
        rows_t[:D] = dot_tn(mixed_q, grad_query_s).astype(bf16)
        rows_t[D : 2 * D] = dot_tn(mixed_q, grad_key_s).astype(bf16)
        rows_t[2 * D : 3 * D] = dot_tn(queries_b, grad_value_s).astype(bf16)

    @pl.when(member == 1)
    def _():
        rows_t[:D] = dot_tn(cross_q, grad_query_c).astype(bf16)
        rows_t[D : 2 * D] = dot_tn(attended, grad_branch).astype(bf16)
        rows_t[ROW_POS:ROW_SMALL] = (grad_mixed_q + cross_pos_grad).astype(bf16)
        rows_t[ROW_SMALL : ROW_SMALL + 32] = small_s[...].astype(bf16)
        rows_t[ROW_SMALL + 32 : ROWS_T] = jnp.zeros((ROWS_T - ROW_SMALL - 32, D), bf16)

    take(queue_t)
    take(queue_k)
    take(queue_f)

    def memory_block(i):
        rows = pl.ds(pl.multiple_of(i * CHUNK, CHUNK), CHUNK)
        both = jnp.concatenate([grad_scores_s[rows], probs_s[rows]], axis=1)
        memory_s[rows] = dot(both, back_s[...]).astype(bf16)
        pltpu.make_async_copy(memory_s.at[rows], memory_grad_hbm.at[0, rows], store_sem.at[i]).start()

    @pl.loop(0, chunks // 2)
    def _(i):
        memory_block(i * 2)
        memory_block(i * 2 + 1)
        at(
            i,
            [
                (3, queue_t),
                (4, queue_k),
                (7, queue_t),
                (8, queue_k),
                (9, queue_f),
                (11, queue_t),
                (12, queue_k),
                (15, queue_t),
            ],
        )

    while queue_f:
        take(queue_f)
    stores = [
        pltpu.make_async_copy(whole, target, load_sem.at[4 + k])
        for k, (whole, target) in enumerate(
            (
                (whole_f, whole_f_hbm),
                (whole_t, whole_t_hbm),
                (whole_k, whole_k_hbm),
            )
        )
    ]
    stores[0].start()
    while queue_t or queue_k:
        take(queue_t)
        take(queue_k)
    for store in stores[1:]:
        store.start()

    @pl.loop(0, chunks)
    def _(i):
        rows = pl.ds(pl.multiple_of(i * CHUNK, CHUNK), CHUNK)
        pltpu.make_async_copy(memory_s.at[rows], memory_grad_hbm.at[0, rows], store_sem.at[i]).wait()

    for store in [*stores, store_result, store_queries]:
        store.wait()


def finish_kernel(
    result_in,
    queries_grad_in,
    memory_grad_in,
    whole_f_hbm,
    whole_t_hbm,
    whole_k_hbm,
    result_hbm,
    queries_grad_hbm,
    memory_grad,
    attn_in_hbm,
    attn_out_hbm,
    attn_bias_hbm,
    ffn_in_hbm,
    ffn_in_bias_hbm,
    ffn_out_hbm,
    ffn_out_bias_hbm,
    norm_gain_hbm,
    norm_bias_hbm,
    query_pos_hbm,
    moved,
    whole_f,
    whole_t,
    whole_k,
    result,
    queries_grad,
    attn_in_grad,
    attn_out_grad,
    attn_bias_grad,
    ffn_in_grad,
    ffn_in_bias_grad,
    ffn_out_grad,
    ffn_out_bias_grad,
    norm_gain_grad,
    norm_bias_grad,
    query_pos_grad,
    in_sem,
    out_sem,
    sum_sem,
    grad_sem,
):
    pieces = in_sem.shape[0]
    piece = moved.shape[0] // pieces

    def fetch(j):
        rows = pl.ds(piece * j, piece)
        return pltpu.make_async_copy(memory_grad_in.at[0, rows], moved.at[rows], in_sem.at[j])

    def write(j):
        rows = pl.ds(piece * j, piece)
        return pltpu.make_async_copy(moved.at[rows], memory_grad.at[0, rows], out_sem.at[j])

    sums = [
        (whole_t_hbm, whole_t),
        (whole_k_hbm, whole_k),
        (whole_f_hbm, whole_f),
        (result_in, result),
        (queries_grad_in, queries_grad),
    ]
    loads = [pltpu.make_async_copy(*pair, sum_sem.at[j]) for j, pair in enumerate(sums)]
    for load in loads:
        load.start()
    for j in range(pieces):
        fetch(j).start()
    blocks = FF // D
    stores = []

    def store(source, target):
        stores.append(pltpu.make_async_copy(source, target, grad_sem.at[len(stores)]))
        stores[-1].start()

    loads[0].wait()
    loads[1].wait()
    for j in range(3):
        attn_in_grad[0, j] = whole_t[0, D * j : D * j + D].astype(f32)
    attn_in_grad[1, 0] = whole_t[1, :D].astype(f32)
    attn_in_grad[1, 1] = whole_k[:D].astype(f32)
    attn_in_grad[1, 2] = whole_k[D : 2 * D].astype(f32)
    store(attn_in_grad, attn_in_hbm)
    attn_out_grad[0] = whole_t[1, D : 2 * D].astype(f32)
    attn_out_grad[1] = whole_k[2 * D : 3 * D].astype(f32)
    store(attn_out_grad, attn_out_hbm)
    loads[2].wait()
    for k in range(2):
        half = slice(FF // 2 * k, FF // 2 * (k + 1))
        ffn_out_grad[half] = whole_f[1, half].astype(f32)
        store(ffn_out_grad.at[half], ffn_out_hbm.at[half])
    for k in range(2):
        half = slice(FF // 2 * k, FF // 2 * (k + 1))
        for j in range(blocks // 2 * k, blocks // 2 * (k + 1)):
            at = slice(D * j, D * j + D)
            ffn_in_grad[:, at] = whole_f[0, at].astype(f32)
        store(ffn_in_grad.at[:, half], ffn_in_hbm.at[:, half])
    for j in range(pieces):
        fetch(j).wait()
        write(j).start()
    loads[3].wait()
    store(result, result_hbm.at[0])
    loads[4].wait()
    store(queries_grad, queries_grad_hbm.at[0])
    query_pos_grad[...] = whole_t[1, ROW_POS:ROW_SMALL].astype(f32)[:NQ]
    store(query_pos_grad, query_pos_hbm)
    small = whole_t[1, ROW_SMALL : ROW_SMALL + 32].astype(f32)
    ffn_in_bias_grad[...] = jnp.concatenate([small[j : j + 1] for j in range(blocks)], axis=1)
    store(ffn_in_bias_grad, ffn_in_bias_hbm)
    ffn_out_bias_grad[...] = small[8:9]
    store(ffn_out_bias_grad, ffn_out_bias_hbm)
    for j, (own, cross) in enumerate(((16, 19), (17, 14), (18, 9))):
        attn_bias_grad[j, 0:1] = small[own : own + 1]
        attn_bias_grad[j, 1:2] = small[cross : cross + 1]
    store(attn_bias_grad, attn_bias_hbm)
    for j, (gain, shift) in enumerate(((20, 21), (12, 13), (10, 11))):
        norm_gain_grad[j : j + 1] = small[gain : gain + 1]
        norm_bias_grad[j : j + 1] = small[shift : shift + 1]
    store(norm_gain_grad, norm_gain_hbm)
    store(norm_bias_grad, norm_bias_hbm)
    for j in range(pieces):
        write(j).wait()
    for copy in stores:
        copy.wait()


def body(
    pages,
    queries,
    memory,
    quarter_turns,
    token_order,
    lengths,
    attn_in,
    attn_out,
    attn_bias,
    ffn_in,
    ffn_in_bias,
    ffn_out,
    ffn_out_bias,
    norm_gain,
    norm_bias,
    query_pos,
    out_grad,
):
    tokens = memory.shape[1]
    chunks = tokens // CHUNK
    groups_f, groups_t, groups_k = sum_groups(pages)
    summed = [
        (padded(ROWS_F, pages), groups_f),
        (padded(ROWS_T, pages), groups_t),
        (padded(ROWS_K, 2 * pages), groups_k),
    ]
    whole_shapes = [(2, rows, D) for rows, _ in summed[:2]] + [(summed[2][0], D)]
    sum_buffers = []
    for (rows, groups), shape in zip(summed, whole_shapes):
        landing = PageSum.landing_rows(pages, groups, rows)
        sum_buffers += [pltpu.VMEM(each, bf16) for each in ((rows, D), (landing, D), shape)]
    copies = 32
    vmem = pl.BlockSpec(memory_space=pltpu.VMEM)
    smem = pl.BlockSpec(memory_space=pltpu.SMEM)
    anywhere = pl.BlockSpec(memory_space=pl.ANY)
    parts = pl.pallas_call(
        functools.partial(layer_kernel, tokens, pages),
        out_shape=[
            jax.ShapeDtypeStruct((NQ, D), bf16),
            jax.ShapeDtypeStruct((NQ, D), bf16),
            jax.ShapeDtypeStruct((1, tokens, D), bf16),
            *(jax.ShapeDtypeStruct(shape, bf16) for shape in whole_shapes),
        ],
        in_specs=[
            vmem,
            anywhere,
            smem,
            vmem,
            smem,
            vmem,
            vmem,
            vmem,
            anywhere,
            vmem,
            anywhere,
            vmem,
            vmem,
            vmem,
            vmem,
            vmem,
            vmem,
        ],
        out_specs=[anywhere] * 6,
        scratch_shapes=[
            pltpu.VMEM((tokens, D), bf16),
            pltpu.VMEM((tokens, D), bf16),
            pltpu.VMEM((tokens, HQ), bf16),
            pltpu.VMEM((tokens, HQ), bf16),
            pltpu.VMEM((1, tokens), f32),
            pltpu.VMEM((D, HQ), bf16),
            pltpu.VMEM((D, HQ), bf16),
            pltpu.VMEM((2 * HQ, D), bf16),
            pltpu.VMEM((4 * SIDE, D), bf16),
            pltpu.VMEM((8, HQ), f32),
            pltpu.VMEM((8, HQ), f32),
            pltpu.VMEM((chunks, HQ), f32),
            pltpu.VMEM((chunks, HQ), f32),
            pltpu.VMEM((8, HQ), f32),
            pltpu.VMEM((D, HQ), f32),
            pltpu.VMEM((3, NP, D), f32),
            pltpu.VMEM((NQ, D), bf16),
            pltpu.VMEM((NQ, D), bf16),
            pltpu.VMEM((D, NP), bf16),
            pltpu.VMEM((D, NP), bf16),
            pltpu.VMEM((2 * HEADS, NP), f32),
            pltpu.VMEM((2 * HEADS, NP), f32),
            pltpu.VMEM((D, NP), bf16),
            pltpu.VMEM((D, NP), bf16),
            pltpu.VMEM((32, D), f32),
            *sum_buffers,
            pltpu.SemaphoreType.DMA((9,)),
            pltpu.SemaphoreType.DMA((chunks,)),
            pltpu.SemaphoreType.DMA((6,)),
            *[pltpu.SemaphoreType.DMA((copies,))] * 6,
        ],
        compiler_params=pltpu.CompilerParams(
            collective_id=0, has_side_effects=True, vmem_limit_bytes=127 * 512 * 1024
        ),
        cost_estimate=pl.CostEstimate(
            flops=2 * 8 * tokens * HQ * D, bytes_accessed=20 << 20, transcendentals=tokens * HQ
        ),
        name="decoder_layer",
    )(
        queries,
        memory,
        quarter_turns,
        token_order,
        lengths,
        attn_in,
        attn_out,
        attn_bias.transpose(1, 0, 2),
        ffn_in,
        ffn_in_bias,
        ffn_out,
        ffn_out_bias,
        norm_gain,
        norm_bias,
        query_pos,
        out_grad,
        jnp.asarray(position_table()),
    )
    outs = pl.pallas_call(
        finish_kernel,
        out_shape=[
            jax.ShapeDtypeStruct((1, NQ, D), bf16),
            jax.ShapeDtypeStruct((1, NQ, D), bf16),
            jax.ShapeDtypeStruct((1, tokens, D), bf16),
            jax.ShapeDtypeStruct((2, 3, D, D), f32),
            jax.ShapeDtypeStruct((2, D, D), f32),
            jax.ShapeDtypeStruct((3, 2, D), f32),
            jax.ShapeDtypeStruct((D, FF), f32),
            jax.ShapeDtypeStruct((1, FF), f32),
            jax.ShapeDtypeStruct((FF, D), f32),
            jax.ShapeDtypeStruct((1, D), f32),
            jax.ShapeDtypeStruct((3, D), f32),
            jax.ShapeDtypeStruct((3, D), f32),
            jax.ShapeDtypeStruct((NQ, D), f32),
        ],
        in_specs=[anywhere] * 6,
        out_specs=[anywhere] * 13,
        scratch_shapes=[
            pltpu.VMEM((tokens, D), bf16),
            *(pltpu.VMEM(shape, bf16) for shape in whole_shapes),
            pltpu.VMEM((NQ, D), bf16),
            pltpu.VMEM((NQ, D), bf16),
            pltpu.VMEM((2, 3, D, D), f32),
            pltpu.VMEM((2, D, D), f32),
            pltpu.VMEM((3, 2, D), f32),
            pltpu.VMEM((D, FF), f32),
            pltpu.VMEM((1, FF), f32),
            pltpu.VMEM((FF, D), f32),
            pltpu.VMEM((1, D), f32),
            pltpu.VMEM((3, D), f32),
            pltpu.VMEM((3, D), f32),
            pltpu.VMEM((NQ, D), f32),
            pltpu.SemaphoreType.DMA((8,)),
            pltpu.SemaphoreType.DMA((8,)),
            pltpu.SemaphoreType.DMA((5,)),
            pltpu.SemaphoreType.DMA((14,)),
        ],
        compiler_params=pltpu.CompilerParams(vmem_limit_bytes=62 * 1024 * 1024),
        name="write_outputs",
    )(*parts)
    return (
        *outs[:5],
        outs[5].transpose(1, 0, 2),
        outs[6],
        outs[7].reshape(FF),
        outs[8],
        outs[9].reshape(D),
        *outs[10:],
    )


def solution(mesh):
    in_specs = (
        P("dp", None, None),
        P("dp", "blk", None),
        P("dp"),
        P("dp", "blk"),
        P("dp"),
        P(),
        P(),
        P(),
        P(),
        P(),
        P(),
        P(),
        P(),
        P(),
        P(),
        P("dp", None, None),
    )
    out_specs = (
        P("dp", None, None),
        P("dp", None, None),
        P("dp", "blk", None),
        P(),
        P(),
        P(),
        P(),
        P(),
        P(),
        P(),
        P(),
        P(),
        P(),
    )
    layer = functools.partial(body, mesh.shape["dp"])
    return jax.shard_map(layer, mesh=mesh, in_specs=in_specs, out_specs=out_specs, check_vma=False)
```
